32 devices in a mesh: wide: 16 (over z, x, core), narrow: 2 (over y).
Axes of the slice: x: 2, y: 2, z: 4, core: 2. Of those that a mesh axis runs over, the one named last changes fastest.
Arguments:
- tokens: bfloat16 [4096, 1024], P('wide', 'narrow'), may hold values from -6 to 6
- norm_gain: float32 [1024], replicated, may hold values from 0.1 to 1.9
- in_weight: bfloat16 [1024, 2, 2048], P(None, None, 'narrow'), may hold values from -0.1875 to 0.1875
- conv_weight: float32 [4, 2048], P(None, 'narrow'), may hold values from -3 to 3
- conv_bias: float32 [2048], P('narrow'), may hold values from -3 to 3
- select_weight: bfloat16 [96, 2048], P(None, 'narrow'), may hold values from -0.125 to 0.125
- step_weight: bfloat16 [64, 2048], P(None, 'narrow'), may hold values from -0.75 to 0.75
- step_bias: float32 [2048], P('narrow'), may hold values from -6 to -2
- decay_log: float32 [16, 2048], P(None, 'narrow'), may hold values from -10 to 1
- skip_gain: float32 [2048], P('narrow'), may hold values from 0.5 to 1.5
- out_weight: bfloat16 [2048, 1024], P('narrow'), may hold values from -0.125 to 0.125
- segment_ids: int32 [4096], P('wide'), may hold values from 0 to 16, as said below
- cotangent: bfloat16 [4096, 1024], P('wide', 'narrow'), may hold values from -6 to 6
Outputs:
- layer_out: bfloat16 [4096, 1024], P('wide', 'narrow')
- tokens_grad: bfloat16 [4096, 1024], P('wide', 'narrow')
- norm_gain_grad: float32 [1024], replicated
- in_weight_grad: float32 [1024, 2, 2048], P(None, None, 'narrow')
- conv_weight_grad: float32 [4, 2048], P(None, 'narrow')
- conv_bias_grad: float32 [2048], P('narrow')
- select_weight_grad: float32 [96, 2048], P(None, 'narrow')
- step_weight_grad: float32 [64, 2048], P(None, 'narrow')
- step_bias_grad: float32 [2048], P('narrow')
- decay_log_grad: float32 [16, 2048], P(None, 'narrow')
- skip_gain_grad: float32 [2048], P('narrow')
- out_weight_grad: float32 [2048, 1024], P('narrow')
The draws below stay inside these ranges and needn't reach their ends.
Inputs may be any that keep to these rules, and one draw needn't show every extreme that they name: `segment_ids`: segment ids never fall along the tokens and the first is 0; they rise by one at a time, exactly 4 times in each aligned block of 1024 tokens, and never at the first token of an aligned block of 256 tokens.
All inputs are finite; a program needn't handle non-finite values.
Results may differ from the reference program's by a relative error of at most 0.0065.
The reference program's roundings to bfloat16 on the way count: a program that leaves them out, or rounds other values in their place, can miss the bound.
Values may be sent and summed in bfloat16 or wider, within the bound.
No kernel may reach another device: no remote copies, remote signals or barrier semaphores. Data moves between devices by JAX's collectives and lax.ppermute only.
A program may use at most 128 MiB of HBM per device.

```python
import jax
import jax.numpy as jnp
from jax import lax

D = 1024
E = 2048
STATE = 16
TAPS = 4
RANK = 64
TOK_DEV = 256
SELECT = 96
TOKENS = 4096


def pick_starts(group_key):
    interior = TOK_DEV - 1
    return jax.random.permutation(group_key, 4 * interior)[:4].astype(jnp.int32)


def draw_segment_ids(key, part):
    key = jax.random.fold_in(key, 7)
    group_rows = 4 * TOK_DEV
    group_count = TOKENS // group_rows
    interior = TOK_DEV - 1
    group_keys = jax.random.split(key, group_count)
    chosen = jax.vmap(pick_starts)(group_keys)
    device_of = (chosen // interior).astype(jnp.int32)
    offset = (1 + chosen % interior).astype(jnp.int32)
    group_start = (jnp.arange(group_count, dtype=jnp.int32) * group_rows)[:, None]
    positions = (group_start + device_of * TOK_DEV + offset).reshape(-1).astype(jnp.int32)
    boundary = jnp.zeros((TOKENS,), jnp.int32).at[positions].set(1)
    return jnp.cumsum(boundary).astype(jnp.int32)


def shard_levels(own_key, shape, cuts, smallest, largest):
    def one(axis_at, blocks):
        draws = jax.random.uniform(jax.random.fold_in(jax.random.fold_in(own_key, 6), axis_at), (blocks,), jnp.float32, smallest / len(cuts), largest / len(cuts))
        return jnp.repeat(jnp.exp(draws), shape[axis_at] // blocks).reshape((-1,) + (1,) * (len(shape) - axis_at - 1))

    gain = one(*cuts[0])
    for cut in cuts[1:]:
        gain = gain * one(*cut)
    return gain


def scatter_about(rng, dims, deviation, bound, shards=(), held_as=jnp.bfloat16):
    values = jax.random.normal(rng, dims, jnp.float32) * deviation
    if len(shards) > 0:
        values = shard_levels(rng, dims, shards, -0.22, 0.18) * values
    return jnp.clip(values, min=-bound, max=bound).astype(held_as)


def setup_inputs(seed: int = 0) -> dict:
    splits = jax.random.split(jax.random.key(seed), 14)
    tokens = scatter_about(splits[0], (TOKENS, D), 1.0, 6.0, ((0, 16), (1, 2)))
    norm_gain = jnp.clip(1.0 + 0.18 * jax.random.normal(splits[1], (D,), jnp.float32), 0.1, 1.9)
    in_weight = scatter_about(splits[2], (D, 2, E), D ** -0.5, 0.1875, ((2, 2),))
    conv_weight = scatter_about(splits[3], (TAPS, E), TAPS ** -0.5, 3.0, ((1, 2),), jnp.float32)
    conv_bias = scatter_about(splits[4], (E,), 0.5, 3.0, ((0, 2),), jnp.float32)
    select_weight = scatter_about(splits[5], (SELECT, E), E ** -0.5, 0.125, ((1, 2),))
    step_weight = scatter_about(splits[6], (RANK, E), RANK ** -0.5, 0.75, ((1, 2),))
    step_bias = jnp.clip(-6.0 + 4.0 * jax.random.uniform(splits[7], (E,), jnp.float32) ** shard_levels(splits[7], (E,), ((0, 2),), -0.2, 0.2), -6.0, -2.0)
    decay_log = jnp.clip(-10.0 + 11.0 * jax.random.uniform(splits[8], (STATE, E), jnp.float32) ** shard_levels(splits[8], (STATE, E), ((1, 2),), -0.2, 0.2), -10.0, 1.0)
    skip_gain = jnp.clip(0.5 + 1.0 * jax.random.uniform(splits[9], (E,), jnp.float32) ** shard_levels(splits[9], (E,), ((0, 2),), -0.2, 0.2), 0.5, 1.5)
    out_weight = scatter_about(splits[10], (E, D), E ** -0.5, 0.125, ((0, 2),))
    segment_ids = draw_segment_ids(jax.random.fold_in(splits[13], 71), 0)
    cotangent = scatter_about(splits[12], (TOKENS, D), 1.0, 6.0, ((0, 16), (1, 2)))
    return {"tokens": tokens, "norm_gain": norm_gain, "in_weight": in_weight, "conv_weight": conv_weight, "conv_bias": conv_bias, "select_weight": select_weight, "step_weight": step_weight, "step_bias": step_bias, "decay_log": decay_log, "skip_gain": skip_gain, "out_weight": out_weight, "segment_ids": segment_ids, "cotangent": cotangent}


epsilon = 1e-05
scan_rows = 256

@jax.custom_vjp
def low(v):
    return lax.optimization_barrier(v.astype(jnp.bfloat16)).astype(jnp.float32)

@jax.custom_vjp
def low_back(v):
    return v

def low_keep(v):
    return (low(v), None)

def low_pass(kept, grad):
    return (grad,)

def back_keep(v):
    return (v, None)

def back_low(kept, grad):
    return (low(grad),)
low.defvjp(low_keep, low_pass)
low_back.defvjp(back_keep, back_low)

def silu_of(values):
    return values * jax.nn.sigmoid(values)

def scan_segment(decay_mat, carried, pieces):

    def advance(current, row_piece):
        act_row, step_row, in_row, read_row, keep_row = row_piece
        current = jnp.exp(step_row[None, :] * decay_mat) * keep_row * current + in_row[:, None] * (step_row * act_row)[None, :]
        return (current, lax.optimization_barrier(jnp.sum(read_row[:, None] * current, axis=0)))
    return lax.scan(advance, carried, pieces)

def selective(activated, step_size, in_coef, read_coef, keep_flag, decay_mat):
    total_rows = activated.shape[0]
    width_all = activated.shape[1]
    block_count = total_rows // scan_rows

    def blocked(operand):
        return operand.reshape((block_count, scan_rows) + operand.shape[1:])
    segment_fn = jax.checkpoint(scan_segment)

    def per_block(carried, pieces):
        return segment_fn(decay_mat, carried, pieces)
    initial = jnp.zeros((decay_mat.shape[0], width_all), jnp.float32)
    ignored, outputs = lax.scan(per_block, initial, (blocked(activated), blocked(step_size), blocked(in_coef), blocked(read_coef), blocked(keep_flag)))
    return outputs.reshape(total_rows, width_all)

def layer(tokens, norm_gain, in_weight, conv_weight, conv_bias, select_weight, step_weight, step_bias, decay_log, skip_gain, out_weight, segment_ids):
    highest = lax.Precision.HIGHEST
    inverse = lax.rsqrt(lax.optimization_barrier(jnp.mean(tokens * tokens, axis=1, keepdims=True)) + epsilon)
    normed = low(tokens * inverse * norm_gain)
    projected = low_back(low(jnp.einsum('td,dce->tce', normed, in_weight, precision=highest)))
    inner_half = projected[:, 0]
    gate_half = projected[:, 1]
    tap_count = conv_weight.shape[0]
    convolved = conv_bias + conv_weight[tap_count - 1] * inner_half
    for lag_rows in range(1, tap_count):
        earlier = jnp.concatenate([jnp.zeros((lag_rows, inner_half.shape[1]), jnp.float32), inner_half[:-lag_rows]], axis=0)
        same_segment = jnp.concatenate([jnp.zeros((lag_rows,), jnp.float32), jnp.where(segment_ids[lag_rows:] == segment_ids[:-lag_rows], 1.0, 0.0).astype(jnp.float32)])
        convolved = convolved + conv_weight[tap_count - 1 - lag_rows] * earlier * same_segment[:, None]
    activated = low(silu_of(convolved))
    selected = low_back(jnp.dot(activated, select_weight.T, precision=highest))
    rank_size = step_weight.shape[0]
    state_count = decay_log.shape[0]
    step_low = low(selected[:, :rank_size])
    in_coef = selected[:, rank_size:rank_size + state_count]
    read_coef = selected[:, rank_size + state_count:]
    step_pre = low_back(jnp.dot(step_low, step_weight, precision=highest) + step_bias)
    step_size = jax.nn.softplus(step_pre)
    decay_mat = -jnp.exp(decay_log)
    keep_flag = jnp.concatenate([jnp.zeros((1,), jnp.float32), jnp.where(segment_ids[1:] == segment_ids[:-1], 1.0, 0.0).astype(jnp.float32)])
    scanned = selective(activated, step_size, in_coef, read_coef, keep_flag, decay_mat) + skip_gain * activated
    gated = low(scanned * silu_of(gate_half))
    return tokens + jnp.dot(gated, out_weight, precision=highest)

def reference(tokens, norm_gain, in_weight, conv_weight, conv_bias, select_weight, step_weight, step_bias, decay_log, skip_gain, out_weight, segment_ids, cotangent):
    floats = (tokens.astype(jnp.float32), norm_gain.astype(jnp.float32), in_weight.astype(jnp.float32), conv_weight.astype(jnp.float32), conv_bias.astype(jnp.float32), select_weight.astype(jnp.float32), step_weight.astype(jnp.float32), step_bias.astype(jnp.float32), decay_log.astype(jnp.float32), skip_gain.astype(jnp.float32), out_weight.astype(jnp.float32))

    def wrapped(*values):
        return layer(*values, segment_ids)
    output, pullback = jax.vjp(wrapped, *floats)
    grads = pullback(cotangent.astype(jnp.float32))
    return (output.astype(jnp.bfloat16), grads[0].astype(jnp.bfloat16), grads[1], grads[2], grads[3], grads[4], grads[5], grads[6], grads[7], grads[8], grads[9], grads[10])
```

```python
import functools

import jax
import jax.numpy as jnp
from jax import lax
from jax.experimental import pallas as pl
from jax.experimental.pallas import tpu as pltpu
from jax.sharding import PartitionSpec as P

epsilon = 1e-05
log2e = 1.4426950408889634
reset_step = 1e30
lanes = 128
body_rows = 32
scan_width = 512
vmem_bytes = 56 * 1024 * 1024
f32 = jnp.float32


def passed_along(array, axis, by):
    peers = lax.axis_size(axis)
    pairs = [(i, i + by) for i in range(peers) if 0 <= i + by < peers]
    return lax.ppermute(array, axis, pairs)


def swapped(array, axis, bit):
    peers = lax.axis_size(axis)
    return lax.ppermute(array, axis, [(i, i ^ bit) for i in range(peers)])


def silu_of(values):
    return values * jax.nn.sigmoid(values)


def silu_slope(values):
    logistic = jax.nn.sigmoid(values)
    return logistic * (1.0 + values * (1.0 - logistic))


def coef_columns(coef_ref, block):
    per_tile = lanes // body_rows
    start = pl.multiple_of((block // per_tile) * lanes, lanes)
    tile = coef_ref[:, pl.ds(start, lanes)]
    back = body_rows * lax.rem(block, per_tile)
    return pltpu.roll(tile, lax.rem(lanes - back, lanes), 1)


def ends_kernel(held_step_ref, drive_ref, grad_ref, coef_ref, decay_ref, out_ref):
    rows = held_step_ref.shape[0]
    count = decay_ref.shape[0]
    decay2 = decay_ref[...]
    zero = jnp.zeros(decay2.shape, f32)

    def body(block, carried):
        state, product, adjoint = carried
        columns = coef_columns(coef_ref, block)
        for i in range(body_rows):
            row = pl.ds(block * body_rows + i, 1)
            factor = jnp.exp2(held_step_ref[row, :] * decay2)
            state = factor * state + columns[:count, i : i + 1] * drive_ref[row, :]
            product = factor * product
            adjoint = adjoint + product * (columns[count:, i : i + 1] * grad_ref[row, :])
        return state, product, adjoint

    state, product, adjoint = lax.fori_loop(0, rows // body_rows, body, (zero, zero + 1.0, zero))
    out_ref[:count, :] = state
    out_ref[count : 2 * count, :] = adjoint
    total = jnp.sum(held_step_ref[...], axis=0, keepdims=True)
    out_ref[2 * count :, :] = jnp.broadcast_to(total, (8, total.shape[1]))


def column_spec(rows, width):
    return pl.BlockSpec((rows, width), lambda j: (0, j))


def whole_spec(rows, width):
    return pl.BlockSpec((rows, width), lambda j: (0, 0))


def scan_ends(held_step, drive, grad, coef, decay2):
    rows, width = held_step.shape
    count = decay2.shape[0]
    return pl.pallas_call(
        ends_kernel,
        grid=(width // scan_width,),
        in_specs=[column_spec(rows, scan_width)] * 3
        + [whole_spec(2 * count, rows), column_spec(count, scan_width)],
        out_specs=column_spec(2 * count + 8, scan_width),
        out_shape=jax.ShapeDtypeStruct((2 * count + 8, width), f32),
        compiler_params=pltpu.CompilerParams(vmem_limit_bytes=vmem_bytes),
        name="scan_ends",
    )(held_step, drive, grad, coef, decay2)


def lane_tiles(values):
    return [values[:, k : k + lanes] for k in range(0, values.shape[1], lanes)]


def tree_sum(parts):
    while len(parts) > 1:
        odd = parts[len(parts) // 2 * 2 :]
        parts = [a + b for a, b in zip(parts[0::2], parts[1::2])] + odd
    return parts[0]


def keep_halves(scratch, i, values):
    for k, tile in enumerate(lane_tiles(values)):
        at = (k * body_rows + i) * 8
        scratch[at : at + 8, :] = tile[:8] + tile[8:]


def put_state_sums(scratch, out_ref, block):
    for group in range(body_rows // 8):
        row = pl.ds(pl.multiple_of(block * body_rows + group * 8, 8), 8)
        for k in range(out_ref.shape[1] // lanes):
            at = (k * body_rows + group * 8) * 8
            total = tree_sum([scratch[pl.ds(at + n, 8, stride=8), :] for n in range(8)])
            out_ref[row, k * lanes : (k + 1) * lanes] = total


def scan_kernel(
    held_step_ref,
    step_ref,
    drive_ref,
    grad_ref,
    coef_ref,
    decay2_ref,
    decay_ref,
    entry_ref,
    tail_ref,
    read_ref,
    weighted_ref,
    held_ref,
    in_sum_ref,
    read_sum_ref,
    decay_grad_ref,
    states,
    factors,
    halves,
    more_halves,
):
    rows = step_ref.shape[0]
    count = decay_ref.shape[0]
    blocks = rows // body_rows
    decay2 = decay2_ref[...]
    decay = decay_ref[...]
    states[:count, :] = entry_ref[...]

    @pl.when(pl.program_id(0) == 0)
    def _():
        in_sum_ref[...] = jnp.zeros(in_sum_ref.shape, f32)
        read_sum_ref[...] = jnp.zeros(read_sum_ref.shape, f32)

    def at_token(t):
        return pl.ds(pl.multiple_of(t * count, count), count)

    def forward(block, state):
        columns = coef_columns(coef_ref, block)
        for i in range(body_rows):
            t = block * body_rows + i
            row = pl.ds(t, 1)
            factor = jnp.exp2(held_step_ref[row, :] * decay2)
            state = factor * state + columns[:count, i : i + 1] * drive_ref[row, :]
            factors[at_token(t), :] = factor
            states[at_token(t + 1), :] = state
            keep_halves(halves, i, columns[count:, i : i + 1] * state)
        put_state_sums(halves, read_ref, block)
        return state

    lax.fori_loop(0, blocks, forward, entry_ref[...])

    def backward(k, carried):
        adjoint, decay_grad = carried
        block = blocks - 1 - k
        columns = coef_columns(coef_ref, block)
        for i in range(body_rows - 1, -1, -1):
            t = block * body_rows + i
            row = pl.ds(t, 1)
            grad = grad_ref[row, :]
            drive = drive_ref[row, :]
            summed = columns[count:, i : i + 1] * grad + adjoint
            read_sum_ref[at_token(t), :] += tree_sum(lane_tiles(grad * states[at_token(t + 1), :]))
            in_sum_ref[at_token(t), :] += tree_sum(lane_tiles(summed * drive))
            keep_halves(halves, i, summed * columns[:count, i : i + 1])
            adjoint = factors[at_token(t), :] * summed
            held = adjoint * states[at_token(t), :]
            decay_grad = decay_grad + held * step_ref[row, :]
            keep_halves(more_halves, i, held * decay)
        put_state_sums(halves, weighted_ref, block)
        put_state_sums(more_halves, held_ref, block)
        return adjoint, decay_grad

    ignored, decay_grad = lax.fori_loop(
        0, blocks, backward, (tail_ref[...], jnp.zeros(decay.shape, f32))
    )
    decay_grad_ref[...] = decay_grad


def scan_full(held_step, step, drive, grad, coef, decay2, decay, entry, tail):
    rows, width = step.shape
    count = decay.shape[0]
    half_rows = 8 * body_rows * (scan_width // lanes)
    return pl.pallas_call(
        scan_kernel,
        grid=(width // scan_width,),
        in_specs=[column_spec(rows, scan_width)] * 4
        + [whole_spec(2 * count, rows)]
        + [column_spec(count, scan_width)] * 4,
        out_specs=[column_spec(rows, scan_width)] * 3
        + [whole_spec(rows * count, lanes)] * 2
        + [column_spec(count, scan_width)],
        out_shape=[jax.ShapeDtypeStruct((rows, width), f32)] * 3
        + [jax.ShapeDtypeStruct((rows * count, lanes), f32)] * 2
        + [jax.ShapeDtypeStruct((count, width), f32)],
        scratch_shapes=[
            pltpu.VMEM(((rows + 1) * count, scan_width), f32),
            pltpu.VMEM((rows * count, scan_width), f32),
            pltpu.VMEM((half_rows, lanes), f32),
            pltpu.VMEM((half_rows, lanes), f32),
        ],
        compiler_params=pltpu.CompilerParams(vmem_limit_bytes=vmem_bytes),
        name="scan_full",
    )(held_step, step, drive, grad, coef, decay2, decay, entry, tail)


def carried(ends, decay):
    count = decay.shape[0]
    place = lax.axis_index("wide")

    def split(packed):
        return packed[:count], packed[count : 2 * count], packed[2 * count : 2 * count + 1]

    def through(total):
        return jnp.exp(decay * total)

    zero = jnp.zeros(decay.shape, f32)
    none = jnp.zeros((1, decay.shape[1]), f32)
    before, before_steps, after, after_steps = zero, none, zero, none
    packed = ends
    for bit in (1, 2):
        second = (place & bit) != 0
        own = split(packed)
        other = split(swapped(packed, "wide", bit))
        early = [jnp.where(second, b, a) for a, b in zip(own, other)]
        late = [jnp.where(second, a, b) for a, b in zip(own, other)]
        before = before + jnp.where(second, through(before_steps) * other[0], 0.0)
        before_steps = before_steps + jnp.where(second, other[2], 0.0)
        after = after + jnp.where(second, 0.0, through(after_steps) * other[1])
        after_steps = after_steps + jnp.where(second, 0.0, other[2])
        state = late[0] + through(late[2]) * early[0]
        adjoint = early[1] + through(early[2]) * late[1]
        packed = jnp.concatenate(
            [state, adjoint, jnp.broadcast_to(early[2] + late[2], (8, decay.shape[1]))]
        )
    from_before = passed_along(packed[:count], "wide", 4)
    from_after = passed_along(packed[count : 2 * count], "wide", -4)
    return (
        before + through(before_steps) * from_before,
        after + through(after_steps) * from_after,
    )


def local(
    tokens,
    norm_gain,
    in_weight,
    conv_weight,
    conv_bias,
    select_weight,
    step_weight,
    step_bias,
    decay_log,
    skip_gain,
    out_weight,
    segment_ids,
    cotangent,
):
    row_count = tokens.shape[0]
    tap_count = conv_weight.shape[0]
    lag_rows = tap_count - 1
    rank_size = step_weight.shape[0]
    state_count = decay_log.shape[0]
    contract_rows = (((0,), (0,)), ((), ()))
    contract_last = (((1,), (1,)), ((), ()))
    whole = lax.all_gather(tokens, "narrow", axis=1, tiled=True).astype(jnp.float32)
    inverse = lax.rsqrt(jnp.mean(whole * whole, axis=1, keepdims=True) + epsilon)
    normed = (whole * inverse * norm_gain).astype(jnp.bfloat16)
    projected = jnp.einsum(
        "td,dce->tce", normed, in_weight, preferred_element_type=jnp.float32
    ).astype(jnp.bfloat16)
    inner_half = projected[:, 0].astype(jnp.float32)
    gate_half = projected[:, 1].astype(jnp.float32)
    seg_float = segment_ids.astype(jnp.float32)
    prior_rows, prior_seg = passed_along(
        (inner_half[row_count - lag_rows :], seg_float[row_count - lag_rows :]), "wide", 1
    )
    extended = jnp.concatenate([prior_rows, inner_half], axis=0)
    ext_seg = jnp.concatenate([prior_seg, seg_float], axis=0)
    masks = []
    convolved = conv_bias + jnp.zeros(inner_half.shape, jnp.float32)
    for tap_index in range(tap_count):
        tap_mask = jnp.where(ext_seg[tap_index : tap_index + row_count] == seg_float, 1.0, 0.0)[
            :, None
        ]
        masks.append(tap_mask)
        convolved = (
            convolved
            + conv_weight[tap_index] * extended[tap_index : tap_index + row_count] * tap_mask
        )
    keep_flag = jnp.where(
        seg_float == jnp.concatenate([prior_seg[lag_rows - 1 :], seg_float[:-1]]), 1.0, 0.0
    )
    activated = silu_of(convolved).astype(jnp.bfloat16)
    act_float = activated.astype(jnp.float32)
    all_act, all_weight = (
        lax.all_gather(activated, "narrow", axis=1, tiled=True),
        lax.all_gather(select_weight, "narrow", axis=1, tiled=True),
    )
    selected = lax.dot_general(
        all_act, all_weight, contract_last, preferred_element_type=jnp.float32
    )
    step_low = selected[:, :rank_size].astype(jnp.bfloat16)
    step_pre = jnp.dot(step_low, step_weight, preferred_element_type=jnp.float32) + step_bias
    step_size = jax.nn.softplus(step_pre)
    decay_mat = -jnp.exp(decay_log)
    decay2 = decay_mat * log2e
    held_step = jnp.where(keep_flag[:, None] > 0.0, step_size, reset_step)
    drive = step_size * act_float
    coef = selected[:, rank_size:].T
    gate_act = silu_of(gate_half)
    cot_whole = lax.all_gather(cotangent, "narrow", axis=1, tiled=True)
    gated_grad = lax.dot_general(
        cot_whole, out_weight, contract_last, preferred_element_type=jnp.float32
    )
    scan_grad = gated_grad * gate_act
    ends = scan_ends(held_step, drive, scan_grad, coef, decay2)
    entry_state, tail_adjoint = carried(ends, decay_mat)
    scanned, weighted, held_sum, in_sum, read_sum, decay_grad = scan_full(
        held_step, step_size, drive, scan_grad, coef, decay2, decay_mat, entry_state, tail_adjoint
    )
    scanned = scanned + skip_gain * act_float
    gated = (scanned * gate_act).astype(jnp.bfloat16)
    out_part = jnp.dot(gated, out_weight, preferred_element_type=jnp.float32)
    out_mine = lax.psum_scatter(out_part, "narrow", scatter_dimension=1, tiled=True)
    layer_out = (tokens.astype(jnp.float32) + out_mine).astype(jnp.bfloat16)
    out_weight_grad = lax.dot_general(
        gated, cot_whole, contract_rows, preferred_element_type=jnp.float32
    )
    gate_grad = (gated_grad * scanned * silu_slope(gate_half)).astype(jnp.bfloat16)
    skip_gain_grad = jnp.sum(scan_grad * act_float, axis=0)
    step_grad = act_float * weighted + held_sum
    act_grad = step_size * weighted
    in_grad = jnp.sum(in_sum, axis=1).reshape(row_count, state_count)
    read_grad = jnp.sum(read_sum, axis=1).reshape(row_count, state_count)
    act_grad = act_grad + skip_gain * scan_grad
    pre_grad = (step_grad * jax.nn.sigmoid(step_pre)).astype(jnp.bfloat16)
    step_bias_grad = jnp.sum(pre_grad.astype(jnp.float32), axis=0)
    step_weight_grad = lax.dot_general(
        step_low, pre_grad, contract_rows, preferred_element_type=jnp.float32
    )
    low_grad = lax.dot_general(
        pre_grad, step_weight, contract_last, preferred_element_type=jnp.float32
    )
    select_grad = lax.psum(
        jnp.concatenate([low_grad, in_grad, read_grad], axis=1), "narrow"
    ).astype(jnp.bfloat16)
    act_total = act_grad + jnp.dot(select_grad, select_weight, preferred_element_type=jnp.float32)
    select_weight_grad = lax.dot_general(
        select_grad, activated, contract_rows, preferred_element_type=jnp.float32
    )
    decay_log_grad = decay_grad * decay_mat
    conv_grad = act_total * silu_slope(convolved)
    conv_bias_grad = jnp.sum(conv_grad, axis=0)
    tap_grads = []
    ext_grad = jnp.zeros(extended.shape, jnp.float32)
    for tap_index in range(tap_count):
        masked = conv_grad * masks[tap_index]
        tap_grads.append(jnp.sum(masked * extended[tap_index : tap_index + row_count], axis=0))
        ext_grad = ext_grad.at[tap_index : tap_index + row_count].add(
            conv_weight[tap_index] * masked
        )
    conv_weight_grad = jnp.stack(tap_grads)
    from_next = passed_along(ext_grad[:lag_rows], "wide", -1)
    inner_grad = jnp.concatenate(
        [ext_grad[lag_rows:row_count], ext_grad[row_count:] + from_next], axis=0
    ).astype(jnp.bfloat16)
    projected_grad = jnp.stack([inner_grad, gate_grad], axis=1)
    normed_part = jnp.einsum(
        "tce,dce->td", projected_grad, in_weight, preferred_element_type=jnp.float32
    )
    normed_grad = lax.psum(normed_part, "narrow")
    scaled = normed_grad * norm_gain
    norm_gain_grad = jnp.sum(normed_grad * whole * inverse, axis=0)
    whole_grad = inverse * scaled - whole * (inverse * inverse * inverse) * jnp.mean(
        scaled * whole, axis=1, keepdims=True
    )
    width_mine = tokens.shape[1]
    mine = lax.dynamic_slice_in_dim(
        whole_grad, lax.axis_index("narrow") * width_mine, width_mine, 1
    )
    tokens_grad = (mine + cotangent.astype(jnp.float32)).astype(jnp.bfloat16)
    in_weight_grad = jnp.einsum(
        "td,tce->dce", normed, projected_grad, preferred_element_type=jnp.float32
    )
    summed_grads = lax.psum(
        (
            in_weight_grad,
            out_weight_grad,
            conv_weight_grad,
            conv_bias_grad,
            select_weight_grad,
            step_weight_grad,
            step_bias_grad,
            decay_log_grad,
            skip_gain_grad,
            norm_gain_grad,
        ),
        "wide",
    )
    (
        in_weight_grad,
        out_weight_grad,
        conv_weight_grad,
        conv_bias_grad,
        select_weight_grad,
        step_weight_grad,
        step_bias_grad,
        decay_log_grad,
        skip_gain_grad,
        norm_gain_grad,
    ) = summed_grads
    return (
        layer_out,
        tokens_grad,
        norm_gain_grad,
        in_weight_grad,
        conv_weight_grad,
        conv_bias_grad,
        select_weight_grad,
        step_weight_grad,
        step_bias_grad,
        decay_log_grad,
        skip_gain_grad,
        out_weight_grad,
    )


def solution(mesh):
    placed = (
        P("wide", "narrow"),
        P(),
        P(None, None, "narrow"),
        P(None, "narrow"),
        P("narrow"),
        P(None, "narrow"),
        P(None, "narrow"),
        P("narrow"),
        P(None, "narrow"),
        P("narrow"),
        P("narrow", None),
        P("wide"),
        P("wide", "narrow"),
    )
    return jax.shard_map(
        local,
        mesh=mesh,
        in_specs=placed,
        out_specs=(
            P("wide", "narrow"),
            P("wide", "narrow"),
            P(),
            P(None, None, "narrow"),
            P(None, "narrow"),
            P("narrow"),
            P(None, "narrow"),
            P(None, "narrow"),
            P("narrow"),
            P(None, "narrow"),
            P("narrow"),
            P("narrow", None),
        ),
        check_vma=False,
    )
```

```python
import functools

import jax
import jax.numpy as jnp
from jax import lax
from jax.experimental import pallas as pl
from jax.experimental.pallas import tpu as pltpu
from jax.sharding import PartitionSpec as P

epsilon = 1e-05
log2e = 1.4426950408889634
reset_step = 1e30
lanes = 128
halo = 16
body_rows = 32
scan_width = 512
vmem_bytes = 56 * 1024 * 1024
f32 = jnp.float32
bf16 = jnp.bfloat16
contract_first = (((0,), (0,)), ((), ()))
contract_last = (((1,), (1,)), ((), ()))


def passed_along(array, axis, by):
    peers = lax.axis_size(axis)
    pairs = [(i, i + by) for i in range(peers) if 0 <= i + by < peers]
    return lax.ppermute(array, axis, pairs)


def swapped(array, axis, bit):
    peers = lax.axis_size(axis)
    return lax.ppermute(array, axis, [(i, i ^ bit) for i in range(peers)])


def wide_bits():
    bit, bits = 1, []
    while bit < lax.axis_size("wide"):
        bits.append(bit)
        bit *= 2
    return bits


def summed_over_wide(keep, send):
    place = lax.axis_index("wide")
    bits = wide_bits()
    piece = keep + swapped(send.astype(bf16), "wide", bits[0]).astype(f32)
    for bit in bits[1:]:
        upper = (place & bit) != 0
        half = piece.shape[0] // 2
        low, high = piece[:half], piece[half:]
        away = jnp.where(upper, low, high).astype(bf16)
        piece = jnp.where(upper, high, low) + swapped(away, "wide", bit).astype(f32)
    held = piece.astype(bf16)
    for bit in reversed(bits):
        upper = (place & bit) != 0
        other = swapped(held, "wide", bit)
        held = jnp.concatenate([jnp.where(upper, other, held), jnp.where(upper, held, other)])
    return held


def halves_of(array, axis):
    upper = lax.axis_index("wide") & 1
    half = array.shape[axis] // 2
    return (
        lax.dynamic_slice_in_dim(array, upper * half, half, axis),
        lax.dynamic_slice_in_dim(array, (1 - upper) * half, half, axis),
    )


def weight_sum(left, right):
    mine, other = halves_of(left, 1)
    send = lax.dot_general(other, right, contract_first, preferred_element_type=f32)
    keep = lax.dot_general(mine, right, contract_first, preferred_element_type=f32)
    return summed_over_wide(keep, send)


def silu_slope(values):
    logistic = jax.nn.sigmoid(values)
    return logistic * (1.0 + values * (1.0 - logistic))


def softplus(values):
    return jnp.maximum(values, 0.0) + jnp.log1p(jnp.exp(-jnp.abs(values)))


def column_spec(rows, width=scan_width):
    return pl.BlockSpec((rows, width), lambda j: (0, j))


def part_spec(part, rows, width=scan_width):
    return pl.BlockSpec((None, rows, width), lambda j: (part, 0, j))


def whole_spec(rows, width):
    return pl.BlockSpec((rows, width), lambda j: (0, 0))


def call(kernel, name, width, in_specs, out_specs, out_shape, scratch, flops, *operands):
    moved = sum(a.size * a.dtype.itemsize for a in operands)
    return pl.pallas_call(
        kernel,
        grid=(width // scan_width,),
        in_specs=in_specs,
        out_specs=out_specs,
        out_shape=out_shape,
        scratch_shapes=scratch,
        compiler_params=pltpu.CompilerParams(vmem_limit_bytes=vmem_bytes),
        cost_estimate=pl.CostEstimate(flops=flops, bytes_accessed=moved, transcendentals=0),
        name=name,
    )(*operands)


def conv_kernel(
    inner_ref,
    conv_weight_ref,
    conv_bias_ref,
    select_ref,
    mask_ref,
    convolved_ref,
    act_ref,
    selected_ref,
    inner,
):
    rows = act_ref.shape[0]
    taps = conv_weight_ref.shape[0]
    inner[...] = inner_ref[...].astype(f32)
    total = conv_bias_ref[...] + conv_weight_ref[taps - 1 :, :] * inner[halo:, :]
    for lag in range(1, taps):
        earlier = inner[pl.ds(halo - lag, rows), :] * mask_ref[:, lag : lag + 1]
        total = total + conv_weight_ref[taps - 1 - lag : taps - lag, :] * earlier
    convolved_ref[...] = total
    act = (total * jax.nn.sigmoid(total)).astype(bf16)
    act_ref[...] = act
    part = lax.dot_general(select_ref[...], act, contract_last, preferred_element_type=f32)

    @pl.when(pl.program_id(0) == 0)
    def _():
        selected_ref[...] = part

    @pl.when(pl.program_id(0) > 0)
    def _():
        selected_ref[...] += part


def convolve(projected, conv_weight, conv_bias, select_weight, masks):
    parts, extended, width = projected.shape
    rows = extended - halo
    taps = conv_weight.shape[0]
    columns = select_weight.shape[0]
    return call(
        conv_kernel,
        "convolve",
        width,
        [
            part_spec(0, extended),
            column_spec(taps),
            column_spec(1),
            column_spec(columns),
            whole_spec(rows, masks.shape[1]),
        ],
        [column_spec(rows), column_spec(rows), whole_spec(columns, rows)],
        [
            jax.ShapeDtypeStruct((rows, width), f32),
            jax.ShapeDtypeStruct((rows, width), bf16),
            jax.ShapeDtypeStruct((columns, rows), f32),
        ],
        [pltpu.VMEM((extended, scan_width), f32)],
        4_000_000_000,
        projected,
        conv_weight,
        conv_bias,
        select_weight,
        masks,
    )


def coef_columns(coef, block):
    per_tile = lanes // body_rows
    start = pl.multiple_of((block // per_tile) * lanes, lanes)
    tile = coef[:, pl.ds(start, lanes)]
    back = body_rows * lax.rem(block, per_tile)
    return pltpu.roll(tile, lax.rem(lanes - back, lanes), 1)


def ends_kernel(
    selected_ref,
    other_ref,
    step_weight_ref,
    step_bias_ref,
    act_ref,
    gate_ref,
    gated_grad_ref,
    mask_ref,
    decay_log_ref,
    step_pre_ref,
    step_ref,
    ends_ref,
    coef,
    held_step,
    drive,
    scan_grad,
):
    rows = act_ref.shape[0]
    count = decay_log_ref.shape[0]
    rank = step_weight_ref.shape[0]
    decay2 = -jnp.exp(decay_log_ref[...]) * log2e
    selected = selected_ref[...] + other_ref[...]
    coef[...] = selected[rank:, :]
    step_low = selected[:rank, :].astype(bf16)
    step_pre = step_bias_ref[...] + lax.dot_general(
        step_low, step_weight_ref[...], contract_first, preferred_element_type=f32
    )
    step_pre_ref[...] = step_pre
    step = softplus(step_pre)
    step_ref[...] = step
    held_step[...] = jnp.where(mask_ref[:, 1:2] > 0.0, step, reset_step)
    drive[...] = step * act_ref[...].astype(f32)
    gate = gate_ref[...].astype(f32)
    scan_grad[...] = gated_grad_ref[...] * (gate * jax.nn.sigmoid(gate))
    zero = jnp.zeros(decay2.shape, f32)

    def body(block, carried):
        state, product, adjoint = carried
        columns = coef_columns(coef, block)
        for i in range(body_rows):
            row = pl.ds(block * body_rows + i, 1)
            factor = jnp.exp2(held_step[row, :] * decay2)
            state = factor * state + columns[:count, i : i + 1] * drive[row, :]
            product = factor * product
            adjoint = adjoint + product * (columns[count:, i : i + 1] * scan_grad[row, :])
        return state, product, adjoint

    state, product, adjoint = lax.fori_loop(0, rows // body_rows, body, (zero, zero + 1.0, zero))
    ends_ref[:count, :] = state
    ends_ref[count : 2 * count, :] = adjoint
    total = jnp.sum(held_step[...], axis=0, keepdims=True)
    ends_ref[2 * count :, :] = jnp.broadcast_to(total, (8, total.shape[1]))


def scan_ends(
    selected, other, step_weight, step_bias, act, projected, gated_grad, masks, decay_log
):
    rows, width = act.shape
    count = decay_log.shape[0]
    columns = selected.shape[0]
    rank = step_weight.shape[0]
    return call(
        ends_kernel,
        "scan_ends",
        width,
        [
            whole_spec(columns, rows),
            whole_spec(columns, rows),
            column_spec(rank),
            column_spec(1),
            column_spec(rows),
            pl.BlockSpec((None, rows, scan_width), lambda j: (0, 0, j)),
            column_spec(rows),
            whole_spec(rows, masks.shape[1]),
            column_spec(count),
        ],
        [column_spec(rows), column_spec(rows), column_spec(2 * count + 8)],
        [
            jax.ShapeDtypeStruct((rows, width), f32),
            jax.ShapeDtypeStruct((rows, width), f32),
            jax.ShapeDtypeStruct((2 * count + 8, width), f32),
        ],
        [pltpu.VMEM((2 * count, rows), f32)] + [pltpu.VMEM((rows, scan_width), f32)] * 3,
        10_000_000_000,
        selected,
        other,
        step_weight,
        step_bias,
        act,
        projected,
        gated_grad,
        masks,
        decay_log,
    )


def lane_tiles(values):
    return [values[:, k : k + lanes] for k in range(0, values.shape[1], lanes)]


def tree_sum(parts):
    while len(parts) > 1:
        odd = parts[len(parts) // 2 * 2 :]
        parts = [a + b for a, b in zip(parts[0::2], parts[1::2])] + odd
    return parts[0]


def keep_halves(scratch, i, values):
    for k, tile in enumerate(lane_tiles(values)):
        at = (k * body_rows + i) * 8
        scratch[at : at + 8, :] = tile[:8] + tile[8:]


def put_state_sums(scratch, out_ref, block):
    for group in range(body_rows // 8):
        row = pl.ds(pl.multiple_of(block * body_rows + group * 8, 8), 8)
        for k in range(out_ref.shape[1] // lanes):
            at = (k * body_rows + group * 8) * 8
            total = tree_sum([scratch[pl.ds(at + n, 8, stride=8), :] for n in range(8)])
            out_ref[row, k * lanes : (k + 1) * lanes] = total


def lane_sums(values):
    ones = jnp.ones((8, lanes), bf16)
    high = values.astype(bf16)
    low = (values - high.astype(f32)).astype(bf16)
    total = lax.dot_general(ones, high, contract_last, preferred_element_type=f32)
    total += lax.dot_general(ones, low, contract_last, preferred_element_type=f32)
    return total[:1, :]


def scan_kernel(
    selected_ref,
    other_ref,
    step_pre_ref,
    step_ref,
    act_ref,
    gate_ref,
    gated_grad_ref,
    mask_ref,
    decay_log_ref,
    entry_ref,
    tail_ref,
    skip_ref,
    step_weight_ref,
    gated_ref,
    gate_grad_ref,
    act_grad_ref,
    select_grad_ref,
    small_ref,
    coef,
    held_step,
    drive,
    scan_grad,
    scanned,
    weighted,
    states,
    factors,
    halves,
    more_halves,
    in_sum,
    read_sum,
):
    rows = step_ref.shape[0]
    count = decay_log_ref.shape[0]
    rank = step_weight_ref.shape[0]
    blocks = rows // body_rows
    first = pl.program_id(0) == 0
    last = pl.program_id(0) == pl.num_programs(0) - 1
    decay = -jnp.exp(decay_log_ref[...])
    decay2 = decay * log2e
    selected = selected_ref[...] + other_ref[...]
    coef[...] = selected[rank:, :]
    step_low = selected[:rank, :].astype(bf16)
    step = step_ref[...]
    act = act_ref[...].astype(f32)
    held_step[...] = jnp.where(mask_ref[:, 1:2] > 0.0, step, reset_step)
    drive[...] = step * act
    states[:count, :] = entry_ref[...]

    @pl.when(first)
    def _():
        in_sum[...] = jnp.zeros(in_sum.shape, f32)
        read_sum[...] = jnp.zeros(read_sum.shape, f32)
        select_grad_ref[...] = jnp.zeros(select_grad_ref.shape, f32)

    def at_token(t):
        return pl.ds(pl.multiple_of(t * count, count), count)

    def forward(block, state):
        columns = coef_columns(coef, block)
        for i in range(body_rows):
            t = block * body_rows + i
            row = pl.ds(t, 1)
            factor = jnp.exp2(held_step[row, :] * decay2)
            state = factor * state + columns[:count, i : i + 1] * drive[row, :]
            factors[at_token(t), :] = factor
            states[at_token(t + 1), :] = state
            keep_halves(halves, i, columns[count:, i : i + 1] * state)
        put_state_sums(halves, scanned, block)
        return state

    lax.fori_loop(0, blocks, forward, entry_ref[...])

    gate = gate_ref[...].astype(f32)
    logistic = jax.nn.sigmoid(gate)
    gate_act = gate * logistic
    gated_grad = gated_grad_ref[...]
    grads = gated_grad * gate_act
    scan_grad[...] = grads
    total = scanned[...] + skip_ref[...] * act
    gated_ref[...] = (total * gate_act).astype(bf16)
    slope = logistic * (1.0 + gate * (1.0 - logistic))
    gate_grad_ref[...] = (gated_grad * total * slope).astype(bf16)
    small_ref[rank + count : rank + count + 1, :] = jnp.sum(grads * act, axis=0, keepdims=True)

    def backward(k, carried):
        adjoint, decay_grad = carried
        block = blocks - 1 - k
        columns = coef_columns(coef, block)
        for i in range(body_rows - 1, -1, -1):
            t = block * body_rows + i
            row = pl.ds(t, 1)
            grad = scan_grad[row, :]
            summed = columns[count:, i : i + 1] * grad + adjoint
            read_sum[at_token(t), :] += tree_sum(lane_tiles(grad * states[at_token(t + 1), :]))
            in_sum[at_token(t), :] += tree_sum(lane_tiles(summed * drive[row, :]))
            keep_halves(halves, i, summed * columns[:count, i : i + 1])
            adjoint = factors[at_token(t), :] * summed
            held = adjoint * states[at_token(t), :]
            decay_grad = decay_grad + held * step_ref[row, :]
            keep_halves(more_halves, i, held * decay)
        put_state_sums(halves, weighted, block)
        put_state_sums(more_halves, scanned, block)
        return adjoint, decay_grad

    ignored, decay_grad = lax.fori_loop(
        0, blocks, backward, (tail_ref[...], jnp.zeros(decay.shape, f32))
    )
    act_grad_ref[...] = step * weighted[...] + skip_ref[...] * scan_grad[...]
    step_grad = act * weighted[...] + scanned[...]
    pre_grad = (step_grad * jax.nn.sigmoid(step_pre_ref[...])).astype(bf16)
    small_ref[:rank, :] = jnp.dot(step_low, pre_grad, preferred_element_type=f32)
    small_ref[rank : rank + count, :] = decay_grad * decay
    bias_grad = jnp.sum(pre_grad.astype(f32), axis=0, keepdims=True)
    small_ref[rank + count + 1 : rank + count + 2, :] = bias_grad
    spare = small_ref.shape[0] - (rank + count + 2)
    small_ref[rank + count + 2 :, :] = jnp.zeros((spare, small_ref.shape[1]), f32)
    select_grad_ref[:rank, :] += lax.dot_general(
        step_weight_ref[...], pre_grad, contract_last, preferred_element_type=f32
    )

    @pl.when(last)
    def _():
        for n in range(count):
            at = pl.ds(n, rows, stride=count)
            select_grad_ref[rank + n : rank + n + 1, :] = lane_sums(in_sum[at, :])
            select_grad_ref[rank + count + n : rank + count + n + 1, :] = lane_sums(read_sum[at, :])


def scan_full(
    selected,
    other,
    step_pre,
    step,
    act,
    projected,
    gated_grad,
    masks,
    decay_log,
    entry,
    tail,
    skip_gain,
    step_weight,
):
    rows, width = step.shape
    count = decay_log.shape[0]
    columns = selected.shape[0]
    rank = step_weight.shape[0]
    half_rows = 8 * body_rows * (scan_width // lanes)
    small = rank + count + 16
    return call(
        scan_kernel,
        "scan_full",
        width,
        [
            whole_spec(columns, rows),
            whole_spec(columns, rows),
            column_spec(rows),
            column_spec(rows),
            column_spec(rows),
            pl.BlockSpec((None, rows, scan_width), lambda j: (0, 0, j)),
            column_spec(rows),
            whole_spec(rows, masks.shape[1]),
            column_spec(count),
            column_spec(count),
            column_spec(count),
            column_spec(1),
            column_spec(rank),
        ],
        [column_spec(rows)] * 3 + [whole_spec(columns, rows), column_spec(small)],
        [
            jax.ShapeDtypeStruct((rows, width), bf16),
            jax.ShapeDtypeStruct((rows, width), bf16),
            jax.ShapeDtypeStruct((rows, width), f32),
            jax.ShapeDtypeStruct((columns, rows), f32),
            jax.ShapeDtypeStruct((small, width), f32),
        ],
        [pltpu.VMEM((2 * count, rows), f32)]
        + [pltpu.VMEM((rows, scan_width), f32)] * 5
        + [
            pltpu.VMEM(((rows + 1) * count, scan_width), f32),
            pltpu.VMEM((rows * count, scan_width), f32),
            pltpu.VMEM((half_rows, lanes), f32),
            pltpu.VMEM((half_rows, lanes), f32),
            pltpu.VMEM((rows * count, lanes), f32),
            pltpu.VMEM((rows * count, lanes), f32),
        ],
        24_000_000_000,
        selected,
        other,
        step_pre,
        step,
        act,
        projected,
        gated_grad,
        masks,
        decay_log,
        entry,
        tail,
        skip_gain,
        step_weight,
    )


def conv_grad_kernel(
    select_grad_ref,
    other_ref,
    select_ref,
    act_grad_ref,
    convolved_ref,
    act_ref,
    inner_ref,
    conv_weight_ref,
    mask_ref,
    inner_grad_ref,
    edge_ref,
    small_ref,
    inner,
    shifted,
):
    rows = act_ref.shape[0]
    taps = conv_weight_ref.shape[0]
    columns = select_ref.shape[0]
    select_grad = (select_grad_ref[...] + other_ref[...]).astype(bf16)
    total = act_grad_ref[...] + lax.dot_general(
        select_grad, select_ref[...], contract_first, preferred_element_type=f32
    )
    conv_grad = total * silu_slope(convolved_ref[...])
    small_ref[:columns, :] = jnp.dot(select_grad, act_ref[...], preferred_element_type=f32)
    inner[...] = inner_ref[...].astype(f32)
    edges = jnp.zeros((8, conv_grad.shape[1]), f32)
    shifted[:8, :] = edges
    shifted[rows + 8 :, :] = edges
    out = conv_weight_ref[taps - 1 :, :] * conv_grad
    before = edges
    small_ref[columns + taps - 1 : columns + taps, :] = jnp.sum(
        conv_grad * inner[halo:, :], axis=0, keepdims=True
    )
    for lag in range(1, taps):
        masked = conv_grad * mask_ref[:, lag : lag + 1]
        at = taps - 1 - lag
        small_ref[columns + at : columns + at + 1, :] = jnp.sum(
            masked * inner[pl.ds(halo - lag, rows), :], axis=0, keepdims=True
        )
        shifted[8 : rows + 8, :] = masked
        weight = conv_weight_ref[at : at + 1, :]
        out = out + weight * shifted[pl.ds(8 + lag, rows), :]
        before = before + weight * shifted[pl.ds(lag, 8), :]
    small_ref[columns + taps : columns + taps + 1, :] = jnp.sum(conv_grad, axis=0, keepdims=True)
    spare = small_ref.shape[0] - (columns + taps + 1)
    small_ref[columns + taps + 1 :, :] = jnp.zeros((spare, small_ref.shape[1]), f32)
    inner_grad_ref[...] = out.astype(bf16)
    edge_ref[:8, :] = before
    edge_ref[8:, :] = out[rows - 8 :, :]


def convolve_grad(
    select_grad, other, select_weight, act_grad, convolved, act, projected, conv_weight, masks
):
    rows, width = act.shape
    extended = rows + halo
    columns = select_weight.shape[0]
    taps = conv_weight.shape[0]
    small = columns + 16
    return call(
        conv_grad_kernel,
        "convolve_grad",
        width,
        [
            whole_spec(columns, rows),
            whole_spec(columns, rows),
            column_spec(columns),
            column_spec(rows),
            column_spec(rows),
            column_spec(rows),
            part_spec(0, extended),
            column_spec(taps),
            whole_spec(rows, masks.shape[1]),
        ],
        [column_spec(rows), column_spec(16), column_spec(small)],
        [
            jax.ShapeDtypeStruct((rows, width), bf16),
            jax.ShapeDtypeStruct((16, width), f32),
            jax.ShapeDtypeStruct((small, width), f32),
        ],
        [pltpu.VMEM((extended, scan_width), f32), pltpu.VMEM((rows + 16, scan_width), f32)],
        6_000_000_000,
        select_grad,
        other,
        select_weight,
        act_grad,
        convolved,
        act,
        projected,
        conv_weight,
        masks,
    )


def join_kernel(inner_ref, gate_ref, out_ref):
    out_ref[:, 0, :] = inner_ref[...].astype(f32)
    out_ref[:, 1, :] = gate_ref[...].astype(f32)


def joined(inner, gate):
    depth, width = inner.shape
    rows = 256
    spec = pl.BlockSpec((rows, width), lambda j: (j, 0))
    return pl.pallas_call(
        join_kernel,
        grid=(depth // rows,),
        in_specs=[spec, spec],
        out_specs=pl.BlockSpec((rows, 2, width), lambda j: (j, 0, 0)),
        out_shape=jax.ShapeDtypeStruct((depth, 2, width), f32),
        compiler_params=pltpu.CompilerParams(vmem_limit_bytes=vmem_bytes),
        name="joined",
    )(inner, gate)


def carried(ends, decay):
    count = decay.shape[0]
    place = lax.axis_index("wide")

    def split(packed):
        return packed[:count], packed[count : 2 * count], packed[2 * count : 2 * count + 1]

    def through(total):
        return jnp.exp(decay * total)

    zero = jnp.zeros(decay.shape, f32)
    none = jnp.zeros((1, decay.shape[1]), f32)
    before, before_steps, after, after_steps = zero, none, zero, none
    packed = ends
    for bit in (1, 2):
        second = (place & bit) != 0
        own = split(packed)
        other = split(swapped(packed, "wide", bit))
        early = [jnp.where(second, b, a) for a, b in zip(own, other)]
        late = [jnp.where(second, a, b) for a, b in zip(own, other)]
        before = before + jnp.where(second, through(before_steps) * other[0], 0.0)
        before_steps = before_steps + jnp.where(second, other[2], 0.0)
        after = after + jnp.where(second, 0.0, through(after_steps) * other[1])
        after_steps = after_steps + jnp.where(second, 0.0, other[2])
        state = late[0] + through(late[2]) * early[0]
        adjoint = early[1] + through(early[2]) * late[1]
        packed = jnp.concatenate(
            [state, adjoint, jnp.broadcast_to(early[2] + late[2], (8, decay.shape[1]))]
        )
    from_before = passed_along(packed[:count], "wide", 4)
    from_after = passed_along(packed[count : 2 * count], "wide", -4)
    return (
        before + through(before_steps) * from_before,
        after + through(after_steps) * from_after,
    )


def local(
    tokens,
    norm_gain,
    in_weight,
    conv_weight,
    conv_bias,
    select_weight,
    step_weight,
    step_bias,
    decay_log,
    skip_gain,
    out_weight,
    segment_ids,
    cotangent,
):
    rows, features = tokens.shape
    taps = conv_weight.shape[0]
    columns = select_weight.shape[0]
    rank = step_weight.shape[0]
    count = decay_log.shape[0]
    right_half = lax.axis_index("narrow") == 1

    def both_halves(own, other):
        return jnp.concatenate(
            [jnp.where(right_half, other, own), jnp.where(right_half, own, other)], axis=1
        )

    last_ids = segment_ids[rows - halo :]
    same_as_last = (last_ids == segment_ids[rows - 1 :])[:, None]
    edge_rows = jnp.where(same_as_last, tokens[rows - halo :], jnp.zeros((), tokens.dtype))
    before_own = passed_along(edge_rows, "wide", 1)
    sent = jnp.concatenate([before_own, tokens])
    whole_ext = both_halves(sent, swapped(sent, "narrow", 1)).astype(f32)
    cot_whole = both_halves(cotangent, swapped(cotangent, "narrow", 1))

    padded_ids = jnp.concatenate([jnp.broadcast_to(segment_ids[:1], (taps - 1,)), segment_ids])
    masks = jnp.stack(
        [
            (padded_ids[taps - 1 - lag : taps - 1 - lag + rows] == segment_ids).astype(f32)
            for lag in range(taps)
        ]
        + [jnp.zeros((rows,), f32)] * (8 - taps),
        axis=1,
    )

    inverse_ext = lax.rsqrt(jnp.mean(whole_ext * whole_ext, axis=1, keepdims=True) + epsilon)
    normed_ext = (whole_ext * inverse_ext * norm_gain).astype(bf16)
    projected = jnp.einsum(
        "td,dce->cte", normed_ext, in_weight, preferred_element_type=f32
    ).astype(bf16)
    gate_half = projected[1:, halo:]
    convolved, act, selected = convolve(
        projected, conv_weight, conv_bias[None], select_weight, masks
    )
    other_selected = swapped(selected, "narrow", 1)
    gated_grad = lax.dot_general(
        cot_whole, out_weight, contract_last, preferred_element_type=f32
    )
    step_pre, step, ends = scan_ends(
        selected,
        other_selected,
        step_weight,
        step_bias[None],
        act,
        gate_half,
        gated_grad,
        masks,
        decay_log,
    )
    entry, tail = carried(ends, -jnp.exp(decay_log))
    gated, gate_grad, act_grad, select_grad, scan_small = scan_full(
        selected,
        other_selected,
        step_pre,
        step,
        act,
        gate_half,
        gated_grad,
        masks,
        decay_log,
        entry,
        tail,
        skip_gain[None],
        step_weight,
    )
    other_select_grad = swapped(select_grad, "narrow", 1)
    out_weight_grad = weight_sum(gated, cot_whole)
    normed = normed_ext[halo:]
    gate_weight_grad = weight_sum(normed, gate_grad)

    def narrow_halves(array):
        low, high = array[:, :features], array[:, features:]
        return jnp.where(right_half, high, low), jnp.where(right_half, low, high)

    out_part = jnp.dot(gated, out_weight, preferred_element_type=f32)
    out_mine, out_other = narrow_halves(out_part)
    out_sum = out_mine + swapped(out_other, "narrow", 1)
    layer_out = (tokens.astype(f32) + out_sum).astype(bf16)

    inner_main, edges, conv_small = convolve_grad(
        select_grad,
        other_select_grad,
        select_weight,
        act_grad,
        convolved,
        act,
        projected,
        conv_weight,
        masks,
    )
    from_next = passed_along(edges[:8], "wide", -1)
    last_rows = edges[8:] + jnp.where(same_as_last[halo - 8 :], from_next, 0.0)
    inner_grad = jnp.concatenate([inner_main[: rows - 8], last_rows.astype(bf16)])
    normed_part = jnp.einsum(
        "cte,dce->td", jnp.stack([inner_grad, gate_grad]), in_weight, preferred_element_type=f32
    )
    inner_weight_grad = weight_sum(normed, inner_grad)

    whole = whole_ext[halo:]
    inverse = inverse_ext[halo:]
    gain_part = jnp.sum(normed_part * whole * inverse, axis=0, keepdims=True)
    row_part = jnp.sum(normed_part * norm_gain * whole, axis=1, keepdims=True)
    normed_mine, normed_other = narrow_halves(normed_part)
    row_sum = row_part + swapped(row_part, "narrow", 1)
    normed_sum = normed_mine + swapped(normed_other, "narrow", 1)
    gain_mine = jnp.where(right_half, norm_gain[features:], norm_gain[:features])
    whole_grad = inverse * (gain_mine * normed_sum) - tokens.astype(f32) * (
        inverse * inverse * inverse
    ) * (row_sum / (2 * features))
    tokens_grad = (whole_grad + cotangent.astype(f32)).astype(bf16)

    gain_sum = gain_part + swapped(gain_part, "narrow", 1)
    spare = -(scan_small.shape[0] + conv_small.shape[0] + 1) % 256
    small = jnp.concatenate(
        [scan_small, conv_small, gain_sum, jnp.zeros((spare, gain_sum.shape[1]), f32)]
    )
    small_sum = summed_over_wide(*halves_of(small, 0)).astype(f32)
    scan_sum = small_sum[: scan_small.shape[0]]
    conv_sum = small_sum[scan_small.shape[0] : scan_small.shape[0] + conv_small.shape[0]]
    norm_gain_grad = small_sum[scan_small.shape[0] + conv_small.shape[0]]
    return (
        layer_out,
        tokens_grad,
        norm_gain_grad,
        joined(inner_weight_grad, gate_weight_grad),
        conv_sum[columns : columns + taps],
        conv_sum[columns + taps],
        conv_sum[:columns],
        scan_sum[:rank],
        scan_sum[rank + count + 1],
        scan_sum[rank : rank + count],
        scan_sum[rank + count],
        out_weight_grad.astype(f32),
    )


def solution(mesh):
    placed = (
        P("wide", "narrow"),
        P(),
        P(None, None, "narrow"),
        P(None, "narrow"),
        P("narrow"),
        P(None, "narrow"),
        P(None, "narrow"),
        P("narrow"),
        P(None, "narrow"),
        P("narrow"),
        P("narrow", None),
        P("wide"),
        P("wide", "narrow"),
    )
    return jax.shard_map(
        local,
        mesh=mesh,
        in_specs=placed,
        out_specs=(
            P("wide", "narrow"),
            P("wide", "narrow"),
            P(),
            P(None, None, "narrow"),
            P(None, "narrow"),
            P("narrow"),
            P(None, "narrow"),
            P(None, "narrow"),
            P("narrow"),
            P(None, "narrow"),
            P("narrow"),
            P("narrow", None),
        ),
        check_vma=False,
    )
```

```python
import functools

import jax
import jax.numpy as jnp
from jax import lax
from jax.experimental import pallas as pl
from jax.experimental.pallas import tpu as pltpu
from jax.sharding import PartitionSpec as P

epsilon = 1e-05
log2e = 1.4426950408889634
reset_step = 1e30
lanes = 128
halo = 16
body_rows = 32
scan_width = 512
vmem_bytes = 56 * 1024 * 1024
f32 = jnp.float32
bf16 = jnp.bfloat16
contract_first = (((0,), (0,)), ((), ()))
contract_last = (((1,), (1,)), ((), ()))


def passed_along(array, axis, by):
    peers = lax.axis_size(axis)
    pairs = [(i, i + by) for i in range(peers) if 0 <= i + by < peers]
    return lax.ppermute(array, axis, pairs)


def swapped(array, axis, bit):
    peers = lax.axis_size(axis)
    return lax.ppermute(array, axis, [(i, i ^ bit) for i in range(peers)])


def wide_bits():
    bit, bits = 1, []
    while bit < lax.axis_size("wide"):
        bits.append(bit)
        bit *= 2
    return bits


def to_next_both(array):
    count, sides = lax.axis_size("wide"), lax.axis_size("narrow")
    pairs = [
        (i * sides + k, (i + 1) * sides + (sides - 1 - k))
        for i in range(count - 1)
        for k in range(sides)
    ]
    return passed_along(array, "wide", 1), lax.ppermute(array, ("wide", "narrow"), pairs)


def is_upper(bit):
    return (lax.axis_index("wide") & bit) != 0


def scatter_step(piece, bit):
    half = piece.shape[0] // 2
    low, high = piece[:half], piece[half:]
    away = jnp.where(is_upper(bit), low, high).astype(bf16)
    return jnp.where(is_upper(bit), high, low) + swapped(away, "wide", bit).astype(f32)


def gather_step(held, bit):
    other = swapped(held, "wide", bit)
    upper = is_upper(bit)
    return jnp.concatenate([jnp.where(upper, other, held), jnp.where(upper, held, other)])


def scattered(piece, bits):
    for bit in bits:
        piece = scatter_step(piece, bit)
    return piece.astype(bf16)


def gathered(held, bits):
    for bit in reversed(bits):
        held = gather_step(held, bit)
    return held


def halves_of(array, axis):
    upper = lax.axis_index("wide") & 1
    half = array.shape[axis] // 2
    return (
        lax.dynamic_slice_in_dim(array, upper * half, half, axis),
        lax.dynamic_slice_in_dim(array, (1 - upper) * half, half, axis),
    )


def packed_rows(product):
    half = product.shape[0] // 2
    return jnp.concatenate([product[:half], product[half:]], axis=1)


def times(left, right):
    return lax.dot_general(left, right, contract_first, preferred_element_type=f32)


def first_step(parts):
    mine, send = [], []
    for left, right, pack in parts:
        own, other = halves_of(left, 1)
        keep_product, send_product = times(own, right), times(other, right)
        mine.append(packed_rows(keep_product) if pack else keep_product)
        send.append(packed_rows(send_product) if pack else send_product)
    away = jnp.concatenate(send).astype(bf16)
    return jnp.concatenate(mine) + swapped(away, "wide", 1).astype(f32)


def silu_slope(values):
    logistic = jax.nn.sigmoid(values)
    return logistic * (1.0 + values * (1.0 - logistic))


def softplus(values):
    return jnp.maximum(values, 0.0) + jnp.log1p(jnp.exp(-jnp.abs(values)))


def column_spec(rows, start=0):
    return pl.BlockSpec((rows, scan_width), lambda j: (0, start + j))


def part_spec(part, rows, start=0):
    return pl.BlockSpec((None, rows, scan_width), lambda j: (part, 0, start + j))


def whole_spec(rows, width):
    return pl.BlockSpec((rows, width), lambda j: (0, 0))


def call(kernel, name, width, in_specs, out_specs, out_shape, scratch, flops, *operands):
    moved = sum(a.size * a.dtype.itemsize for a in operands)
    return pl.pallas_call(
        kernel,
        grid=(width // scan_width,),
        in_specs=in_specs,
        out_specs=out_specs,
        out_shape=out_shape,
        scratch_shapes=scratch,
        compiler_params=pltpu.CompilerParams(vmem_limit_bytes=vmem_bytes),
        cost_estimate=pl.CostEstimate(flops=flops, bytes_accessed=moved, transcendentals=0),
        name=name,
    )(*operands)


def conv_kernel(
    inner_ref,
    conv_weight_ref,
    conv_bias_ref,
    select_ref,
    mask_ref,
    convolved_ref,
    act_ref,
    selected_ref,
    inner,
):
    rows = act_ref.shape[0]
    taps = conv_weight_ref.shape[0]
    inner[:halo, :] = inner_ref[rows:, :].astype(f32)
    inner[halo:, :] = inner_ref[:rows, :].astype(f32)
    total = conv_bias_ref[...] + conv_weight_ref[taps - 1 :, :] * inner[halo:, :]
    for lag in range(1, taps):
        earlier = inner[pl.ds(halo - lag, rows), :] * mask_ref[:, lag : lag + 1]
        total = total + conv_weight_ref[taps - 1 - lag : taps - lag, :] * earlier
    convolved_ref[...] = total
    act = (total * jax.nn.sigmoid(total)).astype(bf16)
    act_ref[...] = act
    part = lax.dot_general(select_ref[...], act, contract_last, preferred_element_type=f32)

    @pl.when(pl.program_id(0) == 0)
    def _():
        selected_ref[...] = part

    @pl.when(pl.program_id(0) > 0)
    def _():
        selected_ref[...] += part


def convolve(projected, conv_weight, conv_bias, select_weight, masks):
    parts, extended, width = projected.shape
    rows = extended - halo
    taps = conv_weight.shape[0]
    columns = select_weight.shape[0]
    return call(
        conv_kernel,
        "convolve",
        width,
        [
            part_spec(0, extended),
            column_spec(taps),
            column_spec(1),
            column_spec(columns),
            whole_spec(rows, masks.shape[1]),
        ],
        [column_spec(rows), column_spec(rows), whole_spec(columns, rows)],
        [
            jax.ShapeDtypeStruct((rows, width), f32),
            jax.ShapeDtypeStruct((rows, width), bf16),
            jax.ShapeDtypeStruct((columns, rows), f32),
        ],
        [pltpu.VMEM((extended, scan_width), f32)],
        4_000_000_000,
        projected,
        conv_weight,
        conv_bias,
        select_weight,
        masks,
    )


def coef_columns(coef, block):
    per_tile = lanes // body_rows
    start = pl.multiple_of((block // per_tile) * lanes, lanes)
    tile = coef[:, pl.ds(start, lanes)]
    back = body_rows * lax.rem(block, per_tile)
    return pltpu.roll(tile, lax.rem(lanes - back, lanes), 1)


def ends_kernel(
    selected_ref,
    other_ref,
    step_weight_ref,
    step_bias_ref,
    act_ref,
    gate_ref,
    gated_grad_ref,
    mask_ref,
    decay_log_ref,
    step_pre_ref,
    step_ref,
    ends_ref,
    coef,
    held_step,
    drive,
    scan_grad,
):
    rows = act_ref.shape[0]
    count = decay_log_ref.shape[0]
    rank = step_weight_ref.shape[0]
    decay2 = -jnp.exp(decay_log_ref[...]) * log2e
    selected = selected_ref[...] + other_ref[...]
    coef[...] = selected[rank:, :]
    step_low = selected[:rank, :].astype(bf16)
    step_pre = step_bias_ref[...] + lax.dot_general(
        step_low, step_weight_ref[...], contract_first, preferred_element_type=f32
    )
    step_pre_ref[...] = step_pre
    step = softplus(step_pre)
    step_ref[...] = step
    held_step[...] = jnp.where(mask_ref[:, 1:2] > 0.0, step, reset_step)
    drive[...] = step * act_ref[...].astype(f32)
    gate = gate_ref[...].astype(f32)
    scan_grad[...] = gated_grad_ref[...] * (gate * jax.nn.sigmoid(gate))
    zero = jnp.zeros(decay2.shape, f32)

    def body(block, carried):
        state, product, adjoint = carried
        columns = coef_columns(coef, block)
        for i in range(body_rows):
            row = pl.ds(block * body_rows + i, 1)
            factor = jnp.exp2(held_step[row, :] * decay2)
            state = factor * state + columns[:count, i : i + 1] * drive[row, :]
            product = factor * product
            adjoint = adjoint + product * (columns[count:, i : i + 1] * scan_grad[row, :])
        return state, product, adjoint

    state, product, adjoint = lax.fori_loop(0, rows // body_rows, body, (zero, zero + 1.0, zero))
    ends_ref[:count, :] = state
    ends_ref[count : 2 * count, :] = adjoint
    total = jnp.sum(held_step[...], axis=0, keepdims=True)
    ends_ref[2 * count :, :] = jnp.broadcast_to(total, (8, total.shape[1]))


def scan_ends(
    part, selected, other, step_weight, step_bias, act, projected, gated_grad, masks, decay_log
):
    rows, width = act.shape[0], scan_width
    count = decay_log.shape[0]
    columns = selected.shape[0]
    rank = step_weight.shape[0]
    return call(
        ends_kernel,
        "scan_ends",
        width,
        [
            whole_spec(columns, rows),
            whole_spec(columns, rows),
            column_spec(rank, part),
            column_spec(1, part),
            column_spec(rows, part),
            part_spec(1, rows, part),
            column_spec(rows, part),
            whole_spec(rows, masks.shape[1]),
            column_spec(count, part),
        ],
        [column_spec(rows), column_spec(rows), column_spec(2 * count + 8)],
        [
            jax.ShapeDtypeStruct((rows, width), f32),
            jax.ShapeDtypeStruct((rows, width), f32),
            jax.ShapeDtypeStruct((2 * count + 8, width), f32),
        ],
        [pltpu.VMEM((2 * count, rows), f32)] + [pltpu.VMEM((rows, scan_width), f32)] * 3,
        5_000_000_000,
        selected,
        other,
        step_weight,
        step_bias,
        act,
        projected,
        gated_grad,
        masks,
        decay_log,
    )


def lane_tiles(values):
    return [values[:, k : k + lanes] for k in range(0, values.shape[1], lanes)]


def tree_sum(parts):
    while len(parts) > 1:
        odd = parts[len(parts) // 2 * 2 :]
        parts = [a + b for a, b in zip(parts[0::2], parts[1::2])] + odd
    return parts[0]


def keep_halves(scratch, i, values):
    for k, tile in enumerate(lane_tiles(values)):
        at = (k * body_rows + i) * 8
        scratch[at : at + 8, :] = tile[:8] + tile[8:]


def put_state_sums(scratch, out_ref, block):
    for group in range(body_rows // 8):
        row = pl.ds(pl.multiple_of(block * body_rows + group * 8, 8), 8)
        for k in range(out_ref.shape[1] // lanes):
            at = (k * body_rows + group * 8) * 8
            total = tree_sum([scratch[pl.ds(at + n, 8, stride=8), :] for n in range(8)])
            out_ref[row, k * lanes : (k + 1) * lanes] = total


def lane_sums(values):
    ones = jnp.ones((8, lanes), bf16)
    high = values.astype(bf16)
    low = (values - high.astype(f32)).astype(bf16)
    total = lax.dot_general(ones, high, contract_last, preferred_element_type=f32)
    total += lax.dot_general(ones, low, contract_last, preferred_element_type=f32)
    return total[:1, :]


def scan_kernel(
    selected_ref,
    other_ref,
    step_pre_ref,
    step_ref,
    act_ref,
    gate_ref,
    gated_grad_ref,
    mask_ref,
    decay_log_ref,
    entry_ref,
    tail_ref,
    skip_ref,
    step_weight_ref,
    before_ref,
    after_ref,
    gated_ref,
    gate_grad_ref,
    act_grad_ref,
    select_grad_ref,
    small_ref,
    coef,
    held_step,
    drive,
    scan_grad,
    scanned,
    weighted,
    states,
    factors,
    halves,
    more_halves,
    in_sum,
    read_sum,
):
    rows = step_ref.shape[0]
    count = decay_log_ref.shape[0]
    rank = step_weight_ref.shape[0]
    blocks = rows // body_rows
    decay = -jnp.exp(decay_log_ref[...])
    decay2 = decay * log2e
    selected = selected_ref[...] + other_ref[...]
    coef[...] = selected[rank:, :]
    step_low = selected[:rank, :].astype(bf16)
    step = step_ref[...]
    act = act_ref[...].astype(f32)
    held_step[...] = jnp.where(mask_ref[:, 1:2] > 0.0, step, reset_step)
    drive[...] = step * act
    states[:count, :] = entry_ref[...]

    def at_token(t):
        return pl.ds(pl.multiple_of(t * count, count), count)

    def forward(block, state):
        columns = coef_columns(coef, block)
        for i in range(body_rows):
            t = block * body_rows + i
            row = pl.ds(t, 1)
            factor = jnp.exp2(held_step[row, :] * decay2)
            state = factor * state + columns[:count, i : i + 1] * drive[row, :]
            factors[at_token(t), :] = factor
            states[at_token(t + 1), :] = state
            keep_halves(halves, i, columns[count:, i : i + 1] * state)
        put_state_sums(halves, scanned, block)
        return state

    lax.fori_loop(0, blocks, forward, entry_ref[...])

    gate = gate_ref[...].astype(f32)
    logistic = jax.nn.sigmoid(gate)
    gate_act = gate * logistic
    gated_grad = gated_grad_ref[...]
    grads = gated_grad * gate_act
    scan_grad[...] = grads
    total = scanned[...] + skip_ref[...] * act
    gated_ref[...] = (total * gate_act).astype(bf16)
    slope = logistic * (1.0 + gate * (1.0 - logistic))
    gate_grad_ref[...] = (gated_grad * total * slope).astype(bf16)
    small_ref[rank + count : rank + count + 1, :] = jnp.sum(grads * act, axis=0, keepdims=True)

    def backward(k, carried):
        adjoint, decay_grad = carried
        block = blocks - 1 - k
        columns = coef_columns(coef, block)
        for i in range(body_rows - 1, -1, -1):
            t = block * body_rows + i
            row = pl.ds(t, 1)
            grad = scan_grad[row, :]
            summed = columns[count:, i : i + 1] * grad + adjoint
            read_sum[at_token(t), :] = tree_sum(lane_tiles(grad * states[at_token(t + 1), :]))
            in_sum[at_token(t), :] = tree_sum(lane_tiles(summed * drive[row, :]))
            keep_halves(halves, i, summed * columns[:count, i : i + 1])
            adjoint = factors[at_token(t), :] * summed
            held = adjoint * states[at_token(t), :]
            decay_grad = decay_grad + held * step_ref[row, :]
            keep_halves(more_halves, i, held * decay)
        put_state_sums(halves, weighted, block)
        put_state_sums(more_halves, scanned, block)
        return adjoint, decay_grad

    ignored, decay_grad = lax.fori_loop(
        0, blocks, backward, (tail_ref[...], jnp.zeros(decay.shape, f32))
    )
    act_grad_ref[...] = step * weighted[...] + skip_ref[...] * scan_grad[...]
    step_grad = act * weighted[...] + scanned[...]
    pre_grad = (step_grad * jax.nn.sigmoid(step_pre_ref[...])).astype(bf16)
    small_ref[:rank, :] = jnp.dot(step_low, pre_grad, preferred_element_type=f32)
    small_ref[rank : rank + count, :] = decay_grad * decay
    bias_grad = jnp.sum(pre_grad.astype(f32), axis=0, keepdims=True)
    small_ref[rank + count + 1 : rank + count + 2, :] = bias_grad
    spare = small_ref.shape[0] - (rank + count + 2)
    small_ref[rank + count + 2 :, :] = jnp.zeros((spare, small_ref.shape[1]), f32)
    before = before_ref[...]
    select_grad_ref[:rank, :] = before[:rank] + lax.dot_general(
        step_weight_ref[...], pre_grad, contract_last, preferred_element_type=f32
    )
    for n in range(count):
        at = pl.ds(n, rows, stride=count)
        low, high = rank + n, rank + count + n
        select_grad_ref[low : low + 1, :] = before[low : low + 1] + lane_sums(in_sum[at, :])
        select_grad_ref[high : high + 1, :] = before[high : high + 1] + lane_sums(read_sum[at, :])


def scan_full(
    part,
    selected,
    other,
    step_pre,
    step,
    act,
    projected,
    gated_grad,
    masks,
    decay_log,
    entry,
    tail,
    skip_gain,
    step_weight,
    before,
    after,
):
    rows, width = step.shape
    count = decay_log.shape[0]
    columns = selected.shape[0]
    rank = step_weight.shape[0]
    half_rows = 8 * body_rows * (scan_width // lanes)
    small = rank + count + 16
    return call(
        scan_kernel,
        "scan_full",
        width,
        [
            whole_spec(columns, rows),
            whole_spec(columns, rows),
            column_spec(rows),
            column_spec(rows),
            column_spec(rows, part),
            part_spec(1, rows, part),
            column_spec(rows, part),
            whole_spec(rows, masks.shape[1]),
            column_spec(count, part),
            column_spec(count),
            column_spec(count),
            column_spec(1, part),
            column_spec(rank, part),
            whole_spec(columns, rows),
            pl.BlockSpec(memory_space=pl.ANY),
        ],
        [column_spec(rows)] * 3 + [whole_spec(columns, rows), column_spec(small)],
        [
            jax.ShapeDtypeStruct((rows, width), bf16),
            jax.ShapeDtypeStruct((rows, width), bf16),
            jax.ShapeDtypeStruct((rows, width), f32),
            jax.ShapeDtypeStruct((columns, rows), f32),
            jax.ShapeDtypeStruct((small, width), f32),
        ],
        [pltpu.VMEM((2 * count, rows), f32)]
        + [pltpu.VMEM((rows, scan_width), f32)] * 5
        + [
            pltpu.VMEM(((rows + 1) * count, scan_width), f32),
            pltpu.VMEM((rows * count, scan_width), f32),
            pltpu.VMEM((half_rows, lanes), f32),
            pltpu.VMEM((half_rows, lanes), f32),
            pltpu.VMEM((rows * count, lanes), f32),
            pltpu.VMEM((rows * count, lanes), f32),
        ],
        13_000_000_000,
        selected,
        other,
        step_pre,
        step,
        act,
        projected,
        gated_grad,
        masks,
        decay_log,
        entry,
        tail,
        skip_gain,
        step_weight,
        before,
        after,
    )


def conv_grad_kernel(
    select_grad_ref,
    other_ref,
    select_ref,
    act_grad_ref,
    convolved_ref,
    act_ref,
    inner_ref,
    conv_weight_ref,
    mask_ref,
    inner_grad_ref,
    edge_ref,
    small_ref,
    inner,
    shifted,
):
    rows = act_ref.shape[0]
    taps = conv_weight_ref.shape[0]
    columns = select_ref.shape[0]
    select_grad = (select_grad_ref[...] + other_ref[...]).astype(bf16)
    total = act_grad_ref[...] + lax.dot_general(
        select_grad, select_ref[...], contract_first, preferred_element_type=f32
    )
    conv_grad = total * silu_slope(convolved_ref[...])
    small_ref[:columns, :] = jnp.dot(select_grad, act_ref[...], preferred_element_type=f32)
    inner[:halo, :] = inner_ref[rows:, :].astype(f32)
    inner[halo:, :] = inner_ref[:rows, :].astype(f32)
    edges = jnp.zeros((8, conv_grad.shape[1]), f32)
    shifted[:8, :] = edges
    shifted[rows + 8 :, :] = edges
    out = conv_weight_ref[taps - 1 :, :] * conv_grad
    before = edges
    small_ref[columns + taps - 1 : columns + taps, :] = jnp.sum(
        conv_grad * inner[halo:, :], axis=0, keepdims=True
    )
    for lag in range(1, taps):
        masked = conv_grad * mask_ref[:, lag : lag + 1]
        at = taps - 1 - lag
        small_ref[columns + at : columns + at + 1, :] = jnp.sum(
            masked * inner[pl.ds(halo - lag, rows), :], axis=0, keepdims=True
        )
        shifted[8 : rows + 8, :] = masked
        weight = conv_weight_ref[at : at + 1, :]
        out = out + weight * shifted[pl.ds(8 + lag, rows), :]
        before = before + weight * shifted[pl.ds(lag, 8), :]
    small_ref[columns + taps : columns + taps + 1, :] = jnp.sum(conv_grad, axis=0, keepdims=True)
    spare = small_ref.shape[0] - (columns + taps + 1)
    small_ref[columns + taps + 1 :, :] = jnp.zeros((spare, small_ref.shape[1]), f32)
    inner_grad_ref[...] = out.astype(bf16)
    edge_ref[:8, :] = before
    edge_ref[8:, :] = out[rows - 8 :, :]


def convolve_grad(
    part, select_grad, other, select_weight, act_grad, convolved, act, projected, conv_weight, masks
):
    rows, width = act_grad.shape
    extended = rows + halo
    columns = select_weight.shape[0]
    taps = conv_weight.shape[0]
    small = columns + 16
    return call(
        conv_grad_kernel,
        "convolve_grad",
        width,
        [
            whole_spec(columns, rows),
            whole_spec(columns, rows),
            column_spec(columns, part),
            column_spec(rows),
            column_spec(rows, part),
            column_spec(rows, part),
            part_spec(0, extended, part),
            column_spec(taps, part),
            whole_spec(rows, masks.shape[1]),
        ],
        [column_spec(rows), column_spec(16), column_spec(small)],
        [
            jax.ShapeDtypeStruct((rows, width), bf16),
            jax.ShapeDtypeStruct((16, width), f32),
            jax.ShapeDtypeStruct((small, width), f32),
        ],
        [pltpu.VMEM((extended, scan_width), f32), pltpu.VMEM((rows + 16, scan_width), f32)],
        3_000_000_000,
        select_grad,
        other,
        select_weight,
        act_grad,
        convolved,
        act,
        projected,
        conv_weight,
        masks,
    )


def normalize_kernel(
    own_ref, other_ref, edge_ref, other_edge_ref, gain_ref, whole_ref, normed_ref, inverse_ref
):
    rows, half = own_ref.shape
    right = lax.axis_index("narrow") == 1
    for at, own, other in ((0, own_ref, other_ref), (rows, edge_ref, other_edge_ref)):
        end = at + own.shape[0]
        whole_ref[at:end, :half] = jnp.where(right, other[...], own[...])
        whole_ref[at:end, half:] = jnp.where(right, own[...], other[...])
    whole = whole_ref[...].astype(f32)
    inverse = lax.rsqrt(jnp.mean(whole * whole, axis=1, keepdims=True) + epsilon)
    normed_ref[...] = (whole * inverse * gain_ref[...]).astype(bf16)
    inverse_ref[...] = inverse[:rows]


def normalized(own, other, edge, other_edge, gain):
    rows, half = own.shape
    extended = rows + edge.shape[0]
    return pl.pallas_call(
        normalize_kernel,
        out_shape=[
            jax.ShapeDtypeStruct((extended, 2 * half), bf16),
            jax.ShapeDtypeStruct((extended, 2 * half), bf16),
            jax.ShapeDtypeStruct((rows, 1), f32),
        ],
        name="normalized",
    )(own, other, edge, other_edge, gain)


def join_kernel(first_ref, second_ref, inner_ref, out_ref):
    half = scan_width
    step = pl.program_id(0)
    rows = first_ref.shape[0]
    core_rows = inner_ref.shape[0] // 2
    out_ref[:, 1, :half] = first_ref[...].astype(f32)
    out_ref[:, 1, half:] = second_ref[...].astype(f32)
    for k in range(4):

        @pl.when(step == k)
        def _():
            at, lane = (k // 2) * core_rows, (k % 2) * half
            for part in range(2):
                block = inner_ref[at + part * rows : at + (part + 1) * rows, lane : lane + half]
                out_ref[:, 0, part * half : (part + 1) * half] = block.astype(f32)


def joined(first, second, inner):
    depth = first.shape[0]
    rows = depth // 4
    spec = pl.BlockSpec((rows, scan_width), lambda j: (1 + 2 * (j // 2), j % 2))
    return pl.pallas_call(
        join_kernel,
        grid=(4,),
        in_specs=[spec, spec, whole_spec(*inner.shape)],
        out_specs=pl.BlockSpec((rows, 2, 2 * scan_width), lambda j: (j, 0, 0)),
        out_shape=jax.ShapeDtypeStruct((depth, 2, 2 * scan_width), f32),
        compiler_params=pltpu.CompilerParams(vmem_limit_bytes=vmem_bytes),
        name="joined",
    )(first, second, inner)


def carried(ends, decay):
    count = decay.shape[0]
    place = lax.axis_index("wide")

    def split(packed):
        return packed[:count], packed[count : 2 * count], packed[2 * count : 2 * count + 1]

    def through(total):
        return jnp.exp(decay * total)

    zero = jnp.zeros(decay.shape, f32)
    none = jnp.zeros((1, decay.shape[1]), f32)
    before, before_steps, after, after_steps = zero, none, zero, none
    packed = ends
    for bit in (1, 2):
        second = (place & bit) != 0
        own = split(packed)
        other = split(swapped(packed, "wide", bit))
        early = [jnp.where(second, b, a) for a, b in zip(own, other)]
        late = [jnp.where(second, a, b) for a, b in zip(own, other)]
        before = before + jnp.where(second, through(before_steps) * other[0], 0.0)
        before_steps = before_steps + jnp.where(second, other[2], 0.0)
        after = after + jnp.where(second, 0.0, through(after_steps) * other[1])
        after_steps = after_steps + jnp.where(second, 0.0, other[2])
        state = late[0] + through(late[2]) * early[0]
        adjoint = early[1] + through(early[2]) * late[1]
        packed = jnp.concatenate(
            [state, adjoint, jnp.broadcast_to(early[2] + late[2], (8, decay.shape[1]))]
        )
    from_before = passed_along(packed[:count], "wide", 4)
    from_after = passed_along(packed[count : 2 * count], "wide", -4)
    return (
        before + through(before_steps) * from_before,
        after + through(after_steps) * from_after,
    )


def local(
    tokens,
    norm_gain,
    in_weight,
    conv_weight,
    conv_bias,
    select_weight,
    step_weight,
    step_bias,
    decay_log,
    skip_gain,
    out_weight,
    segment_ids,
    cotangent,
):
    rows, features = tokens.shape
    taps = conv_weight.shape[0]
    columns = select_weight.shape[0]
    rank = step_weight.shape[0]
    count = decay_log.shape[0]
    right_half = lax.axis_index("narrow") == 1

    def both_halves(own, other):
        return jnp.concatenate(
            [jnp.where(right_half, other, own), jnp.where(right_half, own, other)], axis=1
        )

    other_tokens = swapped(tokens, "narrow", 1)
    other_cot = swapped(cotangent, "narrow", 1)
    same_as_last = (segment_ids[rows - halo :] == segment_ids[rows - 1 :])[:, None]
    edge_rows = jnp.where(same_as_last, tokens[rows - halo :], jnp.zeros((), tokens.dtype))
    edge, other_edge = to_next_both(edge_rows)

    padded_ids = jnp.concatenate([jnp.broadcast_to(segment_ids[:1], (taps - 1,)), segment_ids])
    masks = jnp.stack(
        [
            (padded_ids[taps - 1 - lag : taps - 1 - lag + rows] == segment_ids).astype(f32)
            for lag in range(taps)
        ]
        + [jnp.zeros((rows,), f32)] * (8 - taps),
        axis=1,
    )
    whole_ext, normed_ext, inverse = normalized(
        tokens, other_tokens, edge, other_edge, norm_gain[None]
    )
    projected = jnp.einsum(
        "td,dce->cte", normed_ext, in_weight, preferred_element_type=f32
    ).astype(bf16)
    convolved, act, selected = convolve(
        projected, conv_weight, conv_bias[None], select_weight, masks
    )
    other_selected = swapped(selected, "narrow", 1)
    cot_whole = both_halves(cotangent, other_cot)
    gated_grad = lax.dot_general(
        cot_whole, out_weight, contract_last, preferred_element_type=f32
    )
    parts = range(out_weight.shape[0] // scan_width)
    decay = -jnp.exp(decay_log)
    started = []
    for part in parts:
        step_pre, step, ends = scan_ends(
            part,
            selected,
            other_selected,
            step_weight,
            step_bias[None],
            act,
            projected,
            gated_grad,
            masks,
            decay_log,
        )
        here = decay[:, part * scan_width : (part + 1) * scan_width]
        started.append((step_pre, step, carried(ends, here)))
    normed = normed_ext[:rows]
    bits = wide_bits()
    select_grad = jnp.zeros(selected.shape, f32)
    waited = select_grad
    done, sums = [], []
    for part in parts:
        step_pre, step, (entry, tail) = started[part]
        gated, gate_grad, act_grad, select_grad, small = scan_full(
            part,
            selected,
            other_selected,
            step_pre,
            step,
            act,
            projected,
            gated_grad,
            masks,
            decay_log,
            entry,
            tail,
            skip_gain[None],
            step_weight,
            select_grad,
            waited,
        )
        done.append((gated, gate_grad, act_grad, small))
        waited = first_step([(gated, cot_whole, False), (normed, gate_grad, True)])
        sums.append(waited)
    other_select_grad = swapped(select_grad, "narrow", 1)
    sums = [gathered(scattered(piece, bits[1:]), bits) for piece in sums]
    gated, gate_grad, _, scan_small = [
        jnp.concatenate(pieces, axis=1) for pieces in zip(*done)
    ]

    def narrow_halves(array):
        low, high = array[:, :features], array[:, features:]
        return jnp.where(right_half, high, low), jnp.where(right_half, low, high)

    out_part = jnp.dot(gated, out_weight, preferred_element_type=f32)
    out_mine, out_other = narrow_halves(out_part)
    out_sum = out_mine + swapped(out_other, "narrow", 1)
    layer_out = (tokens.astype(f32) + out_sum).astype(bf16)

    results = [
        convolve_grad(
            part,
            select_grad,
            other_select_grad,
            select_weight,
            done[part][2],
            convolved,
            act,
            projected,
            conv_weight,
            masks,
        )
        for part in parts
    ]
    inner_main, edges, conv_small = [jnp.concatenate(x, axis=1) for x in zip(*results)]
    from_next = passed_along(edges[:8], "wide", -1)
    last_rows = edges[8:] + jnp.where(same_as_last[halo - 8 :], from_next, 0.0)
    inner_grad = jnp.concatenate([inner_main[: rows - 8], last_rows.astype(bf16)])
    inner_piece = first_step(
        [
            (normed, inner_grad[:, part * scan_width : (part + 1) * scan_width], True)
            for part in parts
        ]
    )
    normed_part = jnp.einsum(
        "cte,dce->td", jnp.stack([inner_grad, gate_grad]), in_weight, preferred_element_type=f32
    )
    whole = whole_ext[:rows].astype(f32)
    gain_part = jnp.sum(normed_part * whole * inverse, axis=0, keepdims=True)
    row_part = jnp.sum(normed_part * norm_gain * whole, axis=1, keepdims=True)

    spare = -(scan_small.shape[0] + conv_small.shape[0] + 1) % 256
    small = jnp.concatenate(
        [scan_small, conv_small, gain_part, jnp.zeros((spare, gain_part.shape[1]), f32)]
    )
    small_mine, small_other = halves_of(small, 0)
    small_piece = small_mine + swapped(small_other.astype(bf16), "wide", 1).astype(f32)
    last_piece = scattered(jnp.concatenate([inner_piece, small_piece]), bits[1:])
    inner_sum = gathered(last_piece, bits)

    normed_mine, normed_other = narrow_halves(normed_part)
    row_sum = row_part + swapped(row_part, "narrow", 1)
    normed_sum = normed_mine + swapped(normed_other, "narrow", 1)
    gain_mine = jnp.where(right_half, norm_gain[features:], norm_gain[:features])
    whole_grad = inverse * (gain_mine * normed_sum) - tokens.astype(f32) * (
        inverse * inverse * inverse
    ) * (row_sum / (2 * features))
    tokens_grad = (whole_grad + cotangent.astype(f32)).astype(bf16)

    core_rows = inner_sum.shape[0] // 2
    small_at = inner_piece.shape[0]
    small_sum = jnp.concatenate(
        [inner_sum[small_at:core_rows], inner_sum[core_rows + small_at :]]
    ).astype(f32)
    scan_sum = small_sum[: scan_small.shape[0]]
    conv_sum = small_sum[scan_small.shape[0] : scan_small.shape[0] + conv_small.shape[0]]
    gain_row = scan_small.shape[0] + conv_small.shape[0]
    gain_sum = small_sum[gain_row : gain_row + 1]
    norm_gain_grad = (gain_sum + swapped(gain_sum, "narrow", 1))[0]
    quarter = scan_width // 2
    out_weight_grad = jnp.concatenate(
        [x for total in sums for x in (total[:quarter], total[2 * quarter : 3 * quarter])]
    ).astype(f32)
    return (
        layer_out,
        tokens_grad,
        norm_gain_grad,
        joined(*sums, inner_sum),
        conv_sum[columns : columns + taps],
        conv_sum[columns + taps],
        conv_sum[:columns],
        scan_sum[:rank],
        scan_sum[rank + count + 1],
        scan_sum[rank : rank + count],
        scan_sum[rank + count],
        out_weight_grad,
    )


def solution(mesh):
    placed = (
        P("wide", "narrow"),
        P(),
        P(None, None, "narrow"),
        P(None, "narrow"),
        P("narrow"),
        P(None, "narrow"),
        P(None, "narrow"),
        P("narrow"),
        P(None, "narrow"),
        P("narrow"),
        P("narrow", None),
        P("wide"),
        P("wide", "narrow"),
    )
    return jax.shard_map(
        local,
        mesh=mesh,
        in_specs=placed,
        out_specs=(
            P("wide", "narrow"),
            P("wide", "narrow"),
            P(),
            P(None, None, "narrow"),
            P(None, "narrow"),
            P("narrow"),
            P(None, "narrow"),
            P(None, "narrow"),
            P("narrow"),
            P(None, "narrow"),
            P("narrow"),
            P("narrow", None),
        ),
        check_vma=False,
    )
```

```python
import functools

import jax
import jax.numpy as jnp
from jax import lax
from jax.experimental import pallas as pl
from jax.experimental.pallas import tpu as pltpu
from jax.sharding import PartitionSpec as P

epsilon = 1e-05
log2e = 1.4426950408889634
reset_step = 1e30
lanes = 128
halo = 16
body_rows = 32
scan_width = 512
vmem_bytes = 56 * 1024 * 1024
f32 = jnp.float32
bf16 = jnp.bfloat16
contract_first = (((0,), (0,)), ((), ()))
contract_last = (((1,), (1,)), ((), ()))


def passed_along(array, axis, by):
    peers = lax.axis_size(axis)
    pairs = [(i, i + by) for i in range(peers) if 0 <= i + by < peers]
    return lax.ppermute(array, axis, pairs)


def swapped(array, axis, bit):
    peers = lax.axis_size(axis)
    return lax.ppermute(array, axis, [(i, i ^ bit) for i in range(peers)])


def wide_bits():
    bit, bits = 1, []
    while bit < lax.axis_size("wide"):
        bits.append(bit)
        bit *= 2
    return bits


def to_next_both(array):
    count, sides = lax.axis_size("wide"), lax.axis_size("narrow")
    pairs = [
        (i * sides + k, (i + 1) * sides + (sides - 1 - k))
        for i in range(count - 1)
        for k in range(sides)
    ]
    return passed_along(array, "wide", 1), lax.ppermute(array, ("wide", "narrow"), pairs)


def is_upper(bit):
    return (lax.axis_index("wide") & bit) != 0


def group_bits(size):
    bits, bit = [], 4
    while bit < lax.axis_size("wide"):
        bits.append(bit)
        bit *= 2
    return [tuple(bits[k : k + size]) for k in range(0, len(bits), size)]


def flips(bits):
    return [sum(b for k, b in enumerate(bits) if n >> k & 1) for n in range(2 ** len(bits))]


def scattered(piece, bits):
    rows = piece.shape[0] // 2 ** len(bits)
    here = sum(is_upper(b).astype(jnp.int32) << k for k, b in enumerate(bits))

    def block(n):
        return lax.dynamic_slice_in_dim(piece, (here ^ n) * rows, rows, 0)

    total = block(0).astype(f32)
    for n, flip in enumerate(flips(bits)):
        if n > 0:
            total = total + swapped(block(n).astype(bf16), "wide", flip).astype(f32)
    return total


def gathered(held, bits):
    blocks = [held] + [swapped(held, "wide", flip) for flip in flips(bits)[1:]]
    for bit in bits:
        upper = is_upper(bit)
        blocks = [
            jnp.concatenate([jnp.where(upper, b, a), jnp.where(upper, a, b)])
            for a, b in zip(blocks[0::2], blocks[1::2])
        ]
    return blocks[0]


def summed_above(piece, size):
    for bits in group_bits(size):
        piece = scattered(piece, bits)
    held = piece.astype(bf16)
    for bits in reversed(group_bits(size)):
        held = gathered(held, bits)
    return held


def shared_by_four(array):
    near = jnp.stack([array, swapped(array, "wide", 2)])
    return near, swapped(near, "wide", 1)


def quarter_of_four(array):
    width = array.shape[1] // 4
    here = lax.axis_index("wide") & 3

    def quarter(n):
        return lax.dynamic_slice_in_dim(array, (here ^ n) * width, width, 1)

    return jnp.stack(
        [quarter(0)] + [swapped(quarter(n), "wide", n) for n in (2, 1, 3)]
    )


def silu_slope(values):
    logistic = jax.nn.sigmoid(values)
    return logistic * (1.0 + values * (1.0 - logistic))


def softplus(values):
    return jnp.maximum(values, 0.0) + jnp.log1p(jnp.exp(-jnp.abs(values)))


def column_spec(rows, start=0):
    return pl.BlockSpec((rows, scan_width), lambda j: (0, start + j))


def part_spec(part, rows, start=0):
    return pl.BlockSpec((None, rows, scan_width), lambda j: (part, 0, start + j))


def whole_spec(rows, width):
    return pl.BlockSpec((rows, width), lambda j: (0, 0))


def call(kernel, name, width, in_specs, out_specs, out_shape, scratch, flops, *operands):
    moved = sum(a.size * a.dtype.itemsize for a in operands)
    return pl.pallas_call(
        kernel,
        grid=(width // scan_width,),
        in_specs=in_specs,
        out_specs=out_specs,
        out_shape=out_shape,
        scratch_shapes=scratch,
        compiler_params=pltpu.CompilerParams(vmem_limit_bytes=vmem_bytes),
        cost_estimate=pl.CostEstimate(flops=flops, bytes_accessed=moved, transcendentals=0),
        name=name,
    )(*operands)


def conv_kernel(
    inner_ref,
    conv_weight_ref,
    conv_bias_ref,
    select_ref,
    mask_ref,
    convolved_ref,
    act_ref,
    selected_ref,
    inner,
):
    rows = act_ref.shape[0]
    taps = conv_weight_ref.shape[0]
    inner[:halo, :] = inner_ref[rows:, :].astype(f32)
    inner[halo:, :] = inner_ref[:rows, :].astype(f32)
    total = conv_bias_ref[...] + conv_weight_ref[taps - 1 :, :] * inner[halo:, :]
    for lag in range(1, taps):
        earlier = inner[pl.ds(halo - lag, rows), :] * mask_ref[:, lag : lag + 1]
        total = total + conv_weight_ref[taps - 1 - lag : taps - lag, :] * earlier
    convolved_ref[...] = total
    act = (total * jax.nn.sigmoid(total)).astype(bf16)
    act_ref[...] = act
    part = lax.dot_general(select_ref[...], act, contract_last, preferred_element_type=f32)

    @pl.when(pl.program_id(0) == 0)
    def _():
        selected_ref[...] = part

    @pl.when(pl.program_id(0) > 0)
    def _():
        selected_ref[...] += part


def convolve(projected, conv_weight, conv_bias, select_weight, masks):
    parts, extended, width = projected.shape
    rows = extended - halo
    taps = conv_weight.shape[0]
    columns = select_weight.shape[0]
    return call(
        conv_kernel,
        "convolve",
        width,
        [
            part_spec(0, extended),
            column_spec(taps),
            column_spec(1),
            column_spec(columns),
            whole_spec(rows, masks.shape[1]),
        ],
        [column_spec(rows), column_spec(rows), whole_spec(columns, rows)],
        [
            jax.ShapeDtypeStruct((rows, width), f32),
            jax.ShapeDtypeStruct((rows, width), bf16),
            jax.ShapeDtypeStruct((columns, rows), f32),
        ],
        [pltpu.VMEM((extended, scan_width), f32)],
        4_000_000_000,
        projected,
        conv_weight,
        conv_bias,
        select_weight,
        masks,
    )


def coef_columns(coef, block):
    per_tile = lanes // body_rows
    start = pl.multiple_of((block // per_tile) * lanes, lanes)
    tile = coef[:, pl.ds(start, lanes)]
    back = body_rows * lax.rem(block, per_tile)
    return pltpu.roll(tile, lax.rem(lanes - back, lanes), 1)


def ends_kernel(
    selected_ref,
    other_ref,
    step_weight_ref,
    step_bias_ref,
    act_ref,
    gate_ref,
    gated_grad_ref,
    mask_ref,
    decay_log_ref,
    step_pre_ref,
    step_ref,
    ends_ref,
    coef,
    held_step,
    drive,
    scan_grad,
):
    rows = act_ref.shape[0]
    count = decay_log_ref.shape[0]
    rank = step_weight_ref.shape[0]
    decay2 = -jnp.exp(decay_log_ref[...]) * log2e
    selected = selected_ref[...] + other_ref[...]
    coef[...] = selected[rank:, :]
    step_low = selected[:rank, :].astype(bf16)
    step_pre = step_bias_ref[...] + lax.dot_general(
        step_low, step_weight_ref[...], contract_first, preferred_element_type=f32
    )
    step_pre_ref[...] = step_pre
    step = softplus(step_pre)
    step_ref[...] = step
    held_step[...] = jnp.where(mask_ref[:, 1:2] > 0.0, step, reset_step)
    drive[...] = step * act_ref[...].astype(f32)
    gate = gate_ref[...].astype(f32)
    scan_grad[...] = gated_grad_ref[...] * (gate * jax.nn.sigmoid(gate))
    zero = jnp.zeros(decay2.shape, f32)

    def body(block, carried):
        state, product, adjoint = carried
        columns = coef_columns(coef, block)
        for i in range(body_rows):
            row = pl.ds(block * body_rows + i, 1)
            factor = jnp.exp2(held_step[row, :] * decay2)
            state = factor * state + columns[:count, i : i + 1] * drive[row, :]
            product = factor * product
            adjoint = adjoint + product * (columns[count:, i : i + 1] * scan_grad[row, :])
        return state, product, adjoint

    state, product, adjoint = lax.fori_loop(0, rows // body_rows, body, (zero, zero + 1.0, zero))
    ends_ref[:count, :] = state
    ends_ref[count : 2 * count, :] = adjoint
    total = jnp.sum(held_step[...], axis=0, keepdims=True)
    ends_ref[2 * count :, :] = jnp.broadcast_to(total, (8, total.shape[1]))


def scan_ends(
    part, selected, other, step_weight, step_bias, act, projected, gated_grad, masks, decay_log
):
    rows, width = act.shape[0], scan_width
    count = decay_log.shape[0]
    columns = selected.shape[0]
    rank = step_weight.shape[0]
    return call(
        ends_kernel,
        "scan_ends",
        width,
        [
            whole_spec(columns, rows),
            whole_spec(columns, rows),
            column_spec(rank, part),
            column_spec(1, part),
            column_spec(rows, part),
            part_spec(1, rows, part),
            column_spec(rows, part),
            whole_spec(rows, masks.shape[1]),
            column_spec(count, part),
        ],
        [column_spec(rows), column_spec(rows), column_spec(2 * count + 8)],
        [
            jax.ShapeDtypeStruct((rows, width), f32),
            jax.ShapeDtypeStruct((rows, width), f32),
            jax.ShapeDtypeStruct((2 * count + 8, width), f32),
        ],
        [pltpu.VMEM((2 * count, rows), f32)] + [pltpu.VMEM((rows, scan_width), f32)] * 3,
        5_000_000_000,
        selected,
        other,
        step_weight,
        step_bias,
        act,
        projected,
        gated_grad,
        masks,
        decay_log,
    )


def lane_tiles(values):
    return [values[:, k : k + lanes] for k in range(0, values.shape[1], lanes)]


def tree_sum(parts):
    while len(parts) > 1:
        odd = parts[len(parts) // 2 * 2 :]
        parts = [a + b for a, b in zip(parts[0::2], parts[1::2])] + odd
    return parts[0]


def keep_halves(scratch, i, values):
    for k, tile in enumerate(lane_tiles(values)):
        at = (k * body_rows + i) * 8
        scratch[at : at + 8, :] = tile[:8] + tile[8:]


def put_state_sums(scratch, out_ref, block):
    for group in range(body_rows // 8):
        row = pl.ds(pl.multiple_of(block * body_rows + group * 8, 8), 8)
        for k in range(out_ref.shape[1] // lanes):
            at = (k * body_rows + group * 8) * 8
            total = tree_sum([scratch[pl.ds(at + n, 8, stride=8), :] for n in range(8)])
            out_ref[row, k * lanes : (k + 1) * lanes] = total


def lane_sums(values):
    ones = jnp.ones((8, lanes), bf16)
    high = values.astype(bf16)
    low = (values - high.astype(f32)).astype(bf16)
    total = lax.dot_general(ones, high, contract_last, preferred_element_type=f32)
    total += lax.dot_general(ones, low, contract_last, preferred_element_type=f32)
    return total[:1, :]


def scan_kernel(
    selected_ref,
    other_ref,
    step_pre_ref,
    step_ref,
    act_ref,
    gate_ref,
    gated_grad_ref,
    mask_ref,
    decay_log_ref,
    entry_ref,
    tail_ref,
    skip_ref,
    step_weight_ref,
    before_ref,
    *rest,
    waits,
):
    (
        pair_ref,
        act_grad_ref,
        select_grad_ref,
        small_ref,
        coef,
        held_step,
        drive,
        scan_grad,
        scanned,
        weighted,
        states,
        factors,
        halves,
        more_halves,
        in_sum,
        read_sum,
    ) = rest[waits:]
    rows = step_ref.shape[0]
    count = decay_log_ref.shape[0]
    rank = step_weight_ref.shape[0]
    blocks = rows // body_rows
    decay = -jnp.exp(decay_log_ref[...])
    decay2 = decay * log2e
    selected = selected_ref[...] + other_ref[...]
    coef[...] = selected[rank:, :]
    step_low = selected[:rank, :].astype(bf16)
    step = step_ref[...]
    act = act_ref[...].astype(f32)
    held_step[...] = jnp.where(mask_ref[:, 1:2] > 0.0, step, reset_step)
    drive[...] = step * act
    states[:count, :] = entry_ref[...]

    def at_token(t):
        return pl.ds(pl.multiple_of(t * count, count), count)

    def forward(block, state):
        columns = coef_columns(coef, block)
        for i in range(body_rows):
            t = block * body_rows + i
            row = pl.ds(t, 1)
            factor = jnp.exp2(held_step[row, :] * decay2)
            state = factor * state + columns[:count, i : i + 1] * drive[row, :]
            factors[at_token(t), :] = factor
            states[at_token(t + 1), :] = state
            keep_halves(halves, i, columns[count:, i : i + 1] * state)
        put_state_sums(halves, scanned, block)
        return state

    lax.fori_loop(0, blocks, forward, entry_ref[...])

    gate = gate_ref[...].astype(f32)
    logistic = jax.nn.sigmoid(gate)
    gate_act = gate * logistic
    gated_grad = gated_grad_ref[...]
    grads = gated_grad * gate_act
    scan_grad[...] = grads
    total = scanned[...] + skip_ref[...] * act
    pair_ref[0] = (total * gate_act).astype(bf16)
    slope = logistic * (1.0 + gate * (1.0 - logistic))
    pair_ref[1] = (gated_grad * total * slope).astype(bf16)
    small_ref[rank + count : rank + count + 1, :] = jnp.sum(grads * act, axis=0, keepdims=True)

    def backward(k, carried):
        adjoint, decay_grad = carried
        block = blocks - 1 - k
        columns = coef_columns(coef, block)
        for i in range(body_rows - 1, -1, -1):
            t = block * body_rows + i
            row = pl.ds(t, 1)
            grad = scan_grad[row, :]
            summed = columns[count:, i : i + 1] * grad + adjoint
            read_sum[at_token(t), :] = tree_sum(lane_tiles(grad * states[at_token(t + 1), :]))
            in_sum[at_token(t), :] = tree_sum(lane_tiles(summed * drive[row, :]))
            keep_halves(halves, i, summed * columns[:count, i : i + 1])
            adjoint = factors[at_token(t), :] * summed
            held = adjoint * states[at_token(t), :]
            decay_grad = decay_grad + held * step_ref[row, :]
            keep_halves(more_halves, i, held * decay)
        put_state_sums(halves, weighted, block)
        put_state_sums(more_halves, scanned, block)
        return adjoint, decay_grad

    ignored, decay_grad = lax.fori_loop(
        0, blocks, backward, (tail_ref[...], jnp.zeros(decay.shape, f32))
    )
    act_grad_ref[...] = step * weighted[...] + skip_ref[...] * scan_grad[...]
    step_grad = act * weighted[...] + scanned[...]
    pre_grad = (step_grad * jax.nn.sigmoid(step_pre_ref[...])).astype(bf16)
    small_ref[:rank, :] = jnp.dot(step_low, pre_grad, preferred_element_type=f32)
    small_ref[rank : rank + count, :] = decay_grad * decay
    bias_grad = jnp.sum(pre_grad.astype(f32), axis=0, keepdims=True)
    small_ref[rank + count + 1 : rank + count + 2, :] = bias_grad
    spare = small_ref.shape[0] - (rank + count + 2)
    small_ref[rank + count + 2 :, :] = jnp.zeros((spare, small_ref.shape[1]), f32)
    before = before_ref[...]
    select_grad_ref[:rank, :] = before[:rank] + lax.dot_general(
        step_weight_ref[...], pre_grad, contract_last, preferred_element_type=f32
    )
    for n in range(count):
        at = pl.ds(n, rows, stride=count)
        low, high = rank + n, rank + count + n
        select_grad_ref[low : low + 1, :] = before[low : low + 1] + lane_sums(in_sum[at, :])
        select_grad_ref[high : high + 1, :] = before[high : high + 1] + lane_sums(read_sum[at, :])


def scan_full(
    part,
    selected,
    other,
    step_pre,
    step,
    act,
    projected,
    gated_grad,
    masks,
    decay_log,
    entry,
    tail,
    skip_gain,
    step_weight,
    before,
    waits,
):
    rows, width = step.shape
    count = decay_log.shape[0]
    columns = selected.shape[0]
    rank = step_weight.shape[0]
    half_rows = 8 * body_rows * (scan_width // lanes)
    small = rank + count + 16
    return call(
        functools.partial(scan_kernel, waits=len(waits)),
        "scan_full",
        width,
        [
            whole_spec(columns, rows),
            whole_spec(columns, rows),
            column_spec(rows),
            column_spec(rows),
            column_spec(rows, part),
            part_spec(1, rows, part),
            column_spec(rows, part),
            whole_spec(rows, masks.shape[1]),
            column_spec(count, part),
            column_spec(count),
            column_spec(count),
            column_spec(1, part),
            column_spec(rank, part),
            whole_spec(columns, rows),
        ]
        + [pl.BlockSpec(memory_space=pl.ANY)] * len(waits),
        [
            pl.BlockSpec((2, rows, scan_width), lambda j: (0, 0, j)),
            column_spec(rows),
            whole_spec(columns, rows),
            column_spec(small),
        ],
        [
            jax.ShapeDtypeStruct((2, rows, width), bf16),
            jax.ShapeDtypeStruct((rows, width), f32),
            jax.ShapeDtypeStruct((columns, rows), f32),
            jax.ShapeDtypeStruct((small, width), f32),
        ],
        [pltpu.VMEM((2 * count, rows), f32)]
        + [pltpu.VMEM((rows, scan_width), f32)] * 5
        + [
            pltpu.VMEM(((rows + 1) * count, scan_width), f32),
            pltpu.VMEM((rows * count, scan_width), f32),
            pltpu.VMEM((half_rows, lanes), f32),
            pltpu.VMEM((half_rows, lanes), f32),
            pltpu.VMEM((rows * count, lanes), f32),
            pltpu.VMEM((rows * count, lanes), f32),
        ],
        13_000_000_000,
        selected,
        other,
        step_pre,
        step,
        act,
        projected,
        gated_grad,
        masks,
        decay_log,
        entry,
        tail,
        skip_gain,
        step_weight,
        before,
        *waits,
    )


def conv_grad_kernel(
    select_grad_ref,
    other_ref,
    select_ref,
    act_grad_ref,
    convolved_ref,
    act_ref,
    inner_ref,
    conv_weight_ref,
    mask_ref,
    inner_grad_ref,
    edge_ref,
    small_ref,
    inner,
    shifted,
):
    rows = act_ref.shape[0]
    taps = conv_weight_ref.shape[0]
    columns = select_ref.shape[0]
    select_grad = (select_grad_ref[...] + other_ref[...]).astype(bf16)
    total = act_grad_ref[...] + lax.dot_general(
        select_grad, select_ref[...], contract_first, preferred_element_type=f32
    )
    conv_grad = total * silu_slope(convolved_ref[...])
    small_ref[:columns, :] = jnp.dot(select_grad, act_ref[...], preferred_element_type=f32)
    inner[:halo, :] = inner_ref[rows:, :].astype(f32)
    inner[halo:, :] = inner_ref[:rows, :].astype(f32)
    edges = jnp.zeros((8, conv_grad.shape[1]), f32)
    shifted[:8, :] = edges
    shifted[rows + 8 :, :] = edges
    out = conv_weight_ref[taps - 1 :, :] * conv_grad
    before = edges
    small_ref[columns + taps - 1 : columns + taps, :] = jnp.sum(
        conv_grad * inner[halo:, :], axis=0, keepdims=True
    )
    for lag in range(1, taps):
        masked = conv_grad * mask_ref[:, lag : lag + 1]
        at = taps - 1 - lag
        small_ref[columns + at : columns + at + 1, :] = jnp.sum(
            masked * inner[pl.ds(halo - lag, rows), :], axis=0, keepdims=True
        )
        shifted[8 : rows + 8, :] = masked
        weight = conv_weight_ref[at : at + 1, :]
        out = out + weight * shifted[pl.ds(8 + lag, rows), :]
        before = before + weight * shifted[pl.ds(lag, 8), :]
    small_ref[columns + taps : columns + taps + 1, :] = jnp.sum(conv_grad, axis=0, keepdims=True)
    spare = small_ref.shape[0] - (columns + taps + 1)
    small_ref[columns + taps + 1 :, :] = jnp.zeros((spare, small_ref.shape[1]), f32)
    inner_grad_ref[...] = out.astype(bf16)
    edge_ref[:8, :] = before
    edge_ref[8:, :] = out[rows - 8 :, :]


def convolve_grad(
    part, select_grad, other, select_weight, act_grad, convolved, act, projected, conv_weight, masks
):
    rows, width = act_grad.shape
    extended = rows + halo
    columns = select_weight.shape[0]
    taps = conv_weight.shape[0]
    small = columns + 16
    return call(
        conv_grad_kernel,
        "convolve_grad",
        width,
        [
            whole_spec(columns, rows),
            whole_spec(columns, rows),
            column_spec(columns, part),
            column_spec(rows),
            column_spec(rows, part),
            column_spec(rows, part),
            part_spec(0, extended, part),
            column_spec(taps, part),
            whole_spec(rows, masks.shape[1]),
        ],
        [column_spec(rows), column_spec(16), column_spec(small)],
        [
            jax.ShapeDtypeStruct((rows, width), bf16),
            jax.ShapeDtypeStruct((16, width), f32),
            jax.ShapeDtypeStruct((small, width), f32),
        ],
        [pltpu.VMEM((extended, scan_width), f32), pltpu.VMEM((rows + 16, scan_width), f32)],
        3_000_000_000,
        select_grad,
        other,
        select_weight,
        act_grad,
        convolved,
        act,
        projected,
        conv_weight,
        masks,
    )


def normalize_kernel(
    own_ref, other_ref, edge_ref, other_edge_ref, gain_ref, whole_ref, normed_ref, inverse_ref
):
    rows, half = own_ref.shape
    right = lax.axis_index("narrow") == 1
    for at, own, other in ((0, own_ref, other_ref), (rows, edge_ref, other_edge_ref)):
        end = at + own.shape[0]
        whole_ref[at:end, :half] = jnp.where(right, other[...], own[...])
        whole_ref[at:end, half:] = jnp.where(right, own[...], other[...])
    whole = whole_ref[...].astype(f32)
    inverse = lax.rsqrt(jnp.mean(whole * whole, axis=1, keepdims=True) + epsilon)
    normed_ref[...] = (whole * inverse * gain_ref[...]).astype(bf16)
    inverse_ref[...] = inverse[:rows]


def normalized(own, other, edge, other_edge, gain):
    rows, half = own.shape
    extended = rows + edge.shape[0]
    return pl.pallas_call(
        normalize_kernel,
        out_shape=[
            jax.ShapeDtypeStruct((extended, 2 * half), bf16),
            jax.ShapeDtypeStruct((extended, 2 * half), bf16),
            jax.ShapeDtypeStruct((rows, 1), f32),
        ],
        name="normalized",
    )(own, other, edge, other_edge, gain)


def edge_kernel(ids_ref, tokens_ref, out_ref):
    rows = ids_ref.shape[0]
    taps = 4
    out_ref[...] = tokens_ref[...]
    place = lax.broadcasted_iota(jnp.int32, (halo, 1), 0)
    same = jnp.zeros((halo, 1), f32)
    for lag in range(taps):
        here = jnp.where(ids_ref[rows - 1 - lag] == ids_ref[rows - 1], 1.0, 0.0)
        same = same + jnp.where(place == halo - 1 - lag, here, 0.0)
    out_ref[...] = (tokens_ref[...].astype(f32) * same).astype(bf16)


def edge_rows_of(ids, tokens):
    rows, width = tokens.shape
    return pl.pallas_call(
        edge_kernel,
        grid=(1,),
        in_specs=[
            pl.BlockSpec(memory_space=pltpu.SMEM),
            pl.BlockSpec((halo, width), lambda j: (rows // halo - 1, 0)),
        ],
        out_specs=pl.BlockSpec((halo, width), lambda j: (0, 0)),
        out_shape=jax.ShapeDtypeStruct((halo, width), bf16),
        name="edge_rows",
    )(ids, tokens)


def outer_kernel(near_ref, far_ref, normed_ref, cot_ref, out_ref):
    quarter = cot_ref.shape[2]
    out_sum, gate_sum = None, None
    for n, pair in enumerate((near_ref[0], near_ref[1], far_ref[0], far_ref[1])):
        first = lax.dot_general(pair[0], cot_ref[n], contract_first, preferred_element_type=f32)
        second = lax.dot_general(normed_ref[n], pair[1], contract_first, preferred_element_type=f32)
        out_sum = first if out_sum is None else out_sum + first
        gate_sum = second if gate_sum is None else gate_sum + second
    out_ref[:, :quarter] = out_sum[:quarter]
    out_ref[:, quarter : 2 * quarter] = out_sum[quarter:]
    out_ref[:, 2 * quarter :] = gate_sum


def outer_quarters(near, far, normed, cot):
    quarter = cot.shape[2]
    return pl.pallas_call(
        outer_kernel,
        out_shape=jax.ShapeDtypeStruct((quarter, 4 * quarter), f32),
        compiler_params=pltpu.CompilerParams(vmem_limit_bytes=vmem_bytes),
        cost_estimate=pl.CostEstimate(
            flops=2_000_000_000, bytes_accessed=4_000_000, transcendentals=0
        ),
        name="outer_quarters",
    )(near, far, normed, cot)


def select_block(step, place, refs, use):
    flip = place ^ step
    for core in range(2):

        @pl.when((flip & 1) == core)
        def _():
            use([ref[core] for ref in refs])


def out_join_kernel(place_ref, first_near, first_far, second_near, second_far, out_ref):
    quarter = out_ref.shape[1]

    def use(blocks):
        for part, block in enumerate(blocks):
            for lane in range(2):
                at = (2 * part + lane) * quarter
                out_ref[at : at + quarter, :] = block[0, :, lane * quarter : (lane + 1) * quarter].astype(f32)

    select_block(
        pl.program_id(0), place_ref[0], [(first_near, first_far), (second_near, second_far)], use
    )


def in_join_kernel(
    place_ref,
    first_near,
    first_far,
    second_near,
    second_far,
    inner_near,
    inner_far,
    out_ref,
    small_ref,
    *,
    groups,
):
    rows, half = out_ref.shape[0], out_ref.shape[2] // 2
    piece = inner_near.shape[1] // groups
    inner_rows = rows // groups
    spare = piece - inner_rows

    def use(blocks):
        first, second, inner = blocks
        out_ref[:, 1, :half] = first[0, :, half:].astype(f32)
        out_ref[:, 1, half:] = second[0, :, half:].astype(f32)
        for n in range(groups):
            at = n * piece
            block = inner[0, at : at + piece, :].astype(f32)
            out_ref[n * inner_rows : (n + 1) * inner_rows, 0, :] = block[:inner_rows]
            small_ref[n * spare : (n + 1) * spare, :] = block[inner_rows:]

    select_block(
        pl.program_id(0),
        place_ref[0],
        [(first_near, first_far), (second_near, second_far), (inner_near, inner_far)],
        use,
    )


def from_four(array):
    return pl.BlockSpec((1,) + array.shape[1:], lambda j, place: ((place[0] ^ j) // 2, 0, 0))


def joined_out(place, first, second):
    quarter = first[0].shape[1]
    operands = [*first, *second]
    return pl.pallas_call(
        out_join_kernel,
        grid_spec=pltpu.PrefetchScalarGridSpec(
            num_scalar_prefetch=1,
            grid=(4,),
            in_specs=[from_four(a) for a in operands],
            out_specs=pl.BlockSpec((4 * quarter, quarter), lambda j, place: (0, j)),
        ),
        out_shape=jax.ShapeDtypeStruct((4 * quarter, 4 * quarter), f32),
        compiler_params=pltpu.CompilerParams(vmem_limit_bytes=vmem_bytes),
        name="joined_out",
    )(place, *operands)


def joined_in(place, first, second, inner):
    quarter = first[0].shape[1]
    groups = lax.axis_size("wide") // 4
    small = inner[0].shape[1] - quarter
    operands = [*first, *second, *inner]
    return pl.pallas_call(
        functools.partial(in_join_kernel, groups=groups),
        grid_spec=pltpu.PrefetchScalarGridSpec(
            num_scalar_prefetch=1,
            grid=(4,),
            in_specs=[from_four(a) for a in operands],
            out_specs=[
                pl.BlockSpec((quarter, 2, 4 * quarter), lambda j, place: (j, 0, 0)),
                pl.BlockSpec((small, 4 * quarter), lambda j, place: (j, 0)),
            ],
        ),
        out_shape=[
            jax.ShapeDtypeStruct((4 * quarter, 2, 4 * quarter), f32),
            jax.ShapeDtypeStruct((4 * small, 4 * quarter), f32),
        ],
        compiler_params=pltpu.CompilerParams(vmem_limit_bytes=vmem_bytes),
        name="joined_in",
    )(place, *operands)


def carried(ends, decay):
    count = decay.shape[0]
    place = lax.axis_index("wide")

    def split(packed):
        return packed[:count], packed[count : 2 * count], packed[2 * count : 2 * count + 1]

    def through(total):
        return jnp.exp(decay * total)

    zero = jnp.zeros(decay.shape, f32)
    none = jnp.zeros((1, decay.shape[1]), f32)
    before, before_steps, after, after_steps = zero, none, zero, none
    packed = ends
    for bit in (1, 2):
        second = (place & bit) != 0
        own = split(packed)
        other = split(swapped(packed, "wide", bit))
        early = [jnp.where(second, b, a) for a, b in zip(own, other)]
        late = [jnp.where(second, a, b) for a, b in zip(own, other)]
        before = before + jnp.where(second, through(before_steps) * other[0], 0.0)
        before_steps = before_steps + jnp.where(second, other[2], 0.0)
        after = after + jnp.where(second, 0.0, through(after_steps) * other[1])
        after_steps = after_steps + jnp.where(second, 0.0, other[2])
        state = late[0] + through(late[2]) * early[0]
        adjoint = early[1] + through(early[2]) * late[1]
        packed = jnp.concatenate(
            [state, adjoint, jnp.broadcast_to(early[2] + late[2], (8, decay.shape[1]))]
        )
    from_before = passed_along(packed[:count], "wide", 4)
    from_after = passed_along(packed[count : 2 * count], "wide", -4)
    return (
        before + through(before_steps) * from_before,
        after + through(after_steps) * from_after,
    )


def local(
    tokens,
    norm_gain,
    in_weight,
    conv_weight,
    conv_bias,
    select_weight,
    step_weight,
    step_bias,
    decay_log,
    skip_gain,
    out_weight,
    segment_ids,
    cotangent,
):
    rows, features = tokens.shape
    taps = conv_weight.shape[0]
    columns = select_weight.shape[0]
    rank = step_weight.shape[0]
    count = decay_log.shape[0]
    right_half = lax.axis_index("narrow") == 1

    def both_halves(own, other):
        return jnp.concatenate(
            [jnp.where(right_half, other, own), jnp.where(right_half, own, other)], axis=1
        )

    other_tokens = swapped(tokens, "narrow", 1)
    other_cot = swapped(cotangent, "narrow", 1)
    edge, other_edge = to_next_both(edge_rows_of(segment_ids, tokens))

    same_as_last = (segment_ids[rows - 8 :] == segment_ids[rows - 1 :])[:, None]
    padded_ids = jnp.concatenate([jnp.broadcast_to(segment_ids[:1], (taps - 1,)), segment_ids])
    masks = jnp.stack(
        [
            (padded_ids[taps - 1 - lag : taps - 1 - lag + rows] == segment_ids).astype(f32)
            for lag in range(taps)
        ]
        + [jnp.zeros((rows,), f32)] * (8 - taps),
        axis=1,
    )
    whole_ext, normed_ext, inverse = normalized(
        tokens, other_tokens, edge, other_edge, norm_gain[None]
    )
    projected = jnp.einsum(
        "td,dce->cte", normed_ext, in_weight, preferred_element_type=f32
    ).astype(bf16)
    convolved, act, selected = convolve(
        projected, conv_weight, conv_bias[None], select_weight, masks
    )
    other_selected = swapped(selected, "narrow", 1)
    cot_whole = both_halves(cotangent, other_cot)
    gated_grad = lax.dot_general(
        cot_whole, out_weight, contract_last, preferred_element_type=f32
    )
    parts = range(out_weight.shape[0] // scan_width)
    decay = -jnp.exp(decay_log)
    started = []
    for part in parts:
        step_pre, step, ends = scan_ends(
            part,
            selected,
            other_selected,
            step_weight,
            step_bias[None],
            act,
            projected,
            gated_grad,
            masks,
            decay_log,
        )
        here = decay[:, part * scan_width : (part + 1) * scan_width]
        started.append((step_pre, step, carried(ends, here)))
    normed_four = quarter_of_four(normed_ext[:rows])
    cot_four = quarter_of_four(cot_whole)
    select_grad = jnp.zeros(selected.shape, f32)
    waits = [[started[-1][2][0]], [normed_four, cot_four]]
    done, sums = [], []
    for part in parts:
        step_pre, step, (entry, tail) = started[part]
        pair, act_grad, select_grad, small = scan_full(
            part,
            selected,
            other_selected,
            step_pre,
            step,
            act,
            projected,
            gated_grad,
            masks,
            decay_log,
            entry,
            tail,
            skip_gain[None],
            step_weight,
            select_grad,
            waits[part],
        )
        done.append((pair, act_grad, small))
        sums.append(outer_quarters(*shared_by_four(pair), normed_four, cot_four))
    other_select_grad = swapped(select_grad, "narrow", 1)
    place = (lax.axis_index("wide") & 3).astype(jnp.int32)[None]
    sums = [shared_by_four(summed_above(piece, 1)) for piece in sums]
    out_weight_grad = joined_out(place, *sums)
    scan_small = jnp.concatenate([small for _, _, small in done], axis=1)
    gated = jnp.concatenate([pair[0] for pair, _, _ in done], axis=1)
    gate_grad = jnp.concatenate([pair[1] for pair, _, _ in done], axis=1)

    def narrow_halves(array):
        low, high = array[:, :features], array[:, features:]
        return jnp.where(right_half, high, low), jnp.where(right_half, low, high)

    out_part = jnp.dot(gated, out_weight, preferred_element_type=f32)
    out_mine, out_other = narrow_halves(out_part)
    out_sum = out_mine + swapped(out_other, "narrow", 1)
    layer_out = (tokens.astype(f32) + out_sum).astype(bf16)

    results = [
        convolve_grad(
            part,
            select_grad,
            other_select_grad,
            select_weight,
            done[part][1],
            convolved,
            act,
            projected,
            conv_weight,
            masks,
        )
        for part in parts
    ]
    inner_main, edges, conv_small = [jnp.concatenate(x, axis=1) for x in zip(*results)]
    from_next = passed_along(edges[:8], "wide", -1)
    last_rows = edges[8:] + jnp.where(same_as_last, from_next, 0.0)
    inner_grad = jnp.concatenate([inner_main[: rows - 8], last_rows.astype(bf16)])
    normed_part = jnp.einsum(
        "cte,dce->td", jnp.stack([inner_grad, gate_grad]), in_weight, preferred_element_type=f32
    )
    whole = whole_ext[:rows].astype(f32)
    gain_part = jnp.sum(normed_part * whole * inverse, axis=0, keepdims=True)
    row_part = jnp.sum(normed_part * norm_gain * whole, axis=1, keepdims=True)

    spare = -(scan_small.shape[0] + conv_small.shape[0] + 1) % 256
    small = jnp.concatenate(
        [scan_small, conv_small, gain_part, jnp.zeros((spare, gain_part.shape[1]), f32)]
    )
    near, far = shared_by_four(inner_grad)
    inner_four = jnp.concatenate([near, far]).reshape(4 * rows, -1)
    inner_piece = lax.dot_general(
        normed_four.reshape(4 * rows, -1), inner_four, contract_first, preferred_element_type=f32
    )
    small_piece = scattered(small, (1, 2))
    groups = lax.axis_size("wide") // 4
    last_piece = jnp.concatenate(
        [x.reshape(groups, -1, x.shape[1]) for x in (inner_piece, small_piece)], axis=1
    ).reshape(-1, inner_piece.shape[1])
    inner_sum = shared_by_four(summed_above(last_piece, 2))
    in_weight_grad, small_sum = joined_in(place, *sums, inner_sum)

    normed_mine, normed_other = narrow_halves(normed_part)
    row_sum = row_part + swapped(row_part, "narrow", 1)
    normed_sum = normed_mine + swapped(normed_other, "narrow", 1)
    gain_mine = jnp.where(right_half, norm_gain[features:], norm_gain[:features])
    whole_grad = inverse * (gain_mine * normed_sum) - tokens.astype(f32) * (
        inverse * inverse * inverse
    ) * (row_sum / (2 * features))
    tokens_grad = (whole_grad + cotangent.astype(f32)).astype(bf16)

    scan_sum = small_sum[: scan_small.shape[0]]
    conv_sum = small_sum[scan_small.shape[0] : scan_small.shape[0] + conv_small.shape[0]]
    gain_row = scan_small.shape[0] + conv_small.shape[0]
    gain_sum = small_sum[gain_row : gain_row + 1]
    norm_gain_grad = (gain_sum + swapped(gain_sum, "narrow", 1))[0]
    return (
        layer_out,
        tokens_grad,
        norm_gain_grad,
        in_weight_grad,
        conv_sum[columns : columns + taps],
        conv_sum[columns + taps],
        conv_sum[:columns],
        scan_sum[:rank],
        scan_sum[rank + count + 1],
        scan_sum[rank : rank + count],
        scan_sum[rank + count],
        out_weight_grad,
    )


def solution(mesh):
    placed = (
        P("wide", "narrow"),
        P(),
        P(None, None, "narrow"),
        P(None, "narrow"),
        P("narrow"),
        P(None, "narrow"),
        P(None, "narrow"),
        P("narrow"),
        P(None, "narrow"),
        P("narrow"),
        P("narrow", None),
        P("wide"),
        P("wide", "narrow"),
    )
    return jax.shard_map(
        local,
        mesh=mesh,
        in_specs=placed,
        out_specs=(
            P("wide", "narrow"),
            P("wide", "narrow"),
            P(),
            P(None, None, "narrow"),
            P(None, "narrow"),
            P("narrow"),
            P(None, "narrow"),
            P(None, "narrow"),
            P("narrow"),
            P(None, "narrow"),
            P("narrow"),
            P("narrow", None),
        ),
        check_vma=False,
    )
```

```python
import functools

import jax
import jax.numpy as jnp
from jax import lax
from jax.experimental import pallas as pl
from jax.experimental.pallas import tpu as pltpu
from jax.sharding import PartitionSpec as P

epsilon = 1e-05
log2e = 1.4426950408889634
reset_step = 1e30
lanes = 128
halo = 16
body_rows = 32
scan_width = 512
vmem_bytes = 56 * 1024 * 1024
f32 = jnp.float32
bf16 = jnp.bfloat16
contract_first = (((0,), (0,)), ((), ()))
contract_last = (((1,), (1,)), ((), ()))


def passed_along(array, axis, by):
    peers = lax.axis_size(axis)
    pairs = [(i, i + by) for i in range(peers) if 0 <= i + by < peers]
    return lax.ppermute(array, axis, pairs)


def swapped(array, axis, bit):
    peers = lax.axis_size(axis)
    return lax.ppermute(array, axis, [(i, i ^ bit) for i in range(peers)])


def wide_bits():
    bit, bits = 1, []
    while bit < lax.axis_size("wide"):
        bits.append(bit)
        bit *= 2
    return bits


def to_next_both(array):
    count, sides = lax.axis_size("wide"), lax.axis_size("narrow")
    pairs = [
        (i * sides + k, (i + 1) * sides + (sides - 1 - k))
        for i in range(count - 1)
        for k in range(sides)
    ]
    return passed_along(array, "wide", 1), lax.ppermute(array, ("wide", "narrow"), pairs)


def is_upper(bit):
    return (lax.axis_index("wide") & bit) != 0


def group_bits(size):
    bits, bit = [], 4
    while bit < lax.axis_size("wide"):
        bits.append(bit)
        bit *= 2
    return [tuple(bits[k : k + size]) for k in range(0, len(bits), size)]


def flips(bits):
    return [sum(b for k, b in enumerate(bits) if n >> k & 1) for n in range(2 ** len(bits))]


def scattered(piece, bits):
    rows = piece.shape[0] // 2 ** len(bits)
    here = sum(is_upper(b).astype(jnp.int32) << k for k, b in enumerate(bits))

    def block(n):
        return lax.dynamic_slice_in_dim(piece, (here ^ n) * rows, rows, 0)

    total = block(0).astype(f32)
    for n, flip in enumerate(flips(bits)):
        if n > 0:
            total = total + swapped(block(n).astype(bf16), "wide", flip).astype(f32)
    return total


def gathered(held, bits):
    blocks = [held] + [swapped(held, "wide", flip) for flip in flips(bits)[1:]]
    for bit in bits:
        upper = is_upper(bit)
        blocks = [
            jnp.concatenate([jnp.where(upper, b, a), jnp.where(upper, a, b)])
            for a, b in zip(blocks[0::2], blocks[1::2])
        ]
    return blocks[0]


def quarter_of_four(array):
    width = array.shape[1] // 4
    here = lax.axis_index("wide") & 3

    def quarter(n):
        return lax.dynamic_slice_in_dim(array, (here ^ n) * width, width, 1)

    return jnp.stack(
        [quarter(0)] + [swapped(quarter(n), "wide", n) for n in (2, 1, 3)]
    )


def silu_slope(values):
    logistic = jax.nn.sigmoid(values)
    return logistic * (1.0 + values * (1.0 - logistic))


def softplus(values):
    return jnp.maximum(values, 0.0) + jnp.log1p(jnp.exp(-jnp.abs(values)))


def column_spec(rows, start=0):
    return pl.BlockSpec((rows, scan_width), lambda j: (0, start + j))


def part_spec(part, rows, start=0):
    return pl.BlockSpec((None, rows, scan_width), lambda j: (part, 0, start + j))


def whole_spec(rows, width):
    return pl.BlockSpec((rows, width), lambda j: (0, 0))


def call(kernel, name, width, in_specs, out_specs, out_shape, scratch, flops, *operands):
    moved = sum(a.size * a.dtype.itemsize for a in operands)
    return pl.pallas_call(
        kernel,
        grid=(width // scan_width,),
        in_specs=in_specs,
        out_specs=out_specs,
        out_shape=out_shape,
        scratch_shapes=scratch,
        compiler_params=pltpu.CompilerParams(vmem_limit_bytes=vmem_bytes),
        cost_estimate=pl.CostEstimate(flops=flops, bytes_accessed=moved, transcendentals=0),
        name=name,
    )(*operands)


def conv_kernel(
    inner_ref,
    conv_weight_ref,
    conv_bias_ref,
    select_ref,
    mask_ref,
    convolved_ref,
    act_ref,
    selected_ref,
    inner,
):
    rows = act_ref.shape[0]
    taps = conv_weight_ref.shape[0]
    inner[:halo, :] = inner_ref[rows:, :].astype(f32)
    inner[halo:, :] = inner_ref[:rows, :].astype(f32)
    total = conv_bias_ref[...] + conv_weight_ref[taps - 1 :, :] * inner[halo:, :]
    for lag in range(1, taps):
        earlier = inner[pl.ds(halo - lag, rows), :] * mask_ref[:, lag : lag + 1]
        total = total + conv_weight_ref[taps - 1 - lag : taps - lag, :] * earlier
    convolved_ref[...] = total
    act = (total * jax.nn.sigmoid(total)).astype(bf16)
    act_ref[...] = act
    part = lax.dot_general(select_ref[...], act, contract_last, preferred_element_type=f32)

    @pl.when(pl.program_id(0) == 0)
    def _():
        selected_ref[...] = part

    @pl.when(pl.program_id(0) > 0)
    def _():
        selected_ref[...] += part


def convolve(projected, conv_weight, conv_bias, select_weight, masks):
    parts, extended, width = projected.shape
    rows = extended - halo
    taps = conv_weight.shape[0]
    columns = select_weight.shape[0]
    return call(
        conv_kernel,
        "convolve",
        width,
        [
            part_spec(0, extended),
            column_spec(taps),
            column_spec(1),
            column_spec(columns),
            whole_spec(rows, masks.shape[1]),
        ],
        [column_spec(rows), column_spec(rows), whole_spec(columns, rows)],
        [
            jax.ShapeDtypeStruct((rows, width), f32),
            jax.ShapeDtypeStruct((rows, width), bf16),
            jax.ShapeDtypeStruct((columns, rows), f32),
        ],
        [pltpu.VMEM((extended, scan_width), f32)],
        4_000_000_000,
        projected,
        conv_weight,
        conv_bias,
        select_weight,
        masks,
    )


def coef_columns(coef, block):
    per_tile = lanes // body_rows
    start = pl.multiple_of((block // per_tile) * lanes, lanes)
    tile = coef[:, pl.ds(start, lanes)]
    back = body_rows * lax.rem(block, per_tile)
    return pltpu.roll(tile, lax.rem(lanes - back, lanes), 1)


def ends_kernel(
    selected_ref,
    other_ref,
    step_weight_ref,
    step_bias_ref,
    act_ref,
    gate_ref,
    gated_grad_ref,
    mask_ref,
    decay_log_ref,
    step_pre_ref,
    step_ref,
    ends_ref,
    coef,
    held_step,
    drive,
    scan_grad,
):
    rows = act_ref.shape[0]
    count = decay_log_ref.shape[0]
    rank = step_weight_ref.shape[0]
    decay2 = -jnp.exp(decay_log_ref[...]) * log2e
    selected = selected_ref[...] + other_ref[...]
    coef[...] = selected[rank:, :]
    step_low = selected[:rank, :].astype(bf16)
    step_pre = step_bias_ref[...] + lax.dot_general(
        step_low, step_weight_ref[...], contract_first, preferred_element_type=f32
    )
    step_pre_ref[...] = step_pre
    step = softplus(step_pre)
    step_ref[...] = step
    held_step[...] = jnp.where(mask_ref[:, 1:2] > 0.0, step, reset_step)
    drive[...] = step * act_ref[...].astype(f32)
    gate = gate_ref[...].astype(f32)
    scan_grad[...] = gated_grad_ref[...] * (gate * jax.nn.sigmoid(gate))
    zero = jnp.zeros(decay2.shape, f32)

    def body(block, carried):
        state, product, adjoint = carried
        columns = coef_columns(coef, block)
        for i in range(body_rows):
            row = pl.ds(block * body_rows + i, 1)
            factor = jnp.exp2(held_step[row, :] * decay2)
            state = factor * state + columns[:count, i : i + 1] * drive[row, :]
            product = factor * product
            adjoint = adjoint + product * (columns[count:, i : i + 1] * scan_grad[row, :])
        return state, product, adjoint

    state, product, adjoint = lax.fori_loop(0, rows // body_rows, body, (zero, zero + 1.0, zero))
    ends_ref[:count, :] = state
    ends_ref[count : 2 * count, :] = adjoint
    total = jnp.sum(held_step[...], axis=0, keepdims=True)
    ends_ref[2 * count :, :] = jnp.broadcast_to(total, (8, total.shape[1]))


def scan_ends(
    part, selected, other, step_weight, step_bias, act, projected, gated_grad, masks, decay_log
):
    rows, width = act.shape[0], scan_width
    count = decay_log.shape[0]
    columns = selected.shape[0]
    rank = step_weight.shape[0]
    return call(
        ends_kernel,
        "scan_ends",
        width,
        [
            whole_spec(columns, rows),
            whole_spec(columns, rows),
            column_spec(rank, part),
            column_spec(1, part),
            column_spec(rows, part),
            part_spec(1, rows, part),
            column_spec(rows, part),
            whole_spec(rows, masks.shape[1]),
            column_spec(count, part),
        ],
        [column_spec(rows), column_spec(rows), column_spec(2 * count + 8)],
        [
            jax.ShapeDtypeStruct((rows, width), f32),
            jax.ShapeDtypeStruct((rows, width), f32),
            jax.ShapeDtypeStruct((2 * count + 8, width), f32),
        ],
        [pltpu.VMEM((2 * count, rows), f32)] + [pltpu.VMEM((rows, scan_width), f32)] * 3,
        5_000_000_000,
        selected,
        other,
        step_weight,
        step_bias,
        act,
        projected,
        gated_grad,
        masks,
        decay_log,
    )


def lane_tiles(values):
    return [values[:, k : k + lanes] for k in range(0, values.shape[1], lanes)]


def tree_sum(parts):
    while len(parts) > 1:
        odd = parts[len(parts) // 2 * 2 :]
        parts = [a + b for a, b in zip(parts[0::2], parts[1::2])] + odd
    return parts[0]


def keep_halves(scratch, i, values):
    for k, tile in enumerate(lane_tiles(values)):
        at = (k * body_rows + i) * 8
        scratch[at : at + 8, :] = tile[:8] + tile[8:]


def put_state_sums(scratch, out_ref, block):
    for group in range(body_rows // 8):
        row = pl.ds(pl.multiple_of(block * body_rows + group * 8, 8), 8)
        for k in range(out_ref.shape[1] // lanes):
            at = (k * body_rows + group * 8) * 8
            total = tree_sum([scratch[pl.ds(at + n, 8, stride=8), :] for n in range(8)])
            out_ref[row, k * lanes : (k + 1) * lanes] = total


def lane_sums(values):
    ones = jnp.ones((8, lanes), bf16)
    high = values.astype(bf16)
    low = (values - high.astype(f32)).astype(bf16)
    total = lax.dot_general(ones, high, contract_last, preferred_element_type=f32)
    total += lax.dot_general(ones, low, contract_last, preferred_element_type=f32)
    return total[:1, :]


def scan_kernel(
    selected_ref,
    other_ref,
    step_pre_ref,
    step_ref,
    act_ref,
    gate_ref,
    gated_grad_ref,
    mask_ref,
    decay_log_ref,
    entry_ref,
    tail_ref,
    skip_ref,
    step_weight_ref,
    before_ref,
    *rest,
    waits,
):
    (
        pair_ref,
        act_grad_ref,
        select_grad_ref,
        small_ref,
        coef,
        held_step,
        drive,
        scan_grad,
        scanned,
        weighted,
        states,
        factors,
        halves,
        more_halves,
        in_sum,
        read_sum,
    ) = rest[waits:]
    rows = step_ref.shape[0]
    count = decay_log_ref.shape[0]
    rank = step_weight_ref.shape[0]
    blocks = rows // body_rows
    decay = -jnp.exp(decay_log_ref[...])
    decay2 = decay * log2e
    selected = selected_ref[...] + other_ref[...]
    coef[...] = selected[rank:, :]
    step_low = selected[:rank, :].astype(bf16)
    step = step_ref[...]
    act = act_ref[...].astype(f32)
    held_step[...] = jnp.where(mask_ref[:, 1:2] > 0.0, step, reset_step)
    drive[...] = step * act
    states[:count, :] = entry_ref[...]

    def at_token(t):
        return pl.ds(pl.multiple_of(t * count, count), count)

    def forward(block, state):
        columns = coef_columns(coef, block)
        for i in range(body_rows):
            t = block * body_rows + i
            row = pl.ds(t, 1)
            factor = jnp.exp2(held_step[row, :] * decay2)
            state = factor * state + columns[:count, i : i + 1] * drive[row, :]
            factors[at_token(t), :] = factor
            states[at_token(t + 1), :] = state
            keep_halves(halves, i, columns[count:, i : i + 1] * state)
        put_state_sums(halves, scanned, block)
        return state

    lax.fori_loop(0, blocks, forward, entry_ref[...])

    gate = gate_ref[...].astype(f32)
    logistic = jax.nn.sigmoid(gate)
    gate_act = gate * logistic
    gated_grad = gated_grad_ref[...]
    grads = gated_grad * gate_act
    scan_grad[...] = grads
    total = scanned[...] + skip_ref[...] * act
    pair_ref[0] = (total * gate_act).astype(bf16)
    slope = logistic * (1.0 + gate * (1.0 - logistic))
    pair_ref[1] = (gated_grad * total * slope).astype(bf16)
    small_ref[rank + count : rank + count + 1, :] = jnp.sum(grads * act, axis=0, keepdims=True)

    def backward(k, carried):
        adjoint, decay_grad = carried
        block = blocks - 1 - k
        columns = coef_columns(coef, block)
        for i in range(body_rows - 1, -1, -1):
            t = block * body_rows + i
            row = pl.ds(t, 1)
            grad = scan_grad[row, :]
            summed = columns[count:, i : i + 1] * grad + adjoint
            read_sum[at_token(t), :] = tree_sum(lane_tiles(grad * states[at_token(t + 1), :]))
            in_sum[at_token(t), :] = tree_sum(lane_tiles(summed * drive[row, :]))
            keep_halves(halves, i, summed * columns[:count, i : i + 1])
            adjoint = factors[at_token(t), :] * summed
            held = adjoint * states[at_token(t), :]
            decay_grad = decay_grad + held * step_ref[row, :]
            keep_halves(more_halves, i, held * decay)
        put_state_sums(halves, weighted, block)
        put_state_sums(more_halves, scanned, block)
        return adjoint, decay_grad

    ignored, decay_grad = lax.fori_loop(
        0, blocks, backward, (tail_ref[...], jnp.zeros(decay.shape, f32))
    )
    act_grad_ref[...] = step * weighted[...] + skip_ref[...] * scan_grad[...]
    step_grad = act * weighted[...] + scanned[...]
    pre_grad = (step_grad * jax.nn.sigmoid(step_pre_ref[...])).astype(bf16)
    small_ref[:rank, :] = jnp.dot(step_low, pre_grad, preferred_element_type=f32)
    small_ref[rank : rank + count, :] = decay_grad * decay
    bias_grad = jnp.sum(pre_grad.astype(f32), axis=0, keepdims=True)
    small_ref[rank + count + 1 : rank + count + 2, :] = bias_grad
    spare = small_ref.shape[0] - (rank + count + 2)
    small_ref[rank + count + 2 :, :] = jnp.zeros((spare, small_ref.shape[1]), f32)
    before = before_ref[...]
    select_grad_ref[:rank, :] = before[:rank] + lax.dot_general(
        step_weight_ref[...], pre_grad, contract_last, preferred_element_type=f32
    )
    for n in range(count):
        at = pl.ds(n, rows, stride=count)
        low, high = rank + n, rank + count + n
        select_grad_ref[low : low + 1, :] = before[low : low + 1] + lane_sums(in_sum[at, :])
        select_grad_ref[high : high + 1, :] = before[high : high + 1] + lane_sums(read_sum[at, :])


def scan_full(
    part,
    selected,
    other,
    step_pre,
    step,
    act,
    projected,
    gated_grad,
    masks,
    decay_log,
    entry,
    tail,
    skip_gain,
    step_weight,
    before,
    waits,
):
    rows, width = step.shape
    count = decay_log.shape[0]
    columns = selected.shape[0]
    rank = step_weight.shape[0]
    half_rows = 8 * body_rows * (scan_width // lanes)
    small = rank + count + 16
    return call(
        functools.partial(scan_kernel, waits=len(waits)),
        "scan_full",
        width,
        [
            whole_spec(columns, rows),
            whole_spec(columns, rows),
            column_spec(rows),
            column_spec(rows),
            column_spec(rows, part),
            part_spec(1, rows, part),
            column_spec(rows, part),
            whole_spec(rows, masks.shape[1]),
            column_spec(count, part),
            column_spec(count),
            column_spec(count),
            column_spec(1, part),
            column_spec(rank, part),
            whole_spec(columns, rows),
        ]
        + [pl.BlockSpec(memory_space=pl.ANY)] * len(waits),
        [
            pl.BlockSpec((2, rows, scan_width), lambda j: (0, 0, j)),
            column_spec(rows),
            whole_spec(columns, rows),
            column_spec(small),
        ],
        [
            jax.ShapeDtypeStruct((2, rows, width), bf16),
            jax.ShapeDtypeStruct((rows, width), f32),
            jax.ShapeDtypeStruct((columns, rows), f32),
            jax.ShapeDtypeStruct((small, width), f32),
        ],
        [pltpu.VMEM((2 * count, rows), f32)]
        + [pltpu.VMEM((rows, scan_width), f32)] * 5
        + [
            pltpu.VMEM(((rows + 1) * count, scan_width), f32),
            pltpu.VMEM((rows * count, scan_width), f32),
            pltpu.VMEM((half_rows, lanes), f32),
            pltpu.VMEM((half_rows, lanes), f32),
            pltpu.VMEM((rows * count, lanes), f32),
            pltpu.VMEM((rows * count, lanes), f32),
        ],
        13_000_000_000,
        selected,
        other,
        step_pre,
        step,
        act,
        projected,
        gated_grad,
        masks,
        decay_log,
        entry,
        tail,
        skip_gain,
        step_weight,
        before,
        *waits,
    )


def conv_grad_kernel(
    select_grad_ref,
    other_ref,
    select_ref,
    act_grad_ref,
    convolved_ref,
    act_ref,
    inner_ref,
    conv_weight_ref,
    mask_ref,
    inner_grad_ref,
    edge_ref,
    small_ref,
    inner,
    shifted,
):
    rows = act_ref.shape[0]
    taps = conv_weight_ref.shape[0]
    columns = select_ref.shape[0]
    select_grad = (select_grad_ref[...] + other_ref[...]).astype(bf16)
    total = act_grad_ref[...] + lax.dot_general(
        select_grad, select_ref[...], contract_first, preferred_element_type=f32
    )
    conv_grad = total * silu_slope(convolved_ref[...])
    small_ref[:columns, :] = jnp.dot(select_grad, act_ref[...], preferred_element_type=f32)
    inner[:halo, :] = inner_ref[rows:, :].astype(f32)
    inner[halo:, :] = inner_ref[:rows, :].astype(f32)
    edges = jnp.zeros((8, conv_grad.shape[1]), f32)
    shifted[:8, :] = edges
    shifted[rows + 8 :, :] = edges
    out = conv_weight_ref[taps - 1 :, :] * conv_grad
    before = edges
    small_ref[columns + taps - 1 : columns + taps, :] = jnp.sum(
        conv_grad * inner[halo:, :], axis=0, keepdims=True
    )
    for lag in range(1, taps):
        masked = conv_grad * mask_ref[:, lag : lag + 1]
        at = taps - 1 - lag
        small_ref[columns + at : columns + at + 1, :] = jnp.sum(
            masked * inner[pl.ds(halo - lag, rows), :], axis=0, keepdims=True
        )
        shifted[8 : rows + 8, :] = masked
        weight = conv_weight_ref[at : at + 1, :]
        out = out + weight * shifted[pl.ds(8 + lag, rows), :]
        before = before + weight * shifted[pl.ds(lag, 8), :]
    small_ref[columns + taps : columns + taps + 1, :] = jnp.sum(conv_grad, axis=0, keepdims=True)
    spare = small_ref.shape[0] - (columns + taps + 1)
    small_ref[columns + taps + 1 :, :] = jnp.zeros((spare, small_ref.shape[1]), f32)
    inner_grad_ref[...] = out.astype(bf16)
    edge_ref[:8, :] = before
    edge_ref[8:, :] = out[rows - 8 :, :]


def convolve_grad(
    part, select_grad, other, select_weight, act_grad, convolved, act, projected, conv_weight, masks
):
    rows, width = act_grad.shape
    extended = rows + halo
    columns = select_weight.shape[0]
    taps = conv_weight.shape[0]
    small = columns + 16
    return call(
        conv_grad_kernel,
        "convolve_grad",
        width,
        [
            whole_spec(columns, rows),
            whole_spec(columns, rows),
            column_spec(columns, part),
            column_spec(rows),
            column_spec(rows, part),
            column_spec(rows, part),
            part_spec(0, extended, part),
            column_spec(taps, part),
            whole_spec(rows, masks.shape[1]),
        ],
        [column_spec(rows), column_spec(16), column_spec(small)],
        [
            jax.ShapeDtypeStruct((rows, width), bf16),
            jax.ShapeDtypeStruct((16, width), f32),
            jax.ShapeDtypeStruct((small, width), f32),
        ],
        [pltpu.VMEM((extended, scan_width), f32), pltpu.VMEM((rows + 16, scan_width), f32)],
        3_000_000_000,
        select_grad,
        other,
        select_weight,
        act_grad,
        convolved,
        act,
        projected,
        conv_weight,
        masks,
    )


def normalize_kernel(
    own_ref, other_ref, edge_ref, other_edge_ref, gain_ref, whole_ref, normed_ref, inverse_ref
):
    rows, half = own_ref.shape
    right = lax.axis_index("narrow") == 1
    for at, own, other in ((0, own_ref, other_ref), (rows, edge_ref, other_edge_ref)):
        end = at + own.shape[0]
        whole_ref[at:end, :half] = jnp.where(right, other[...], own[...])
        whole_ref[at:end, half:] = jnp.where(right, own[...], other[...])
    whole = whole_ref[...].astype(f32)
    inverse = lax.rsqrt(jnp.mean(whole * whole, axis=1, keepdims=True) + epsilon)
    normed_ref[...] = (whole * inverse * gain_ref[...]).astype(bf16)
    inverse_ref[...] = inverse[:rows]


def normalized(own, other, edge, other_edge, gain):
    rows, half = own.shape
    extended = rows + edge.shape[0]
    return pl.pallas_call(
        normalize_kernel,
        out_shape=[
            jax.ShapeDtypeStruct((extended, 2 * half), bf16),
            jax.ShapeDtypeStruct((extended, 2 * half), bf16),
            jax.ShapeDtypeStruct((rows, 1), f32),
        ],
        name="normalized",
    )(own, other, edge, other_edge, gain)


def edge_kernel(ids_ref, tokens_ref, out_ref):
    rows = ids_ref.shape[0]
    taps = 4
    out_ref[...] = tokens_ref[...]
    place = lax.broadcasted_iota(jnp.int32, (halo, 1), 0)
    same = jnp.zeros((halo, 1), f32)
    for lag in range(taps):
        here = jnp.where(ids_ref[rows - 1 - lag] == ids_ref[rows - 1], 1.0, 0.0)
        same = same + jnp.where(place == halo - 1 - lag, here, 0.0)
    out_ref[...] = (tokens_ref[...].astype(f32) * same).astype(bf16)


def edge_rows_of(ids, tokens):
    rows, width = tokens.shape
    return pl.pallas_call(
        edge_kernel,
        grid=(1,),
        in_specs=[
            pl.BlockSpec(memory_space=pltpu.SMEM),
            pl.BlockSpec((halo, width), lambda j: (rows // halo - 1, 0)),
        ],
        out_specs=pl.BlockSpec((halo, width), lambda j: (0, 0)),
        out_shape=jax.ShapeDtypeStruct((halo, width), bf16),
        name="edge_rows",
    )(ids, tokens)


def quarter_kernel(
    place_ref, own_ref, near_ref, far_ref, last_ref, normed_ref, small_ref, keep_ref, send_refs, piece
):
    total = None
    for n, grads in enumerate((own_ref, near_ref, far_ref, last_ref)):
        part = lax.dot_general(normed_ref[n], grads[...], contract_first, preferred_element_type=f32)
        total = part if total is None else total + part
    piece[...] = total
    for n in range(4):
        block = place_ref[0] ^ n
        rows, spare = piece.shape[0] // 4, small_ref.shape[0] // 4
        inner = piece[pl.ds(pl.multiple_of(block * rows, rows), rows), :]
        small = small_ref[pl.ds(pl.multiple_of(block * spare, spare), spare), :]
        if n == 0:
            keep_ref[:rows, :] = inner
            keep_ref[rows:, :] = small
        else:
            send_refs[n - 1, :rows, :] = inner.astype(bf16)
            send_refs[n - 1, rows:, :] = small.astype(bf16)


def inner_quarter(place, own, near, far, last, normed, small):
    width = own.shape[1]
    quarter = normed.shape[2]
    rows = (quarter + small.shape[0]) // 4
    return pl.pallas_call(
        quarter_kernel,
        in_specs=[pl.BlockSpec(memory_space=pltpu.SMEM)]
        + [pl.BlockSpec(memory_space=pltpu.VMEM)] * 6,
        out_shape=[
            jax.ShapeDtypeStruct((rows, width), f32),
            jax.ShapeDtypeStruct((3, rows, width), bf16),
        ],
        scratch_shapes=[pltpu.VMEM((quarter, width), f32)],
        compiler_params=pltpu.CompilerParams(vmem_limit_bytes=vmem_bytes),
        cost_estimate=pl.CostEstimate(
            flops=2_000_000_000, bytes_accessed=4_000_000, transcendentals=0
        ),
        name="inner_quarter",
    )(place, own, near, far, last, normed, small)


def join_kernel(place_ref, first_ref, second_ref, inner_ref, *rest):
    out_ref, small_ref = rest[-2:]
    half = out_ref.shape[2] // 2
    rows, spare = out_ref.shape[0] // 2, small_ref.shape[0] // 2
    out_ref[:, 1, :half] = first_ref[...].astype(f32)
    out_ref[:, 1, half:] = second_ref[...].astype(f32)
    for n in range(2):
        at = n * (rows + spare)
        block = inner_ref[at : at + rows + spare, :].astype(f32)
        out_ref[n * rows : (n + 1) * rows, 0, :] = block[:rows]
        small_ref[n * spare : (n + 1) * spare, :] = block[rows:]


def joined(place, flip, first, second, inner, before, waits):
    depth = first.shape[0]
    quarter, width = depth // 4, 2 * scan_width
    small = inner.shape[0] - quarter

    def source(j, place):
        number = place[0] ^ flip
        return 4 + 2 * lax.rem(number, 2) + j, number // 2

    untouched = [*before, *waits]
    return pl.pallas_call(
        join_kernel,
        grid_spec=pltpu.PrefetchScalarGridSpec(
            num_scalar_prefetch=1,
            grid=(2,),
            in_specs=[
                pl.BlockSpec((quarter // 2, scan_width), source),
                pl.BlockSpec((quarter // 2, scan_width), source),
                pl.BlockSpec((inner.shape[0] // 2, width), lambda j, place: (j, 0)),
            ]
            + [pl.BlockSpec(memory_space=pl.ANY)] * len(untouched),
            out_specs=[
                pl.BlockSpec(
                    (quarter // 2, 2, width), lambda j, place: (2 * (place[0] ^ flip) + j, 0, 0)
                ),
                pl.BlockSpec((small // 2, width), lambda j, place: (2 * (place[0] ^ flip) + j, 0)),
            ],
        ),
        out_shape=[
            jax.ShapeDtypeStruct((depth, 2, width), f32),
            jax.ShapeDtypeStruct((4 * small, width), f32),
        ],
        input_output_aliases={4 + k: k for k in range(len(before))},
        compiler_params=pltpu.CompilerParams(vmem_limit_bytes=vmem_bytes),
        name="joined",
    )(place, first, second, inner, *untouched)


def carried(ends, decay):
    count = decay.shape[0]
    place = lax.axis_index("wide")

    def split(packed):
        return packed[:count], packed[count : 2 * count], packed[2 * count : 2 * count + 1]

    def through(total):
        return jnp.exp(decay * total)

    zero = jnp.zeros(decay.shape, f32)
    none = jnp.zeros((1, decay.shape[1]), f32)
    before, before_steps, after, after_steps = zero, none, zero, none
    packed = ends
    for bit in (1, 2):
        second = (place & bit) != 0
        own = split(packed)
        other = split(swapped(packed, "wide", bit))
        early = [jnp.where(second, b, a) for a, b in zip(own, other)]
        late = [jnp.where(second, a, b) for a, b in zip(own, other)]
        before = before + jnp.where(second, through(before_steps) * other[0], 0.0)
        before_steps = before_steps + jnp.where(second, other[2], 0.0)
        after = after + jnp.where(second, 0.0, through(after_steps) * other[1])
        after_steps = after_steps + jnp.where(second, 0.0, other[2])
        state = late[0] + through(late[2]) * early[0]
        adjoint = early[1] + through(early[2]) * late[1]
        packed = jnp.concatenate(
            [state, adjoint, jnp.broadcast_to(early[2] + late[2], (8, decay.shape[1]))]
        )
    from_before = passed_along(packed[:count], "wide", 4)
    from_after = passed_along(packed[count : 2 * count], "wide", -4)
    return (
        before + through(before_steps) * from_before,
        after + through(after_steps) * from_after,
    )


def local(
    tokens,
    norm_gain,
    in_weight,
    conv_weight,
    conv_bias,
    select_weight,
    step_weight,
    step_bias,
    decay_log,
    skip_gain,
    out_weight,
    segment_ids,
    cotangent,
):
    rows, features = tokens.shape
    taps = conv_weight.shape[0]
    columns = select_weight.shape[0]
    rank = step_weight.shape[0]
    count = decay_log.shape[0]
    right_half = lax.axis_index("narrow") == 1

    def both_halves(own, other):
        return jnp.concatenate(
            [jnp.where(right_half, other, own), jnp.where(right_half, own, other)], axis=1
        )

    other_tokens = swapped(tokens, "narrow", 1)
    other_cot = swapped(cotangent, "narrow", 1)
    edge, other_edge = to_next_both(edge_rows_of(segment_ids, tokens))

    same_as_last = (segment_ids[rows - 8 :] == segment_ids[rows - 1 :])[:, None]
    padded_ids = jnp.concatenate([jnp.broadcast_to(segment_ids[:1], (taps - 1,)), segment_ids])
    masks = jnp.stack(
        [
            (padded_ids[taps - 1 - lag : taps - 1 - lag + rows] == segment_ids).astype(f32)
            for lag in range(taps)
        ]
        + [jnp.zeros((rows,), f32)] * (8 - taps),
        axis=1,
    )
    whole_ext, normed_ext, inverse = normalized(
        tokens, other_tokens, edge, other_edge, norm_gain[None]
    )
    projected = jnp.einsum(
        "td,dce->cte", normed_ext, in_weight, preferred_element_type=f32
    ).astype(bf16)
    convolved, act, selected = convolve(
        projected, conv_weight, conv_bias[None], select_weight, masks
    )
    other_selected = swapped(selected, "narrow", 1)
    cot_whole = both_halves(cotangent, other_cot)
    gated_grad = lax.dot_general(
        cot_whole, out_weight, contract_last, preferred_element_type=f32
    )
    parts = range(out_weight.shape[0] // scan_width)
    decay = -jnp.exp(decay_log)
    started = []
    for part in parts:
        step_pre, step, ends = scan_ends(
            part,
            selected,
            other_selected,
            step_weight,
            step_bias[None],
            act,
            projected,
            gated_grad,
            masks,
            decay_log,
        )
        here = decay[:, part * scan_width : (part + 1) * scan_width]
        started.append((step_pre, step, carried(ends, here)))
    normed = normed_ext[:rows]
    normed_four = quarter_of_four(normed)
    select_grad = jnp.zeros(selected.shape, f32)
    waits = [[started[-1][2][0]], [normed_four]]
    done, sums = [], []
    for part in parts:
        step_pre, step, (entry, tail) = started[part]
        pair, act_grad, select_grad, small = scan_full(
            part,
            selected,
            other_selected,
            step_pre,
            step,
            act,
            projected,
            gated_grad,
            masks,
            decay_log,
            entry,
            tail,
            skip_gain[None],
            step_weight,
            select_grad,
            waits[part],
        )
        done.append((pair, act_grad, small))
        out_rows = lax.dot_general(pair[0], cot_whole, contract_first, preferred_element_type=f32)
        gate_rows = lax.dot_general(normed, pair[1], contract_first, preferred_element_type=f32)
        half = gate_rows.shape[0] // 2
        product = jnp.concatenate(
            [out_rows, jnp.concatenate([gate_rows[:half], gate_rows[half:]], axis=1)]
        ).astype(bf16)
        waits[-1].append(product)
        if part == 0:
            share = lax.psum_scatter(product, "wide", scatter_dimension=0, tiled=True)
            sums.append(lax.all_gather(share, "wide", axis=0, tiled=True))
        else:
            sums.append(lax.psum(product, "wide"))
    other_select_grad = swapped(select_grad, "narrow", 1)
    scan_small = jnp.concatenate([small for _, _, small in done], axis=1)
    gated = jnp.concatenate([pair[0] for pair, _, _ in done], axis=1)
    gate_grad = jnp.concatenate([pair[1] for pair, _, _ in done], axis=1)

    def narrow_halves(array):
        low, high = array[:, :features], array[:, features:]
        return jnp.where(right_half, high, low), jnp.where(right_half, low, high)

    out_part = jnp.dot(gated, out_weight, preferred_element_type=f32)
    out_mine, out_other = narrow_halves(out_part)
    out_sum = out_mine + swapped(out_other, "narrow", 1)
    layer_out = (tokens.astype(f32) + out_sum).astype(bf16)

    results = [
        convolve_grad(
            part,
            select_grad,
            other_select_grad,
            select_weight,
            done[part][1],
            convolved,
            act,
            projected,
            conv_weight,
            masks,
        )
        for part in parts
    ]
    inner_main, edges, conv_small = [jnp.concatenate(x, axis=1) for x in zip(*results)]
    from_next = passed_along(edges[:8], "wide", -1)
    last_rows = edges[8:] + jnp.where(same_as_last, from_next, 0.0)
    inner_grad = jnp.concatenate([inner_main[: rows - 8], last_rows.astype(bf16)])
    normed_part = jnp.einsum(
        "cte,dce->td", jnp.stack([inner_grad, gate_grad]), in_weight, preferred_element_type=f32
    )
    whole = whole_ext[:rows].astype(f32)
    gain_part = jnp.sum(normed_part * whole * inverse, axis=0, keepdims=True)
    row_part = jnp.sum(normed_part * norm_gain * whole, axis=1, keepdims=True)

    spare = -(scan_small.shape[0] + conv_small.shape[0] + 1) % 256
    small = jnp.concatenate(
        [scan_small, conv_small, gain_part, jnp.zeros((spare, gain_part.shape[1]), f32)]
    )
    small_piece = scattered(small, (1, 2))
    near = swapped(inner_grad, "wide", 2)
    wide_place = lax.axis_index("wide").astype(jnp.int32)
    keep, sends = inner_quarter(
        (wide_place >> 2 & 3)[None],
        inner_grad,
        near,
        swapped(inner_grad, "wide", 1),
        swapped(near, "wide", 1),
        normed_four,
        small_piece,
    )
    first_bits, *more_bits = group_bits(2)
    held = keep
    for n, flip in enumerate(flips(first_bits)[1:]):
        held = held + swapped(sends[n], "wide", flip).astype(f32)
    for bits in more_bits:
        held = scattered(held, bits)
    held = held.astype(bf16)
    for bits in reversed(group_bits(2)):
        held = gathered(held, bits)
    normed_mine, normed_other = narrow_halves(normed_part)
    row_sum = row_part + swapped(row_part, "narrow", 1)
    normed_sum = normed_mine + swapped(normed_other, "narrow", 1)
    gain_mine = jnp.where(right_half, norm_gain[features:], norm_gain[:features])
    whole_grad = inverse * (gain_mine * normed_sum) - tokens.astype(f32) * (
        inverse * inverse * inverse
    ) * (row_sum / (2 * features))
    tokens_grad = (whole_grad + cotangent.astype(f32)).astype(bf16)

    out_weight_grad = jnp.concatenate([total[:scan_width] for total in sums]).astype(f32)
    near = swapped(held, "wide", 2)
    quarters = (held, swapped(held, "wide", 1), near, swapped(near, "wide", 1))
    results = []
    for flip, quarter in enumerate(quarters):
        results = joined(
            (wide_place & 3)[None],
            flip,
            *sums,
            quarter,
            results,
            [layer_out, tokens_grad, out_weight_grad] if flip == 2 else [],
        )
    in_weight_grad, small_sum = results
    scan_sum = small_sum[: scan_small.shape[0]]
    conv_sum = small_sum[scan_small.shape[0] : scan_small.shape[0] + conv_small.shape[0]]
    gain_row = scan_small.shape[0] + conv_small.shape[0]
    gain_sum = small_sum[gain_row : gain_row + 1]
    norm_gain_grad = (gain_sum + swapped(gain_sum, "narrow", 1))[0]
    return (
        layer_out,
        tokens_grad,
        norm_gain_grad,
        in_weight_grad,
        conv_sum[columns : columns + taps],
        conv_sum[columns + taps],
        conv_sum[:columns],
        scan_sum[:rank],
        scan_sum[rank + count + 1],
        scan_sum[rank : rank + count],
        scan_sum[rank + count],
        out_weight_grad,
    )


def solution(mesh):
    placed = (
        P("wide", "narrow"),
        P(),
        P(None, None, "narrow"),
        P(None, "narrow"),
        P("narrow"),
        P(None, "narrow"),
        P(None, "narrow"),
        P("narrow"),
        P(None, "narrow"),
        P("narrow"),
        P("narrow", None),
        P("wide"),
        P("wide", "narrow"),
    )
    return jax.shard_map(
        local,
        mesh=mesh,
        in_specs=placed,
        out_specs=(
            P("wide", "narrow"),
            P("wide", "narrow"),
            P(),
            P(None, None, "narrow"),
            P(None, "narrow"),
            P("narrow"),
            P(None, "narrow"),
            P(None, "narrow"),
            P("narrow"),
            P(None, "narrow"),
            P("narrow"),
            P("narrow", None),
        ),
        check_vma=False,
    )
```

```python
import functools

import jax
import jax.numpy as jnp
from jax import lax
from jax.experimental import pallas as pl
from jax.experimental.pallas import tpu as pltpu
from jax.sharding import PartitionSpec as P

epsilon = 1e-05
log2e = 1.4426950408889634
reset_step = 1e30
lanes = 128
halo = 16
body_rows = 32
scan_width = 512
vmem_bytes = 56 * 1024 * 1024
f32 = jnp.float32
bf16 = jnp.bfloat16
contract_first = (((0,), (0,)), ((), ()))
contract_last = (((1,), (1,)), ((), ()))


def passed_along(array, axis, by):
    peers = lax.axis_size(axis)
    pairs = [(i, i + by) for i in range(peers) if 0 <= i + by < peers]
    return lax.ppermute(array, axis, pairs)


def swapped(array, axis, bit):
    peers = lax.axis_size(axis)
    return lax.ppermute(array, axis, [(i, i ^ bit) for i in range(peers)])


def wide_bits():
    bit, bits = 1, []
    while bit < lax.axis_size("wide"):
        bits.append(bit)
        bit *= 2
    return bits


def to_next_both(array):
    count, sides = lax.axis_size("wide"), lax.axis_size("narrow")
    pairs = [
        (i * sides + k, (i + 1) * sides + (sides - 1 - k))
        for i in range(count - 1)
        for k in range(sides)
    ]
    return passed_along(array, "wide", 1), lax.ppermute(array, ("wide", "narrow"), pairs)


def is_upper(bit):
    return (lax.axis_index("wide") & bit) != 0


def group_bits(size):
    bits, bit = [], 4
    while bit < lax.axis_size("wide"):
        bits.append(bit)
        bit *= 2
    return [tuple(bits[k : k + size]) for k in range(0, len(bits), size)]


def flips(bits):
    return [sum(b for k, b in enumerate(bits) if n >> k & 1) for n in range(2 ** len(bits))]


def scattered(piece, bits):
    rows = piece.shape[0] // 2 ** len(bits)
    here = sum(is_upper(b).astype(jnp.int32) << k for k, b in enumerate(bits))

    def block(n):
        return lax.dynamic_slice_in_dim(piece, (here ^ n) * rows, rows, 0)

    total = block(0).astype(f32)
    for n, flip in enumerate(flips(bits)):
        if n > 0:
            total = total + swapped(block(n).astype(bf16), "wide", flip).astype(f32)
    return total


def gathered(held, bits):
    blocks = [held] + [swapped(held, "wide", flip) for flip in flips(bits)[1:]]
    for bit in bits:
        upper = is_upper(bit)
        blocks = [
            jnp.concatenate([jnp.where(upper, b, a), jnp.where(upper, a, b)])
            for a, b in zip(blocks[0::2], blocks[1::2])
        ]
    return blocks[0]


def quarter_of_four(array):
    width = array.shape[1] // 4
    here = lax.axis_index("wide") & 3

    def quarter(n):
        return lax.dynamic_slice_in_dim(array, (here ^ n) * width, width, 1)

    return jnp.stack(
        [quarter(0)] + [swapped(quarter(n), "wide", n) for n in (2, 1, 3)]
    )


def silu_slope(values):
    logistic = jax.nn.sigmoid(values)
    return logistic * (1.0 + values * (1.0 - logistic))


def softplus(values):
    return jnp.maximum(values, 0.0) + jnp.log1p(jnp.exp(-jnp.abs(values)))


def column_spec(rows, start=0):
    return pl.BlockSpec((rows, scan_width), lambda j: (0, start + j))


def part_spec(part, rows, start=0):
    return pl.BlockSpec((None, rows, scan_width), lambda j: (part, 0, start + j))


def whole_spec(rows, width):
    return pl.BlockSpec((rows, width), lambda j: (0, 0))


def call(kernel, name, width, in_specs, out_specs, out_shape, scratch, flops, *operands):
    moved = sum(a.size * a.dtype.itemsize for a in operands)
    return pl.pallas_call(
        kernel,
        grid=(width // scan_width,),
        in_specs=in_specs,
        out_specs=out_specs,
        out_shape=out_shape,
        scratch_shapes=scratch,
        compiler_params=pltpu.CompilerParams(vmem_limit_bytes=vmem_bytes),
        cost_estimate=pl.CostEstimate(flops=flops, bytes_accessed=moved, transcendentals=0),
        name=name,
    )(*operands)


def conv_kernel(
    inner_ref,
    conv_weight_ref,
    conv_bias_ref,
    select_ref,
    mask_ref,
    convolved_ref,
    act_ref,
    selected_ref,
    inner,
):
    rows = act_ref.shape[0]
    taps = conv_weight_ref.shape[0]
    inner[:halo, :] = inner_ref[rows:, :].astype(f32)
    inner[halo:, :] = inner_ref[:rows, :].astype(f32)
    total = conv_bias_ref[...] + conv_weight_ref[taps - 1 :, :] * inner[halo:, :]
    for lag in range(1, taps):
        earlier = inner[pl.ds(halo - lag, rows), :] * mask_ref[:, lag : lag + 1]
        total = total + conv_weight_ref[taps - 1 - lag : taps - lag, :] * earlier
    convolved_ref[...] = total
    act = (total * jax.nn.sigmoid(total)).astype(bf16)
    act_ref[...] = act
    part = lax.dot_general(select_ref[...], act, contract_last, preferred_element_type=f32)

    @pl.when(pl.program_id(0) == 0)
    def _():
        selected_ref[...] = part

    @pl.when(pl.program_id(0) > 0)
    def _():
        selected_ref[...] += part


def convolve(projected, conv_weight, conv_bias, select_weight, masks):
    parts, extended, width = projected.shape
    rows = extended - halo
    taps = conv_weight.shape[0]
    columns = select_weight.shape[0]
    return call(
        conv_kernel,
        "convolve",
        width,
        [
            part_spec(0, extended),
            column_spec(taps),
            column_spec(1),
            column_spec(columns),
            whole_spec(rows, masks.shape[1]),
        ],
        [column_spec(rows), column_spec(rows), whole_spec(columns, rows)],
        [
            jax.ShapeDtypeStruct((rows, width), f32),
            jax.ShapeDtypeStruct((rows, width), bf16),
            jax.ShapeDtypeStruct((columns, rows), f32),
        ],
        [pltpu.VMEM((extended, scan_width), f32)],
        4_000_000_000,
        projected,
        conv_weight,
        conv_bias,
        select_weight,
        masks,
    )


def coef_columns(coef, block):
    per_tile = lanes // body_rows
    start = pl.multiple_of((block // per_tile) * lanes, lanes)
    tile = coef[:, pl.ds(start, lanes)]
    back = body_rows * lax.rem(block, per_tile)
    return pltpu.roll(tile, lax.rem(lanes - back, lanes), 1)


def ends_kernel(
    selected_ref,
    other_ref,
    step_weight_ref,
    step_bias_ref,
    act_ref,
    gate_ref,
    gated_grad_ref,
    mask_ref,
    decay_log_ref,
    step_pre_ref,
    step_ref,
    ends_ref,
    coef,
    held_step,
    drive,
    scan_grad,
):
    rows = act_ref.shape[0]
    count = decay_log_ref.shape[0]
    rank = step_weight_ref.shape[0]
    decay2 = -jnp.exp(decay_log_ref[...]) * log2e
    selected = selected_ref[...] + other_ref[...]
    coef[...] = selected[rank:, :]
    step_low = selected[:rank, :].astype(bf16)
    step_pre = step_bias_ref[...] + lax.dot_general(
        step_low, step_weight_ref[...], contract_first, preferred_element_type=f32
    )
    step_pre_ref[...] = step_pre
    step = softplus(step_pre)
    step_ref[...] = step
    held_step[...] = jnp.where(mask_ref[:, 1:2] > 0.0, step, reset_step)
    drive[...] = step * act_ref[...].astype(f32)
    gate = gate_ref[...].astype(f32)
    scan_grad[...] = gated_grad_ref[...] * (gate * jax.nn.sigmoid(gate))
    zero = jnp.zeros(decay2.shape, f32)

    def body(block, carried):
        state, product, adjoint = carried
        columns = coef_columns(coef, block)
        for i in range(body_rows):
            row = pl.ds(block * body_rows + i, 1)
            factor = jnp.exp2(held_step[row, :] * decay2)
            state = factor * state + columns[:count, i : i + 1] * drive[row, :]
            product = factor * product
            adjoint = adjoint + product * (columns[count:, i : i + 1] * scan_grad[row, :])
        return state, product, adjoint

    state, product, adjoint = lax.fori_loop(0, rows // body_rows, body, (zero, zero + 1.0, zero))
    ends_ref[:count, :] = state
    ends_ref[count : 2 * count, :] = adjoint
    total = jnp.sum(held_step[...], axis=0, keepdims=True)
    ends_ref[2 * count :, :] = jnp.broadcast_to(total, (8, total.shape[1]))


def scan_ends(
    selected, other, step_weight, step_bias, act, projected, gated_grad, masks, decay_log
):
    rows, width = act.shape
    count = decay_log.shape[0]
    columns = selected.shape[0]
    rank = step_weight.shape[0]
    return call(
        ends_kernel,
        "scan_ends",
        width,
        [
            whole_spec(columns, rows),
            whole_spec(columns, rows),
            column_spec(rank),
            column_spec(1),
            column_spec(rows),
            part_spec(1, rows),
            column_spec(rows),
            whole_spec(rows, masks.shape[1]),
            column_spec(count),
        ],
        [column_spec(rows), column_spec(rows), column_spec(2 * count + 8)],
        [
            jax.ShapeDtypeStruct((rows, width), f32),
            jax.ShapeDtypeStruct((rows, width), f32),
            jax.ShapeDtypeStruct((2 * count + 8, width), f32),
        ],
        [pltpu.VMEM((2 * count, rows), f32)] + [pltpu.VMEM((rows, scan_width), f32)] * 3,
        10_000_000_000,
        selected,
        other,
        step_weight,
        step_bias,
        act,
        projected,
        gated_grad,
        masks,
        decay_log,
    )


def lane_tiles(values):
    return [values[:, k : k + lanes] for k in range(0, values.shape[1], lanes)]


def tree_sum(parts):
    while len(parts) > 1:
        odd = parts[len(parts) // 2 * 2 :]
        parts = [a + b for a, b in zip(parts[0::2], parts[1::2])] + odd
    return parts[0]


def keep_halves(scratch, i, values):
    for k, tile in enumerate(lane_tiles(values)):
        at = (k * body_rows + i) * 8
        scratch[at : at + 8, :] = tile[:8] + tile[8:]


def put_state_sums(scratch, out_ref, block):
    for group in range(body_rows // 8):
        row = pl.ds(pl.multiple_of(block * body_rows + group * 8, 8), 8)
        for k in range(out_ref.shape[1] // lanes):
            at = (k * body_rows + group * 8) * 8
            total = tree_sum([scratch[pl.ds(at + n, 8, stride=8), :] for n in range(8)])
            out_ref[row, k * lanes : (k + 1) * lanes] = total


def lane_sums(values):
    ones = jnp.ones((8, lanes), bf16)
    high = values.astype(bf16)
    low = (values - high.astype(f32)).astype(bf16)
    total = lax.dot_general(ones, high, contract_last, preferred_element_type=f32)
    total += lax.dot_general(ones, low, contract_last, preferred_element_type=f32)
    return total[:1, :]


def at_token(t, count):
    return pl.ds(pl.multiple_of(t * count, count), count)


def forward_kernel(
    selected_ref,
    other_ref,
    step_ref,
    act_ref,
    gate_ref,
    gated_grad_ref,
    mask_ref,
    decay_log_ref,
    entry_ref,
    skip_ref,
    pair_ref,
    coef,
    held_step,
    drive,
    scanned,
    halves,
):
    rows = step_ref.shape[0]
    count = decay_log_ref.shape[0]
    rank = selected_ref.shape[0] - 2 * count
    decay2 = -jnp.exp(decay_log_ref[...]) * log2e
    coef[...] = selected_ref[rank:, :] + other_ref[rank:, :]
    act = act_ref[...].astype(f32)
    held_step[...] = jnp.where(mask_ref[:, 1:2] > 0.0, step_ref[...], reset_step)
    drive[...] = step_ref[...] * act

    def forward(block, state):
        columns = coef_columns(coef, block)
        for i in range(body_rows):
            row = pl.ds(block * body_rows + i, 1)
            factor = jnp.exp2(held_step[row, :] * decay2)
            state = factor * state + columns[:count, i : i + 1] * drive[row, :]
            keep_halves(halves, i, columns[count:, i : i + 1] * state)
        put_state_sums(halves, scanned, block)
        return state

    lax.fori_loop(0, rows // body_rows, forward, entry_ref[...])
    gate = gate_ref[...].astype(f32)
    logistic = jax.nn.sigmoid(gate)
    total = scanned[...] + skip_ref[...] * act
    pair_ref[0] = (total * (gate * logistic)).astype(bf16)
    slope = logistic * (1.0 + gate * (1.0 - logistic))
    pair_ref[1] = (gated_grad_ref[...] * total * slope).astype(bf16)


def scan_forward(
    selected, other, step, act, projected, gated_grad, masks, decay_log, entry, skip_gain
):
    rows, width = step.shape
    count = decay_log.shape[0]
    columns = selected.shape[0]
    return call(
        forward_kernel,
        "scan_forward",
        width,
        [
            whole_spec(columns, rows),
            whole_spec(columns, rows),
            column_spec(rows),
            column_spec(rows),
            part_spec(1, rows),
            column_spec(rows),
            whole_spec(rows, masks.shape[1]),
            column_spec(count),
            column_spec(count),
            column_spec(1),
        ],
        pl.BlockSpec((2, rows, scan_width), lambda j: (0, 0, j)),
        jax.ShapeDtypeStruct((2, rows, width), bf16),
        [pltpu.VMEM((2 * count, rows), f32)]
        + [pltpu.VMEM((rows, scan_width), f32)] * 3
        + [pltpu.VMEM((8 * body_rows * (scan_width // lanes), lanes), f32)],
        10_000_000_000,
        selected,
        other,
        step,
        act,
        projected,
        gated_grad,
        masks,
        decay_log,
        entry,
        skip_gain,
    )


def backward_kernel(
    selected_ref,
    other_ref,
    step_pre_ref,
    step_ref,
    act_ref,
    gate_ref,
    gated_grad_ref,
    mask_ref,
    decay_log_ref,
    entry_ref,
    tail_ref,
    skip_ref,
    step_weight_ref,
    *rest,
    waits,
):
    (
        act_grad_ref,
        select_grad_ref,
        small_ref,
        coef,
        held_step,
        drive,
        scan_grad,
        weighted,
        held_sum,
        states,
        factors,
        halves,
        more_halves,
        in_sum,
        read_sum,
    ) = rest[waits:]
    rows = step_ref.shape[0]
    count = decay_log_ref.shape[0]
    rank = step_weight_ref.shape[0]
    blocks = rows // body_rows
    decay = -jnp.exp(decay_log_ref[...])
    decay2 = decay * log2e
    selected = selected_ref[...] + other_ref[...]
    coef[...] = selected[rank:, :]
    step_low = selected[:rank, :].astype(bf16)
    step = step_ref[...]
    act = act_ref[...].astype(f32)
    held_step[...] = jnp.where(mask_ref[:, 1:2] > 0.0, step, reset_step)
    drive[...] = step * act
    gate = gate_ref[...].astype(f32)
    grads = gated_grad_ref[...] * (gate * jax.nn.sigmoid(gate))
    scan_grad[...] = grads
    small_ref[rank + count : rank + count + 1, :] = jnp.sum(grads * act, axis=0, keepdims=True)
    states[:count, :] = entry_ref[...]

    @pl.when(pl.program_id(0) == 0)
    def _():
        in_sum[...] = jnp.zeros(in_sum.shape, f32)
        read_sum[...] = jnp.zeros(read_sum.shape, f32)
        select_grad_ref[...] = jnp.zeros(select_grad_ref.shape, f32)

    def forward(block, state):
        columns = coef_columns(coef, block)
        for i in range(body_rows):
            t = block * body_rows + i
            row = pl.ds(t, 1)
            factor = jnp.exp2(held_step[row, :] * decay2)
            state = factor * state + columns[:count, i : i + 1] * drive[row, :]
            factors[at_token(t, count), :] = factor
            states[at_token(t + 1, count), :] = state
        return state

    lax.fori_loop(0, blocks, forward, entry_ref[...])

    def backward(k, carried):
        adjoint, decay_grad = carried
        block = blocks - 1 - k
        columns = coef_columns(coef, block)
        for i in range(body_rows - 1, -1, -1):
            t = block * body_rows + i
            row = pl.ds(t, 1)
            here = at_token(t, count)
            grad = scan_grad[row, :]
            summed = columns[count:, i : i + 1] * grad + adjoint
            read_sum[here, :] += tree_sum(lane_tiles(grad * states[at_token(t + 1, count), :]))
            in_sum[here, :] += tree_sum(lane_tiles(summed * drive[row, :]))
            keep_halves(halves, i, summed * columns[:count, i : i + 1])
            adjoint = factors[here, :] * summed
            held = adjoint * states[here, :]
            decay_grad = decay_grad + held * step_ref[row, :]
            keep_halves(more_halves, i, held * decay)
        put_state_sums(halves, weighted, block)
        put_state_sums(more_halves, held_sum, block)
        return adjoint, decay_grad

    ignored, decay_grad = lax.fori_loop(
        0, blocks, backward, (tail_ref[...], jnp.zeros(decay.shape, f32))
    )
    act_grad_ref[...] = step * weighted[...] + skip_ref[...] * scan_grad[...]
    step_grad = act * weighted[...] + held_sum[...]
    pre_grad = (step_grad * jax.nn.sigmoid(step_pre_ref[...])).astype(bf16)
    small_ref[:rank, :] = jnp.dot(step_low, pre_grad, preferred_element_type=f32)
    small_ref[rank : rank + count, :] = decay_grad * decay
    bias_grad = jnp.sum(pre_grad.astype(f32), axis=0, keepdims=True)
    small_ref[rank + count + 1 : rank + count + 2, :] = bias_grad
    spare = small_ref.shape[0] - (rank + count + 2)
    small_ref[rank + count + 2 :, :] = jnp.zeros((spare, small_ref.shape[1]), f32)
    select_grad_ref[:rank, :] += lax.dot_general(
        step_weight_ref[...], pre_grad, contract_last, preferred_element_type=f32
    )

    @pl.when(pl.program_id(0) == pl.num_programs(0) - 1)
    def _():
        for n in range(count):
            at = pl.ds(n, rows, stride=count)
            select_grad_ref[rank + n : rank + n + 1, :] = lane_sums(in_sum[at, :])
            select_grad_ref[rank + count + n : rank + count + n + 1, :] = lane_sums(read_sum[at, :])


def scan_backward(
    selected,
    other,
    step_pre,
    step,
    act,
    projected,
    gated_grad,
    masks,
    decay_log,
    entry,
    tail,
    skip_gain,
    step_weight,
    waits,
):
    rows, width = step.shape
    count = decay_log.shape[0]
    columns = selected.shape[0]
    rank = step_weight.shape[0]
    half_rows = 8 * body_rows * (scan_width // lanes)
    small = rank + count + 16
    return call(
        functools.partial(backward_kernel, waits=len(waits)),
        "scan_backward",
        width,
        [
            whole_spec(columns, rows),
            whole_spec(columns, rows),
            column_spec(rows),
            column_spec(rows),
            column_spec(rows),
            part_spec(1, rows),
            column_spec(rows),
            whole_spec(rows, masks.shape[1]),
            column_spec(count),
            column_spec(count),
            column_spec(count),
            column_spec(1),
            column_spec(rank),
        ]
        + [pl.BlockSpec(memory_space=pl.ANY)] * len(waits),
        [column_spec(rows), whole_spec(columns, rows), column_spec(small)],
        [
            jax.ShapeDtypeStruct((rows, width), f32),
            jax.ShapeDtypeStruct((columns, rows), f32),
            jax.ShapeDtypeStruct((small, width), f32),
        ],
        [pltpu.VMEM((2 * count, rows), f32)]
        + [pltpu.VMEM((rows, scan_width), f32)] * 5
        + [
            pltpu.VMEM(((rows + 1) * count, scan_width), f32),
            pltpu.VMEM((rows * count, scan_width), f32),
            pltpu.VMEM((half_rows, lanes), f32),
            pltpu.VMEM((half_rows, lanes), f32),
            pltpu.VMEM((rows * count, lanes), f32),
            pltpu.VMEM((rows * count, lanes), f32),
        ],
        22_000_000_000,
        selected,
        other,
        step_pre,
        step,
        act,
        projected,
        gated_grad,
        masks,
        decay_log,
        entry,
        tail,
        skip_gain,
        step_weight,
        *waits,
    )


def conv_grad_kernel(
    select_grad_ref,
    other_ref,
    select_ref,
    act_grad_ref,
    convolved_ref,
    act_ref,
    inner_ref,
    conv_weight_ref,
    mask_ref,
    inner_grad_ref,
    edge_ref,
    small_ref,
    inner,
    shifted,
):
    rows = act_ref.shape[0]
    taps = conv_weight_ref.shape[0]
    columns = select_ref.shape[0]
    select_grad = (select_grad_ref[...] + other_ref[...]).astype(bf16)
    total = act_grad_ref[...] + lax.dot_general(
        select_grad, select_ref[...], contract_first, preferred_element_type=f32
    )
    conv_grad = total * silu_slope(convolved_ref[...])
    small_ref[:columns, :] = jnp.dot(select_grad, act_ref[...], preferred_element_type=f32)
    inner[:halo, :] = inner_ref[rows:, :].astype(f32)
    inner[halo:, :] = inner_ref[:rows, :].astype(f32)
    edges = jnp.zeros((8, conv_grad.shape[1]), f32)
    shifted[:8, :] = edges
    shifted[rows + 8 :, :] = edges
    out = conv_weight_ref[taps - 1 :, :] * conv_grad
    before = edges
    small_ref[columns + taps - 1 : columns + taps, :] = jnp.sum(
        conv_grad * inner[halo:, :], axis=0, keepdims=True
    )
    for lag in range(1, taps):
        masked = conv_grad * mask_ref[:, lag : lag + 1]
        at = taps - 1 - lag
        small_ref[columns + at : columns + at + 1, :] = jnp.sum(
            masked * inner[pl.ds(halo - lag, rows), :], axis=0, keepdims=True
        )
        shifted[8 : rows + 8, :] = masked
        weight = conv_weight_ref[at : at + 1, :]
        out = out + weight * shifted[pl.ds(8 + lag, rows), :]
        before = before + weight * shifted[pl.ds(lag, 8), :]
    small_ref[columns + taps : columns + taps + 1, :] = jnp.sum(conv_grad, axis=0, keepdims=True)
    spare = small_ref.shape[0] - (columns + taps + 1)
    small_ref[columns + taps + 1 :, :] = jnp.zeros((spare, small_ref.shape[1]), f32)
    inner_grad_ref[...] = out.astype(bf16)
    edge_ref[:8, :] = before
    edge_ref[8:, :] = out[rows - 8 :, :]


def convolve_grad(
    select_grad, other, select_weight, act_grad, convolved, act, projected, conv_weight, masks
):
    rows, width = act.shape
    extended = rows + halo
    columns = select_weight.shape[0]
    taps = conv_weight.shape[0]
    small = columns + 16
    return call(
        conv_grad_kernel,
        "convolve_grad",
        width,
        [
            whole_spec(columns, rows),
            whole_spec(columns, rows),
            column_spec(columns),
            column_spec(rows),
            column_spec(rows),
            column_spec(rows),
            part_spec(0, extended),
            column_spec(taps),
            whole_spec(rows, masks.shape[1]),
        ],
        [column_spec(rows), column_spec(16), column_spec(small)],
        [
            jax.ShapeDtypeStruct((rows, width), bf16),
            jax.ShapeDtypeStruct((16, width), f32),
            jax.ShapeDtypeStruct((small, width), f32),
        ],
        [pltpu.VMEM((extended, scan_width), f32), pltpu.VMEM((rows + 16, scan_width), f32)],
        5_000_000_000,
        select_grad,
        other,
        select_weight,
        act_grad,
        convolved,
        act,
        projected,
        conv_weight,
        masks,
    )


def normalize_kernel(
    own_ref, other_ref, edge_ref, other_edge_ref, gain_ref, whole_ref, normed_ref, inverse_ref
):
    rows, half = own_ref.shape
    right = lax.axis_index("narrow") == 1
    for at, own, other in ((0, own_ref, other_ref), (rows, edge_ref, other_edge_ref)):
        end = at + own.shape[0]
        whole_ref[at:end, :half] = jnp.where(right, other[...], own[...])
        whole_ref[at:end, half:] = jnp.where(right, own[...], other[...])
    whole = whole_ref[...].astype(f32)
    inverse = lax.rsqrt(jnp.mean(whole * whole, axis=1, keepdims=True) + epsilon)
    normed_ref[...] = (whole * inverse * gain_ref[...]).astype(bf16)
    inverse_ref[...] = inverse[:rows]


def normalized(own, other, edge, other_edge, gain):
    rows, half = own.shape
    extended = rows + edge.shape[0]
    return pl.pallas_call(
        normalize_kernel,
        out_shape=[
            jax.ShapeDtypeStruct((extended, 2 * half), bf16),
            jax.ShapeDtypeStruct((extended, 2 * half), bf16),
            jax.ShapeDtypeStruct((rows, 1), f32),
        ],
        name="normalized",
    )(own, other, edge, other_edge, gain)


def edge_kernel(ids_ref, tokens_ref, out_ref):
    rows = ids_ref.shape[0]
    taps = 4
    out_ref[...] = tokens_ref[...]
    place = lax.broadcasted_iota(jnp.int32, (halo, 1), 0)
    same = jnp.zeros((halo, 1), f32)
    for lag in range(taps):
        here = jnp.where(ids_ref[rows - 1 - lag] == ids_ref[rows - 1], 1.0, 0.0)
        same = same + jnp.where(place == halo - 1 - lag, here, 0.0)
    out_ref[...] = (tokens_ref[...].astype(f32) * same).astype(bf16)


def edge_rows_of(ids, tokens):
    rows, width = tokens.shape
    return pl.pallas_call(
        edge_kernel,
        grid=(1,),
        in_specs=[
            pl.BlockSpec(memory_space=pltpu.SMEM),
            pl.BlockSpec((halo, width), lambda j: (rows // halo - 1, 0)),
        ],
        out_specs=pl.BlockSpec((halo, width), lambda j: (0, 0)),
        out_shape=jax.ShapeDtypeStruct((halo, width), bf16),
        name="edge_rows",
    )(ids, tokens)


def quarter_kernel(
    place_ref, own_ref, near_ref, far_ref, last_ref, normed_ref, small_ref, keep_ref, send_refs, piece
):
    total = None
    for n, grads in enumerate((own_ref, near_ref, far_ref, last_ref)):
        part = lax.dot_general(normed_ref[n], grads[...], contract_first, preferred_element_type=f32)
        total = part if total is None else total + part
    piece[...] = total
    for n in range(4):
        block = place_ref[0] ^ n
        rows, spare = piece.shape[0] // 4, small_ref.shape[0] // 4
        inner = piece[pl.ds(pl.multiple_of(block * rows, rows), rows), :]
        small = small_ref[pl.ds(pl.multiple_of(block * spare, spare), spare), :]
        if n == 0:
            keep_ref[:rows, :] = inner
            keep_ref[rows:, :] = small
        else:
            send_refs[n - 1, :rows, :] = inner.astype(bf16)
            send_refs[n - 1, rows:, :] = small.astype(bf16)


def inner_quarter(place, own, near, far, last, normed, small):
    width = own.shape[1]
    quarter = normed.shape[2]
    rows = (quarter + small.shape[0]) // 4
    return pl.pallas_call(
        quarter_kernel,
        in_specs=[pl.BlockSpec(memory_space=pltpu.SMEM)]
        + [pl.BlockSpec(memory_space=pltpu.VMEM)] * 6,
        out_shape=[
            jax.ShapeDtypeStruct((rows, width), f32),
            jax.ShapeDtypeStruct((3, rows, width), bf16),
        ],
        scratch_shapes=[pltpu.VMEM((quarter, width), f32)],
        compiler_params=pltpu.CompilerParams(vmem_limit_bytes=vmem_bytes),
        cost_estimate=pl.CostEstimate(
            flops=2_000_000_000, bytes_accessed=4_000_000, transcendentals=0
        ),
        name="inner_quarter",
    )(place, own, near, far, last, normed, small)


def join_kernel(place_ref, gate_ref, inner_ref, *rest):
    out_ref, small_ref = rest[-2:]
    rows, spare = out_ref.shape[0] // 2, small_ref.shape[0] // 2
    out_ref[:, 1, :] = gate_ref[...].astype(f32)
    for n in range(2):
        at = n * (rows + spare)
        block = inner_ref[at : at + rows + spare, :].astype(f32)
        out_ref[n * rows : (n + 1) * rows, 0, :] = block[:rows]
        small_ref[n * spare : (n + 1) * spare, :] = block[rows:]


def joined(place, flip, gate, inner, before, waits):
    depth, width = gate.shape
    quarter = depth // 4
    small = inner.shape[0] - quarter
    untouched = [*before, *waits]
    return pl.pallas_call(
        join_kernel,
        grid_spec=pltpu.PrefetchScalarGridSpec(
            num_scalar_prefetch=1,
            grid=(2,),
            in_specs=[
                pl.BlockSpec((quarter // 2, width), lambda j, place: (2 * (place[0] ^ flip) + j, 0)),
                pl.BlockSpec((inner.shape[0] // 2, width), lambda j, place: (j, 0)),
            ]
            + [pl.BlockSpec(memory_space=pl.ANY)] * len(untouched),
            out_specs=[
                pl.BlockSpec(
                    (quarter // 2, 2, width), lambda j, place: (2 * (place[0] ^ flip) + j, 0, 0)
                ),
                pl.BlockSpec((small // 2, width), lambda j, place: (2 * (place[0] ^ flip) + j, 0)),
            ],
        ),
        out_shape=[
            jax.ShapeDtypeStruct((depth, 2, width), f32),
            jax.ShapeDtypeStruct((4 * small, width), f32),
        ],
        input_output_aliases={3 + k: k for k in range(len(before))},
        compiler_params=pltpu.CompilerParams(vmem_limit_bytes=vmem_bytes),
        name="joined",
    )(place, gate, inner, *untouched)


def parts_kernel(small_ref, *out_refs, starts):
    for ref, start in zip(out_refs, starts):
        ref[...] = small_ref[start : start + ref.shape[0], :]


def small_parts(small, sizes):
    width = small.shape[1]
    return pl.pallas_call(
        functools.partial(parts_kernel, starts=[start for start, _ in sizes]),
        out_shape=[jax.ShapeDtypeStruct((rows, width), f32) for _, rows in sizes],
        name="small_parts",
    )(small)


def carried(ends, decay):
    count = decay.shape[0]
    place = lax.axis_index("wide")

    def split(packed):
        return packed[:count], packed[count : 2 * count], packed[2 * count : 2 * count + 1]

    def through(total):
        return jnp.exp(decay * total)

    zero = jnp.zeros(decay.shape, f32)
    none = jnp.zeros((1, decay.shape[1]), f32)
    before, before_steps, after, after_steps = zero, none, zero, none
    packed = ends
    for bit in (1, 2):
        second = (place & bit) != 0
        own = split(packed)
        other = split(swapped(packed, "wide", bit))
        early = [jnp.where(second, b, a) for a, b in zip(own, other)]
        late = [jnp.where(second, a, b) for a, b in zip(own, other)]
        before = before + jnp.where(second, through(before_steps) * other[0], 0.0)
        before_steps = before_steps + jnp.where(second, other[2], 0.0)
        after = after + jnp.where(second, 0.0, through(after_steps) * other[1])
        after_steps = after_steps + jnp.where(second, 0.0, other[2])
        state = late[0] + through(late[2]) * early[0]
        adjoint = early[1] + through(early[2]) * late[1]
        packed = jnp.concatenate(
            [state, adjoint, jnp.broadcast_to(early[2] + late[2], (8, decay.shape[1]))]
        )
    from_before = passed_along(packed[:count], "wide", 4)
    from_after = passed_along(packed[count : 2 * count], "wide", -4)
    return (
        before + through(before_steps) * from_before,
        after + through(after_steps) * from_after,
    )


def local(
    tokens,
    norm_gain,
    in_weight,
    conv_weight,
    conv_bias,
    select_weight,
    step_weight,
    step_bias,
    decay_log,
    skip_gain,
    out_weight,
    segment_ids,
    cotangent,
):
    rows, features = tokens.shape
    taps = conv_weight.shape[0]
    columns = select_weight.shape[0]
    rank = step_weight.shape[0]
    count = decay_log.shape[0]
    right_half = lax.axis_index("narrow") == 1

    def both_halves(own, other):
        return jnp.concatenate(
            [jnp.where(right_half, other, own), jnp.where(right_half, own, other)], axis=1
        )

    other_tokens = swapped(tokens, "narrow", 1)
    other_cot = swapped(cotangent, "narrow", 1)
    edge, other_edge = to_next_both(edge_rows_of(segment_ids, tokens))

    same_as_last = (segment_ids[rows - 8 :] == segment_ids[rows - 1 :])[:, None]
    padded_ids = jnp.concatenate([jnp.broadcast_to(segment_ids[:1], (taps - 1,)), segment_ids])
    masks = jnp.stack(
        [
            (padded_ids[taps - 1 - lag : taps - 1 - lag + rows] == segment_ids).astype(f32)
            for lag in range(taps)
        ]
        + [jnp.zeros((rows,), f32)] * (8 - taps),
        axis=1,
    )
    whole_ext, normed_ext, inverse = normalized(
        tokens, other_tokens, edge, other_edge, norm_gain[None]
    )
    projected = jnp.einsum(
        "td,dce->cte", normed_ext, in_weight, preferred_element_type=f32
    ).astype(bf16)
    convolved, act, selected = convolve(
        projected, conv_weight, conv_bias[None], select_weight, masks
    )
    other_selected = swapped(selected, "narrow", 1)
    cot_whole = both_halves(cotangent, other_cot)
    gated_grad = lax.dot_general(
        cot_whole, out_weight, contract_last, preferred_element_type=f32
    )
    step_pre, step, ends = scan_ends(
        selected,
        other_selected,
        step_weight,
        step_bias[None],
        act,
        projected,
        gated_grad,
        masks,
        decay_log,
    )
    entry, tail = carried(ends, -jnp.exp(decay_log))
    pair = scan_forward(
        selected,
        other_selected,
        step,
        act,
        projected,
        gated_grad,
        masks,
        decay_log,
        entry,
        skip_gain[None],
    )
    gated, gate_grad = pair[0], pair[1]
    normed = normed_ext[:rows]
    normed_four = quarter_of_four(normed)
    products = (
        lax.dot_general(gated, cot_whole, contract_first, preferred_element_type=f32).astype(bf16),
        lax.dot_general(normed, gate_grad, contract_first, preferred_element_type=f32).astype(bf16),
    )
    out_sum, gate_sum = lax.psum(products, "wide")
    act_grad, select_grad, scan_small = scan_backward(
        selected,
        other_selected,
        step_pre,
        step,
        act,
        projected,
        gated_grad,
        masks,
        decay_log,
        entry,
        tail,
        skip_gain[None],
        step_weight,
        [normed_four, *products],
    )
    other_select_grad = swapped(select_grad, "narrow", 1)

    def narrow_halves(array):
        low, high = array[:, :features], array[:, features:]
        return jnp.where(right_half, high, low), jnp.where(right_half, low, high)

    out_part = jnp.dot(gated, out_weight, preferred_element_type=f32)
    out_mine, out_other = narrow_halves(out_part)
    out_total = out_mine + swapped(out_other, "narrow", 1)
    layer_out = (tokens.astype(f32) + out_total).astype(bf16)

    inner_main, edges, conv_small = convolve_grad(
        select_grad,
        other_select_grad,
        select_weight,
        act_grad,
        convolved,
        act,
        projected,
        conv_weight,
        masks,
    )
    from_next = passed_along(edges[:8], "wide", -1)
    last_rows = edges[8:] + jnp.where(same_as_last, from_next, 0.0)
    inner_grad = jnp.concatenate([inner_main[: rows - 8], last_rows.astype(bf16)])
    normed_part = jnp.einsum(
        "cte,dce->td", jnp.stack([inner_grad, gate_grad]), in_weight, preferred_element_type=f32
    )
    whole = whole_ext[:rows].astype(f32)
    gain_part = jnp.sum(normed_part * whole * inverse, axis=0, keepdims=True)
    row_part = jnp.sum(normed_part * norm_gain * whole, axis=1, keepdims=True)

    gain_sum = gain_part + swapped(gain_part, "narrow", 1)
    spare = -(scan_small.shape[0] + conv_small.shape[0] + 1) % 256
    small = jnp.concatenate(
        [scan_small, conv_small, gain_sum, jnp.zeros((spare, gain_sum.shape[1]), f32)]
    )
    small_piece = scattered(small, (1, 2))
    near = swapped(inner_grad, "wide", 2)
    wide_place = lax.axis_index("wide").astype(jnp.int32)
    keep, sends = inner_quarter(
        (wide_place >> 2 & 3)[None],
        inner_grad,
        near,
        swapped(inner_grad, "wide", 1),
        swapped(near, "wide", 1),
        normed_four,
        small_piece,
    )
    first_bits, *more_bits = group_bits(2)
    held = keep
    for n, flip in enumerate(flips(first_bits)[1:]):
        held = held + swapped(sends[n], "wide", flip).astype(f32)
    for bits in more_bits:
        held = scattered(held, bits)
    held = held.astype(bf16)
    for bits in reversed(group_bits(2)):
        held = gathered(held, bits)
    normed_mine, normed_other = narrow_halves(normed_part)
    row_sum = row_part + swapped(row_part, "narrow", 1)
    normed_sum = normed_mine + swapped(normed_other, "narrow", 1)
    gain_mine = jnp.where(right_half, norm_gain[features:], norm_gain[:features])
    whole_grad = inverse * (gain_mine * normed_sum) - tokens.astype(f32) * (
        inverse * inverse * inverse
    ) * (row_sum / (2 * features))
    tokens_grad = (whole_grad + cotangent.astype(f32)).astype(bf16)

    out_weight_grad = out_sum.astype(f32)
    near = swapped(held, "wide", 2)
    quarters = (held, swapped(held, "wide", 1), near, swapped(near, "wide", 1))
    results = []
    for flip, quarter in enumerate(quarters):
        results = joined(
            (wide_place & 3)[None],
            flip,
            gate_sum,
            quarter,
            results,
            [layer_out, tokens_grad] if flip == 1 else [],
        )
    in_weight_grad, small_sum = results
    conv_at = scan_small.shape[0]
    gain_at = conv_at + conv_small.shape[0]
    (
        step_weight_grad,
        decay_log_grad,
        skip_gain_grad,
        step_bias_grad,
        select_weight_grad,
        conv_weight_grad,
        conv_bias_grad,
        norm_gain_grad,
    ) = small_parts(
        small_sum,
        [
            (0, rank),
            (rank, count),
            (rank + count, 1),
            (rank + count + 1, 1),
            (conv_at, columns),
            (conv_at + columns, taps),
            (conv_at + columns + taps, 1),
            (gain_at, 1),
        ],
    )
    return (
        layer_out,
        tokens_grad,
        norm_gain_grad[0],
        in_weight_grad,
        conv_weight_grad,
        conv_bias_grad[0],
        select_weight_grad,
        step_weight_grad,
        step_bias_grad[0],
        decay_log_grad,
        skip_gain_grad[0],
        out_weight_grad,
    )


def solution(mesh):
    placed = (
        P("wide", "narrow"),
        P(),
        P(None, None, "narrow"),
        P(None, "narrow"),
        P("narrow"),
        P(None, "narrow"),
        P(None, "narrow"),
        P("narrow"),
        P(None, "narrow"),
        P("narrow"),
        P("narrow", None),
        P("wide"),
        P("wide", "narrow"),
    )
    return jax.shard_map(
        local,
        mesh=mesh,
        in_specs=placed,
        out_specs=(
            P("wide", "narrow"),
            P("wide", "narrow"),
            P(),
            P(None, None, "narrow"),
            P(None, "narrow"),
            P("narrow"),
            P(None, "narrow"),
            P(None, "narrow"),
            P("narrow"),
            P(None, "narrow"),
            P("narrow"),
            P("narrow", None),
        ),
        check_vma=False,
    )
```

```python
import functools

import jax
import jax.numpy as jnp
from jax import lax
from jax.experimental import pallas as pl
from jax.experimental.pallas import tpu as pltpu
from jax.sharding import PartitionSpec as P

epsilon = 1e-05
log2e = 1.4426950408889634
reset_step = 1e30
lanes = 128
halo = 16
body_rows = 32
scan_width = 512
vmem_bytes = 56 * 1024 * 1024
tiny_cost = pl.CostEstimate(flops=1, bytes_accessed=1, transcendentals=0)
f32 = jnp.float32
bf16 = jnp.bfloat16
contract_first = (((0,), (0,)), ((), ()))
contract_last = (((1,), (1,)), ((), ()))


def passed_along(array, axis, by):
    peers = lax.axis_size(axis)
    pairs = [(i, i + by) for i in range(peers) if 0 <= i + by < peers]
    return lax.ppermute(array, axis, pairs)


def swapped(array, axis, bit):
    peers = lax.axis_size(axis)
    return lax.ppermute(array, axis, [(i, i ^ bit) for i in range(peers)])


def wide_bits():
    bit, bits = 1, []
    while bit < lax.axis_size("wide"):
        bits.append(bit)
        bit *= 2
    return bits


def to_next_both(array):
    count, sides = lax.axis_size("wide"), lax.axis_size("narrow")
    pairs = [
        (i * sides + k, (i + 1) * sides + (sides - 1 - k))
        for i in range(count - 1)
        for k in range(sides)
    ]
    return passed_along(array, "wide", 1), lax.ppermute(array, ("wide", "narrow"), pairs)


def is_upper(bit):
    return (lax.axis_index("wide") & bit) != 0


def group_bits(size):
    bits, bit = [], 4
    while bit < lax.axis_size("wide"):
        bits.append(bit)
        bit *= 2
    return [tuple(bits[k : k + size]) for k in range(0, len(bits), size)]


def flips(bits):
    return [sum(b for k, b in enumerate(bits) if n >> k & 1) for n in range(2 ** len(bits))]


def scattered(piece, bits):
    rows = piece.shape[0] // 2 ** len(bits)
    here = sum(is_upper(b).astype(jnp.int32) << k for k, b in enumerate(bits))

    def block(n):
        return lax.dynamic_slice_in_dim(piece, (here ^ n) * rows, rows, 0)

    total = block(0).astype(f32)
    for n, flip in enumerate(flips(bits)):
        if n > 0:
            total = total + swapped(block(n).astype(bf16), "wide", flip).astype(f32)
    return total


def gathered(held, bits):
    blocks = [held] + [swapped(held, "wide", flip) for flip in flips(bits)[1:]]
    for bit in bits:
        upper = is_upper(bit)
        blocks = [
            jnp.concatenate([jnp.where(upper, b, a), jnp.where(upper, a, b)])
            for a, b in zip(blocks[0::2], blocks[1::2])
        ]
    return blocks[0]


def quarter_of_four(array):
    width = array.shape[1] // 4
    here = lax.axis_index("wide") & 3

    def quarter(n):
        return lax.dynamic_slice_in_dim(array, (here ^ n) * width, width, 1)

    return jnp.stack(
        [quarter(0)] + [swapped(quarter(n), "wide", n) for n in (2, 1, 3)]
    )


def silu_slope(values):
    logistic = jax.nn.sigmoid(values)
    return logistic * (1.0 + values * (1.0 - logistic))


def softplus(values):
    return jnp.maximum(values, 0.0) + jnp.log1p(jnp.exp(-jnp.abs(values)))


def column_spec(rows, start=0):
    return pl.BlockSpec((rows, scan_width), lambda j: (0, start + j))


def part_spec(part, rows, start=0):
    return pl.BlockSpec((None, rows, scan_width), lambda j: (part, 0, start + j))


def whole_spec(rows, width):
    return pl.BlockSpec((rows, width), lambda j: (0, 0))


def call(kernel, name, width, in_specs, out_specs, out_shape, scratch, *operands):
    return pl.pallas_call(
        kernel,
        grid=(width // scan_width,),
        in_specs=in_specs,
        out_specs=out_specs,
        out_shape=out_shape,
        scratch_shapes=scratch,
        compiler_params=pltpu.CompilerParams(vmem_limit_bytes=vmem_bytes),
        cost_estimate=tiny_cost,
        name=name,
    )(*operands)


def conv_kernel(
    inner_ref,
    conv_weight_ref,
    conv_bias_ref,
    select_ref,
    mask_ref,
    convolved_ref,
    act_ref,
    selected_ref,
    inner,
):
    rows = act_ref.shape[0]
    taps = conv_weight_ref.shape[0]
    inner[:halo, :] = inner_ref[rows:, :].astype(f32)
    inner[halo:, :] = inner_ref[:rows, :].astype(f32)
    total = conv_bias_ref[...] + conv_weight_ref[taps - 1 :, :] * inner[halo:, :]
    for lag in range(1, taps):
        earlier = inner[pl.ds(halo - lag, rows), :] * mask_ref[:, lag : lag + 1]
        total = total + conv_weight_ref[taps - 1 - lag : taps - lag, :] * earlier
    convolved_ref[...] = total
    act = (total * jax.nn.sigmoid(total)).astype(bf16)
    act_ref[...] = act
    part = lax.dot_general(select_ref[...], act, contract_last, preferred_element_type=f32)

    @pl.when(pl.program_id(0) == 0)
    def _():
        selected_ref[...] = part

    @pl.when(pl.program_id(0) > 0)
    def _():
        selected_ref[...] += part


def convolve(projected, conv_weight, conv_bias, select_weight, masks):
    parts, extended, width = projected.shape
    rows = extended - halo
    taps = conv_weight.shape[0]
    columns = select_weight.shape[0]
    return call(
        conv_kernel,
        "convolve",
        width,
        [
            part_spec(0, extended),
            column_spec(taps),
            column_spec(1),
            column_spec(columns),
            whole_spec(rows, masks.shape[1]),
        ],
        [column_spec(rows), column_spec(rows), whole_spec(columns, rows)],
        [
            jax.ShapeDtypeStruct((rows, width), f32),
            jax.ShapeDtypeStruct((rows, width), bf16),
            jax.ShapeDtypeStruct((columns, rows), f32),
        ],
        [pltpu.VMEM((extended, scan_width), f32)],
        projected,
        conv_weight,
        conv_bias,
        select_weight,
        masks,
    )


def coef_columns(coef, block):
    per_tile = lanes // body_rows
    start = pl.multiple_of((block // per_tile) * lanes, lanes)
    tile = coef[:, pl.ds(start, lanes)]
    back = body_rows * lax.rem(block, per_tile)
    return pltpu.roll(tile, lax.rem(lanes - back, lanes), 1)


def ends_kernel(
    selected_ref,
    other_ref,
    step_weight_ref,
    step_bias_ref,
    act_ref,
    gate_ref,
    gated_grad_ref,
    mask_ref,
    decay_log_ref,
    step_pre_ref,
    step_ref,
    ends_ref,
    coef,
    held_step,
    drive,
    scan_grad,
):
    rows = act_ref.shape[0]
    count = decay_log_ref.shape[0]
    rank = step_weight_ref.shape[0]
    decay2 = -jnp.exp(decay_log_ref[...]) * log2e
    selected = selected_ref[...] + other_ref[...]
    coef[...] = selected[rank:, :]
    step_low = selected[:rank, :].astype(bf16)
    step_pre = step_bias_ref[...] + lax.dot_general(
        step_low, step_weight_ref[...], contract_first, preferred_element_type=f32
    )
    step_pre_ref[...] = step_pre
    step = softplus(step_pre)
    step_ref[...] = step
    held_step[...] = jnp.where(mask_ref[:, 1:2] > 0.0, step, reset_step)
    drive[...] = step * act_ref[...].astype(f32)
    gate = gate_ref[...].astype(f32)
    scan_grad[...] = gated_grad_ref[...] * (gate * jax.nn.sigmoid(gate))
    zero = jnp.zeros(decay2.shape, f32)

    def body(block, carried):
        state, product, adjoint = carried
        columns = coef_columns(coef, block)
        for i in range(body_rows):
            row = pl.ds(block * body_rows + i, 1)
            factor = jnp.exp2(held_step[row, :] * decay2)
            state = factor * state + columns[:count, i : i + 1] * drive[row, :]
            product = factor * product
            adjoint = adjoint + product * (columns[count:, i : i + 1] * scan_grad[row, :])
        return state, product, adjoint

    state, product, adjoint = lax.fori_loop(0, rows // body_rows, body, (zero, zero + 1.0, zero))
    ends_ref[:count, :] = state
    ends_ref[count : 2 * count, :] = adjoint
    total = jnp.sum(held_step[...], axis=0, keepdims=True)
    ends_ref[2 * count :, :] = jnp.broadcast_to(total, (8, total.shape[1]))


def scan_ends(
    selected, other, step_weight, step_bias, act, projected, gated_grad, masks, decay_log
):
    rows, width = act.shape
    count = decay_log.shape[0]
    columns = selected.shape[0]
    rank = step_weight.shape[0]
    return call(
        ends_kernel,
        "scan_ends",
        width,
        [
            whole_spec(columns, rows),
            whole_spec(columns, rows),
            column_spec(rank),
            column_spec(1),
            column_spec(rows),
            part_spec(1, rows),
            column_spec(rows),
            whole_spec(rows, masks.shape[1]),
            column_spec(count),
        ],
        [column_spec(rows), column_spec(rows), column_spec(2 * count + 8)],
        [
            jax.ShapeDtypeStruct((rows, width), f32),
            jax.ShapeDtypeStruct((rows, width), f32),
            jax.ShapeDtypeStruct((2 * count + 8, width), f32),
        ],
        [pltpu.VMEM((2 * count, rows), f32)] + [pltpu.VMEM((rows, scan_width), f32)] * 3,
        selected,
        other,
        step_weight,
        step_bias,
        act,
        projected,
        gated_grad,
        masks,
        decay_log,
    )


def lane_tiles(values):
    return [values[:, k : k + lanes] for k in range(0, values.shape[1], lanes)]


def tree_sum(parts):
    while len(parts) > 1:
        odd = parts[len(parts) // 2 * 2 :]
        parts = [a + b for a, b in zip(parts[0::2], parts[1::2])] + odd
    return parts[0]


def keep_halves(scratch, i, values):
    for k, tile in enumerate(lane_tiles(values)):
        at = (k * body_rows + i) * 8
        scratch[at : at + 8, :] = tile[:8] + tile[8:]


def put_state_sums(scratch, out_ref, block):
    for group in range(body_rows // 8):
        row = pl.ds(pl.multiple_of(block * body_rows + group * 8, 8), 8)
        for k in range(out_ref.shape[1] // lanes):
            at = (k * body_rows + group * 8) * 8
            total = tree_sum([scratch[pl.ds(at + n, 8, stride=8), :] for n in range(8)])
            out_ref[row, k * lanes : (k + 1) * lanes] = total


def lane_sums(values):
    ones = jnp.ones((8, lanes), bf16)
    high = values.astype(bf16)
    low = (values - high.astype(f32)).astype(bf16)
    total = lax.dot_general(ones, high, contract_last, preferred_element_type=f32)
    total += lax.dot_general(ones, low, contract_last, preferred_element_type=f32)
    return total[:1, :]


def at_token(t, count):
    return pl.ds(pl.multiple_of(t * count, count), count)


def forward_kernel(
    selected_ref,
    other_ref,
    step_ref,
    act_ref,
    gate_ref,
    gated_grad_ref,
    mask_ref,
    decay_log_ref,
    entry_ref,
    skip_ref,
    pair_ref,
    coef,
    held_step,
    drive,
    scanned,
    halves,
):
    rows = step_ref.shape[0]
    count = decay_log_ref.shape[0]
    rank = selected_ref.shape[0] - 2 * count
    decay2 = -jnp.exp(decay_log_ref[...]) * log2e
    coef[...] = selected_ref[rank:, :] + other_ref[rank:, :]
    act = act_ref[...].astype(f32)
    held_step[...] = jnp.where(mask_ref[:, 1:2] > 0.0, step_ref[...], reset_step)
    drive[...] = step_ref[...] * act

    def forward(block, state):
        columns = coef_columns(coef, block)
        for i in range(body_rows):
            row = pl.ds(block * body_rows + i, 1)
            factor = jnp.exp2(held_step[row, :] * decay2)
            state = factor * state + columns[:count, i : i + 1] * drive[row, :]
            keep_halves(halves, i, columns[count:, i : i + 1] * state)
        put_state_sums(halves, scanned, block)
        return state

    lax.fori_loop(0, rows // body_rows, forward, entry_ref[...])
    gate = gate_ref[...].astype(f32)
    logistic = jax.nn.sigmoid(gate)
    total = scanned[...] + skip_ref[...] * act
    pair_ref[0] = (total * (gate * logistic)).astype(bf16)
    slope = logistic * (1.0 + gate * (1.0 - logistic))
    pair_ref[1] = (gated_grad_ref[...] * total * slope).astype(bf16)


def scan_forward(
    selected, other, step, act, projected, gated_grad, masks, decay_log, entry, skip_gain
):
    rows, width = step.shape
    count = decay_log.shape[0]
    columns = selected.shape[0]
    return call(
        forward_kernel,
        "scan_forward",
        width,
        [
            whole_spec(columns, rows),
            whole_spec(columns, rows),
            column_spec(rows),
            column_spec(rows),
            part_spec(1, rows),
            column_spec(rows),
            whole_spec(rows, masks.shape[1]),
            column_spec(count),
            column_spec(count),
            column_spec(1),
        ],
        pl.BlockSpec((2, rows, scan_width), lambda j: (0, 0, j)),
        jax.ShapeDtypeStruct((2, rows, width), bf16),
        [pltpu.VMEM((2 * count, rows), f32)]
        + [pltpu.VMEM((rows, scan_width), f32)] * 3
        + [pltpu.VMEM((8 * body_rows * (scan_width // lanes), lanes), f32)],
        selected,
        other,
        step,
        act,
        projected,
        gated_grad,
        masks,
        decay_log,
        entry,
        skip_gain,
    )


def backward_kernel(
    selected_ref,
    other_ref,
    step_pre_ref,
    step_ref,
    act_ref,
    gate_ref,
    gated_grad_ref,
    mask_ref,
    decay_log_ref,
    entry_ref,
    tail_ref,
    skip_ref,
    step_weight_ref,
    *rest,
    waits,
):
    (
        act_grad_ref,
        select_grad_ref,
        small_ref,
        coef,
        held_step,
        drive,
        scan_grad,
        weighted,
        held_sum,
        states,
        factors,
        halves,
        more_halves,
        in_sum,
        read_sum,
    ) = rest[waits:]
    rows = step_ref.shape[0]
    count = decay_log_ref.shape[0]
    rank = step_weight_ref.shape[0]
    blocks = rows // body_rows
    decay = -jnp.exp(decay_log_ref[...])
    decay2 = decay * log2e
    selected = selected_ref[...] + other_ref[...]
    coef[...] = selected[rank:, :]
    step_low = selected[:rank, :].astype(bf16)
    step = step_ref[...]
    act = act_ref[...].astype(f32)
    held_step[...] = jnp.where(mask_ref[:, 1:2] > 0.0, step, reset_step)
    drive[...] = step * act
    gate = gate_ref[...].astype(f32)
    grads = gated_grad_ref[...] * (gate * jax.nn.sigmoid(gate))
    scan_grad[...] = grads
    small_ref[rank + count : rank + count + 1, :] = jnp.sum(grads * act, axis=0, keepdims=True)
    states[:count, :] = entry_ref[...]

    @pl.when(pl.program_id(0) == 0)
    def _():
        in_sum[...] = jnp.zeros(in_sum.shape, f32)
        read_sum[...] = jnp.zeros(read_sum.shape, f32)
        select_grad_ref[...] = jnp.zeros(select_grad_ref.shape, f32)

    def forward(block, state):
        columns = coef_columns(coef, block)
        for i in range(body_rows):
            t = block * body_rows + i
            row = pl.ds(t, 1)
            factor = jnp.exp2(held_step[row, :] * decay2)
            state = factor * state + columns[:count, i : i + 1] * drive[row, :]
            factors[at_token(t, count), :] = factor
            states[at_token(t + 1, count), :] = state
        return state

    lax.fori_loop(0, blocks, forward, entry_ref[...])

    def backward(k, carried):
        adjoint, decay_grad = carried
        block = blocks - 1 - k
        columns = coef_columns(coef, block)
        for i in range(body_rows - 1, -1, -1):
            t = block * body_rows + i
            row = pl.ds(t, 1)
            here = at_token(t, count)
            grad = scan_grad[row, :]
            summed = columns[count:, i : i + 1] * grad + adjoint
            read_sum[here, :] += tree_sum(lane_tiles(grad * states[at_token(t + 1, count), :]))
            in_sum[here, :] += tree_sum(lane_tiles(summed * drive[row, :]))
            keep_halves(halves, i, summed * columns[:count, i : i + 1])
            adjoint = factors[here, :] * summed
            held = adjoint * states[here, :]
            decay_grad = decay_grad + held * step_ref[row, :]
            keep_halves(more_halves, i, held * decay)
        put_state_sums(halves, weighted, block)
        put_state_sums(more_halves, held_sum, block)
        return adjoint, decay_grad

    ignored, decay_grad = lax.fori_loop(
        0, blocks, backward, (tail_ref[...], jnp.zeros(decay.shape, f32))
    )
    act_grad_ref[...] = step * weighted[...] + skip_ref[...] * scan_grad[...]
    step_grad = act * weighted[...] + held_sum[...]
    pre_grad = (step_grad * jax.nn.sigmoid(step_pre_ref[...])).astype(bf16)
    small_ref[:rank, :] = jnp.dot(step_low, pre_grad, preferred_element_type=f32)
    small_ref[rank : rank + count, :] = decay_grad * decay
    bias_grad = jnp.sum(pre_grad.astype(f32), axis=0, keepdims=True)
    small_ref[rank + count + 1 : rank + count + 2, :] = bias_grad
    spare = small_ref.shape[0] - (rank + count + 2)
    small_ref[rank + count + 2 :, :] = jnp.zeros((spare, small_ref.shape[1]), f32)
    select_grad_ref[:rank, :] += lax.dot_general(
        step_weight_ref[...], pre_grad, contract_last, preferred_element_type=f32
    )

    @pl.when(pl.program_id(0) == pl.num_programs(0) - 1)
    def _():
        for n in range(count):
            at = pl.ds(n, rows, stride=count)
            select_grad_ref[rank + n : rank + n + 1, :] = lane_sums(in_sum[at, :])
            select_grad_ref[rank + count + n : rank + count + n + 1, :] = lane_sums(read_sum[at, :])


def scan_backward(
    selected,
    other,
    step_pre,
    step,
    act,
    projected,
    gated_grad,
    masks,
    decay_log,
    entry,
    tail,
    skip_gain,
    step_weight,
    waits,
):
    rows, width = step.shape
    count = decay_log.shape[0]
    columns = selected.shape[0]
    rank = step_weight.shape[0]
    half_rows = 8 * body_rows * (scan_width // lanes)
    small = rank + count + 16
    return call(
        functools.partial(backward_kernel, waits=len(waits)),
        "scan_backward",
        width,
        [
            whole_spec(columns, rows),
            whole_spec(columns, rows),
            column_spec(rows),
            column_spec(rows),
            column_spec(rows),
            part_spec(1, rows),
            column_spec(rows),
            whole_spec(rows, masks.shape[1]),
            column_spec(count),
            column_spec(count),
            column_spec(count),
            column_spec(1),
            column_spec(rank),
        ]
        + [pl.BlockSpec(memory_space=pl.ANY)] * len(waits),
        [column_spec(rows), whole_spec(columns, rows), column_spec(small)],
        [
            jax.ShapeDtypeStruct((rows, width), f32),
            jax.ShapeDtypeStruct((columns, rows), f32),
            jax.ShapeDtypeStruct((small, width), f32),
        ],
        [pltpu.VMEM((2 * count, rows), f32)]
        + [pltpu.VMEM((rows, scan_width), f32)] * 5
        + [
            pltpu.VMEM(((rows + 1) * count, scan_width), f32),
            pltpu.VMEM((rows * count, scan_width), f32),
            pltpu.VMEM((half_rows, lanes), f32),
            pltpu.VMEM((half_rows, lanes), f32),
            pltpu.VMEM((rows * count, lanes), f32),
            pltpu.VMEM((rows * count, lanes), f32),
        ],
        selected,
        other,
        step_pre,
        step,
        act,
        projected,
        gated_grad,
        masks,
        decay_log,
        entry,
        tail,
        skip_gain,
        step_weight,
        *waits,
    )


def conv_grad_kernel(
    select_grad_ref,
    other_ref,
    select_ref,
    act_grad_ref,
    convolved_ref,
    act_ref,
    inner_ref,
    conv_weight_ref,
    mask_ref,
    inner_grad_ref,
    edge_ref,
    small_ref,
    inner,
    shifted,
):
    rows = act_ref.shape[0]
    taps = conv_weight_ref.shape[0]
    columns = select_ref.shape[0]
    select_grad = (select_grad_ref[...] + other_ref[...]).astype(bf16)
    total = act_grad_ref[...] + lax.dot_general(
        select_grad, select_ref[...], contract_first, preferred_element_type=f32
    )
    conv_grad = total * silu_slope(convolved_ref[...])
    small_ref[:columns, :] = jnp.dot(select_grad, act_ref[...], preferred_element_type=f32)
    inner[:halo, :] = inner_ref[rows:, :].astype(f32)
    inner[halo:, :] = inner_ref[:rows, :].astype(f32)
    edges = jnp.zeros((8, conv_grad.shape[1]), f32)
    shifted[:8, :] = edges
    shifted[rows + 8 :, :] = edges
    out = conv_weight_ref[taps - 1 :, :] * conv_grad
    before = edges
    small_ref[columns + taps - 1 : columns + taps, :] = jnp.sum(
        conv_grad * inner[halo:, :], axis=0, keepdims=True
    )
    for lag in range(1, taps):
        masked = conv_grad * mask_ref[:, lag : lag + 1]
        at = taps - 1 - lag
        small_ref[columns + at : columns + at + 1, :] = jnp.sum(
            masked * inner[pl.ds(halo - lag, rows), :], axis=0, keepdims=True
        )
        shifted[8 : rows + 8, :] = masked
        weight = conv_weight_ref[at : at + 1, :]
        out = out + weight * shifted[pl.ds(8 + lag, rows), :]
        before = before + weight * shifted[pl.ds(lag, 8), :]
    small_ref[columns + taps : columns + taps + 1, :] = jnp.sum(conv_grad, axis=0, keepdims=True)
    spare = small_ref.shape[0] - (columns + taps + 1)
    small_ref[columns + taps + 1 :, :] = jnp.zeros((spare, small_ref.shape[1]), f32)
    inner_grad_ref[...] = out.astype(bf16)
    edge_ref[:8, :] = before
    edge_ref[8:, :] = out[rows - 8 :, :]


def convolve_grad(
    select_grad, other, select_weight, act_grad, convolved, act, projected, conv_weight, masks
):
    rows, width = act.shape
    extended = rows + halo
    columns = select_weight.shape[0]
    taps = conv_weight.shape[0]
    small = columns + 16
    return call(
        conv_grad_kernel,
        "convolve_grad",
        width,
        [
            whole_spec(columns, rows),
            whole_spec(columns, rows),
            column_spec(columns),
            column_spec(rows),
            column_spec(rows),
            column_spec(rows),
            part_spec(0, extended),
            column_spec(taps),
            whole_spec(rows, masks.shape[1]),
        ],
        [column_spec(rows), column_spec(16), column_spec(small)],
        [
            jax.ShapeDtypeStruct((rows, width), bf16),
            jax.ShapeDtypeStruct((16, width), f32),
            jax.ShapeDtypeStruct((small, width), f32),
        ],
        [pltpu.VMEM((extended, scan_width), f32), pltpu.VMEM((rows + 16, scan_width), f32)],
        select_grad,
        other,
        select_weight,
        act_grad,
        convolved,
        act,
        projected,
        conv_weight,
        masks,
    )


def normalize_kernel(
    own_ref, other_ref, edge_ref, other_edge_ref, gain_ref, whole_ref, normed_ref, inverse_ref
):
    rows, half = own_ref.shape
    right = lax.axis_index("narrow") == 1
    for at, own, other in ((0, own_ref, other_ref), (rows, edge_ref, other_edge_ref)):
        end = at + own.shape[0]
        whole_ref[at:end, :half] = jnp.where(right, other[...], own[...])
        whole_ref[at:end, half:] = jnp.where(right, own[...], other[...])
    whole = whole_ref[...].astype(f32)
    inverse = lax.rsqrt(jnp.mean(whole * whole, axis=1, keepdims=True) + epsilon)
    normed_ref[...] = (whole * inverse * gain_ref[...]).astype(bf16)
    inverse_ref[...] = inverse[:rows]


def normalized(own, other, edge, other_edge, gain):
    rows, half = own.shape
    extended = rows + edge.shape[0]
    return pl.pallas_call(
        normalize_kernel,
        out_shape=[
            jax.ShapeDtypeStruct((extended, 2 * half), bf16),
            jax.ShapeDtypeStruct((extended, 2 * half), bf16),
            jax.ShapeDtypeStruct((rows, 1), f32),
        ],
        cost_estimate=tiny_cost,
        name="normalized",
    )(own, other, edge, other_edge, gain)


def edge_kernel(ids_ref, tokens_ref, out_ref):
    rows = ids_ref.shape[0]
    taps = 4
    out_ref[...] = tokens_ref[...]
    place = lax.broadcasted_iota(jnp.int32, (halo, 1), 0)
    same = jnp.zeros((halo, 1), f32)
    for lag in range(taps):
        here = jnp.where(ids_ref[rows - 1 - lag] == ids_ref[rows - 1], 1.0, 0.0)
        same = same + jnp.where(place == halo - 1 - lag, here, 0.0)
    out_ref[...] = (tokens_ref[...].astype(f32) * same).astype(bf16)


def edge_rows_of(ids, tokens):
    rows, width = tokens.shape
    return pl.pallas_call(
        edge_kernel,
        grid=(1,),
        in_specs=[
            pl.BlockSpec(memory_space=pltpu.SMEM),
            pl.BlockSpec((halo, width), lambda j: (rows // halo - 1, 0)),
        ],
        out_specs=pl.BlockSpec((halo, width), lambda j: (0, 0)),
        out_shape=jax.ShapeDtypeStruct((halo, width), bf16),
        cost_estimate=tiny_cost,
        name="edge_rows",
    )(ids, tokens)


def quarter_kernel(
    place_ref, own_ref, near_ref, far_ref, last_ref, normed_ref, small_ref, keep_ref, send_refs, piece
):
    total = None
    for n, grads in enumerate((own_ref, near_ref, far_ref, last_ref)):
        part = lax.dot_general(normed_ref[n], grads[...], contract_first, preferred_element_type=f32)
        total = part if total is None else total + part
    piece[...] = total
    for n in range(4):
        block = place_ref[0] ^ n
        rows, spare = piece.shape[0] // 4, small_ref.shape[0] // 4
        inner = piece[pl.ds(pl.multiple_of(block * rows, rows), rows), :]
        small = small_ref[pl.ds(pl.multiple_of(block * spare, spare), spare), :]
        if n == 0:
            keep_ref[:rows, :] = inner
            keep_ref[rows:, :] = small
        else:
            send_refs[n - 1, :rows, :] = inner.astype(bf16)
            send_refs[n - 1, rows:, :] = small.astype(bf16)


def inner_quarter(place, own, near, far, last, normed, small):
    width = own.shape[1]
    quarter = normed.shape[2]
    rows = (quarter + small.shape[0]) // 4
    return pl.pallas_call(
        quarter_kernel,
        in_specs=[pl.BlockSpec(memory_space=pltpu.SMEM)]
        + [pl.BlockSpec(memory_space=pltpu.VMEM)] * 6,
        out_shape=[
            jax.ShapeDtypeStruct((rows, width), f32),
            jax.ShapeDtypeStruct((3, rows, width), bf16),
        ],
        scratch_shapes=[pltpu.VMEM((quarter, width), f32)],
        compiler_params=pltpu.CompilerParams(vmem_limit_bytes=vmem_bytes),
        cost_estimate=tiny_cost,
        name="inner_quarter",
    )(place, own, near, far, last, normed, small)


def join_kernel(place_ref, gate_ref, inner_ref, *rest):
    out_ref, small_ref = rest[-2:]
    rows, spare = out_ref.shape[0] // 2, small_ref.shape[0] // 2
    out_ref[:, 1, :] = gate_ref[...].astype(f32)
    for n in range(2):
        at = n * (rows + spare)
        block = inner_ref[at : at + rows + spare, :].astype(f32)
        out_ref[n * rows : (n + 1) * rows, 0, :] = block[:rows]
        small_ref[n * spare : (n + 1) * spare, :] = block[rows:]


def joined(place, flip, gate, inner, before, waits):
    depth, width = gate.shape
    quarter = depth // 4
    small = inner.shape[0] - quarter
    untouched = [*before, *waits]
    return pl.pallas_call(
        join_kernel,
        grid_spec=pltpu.PrefetchScalarGridSpec(
            num_scalar_prefetch=1,
            grid=(2,),
            in_specs=[
                pl.BlockSpec((quarter // 2, width), lambda j, place: (2 * (place[0] ^ flip) + j, 0)),
                pl.BlockSpec((inner.shape[0] // 2, width), lambda j, place: (j, 0)),
            ]
            + [pl.BlockSpec(memory_space=pl.ANY)] * len(untouched),
            out_specs=[
                pl.BlockSpec(
                    (quarter // 2, 2, width), lambda j, place: (2 * (place[0] ^ flip) + j, 0, 0)
                ),
                pl.BlockSpec((small // 2, width), lambda j, place: (2 * (place[0] ^ flip) + j, 0)),
            ],
        ),
        out_shape=[
            jax.ShapeDtypeStruct((depth, 2, width), f32),
            jax.ShapeDtypeStruct((4 * small, width), f32),
        ],
        input_output_aliases={3 + k: k for k in range(len(before))},
        compiler_params=pltpu.CompilerParams(vmem_limit_bytes=vmem_bytes),
        cost_estimate=tiny_cost,
        name="joined",
    )(place, gate, inner, *untouched)


def parts_kernel(small_ref, *out_refs, starts):
    for ref, start in zip(out_refs, starts):
        ref[...] = small_ref[start : start + ref.shape[0], :]


def small_parts(small, sizes):
    width = small.shape[1]
    return pl.pallas_call(
        functools.partial(parts_kernel, starts=[start for start, _ in sizes]),
        out_shape=[jax.ShapeDtypeStruct((rows, width), f32) for _, rows in sizes],
        cost_estimate=tiny_cost,
        name="small_parts",
    )(small)


def carried(ends, decay):
    count = decay.shape[0]
    place = lax.axis_index("wide")

    def split(packed):
        return packed[:count], packed[count : 2 * count], packed[2 * count : 2 * count + 1]

    def through(total):
        return jnp.exp(decay * total)

    zero = jnp.zeros(decay.shape, f32)
    none = jnp.zeros((1, decay.shape[1]), f32)
    before, before_steps, after, after_steps = zero, none, zero, none
    packed = ends
    for bit in (1, 2):
        second = (place & bit) != 0
        own = split(packed)
        other = split(swapped(packed, "wide", bit))
        early = [jnp.where(second, b, a) for a, b in zip(own, other)]
        late = [jnp.where(second, a, b) for a, b in zip(own, other)]
        before = before + jnp.where(second, through(before_steps) * other[0], 0.0)
        before_steps = before_steps + jnp.where(second, other[2], 0.0)
        after = after + jnp.where(second, 0.0, through(after_steps) * other[1])
        after_steps = after_steps + jnp.where(second, 0.0, other[2])
        state = late[0] + through(late[2]) * early[0]
        adjoint = early[1] + through(early[2]) * late[1]
        packed = jnp.concatenate(
            [state, adjoint, jnp.broadcast_to(early[2] + late[2], (8, decay.shape[1]))]
        )
    from_before = passed_along(packed[:count], "wide", 4)
    from_after = passed_along(packed[count : 2 * count], "wide", -4)
    return (
        before + through(before_steps) * from_before,
        after + through(after_steps) * from_after,
    )


def local(
    tokens,
    norm_gain,
    in_weight,
    conv_weight,
    conv_bias,
    select_weight,
    step_weight,
    step_bias,
    decay_log,
    skip_gain,
    out_weight,
    segment_ids,
    cotangent,
):
    rows, features = tokens.shape
    taps = conv_weight.shape[0]
    columns = select_weight.shape[0]
    rank = step_weight.shape[0]
    count = decay_log.shape[0]
    right_half = lax.axis_index("narrow") == 1

    def both_halves(own, other):
        return jnp.concatenate(
            [jnp.where(right_half, other, own), jnp.where(right_half, own, other)], axis=1
        )

    other_tokens = swapped(tokens, "narrow", 1)
    other_cot = swapped(cotangent, "narrow", 1)
    edge, other_edge = to_next_both(edge_rows_of(segment_ids, tokens))

    same_as_last = (segment_ids[rows - 8 :] == segment_ids[rows - 1 :])[:, None]
    padded_ids = jnp.concatenate([jnp.broadcast_to(segment_ids[:1], (taps - 1,)), segment_ids])
    masks = jnp.stack(
        [
            (padded_ids[taps - 1 - lag : taps - 1 - lag + rows] == segment_ids).astype(f32)
            for lag in range(taps)
        ]
        + [jnp.zeros((rows,), f32)] * (8 - taps),
        axis=1,
    )
    whole_ext, normed_ext, inverse = normalized(
        tokens, other_tokens, edge, other_edge, norm_gain[None]
    )
    projected = jnp.einsum(
        "td,dce->cte", normed_ext, in_weight, preferred_element_type=f32
    ).astype(bf16)
    convolved, act, selected = convolve(
        projected, conv_weight, conv_bias[None], select_weight, masks
    )
    other_selected = swapped(selected, "narrow", 1)
    cot_whole = both_halves(cotangent, other_cot)
    gated_grad = lax.dot_general(
        cot_whole, out_weight, contract_last, preferred_element_type=f32
    )
    step_pre, step, ends = scan_ends(
        selected,
        other_selected,
        step_weight,
        step_bias[None],
        act,
        projected,
        gated_grad,
        masks,
        decay_log,
    )
    entry, tail = carried(ends, -jnp.exp(decay_log))
    pair = scan_forward(
        selected,
        other_selected,
        step,
        act,
        projected,
        gated_grad,
        masks,
        decay_log,
        entry,
        skip_gain[None],
    )
    gated, gate_grad = pair[0], pair[1]
    normed = normed_ext[:rows]
    normed_four = quarter_of_four(normed)
    products = (
        lax.dot_general(gated, cot_whole, contract_first, preferred_element_type=f32).astype(bf16),
        lax.dot_general(normed, gate_grad, contract_first, preferred_element_type=f32).astype(bf16),
    )
    out_sum, gate_sum = lax.psum(products, "wide")
    whole = whole_ext[:rows].astype(f32)
    wide_place = lax.axis_index("wide").astype(jnp.int32)

    def after_forward(pair):
        act_grad, select_grad, scan_small = scan_backward(
            selected,
            other_selected,
            step_pre,
            step,
            act,
            projected,
            gated_grad,
            masks,
            decay_log,
            entry,
            tail,
            skip_gain[None],
            step_weight,
            [normed_four, *products],
        )
        other_select_grad = swapped(select_grad, "narrow", 1)

        inner_main, edges, conv_small = convolve_grad(
            select_grad,
            other_select_grad,
            select_weight,
            act_grad,
            convolved,
            act,
            projected,
            conv_weight,
            masks,
        )
        from_next = passed_along(edges[:8], "wide", -1)
        last_rows = edges[8:] + jnp.where(same_as_last, from_next, 0.0)
        inner_grad = jnp.concatenate([inner_main[: rows - 8], last_rows.astype(bf16)])
        normed_part = jnp.einsum(
            "cte,dce->td", jnp.stack([inner_grad, gate_grad]), in_weight, preferred_element_type=f32
        )
        gain_part = jnp.sum(normed_part * whole * inverse, axis=0, keepdims=True)
        row_part = jnp.sum(normed_part * norm_gain * whole, axis=1, keepdims=True)

        gain_sum = gain_part + swapped(gain_part, "narrow", 1)
        spare = -(scan_small.shape[0] + conv_small.shape[0] + 1) % 256
        small = jnp.concatenate(
            [scan_small, conv_small, gain_sum, jnp.zeros((spare, gain_sum.shape[1]), f32)]
        )
        small_piece = scattered(small, (1, 2))
        near = swapped(inner_grad, "wide", 2)
        keep, sends = inner_quarter(
            (wide_place >> 2 & 3)[None],
            inner_grad,
            near,
            swapped(inner_grad, "wide", 1),
            swapped(near, "wide", 1),
            normed_four,
            small_piece,
        )
        first_bits, *more_bits = group_bits(2)
        held = keep
        for n, flip in enumerate(flips(first_bits)[1:]):
            held = held + swapped(sends[n], "wide", flip).astype(f32)
        for bits in more_bits:
            held = scattered(held, bits)
        held = held.astype(bf16)
        for bits in reversed(group_bits(2)):
            held = gathered(held, bits)
        return held, normed_part, row_part

    kinds = jax.eval_shape(after_forward, pair)
    held, normed_part, row_part = lax.cond(
        segment_ids[0] >= 0,
        after_forward,
        lambda pair: jax.tree.map(lambda kind: jnp.zeros(kind.shape, kind.dtype), kinds),
        pair,
    )

    def narrow_halves(array):
        low, high = array[:, :features], array[:, features:]
        return jnp.where(right_half, high, low), jnp.where(right_half, low, high)

    out_part = jnp.dot(gated, out_weight, preferred_element_type=f32)
    out_mine, out_other = narrow_halves(out_part)
    out_total = out_mine + swapped(out_other, "narrow", 1)
    layer_out = (tokens.astype(f32) + out_total).astype(bf16)

    normed_mine, normed_other = narrow_halves(normed_part)
    row_sum = row_part + swapped(row_part, "narrow", 1)
    normed_sum = normed_mine + swapped(normed_other, "narrow", 1)
    gain_mine = jnp.where(right_half, norm_gain[features:], norm_gain[:features])
    whole_grad = inverse * (gain_mine * normed_sum) - tokens.astype(f32) * (
        inverse * inverse * inverse
    ) * (row_sum / (2 * features))
    tokens_grad = (whole_grad + cotangent.astype(f32)).astype(bf16)

    out_weight_grad = out_sum.astype(f32)
    near = swapped(held, "wide", 2)
    quarters = (held, swapped(held, "wide", 1), near, swapped(near, "wide", 1))
    results = []
    for flip, quarter in enumerate(quarters):
        results = joined(
            (wide_place & 3)[None],
            flip,
            gate_sum,
            quarter,
            results,
            [layer_out, tokens_grad] if flip == 1 else [],
        )
    in_weight_grad, small_sum = results
    conv_at = rank + count + 16
    gain_at = conv_at + columns + 16
    (
        step_weight_grad,
        decay_log_grad,
        skip_gain_grad,
        step_bias_grad,
        select_weight_grad,
        conv_weight_grad,
        conv_bias_grad,
        norm_gain_grad,
    ) = small_parts(
        small_sum,
        [
            (0, rank),
            (rank, count),
            (rank + count, 1),
            (rank + count + 1, 1),
            (conv_at, columns),
            (conv_at + columns, taps),
            (conv_at + columns + taps, 1),
            (gain_at, 1),
        ],
    )
    return (
        layer_out,
        tokens_grad,
        norm_gain_grad[0],
        in_weight_grad,
        conv_weight_grad,
        conv_bias_grad[0],
        select_weight_grad,
        step_weight_grad,
        step_bias_grad[0],
        decay_log_grad,
        skip_gain_grad[0],
        out_weight_grad,
    )


def solution(mesh):
    placed = (
        P("wide", "narrow"),
        P(),
        P(None, None, "narrow"),
        P(None, "narrow"),
        P("narrow"),
        P(None, "narrow"),
        P(None, "narrow"),
        P("narrow"),
        P(None, "narrow"),
        P("narrow"),
        P("narrow", None),
        P("wide"),
        P("wide", "narrow"),
    )
    return jax.shard_map(
        local,
        mesh=mesh,
        in_specs=placed,
        out_specs=(
            P("wide", "narrow"),
            P("wide", "narrow"),
            P(),
            P(None, None, "narrow"),
            P(None, "narrow"),
            P("narrow"),
            P(None, "narrow"),
            P(None, "narrow"),
            P("narrow"),
            P(None, "narrow"),
            P("narrow"),
            P("narrow", None),
        ),
        check_vma=False,
    )
```

```python
import functools

import jax
import jax.numpy as jnp
from jax import lax
from jax.experimental import pallas as pl
from jax.experimental.pallas import tpu as pltpu
from jax.sharding import PartitionSpec as P

epsilon = 1e-05
log2e = 1.4426950408889634
reset_step = 1e30
lanes = 128
halo = 16
body_rows = 32
scan_width = 512
vmem_bytes = 56 * 1024 * 1024
tiny_cost = pl.CostEstimate(flops=1, bytes_accessed=1, transcendentals=0)
f32 = jnp.float32
bf16 = jnp.bfloat16
contract_first = (((0,), (0,)), ((), ()))
contract_last = (((1,), (1,)), ((), ()))


def passed_along(array, axis, by):
    peers = lax.axis_size(axis)
    pairs = [(i, i + by) for i in range(peers) if 0 <= i + by < peers]
    return lax.ppermute(array, axis, pairs)


def swapped(array, axis, bit):
    peers = lax.axis_size(axis)
    return lax.ppermute(array, axis, [(i, i ^ bit) for i in range(peers)])


def wide_bits():
    bit, bits = 1, []
    while bit < lax.axis_size("wide"):
        bits.append(bit)
        bit *= 2
    return bits


def to_next_both(array):
    count, sides = lax.axis_size("wide"), lax.axis_size("narrow")
    pairs = [
        (i * sides + k, (i + 1) * sides + (sides - 1 - k))
        for i in range(count - 1)
        for k in range(sides)
    ]
    return passed_along(array, "wide", 1), lax.ppermute(array, ("wide", "narrow"), pairs)


def is_upper(bit):
    return (lax.axis_index("wide") & bit) != 0


def group_bits(size):
    bits, bit = [], 4
    while bit < lax.axis_size("wide"):
        bits.append(bit)
        bit *= 2
    return [tuple(bits[k : k + size]) for k in range(0, len(bits), size)]


def flips(bits):
    return [sum(b for k, b in enumerate(bits) if n >> k & 1) for n in range(2 ** len(bits))]


def scattered(piece, bits):
    rows = piece.shape[0] // 2 ** len(bits)
    here = sum(is_upper(b).astype(jnp.int32) << k for k, b in enumerate(bits))

    def block(n):
        return lax.dynamic_slice_in_dim(piece, (here ^ n) * rows, rows, 0)

    total = block(0).astype(f32)
    for n, flip in enumerate(flips(bits)):
        if n > 0:
            total = total + swapped(block(n).astype(bf16), "wide", flip).astype(f32)
    return total


def gathered(held, bits):
    blocks = [held] + [swapped(held, "wide", flip) for flip in flips(bits)[1:]]
    for bit in bits:
        upper = is_upper(bit)
        blocks = [
            jnp.concatenate([jnp.where(upper, b, a), jnp.where(upper, a, b)])
            for a, b in zip(blocks[0::2], blocks[1::2])
        ]
    return blocks[0]


def quarter_of_four(array):
    width = array.shape[1] // 4
    here = lax.axis_index("wide") & 3

    def quarter(n):
        return lax.dynamic_slice_in_dim(array, (here ^ n) * width, width, 1)

    return jnp.stack(
        [quarter(0)] + [swapped(quarter(n), "wide", n) for n in (2, 1, 3)]
    )


def silu_slope(values):
    logistic = jax.nn.sigmoid(values)
    return logistic * (1.0 + values * (1.0 - logistic))


def softplus(values):
    return jnp.maximum(values, 0.0) + jnp.log1p(jnp.exp(-jnp.abs(values)))


def column_spec(rows, start=0):
    return pl.BlockSpec((rows, scan_width), lambda j: (0, start + j))


def part_spec(part, rows, start=0):
    return pl.BlockSpec((None, rows, scan_width), lambda j: (part, 0, start + j))


def whole_spec(rows, width):
    return pl.BlockSpec((rows, width), lambda j: (0, 0))


def call(kernel, name, width, in_specs, out_specs, out_shape, scratch, *operands):
    return pl.pallas_call(
        kernel,
        grid=(width // scan_width,),
        in_specs=in_specs,
        out_specs=out_specs,
        out_shape=out_shape,
        scratch_shapes=scratch,
        compiler_params=pltpu.CompilerParams(vmem_limit_bytes=vmem_bytes),
        cost_estimate=tiny_cost,
        name=name,
    )(*operands)


def conv_kernel(
    inner_ref,
    conv_weight_ref,
    conv_bias_ref,
    select_ref,
    mask_ref,
    convolved_ref,
    act_ref,
    selected_ref,
    inner,
):
    rows = act_ref.shape[0]
    taps = conv_weight_ref.shape[0]
    inner[:halo, :] = inner_ref[rows:, :].astype(f32)
    inner[halo:, :] = inner_ref[:rows, :].astype(f32)
    total = conv_bias_ref[...] + conv_weight_ref[taps - 1 :, :] * inner[halo:, :]
    for lag in range(1, taps):
        earlier = inner[pl.ds(halo - lag, rows), :] * mask_ref[:, lag : lag + 1]
        total = total + conv_weight_ref[taps - 1 - lag : taps - lag, :] * earlier
    convolved_ref[...] = total
    act = (total * jax.nn.sigmoid(total)).astype(bf16)
    act_ref[...] = act
    part = lax.dot_general(select_ref[...], act, contract_last, preferred_element_type=f32)

    @pl.when(pl.program_id(0) == 0)
    def _():
        selected_ref[...] = part

    @pl.when(pl.program_id(0) > 0)
    def _():
        selected_ref[...] += part


def convolve(projected, conv_weight, conv_bias, select_weight, masks):
    parts, extended, width = projected.shape
    rows = extended - halo
    taps = conv_weight.shape[0]
    columns = select_weight.shape[0]
    return call(
        conv_kernel,
        "convolve",
        width,
        [
            part_spec(0, extended),
            column_spec(taps),
            column_spec(1),
            column_spec(columns),
            whole_spec(rows, masks.shape[1]),
        ],
        [column_spec(rows), column_spec(rows), whole_spec(columns, rows)],
        [
            jax.ShapeDtypeStruct((rows, width), f32),
            jax.ShapeDtypeStruct((rows, width), bf16),
            jax.ShapeDtypeStruct((columns, rows), f32),
        ],
        [pltpu.VMEM((extended, scan_width), f32)],
        projected,
        conv_weight,
        conv_bias,
        select_weight,
        masks,
    )


def coef_columns(coef, block):
    per_tile = lanes // body_rows
    start = pl.multiple_of((block // per_tile) * lanes, lanes)
    tile = coef[:, pl.ds(start, lanes)]
    back = body_rows * lax.rem(block, per_tile)
    return pltpu.roll(tile, lax.rem(lanes - back, lanes), 1)


def ends_kernel(
    selected_ref,
    other_ref,
    step_weight_ref,
    step_bias_ref,
    act_ref,
    gate_ref,
    gated_grad_ref,
    mask_ref,
    decay_log_ref,
    step_pre_ref,
    step_ref,
    ends_ref,
    coef,
    held_step,
    drive,
    scan_grad,
):
    rows = act_ref.shape[0]
    count = decay_log_ref.shape[0]
    rank = step_weight_ref.shape[0]
    decay2 = -jnp.exp(decay_log_ref[...]) * log2e
    selected = selected_ref[...] + other_ref[...]
    coef[...] = selected[rank:, :]
    step_low = selected[:rank, :].astype(bf16)
    step_pre = step_bias_ref[...] + lax.dot_general(
        step_low, step_weight_ref[...], contract_first, preferred_element_type=f32
    )
    step_pre_ref[...] = step_pre
    step = softplus(step_pre)
    step_ref[...] = step
    held_step[...] = jnp.where(mask_ref[:, 1:2] > 0.0, step, reset_step)
    drive[...] = step * act_ref[...].astype(f32)
    gate = gate_ref[...].astype(f32)
    scan_grad[...] = gated_grad_ref[...] * (gate * jax.nn.sigmoid(gate))
    zero = jnp.zeros(decay2.shape, f32)

    def body(block, carried):
        state, product, adjoint = carried
        columns = coef_columns(coef, block)
        for i in range(body_rows):
            row = pl.ds(block * body_rows + i, 1)
            factor = jnp.exp2(held_step[row, :] * decay2)
            state = factor * state + columns[:count, i : i + 1] * drive[row, :]
            product = factor * product
            adjoint = adjoint + product * (columns[count:, i : i + 1] * scan_grad[row, :])
        return state, product, adjoint

    state, product, adjoint = lax.fori_loop(0, rows // body_rows, body, (zero, zero + 1.0, zero))
    ends_ref[:count, :] = state
    ends_ref[count : 2 * count, :] = adjoint
    total = jnp.sum(held_step[...], axis=0, keepdims=True)
    ends_ref[2 * count :, :] = jnp.broadcast_to(total, (8, total.shape[1]))


def scan_ends(
    selected, other, step_weight, step_bias, act, projected, gated_grad, masks, decay_log
):
    rows, width = act.shape
    count = decay_log.shape[0]
    columns = selected.shape[0]
    rank = step_weight.shape[0]
    return call(
        ends_kernel,
        "scan_ends",
        width,
        [
            whole_spec(columns, rows),
            whole_spec(columns, rows),
            column_spec(rank),
            column_spec(1),
            column_spec(rows),
            part_spec(1, rows),
            column_spec(rows),
            whole_spec(rows, masks.shape[1]),
            column_spec(count),
        ],
        [column_spec(rows), column_spec(rows), column_spec(2 * count + 8)],
        [
            jax.ShapeDtypeStruct((rows, width), f32),
            jax.ShapeDtypeStruct((rows, width), f32),
            jax.ShapeDtypeStruct((2 * count + 8, width), f32),
        ],
        [pltpu.VMEM((2 * count, rows), f32)] + [pltpu.VMEM((rows, scan_width), f32)] * 3,
        selected,
        other,
        step_weight,
        step_bias,
        act,
        projected,
        gated_grad,
        masks,
        decay_log,
    )


def lane_tiles(values):
    return [values[:, k : k + lanes] for k in range(0, values.shape[1], lanes)]


def tree_sum(parts):
    while len(parts) > 1:
        odd = parts[len(parts) // 2 * 2 :]
        parts = [a + b for a, b in zip(parts[0::2], parts[1::2])] + odd
    return parts[0]


def keep_halves(scratch, i, values):
    for k, tile in enumerate(lane_tiles(values)):
        at = (k * body_rows + i) * 8
        scratch[at : at + 8, :] = tile[:8] + tile[8:]


def put_state_sums(scratch, out_ref, block):
    for group in range(body_rows // 8):
        row = pl.ds(pl.multiple_of(block * body_rows + group * 8, 8), 8)
        for k in range(out_ref.shape[1] // lanes):
            at = (k * body_rows + group * 8) * 8
            total = tree_sum([scratch[pl.ds(at + n, 8, stride=8), :] for n in range(8)])
            out_ref[row, k * lanes : (k + 1) * lanes] = total


def lane_sums(values):
    ones = jnp.ones((8, lanes), bf16)
    high = values.astype(bf16)
    low = (values - high.astype(f32)).astype(bf16)
    total = lax.dot_general(ones, high, contract_last, preferred_element_type=f32)
    total += lax.dot_general(ones, low, contract_last, preferred_element_type=f32)
    return total[:1, :]


def at_token(t, count):
    return pl.ds(pl.multiple_of(t * count, count), count)


def forward_kernel(
    selected_ref,
    other_ref,
    step_ref,
    act_ref,
    gate_ref,
    gated_grad_ref,
    mask_ref,
    decay_log_ref,
    passed_ref,
    entering_ref,
    skip_ref,
    pair_ref,
    entry_ref,
    coef,
    held_step,
    drive,
    scanned,
    halves,
):
    rows = step_ref.shape[0]
    count = decay_log_ref.shape[0]
    rank = selected_ref.shape[0] - 2 * count
    decay = -jnp.exp(decay_log_ref[...])
    decay2 = decay * log2e
    before_steps = passed_ref[2 * count : 2 * count + 1, :]
    entry = passed_ref[:count, :] + through(decay, before_steps) * entering_ref[...]
    entry_ref[...] = entry
    coef[...] = selected_ref[rank:, :] + other_ref[rank:, :]
    act = act_ref[...].astype(f32)
    held_step[...] = jnp.where(mask_ref[:, 1:2] > 0.0, step_ref[...], reset_step)
    drive[...] = step_ref[...] * act

    def forward(block, state):
        columns = coef_columns(coef, block)
        for i in range(body_rows):
            row = pl.ds(block * body_rows + i, 1)
            factor = jnp.exp2(held_step[row, :] * decay2)
            state = factor * state + columns[:count, i : i + 1] * drive[row, :]
            keep_halves(halves, i, columns[count:, i : i + 1] * state)
        put_state_sums(halves, scanned, block)
        return state

    lax.fori_loop(0, rows // body_rows, forward, entry)
    gate = gate_ref[...].astype(f32)
    logistic = jax.nn.sigmoid(gate)
    total = scanned[...] + skip_ref[...] * act
    pair_ref[0] = (total * (gate * logistic)).astype(bf16)
    slope = logistic * (1.0 + gate * (1.0 - logistic))
    pair_ref[1] = (gated_grad_ref[...] * total * slope).astype(bf16)


def scan_forward(
    selected, other, step, act, projected, gated_grad, masks, decay_log, passed, entering, skip_gain
):
    rows, width = step.shape
    count = decay_log.shape[0]
    columns = selected.shape[0]
    return call(
        forward_kernel,
        "scan_forward",
        width,
        [
            whole_spec(columns, rows),
            whole_spec(columns, rows),
            column_spec(rows),
            column_spec(rows),
            part_spec(1, rows),
            column_spec(rows),
            whole_spec(rows, masks.shape[1]),
            column_spec(count),
            column_spec(2 * count + 8),
            column_spec(count),
            column_spec(1),
        ],
        [pl.BlockSpec((2, rows, scan_width), lambda j: (0, 0, j)), column_spec(count)],
        [
            jax.ShapeDtypeStruct((2, rows, width), bf16),
            jax.ShapeDtypeStruct((count, width), f32),
        ],
        [pltpu.VMEM((2 * count, rows), f32)]
        + [pltpu.VMEM((rows, scan_width), f32)] * 3
        + [pltpu.VMEM((8 * body_rows * (scan_width // lanes), lanes), f32)],
        selected,
        other,
        step,
        act,
        projected,
        gated_grad,
        masks,
        decay_log,
        passed,
        entering,
        skip_gain,
    )


def backward_kernel(
    selected_ref,
    other_ref,
    step_pre_ref,
    step_ref,
    act_ref,
    gate_ref,
    gated_grad_ref,
    mask_ref,
    decay_log_ref,
    entry_ref,
    passed_ref,
    returning_ref,
    skip_ref,
    step_weight_ref,
    act_grad_ref,
    select_grad_ref,
    small_ref,
    coef,
    held_step,
    drive,
    scan_grad,
    weighted,
    held_sum,
    states,
    factors,
    halves,
    more_halves,
    in_sum,
    read_sum,
):
    rows = step_ref.shape[0]
    count = decay_log_ref.shape[0]
    rank = step_weight_ref.shape[0]
    blocks = rows // body_rows
    decay = -jnp.exp(decay_log_ref[...])
    decay2 = decay * log2e
    after_steps = passed_ref[2 * count + 1 : 2 * count + 2, :]
    tail = passed_ref[count : 2 * count, :] + through(decay, after_steps) * returning_ref[...]
    selected = selected_ref[...] + other_ref[...]
    coef[...] = selected[rank:, :]
    step_low = selected[:rank, :].astype(bf16)
    step = step_ref[...]
    act = act_ref[...].astype(f32)
    held_step[...] = jnp.where(mask_ref[:, 1:2] > 0.0, step, reset_step)
    drive[...] = step * act
    gate = gate_ref[...].astype(f32)
    grads = gated_grad_ref[...] * (gate * jax.nn.sigmoid(gate))
    scan_grad[...] = grads
    small_ref[rank + count : rank + count + 1, :] = jnp.sum(grads * act, axis=0, keepdims=True)
    states[:count, :] = entry_ref[...]

    @pl.when(pl.program_id(0) == 0)
    def _():
        in_sum[...] = jnp.zeros(in_sum.shape, f32)
        read_sum[...] = jnp.zeros(read_sum.shape, f32)
        select_grad_ref[...] = jnp.zeros(select_grad_ref.shape, f32)

    def forward(block, state):
        columns = coef_columns(coef, block)
        for i in range(body_rows):
            t = block * body_rows + i
            row = pl.ds(t, 1)
            factor = jnp.exp2(held_step[row, :] * decay2)
            state = factor * state + columns[:count, i : i + 1] * drive[row, :]
            factors[at_token(t, count), :] = factor
            states[at_token(t + 1, count), :] = state
        return state

    lax.fori_loop(0, blocks, forward, entry_ref[...])

    def backward(k, carried):
        adjoint, decay_grad = carried
        block = blocks - 1 - k
        columns = coef_columns(coef, block)
        for i in range(body_rows - 1, -1, -1):
            t = block * body_rows + i
            row = pl.ds(t, 1)
            here = at_token(t, count)
            grad = scan_grad[row, :]
            summed = columns[count:, i : i + 1] * grad + adjoint
            read_sum[here, :] += tree_sum(lane_tiles(grad * states[at_token(t + 1, count), :]))
            in_sum[here, :] += tree_sum(lane_tiles(summed * drive[row, :]))
            keep_halves(halves, i, summed * columns[:count, i : i + 1])
            adjoint = factors[here, :] * summed
            held = adjoint * states[here, :]
            decay_grad = decay_grad + held * step_ref[row, :]
            keep_halves(more_halves, i, held * decay)
        put_state_sums(halves, weighted, block)
        put_state_sums(more_halves, held_sum, block)
        return adjoint, decay_grad

    ignored, decay_grad = lax.fori_loop(
        0, blocks, backward, (tail, jnp.zeros(decay.shape, f32))
    )
    act_grad_ref[...] = step * weighted[...] + skip_ref[...] * scan_grad[...]
    step_grad = act * weighted[...] + held_sum[...]
    pre_grad = (step_grad * jax.nn.sigmoid(step_pre_ref[...])).astype(bf16)
    small_ref[:rank, :] = jnp.dot(step_low, pre_grad, preferred_element_type=f32)
    small_ref[rank : rank + count, :] = decay_grad * decay
    bias_grad = jnp.sum(pre_grad.astype(f32), axis=0, keepdims=True)
    small_ref[rank + count + 1 : rank + count + 2, :] = bias_grad
    spare = small_ref.shape[0] - (rank + count + 2)
    small_ref[rank + count + 2 :, :] = jnp.zeros((spare, small_ref.shape[1]), f32)
    select_grad_ref[:rank, :] += lax.dot_general(
        step_weight_ref[...], pre_grad, contract_last, preferred_element_type=f32
    )

    @pl.when(pl.program_id(0) == pl.num_programs(0) - 1)
    def _():
        for n in range(count):
            at = pl.ds(n, rows, stride=count)
            select_grad_ref[rank + n : rank + n + 1, :] = lane_sums(in_sum[at, :])
            select_grad_ref[rank + count + n : rank + count + n + 1, :] = lane_sums(read_sum[at, :])


def scan_backward(
    selected,
    other,
    step_pre,
    step,
    act,
    projected,
    gated_grad,
    masks,
    decay_log,
    entry,
    passed,
    returning,
    skip_gain,
    step_weight,
):
    rows, width = step.shape
    count = decay_log.shape[0]
    columns = selected.shape[0]
    rank = step_weight.shape[0]
    half_rows = 8 * body_rows * (scan_width // lanes)
    small = rank + count + 16
    return call(
        backward_kernel,
        "scan_backward",
        width,
        [
            whole_spec(columns, rows),
            whole_spec(columns, rows),
            column_spec(rows),
            column_spec(rows),
            column_spec(rows),
            part_spec(1, rows),
            column_spec(rows),
            whole_spec(rows, masks.shape[1]),
            column_spec(count),
            column_spec(count),
            column_spec(2 * count + 8),
            column_spec(count),
            column_spec(1),
            column_spec(rank),
        ],
        [column_spec(rows), whole_spec(columns, rows), column_spec(small)],
        [
            jax.ShapeDtypeStruct((rows, width), f32),
            jax.ShapeDtypeStruct((columns, rows), f32),
            jax.ShapeDtypeStruct((small, width), f32),
        ],
        [pltpu.VMEM((2 * count, rows), f32)]
        + [pltpu.VMEM((rows, scan_width), f32)] * 5
        + [
            pltpu.VMEM(((rows + 1) * count, scan_width), f32),
            pltpu.VMEM((rows * count, scan_width), f32),
            pltpu.VMEM((half_rows, lanes), f32),
            pltpu.VMEM((half_rows, lanes), f32),
            pltpu.VMEM((rows * count, lanes), f32),
            pltpu.VMEM((rows * count, lanes), f32),
        ],
        selected,
        other,
        step_pre,
        step,
        act,
        projected,
        gated_grad,
        masks,
        decay_log,
        entry,
        passed,
        returning,
        skip_gain,
        step_weight,
    )


def conv_grad_kernel(
    select_grad_ref,
    other_ref,
    select_ref,
    act_grad_ref,
    convolved_ref,
    act_ref,
    inner_ref,
    conv_weight_ref,
    mask_ref,
    wait_ref,
    inner_grad_ref,
    edge_ref,
    small_ref,
    inner,
    shifted,
):
    rows = act_ref.shape[0]
    taps = conv_weight_ref.shape[0]
    columns = select_ref.shape[0]
    select_grad = (select_grad_ref[...] + other_ref[...]).astype(bf16)
    total = act_grad_ref[...] + lax.dot_general(
        select_grad, select_ref[...], contract_first, preferred_element_type=f32
    )
    conv_grad = total * silu_slope(convolved_ref[...])
    small_ref[:columns, :] = jnp.dot(select_grad, act_ref[...], preferred_element_type=f32)
    inner[:halo, :] = inner_ref[rows:, :].astype(f32)
    inner[halo:, :] = inner_ref[:rows, :].astype(f32)
    edges = jnp.zeros((8, conv_grad.shape[1]), f32)
    shifted[:8, :] = edges
    shifted[rows + 8 :, :] = edges
    out = conv_weight_ref[taps - 1 :, :] * conv_grad
    before = edges
    small_ref[columns + taps - 1 : columns + taps, :] = jnp.sum(
        conv_grad * inner[halo:, :], axis=0, keepdims=True
    )
    for lag in range(1, taps):
        masked = conv_grad * mask_ref[:, lag : lag + 1]
        at = taps - 1 - lag
        small_ref[columns + at : columns + at + 1, :] = jnp.sum(
            masked * inner[pl.ds(halo - lag, rows), :], axis=0, keepdims=True
        )
        shifted[8 : rows + 8, :] = masked
        weight = conv_weight_ref[at : at + 1, :]
        out = out + weight * shifted[pl.ds(8 + lag, rows), :]
        before = before + weight * shifted[pl.ds(lag, 8), :]
    small_ref[columns + taps : columns + taps + 1, :] = jnp.sum(conv_grad, axis=0, keepdims=True)
    spare = small_ref.shape[0] - (columns + taps + 1)
    small_ref[columns + taps + 1 :, :] = jnp.zeros((spare, small_ref.shape[1]), f32)
    inner_grad_ref[...] = out.astype(bf16)
    edge_ref[:8, :] = before
    edge_ref[8:, :] = out[rows - 8 :, :]


def convolve_grad(
    select_grad, other, select_weight, act_grad, convolved, act, projected, conv_weight, masks, wait
):
    rows, width = act.shape
    extended = rows + halo
    columns = select_weight.shape[0]
    taps = conv_weight.shape[0]
    small = columns + 16
    return call(
        conv_grad_kernel,
        "convolve_grad",
        width,
        [
            whole_spec(columns, rows),
            whole_spec(columns, rows),
            column_spec(columns),
            column_spec(rows),
            column_spec(rows),
            column_spec(rows),
            part_spec(0, extended),
            column_spec(taps),
            whole_spec(rows, masks.shape[1]),
            pl.BlockSpec(memory_space=pl.ANY),
        ],
        [column_spec(rows), column_spec(16), column_spec(small)],
        [
            jax.ShapeDtypeStruct((rows, width), bf16),
            jax.ShapeDtypeStruct((16, width), f32),
            jax.ShapeDtypeStruct((small, width), f32),
        ],
        [pltpu.VMEM((extended, scan_width), f32), pltpu.VMEM((rows + 16, scan_width), f32)],
        select_grad,
        other,
        select_weight,
        act_grad,
        convolved,
        act,
        projected,
        conv_weight,
        masks,
        wait,
    )


def normalize_kernel(
    own_ref,
    other_ref,
    edge_ref,
    other_edge_ref,
    gain_ref,
    ids_ref,
    whole_ref,
    normed_ref,
    inverse_ref,
    mask_ref,
):
    rows, half = own_ref.shape
    ids = ids_ref[...].astype(f32)
    place = lax.broadcasted_iota(jnp.int32, ids.shape, 1)
    same = []
    for lag in range(8):
        earlier = jnp.where(place < lag, ids[:, :1], pltpu.roll(ids, lag, 1)) if lag else ids
        same.append(jnp.where(earlier == ids, 1.0, 0.0))
    spare = jnp.zeros((lanes - 8, rows), f32)
    mask_ref[...] = jnp.concatenate(same + [spare]).T
    right = lax.axis_index("narrow") == 1
    for at, own, other in ((0, own_ref, other_ref), (rows, edge_ref, other_edge_ref)):
        end = at + own.shape[0]
        whole_ref[at:end, :half] = jnp.where(right, other[...], own[...])
        whole_ref[at:end, half:] = jnp.where(right, own[...], other[...])
    whole = whole_ref[...].astype(f32)
    inverse = lax.rsqrt(jnp.mean(whole * whole, axis=1, keepdims=True) + epsilon)
    normed_ref[...] = (whole * inverse * gain_ref[...]).astype(bf16)
    inverse_ref[...] = inverse[:rows]


def normalized(own, other, edge, other_edge, gain, ids):
    rows, half = own.shape
    extended = rows + edge.shape[0]
    return pl.pallas_call(
        normalize_kernel,
        out_shape=[
            jax.ShapeDtypeStruct((extended, 2 * half), bf16),
            jax.ShapeDtypeStruct((extended, 2 * half), bf16),
            jax.ShapeDtypeStruct((rows, 1), f32),
            jax.ShapeDtypeStruct((rows, lanes), f32),
        ],
        cost_estimate=tiny_cost,
        name="normalized",
    )(own, other, edge, other_edge, gain, ids)


def after(array, *waits):
    anywhere = pl.BlockSpec(memory_space=pl.ANY)
    return pl.pallas_call(
        lambda *refs: None,
        in_specs=[anywhere] * (1 + len(waits)),
        out_specs=anywhere,
        out_shape=jax.ShapeDtypeStruct(array.shape, array.dtype),
        input_output_aliases={0: 0},
        cost_estimate=tiny_cost,
        name="after",
    )(array, *waits)


def edge_kernel(ids_ref, tokens_ref, out_ref):
    rows = ids_ref.shape[0]
    taps = 4
    out_ref[...] = tokens_ref[...]
    place = lax.broadcasted_iota(jnp.int32, (halo, 1), 0)
    same = jnp.zeros((halo, 1), f32)
    for lag in range(taps):
        here = jnp.where(ids_ref[rows - 1 - lag] == ids_ref[rows - 1], 1.0, 0.0)
        same = same + jnp.where(place == halo - 1 - lag, here, 0.0)
    out_ref[...] = (tokens_ref[...].astype(f32) * same).astype(bf16)


def edge_rows_of(ids, tokens):
    rows, width = tokens.shape
    return pl.pallas_call(
        edge_kernel,
        grid=(1,),
        in_specs=[
            pl.BlockSpec(memory_space=pltpu.SMEM),
            pl.BlockSpec((halo, width), lambda j: (rows // halo - 1, 0)),
        ],
        out_specs=pl.BlockSpec((halo, width), lambda j: (0, 0)),
        out_shape=jax.ShapeDtypeStruct((halo, width), bf16),
        cost_estimate=tiny_cost,
        name="edge_rows",
    )(ids, tokens)


def small_kernel(place_ref, scan_ref, conv_ref, gain_ref, other_gain_ref, keep_ref, sends_ref, rows):
    at = 0
    for ref in (scan_ref, conv_ref):
        rows[at : at + ref.shape[0], :] = ref[...]
        at += ref.shape[0]
    rows[at:, :] = jnp.broadcast_to(
        gain_ref[...] + other_gain_ref[...], (rows.shape[0] - at, rows.shape[1])
    )
    quarter = keep_ref.shape[0]
    for n in range(4):
        start = pl.multiple_of((place_ref[0] ^ n) * quarter, quarter)
        block = rows[pl.ds(start, quarter), :]
        if n == 0:
            keep_ref[...] = block
        else:
            sends_ref[n - 1] = block.astype(bf16)


def small_quarters(place, scan_small, conv_small, gain, other_gain):
    width = scan_small.shape[1]
    rows = -(-(scan_small.shape[0] + conv_small.shape[0] + 1) // 256) * 256
    return pl.pallas_call(
        small_kernel,
        in_specs=[pl.BlockSpec(memory_space=pltpu.SMEM)]
        + [pl.BlockSpec(memory_space=pltpu.VMEM)] * 4,
        out_shape=[
            jax.ShapeDtypeStruct((rows // 4, width), f32),
            jax.ShapeDtypeStruct((3, rows // 4, width), bf16),
        ],
        scratch_shapes=[pltpu.VMEM((rows, width), f32)],
        cost_estimate=tiny_cost,
        name="small_quarters",
    )(place, scan_small, conv_small, gain, other_gain)


def quarter_kernel(
    place_ref,
    own_ref,
    near_ref,
    far_ref,
    last_ref,
    normed_ref,
    small_ref,
    first_ref,
    second_ref,
    third_ref,
    *rest,
):
    keep_ref, sends_ref, piece, small = rest[-4:]
    total = None
    for n, grads in enumerate((own_ref, near_ref, far_ref, last_ref)):
        part = lax.dot_general(normed_ref[n], grads[...], contract_first, preferred_element_type=f32)
        total = part if total is None else total + part
    piece[...] = total
    small[...] = small_ref[...] + sum(
        ref[...].astype(f32) for ref in (first_ref, second_ref, third_ref)
    )
    rows, spare = piece.shape[0] // 4, small.shape[0] // 4
    for n in range(4):
        block = place_ref[0] ^ n
        inner_rows = piece[pl.ds(pl.multiple_of(block * rows, rows), rows), :]
        small_rows = small[pl.ds(pl.multiple_of(block * spare, spare), spare), :]
        if n == 0:
            keep_ref[:rows, :] = inner_rows
            keep_ref[rows:, :] = small_rows
        else:
            sends_ref[n - 1, :rows, :] = inner_rows.astype(bf16)
            sends_ref[n - 1, rows:, :] = small_rows.astype(bf16)


def inner_quarter(place, own, near, far, last, normed, smalls, waits):
    width = own.shape[1]
    quarter = normed.shape[2]
    spare = smalls[0].shape[0]
    rows = (quarter + spare) // 4
    return pl.pallas_call(
        quarter_kernel,
        in_specs=[pl.BlockSpec(memory_space=pltpu.SMEM)]
        + [pl.BlockSpec(memory_space=pltpu.VMEM)] * 9
        + [pl.BlockSpec(memory_space=pl.ANY)] * len(waits),
        out_shape=[
            jax.ShapeDtypeStruct((rows, width), f32),
            jax.ShapeDtypeStruct((3, rows, width), bf16),
        ],
        scratch_shapes=[pltpu.VMEM((quarter, width), f32), pltpu.VMEM((spare, width), f32)],
        compiler_params=pltpu.CompilerParams(vmem_limit_bytes=vmem_bytes),
        cost_estimate=tiny_cost,
        name="inner_quarter",
    )(place, own, near, far, last, normed, *smalls, *waits)


def join_kernel(place_ref, gate_ref, inner_ref, *rest):
    out_ref, small_ref = rest[-2:]
    rows, spare = out_ref.shape[0] // 2, small_ref.shape[0] // 2
    out_ref[:, 1, :] = gate_ref[...].astype(f32)
    for n in range(2):
        at = n * (rows + spare)
        block = inner_ref[at : at + rows + spare, :].astype(f32)
        out_ref[n * rows : (n + 1) * rows, 0, :] = block[:rows]
        small_ref[n * spare : (n + 1) * spare, :] = block[rows:]


def joined(place, flip, gate, inner, before, waits):
    depth, width = gate.shape
    quarter = depth // 4
    small = inner.shape[0] - quarter
    untouched = [*before, *waits]
    return pl.pallas_call(
        join_kernel,
        grid_spec=pltpu.PrefetchScalarGridSpec(
            num_scalar_prefetch=1,
            grid=(2,),
            in_specs=[
                pl.BlockSpec((quarter // 2, width), lambda j, place: (2 * (place[0] ^ flip) + j, 0)),
                pl.BlockSpec((inner.shape[0] // 2, width), lambda j, place: (j, 0)),
            ]
            + [pl.BlockSpec(memory_space=pl.ANY)] * len(untouched),
            out_specs=[
                pl.BlockSpec(
                    (quarter // 2, 2, width), lambda j, place: (2 * (place[0] ^ flip) + j, 0, 0)
                ),
                pl.BlockSpec((small // 2, width), lambda j, place: (2 * (place[0] ^ flip) + j, 0)),
            ],
        ),
        out_shape=[
            jax.ShapeDtypeStruct((depth, 2, width), f32),
            jax.ShapeDtypeStruct((4 * small, width), f32),
        ],
        input_output_aliases={3 + k: k for k in range(len(before))},
        compiler_params=pltpu.CompilerParams(vmem_limit_bytes=vmem_bytes),
        cost_estimate=tiny_cost,
        name="joined",
    )(place, gate, inner, *untouched)


def parts_kernel(small_ref, *out_refs, starts):
    for ref, start in zip(out_refs, starts):
        ref[...] = small_ref[start : start + ref.shape[0], :]


def small_parts(small, sizes):
    width = small.shape[1]
    return pl.pallas_call(
        functools.partial(parts_kernel, starts=[start for start, _ in sizes]),
        out_shape=[jax.ShapeDtypeStruct((rows, width), f32) for _, rows in sizes],
        cost_estimate=tiny_cost,
        name="small_parts",
    )(small)


def through(decay, total):
    return jnp.exp(decay * total)


def round_kernel(second_ref, decay_log_ref, own_ref, other_ref, passed_ref, ends_ref, new_passed_ref):
    count = decay_log_ref.shape[0]
    decay = -jnp.exp(decay_log_ref[...])
    second = second_ref[0] > 0

    def split(ref):
        return ref[:count], ref[count : 2 * count], ref[2 * count : 2 * count + 1]

    own, other = split(own_ref), split(other_ref)
    early = [jnp.where(second, b, a) for a, b in zip(own, other)]
    late = [jnp.where(second, a, b) for a, b in zip(own, other)]
    ends_ref[:count, :] = late[0] + through(decay, late[2]) * early[0]
    ends_ref[count : 2 * count, :] = early[1] + through(decay, early[2]) * late[1]
    ends_ref[2 * count :, :] = jnp.broadcast_to(early[2] + late[2], (8, decay.shape[1]))
    before, after = passed_ref[:count], passed_ref[count : 2 * count]
    before_steps = passed_ref[2 * count : 2 * count + 1]
    after_steps = passed_ref[2 * count + 1 : 2 * count + 2]
    new_passed_ref[:count, :] = before + jnp.where(second, through(decay, before_steps) * other[0], 0.0)
    new_passed_ref[count : 2 * count, :] = after + jnp.where(
        second, 0.0, through(decay, after_steps) * other[1]
    )
    new_passed_ref[2 * count : 2 * count + 1, :] = before_steps + jnp.where(second, other[2], 0.0)
    new_passed_ref[2 * count + 1 : 2 * count + 2, :] = after_steps + jnp.where(second, 0.0, other[2])


def carried(ends, decay_log):
    count, width = decay_log.shape
    place = lax.axis_index("wide").astype(jnp.int32)
    passed = jnp.zeros((2 * count + 8, width), f32)
    packed = ends
    vmem = pl.BlockSpec(memory_space=pltpu.VMEM)
    for k in range(2):
        packed, passed = pl.pallas_call(
            round_kernel,
            in_specs=[pl.BlockSpec(memory_space=pltpu.SMEM)] + [vmem] * 4,
            out_shape=[
                jax.ShapeDtypeStruct(ends.shape, f32),
                jax.ShapeDtypeStruct(passed.shape, f32),
            ],
            cost_estimate=tiny_cost,
            name="carry_round",
        )((place >> k & 1)[None], decay_log, packed, swapped(packed, "wide", 2**k), passed)
    from_before = passed_along(packed[:count], "wide", 4)
    from_after = passed_along(packed[count : 2 * count], "wide", -4)
    return passed, from_before, from_after


def local(
    tokens,
    norm_gain,
    in_weight,
    conv_weight,
    conv_bias,
    select_weight,
    step_weight,
    step_bias,
    decay_log,
    skip_gain,
    out_weight,
    segment_ids,
    cotangent,
):
    rows, features = tokens.shape
    taps = conv_weight.shape[0]
    columns = select_weight.shape[0]
    rank = step_weight.shape[0]
    count = decay_log.shape[0]
    right_half = lax.axis_index("narrow") == 1

    def both_halves(own, other):
        return jnp.concatenate(
            [jnp.where(right_half, other, own), jnp.where(right_half, own, other)], axis=1
        )

    other_tokens = swapped(tokens, "narrow", 1)
    other_cot = swapped(cotangent, "narrow", 1)
    edge, other_edge = to_next_both(edge_rows_of(segment_ids, tokens))

    same_as_last = (segment_ids[rows - 8 :] == segment_ids[rows - 1 :])[:, None]
    whole_ext, normed_ext, inverse, masks = normalized(
        tokens, other_tokens, edge, other_edge, norm_gain[None], segment_ids[None]
    )
    projected = jnp.einsum(
        "td,dce->cte", normed_ext, in_weight, preferred_element_type=f32
    ).astype(bf16)
    convolved, act, selected = convolve(
        projected, conv_weight, conv_bias[None], select_weight, masks
    )
    other_selected = swapped(selected, "narrow", 1)
    cot_whole = both_halves(cotangent, other_cot)
    gated_grad = lax.dot_general(
        cot_whole, out_weight, contract_last, preferred_element_type=f32
    )
    step_pre, step, ends = scan_ends(
        selected,
        other_selected,
        step_weight,
        step_bias[None],
        act,
        projected,
        gated_grad,
        masks,
        decay_log,
    )
    passed, entering, returning = carried(ends, decay_log)
    pair, entry = scan_forward(
        selected,
        other_selected,
        step,
        act,
        projected,
        gated_grad,
        masks,
        decay_log,
        passed,
        entering,
        skip_gain[None],
    )
    gated, gate_grad = pair[0], pair[1]
    normed = normed_ext[:rows]
    normed_four = quarter_of_four(after(normed, pair))
    products = (
        lax.dot_general(gated, cot_whole, contract_first, preferred_element_type=f32).astype(bf16),
        lax.dot_general(normed, gate_grad, contract_first, preferred_element_type=f32).astype(bf16),
    )
    out_sum, gate_sum = lax.psum(products, "wide")
    whole = whole_ext[:rows].astype(f32)
    wide_place = lax.axis_index("wide").astype(jnp.int32)
    four_place = (wide_place & 3)[None]

    def narrow_halves(array):
        low, high = array[:, :features], array[:, features:]
        return jnp.where(right_half, high, low), jnp.where(right_half, low, high)

    def after_forward(products):
        out_part = jnp.dot(gated, out_weight, preferred_element_type=f32)
        out_mine, out_other = narrow_halves(out_part)
        out_theirs = swapped(out_other, "narrow", 1)
        act_grad, select_grad, scan_small = scan_backward(
            selected,
            other_selected,
            step_pre,
            step,
            act,
            projected,
            gated_grad,
            masks,
            decay_log,
            entry,
            passed,
            returning,
            skip_gain[None],
            step_weight,
        )
        layer_out = (tokens.astype(f32) + (out_mine + out_theirs)).astype(bf16)
        inner_main, edges, conv_small = convolve_grad(
            select_grad,
            swapped(select_grad, "narrow", 1),
            select_weight,
            act_grad,
            convolved,
            act,
            projected,
            conv_weight,
            masks,
            out_theirs,
        )
        from_next = passed_along(edges[:8], "wide", -1)
        last_rows = edges[8:] + jnp.where(same_as_last, from_next, 0.0)
        inner_grad = jnp.concatenate([inner_main[: rows - 8], last_rows.astype(bf16)])
        near = swapped(inner_grad, "wide", 2)
        far = swapped(inner_grad, "wide", 1)
        normed_part = jnp.einsum(
            "cte,dce->td", jnp.stack([inner_grad, gate_grad]), in_weight, preferred_element_type=f32
        )
        gain_part = jnp.sum(normed_part * whole * inverse, axis=0, keepdims=True)
        row_part = jnp.sum(normed_part * norm_gain * whole, axis=1)[None]
        keep, sends = small_quarters(
            four_place, scan_small, conv_small, gain_part, swapped(gain_part, "narrow", 1)
        )
        smalls = [keep] + [swapped(sends[n - 1], "wide", n) for n in (1, 2, 3)]
        normed_mine, normed_other = narrow_halves(normed_part)
        row_theirs = swapped(row_part, "narrow", 1)
        normed_theirs = swapped(normed_other, "narrow", 1)
        keep, sends = inner_quarter(
            (wide_place >> 2 & 3)[None],
            inner_grad,
            near,
            far,
            swapped(after(near, sends), "wide", 1),
            normed_four,
            smalls,
            [row_theirs],
        )
        row_sum = (row_part + row_theirs).reshape(rows, 1)
        gain_mine = jnp.where(right_half, norm_gain[features:], norm_gain[:features])
        whole_grad = inverse * (gain_mine * (normed_mine + normed_theirs)) - tokens.astype(f32) * (
            inverse * inverse * inverse
        ) * (row_sum / (2 * features))
        tokens_grad = (whole_grad + cotangent.astype(f32)).astype(bf16)
        first_bits, *more_bits = group_bits(2)
        held = keep
        for n, flip in enumerate(flips(first_bits)[1:]):
            held = held + swapped(sends[n], "wide", flip).astype(f32)
        for bits in more_bits:
            held = scattered(held, bits)
        held = held.astype(bf16)
        for bits in reversed(group_bits(2)):
            held = gathered(held, bits)
        return held, layer_out, tokens_grad

    kinds = jax.eval_shape(after_forward, products)
    held, layer_out, tokens_grad = lax.cond(
        segment_ids[0] >= 0,
        after_forward,
        lambda pair: jax.tree.map(lambda kind: jnp.zeros(kind.shape, kind.dtype), kinds),
        products,
    )

    out_weight_grad = out_sum.astype(f32)
    near = swapped(held, "wide", 2)
    quarters = (held, swapped(held, "wide", 1), near, swapped(near, "wide", 1))
    results = []
    for flip, quarter in enumerate(quarters):
        results = joined(
            four_place, flip, gate_sum, quarter, results, [] if flip else [out_weight_grad]
        )
    in_weight_grad, small_sum = results
    conv_at = rank + count + 16
    gain_at = conv_at + columns + 16
    (
        step_weight_grad,
        decay_log_grad,
        skip_gain_grad,
        step_bias_grad,
        select_weight_grad,
        conv_weight_grad,
        conv_bias_grad,
        norm_gain_grad,
    ) = small_parts(
        small_sum,
        [
            (0, rank),
            (rank, count),
            (rank + count, 1),
            (rank + count + 1, 1),
            (conv_at, columns),
            (conv_at + columns, taps),
            (conv_at + columns + taps, 1),
            (gain_at, 1),
        ],
    )
    return (
        layer_out,
        tokens_grad,
        norm_gain_grad[0],
        in_weight_grad,
        conv_weight_grad,
        conv_bias_grad[0],
        select_weight_grad,
        step_weight_grad,
        step_bias_grad[0],
        decay_log_grad,
        skip_gain_grad[0],
        out_weight_grad,
    )


def solution(mesh):
    placed = (
        P("wide", "narrow"),
        P(),
        P(None, None, "narrow"),
        P(None, "narrow"),
        P("narrow"),
        P(None, "narrow"),
        P(None, "narrow"),
        P("narrow"),
        P(None, "narrow"),
        P("narrow"),
        P("narrow", None),
        P("wide"),
        P("wide", "narrow"),
    )
    return jax.shard_map(
        local,
        mesh=mesh,
        in_specs=placed,
        out_specs=(
            P("wide", "narrow"),
            P("wide", "narrow"),
            P(),
            P(None, None, "narrow"),
            P(None, "narrow"),
            P("narrow"),
            P(None, "narrow"),
            P(None, "narrow"),
            P("narrow"),
            P(None, "narrow"),
            P("narrow"),
            P("narrow", None),
        ),
        check_vma=False,
    )
```

```python
import functools

import jax
import jax.numpy as jnp
from jax import lax
from jax.experimental import pallas as pl
from jax.experimental.pallas import tpu as pltpu
from jax.sharding import PartitionSpec as P

epsilon = 1e-05
log2e = 1.4426950408889634
reset_step = 1e30
lanes = 128
halo = 16
body_rows = 32
scan_width = 512
vmem_bytes = 56 * 1024 * 1024
tiny_cost = pl.CostEstimate(flops=1, bytes_accessed=1, transcendentals=0)
f32 = jnp.float32
bf16 = jnp.bfloat16
contract_first = (((0,), (0,)), ((), ()))
contract_last = (((1,), (1,)), ((), ()))


def passed_along(array, axis, by):
    peers = lax.axis_size(axis)
    pairs = [(i, i + by) for i in range(peers) if 0 <= i + by < peers]
    return lax.ppermute(array, axis, pairs)


def swapped(array, axis, bit):
    peers = lax.axis_size(axis)
    return lax.ppermute(array, axis, [(i, i ^ bit) for i in range(peers)])


def wide_bits():
    bit, bits = 1, []
    while bit < lax.axis_size("wide"):
        bits.append(bit)
        bit *= 2
    return bits


def to_next_both(array):
    count, sides = lax.axis_size("wide"), lax.axis_size("narrow")
    pairs = [
        (i * sides + k, (i + 1) * sides + (sides - 1 - k))
        for i in range(count - 1)
        for k in range(sides)
    ]
    return passed_along(array, "wide", 1), lax.ppermute(array, ("wide", "narrow"), pairs)


def is_upper(bit):
    return (lax.axis_index("wide") & bit) != 0


def group_bits(size):
    bits, bit = [], 4
    while bit < lax.axis_size("wide"):
        bits.append(bit)
        bit *= 2
    return [tuple(bits[k : k + size]) for k in range(0, len(bits), size)]


def flips(bits):
    return [sum(b for k, b in enumerate(bits) if n >> k & 1) for n in range(2 ** len(bits))]


def scattered(piece, bits):
    rows = piece.shape[0] // 2 ** len(bits)
    here = sum(is_upper(b).astype(jnp.int32) << k for k, b in enumerate(bits))

    def block(n):
        return lax.dynamic_slice_in_dim(piece, (here ^ n) * rows, rows, 0)

    total = block(0).astype(f32)
    for n, flip in enumerate(flips(bits)):
        if n > 0:
            total = total + swapped(block(n).astype(bf16), "wide", flip).astype(f32)
    return total


def gathered(held, bits):
    blocks = [held] + [swapped(held, "wide", flip) for flip in flips(bits)[1:]]
    for bit in bits:
        upper = is_upper(bit)
        blocks = [
            jnp.concatenate([jnp.where(upper, b, a), jnp.where(upper, a, b)])
            for a, b in zip(blocks[0::2], blocks[1::2])
        ]
    return blocks[0]


def quarter_of_four(array):
    width = array.shape[1] // 4
    here = lax.axis_index("wide") & 3

    def quarter(n):
        return lax.dynamic_slice_in_dim(array, (here ^ n) * width, width, 1)

    return jnp.stack(
        [quarter(0)] + [swapped(quarter(n), "wide", n) for n in (2, 1, 3)]
    )


def silu_slope(values):
    logistic = jax.nn.sigmoid(values)
    return logistic * (1.0 + values * (1.0 - logistic))


def softplus(values):
    return jnp.maximum(values, 0.0) + jnp.log1p(jnp.exp(-jnp.abs(values)))


def column_spec(rows, start=0):
    return pl.BlockSpec((rows, scan_width), lambda j: (0, start + j))


def part_spec(part, rows, start=0):
    return pl.BlockSpec((None, rows, scan_width), lambda j: (part, 0, start + j))


def whole_spec(rows, width):
    return pl.BlockSpec((rows, width), lambda j: (0, 0))


def call(kernel, name, width, in_specs, out_specs, out_shape, scratch, *operands):
    return pl.pallas_call(
        kernel,
        grid=(width // scan_width,),
        in_specs=in_specs,
        out_specs=out_specs,
        out_shape=out_shape,
        scratch_shapes=scratch,
        compiler_params=pltpu.CompilerParams(vmem_limit_bytes=vmem_bytes),
        cost_estimate=tiny_cost,
        name=name,
    )(*operands)


def conv_kernel(
    inner_ref,
    conv_weight_ref,
    conv_bias_ref,
    select_ref,
    mask_ref,
    convolved_ref,
    act_ref,
    selected_ref,
    inner,
):
    rows = act_ref.shape[0]
    taps = conv_weight_ref.shape[0]
    inner[:halo, :] = inner_ref[rows:, :].astype(f32)
    inner[halo:, :] = inner_ref[:rows, :].astype(f32)
    total = conv_bias_ref[...] + conv_weight_ref[taps - 1 :, :] * inner[halo:, :]
    for lag in range(1, taps):
        earlier = inner[pl.ds(halo - lag, rows), :] * mask_ref[:, lag : lag + 1]
        total = total + conv_weight_ref[taps - 1 - lag : taps - lag, :] * earlier
    convolved_ref[...] = total
    act = (total * jax.nn.sigmoid(total)).astype(bf16)
    act_ref[...] = act
    part = lax.dot_general(select_ref[...], act, contract_last, preferred_element_type=f32)

    @pl.when(pl.program_id(0) == 0)
    def _():
        selected_ref[...] = part

    @pl.when(pl.program_id(0) > 0)
    def _():
        selected_ref[...] += part


def convolve(projected, conv_weight, conv_bias, select_weight, masks):
    parts, extended, width = projected.shape
    rows = extended - halo
    taps = conv_weight.shape[0]
    columns = select_weight.shape[0]
    return call(
        conv_kernel,
        "convolve",
        width,
        [
            part_spec(0, extended),
            column_spec(taps),
            column_spec(1),
            column_spec(columns),
            whole_spec(rows, masks.shape[1]),
        ],
        [column_spec(rows), column_spec(rows), whole_spec(columns, rows)],
        [
            jax.ShapeDtypeStruct((rows, width), f32),
            jax.ShapeDtypeStruct((rows, width), bf16),
            jax.ShapeDtypeStruct((columns, rows), f32),
        ],
        [pltpu.VMEM((extended, scan_width), f32)],
        projected,
        conv_weight,
        conv_bias,
        select_weight,
        masks,
    )


def coef_columns(coef, block):
    per_tile = lanes // body_rows
    start = pl.multiple_of((block // per_tile) * lanes, lanes)
    tile = coef[:, pl.ds(start, lanes)]
    back = body_rows * lax.rem(block, per_tile)
    return pltpu.roll(tile, lax.rem(lanes - back, lanes), 1)


def ends_kernel(
    selected_ref,
    other_ref,
    step_weight_ref,
    step_bias_ref,
    act_ref,
    gate_ref,
    gated_grad_ref,
    mask_ref,
    decay_log_ref,
    step_pre_ref,
    step_ref,
    ends_ref,
    coef,
    held_step,
    drive,
    scan_grad,
):
    rows = act_ref.shape[0]
    count = decay_log_ref.shape[0]
    rank = step_weight_ref.shape[0]
    decay2 = -jnp.exp(decay_log_ref[...]) * log2e
    selected = selected_ref[...] + other_ref[...]
    coef[...] = selected[rank:, :]
    step_low = selected[:rank, :].astype(bf16)
    step_pre = step_bias_ref[...] + lax.dot_general(
        step_low, step_weight_ref[...], contract_first, preferred_element_type=f32
    )
    step_pre_ref[...] = step_pre
    step = softplus(step_pre)
    step_ref[...] = step
    held_step[...] = jnp.where(mask_ref[:, 1:2] > 0.0, step, reset_step)
    drive[...] = step * act_ref[...].astype(f32)
    gate = gate_ref[...].astype(f32)
    scan_grad[...] = gated_grad_ref[...] * (gate * jax.nn.sigmoid(gate))
    zero = jnp.zeros(decay2.shape, f32)

    def body(block, carried):
        state, product, adjoint = carried
        columns = coef_columns(coef, block)
        for i in range(body_rows):
            row = pl.ds(block * body_rows + i, 1)
            factor = jnp.exp2(held_step[row, :] * decay2)
            state = factor * state + columns[:count, i : i + 1] * drive[row, :]
            product = factor * product
            adjoint = adjoint + product * (columns[count:, i : i + 1] * scan_grad[row, :])
        return state, product, adjoint

    state, product, adjoint = lax.fori_loop(0, rows // body_rows, body, (zero, zero + 1.0, zero))
    ends_ref[:count, :] = state
    ends_ref[count : 2 * count, :] = adjoint
    total = jnp.sum(held_step[...], axis=0, keepdims=True)
    ends_ref[2 * count :, :] = jnp.broadcast_to(total, (8, total.shape[1]))


def scan_ends(
    selected, other, step_weight, step_bias, act, projected, gated_grad, masks, decay_log
):
    rows, width = act.shape
    count = decay_log.shape[0]
    columns = selected.shape[0]
    rank = step_weight.shape[0]
    return call(
        ends_kernel,
        "scan_ends",
        width,
        [
            whole_spec(columns, rows),
            whole_spec(columns, rows),
            column_spec(rank),
            column_spec(1),
            column_spec(rows),
            part_spec(1, rows),
            column_spec(rows),
            whole_spec(rows, masks.shape[1]),
            column_spec(count),
        ],
        [column_spec(rows), column_spec(rows), column_spec(2 * count + 8)],
        [
            jax.ShapeDtypeStruct((rows, width), f32),
            jax.ShapeDtypeStruct((rows, width), f32),
            jax.ShapeDtypeStruct((2 * count + 8, width), f32),
        ],
        [pltpu.VMEM((2 * count, rows), f32)] + [pltpu.VMEM((rows, scan_width), f32)] * 3,
        selected,
        other,
        step_weight,
        step_bias,
        act,
        projected,
        gated_grad,
        masks,
        decay_log,
    )


def lane_tiles(values):
    return [values[:, k : k + lanes] for k in range(0, values.shape[1], lanes)]


def tree_sum(parts):
    while len(parts) > 1:
        odd = parts[len(parts) // 2 * 2 :]
        parts = [a + b for a, b in zip(parts[0::2], parts[1::2])] + odd
    return parts[0]


def keep_halves(scratch, i, values):
    for k, tile in enumerate(lane_tiles(values)):
        at = (k * body_rows + i) * 8
        scratch[at : at + 8, :] = tile[:8] + tile[8:]


def put_state_sums(scratch, out_ref, block):
    for group in range(body_rows // 8):
        row = pl.ds(pl.multiple_of(block * body_rows + group * 8, 8), 8)
        for k in range(out_ref.shape[1] // lanes):
            at = (k * body_rows + group * 8) * 8
            total = tree_sum([scratch[pl.ds(at + n, 8, stride=8), :] for n in range(8)])
            out_ref[row, k * lanes : (k + 1) * lanes] = total


def lane_sums(values):
    ones = jnp.ones((8, lanes), bf16)
    high = values.astype(bf16)
    low = (values - high.astype(f32)).astype(bf16)
    total = lax.dot_general(ones, high, contract_last, preferred_element_type=f32)
    total += lax.dot_general(ones, low, contract_last, preferred_element_type=f32)
    return total[:1, :]


def at_token(t, count):
    return pl.ds(pl.multiple_of(t * count, count), count)


def forward_kernel(
    selected_ref,
    other_ref,
    step_ref,
    act_ref,
    gate_ref,
    gated_grad_ref,
    mask_ref,
    decay_log_ref,
    passed_ref,
    entering_ref,
    skip_ref,
    pair_ref,
    entry_ref,
    coef,
    held_step,
    drive,
    scanned,
    halves,
):
    rows = step_ref.shape[0]
    count = decay_log_ref.shape[0]
    rank = selected_ref.shape[0] - 2 * count
    decay = -jnp.exp(decay_log_ref[...])
    decay2 = decay * log2e
    before_steps = passed_ref[2 * count : 2 * count + 1, :]
    entry = passed_ref[:count, :] + through(decay, before_steps) * entering_ref[...]
    entry_ref[...] = entry
    coef[...] = selected_ref[rank:, :] + other_ref[rank:, :]
    act = act_ref[...].astype(f32)
    held_step[...] = jnp.where(mask_ref[:, 1:2] > 0.0, step_ref[...], reset_step)
    drive[...] = step_ref[...] * act

    def forward(block, state):
        columns = coef_columns(coef, block)
        for i in range(body_rows):
            row = pl.ds(block * body_rows + i, 1)
            factor = jnp.exp2(held_step[row, :] * decay2)
            state = factor * state + columns[:count, i : i + 1] * drive[row, :]
            keep_halves(halves, i, columns[count:, i : i + 1] * state)
        put_state_sums(halves, scanned, block)
        return state

    lax.fori_loop(0, rows // body_rows, forward, entry)
    gate = gate_ref[...].astype(f32)
    logistic = jax.nn.sigmoid(gate)
    total = scanned[...] + skip_ref[...] * act
    pair_ref[0] = (total * (gate * logistic)).astype(bf16)
    slope = logistic * (1.0 + gate * (1.0 - logistic))
    pair_ref[1] = (gated_grad_ref[...] * total * slope).astype(bf16)


def scan_forward(
    selected, other, step, act, projected, gated_grad, masks, decay_log, passed, entering, skip_gain
):
    rows, width = step.shape
    count = decay_log.shape[0]
    columns = selected.shape[0]
    return call(
        forward_kernel,
        "scan_forward",
        width,
        [
            whole_spec(columns, rows),
            whole_spec(columns, rows),
            column_spec(rows),
            column_spec(rows),
            part_spec(1, rows),
            column_spec(rows),
            whole_spec(rows, masks.shape[1]),
            column_spec(count),
            column_spec(2 * count + 8),
            column_spec(count),
            column_spec(1),
        ],
        [pl.BlockSpec((2, rows, scan_width), lambda j: (0, 0, j)), column_spec(count)],
        [
            jax.ShapeDtypeStruct((2, rows, width), bf16),
            jax.ShapeDtypeStruct((count, width), f32),
        ],
        [pltpu.VMEM((2 * count, rows), f32)]
        + [pltpu.VMEM((rows, scan_width), f32)] * 3
        + [pltpu.VMEM((8 * body_rows * (scan_width // lanes), lanes), f32)],
        selected,
        other,
        step,
        act,
        projected,
        gated_grad,
        masks,
        decay_log,
        passed,
        entering,
        skip_gain,
    )


def backward_kernel(
    selected_ref,
    other_ref,
    step_pre_ref,
    step_ref,
    act_ref,
    gate_ref,
    gated_grad_ref,
    mask_ref,
    decay_log_ref,
    entry_ref,
    passed_ref,
    returning_ref,
    skip_ref,
    step_weight_ref,
    act_grad_ref,
    select_grad_ref,
    small_ref,
    coef,
    held_step,
    drive,
    scan_grad,
    weighted,
    held_sum,
    states,
    factors,
    halves,
    more_halves,
    in_sum,
    read_sum,
):
    rows = step_ref.shape[0]
    count = decay_log_ref.shape[0]
    rank = step_weight_ref.shape[0]
    blocks = rows // body_rows
    decay = -jnp.exp(decay_log_ref[...])
    decay2 = decay * log2e
    after_steps = passed_ref[2 * count + 1 : 2 * count + 2, :]
    tail = passed_ref[count : 2 * count, :] + through(decay, after_steps) * returning_ref[...]
    selected = selected_ref[...] + other_ref[...]
    coef[...] = selected[rank:, :]
    step_low = selected[:rank, :].astype(bf16)
    step = step_ref[...]
    act = act_ref[...].astype(f32)
    held_step[...] = jnp.where(mask_ref[:, 1:2] > 0.0, step, reset_step)
    drive[...] = step * act
    gate = gate_ref[...].astype(f32)
    grads = gated_grad_ref[...] * (gate * jax.nn.sigmoid(gate))
    scan_grad[...] = grads
    small_ref[rank + count : rank + count + 1, :] = jnp.sum(grads * act, axis=0, keepdims=True)
    states[:count, :] = entry_ref[...]

    @pl.when(pl.program_id(0) == 0)
    def _():
        in_sum[...] = jnp.zeros(in_sum.shape, f32)
        read_sum[...] = jnp.zeros(read_sum.shape, f32)
        select_grad_ref[...] = jnp.zeros(select_grad_ref.shape, f32)

    def forward(block, state):
        columns = coef_columns(coef, block)
        for i in range(body_rows):
            t = block * body_rows + i
            row = pl.ds(t, 1)
            factor = jnp.exp2(held_step[row, :] * decay2)
            state = factor * state + columns[:count, i : i + 1] * drive[row, :]
            factors[at_token(t, count), :] = factor
            states[at_token(t + 1, count), :] = state
        return state

    lax.fori_loop(0, blocks, forward, entry_ref[...])

    def backward(k, carried):
        adjoint, decay_grad = carried
        block = blocks - 1 - k
        columns = coef_columns(coef, block)
        for i in range(body_rows - 1, -1, -1):
            t = block * body_rows + i
            row = pl.ds(t, 1)
            here = at_token(t, count)
            grad = scan_grad[row, :]
            summed = columns[count:, i : i + 1] * grad + adjoint
            read_sum[here, :] += tree_sum(lane_tiles(grad * states[at_token(t + 1, count), :]))
            in_sum[here, :] += tree_sum(lane_tiles(summed * drive[row, :]))
            keep_halves(halves, i, summed * columns[:count, i : i + 1])
            adjoint = factors[here, :] * summed
            held = adjoint * states[here, :]
            decay_grad = decay_grad + held * step_ref[row, :]
            keep_halves(more_halves, i, held * decay)
        put_state_sums(halves, weighted, block)
        put_state_sums(more_halves, held_sum, block)
        return adjoint, decay_grad

    ignored, decay_grad = lax.fori_loop(
        0, blocks, backward, (tail, jnp.zeros(decay.shape, f32))
    )
    act_grad_ref[...] = step * weighted[...] + skip_ref[...] * scan_grad[...]
    step_grad = act * weighted[...] + held_sum[...]
    pre_grad = (step_grad * jax.nn.sigmoid(step_pre_ref[...])).astype(bf16)
    small_ref[:rank, :] = jnp.dot(step_low, pre_grad, preferred_element_type=f32)
    small_ref[rank : rank + count, :] = decay_grad * decay
    bias_grad = jnp.sum(pre_grad.astype(f32), axis=0, keepdims=True)
    small_ref[rank + count + 1 : rank + count + 2, :] = bias_grad
    spare = small_ref.shape[0] - (rank + count + 2)
    small_ref[rank + count + 2 :, :] = jnp.zeros((spare, small_ref.shape[1]), f32)
    select_grad_ref[:rank, :] += lax.dot_general(
        step_weight_ref[...], pre_grad, contract_last, preferred_element_type=f32
    )

    @pl.when(pl.program_id(0) == pl.num_programs(0) - 1)
    def _():
        for n in range(count):
            at = pl.ds(n, rows, stride=count)
            select_grad_ref[rank + n : rank + n + 1, :] = lane_sums(in_sum[at, :])
            select_grad_ref[rank + count + n : rank + count + n + 1, :] = lane_sums(read_sum[at, :])


def scan_backward(
    selected,
    other,
    step_pre,
    step,
    act,
    projected,
    gated_grad,
    masks,
    decay_log,
    entry,
    passed,
    returning,
    skip_gain,
    step_weight,
):
    rows, width = step.shape
    count = decay_log.shape[0]
    columns = selected.shape[0]
    rank = step_weight.shape[0]
    half_rows = 8 * body_rows * (scan_width // lanes)
    small = rank + count + 16
    return call(
        backward_kernel,
        "scan_backward",
        width,
        [
            whole_spec(columns, rows),
            whole_spec(columns, rows),
            column_spec(rows),
            column_spec(rows),
            column_spec(rows),
            part_spec(1, rows),
            column_spec(rows),
            whole_spec(rows, masks.shape[1]),
            column_spec(count),
            column_spec(count),
            column_spec(2 * count + 8),
            column_spec(count),
            column_spec(1),
            column_spec(rank),
        ],
        [column_spec(rows), whole_spec(columns, rows), column_spec(small)],
        [
            jax.ShapeDtypeStruct((rows, width), f32),
            jax.ShapeDtypeStruct((columns, rows), f32),
            jax.ShapeDtypeStruct((small, width), f32),
        ],
        [pltpu.VMEM((2 * count, rows), f32)]
        + [pltpu.VMEM((rows, scan_width), f32)] * 5
        + [
            pltpu.VMEM(((rows + 1) * count, scan_width), f32),
            pltpu.VMEM((rows * count, scan_width), f32),
            pltpu.VMEM((half_rows, lanes), f32),
            pltpu.VMEM((half_rows, lanes), f32),
            pltpu.VMEM((rows * count, lanes), f32),
            pltpu.VMEM((rows * count, lanes), f32),
        ],
        selected,
        other,
        step_pre,
        step,
        act,
        projected,
        gated_grad,
        masks,
        decay_log,
        entry,
        passed,
        returning,
        skip_gain,
        step_weight,
    )


def conv_grad_kernel(
    select_grad_ref,
    other_ref,
    select_ref,
    act_grad_ref,
    convolved_ref,
    act_ref,
    inner_ref,
    conv_weight_ref,
    mask_ref,
    *rest,
):
    inner_grad_ref, edge_ref, small_ref, inner, shifted = rest[-5:]
    rows = act_ref.shape[0]
    taps = conv_weight_ref.shape[0]
    columns = select_ref.shape[0]
    select_grad = (select_grad_ref[...] + other_ref[...]).astype(bf16)
    total = act_grad_ref[...] + lax.dot_general(
        select_grad, select_ref[...], contract_first, preferred_element_type=f32
    )
    conv_grad = total * silu_slope(convolved_ref[...])
    small_ref[:columns, :] = jnp.dot(select_grad, act_ref[...], preferred_element_type=f32)
    inner[:halo, :] = inner_ref[rows:, :].astype(f32)
    inner[halo:, :] = inner_ref[:rows, :].astype(f32)
    edges = jnp.zeros((8, conv_grad.shape[1]), f32)
    shifted[:8, :] = edges
    shifted[rows + 8 :, :] = edges
    out = conv_weight_ref[taps - 1 :, :] * conv_grad
    before = edges
    small_ref[columns + taps - 1 : columns + taps, :] = jnp.sum(
        conv_grad * inner[halo:, :], axis=0, keepdims=True
    )
    for lag in range(1, taps):
        masked = conv_grad * mask_ref[:, lag : lag + 1]
        at = taps - 1 - lag
        small_ref[columns + at : columns + at + 1, :] = jnp.sum(
            masked * inner[pl.ds(halo - lag, rows), :], axis=0, keepdims=True
        )
        shifted[8 : rows + 8, :] = masked
        weight = conv_weight_ref[at : at + 1, :]
        out = out + weight * shifted[pl.ds(8 + lag, rows), :]
        before = before + weight * shifted[pl.ds(lag, 8), :]
    small_ref[columns + taps : columns + taps + 1, :] = jnp.sum(conv_grad, axis=0, keepdims=True)
    spare = small_ref.shape[0] - (columns + taps + 1)
    small_ref[columns + taps + 1 :, :] = jnp.zeros((spare, small_ref.shape[1]), f32)
    inner_grad_ref[...] = out.astype(bf16)
    edge_ref[:8, :] = before
    edge_ref[8:, :] = out[rows - 8 :, :]


def convolve_grad(
    select_grad, other, select_weight, act_grad, convolved, act, projected, conv_weight, masks, waits
):
    rows, width = act.shape
    extended = rows + halo
    columns = select_weight.shape[0]
    taps = conv_weight.shape[0]
    small = columns + 16
    return call(
        conv_grad_kernel,
        "convolve_grad",
        width,
        [
            whole_spec(columns, rows),
            whole_spec(columns, rows),
            column_spec(columns),
            column_spec(rows),
            column_spec(rows),
            column_spec(rows),
            part_spec(0, extended),
            column_spec(taps),
            whole_spec(rows, masks.shape[1]),
        ]
        + [pl.BlockSpec(memory_space=pl.ANY)] * len(waits),
        [column_spec(rows), column_spec(16), column_spec(small)],
        [
            jax.ShapeDtypeStruct((rows, width), bf16),
            jax.ShapeDtypeStruct((16, width), f32),
            jax.ShapeDtypeStruct((small, width), f32),
        ],
        [pltpu.VMEM((extended, scan_width), f32), pltpu.VMEM((rows + 16, scan_width), f32)],
        select_grad,
        other,
        select_weight,
        act_grad,
        convolved,
        act,
        projected,
        conv_weight,
        masks,
        *waits,
    )


def normalize_kernel(
    own_ref,
    other_ref,
    edge_ref,
    other_edge_ref,
    gain_ref,
    ids_ref,
    whole_ref,
    normed_ref,
    inverse_ref,
    mask_ref,
):
    rows, half = own_ref.shape
    ids = ids_ref[...].astype(f32)
    place = lax.broadcasted_iota(jnp.int32, ids.shape, 1)
    same = []
    for lag in range(8):
        earlier = jnp.where(place < lag, ids[:, :1], pltpu.roll(ids, lag, 1)) if lag else ids
        same.append(jnp.where(earlier == ids, 1.0, 0.0))
    spare = jnp.zeros((lanes - 8, rows), f32)
    mask_ref[...] = jnp.concatenate(same + [spare]).T
    right = lax.axis_index("narrow") == 1
    for at, own, other in ((0, own_ref, other_ref), (rows, edge_ref, other_edge_ref)):
        end = at + own.shape[0]
        whole_ref[at:end, :half] = jnp.where(right, other[...], own[...])
        whole_ref[at:end, half:] = jnp.where(right, own[...], other[...])
    whole = whole_ref[...].astype(f32)
    inverse = lax.rsqrt(jnp.mean(whole * whole, axis=1, keepdims=True) + epsilon)
    normed_ref[...] = (whole * inverse * gain_ref[...]).astype(bf16)
    inverse_ref[...] = inverse[:rows]


def normalized(own, other, edge, other_edge, gain, ids):
    rows, half = own.shape
    extended = rows + edge.shape[0]
    return pl.pallas_call(
        normalize_kernel,
        out_shape=[
            jax.ShapeDtypeStruct((extended, 2 * half), bf16),
            jax.ShapeDtypeStruct((extended, 2 * half), bf16),
            jax.ShapeDtypeStruct((rows, 1), f32),
            jax.ShapeDtypeStruct((rows, lanes), f32),
        ],
        cost_estimate=tiny_cost,
        name="normalized",
    )(own, other, edge, other_edge, gain, ids)


def after(array, *waits):
    anywhere = pl.BlockSpec(memory_space=pl.ANY)
    return pl.pallas_call(
        lambda *refs: None,
        in_specs=[anywhere] * (1 + len(waits)),
        out_specs=anywhere,
        out_shape=jax.ShapeDtypeStruct(array.shape, array.dtype),
        input_output_aliases={0: 0},
        cost_estimate=tiny_cost,
        name="after",
    )(array, *waits)


def edge_kernel(ids_ref, tokens_ref, out_ref):
    rows = ids_ref.shape[0]
    taps = 4
    out_ref[...] = tokens_ref[...]
    place = lax.broadcasted_iota(jnp.int32, (halo, 1), 0)
    same = jnp.zeros((halo, 1), f32)
    for lag in range(taps):
        here = jnp.where(ids_ref[rows - 1 - lag] == ids_ref[rows - 1], 1.0, 0.0)
        same = same + jnp.where(place == halo - 1 - lag, here, 0.0)
    out_ref[...] = (tokens_ref[...].astype(f32) * same).astype(bf16)


def edge_rows_of(ids, tokens):
    rows, width = tokens.shape
    return pl.pallas_call(
        edge_kernel,
        grid=(1,),
        in_specs=[
            pl.BlockSpec(memory_space=pltpu.SMEM),
            pl.BlockSpec((halo, width), lambda j: (rows // halo - 1, 0)),
        ],
        out_specs=pl.BlockSpec((halo, width), lambda j: (0, 0)),
        out_shape=jax.ShapeDtypeStruct((halo, width), bf16),
        cost_estimate=tiny_cost,
        name="edge_rows",
    )(ids, tokens)


def small_kernel(place_ref, scan_ref, conv_ref, gain_ref, other_gain_ref, keep_ref, *rest):
    sends_refs, rows = rest[:3], rest[3]
    at = 0
    for ref in (scan_ref, conv_ref):
        rows[at : at + ref.shape[0], :] = ref[...]
        at += ref.shape[0]
    rows[at:, :] = jnp.broadcast_to(
        gain_ref[...] + other_gain_ref[...], (rows.shape[0] - at, rows.shape[1])
    )
    quarter = keep_ref.shape[0]
    for n in range(4):
        start = pl.multiple_of((place_ref[0] ^ n) * quarter, quarter)
        block = rows[pl.ds(start, quarter), :]
        if n == 0:
            keep_ref[...] = block
        else:
            sends_refs[n - 1][...] = block.astype(bf16)


def small_quarters(place, scan_small, conv_small, gain, other_gain):
    width = scan_small.shape[1]
    rows = -(-(scan_small.shape[0] + conv_small.shape[0] + 1) // 256) * 256
    return pl.pallas_call(
        small_kernel,
        in_specs=[pl.BlockSpec(memory_space=pltpu.SMEM)]
        + [pl.BlockSpec(memory_space=pltpu.VMEM)] * 4,
        out_shape=[jax.ShapeDtypeStruct((rows // 4, width), f32)]
        + [jax.ShapeDtypeStruct((rows // 4, width), bf16)] * 3,
        scratch_shapes=[pltpu.VMEM((rows, width), f32)],
        cost_estimate=tiny_cost,
        name="small_quarters",
    )(place, scan_small, conv_small, gain, other_gain)


def quarter_kernel(
    place_ref,
    own_ref,
    near_ref,
    far_ref,
    last_ref,
    normed_ref,
    small_ref,
    first_ref,
    second_ref,
    third_ref,
    *rest,
):
    keep_ref, *sends_refs, piece, small = rest[-6:]
    total = None
    for n, grads in enumerate((own_ref, near_ref, far_ref, last_ref)):
        part = lax.dot_general(normed_ref[n], grads[...], contract_first, preferred_element_type=f32)
        total = part if total is None else total + part
    piece[...] = total
    small[...] = small_ref[...] + sum(
        ref[...].astype(f32) for ref in (first_ref, second_ref, third_ref)
    )
    rows, spare = piece.shape[0] // 4, small.shape[0] // 4
    for n in range(4):
        block = place_ref[0] ^ n
        inner_rows = piece[pl.ds(pl.multiple_of(block * rows, rows), rows), :]
        small_rows = small[pl.ds(pl.multiple_of(block * spare, spare), spare), :]
        if n == 0:
            keep_ref[:rows, :] = inner_rows
            keep_ref[rows:, :] = small_rows
        else:
            sends_refs[n - 1][:rows, :] = inner_rows.astype(bf16)
            sends_refs[n - 1][rows:, :] = small_rows.astype(bf16)


def inner_quarter(place, own, near, far, last, normed, smalls, waits):
    width = own.shape[1]
    quarter = normed.shape[2]
    spare = smalls[0].shape[0]
    rows = (quarter + spare) // 4
    return pl.pallas_call(
        quarter_kernel,
        in_specs=[pl.BlockSpec(memory_space=pltpu.SMEM)]
        + [pl.BlockSpec(memory_space=pltpu.VMEM)] * 9
        + [pl.BlockSpec(memory_space=pl.ANY)] * len(waits),
        out_shape=[jax.ShapeDtypeStruct((rows, width), f32)]
        + [jax.ShapeDtypeStruct((rows, width), bf16)] * 3,
        scratch_shapes=[pltpu.VMEM((quarter, width), f32), pltpu.VMEM((spare, width), f32)],
        compiler_params=pltpu.CompilerParams(vmem_limit_bytes=vmem_bytes),
        cost_estimate=tiny_cost,
        name="inner_quarter",
    )(place, own, near, far, last, normed, *smalls, *waits)


def join_kernel(place_ref, gate_ref, inner_ref, *rest):
    out_ref, small_ref = rest[-2:]
    rows, spare = out_ref.shape[0] // 2, small_ref.shape[0] // 2
    out_ref[:, 1, :] = gate_ref[...].astype(f32)
    for n in range(2):
        at = n * (rows + spare)
        block = inner_ref[at : at + rows + spare, :].astype(f32)
        out_ref[n * rows : (n + 1) * rows, 0, :] = block[:rows]
        small_ref[n * spare : (n + 1) * spare, :] = block[rows:]


def joined(place, flip, gate, inner, before, waits):
    depth, width = gate.shape
    quarter = depth // 4
    small = inner.shape[0] - quarter
    untouched = [*before, *waits]
    return pl.pallas_call(
        join_kernel,
        grid_spec=pltpu.PrefetchScalarGridSpec(
            num_scalar_prefetch=1,
            grid=(2,),
            in_specs=[
                pl.BlockSpec((quarter // 2, width), lambda j, place: (2 * (place[0] ^ flip) + j, 0)),
                pl.BlockSpec((inner.shape[0] // 2, width), lambda j, place: (j, 0)),
            ]
            + [pl.BlockSpec(memory_space=pl.ANY)] * len(untouched),
            out_specs=[
                pl.BlockSpec(
                    (quarter // 2, 2, width), lambda j, place: (2 * (place[0] ^ flip) + j, 0, 0)
                ),
                pl.BlockSpec((small // 2, width), lambda j, place: (2 * (place[0] ^ flip) + j, 0)),
            ],
        ),
        out_shape=[
            jax.ShapeDtypeStruct((depth, 2, width), f32),
            jax.ShapeDtypeStruct((4 * small, width), f32),
        ],
        input_output_aliases={3 + k: k for k in range(len(before))},
        compiler_params=pltpu.CompilerParams(vmem_limit_bytes=vmem_bytes),
        cost_estimate=tiny_cost,
        name="joined",
    )(place, gate, inner, *untouched)


def parts_kernel(small_ref, *out_refs, starts):
    for ref, start in zip(out_refs, starts):
        ref[...] = small_ref[start : start + ref.shape[0], :]


def small_parts(small, sizes):
    width = small.shape[1]
    return pl.pallas_call(
        functools.partial(parts_kernel, starts=[start for start, _ in sizes]),
        out_shape=[jax.ShapeDtypeStruct((rows, width), f32) for _, rows in sizes],
        cost_estimate=tiny_cost,
        name="small_parts",
    )(small)


def through(decay, total):
    return jnp.exp(decay * total)


def round_kernel(second_ref, decay_log_ref, own_ref, other_ref, passed_ref, new_passed_ref, *ends_refs):
    count = decay_log_ref.shape[0]
    decay = -jnp.exp(decay_log_ref[...])
    second = second_ref[0] > 0

    def split(ref):
        return ref[:count], ref[count : 2 * count], ref[2 * count : 2 * count + 1]

    own, other = split(own_ref), split(other_ref)
    early = [jnp.where(second, b, a) for a, b in zip(own, other)]
    late = [jnp.where(second, a, b) for a, b in zip(own, other)]
    state = late[0] + through(decay, late[2]) * early[0]
    adjoint = early[1] + through(decay, early[2]) * late[1]
    if len(ends_refs) == 2:
        ends_refs[0][...] = state
        ends_refs[1][...] = adjoint
    else:
        ends_refs[0][:count, :] = state
        ends_refs[0][count : 2 * count, :] = adjoint
        ends_refs[0][2 * count :, :] = jnp.broadcast_to(early[2] + late[2], (8, decay.shape[1]))
    before, after = passed_ref[:count], passed_ref[count : 2 * count]
    before_steps = passed_ref[2 * count : 2 * count + 1]
    after_steps = passed_ref[2 * count + 1 : 2 * count + 2]
    new_passed_ref[:count, :] = before + jnp.where(second, through(decay, before_steps) * other[0], 0.0)
    new_passed_ref[count : 2 * count, :] = after + jnp.where(
        second, 0.0, through(decay, after_steps) * other[1]
    )
    new_passed_ref[2 * count : 2 * count + 1, :] = before_steps + jnp.where(second, other[2], 0.0)
    new_passed_ref[2 * count + 1 : 2 * count + 2, :] = after_steps + jnp.where(second, 0.0, other[2])


def carried(ends, decay_log):
    count, width = decay_log.shape
    place = lax.axis_index("wide").astype(jnp.int32)
    passed = jnp.zeros((2 * count + 8, width), f32)
    packed = ends
    vmem = pl.BlockSpec(memory_space=pltpu.VMEM)
    for k, kinds in enumerate(([ends], [decay_log, decay_log])):
        passed, *out = pl.pallas_call(
            round_kernel,
            in_specs=[pl.BlockSpec(memory_space=pltpu.SMEM)] + [vmem] * 4,
            out_shape=[jax.ShapeDtypeStruct(kind.shape, f32) for kind in [passed] + kinds],
            cost_estimate=tiny_cost,
            name="carry_round",
        )((place >> k & 1)[None], decay_log, packed, swapped(packed, "wide", 2**k), passed)
        packed = out[0]
    from_before = passed_along(out[0], "wide", 4)
    from_after = passed_along(out[1], "wide", -4)
    return passed, from_before, from_after


def local(
    tokens,
    norm_gain,
    in_weight,
    conv_weight,
    conv_bias,
    select_weight,
    step_weight,
    step_bias,
    decay_log,
    skip_gain,
    out_weight,
    segment_ids,
    cotangent,
):
    rows, features = tokens.shape
    taps = conv_weight.shape[0]
    columns = select_weight.shape[0]
    rank = step_weight.shape[0]
    count = decay_log.shape[0]
    right_half = lax.axis_index("narrow") == 1

    def both_halves(own, other):
        return jnp.concatenate(
            [jnp.where(right_half, other, own), jnp.where(right_half, own, other)], axis=1
        )

    other_tokens = swapped(tokens, "narrow", 1)
    other_cot = swapped(cotangent, "narrow", 1)
    edge, other_edge = to_next_both(edge_rows_of(segment_ids, tokens))

    same_as_last = (segment_ids[rows - 8 :] == segment_ids[rows - 1 :])[:, None]
    whole_ext, normed_ext, inverse, masks = normalized(
        tokens, other_tokens, edge, other_edge, norm_gain[None], segment_ids[None]
    )
    projected = jnp.einsum(
        "td,dce->cte", normed_ext, in_weight, preferred_element_type=f32
    ).astype(bf16)
    convolved, act, selected = convolve(
        projected, conv_weight, conv_bias[None], select_weight, masks
    )
    other_selected = swapped(selected, "narrow", 1)
    cot_whole = both_halves(cotangent, other_cot)
    gated_grad = lax.dot_general(
        cot_whole, out_weight, contract_last, preferred_element_type=f32
    )
    step_pre, step, ends = scan_ends(
        selected,
        other_selected,
        step_weight,
        step_bias[None],
        act,
        projected,
        gated_grad,
        masks,
        decay_log,
    )
    passed, entering, returning = carried(ends, decay_log)
    pair, entry = scan_forward(
        selected,
        other_selected,
        step,
        act,
        projected,
        gated_grad,
        masks,
        decay_log,
        passed,
        entering,
        skip_gain[None],
    )
    gated, gate_grad = pair[0], pair[1]
    normed = normed_ext[:rows]
    products = (
        lax.dot_general(gated, cot_whole, contract_first, preferred_element_type=f32).astype(bf16),
        lax.dot_general(normed, gate_grad, contract_first, preferred_element_type=f32).astype(bf16),
    )
    out_sum, gate_sum = lax.psum(products, "wide")
    whole = whole_ext[:rows].astype(f32)
    wide_place = lax.axis_index("wide").astype(jnp.int32)
    four_place = (wide_place & 3)[None]

    def narrow_halves(array):
        low, high = array[:, :features], array[:, features:]
        return jnp.where(right_half, high, low), jnp.where(right_half, low, high)

    def after_forward(products):
        normed_four = quarter_of_four(normed)
        out_part = jnp.dot(gated, out_weight, preferred_element_type=f32)
        out_mine, out_other = narrow_halves(out_part)
        out_theirs = swapped(out_other, "narrow", 1)
        act_grad, select_grad, scan_small = scan_backward(
            selected,
            other_selected,
            step_pre,
            step,
            act,
            projected,
            gated_grad,
            masks,
            decay_log,
            entry,
            passed,
            returning,
            skip_gain[None],
            step_weight,
        )
        layer_out = (tokens.astype(f32) + (out_mine + out_theirs)).astype(bf16)
        inner_main, edges, conv_small = convolve_grad(
            select_grad,
            swapped(select_grad, "narrow", 1),
            select_weight,
            act_grad,
            convolved,
            act,
            projected,
            conv_weight,
            masks,
            [out_theirs, normed_four],
        )
        from_next = passed_along(edges[:8], "wide", -1)
        last_rows = edges[8:] + jnp.where(same_as_last, from_next, 0.0)
        inner_grad = jnp.concatenate([inner_main[: rows - 8], last_rows.astype(bf16)])
        near = swapped(inner_grad, "wide", 2)
        far = swapped(inner_grad, "wide", 1)
        normed_part = jnp.einsum(
            "cte,dce->td", jnp.stack([inner_grad, gate_grad]), in_weight, preferred_element_type=f32
        )
        gain_part = jnp.sum(normed_part * whole * inverse, axis=0, keepdims=True)
        row_part = jnp.sum(normed_part * norm_gain * whole, axis=1)[None]
        keep, *sends = small_quarters(
            four_place, scan_small, conv_small, gain_part, swapped(gain_part, "narrow", 1)
        )
        smalls = [keep] + [swapped(sends[n - 1], "wide", n) for n in (1, 2, 3)]
        normed_mine, normed_other = narrow_halves(normed_part)
        row_theirs = swapped(row_part, "narrow", 1)
        normed_theirs = swapped(normed_other, "narrow", 1)
        near = after(near, *sends)
        keep, *sends = inner_quarter(
            (wide_place >> 2 & 3)[None],
            inner_grad,
            near,
            far,
            swapped(near, "wide", 1),
            normed_four,
            smalls,
            [row_theirs],
        )
        row_sum = (row_part + row_theirs).reshape(rows, 1)
        gain_mine = jnp.where(right_half, norm_gain[features:], norm_gain[:features])
        whole_grad = inverse * (gain_mine * (normed_mine + normed_theirs)) - tokens.astype(f32) * (
            inverse * inverse * inverse
        ) * (row_sum / (2 * features))
        tokens_grad = (whole_grad + cotangent.astype(f32)).astype(bf16)
        first_bits, *more_bits = group_bits(2)
        held = keep
        for n, flip in enumerate(flips(first_bits)[1:]):
            held = held + swapped(sends[n], "wide", flip).astype(f32)
        for bits in more_bits:
            held = scattered(held, bits)
        held = held.astype(bf16)
        for bits in reversed(group_bits(2)):
            held = gathered(held, bits)
        return held, layer_out, tokens_grad

    kinds = jax.eval_shape(after_forward, products)
    held, layer_out, tokens_grad = lax.cond(
        segment_ids[0] >= 0,
        after_forward,
        lambda pair: jax.tree.map(lambda kind: jnp.zeros(kind.shape, kind.dtype), kinds),
        products,
    )

    out_weight_grad = out_sum.astype(f32)
    def join(flip, quarter, *waits):
        return joined(four_place, flip, gate_sum, quarter, results, waits)

    results = []
    results = join(0, held, out_weight_grad)
    results = join(1, swapped(held, "wide", 1))
    near = after(swapped(held, "wide", 2), results[1])
    far = swapped(near, "wide", 1)
    results = join(2, near)
    results = join(3, far)
    in_weight_grad, small_sum = results
    conv_at = rank + count + 16
    gain_at = conv_at + columns + 16
    (
        step_weight_grad,
        decay_log_grad,
        skip_gain_grad,
        step_bias_grad,
        select_weight_grad,
        conv_weight_grad,
        conv_bias_grad,
        norm_gain_grad,
    ) = small_parts(
        small_sum,
        [
            (0, rank),
            (rank, count),
            (rank + count, 1),
            (rank + count + 1, 1),
            (conv_at, columns),
            (conv_at + columns, taps),
            (conv_at + columns + taps, 1),
            (gain_at, 1),
        ],
    )
    return (
        layer_out,
        tokens_grad,
        norm_gain_grad[0],
        in_weight_grad,
        conv_weight_grad,
        conv_bias_grad[0],
        select_weight_grad,
        step_weight_grad,
        step_bias_grad[0],
        decay_log_grad,
        skip_gain_grad[0],
        out_weight_grad,
    )


def solution(mesh):
    placed = (
        P("wide", "narrow"),
        P(),
        P(None, None, "narrow"),
        P(None, "narrow"),
        P("narrow"),
        P(None, "narrow"),
        P(None, "narrow"),
        P("narrow"),
        P(None, "narrow"),
        P("narrow"),
        P("narrow", None),
        P("wide"),
        P("wide", "narrow"),
    )
    return jax.shard_map(
        local,
        mesh=mesh,
        in_specs=placed,
        out_specs=(
            P("wide", "narrow"),
            P("wide", "narrow"),
            P(),
            P(None, None, "narrow"),
            P(None, "narrow"),
            P("narrow"),
            P(None, "narrow"),
            P(None, "narrow"),
            P("narrow"),
            P(None, "narrow"),
            P("narrow"),
            P("narrow", None),
        ),
        check_vma=False,
    )
```

```python
import functools

import jax
import jax.numpy as jnp
from jax import lax
from jax.experimental import pallas as pl
from jax.experimental.pallas import tpu as pltpu
from jax.sharding import PartitionSpec as P

epsilon = 1e-05
log2e = 1.4426950408889634
reset_step = 1e30
lanes = 128
halo = 16
body_rows = 32
scan_width = 512
vmem_bytes = 56 * 1024 * 1024
tiny_cost = pl.CostEstimate(flops=1, bytes_accessed=1, transcendentals=0)
f32 = jnp.float32
bf16 = jnp.bfloat16
contract_first = (((0,), (0,)), ((), ()))
contract_last = (((1,), (1,)), ((), ()))


def passed_along(array, axis, by):
    peers = lax.axis_size(axis)
    pairs = [(i, i + by) for i in range(peers) if 0 <= i + by < peers]
    return lax.ppermute(array, axis, pairs)


def swapped(array, axis, bit):
    peers = lax.axis_size(axis)
    return lax.ppermute(array, axis, [(i, i ^ bit) for i in range(peers)])


def wide_bits():
    bit, bits = 1, []
    while bit < lax.axis_size("wide"):
        bits.append(bit)
        bit *= 2
    return bits


def to_next_both(array):
    count, sides = lax.axis_size("wide"), lax.axis_size("narrow")
    pairs = [
        (i * sides + k, (i + 1) * sides + (sides - 1 - k))
        for i in range(count - 1)
        for k in range(sides)
    ]
    return passed_along(array, "wide", 1), lax.ppermute(array, ("wide", "narrow"), pairs)


def is_upper(bit):
    return (lax.axis_index("wide") & bit) != 0


def group_bits(size):
    bits, bit = [], 4
    while bit < lax.axis_size("wide"):
        bits.append(bit)
        bit *= 2
    return [tuple(bits[k : k + size]) for k in range(0, len(bits), size)]


def flips(bits):
    return [sum(b for k, b in enumerate(bits) if n >> k & 1) for n in range(2 ** len(bits))]


def scattered(piece, bits):
    rows = piece.shape[0] // 2 ** len(bits)
    here = sum(is_upper(b).astype(jnp.int32) << k for k, b in enumerate(bits))

    def block(n):
        return lax.dynamic_slice_in_dim(piece, (here ^ n) * rows, rows, 0)

    total = block(0).astype(f32)
    for n, flip in enumerate(flips(bits)):
        if n > 0:
            total = total + swapped(block(n).astype(bf16), "wide", flip).astype(f32)
    return total


def gathered(held, bits):
    blocks = [held] + [swapped(held, "wide", flip) for flip in flips(bits)[1:]]
    for bit in bits:
        upper = is_upper(bit)
        blocks = [
            jnp.concatenate([jnp.where(upper, b, a), jnp.where(upper, a, b)])
            for a, b in zip(blocks[0::2], blocks[1::2])
        ]
    return blocks[0]


def quarter_of_four(array):
    width = array.shape[1] // 4
    here = lax.axis_index("wide") & 3

    def quarter(n):
        return lax.dynamic_slice_in_dim(array, (here ^ n) * width, width, 1)

    return [quarter(0)] + [swapped(quarter(n), "wide", n) for n in (2, 1, 3)]


def silu_slope(values):
    logistic = jax.nn.sigmoid(values)
    return logistic * (1.0 + values * (1.0 - logistic))


def softplus(values):
    return jnp.maximum(values, 0.0) + jnp.log1p(jnp.exp(-jnp.abs(values)))


def column_spec(rows, start=0):
    return pl.BlockSpec((rows, scan_width), lambda j: (0, start + j))


def part_spec(part, rows, start=0):
    return pl.BlockSpec((None, rows, scan_width), lambda j: (part, 0, start + j))


def whole_spec(rows, width):
    return pl.BlockSpec((rows, width), lambda j: (0, 0))


def call(kernel, name, width, in_specs, out_specs, out_shape, scratch, *operands):
    return pl.pallas_call(
        kernel,
        grid=(width // scan_width,),
        in_specs=in_specs,
        out_specs=out_specs,
        out_shape=out_shape,
        scratch_shapes=scratch,
        compiler_params=pltpu.CompilerParams(vmem_limit_bytes=vmem_bytes),
        cost_estimate=tiny_cost,
        name=name,
    )(*operands)


def conv_kernel(
    inner_ref,
    conv_weight_ref,
    conv_bias_ref,
    select_ref,
    mask_ref,
    convolved_ref,
    act_ref,
    selected_ref,
    inner,
):
    rows = act_ref.shape[0]
    taps = conv_weight_ref.shape[0]
    inner[:halo, :] = inner_ref[rows:, :].astype(f32)
    inner[halo:, :] = inner_ref[:rows, :].astype(f32)
    total = conv_bias_ref[...] + conv_weight_ref[taps - 1 :, :] * inner[halo:, :]
    for lag in range(1, taps):
        earlier = inner[pl.ds(halo - lag, rows), :] * mask_ref[:, lag : lag + 1]
        total = total + conv_weight_ref[taps - 1 - lag : taps - lag, :] * earlier
    convolved_ref[...] = total
    act = (total * jax.nn.sigmoid(total)).astype(bf16)
    act_ref[...] = act
    part = lax.dot_general(select_ref[...], act, contract_last, preferred_element_type=f32)

    @pl.when(pl.program_id(0) == 0)
    def _():
        selected_ref[...] = part

    @pl.when(pl.program_id(0) > 0)
    def _():
        selected_ref[...] += part


def convolve(projected, conv_weight, conv_bias, select_weight, masks):
    parts, extended, width = projected.shape
    rows = extended - halo
    taps = conv_weight.shape[0]
    columns = select_weight.shape[0]
    return call(
        conv_kernel,
        "convolve",
        width,
        [
            part_spec(0, extended),
            column_spec(taps),
            column_spec(1),
            column_spec(columns),
            whole_spec(rows, masks.shape[1]),
        ],
        [column_spec(rows), column_spec(rows), whole_spec(columns, rows)],
        [
            jax.ShapeDtypeStruct((rows, width), f32),
            jax.ShapeDtypeStruct((rows, width), bf16),
            jax.ShapeDtypeStruct((columns, rows), f32),
        ],
        [pltpu.VMEM((extended, scan_width), f32)],
        projected,
        conv_weight,
        conv_bias,
        select_weight,
        masks,
    )


def coef_columns(coef, block):
    per_tile = lanes // body_rows
    start = pl.multiple_of((block // per_tile) * lanes, lanes)
    tile = coef[:, pl.ds(start, lanes)]
    back = body_rows * lax.rem(block, per_tile)
    return pltpu.roll(tile, lax.rem(lanes - back, lanes), 1)


def ends_kernel(
    selected_ref,
    other_ref,
    step_weight_ref,
    step_bias_ref,
    act_ref,
    gate_ref,
    gated_grad_ref,
    mask_ref,
    decay_log_ref,
    step_pre_ref,
    step_ref,
    ends_ref,
    coef,
    held_step,
    drive,
    scan_grad,
):
    rows = act_ref.shape[0]
    count = decay_log_ref.shape[0]
    rank = step_weight_ref.shape[0]
    decay2 = -jnp.exp(decay_log_ref[...]) * log2e
    selected = selected_ref[...] + other_ref[...]
    coef[...] = selected[rank:, :]
    step_low = selected[:rank, :].astype(bf16)
    step_pre = step_bias_ref[...] + lax.dot_general(
        step_low, step_weight_ref[...], contract_first, preferred_element_type=f32
    )
    step_pre_ref[...] = step_pre
    step = softplus(step_pre)
    step_ref[...] = step
    held_step[...] = jnp.where(mask_ref[:, 1:2] > 0.0, step, reset_step)
    drive[...] = step * act_ref[...].astype(f32)
    gate = gate_ref[...].astype(f32)
    scan_grad[...] = gated_grad_ref[...] * (gate * jax.nn.sigmoid(gate))
    zero = jnp.zeros(decay2.shape, f32)

    def body(block, carried):
        state, product, adjoint = carried
        columns = coef_columns(coef, block)
        for i in range(body_rows):
            row = pl.ds(block * body_rows + i, 1)
            factor = jnp.exp2(held_step[row, :] * decay2)
            state = factor * state + columns[:count, i : i + 1] * drive[row, :]
            product = factor * product
            adjoint = adjoint + product * (columns[count:, i : i + 1] * scan_grad[row, :])
        return state, product, adjoint

    state, product, adjoint = lax.fori_loop(0, rows // body_rows, body, (zero, zero + 1.0, zero))
    ends_ref[:count, :] = state
    ends_ref[count : 2 * count, :] = adjoint
    total = jnp.sum(held_step[...], axis=0, keepdims=True)
    ends_ref[2 * count :, :] = jnp.broadcast_to(total, (8, total.shape[1]))


def scan_ends(
    selected, other, step_weight, step_bias, act, projected, gated_grad, masks, decay_log
):
    rows, width = act.shape
    count = decay_log.shape[0]
    columns = selected.shape[0]
    rank = step_weight.shape[0]
    return call(
        ends_kernel,
        "scan_ends",
        width,
        [
            whole_spec(columns, rows),
            whole_spec(columns, rows),
            column_spec(rank),
            column_spec(1),
            column_spec(rows),
            part_spec(1, rows),
            column_spec(rows),
            whole_spec(rows, masks.shape[1]),
            column_spec(count),
        ],
        [column_spec(rows), column_spec(rows), column_spec(2 * count + 8)],
        [
            jax.ShapeDtypeStruct((rows, width), f32),
            jax.ShapeDtypeStruct((rows, width), f32),
            jax.ShapeDtypeStruct((2 * count + 8, width), f32),
        ],
        [pltpu.VMEM((2 * count, rows), f32)] + [pltpu.VMEM((rows, scan_width), f32)] * 3,
        selected,
        other,
        step_weight,
        step_bias,
        act,
        projected,
        gated_grad,
        masks,
        decay_log,
    )


def lane_tiles(values):
    return [values[:, k : k + lanes] for k in range(0, values.shape[1], lanes)]


def tree_sum(parts):
    while len(parts) > 1:
        odd = parts[len(parts) // 2 * 2 :]
        parts = [a + b for a, b in zip(parts[0::2], parts[1::2])] + odd
    return parts[0]


def keep_halves(scratch, i, values):
    for k, tile in enumerate(lane_tiles(values)):
        at = (k * body_rows + i) * 8
        scratch[at : at + 8, :] = tile[:8] + tile[8:]


def put_state_sums(scratch, out_ref, block):
    for group in range(body_rows // 8):
        row = pl.ds(pl.multiple_of(block * body_rows + group * 8, 8), 8)
        for k in range(out_ref.shape[1] // lanes):
            at = (k * body_rows + group * 8) * 8
            total = tree_sum([scratch[pl.ds(at + n, 8, stride=8), :] for n in range(8)])
            out_ref[row, k * lanes : (k + 1) * lanes] = total


def lane_sums(values):
    ones = jnp.ones((8, lanes), bf16)
    high = values.astype(bf16)
    low = (values - high.astype(f32)).astype(bf16)
    total = lax.dot_general(ones, high, contract_last, preferred_element_type=f32)
    total += lax.dot_general(ones, low, contract_last, preferred_element_type=f32)
    return total[:1, :]


def at_token(t, count):
    return pl.ds(pl.multiple_of(t * count, count), count)


def forward_kernel(
    selected_ref,
    other_ref,
    step_ref,
    act_ref,
    gate_ref,
    gated_grad_ref,
    mask_ref,
    decay_log_ref,
    passed_ref,
    entering_ref,
    skip_ref,
    wait_ref,
    gated_ref,
    gate_grad_ref,
    entry_ref,
    coef,
    held_step,
    drive,
    scanned,
    halves,
):
    rows = step_ref.shape[0]
    count = decay_log_ref.shape[0]
    rank = selected_ref.shape[0] - 2 * count
    decay = -jnp.exp(decay_log_ref[...])
    decay2 = decay * log2e
    before_steps = passed_ref[2 * count : 2 * count + 1, :]
    entry = passed_ref[:count, :] + through(decay, before_steps) * entering_ref[...]
    entry_ref[...] = entry
    coef[...] = selected_ref[rank:, :] + other_ref[rank:, :]
    act = act_ref[...].astype(f32)
    held_step[...] = jnp.where(mask_ref[:, 1:2] > 0.0, step_ref[...], reset_step)
    drive[...] = step_ref[...] * act

    def forward(block, state):
        columns = coef_columns(coef, block)
        for i in range(body_rows):
            row = pl.ds(block * body_rows + i, 1)
            factor = jnp.exp2(held_step[row, :] * decay2)
            state = factor * state + columns[:count, i : i + 1] * drive[row, :]
            keep_halves(halves, i, columns[count:, i : i + 1] * state)
        put_state_sums(halves, scanned, block)
        return state

    lax.fori_loop(0, rows // body_rows, forward, entry)
    gate = gate_ref[...].astype(f32)
    logistic = jax.nn.sigmoid(gate)
    total = scanned[...] + skip_ref[...] * act
    gated_ref[...] = (total * (gate * logistic)).astype(bf16)
    slope = logistic * (1.0 + gate * (1.0 - logistic))
    gate_grad_ref[...] = (gated_grad_ref[...] * total * slope).astype(bf16)


def scan_forward(
    selected, other, step, act, projected, gated_grad, masks, decay_log, passed, entering, skip_gain, wait
):
    rows, width = step.shape
    count = decay_log.shape[0]
    columns = selected.shape[0]
    return call(
        forward_kernel,
        "scan_forward",
        width,
        [
            whole_spec(columns, rows),
            whole_spec(columns, rows),
            column_spec(rows),
            column_spec(rows),
            part_spec(1, rows),
            column_spec(rows),
            whole_spec(rows, masks.shape[1]),
            column_spec(count),
            column_spec(2 * count + 8),
            column_spec(count),
            column_spec(1),
            pl.BlockSpec(memory_space=pl.ANY),
        ],
        [column_spec(rows), column_spec(rows), column_spec(count)],
        [
            jax.ShapeDtypeStruct((rows, width), bf16),
            jax.ShapeDtypeStruct((rows, width), bf16),
            jax.ShapeDtypeStruct((count, width), f32),
        ],
        [pltpu.VMEM((2 * count, rows), f32)]
        + [pltpu.VMEM((rows, scan_width), f32)] * 3
        + [pltpu.VMEM((8 * body_rows * (scan_width // lanes), lanes), f32)],
        selected,
        other,
        step,
        act,
        projected,
        gated_grad,
        masks,
        decay_log,
        passed,
        entering,
        skip_gain,
        wait,
    )


def backward_kernel(
    selected_ref,
    other_ref,
    step_pre_ref,
    step_ref,
    act_ref,
    gate_ref,
    gated_grad_ref,
    mask_ref,
    decay_log_ref,
    entry_ref,
    passed_ref,
    returning_ref,
    skip_ref,
    step_weight_ref,
    act_grad_ref,
    select_grad_ref,
    small_ref,
    coef,
    held_step,
    drive,
    scan_grad,
    weighted,
    held_sum,
    states,
    factors,
    halves,
    more_halves,
    in_sum,
    read_sum,
):
    rows = step_ref.shape[0]
    count = decay_log_ref.shape[0]
    rank = step_weight_ref.shape[0]
    blocks = rows // body_rows
    decay = -jnp.exp(decay_log_ref[...])
    decay2 = decay * log2e
    after_steps = passed_ref[2 * count + 1 : 2 * count + 2, :]
    tail = passed_ref[count : 2 * count, :] + through(decay, after_steps) * returning_ref[...]
    selected = selected_ref[...] + other_ref[...]
    coef[...] = selected[rank:, :]
    step_low = selected[:rank, :].astype(bf16)
    step = step_ref[...]
    act = act_ref[...].astype(f32)
    held_step[...] = jnp.where(mask_ref[:, 1:2] > 0.0, step, reset_step)
    drive[...] = step * act
    gate = gate_ref[...].astype(f32)
    grads = gated_grad_ref[...] * (gate * jax.nn.sigmoid(gate))
    scan_grad[...] = grads
    small_ref[rank + count : rank + count + 1, :] = jnp.sum(grads * act, axis=0, keepdims=True)
    states[:count, :] = entry_ref[...]

    @pl.when(pl.program_id(0) == 0)
    def _():
        in_sum[...] = jnp.zeros(in_sum.shape, f32)
        read_sum[...] = jnp.zeros(read_sum.shape, f32)
        select_grad_ref[...] = jnp.zeros(select_grad_ref.shape, f32)

    def forward(block, state):
        columns = coef_columns(coef, block)
        for i in range(body_rows):
            t = block * body_rows + i
            row = pl.ds(t, 1)
            factor = jnp.exp2(held_step[row, :] * decay2)
            state = factor * state + columns[:count, i : i + 1] * drive[row, :]
            factors[at_token(t, count), :] = factor
            states[at_token(t + 1, count), :] = state
        return state

    lax.fori_loop(0, blocks, forward, entry_ref[...])

    def backward(k, carried):
        adjoint, decay_grad = carried
        block = blocks - 1 - k
        columns = coef_columns(coef, block)
        for i in range(body_rows - 1, -1, -1):
            t = block * body_rows + i
            row = pl.ds(t, 1)
            here = at_token(t, count)
            grad = scan_grad[row, :]
            summed = columns[count:, i : i + 1] * grad + adjoint
            read_sum[here, :] += tree_sum(lane_tiles(grad * states[at_token(t + 1, count), :]))
            in_sum[here, :] += tree_sum(lane_tiles(summed * drive[row, :]))
            keep_halves(halves, i, summed * columns[:count, i : i + 1])
            adjoint = factors[here, :] * summed
            held = adjoint * states[here, :]
            decay_grad = decay_grad + held * step_ref[row, :]
            keep_halves(more_halves, i, held * decay)
        put_state_sums(halves, weighted, block)
        put_state_sums(more_halves, held_sum, block)
        return adjoint, decay_grad

    ignored, decay_grad = lax.fori_loop(
        0, blocks, backward, (tail, jnp.zeros(decay.shape, f32))
    )
    act_grad_ref[...] = step * weighted[...] + skip_ref[...] * scan_grad[...]
    step_grad = act * weighted[...] + held_sum[...]
    pre_grad = (step_grad * jax.nn.sigmoid(step_pre_ref[...])).astype(bf16)
    small_ref[:rank, :] = jnp.dot(step_low, pre_grad, preferred_element_type=f32)
    small_ref[rank : rank + count, :] = decay_grad * decay
    bias_grad = jnp.sum(pre_grad.astype(f32), axis=0, keepdims=True)
    small_ref[rank + count + 1 : rank + count + 2, :] = bias_grad
    select_grad_ref[:rank, :] += lax.dot_general(
        step_weight_ref[...], pre_grad, contract_last, preferred_element_type=f32
    )

    @pl.when(pl.program_id(0) == pl.num_programs(0) - 1)
    def _():
        for n in range(count):
            at = pl.ds(n, rows, stride=count)
            select_grad_ref[rank + n : rank + n + 1, :] = lane_sums(in_sum[at, :])
            select_grad_ref[rank + count + n : rank + count + n + 1, :] = lane_sums(read_sum[at, :])


def scan_backward(
    selected,
    other,
    step_pre,
    step,
    act,
    projected,
    gated_grad,
    masks,
    decay_log,
    entry,
    passed,
    returning,
    skip_gain,
    step_weight,
):
    rows, width = step.shape
    count = decay_log.shape[0]
    columns = selected.shape[0]
    rank = step_weight.shape[0]
    half_rows = 8 * body_rows * (scan_width // lanes)
    small = rank + count + 2
    return call(
        backward_kernel,
        "scan_backward",
        width,
        [
            whole_spec(columns, rows),
            whole_spec(columns, rows),
            column_spec(rows),
            column_spec(rows),
            column_spec(rows),
            part_spec(1, rows),
            column_spec(rows),
            whole_spec(rows, masks.shape[1]),
            column_spec(count),
            column_spec(count),
            column_spec(2 * count + 8),
            column_spec(count),
            column_spec(1),
            column_spec(rank),
        ],
        [column_spec(rows), whole_spec(columns, rows), column_spec(small)],
        [
            jax.ShapeDtypeStruct((rows, width), f32),
            jax.ShapeDtypeStruct((columns, rows), f32),
            jax.ShapeDtypeStruct((small, width), f32),
        ],
        [pltpu.VMEM((2 * count, rows), f32)]
        + [pltpu.VMEM((rows, scan_width), f32)] * 5
        + [
            pltpu.VMEM(((rows + 1) * count, scan_width), f32),
            pltpu.VMEM((rows * count, scan_width), f32),
            pltpu.VMEM((half_rows, lanes), f32),
            pltpu.VMEM((half_rows, lanes), f32),
            pltpu.VMEM((rows * count, lanes), f32),
            pltpu.VMEM((rows * count, lanes), f32),
        ],
        selected,
        other,
        step_pre,
        step,
        act,
        projected,
        gated_grad,
        masks,
        decay_log,
        entry,
        passed,
        returning,
        skip_gain,
        step_weight,
    )


def conv_grad_kernel(
    select_grad_ref,
    other_ref,
    select_ref,
    act_grad_ref,
    convolved_ref,
    act_ref,
    inner_ref,
    conv_weight_ref,
    mask_ref,
    *rest,
):
    inner_grad_ref, before_ref, last_ref, small_ref, inner, shifted = rest[-6:]
    rows = act_ref.shape[0]
    taps = conv_weight_ref.shape[0]
    columns = select_ref.shape[0]
    select_grad = (select_grad_ref[...] + other_ref[...]).astype(bf16)
    total = act_grad_ref[...] + lax.dot_general(
        select_grad, select_ref[...], contract_first, preferred_element_type=f32
    )
    conv_grad = total * silu_slope(convolved_ref[...])
    small_ref[:columns, :] = jnp.dot(select_grad, act_ref[...], preferred_element_type=f32)
    inner[:halo, :] = inner_ref[rows:, :].astype(f32)
    inner[halo:, :] = inner_ref[:rows, :].astype(f32)
    edges = jnp.zeros((8, conv_grad.shape[1]), f32)
    shifted[:8, :] = edges
    shifted[rows + 8 :, :] = edges
    out = conv_weight_ref[taps - 1 :, :] * conv_grad
    before = edges
    small_ref[columns + taps - 1 : columns + taps, :] = jnp.sum(
        conv_grad * inner[halo:, :], axis=0, keepdims=True
    )
    for lag in range(1, taps):
        masked = conv_grad * mask_ref[:, lag : lag + 1]
        at = taps - 1 - lag
        small_ref[columns + at : columns + at + 1, :] = jnp.sum(
            masked * inner[pl.ds(halo - lag, rows), :], axis=0, keepdims=True
        )
        shifted[8 : rows + 8, :] = masked
        weight = conv_weight_ref[at : at + 1, :]
        out = out + weight * shifted[pl.ds(8 + lag, rows), :]
        before = before + weight * shifted[pl.ds(lag, 8), :]
    small_ref[columns + taps : columns + taps + 1, :] = jnp.sum(conv_grad, axis=0, keepdims=True)
    inner_grad_ref[...] = out.astype(bf16)
    before_ref[...] = before
    last_ref[...] = out[rows - 8 :, :]


def convolve_grad(
    select_grad, other, select_weight, act_grad, convolved, act, projected, conv_weight, masks, waits
):
    rows, width = act.shape
    extended = rows + halo
    columns = select_weight.shape[0]
    taps = conv_weight.shape[0]
    small = columns + taps + 1
    return call(
        conv_grad_kernel,
        "convolve_grad",
        width,
        [
            whole_spec(columns, rows),
            whole_spec(columns, rows),
            column_spec(columns),
            column_spec(rows),
            column_spec(rows),
            column_spec(rows),
            part_spec(0, extended),
            column_spec(taps),
            whole_spec(rows, masks.shape[1]),
        ]
        + [pl.BlockSpec(memory_space=pl.ANY)] * len(waits),
        [column_spec(rows), column_spec(8), column_spec(8), column_spec(small)],
        [
            jax.ShapeDtypeStruct((rows, width), bf16),
            jax.ShapeDtypeStruct((8, width), f32),
            jax.ShapeDtypeStruct((8, width), f32),
            jax.ShapeDtypeStruct((small, width), f32),
        ],
        [pltpu.VMEM((extended, scan_width), f32), pltpu.VMEM((rows + 16, scan_width), f32)],
        select_grad,
        other,
        select_weight,
        act_grad,
        convolved,
        act,
        projected,
        conv_weight,
        masks,
        *waits,
    )


def normalize_kernel(
    own_ref,
    other_ref,
    edge_ref,
    other_edge_ref,
    gain_ref,
    ids_ref,
    whole_ref,
    extended_ref,
    normed_ref,
    inverse_ref,
    mask_ref,
    rows_ref,
):
    rows, half = own_ref.shape
    ids = ids_ref[...].astype(f32)
    place = lax.broadcasted_iota(jnp.int32, ids.shape, 1)
    same = []
    for lag in range(8):
        earlier = jnp.where(place < lag, ids[:, :1], pltpu.roll(ids, lag, 1)) if lag else ids
        same.append(jnp.where(earlier == ids, 1.0, 0.0))
    spare = jnp.zeros((lanes - 8, rows), f32)
    mask_ref[...] = jnp.concatenate(same + [spare]).T
    right = lax.axis_index("narrow") == 1
    for at, own, other in ((0, own_ref, other_ref), (rows, edge_ref, other_edge_ref)):
        end = at + own.shape[0]
        rows_ref[at:end, :half] = jnp.where(right, other[...], own[...])
        rows_ref[at:end, half:] = jnp.where(right, own[...], other[...])
    whole_ref[...] = rows_ref[:rows, :]
    whole = rows_ref[...].astype(f32)
    inverse = lax.rsqrt(jnp.mean(whole * whole, axis=1, keepdims=True) + epsilon)
    normed = (whole * inverse * gain_ref[...]).astype(bf16)
    extended_ref[...] = normed
    normed_ref[...] = normed[:rows]
    inverse_ref[...] = inverse[:rows]


def normalized(own, other, edge, other_edge, gain, ids):
    rows, half = own.shape
    extended = rows + edge.shape[0]
    return pl.pallas_call(
        normalize_kernel,
        out_shape=[
            jax.ShapeDtypeStruct((rows, 2 * half), bf16),
            jax.ShapeDtypeStruct((extended, 2 * half), bf16),
            jax.ShapeDtypeStruct((rows, 2 * half), bf16),
            jax.ShapeDtypeStruct((rows, 1), f32),
            jax.ShapeDtypeStruct((rows, lanes), f32),
        ],
        scratch_shapes=[pltpu.VMEM((extended, 2 * half), bf16)],
        cost_estimate=tiny_cost,
        name="normalized",
    )(own, other, edge, other_edge, gain, ids)


def after(array, *waits):
    anywhere = pl.BlockSpec(memory_space=pl.ANY)
    return pl.pallas_call(
        lambda *refs: None,
        in_specs=[anywhere] * (1 + len(waits)),
        out_specs=anywhere,
        out_shape=jax.ShapeDtypeStruct(array.shape, array.dtype),
        input_output_aliases={0: 0},
        cost_estimate=tiny_cost,
        name="after",
    )(array, *waits)


def patch_kernel(ids_ref, rows_ref, last_ref, next_ref, out_ref):
    count = ids_ref.shape[0]
    place = lax.broadcasted_iota(jnp.int32, (8, 1), 0)
    same = jnp.zeros((8, 1), f32)
    for lag in range(8):
        here = jnp.where(ids_ref[count - 1 - lag] == ids_ref[count - 1], 1.0, 0.0)
        same = same + jnp.where(place == 7 - lag, here, 0.0)
    total = last_ref[...] + next_ref[...] * same
    rows = rows_ref[...].astype(f32)
    out_ref[...] = jnp.concatenate([rows[: halo - 8], total]).astype(bf16)


def patched(ids, grads, last, following):
    rows, width = grads.shape
    block = pl.BlockSpec((halo, width), lambda j: (rows // halo - 1, 0))
    edge = pl.BlockSpec((8, width), lambda j: (0, 0))
    return pl.pallas_call(
        patch_kernel,
        grid=(1,),
        in_specs=[pl.BlockSpec(memory_space=pltpu.SMEM), block, edge, edge],
        out_specs=block,
        out_shape=jax.ShapeDtypeStruct((rows, width), bf16),
        input_output_aliases={1: 0},
        cost_estimate=tiny_cost,
        name="patched",
    )(ids, grads, last, following)


def edge_kernel(ids_ref, tokens_ref, out_ref):
    rows = ids_ref.shape[0]
    taps = 4
    out_ref[...] = tokens_ref[...]
    place = lax.broadcasted_iota(jnp.int32, (halo, 1), 0)
    same = jnp.zeros((halo, 1), f32)
    for lag in range(taps):
        here = jnp.where(ids_ref[rows - 1 - lag] == ids_ref[rows - 1], 1.0, 0.0)
        same = same + jnp.where(place == halo - 1 - lag, here, 0.0)
    out_ref[...] = (tokens_ref[...].astype(f32) * same).astype(bf16)


def edge_rows_of(ids, tokens):
    rows, width = tokens.shape
    return pl.pallas_call(
        edge_kernel,
        grid=(1,),
        in_specs=[
            pl.BlockSpec(memory_space=pltpu.SMEM),
            pl.BlockSpec((halo, width), lambda j: (rows // halo - 1, 0)),
        ],
        out_specs=pl.BlockSpec((halo, width), lambda j: (0, 0)),
        out_shape=jax.ShapeDtypeStruct((halo, width), bf16),
        cost_estimate=tiny_cost,
        name="edge_rows",
    )(ids, tokens)


block_rows, used_rows = 16, 12


def small_kernel(place_ref, scan_ref, conv_ref, keep_ref, *rest):
    *sends_refs, rows, blocks = rest
    rows[...] = jnp.zeros(rows.shape, f32)
    rows[: scan_ref.shape[0], :] = scan_ref[...]
    rows[scan_ref.shape[0] : scan_ref.shape[0] + conv_ref.shape[0], :] = conv_ref[...]
    blocks[...] = jnp.zeros(blocks.shape, f32)
    for n in range(16):
        blocks[n * block_rows : n * block_rows + used_rows, :] = rows[
            n * used_rows : (n + 1) * used_rows, :
        ]
    quarter = keep_ref.shape[0]
    for n in range(4):
        start = pl.multiple_of((place_ref[0] ^ n) * quarter, quarter)
        block = blocks[pl.ds(start, quarter), :]
        if n == 0:
            keep_ref[...] = block
        else:
            sends_refs[n - 1][...] = block.astype(bf16)


def small_quarters(place, scan_small, conv_small):
    width = scan_small.shape[1]
    return pl.pallas_call(
        small_kernel,
        in_specs=[pl.BlockSpec(memory_space=pltpu.SMEM)]
        + [pl.BlockSpec(memory_space=pltpu.VMEM)] * 2,
        out_shape=[jax.ShapeDtypeStruct((4 * block_rows, width), f32)]
        + [jax.ShapeDtypeStruct((4 * block_rows, width), bf16)] * 3,
        scratch_shapes=[
            pltpu.VMEM((16 * used_rows, width), f32),
            pltpu.VMEM((16 * block_rows, width), f32),
        ],
        cost_estimate=tiny_cost,
        name="small_quarters",
    )(place, scan_small, conv_small)


def quarter_kernel(
    place_ref,
    own_ref,
    near_ref,
    far_ref,
    last_ref,
    normed_0,
    normed_1,
    normed_2,
    normed_3,
    small_ref,
    first_ref,
    second_ref,
    third_ref,
    *rest,
):
    keep_ref, *sends_refs, piece, small = rest[-6:]
    total = None
    grads = (own_ref, near_ref, far_ref, last_ref)
    for left, right in zip((normed_0, normed_1, normed_2, normed_3), grads):
        part = lax.dot_general(left[...], right[...], contract_first, preferred_element_type=f32)
        total = part if total is None else total + part
    piece[...] = total
    small[...] = small_ref[...] + sum(
        ref[...].astype(f32) for ref in (first_ref, second_ref, third_ref)
    )
    rows, spare = piece.shape[0] // 4, small.shape[0] // 4
    for n in range(4):
        block = place_ref[0] ^ n
        inner_rows = piece[pl.ds(pl.multiple_of(block * rows, rows), rows), :]
        small_rows = small[pl.ds(pl.multiple_of(block * spare, spare), spare), :]
        if n == 0:
            keep_ref[:rows, :] = inner_rows
            keep_ref[rows:, :] = small_rows
        else:
            sends_refs[n - 1][:rows, :] = inner_rows.astype(bf16)
            sends_refs[n - 1][rows:, :] = small_rows.astype(bf16)


def inner_quarter(place, own, near, far, last, normed, smalls, waits):
    width = own.shape[1]
    quarter = normed[0].shape[1]
    spare = smalls[0].shape[0]
    rows = (quarter + spare) // 4
    return pl.pallas_call(
        quarter_kernel,
        in_specs=[pl.BlockSpec(memory_space=pltpu.SMEM)]
        + [pl.BlockSpec(memory_space=pltpu.VMEM)] * 12
        + [pl.BlockSpec(memory_space=pl.ANY)] * len(waits),
        out_shape=[jax.ShapeDtypeStruct((rows, width), f32)]
        + [jax.ShapeDtypeStruct((rows, width), bf16)] * 3,
        scratch_shapes=[pltpu.VMEM((quarter, width), f32), pltpu.VMEM((spare, width), f32)],
        compiler_params=pltpu.CompilerParams(vmem_limit_bytes=vmem_bytes),
        cost_estimate=tiny_cost,
        name="inner_quarter",
    )(place, own, near, far, last, *normed, *smalls, *waits)


def join_kernel(place_ref, gate_ref, first_ref, second_ref, *rest, small_rows):
    at_end = 2 + len(small_rows) if small_rows else 0
    out_ref = rest[-1 - at_end]
    step = pl.program_id(0)
    rows = out_ref.shape[0] // 2
    out_ref[:, 1, :] = gate_ref[...].astype(f32)

    def put(ref):
        for n in range(2):
            at = n * (rows + block_rows)
            out_ref[n * rows : (n + 1) * rows, 0, :] = ref[at : at + rows, :].astype(f32)

    @pl.when(step < 2)
    def _():
        put(first_ref)

    @pl.when(step >= 2)
    def _():
        put(second_ref)

    if not small_rows:
        return
    *row_refs, gain_ref, blocks = rest[-at_end:]

    @pl.when(step == 3)
    def _():
        for flip, ref in enumerate(rest[:4]):
            for n in range(4):
                at = ((place_ref[0] ^ flip) * 4 + n) * block_rows
                taken = ref[(n + 1) * rows + n * block_rows : (n + 1) * (rows + block_rows), :]
                blocks[pl.ds(pl.multiple_of(at, block_rows), block_rows), :] = taken.astype(f32)
        for ref, start in zip(row_refs, small_rows):
            for row in range(ref.shape[0]):
                at = (start + row) // used_rows * block_rows + (start + row) % used_rows
                ref[row : row + 1, :] = blocks[at : at + 1, :]
        gain_ref[...] = sum(
            blocks[n * block_rows + used_rows : n * block_rows + used_rows + 1, :] for n in range(16)
        )


def joined(place, flip, gate, first, second, before, waits, held=(), small_rows=(), small_counts=()):
    depth, width = gate.shape
    quarter = depth // 4
    block = quarter // 2
    piece = first.shape[0] // 2

    def target(j, place):
        return 2 * (place[0] ^ (flip + j // 2)) + lax.rem(j, 2)

    vmem = pl.BlockSpec(memory_space=pltpu.VMEM)
    untouched = [*before, *waits]
    return pl.pallas_call(
        functools.partial(join_kernel, small_rows=small_rows),
        grid_spec=pltpu.PrefetchScalarGridSpec(
            num_scalar_prefetch=1,
            grid=(4,),
            in_specs=[
                pl.BlockSpec((block, width), lambda j, place: (target(j, place), 0)),
                pl.BlockSpec((piece, width), lambda j, place: (jnp.minimum(j, 1), 0)),
                pl.BlockSpec((piece, width), lambda j, place: (jnp.maximum(j - 2, 0), 0)),
            ]
            + [vmem] * len(held)
            + [pl.BlockSpec(memory_space=pl.ANY)] * len(untouched),
            out_specs=[pl.BlockSpec((block, 2, width), lambda j, place: (target(j, place), 0, 0))]
            + [pl.BlockSpec((rows, width), lambda j, place: (0, 0)) for rows in small_counts],
            scratch_shapes=[pltpu.VMEM((16 * block_rows, width), f32)] if small_rows else [],
        ),
        out_shape=[jax.ShapeDtypeStruct((depth, 2, width), f32)]
        + [jax.ShapeDtypeStruct((rows, width), f32) for rows in small_counts],
        input_output_aliases={4 + len(held) + k: k for k in range(len(before))},
        compiler_params=pltpu.CompilerParams(vmem_limit_bytes=vmem_bytes),
        cost_estimate=tiny_cost,
        name="joined",
    )(place, gate, first, second, *held, *untouched)


def through(decay, total):
    return jnp.exp(decay * total)


def round_kernel(second_ref, decay_log_ref, own_ref, other_ref, passed_ref, new_passed_ref, *ends_refs):
    count = decay_log_ref.shape[0]
    decay = -jnp.exp(decay_log_ref[...])
    second = second_ref[0] > 0

    def split(ref):
        return ref[:count], ref[count : 2 * count], ref[2 * count : 2 * count + 1]

    own, other = split(own_ref), split(other_ref)
    early = [jnp.where(second, b, a) for a, b in zip(own, other)]
    late = [jnp.where(second, a, b) for a, b in zip(own, other)]
    state = late[0] + through(decay, late[2]) * early[0]
    adjoint = early[1] + through(decay, early[2]) * late[1]
    if len(ends_refs) == 2:
        ends_refs[0][...] = state
        ends_refs[1][...] = adjoint
    else:
        ends_refs[0][:count, :] = state
        ends_refs[0][count : 2 * count, :] = adjoint
        ends_refs[0][2 * count :, :] = jnp.broadcast_to(early[2] + late[2], (8, decay.shape[1]))
    before, after = passed_ref[:count], passed_ref[count : 2 * count]
    before_steps = passed_ref[2 * count : 2 * count + 1]
    after_steps = passed_ref[2 * count + 1 : 2 * count + 2]
    new_passed_ref[:count, :] = before + jnp.where(second, through(decay, before_steps) * other[0], 0.0)
    new_passed_ref[count : 2 * count, :] = after + jnp.where(
        second, 0.0, through(decay, after_steps) * other[1]
    )
    new_passed_ref[2 * count : 2 * count + 1, :] = before_steps + jnp.where(second, other[2], 0.0)
    new_passed_ref[2 * count + 1 : 2 * count + 2, :] = after_steps + jnp.where(second, 0.0, other[2])


def carried(ends, decay_log):
    count, width = decay_log.shape
    place = lax.axis_index("wide").astype(jnp.int32)
    passed = jnp.zeros((2 * count + 8, width), f32)
    packed = ends
    vmem = pl.BlockSpec(memory_space=pltpu.VMEM)
    for k, kinds in enumerate(([ends], [decay_log, decay_log])):
        passed, *out = pl.pallas_call(
            round_kernel,
            in_specs=[pl.BlockSpec(memory_space=pltpu.SMEM)] + [vmem] * 4,
            out_shape=[jax.ShapeDtypeStruct(kind.shape, f32) for kind in [passed] + kinds],
            cost_estimate=tiny_cost,
            name="carry_round",
        )((place >> k & 1)[None], decay_log, packed, swapped(packed, "wide", 2**k), passed)
        packed = out[0]
    from_before = passed_along(out[0], "wide", 4)
    from_after = passed_along(out[1], "wide", -4)
    return passed, from_before, from_after


def local(
    tokens,
    norm_gain,
    in_weight,
    conv_weight,
    conv_bias,
    select_weight,
    step_weight,
    step_bias,
    decay_log,
    skip_gain,
    out_weight,
    segment_ids,
    cotangent,
):
    rows, features = tokens.shape
    taps = conv_weight.shape[0]
    columns = select_weight.shape[0]
    rank = step_weight.shape[0]
    count = decay_log.shape[0]
    right_half = lax.axis_index("narrow") == 1

    def both_halves(own, other):
        return jnp.concatenate(
            [jnp.where(right_half, other, own), jnp.where(right_half, own, other)], axis=1
        )

    other_tokens = swapped(tokens, "narrow", 1)
    other_cot = swapped(cotangent, "narrow", 1)
    edge, other_edge = to_next_both(edge_rows_of(segment_ids, tokens))

    whole_low, normed_ext, normed, inverse, masks = normalized(
        tokens, other_tokens, edge, other_edge, norm_gain[None], segment_ids[None]
    )
    projected = jnp.einsum(
        "td,dce->cte", normed_ext, in_weight, preferred_element_type=f32
    ).astype(bf16)
    convolved, act, selected = convolve(
        projected, conv_weight, conv_bias[None], select_weight, masks
    )
    other_selected = swapped(selected, "narrow", 1)
    cot_whole = both_halves(cotangent, other_cot)
    gated_grad = lax.dot_general(
        cot_whole, out_weight, contract_last, preferred_element_type=f32
    )
    step_pre, step, ends = scan_ends(
        selected,
        other_selected,
        step_weight,
        step_bias[None],
        act,
        projected,
        gated_grad,
        masks,
        decay_log,
    )
    passed, entering, returning = carried(ends, decay_log)
    gated, gate_grad, entry = scan_forward(
        selected,
        other_selected,
        step,
        act,
        projected,
        gated_grad,
        masks,
        decay_log,
        passed,
        entering,
        skip_gain[None],
        returning,
    )
    products = (
        lax.dot_general(gated, cot_whole, contract_first, preferred_element_type=f32).astype(bf16),
        lax.dot_general(normed, gate_grad, contract_first, preferred_element_type=f32).astype(bf16),
    )
    out_sum, gate_sum = lax.psum(products, "wide")
    wide_place = lax.axis_index("wide").astype(jnp.int32)
    four_place = (wide_place & 3)[None]

    def narrow_halves(array):
        low, high = array[:, :features], array[:, features:]
        return jnp.where(right_half, high, low), jnp.where(right_half, low, high)

    def after_forward(products):
        whole = whole_low.astype(f32)
        normed_four = quarter_of_four(normed)
        out_part = jnp.dot(gated, out_weight, preferred_element_type=f32)
        out_mine, out_other = narrow_halves(out_part)
        out_theirs = swapped(out_other, "narrow", 1)
        act_grad, select_grad, scan_small = scan_backward(
            selected,
            other_selected,
            step_pre,
            step,
            act,
            projected,
            gated_grad,
            masks,
            decay_log,
            entry,
            passed,
            returning,
            skip_gain[None],
            step_weight,
        )
        layer_out = (tokens.astype(f32) + (out_mine + out_theirs)).astype(bf16)
        inner_main, before, last, conv_small = convolve_grad(
            select_grad,
            swapped(select_grad, "narrow", 1),
            select_weight,
            act_grad,
            convolved,
            act,
            projected,
            conv_weight,
            masks,
            [out_theirs, *normed_four],
        )
        inner_grad = patched(segment_ids, inner_main, last, passed_along(before, "wide", -1))
        near = swapped(inner_grad, "wide", 2)
        far = swapped(inner_grad, "wide", 1)
        keep, *sends = small_quarters(four_place, scan_small, conv_small)
        smalls = [keep] + [swapped(sends[n - 1], "wide", n) for n in (1, 2, 3)]
        normed_part = jnp.einsum(
            "cte,dce->td", jnp.stack([inner_grad, gate_grad]), in_weight, preferred_element_type=f32
        )
        gain_part = jnp.sum(normed_part * whole * inverse, axis=0, keepdims=True)
        row_part = jnp.sum(normed_part * norm_gain * whole, axis=1)[None]
        normed_mine, normed_other = narrow_halves(normed_part)
        row_theirs = swapped(row_part, "narrow", 1)
        normed_theirs = swapped(normed_other, "narrow", 1)
        near = after(near, *smalls[1:])
        keep, *sends = inner_quarter(
            (wide_place >> 2 & 3)[None],
            inner_grad,
            near,
            far,
            swapped(near, "wide", 1),
            normed_four,
            smalls,
            [row_theirs],
        )
        row_sum = (row_part + row_theirs).reshape(rows, 1)
        gain_mine = jnp.where(right_half, norm_gain[features:], norm_gain[:features])
        whole_grad = inverse * (gain_mine * (normed_mine + normed_theirs)) - tokens.astype(f32) * (
            inverse * inverse * inverse
        ) * (row_sum / (2 * features))
        tokens_grad = (whole_grad + cotangent.astype(f32)).astype(bf16)
        first_bits, *more_bits = group_bits(2)
        gain_sum = gain_part + swapped(gain_part, "narrow", 1)
        for bit in (bit for bits in more_bits for bit in bits):
            gain_sum = gain_sum + swapped(gain_sum, "wide", bit)
        held = keep
        for n, flip in enumerate(flips(first_bits)[1:]):
            held = held + swapped(sends[n], "wide", flip).astype(f32)
        for bits in more_bits:
            held = scattered(held, bits)
        held = held.astype(bf16)
        for bits in reversed(more_bits):
            held = gathered(held, bits)
        spare = jnp.broadcast_to(gain_sum, (block_rows - used_rows, gain_sum.shape[1]))
        held = jnp.concatenate([held[: held.shape[0] - spare.shape[0]], spare.astype(bf16)])
        held = gathered(held, first_bits)
        return held, layer_out, tokens_grad

    kinds = jax.eval_shape(after_forward, products)
    held, layer_out, tokens_grad = lax.cond(
        segment_ids[0] >= 0,
        after_forward,
        lambda pair: jax.tree.map(lambda kind: jnp.zeros(kind.shape, kind.dtype), kinds),
        products,
    )

    out_weight_grad = out_sum.astype(f32)
    core = swapped(held, "wide", 1)
    (begun,) = joined(four_place, 0, gate_sum, held, core, (), (out_weight_grad,))
    near = after(swapped(held, "wide", 2), begun)
    far = swapped(near, "wide", 1)
    conv_at = rank + count + 2
    (
        in_weight_grad,
        step_weight_grad,
        decay_log_grad,
        skip_gain_grad,
        step_bias_grad,
        select_weight_grad,
        conv_weight_grad,
        conv_bias_grad,
        norm_gain_grad,
    ) = joined(
        four_place,
        2,
        gate_sum,
        near,
        far,
        (begun,),
        (),
        (held, core, near, far),
        (0, rank, rank + count, rank + count + 1, conv_at, conv_at + columns, conv_at + columns + taps),
        (rank, count, 1, 1, columns, taps, 1, 1),
    )
    return (
        layer_out,
        tokens_grad,
        norm_gain_grad[0],
        in_weight_grad,
        conv_weight_grad,
        conv_bias_grad[0],
        select_weight_grad,
        step_weight_grad,
        step_bias_grad[0],
        decay_log_grad,
        skip_gain_grad[0],
        out_weight_grad,
    )


def solution(mesh):
    placed = (
        P("wide", "narrow"),
        P(),
        P(None, None, "narrow"),
        P(None, "narrow"),
        P("narrow"),
        P(None, "narrow"),
        P(None, "narrow"),
        P("narrow"),
        P(None, "narrow"),
        P("narrow"),
        P("narrow", None),
        P("wide"),
        P("wide", "narrow"),
    )
    return jax.shard_map(
        local,
        mesh=mesh,
        in_specs=placed,
        out_specs=(
            P("wide", "narrow"),
            P("wide", "narrow"),
            P(),
            P(None, None, "narrow"),
            P(None, "narrow"),
            P("narrow"),
            P(None, "narrow"),
            P(None, "narrow"),
            P("narrow"),
            P(None, "narrow"),
            P("narrow"),
            P("narrow", None),
        ),
        check_vma=False,
    )
```

```python
import functools

import jax
import jax.numpy as jnp
from jax import lax
from jax.experimental import pallas as pl
from jax.experimental.pallas import tpu as pltpu
from jax.sharding import PartitionSpec as P

epsilon = 1e-05
log2e = 1.4426950408889634
reset_step = 1e30
lanes = 128
halo = 16
body_rows = 32
scan_width = 512
vmem_bytes = 56 * 1024 * 1024
tiny_cost = pl.CostEstimate(flops=1, bytes_accessed=1, transcendentals=0)
f32 = jnp.float32
bf16 = jnp.bfloat16
contract_first = (((0,), (0,)), ((), ()))
contract_last = (((1,), (1,)), ((), ()))


def passed_along(array, axis, by):
    peers = lax.axis_size(axis)
    pairs = [(i, i + by) for i in range(peers) if 0 <= i + by < peers]
    return lax.ppermute(array, axis, pairs)


def swapped(array, axis, bit):
    peers = lax.axis_size(axis)
    return lax.ppermute(array, axis, [(i, i ^ bit) for i in range(peers)])


def wide_bits():
    bit, bits = 1, []
    while bit < lax.axis_size("wide"):
        bits.append(bit)
        bit *= 2
    return bits


def to_next_both(array):
    count, sides = lax.axis_size("wide"), lax.axis_size("narrow")
    pairs = [
        (i * sides + k, (i + 1) * sides + (sides - 1 - k))
        for i in range(count - 1)
        for k in range(sides)
    ]
    return passed_along(array, "wide", 1), lax.ppermute(array, ("wide", "narrow"), pairs)


def is_upper(bit):
    return (lax.axis_index("wide") & bit) != 0


def group_bits(size):
    bits, bit = [], 4
    while bit < lax.axis_size("wide"):
        bits.append(bit)
        bit *= 2
    return [tuple(bits[k : k + size]) for k in range(0, len(bits), size)]


def flips(bits):
    return [sum(b for k, b in enumerate(bits) if n >> k & 1) for n in range(2 ** len(bits))]


def scattered(piece, bits):
    rows = piece.shape[0] // 2 ** len(bits)
    here = sum(is_upper(b).astype(jnp.int32) << k for k, b in enumerate(bits))

    def block(n):
        return lax.dynamic_slice_in_dim(piece, (here ^ n) * rows, rows, 0)

    total = block(0).astype(f32)
    for n, flip in enumerate(flips(bits)):
        if n > 0:
            total = total + swapped(block(n).astype(bf16), "wide", flip).astype(f32)
    return total


def gathered(held, bits, *waits):
    blocks = [held] + [swapped(held, "wide", flip) for flip in flips(bits)[1:]]
    if waits:
        blocks[1] = after(blocks[1], *waits)
    for bit in bits:
        upper = is_upper(bit)
        blocks = [
            jnp.concatenate([jnp.where(upper, b, a), jnp.where(upper, a, b)])
            for a, b in zip(blocks[0::2], blocks[1::2])
        ]
    return blocks[0]


def halves_of(array, axis):
    upper = is_upper(1).astype(jnp.int32)
    half = array.shape[axis] // 2
    return (
        lax.dynamic_slice_in_dim(array, upper * half, half, axis),
        lax.dynamic_slice_in_dim(array, (1 - upper) * half, half, axis),
    )


def folded(keep, arrived, bit):
    half = keep.shape[0] // 2
    upper = is_upper(bit).astype(jnp.int32)

    def rows(start):
        return lax.dynamic_slice_in_dim(keep, start, half, 0) + lax.dynamic_slice_in_dim(
            arrived, start, half, 0
        ).astype(f32)

    return rows(upper * half), rows((1 - upper) * half).astype(bf16)


def unfolded(held, arrived, bit):
    upper = is_upper(bit)
    return jnp.concatenate([jnp.where(upper, arrived, held), jnp.where(upper, held, arrived)])


def quarter_of_four(array):
    width = array.shape[1] // 4
    here = lax.axis_index("wide") & 3

    def quarter(n):
        return lax.dynamic_slice_in_dim(array, (here ^ n) * width, width, 1)

    return [quarter(0)] + [swapped(quarter(n), "wide", n) for n in (2, 1, 3)]


def silu_slope(values):
    logistic = jax.nn.sigmoid(values)
    return logistic * (1.0 + values * (1.0 - logistic))


def softplus(values):
    return jnp.maximum(values, 0.0) + jnp.log1p(jnp.exp(-jnp.abs(values)))


def column_spec(rows, start=0):
    return pl.BlockSpec((rows, scan_width), lambda j: (0, start + j))


def part_spec(part, rows, start=0):
    return pl.BlockSpec((None, rows, scan_width), lambda j: (part, 0, start + j))


def whole_spec(rows, width):
    return pl.BlockSpec((rows, width), lambda j: (0, 0))


def call(kernel, name, width, in_specs, out_specs, out_shape, scratch, *operands):
    return pl.pallas_call(
        kernel,
        grid=(width // scan_width,),
        in_specs=in_specs,
        out_specs=out_specs,
        out_shape=out_shape,
        scratch_shapes=scratch,
        compiler_params=pltpu.CompilerParams(vmem_limit_bytes=vmem_bytes),
        cost_estimate=tiny_cost,
        name=name,
    )(*operands)


def conv_kernel(
    inner_ref,
    conv_weight_ref,
    conv_bias_ref,
    select_ref,
    mask_ref,
    convolved_ref,
    act_ref,
    selected_ref,
    inner,
):
    rows = act_ref.shape[0]
    taps = conv_weight_ref.shape[0]
    inner[:halo, :] = inner_ref[rows:, :].astype(f32)
    inner[halo:, :] = inner_ref[:rows, :].astype(f32)
    total = conv_bias_ref[...] + conv_weight_ref[taps - 1 :, :] * inner[halo:, :]
    for lag in range(1, taps):
        earlier = inner[pl.ds(halo - lag, rows), :] * mask_ref[:, lag : lag + 1]
        total = total + conv_weight_ref[taps - 1 - lag : taps - lag, :] * earlier
    convolved_ref[...] = total
    act = (total * jax.nn.sigmoid(total)).astype(bf16)
    act_ref[...] = act
    part = lax.dot_general(select_ref[...], act, contract_last, preferred_element_type=f32)

    @pl.when(pl.program_id(0) == 0)
    def _():
        selected_ref[...] = part

    @pl.when(pl.program_id(0) > 0)
    def _():
        selected_ref[...] += part


def convolve(projected, conv_weight, conv_bias, select_weight, masks):
    parts, extended, width = projected.shape
    rows = extended - halo
    taps = conv_weight.shape[0]
    columns = select_weight.shape[0]
    return call(
        conv_kernel,
        "convolve",
        width,
        [
            part_spec(0, extended),
            column_spec(taps),
            column_spec(1),
            column_spec(columns),
            whole_spec(rows, masks.shape[1]),
        ],
        [column_spec(rows), column_spec(rows), whole_spec(columns, rows)],
        [
            jax.ShapeDtypeStruct((rows, width), f32),
            jax.ShapeDtypeStruct((rows, width), bf16),
            jax.ShapeDtypeStruct((columns, rows), f32),
        ],
        [pltpu.VMEM((extended, scan_width), f32)],
        projected,
        conv_weight,
        conv_bias,
        select_weight,
        masks,
    )


def coef_columns(coef, block):
    per_tile = lanes // body_rows
    start = pl.multiple_of((block // per_tile) * lanes, lanes)
    tile = coef[:, pl.ds(start, lanes)]
    back = body_rows * lax.rem(block, per_tile)
    return pltpu.roll(tile, lax.rem(lanes - back, lanes), 1)


def ends_kernel(
    selected_ref,
    other_ref,
    step_weight_ref,
    step_bias_ref,
    act_ref,
    gate_ref,
    gated_grad_ref,
    mask_ref,
    decay_log_ref,
    step_pre_ref,
    step_ref,
    ends_ref,
    coef,
    held_step,
    drive,
    scan_grad,
):
    rows = act_ref.shape[0]
    count = decay_log_ref.shape[0]
    rank = step_weight_ref.shape[0]
    decay2 = -jnp.exp(decay_log_ref[...]) * log2e
    selected = selected_ref[...] + other_ref[...]
    coef[...] = selected[rank:, :]
    step_low = selected[:rank, :].astype(bf16)
    step_pre = step_bias_ref[...] + lax.dot_general(
        step_low, step_weight_ref[...], contract_first, preferred_element_type=f32
    )
    step_pre_ref[...] = step_pre
    step = softplus(step_pre)
    step_ref[...] = step
    held_step[...] = jnp.where(mask_ref[:, 1:2] > 0.0, step, reset_step)
    drive[...] = step * act_ref[...].astype(f32)
    gate = gate_ref[...].astype(f32)
    scan_grad[...] = gated_grad_ref[...] * (gate * jax.nn.sigmoid(gate))
    zero = jnp.zeros(decay2.shape, f32)

    def body(block, carried):
        state, product, adjoint = carried
        columns = coef_columns(coef, block)
        for i in range(body_rows):
            row = pl.ds(block * body_rows + i, 1)
            factor = jnp.exp2(held_step[row, :] * decay2)
            state = factor * state + columns[:count, i : i + 1] * drive[row, :]
            product = factor * product
            adjoint = adjoint + product * (columns[count:, i : i + 1] * scan_grad[row, :])
        return state, product, adjoint

    state, product, adjoint = lax.fori_loop(0, rows // body_rows, body, (zero, zero + 1.0, zero))
    ends_ref[:count, :] = state
    ends_ref[count : 2 * count, :] = adjoint
    total = jnp.sum(held_step[...], axis=0, keepdims=True)
    ends_ref[2 * count :, :] = jnp.broadcast_to(total, (8, total.shape[1]))


def scan_ends(
    selected, other, step_weight, step_bias, act, projected, gated_grad, masks, decay_log
):
    rows, width = act.shape
    count = decay_log.shape[0]
    columns = selected.shape[0]
    rank = step_weight.shape[0]
    return call(
        ends_kernel,
        "scan_ends",
        width,
        [
            whole_spec(columns, rows),
            whole_spec(columns, rows),
            column_spec(rank),
            column_spec(1),
            column_spec(rows),
            part_spec(1, rows),
            column_spec(rows),
            whole_spec(rows, masks.shape[1]),
            column_spec(count),
        ],
        [column_spec(rows), column_spec(rows), column_spec(2 * count + 8)],
        [
            jax.ShapeDtypeStruct((rows, width), f32),
            jax.ShapeDtypeStruct((rows, width), f32),
            jax.ShapeDtypeStruct((2 * count + 8, width), f32),
        ],
        [pltpu.VMEM((2 * count, rows), f32)] + [pltpu.VMEM((rows, scan_width), f32)] * 3,
        selected,
        other,
        step_weight,
        step_bias,
        act,
        projected,
        gated_grad,
        masks,
        decay_log,
    )


def lane_tiles(values):
    return [values[:, k : k + lanes] for k in range(0, values.shape[1], lanes)]


def tree_sum(parts):
    while len(parts) > 1:
        odd = parts[len(parts) // 2 * 2 :]
        parts = [a + b for a, b in zip(parts[0::2], parts[1::2])] + odd
    return parts[0]


def keep_halves(scratch, i, values):
    for k, tile in enumerate(lane_tiles(values)):
        at = (k * body_rows + i) * 8
        scratch[at : at + 8, :] = tile[:8] + tile[8:]


def put_state_sums(scratch, out_ref, block):
    for group in range(body_rows // 8):
        row = pl.ds(pl.multiple_of(block * body_rows + group * 8, 8), 8)
        for k in range(out_ref.shape[1] // lanes):
            at = (k * body_rows + group * 8) * 8
            total = tree_sum([scratch[pl.ds(at + n, 8, stride=8), :] for n in range(8)])
            out_ref[row, k * lanes : (k + 1) * lanes] = total


def lane_sums(values):
    ones = jnp.ones((8, lanes), bf16)
    high = values.astype(bf16)
    low = (values - high.astype(f32)).astype(bf16)
    total = lax.dot_general(ones, high, contract_last, preferred_element_type=f32)
    total += lax.dot_general(ones, low, contract_last, preferred_element_type=f32)
    return total[:1, :]


def at_token(t, count):
    return pl.ds(pl.multiple_of(t * count, count), count)


def forward_kernel(
    selected_ref,
    other_ref,
    step_ref,
    act_ref,
    gate_ref,
    gated_grad_ref,
    mask_ref,
    decay_log_ref,
    passed_ref,
    entering_ref,
    skip_ref,
    gated_ref,
    gate_grad_ref,
    entry_ref,
    coef,
    held_step,
    drive,
    scanned,
    halves,
):
    rows = step_ref.shape[0]
    count = decay_log_ref.shape[0]
    rank = selected_ref.shape[0] - 2 * count
    decay = -jnp.exp(decay_log_ref[...])
    decay2 = decay * log2e
    before_steps = passed_ref[2 * count : 2 * count + 1, :]
    entry = passed_ref[:count, :] + through(decay, before_steps) * entering_ref[...]
    entry_ref[...] = entry
    coef[...] = selected_ref[rank:, :] + other_ref[rank:, :]
    act = act_ref[...].astype(f32)
    held_step[...] = jnp.where(mask_ref[:, 1:2] > 0.0, step_ref[...], reset_step)
    drive[...] = step_ref[...] * act

    def forward(block, state):
        columns = coef_columns(coef, block)
        for i in range(body_rows):
            row = pl.ds(block * body_rows + i, 1)
            factor = jnp.exp2(held_step[row, :] * decay2)
            state = factor * state + columns[:count, i : i + 1] * drive[row, :]
            keep_halves(halves, i, columns[count:, i : i + 1] * state)
        put_state_sums(halves, scanned, block)
        return state

    lax.fori_loop(0, rows // body_rows, forward, entry)
    gate = gate_ref[...].astype(f32)
    logistic = jax.nn.sigmoid(gate)
    total = scanned[...] + skip_ref[...] * act
    gated_ref[...] = (total * (gate * logistic)).astype(bf16)
    slope = logistic * (1.0 + gate * (1.0 - logistic))
    gate_grad_ref[...] = (gated_grad_ref[...] * total * slope).astype(bf16)


def scan_forward(
    selected, other, step, act, projected, gated_grad, masks, decay_log, passed, entering, skip_gain
):
    rows, width = step.shape
    count = decay_log.shape[0]
    columns = selected.shape[0]
    return call(
        forward_kernel,
        "scan_forward",
        width,
        [
            whole_spec(columns, rows),
            whole_spec(columns, rows),
            column_spec(rows),
            column_spec(rows),
            part_spec(1, rows),
            column_spec(rows),
            whole_spec(rows, masks.shape[1]),
            column_spec(count),
            column_spec(2 * count + 8),
            column_spec(count),
            column_spec(1),
        ],
        [column_spec(rows), column_spec(rows), column_spec(count)],
        [
            jax.ShapeDtypeStruct((rows, width), bf16),
            jax.ShapeDtypeStruct((rows, width), bf16),
            jax.ShapeDtypeStruct((count, width), f32),
        ],
        [pltpu.VMEM((2 * count, rows), f32)]
        + [pltpu.VMEM((rows, scan_width), f32)] * 3
        + [pltpu.VMEM((8 * body_rows * (scan_width // lanes), lanes), f32)],
        selected,
        other,
        step,
        act,
        projected,
        gated_grad,
        masks,
        decay_log,
        passed,
        entering,
        skip_gain,
    )


def backward_kernel(
    selected_ref,
    other_ref,
    step_pre_ref,
    step_ref,
    act_ref,
    gate_ref,
    gated_grad_ref,
    mask_ref,
    decay_log_ref,
    entry_ref,
    passed_ref,
    returning_ref,
    skip_ref,
    step_weight_ref,
    wait_ref,
    act_grad_ref,
    select_grad_ref,
    small_ref,
    coef,
    held_step,
    drive,
    scan_grad,
    weighted,
    held_sum,
    states,
    factors,
    halves,
    more_halves,
    in_sum,
    read_sum,
):
    rows = step_ref.shape[0]
    count = decay_log_ref.shape[0]
    rank = step_weight_ref.shape[0]
    blocks = rows // body_rows
    decay = -jnp.exp(decay_log_ref[...])
    decay2 = decay * log2e
    after_steps = passed_ref[2 * count + 1 : 2 * count + 2, :]
    tail = passed_ref[count : 2 * count, :] + through(decay, after_steps) * returning_ref[...]
    selected = selected_ref[...] + other_ref[...]
    coef[...] = selected[rank:, :]
    step_low = selected[:rank, :].astype(bf16)
    step = step_ref[...]
    act = act_ref[...].astype(f32)
    held_step[...] = jnp.where(mask_ref[:, 1:2] > 0.0, step, reset_step)
    drive[...] = step * act
    gate = gate_ref[...].astype(f32)
    grads = gated_grad_ref[...] * (gate * jax.nn.sigmoid(gate))
    scan_grad[...] = grads
    small_ref[rank + count : rank + count + 1, :] = jnp.sum(grads * act, axis=0, keepdims=True)
    states[:count, :] = entry_ref[...]

    @pl.when(pl.program_id(0) == 0)
    def _():
        in_sum[...] = jnp.zeros(in_sum.shape, f32)
        read_sum[...] = jnp.zeros(read_sum.shape, f32)
        select_grad_ref[...] = jnp.zeros(select_grad_ref.shape, f32)

    def forward(block, state):
        columns = coef_columns(coef, block)
        for i in range(body_rows):
            t = block * body_rows + i
            row = pl.ds(t, 1)
            factor = jnp.exp2(held_step[row, :] * decay2)
            state = factor * state + columns[:count, i : i + 1] * drive[row, :]
            factors[at_token(t, count), :] = factor
            states[at_token(t + 1, count), :] = state
        return state

    lax.fori_loop(0, blocks, forward, entry_ref[...])

    def backward(k, carried):
        adjoint, decay_grad = carried
        block = blocks - 1 - k
        columns = coef_columns(coef, block)
        for i in range(body_rows - 1, -1, -1):
            t = block * body_rows + i
            row = pl.ds(t, 1)
            here = at_token(t, count)
            grad = scan_grad[row, :]
            summed = columns[count:, i : i + 1] * grad + adjoint
            read_sum[here, :] += tree_sum(lane_tiles(grad * states[at_token(t + 1, count), :]))
            in_sum[here, :] += tree_sum(lane_tiles(summed * drive[row, :]))
            keep_halves(halves, i, summed * columns[:count, i : i + 1])
            adjoint = factors[here, :] * summed
            held = adjoint * states[here, :]
            decay_grad = decay_grad + held * step_ref[row, :]
            keep_halves(more_halves, i, held * decay)
        put_state_sums(halves, weighted, block)
        put_state_sums(more_halves, held_sum, block)
        return adjoint, decay_grad

    ignored, decay_grad = lax.fori_loop(
        0, blocks, backward, (tail, jnp.zeros(decay.shape, f32))
    )
    act_grad_ref[...] = step * weighted[...] + skip_ref[...] * scan_grad[...]
    step_grad = act * weighted[...] + held_sum[...]
    pre_grad = (step_grad * jax.nn.sigmoid(step_pre_ref[...])).astype(bf16)
    small_ref[:rank, :] = jnp.dot(step_low, pre_grad, preferred_element_type=f32)
    small_ref[rank : rank + count, :] = decay_grad * decay
    bias_grad = jnp.sum(pre_grad.astype(f32), axis=0, keepdims=True)
    small_ref[rank + count + 1 : rank + count + 2, :] = bias_grad
    select_grad_ref[:rank, :] += lax.dot_general(
        step_weight_ref[...], pre_grad, contract_last, preferred_element_type=f32
    )

    @pl.when(pl.program_id(0) == pl.num_programs(0) - 1)
    def _():
        for n in range(count):
            at = pl.ds(n, rows, stride=count)
            select_grad_ref[rank + n : rank + n + 1, :] = lane_sums(in_sum[at, :])
            select_grad_ref[rank + count + n : rank + count + n + 1, :] = lane_sums(read_sum[at, :])


def scan_backward(
    selected,
    other,
    step_pre,
    step,
    act,
    projected,
    gated_grad,
    masks,
    decay_log,
    entry,
    passed,
    returning,
    skip_gain,
    step_weight,
    wait,
):
    rows, width = step.shape
    count = decay_log.shape[0]
    columns = selected.shape[0]
    rank = step_weight.shape[0]
    half_rows = 8 * body_rows * (scan_width // lanes)
    small = rank + count + 2
    return call(
        backward_kernel,
        "scan_backward",
        width,
        [
            whole_spec(columns, rows),
            whole_spec(columns, rows),
            column_spec(rows),
            column_spec(rows),
            column_spec(rows),
            part_spec(1, rows),
            column_spec(rows),
            whole_spec(rows, masks.shape[1]),
            column_spec(count),
            column_spec(count),
            column_spec(2 * count + 8),
            column_spec(count),
            column_spec(1),
            column_spec(rank),
            pl.BlockSpec(memory_space=pl.ANY),
        ],
        [column_spec(rows), whole_spec(columns, rows), column_spec(small)],
        [
            jax.ShapeDtypeStruct((rows, width), f32),
            jax.ShapeDtypeStruct((columns, rows), f32),
            jax.ShapeDtypeStruct((small, width), f32),
        ],
        [pltpu.VMEM((2 * count, rows), f32)]
        + [pltpu.VMEM((rows, scan_width), f32)] * 5
        + [
            pltpu.VMEM(((rows + 1) * count, scan_width), f32),
            pltpu.VMEM((rows * count, scan_width), f32),
            pltpu.VMEM((half_rows, lanes), f32),
            pltpu.VMEM((half_rows, lanes), f32),
            pltpu.VMEM((rows * count, lanes), f32),
            pltpu.VMEM((rows * count, lanes), f32),
        ],
        selected,
        other,
        step_pre,
        step,
        act,
        projected,
        gated_grad,
        masks,
        decay_log,
        entry,
        passed,
        returning,
        skip_gain,
        step_weight,
        wait,
    )


def conv_grad_kernel(
    select_grad_ref,
    other_ref,
    select_ref,
    act_grad_ref,
    convolved_ref,
    act_ref,
    inner_ref,
    conv_weight_ref,
    mask_ref,
    *rest,
):
    inner_grad_ref, before_ref, last_ref, small_ref, inner, shifted = rest[-6:]
    rows = act_ref.shape[0]
    taps = conv_weight_ref.shape[0]
    columns = select_ref.shape[0]
    select_grad = (select_grad_ref[...] + other_ref[...]).astype(bf16)
    total = act_grad_ref[...] + lax.dot_general(
        select_grad, select_ref[...], contract_first, preferred_element_type=f32
    )
    conv_grad = total * silu_slope(convolved_ref[...])
    small_ref[:columns, :] = jnp.dot(select_grad, act_ref[...], preferred_element_type=f32)
    inner[:halo, :] = inner_ref[rows:, :].astype(f32)
    inner[halo:, :] = inner_ref[:rows, :].astype(f32)
    edges = jnp.zeros((8, conv_grad.shape[1]), f32)
    shifted[:8, :] = edges
    shifted[rows + 8 :, :] = edges
    out = conv_weight_ref[taps - 1 :, :] * conv_grad
    before = edges
    small_ref[columns + taps - 1 : columns + taps, :] = jnp.sum(
        conv_grad * inner[halo:, :], axis=0, keepdims=True
    )
    for lag in range(1, taps):
        masked = conv_grad * mask_ref[:, lag : lag + 1]
        at = taps - 1 - lag
        small_ref[columns + at : columns + at + 1, :] = jnp.sum(
            masked * inner[pl.ds(halo - lag, rows), :], axis=0, keepdims=True
        )
        shifted[8 : rows + 8, :] = masked
        weight = conv_weight_ref[at : at + 1, :]
        out = out + weight * shifted[pl.ds(8 + lag, rows), :]
        before = before + weight * shifted[pl.ds(lag, 8), :]
    small_ref[columns + taps : columns + taps + 1, :] = jnp.sum(conv_grad, axis=0, keepdims=True)
    inner_grad_ref[...] = out.astype(bf16)
    before_ref[...] = before
    last_ref[...] = out[rows - 8 :, :]


def convolve_grad(
    select_grad, other, select_weight, act_grad, convolved, act, projected, conv_weight, masks, waits
):
    rows, width = act.shape
    extended = rows + halo
    columns = select_weight.shape[0]
    taps = conv_weight.shape[0]
    small = columns + taps + 1
    return call(
        conv_grad_kernel,
        "convolve_grad",
        width,
        [
            whole_spec(columns, rows),
            whole_spec(columns, rows),
            column_spec(columns),
            column_spec(rows),
            column_spec(rows),
            column_spec(rows),
            part_spec(0, extended),
            column_spec(taps),
            whole_spec(rows, masks.shape[1]),
        ]
        + [pl.BlockSpec(memory_space=pl.ANY)] * len(waits),
        [column_spec(rows), column_spec(8), column_spec(8), column_spec(small)],
        [
            jax.ShapeDtypeStruct((rows, width), bf16),
            jax.ShapeDtypeStruct((8, width), f32),
            jax.ShapeDtypeStruct((8, width), f32),
            jax.ShapeDtypeStruct((small, width), f32),
        ],
        [pltpu.VMEM((extended, scan_width), f32), pltpu.VMEM((rows + 16, scan_width), f32)],
        select_grad,
        other,
        select_weight,
        act_grad,
        convolved,
        act,
        projected,
        conv_weight,
        masks,
        *waits,
    )


def normalize_kernel(
    own_ref,
    other_ref,
    edge_ref,
    other_edge_ref,
    gain_ref,
    ids_ref,
    whole_ref,
    extended_ref,
    normed_ref,
    inverse_ref,
    mask_ref,
    rows_ref,
):
    rows, half = own_ref.shape
    ids = ids_ref[...].astype(f32)
    place = lax.broadcasted_iota(jnp.int32, ids.shape, 1)
    same = []
    for lag in range(8):
        earlier = jnp.where(place < lag, ids[:, :1], pltpu.roll(ids, lag, 1)) if lag else ids
        same.append(jnp.where(earlier == ids, 1.0, 0.0))
    spare = jnp.zeros((lanes - 8, rows), f32)
    mask_ref[...] = jnp.concatenate(same + [spare]).T
    right = lax.axis_index("narrow") == 1
    for at, own, other in ((0, own_ref, other_ref), (rows, edge_ref, other_edge_ref)):
        end = at + own.shape[0]
        rows_ref[at:end, :half] = jnp.where(right, other[...], own[...])
        rows_ref[at:end, half:] = jnp.where(right, own[...], other[...])
    whole_ref[...] = rows_ref[:rows, :]
    whole = rows_ref[...].astype(f32)
    inverse = lax.rsqrt(jnp.mean(whole * whole, axis=1, keepdims=True) + epsilon)
    normed = (whole * inverse * gain_ref[...]).astype(bf16)
    extended_ref[...] = normed
    normed_ref[...] = normed[:rows]
    inverse_ref[...] = inverse[:rows]


def normalized(own, other, edge, other_edge, gain, ids):
    rows, half = own.shape
    extended = rows + edge.shape[0]
    return pl.pallas_call(
        normalize_kernel,
        out_shape=[
            jax.ShapeDtypeStruct((rows, 2 * half), bf16),
            jax.ShapeDtypeStruct((extended, 2 * half), bf16),
            jax.ShapeDtypeStruct((rows, 2 * half), bf16),
            jax.ShapeDtypeStruct((rows, 1), f32),
            jax.ShapeDtypeStruct((rows, lanes), f32),
        ],
        scratch_shapes=[pltpu.VMEM((extended, 2 * half), bf16)],
        cost_estimate=tiny_cost,
        name="normalized",
    )(own, other, edge, other_edge, gain, ids)


def after(array, *waits):
    anywhere = pl.BlockSpec(memory_space=pl.ANY)
    return pl.pallas_call(
        lambda *refs: None,
        in_specs=[anywhere] * (1 + len(waits)),
        out_specs=anywhere,
        out_shape=jax.ShapeDtypeStruct(array.shape, array.dtype),
        input_output_aliases={0: 0},
        cost_estimate=tiny_cost,
        name="after",
    )(array, *waits)


def patch_kernel(ids_ref, rows_ref, last_ref, next_ref, out_ref):
    count = ids_ref.shape[0]
    place = lax.broadcasted_iota(jnp.int32, (8, 1), 0)
    same = jnp.zeros((8, 1), f32)
    for lag in range(8):
        here = jnp.where(ids_ref[count - 1 - lag] == ids_ref[count - 1], 1.0, 0.0)
        same = same + jnp.where(place == 7 - lag, here, 0.0)
    total = last_ref[...] + next_ref[...] * same
    rows = rows_ref[...].astype(f32)
    out_ref[...] = jnp.concatenate([rows[: halo - 8], total]).astype(bf16)


def patched(ids, grads, last, following):
    rows, width = grads.shape
    block = pl.BlockSpec((halo, width), lambda j: (rows // halo - 1, 0))
    edge = pl.BlockSpec((8, width), lambda j: (0, 0))
    return pl.pallas_call(
        patch_kernel,
        grid=(1,),
        in_specs=[pl.BlockSpec(memory_space=pltpu.SMEM), block, edge, edge],
        out_specs=block,
        out_shape=jax.ShapeDtypeStruct((rows, width), bf16),
        input_output_aliases={1: 0},
        cost_estimate=tiny_cost,
        name="patched",
    )(ids, grads, last, following)


def edge_kernel(ids_ref, tokens_ref, out_ref):
    rows = ids_ref.shape[0]
    taps = 4
    out_ref[...] = tokens_ref[...]
    place = lax.broadcasted_iota(jnp.int32, (halo, 1), 0)
    same = jnp.zeros((halo, 1), f32)
    for lag in range(taps):
        here = jnp.where(ids_ref[rows - 1 - lag] == ids_ref[rows - 1], 1.0, 0.0)
        same = same + jnp.where(place == halo - 1 - lag, here, 0.0)
    out_ref[...] = (tokens_ref[...].astype(f32) * same).astype(bf16)


def edge_rows_of(ids, tokens):
    rows, width = tokens.shape
    return pl.pallas_call(
        edge_kernel,
        grid=(1,),
        in_specs=[
            pl.BlockSpec(memory_space=pltpu.SMEM),
            pl.BlockSpec((halo, width), lambda j: (rows // halo - 1, 0)),
        ],
        out_specs=pl.BlockSpec((halo, width), lambda j: (0, 0)),
        out_shape=jax.ShapeDtypeStruct((halo, width), bf16),
        cost_estimate=tiny_cost,
        name="edge_rows",
    )(ids, tokens)


block_rows, used_rows = 16, 12


def small_kernel(place_ref, scan_ref, conv_ref, keep_ref, *rest):
    *sends_refs, rows, blocks = rest
    rows[...] = jnp.zeros(rows.shape, f32)
    rows[: scan_ref.shape[0], :] = scan_ref[...]
    rows[scan_ref.shape[0] : scan_ref.shape[0] + conv_ref.shape[0], :] = conv_ref[...]
    blocks[...] = jnp.zeros(blocks.shape, f32)
    for n in range(16):
        blocks[n * block_rows : n * block_rows + used_rows, :] = rows[
            n * used_rows : (n + 1) * used_rows, :
        ]
    quarter = keep_ref.shape[0]
    for n in range(4):
        start = pl.multiple_of((place_ref[0] ^ n) * quarter, quarter)
        block = blocks[pl.ds(start, quarter), :]
        if n == 0:
            keep_ref[...] = block
        else:
            sends_refs[n - 1][...] = block.astype(bf16)


def small_quarters(place, scan_small, conv_small):
    width = scan_small.shape[1]
    return pl.pallas_call(
        small_kernel,
        in_specs=[pl.BlockSpec(memory_space=pltpu.SMEM)]
        + [pl.BlockSpec(memory_space=pltpu.VMEM)] * 2,
        out_shape=[jax.ShapeDtypeStruct((4 * block_rows, width), f32)]
        + [jax.ShapeDtypeStruct((4 * block_rows, width), bf16)] * 3,
        scratch_shapes=[
            pltpu.VMEM((16 * used_rows, width), f32),
            pltpu.VMEM((16 * block_rows, width), f32),
        ],
        cost_estimate=tiny_cost,
        name="small_quarters",
    )(place, scan_small, conv_small)


def quarter_kernel(
    place_ref,
    own_ref,
    near_ref,
    far_ref,
    last_ref,
    normed_0,
    normed_1,
    normed_2,
    normed_3,
    small_ref,
    first_ref,
    second_ref,
    third_ref,
    *rest,
):
    keep_ref, *sends_refs, piece, small = rest[-6:]
    total = None
    grads = (own_ref, near_ref, far_ref, last_ref)
    for left, right in zip((normed_0, normed_1, normed_2, normed_3), grads):
        part = lax.dot_general(left[...], right[...], contract_first, preferred_element_type=f32)
        total = part if total is None else total + part
    piece[...] = total
    small[...] = small_ref[...] + sum(
        ref[...].astype(f32) for ref in (first_ref, second_ref, third_ref)
    )
    rows, spare = piece.shape[0] // 4, small.shape[0] // 4
    for n in range(4):
        block = place_ref[0] ^ n
        inner_rows = piece[pl.ds(pl.multiple_of(block * rows, rows), rows), :]
        small_rows = small[pl.ds(pl.multiple_of(block * spare, spare), spare), :]
        if n == 0:
            keep_ref[:rows, :] = inner_rows
            keep_ref[rows:, :] = small_rows
        else:
            sends_refs[n - 1][:rows, :] = inner_rows.astype(bf16)
            sends_refs[n - 1][rows:, :] = small_rows.astype(bf16)


def inner_quarter(place, own, near, far, last, normed, smalls, waits):
    width = own.shape[1]
    quarter = normed[0].shape[1]
    spare = smalls[0].shape[0]
    rows = (quarter + spare) // 4
    return pl.pallas_call(
        quarter_kernel,
        in_specs=[pl.BlockSpec(memory_space=pltpu.SMEM)]
        + [pl.BlockSpec(memory_space=pltpu.VMEM)] * 12
        + [pl.BlockSpec(memory_space=pl.ANY)] * len(waits),
        out_shape=[jax.ShapeDtypeStruct((rows, width), f32)]
        + [jax.ShapeDtypeStruct((rows, width), bf16)] * 3,
        scratch_shapes=[pltpu.VMEM((quarter, width), f32), pltpu.VMEM((spare, width), f32)],
        compiler_params=pltpu.CompilerParams(vmem_limit_bytes=vmem_bytes),
        cost_estimate=tiny_cost,
        name="inner_quarter",
    )(place, own, near, far, last, *normed, *smalls, *waits)


def join_kernel(place_ref, gate_ref, first_ref, second_ref, *rest, small_rows):
    at_end = 2 + len(small_rows) if small_rows else 0
    out_ref = rest[-1 - at_end]
    step = pl.program_id(0)
    rows = out_ref.shape[0] // 2
    out_ref[:, 1, :] = gate_ref[...].astype(f32)

    def put(ref):
        for n in range(2):
            at = n * (rows + block_rows)
            out_ref[n * rows : (n + 1) * rows, 0, :] = ref[at : at + rows, :].astype(f32)

    @pl.when(step < 2)
    def _():
        put(first_ref)

    @pl.when(step >= 2)
    def _():
        put(second_ref)

    if not small_rows:
        return
    *row_refs, gain_ref, blocks = rest[-at_end:]

    @pl.when(step == 3)
    def _():
        for flip, ref in enumerate(rest[:4]):
            for n in range(4):
                at = ((place_ref[0] ^ flip) * 4 + n) * block_rows
                taken = ref[(n + 1) * rows + n * block_rows : (n + 1) * (rows + block_rows), :]
                blocks[pl.ds(pl.multiple_of(at, block_rows), block_rows), :] = taken.astype(f32)
        for ref, start in zip(row_refs, small_rows):
            for row in range(ref.shape[0]):
                at = (start + row) // used_rows * block_rows + (start + row) % used_rows
                ref[row : row + 1, :] = blocks[at : at + 1, :]
        gain_ref[...] = sum(
            blocks[n * block_rows + used_rows : n * block_rows + used_rows + 1, :] for n in range(16)
        )


def joined(place, flip, gate, first, second, before, waits, held=(), small_rows=(), small_counts=()):
    depth, width = gate.shape
    quarter = depth // 4
    block = quarter // 2
    piece = first.shape[0] // 2

    def target(j, place):
        return 2 * (place[0] ^ (flip + j // 2)) + lax.rem(j, 2)

    vmem = pl.BlockSpec(memory_space=pltpu.VMEM)
    untouched = [*before, *waits]
    return pl.pallas_call(
        functools.partial(join_kernel, small_rows=small_rows),
        grid_spec=pltpu.PrefetchScalarGridSpec(
            num_scalar_prefetch=1,
            grid=(4,),
            in_specs=[
                pl.BlockSpec((block, width), lambda j, place: (target(j, place), 0)),
                pl.BlockSpec((piece, width), lambda j, place: (jnp.minimum(j, 1), 0)),
                pl.BlockSpec((piece, width), lambda j, place: (jnp.maximum(j - 2, 0), 0)),
            ]
            + [vmem] * len(held)
            + [pl.BlockSpec(memory_space=pl.ANY)] * len(untouched),
            out_specs=[pl.BlockSpec((block, 2, width), lambda j, place: (target(j, place), 0, 0))]
            + [pl.BlockSpec((rows, width), lambda j, place: (0, 0)) for rows in small_counts],
            scratch_shapes=[pltpu.VMEM((16 * block_rows, width), f32)] if small_rows else [],
        ),
        out_shape=[jax.ShapeDtypeStruct((depth, 2, width), f32)]
        + [jax.ShapeDtypeStruct((rows, width), f32) for rows in small_counts],
        input_output_aliases={4 + len(held) + k: k for k in range(len(before))},
        compiler_params=pltpu.CompilerParams(vmem_limit_bytes=vmem_bytes),
        cost_estimate=tiny_cost,
        name="joined",
    )(place, gate, first, second, *held, *untouched)


def early_kernel(place_ref, own_ref, near_ref, far_ref, last_ref, out_ref, gate_ref):
    rows = own_ref.shape[0]
    for flip, ref in enumerate((own_ref, far_ref, near_ref, last_ref)):
        place = place_ref[0] ^ flip
        at = pl.ds(pl.multiple_of((place & 1) * rows, rows), rows)

        @pl.when(place < 2)
        def _():
            out_ref[at, :] = ref[...].astype(f32)

        @pl.when(place >= 2)
        def _():
            gate_ref[at, :] = ref[...]


def early_joined(place, own, near, far, last):
    rows, width = own.shape
    return pl.pallas_call(
        early_kernel,
        in_specs=[pl.BlockSpec(memory_space=pltpu.SMEM)]
        + [pl.BlockSpec(memory_space=pltpu.VMEM)] * 4,
        out_shape=[
            jax.ShapeDtypeStruct((2 * rows, width), f32),
            jax.ShapeDtypeStruct((2 * rows, width), bf16),
        ],
        compiler_params=pltpu.CompilerParams(vmem_limit_bytes=vmem_bytes),
        cost_estimate=tiny_cost,
        name="early_joined",
    )(place, own, near, far, last)


def through(decay, total):
    return jnp.exp(decay * total)


def round_kernel(second_ref, decay_log_ref, own_ref, other_ref, passed_ref, new_passed_ref, *ends_refs):
    count = decay_log_ref.shape[0]
    decay = -jnp.exp(decay_log_ref[...])
    second = second_ref[0] > 0

    def split(ref):
        return ref[:count], ref[count : 2 * count], ref[2 * count : 2 * count + 1]

    own, other = split(own_ref), split(other_ref)
    early = [jnp.where(second, b, a) for a, b in zip(own, other)]
    late = [jnp.where(second, a, b) for a, b in zip(own, other)]
    state = late[0] + through(decay, late[2]) * early[0]
    adjoint = early[1] + through(decay, early[2]) * late[1]
    if len(ends_refs) == 2:
        ends_refs[0][...] = state
        ends_refs[1][...] = adjoint
    else:
        ends_refs[0][:count, :] = state
        ends_refs[0][count : 2 * count, :] = adjoint
        ends_refs[0][2 * count :, :] = jnp.broadcast_to(early[2] + late[2], (8, decay.shape[1]))
    before, after = passed_ref[:count], passed_ref[count : 2 * count]
    before_steps = passed_ref[2 * count : 2 * count + 1]
    after_steps = passed_ref[2 * count + 1 : 2 * count + 2]
    new_passed_ref[:count, :] = before + jnp.where(second, through(decay, before_steps) * other[0], 0.0)
    new_passed_ref[count : 2 * count, :] = after + jnp.where(
        second, 0.0, through(decay, after_steps) * other[1]
    )
    new_passed_ref[2 * count : 2 * count + 1, :] = before_steps + jnp.where(second, other[2], 0.0)
    new_passed_ref[2 * count + 1 : 2 * count + 2, :] = after_steps + jnp.where(second, 0.0, other[2])


def carried(ends, decay_log):
    count, width = decay_log.shape
    place = lax.axis_index("wide").astype(jnp.int32)
    passed = jnp.zeros((2 * count + 8, width), f32)
    packed = ends
    vmem = pl.BlockSpec(memory_space=pltpu.VMEM)
    for k, kinds in enumerate(([ends], [decay_log, decay_log])):
        passed, *out = pl.pallas_call(
            round_kernel,
            in_specs=[pl.BlockSpec(memory_space=pltpu.SMEM)] + [vmem] * 4,
            out_shape=[jax.ShapeDtypeStruct(kind.shape, f32) for kind in [passed] + kinds],
            cost_estimate=tiny_cost,
            name="carry_round",
        )((place >> k & 1)[None], decay_log, packed, swapped(packed, "wide", 2**k), passed)
        packed = out[0]
    from_before = passed_along(out[0], "wide", 4)
    from_after = passed_along(out[1], "wide", -4)
    return passed, from_before, from_after


def local(
    tokens,
    norm_gain,
    in_weight,
    conv_weight,
    conv_bias,
    select_weight,
    step_weight,
    step_bias,
    decay_log,
    skip_gain,
    out_weight,
    segment_ids,
    cotangent,
):
    rows, features = tokens.shape
    taps = conv_weight.shape[0]
    columns = select_weight.shape[0]
    rank = step_weight.shape[0]
    count = decay_log.shape[0]
    right_half = lax.axis_index("narrow") == 1

    def both_halves(own, other):
        return jnp.concatenate(
            [jnp.where(right_half, other, own), jnp.where(right_half, own, other)], axis=1
        )

    other_tokens = swapped(tokens, "narrow", 1)
    other_cot = swapped(cotangent, "narrow", 1)
    edge, other_edge = to_next_both(edge_rows_of(segment_ids, tokens))

    whole_low, normed_ext, normed, inverse, masks = normalized(
        tokens, other_tokens, edge, other_edge, norm_gain[None], segment_ids[None]
    )
    projected = jnp.einsum(
        "td,dce->cte", normed_ext, in_weight, preferred_element_type=f32
    ).astype(bf16)
    convolved, act, selected = convolve(
        projected, conv_weight, conv_bias[None], select_weight, masks
    )
    other_selected = swapped(selected, "narrow", 1)
    cot_whole = both_halves(cotangent, other_cot)
    gated_grad = lax.dot_general(
        cot_whole, out_weight, contract_last, preferred_element_type=f32
    )
    step_pre, step, ends = scan_ends(
        selected,
        other_selected,
        step_weight,
        step_bias[None],
        act,
        projected,
        gated_grad,
        masks,
        decay_log,
    )
    passed, entering, returning = carried(ends, decay_log)
    gated, gate_grad, entry = scan_forward(
        selected,
        other_selected,
        step,
        act,
        projected,
        gated_grad,
        masks,
        decay_log,
        passed,
        entering,
        skip_gain[None],
    )
    wide_place = lax.axis_index("wide").astype(jnp.int32)
    four_place = (wide_place & 3)[None]
    first_bits, *more_bits = group_bits(2)
    low_bit, high_bit = first_bits
    whole = whole_low.astype(f32)

    def narrow_halves(array):
        low, high = array[:, :features], array[:, features:]
        return jnp.where(right_half, high, low), jnp.where(right_half, low, high)

    def times(left, right):
        return lax.dot_general(left, right, contract_first, preferred_element_type=f32)

    gated_mine, gated_other = halves_of(gated, 1)
    normed_mine, normed_other = halves_of(normed, 1)
    early = jnp.concatenate([times(gated_other, cot_whole), times(normed_other, gate_grad)])
    arrived = swapped(early.astype(bf16), "wide", 1)
    early = jnp.concatenate([times(gated_mine, cot_whole), times(normed_mine, gate_grad)])
    normed_four = quarter_of_four(normed)
    early, send = folded(early, after(arrived, returning, *normed_four), 2)
    arrived = swapped(send, "wide", 2)
    out_part = jnp.dot(gated, out_weight, preferred_element_type=f32)
    out_mine, out_other = narrow_halves(out_part)
    out_theirs = swapped(out_other, "narrow", 1)
    act_grad, select_grad, scan_small = scan_backward(
        selected,
        other_selected,
        step_pre,
        step,
        act,
        projected,
        gated_grad,
        masks,
        decay_log,
        entry,
        passed,
        returning,
        skip_gain[None],
        step_weight,
        send,
    )
    layer_out = (tokens.astype(f32) + (out_mine + out_theirs)).astype(bf16)
    other_select_grad = swapped(select_grad, "narrow", 1)
    early, send = folded(early, after(arrived, select_grad), low_bit)
    arrived = swapped(send, "wide", low_bit)
    inner_main, before, last, conv_small = convolve_grad(
        select_grad,
        other_select_grad,
        select_weight,
        act_grad,
        convolved,
        act,
        projected,
        conv_weight,
        masks,
        [out_theirs, send],
    )
    inner_grad = patched(segment_ids, inner_main, last, passed_along(before, "wide", -1))
    near = swapped(inner_grad, "wide", 2)
    far = swapped(inner_grad, "wide", 1)
    keep, *sends = small_quarters(four_place, scan_small, conv_small)
    smalls = [keep] + [swapped(sends[n - 1], "wide", n) for n in (1, 2, 3)]
    early, send = folded(early, after(arrived, inner_grad, *sends), high_bit)
    arrived = swapped(send, "wide", high_bit)
    normed_part = jnp.einsum(
        "cte,dce->td", jnp.stack([inner_grad, gate_grad]), in_weight, preferred_element_type=f32
    )
    gain_part = jnp.sum(normed_part * whole * inverse, axis=0, keepdims=True)
    row_part = jnp.sum(normed_part * norm_gain * whole, axis=1)[None]
    gain_sum = gain_part + swapped(gain_part, "narrow", 1)
    for bit in (bit for bits in more_bits for bit in bits):
        gain_sum = gain_sum + swapped(gain_sum, "wide", bit)
    normed_mine, normed_other = narrow_halves(normed_part)
    row_theirs = swapped(row_part, "narrow", 1)
    normed_theirs = swapped(normed_other, "narrow", 1)
    near = after(near, send, gain_part, *smalls[1:])
    last = swapped(near, "wide", 1)
    early = early + after(arrived, near).astype(f32)
    for bits in more_bits:
        early = scattered(early, bits)
    early = early.astype(bf16)
    keep, *sends = inner_quarter(
        (wide_place >> 2 & 3)[None],
        inner_grad,
        near,
        far,
        last,
        normed_four,
        smalls,
        [row_theirs, early],
    )
    for bits in reversed(more_bits):
        early = gathered(early, bits)
    early = unfolded(early, after(swapped(early, "wide", high_bit), keep), high_bit)
    row_sum = (row_part + row_theirs).reshape(rows, 1)
    gain_mine = jnp.where(right_half, norm_gain[features:], norm_gain[:features])
    whole_grad = inverse * (gain_mine * (normed_mine + normed_theirs)) - tokens.astype(f32) * (
        inverse * inverse * inverse
    ) * (row_sum / (2 * features))
    tokens_grad = (whole_grad + cotangent.astype(f32)).astype(bf16)
    arrived = [swapped(sends[n - 1], "wide", flips(first_bits)[n]) for n in (1, 2, 3)]
    arrived[0] = after(arrived[0], early)
    held = keep + sum(a.astype(f32) for a in arrived)
    for bits in more_bits:
        held = scattered(held, bits)
    held = held.astype(bf16)
    for bits in reversed(more_bits):
        held = gathered(held, bits)
    spare = jnp.broadcast_to(gain_sum, (block_rows - used_rows, gain_sum.shape[1]))
    held = jnp.concatenate([held[: held.shape[0] - spare.shape[0]], spare.astype(bf16)])
    early = unfolded(early, after(swapped(early, "wide", low_bit), held), low_bit)
    early_near = swapped(early, "wide", 2)
    early_far = swapped(early, "wide", 1)
    held = gathered(held, first_bits, early)
    core = swapped(held, "wide", 1)
    out_weight_grad, gate_sum = early_joined(
        four_place, early, early_near, early_far, swapped(early_near, "wide", 1)
    )
    (begun,) = joined(four_place, 0, gate_sum, held, core, (), ())
    near = after(swapped(held, "wide", 2), begun)
    far = swapped(near, "wide", 1)
    conv_at = rank + count + 2
    (
        in_weight_grad,
        step_weight_grad,
        decay_log_grad,
        skip_gain_grad,
        step_bias_grad,
        select_weight_grad,
        conv_weight_grad,
        conv_bias_grad,
        norm_gain_grad,
    ) = joined(
        four_place,
        2,
        gate_sum,
        near,
        far,
        (begun,),
        (),
        (held, core, near, far),
        (0, rank, rank + count, rank + count + 1, conv_at, conv_at + columns, conv_at + columns + taps),
        (rank, count, 1, 1, columns, taps, 1, 1),
    )
    return (
        layer_out,
        tokens_grad,
        norm_gain_grad[0],
        in_weight_grad,
        conv_weight_grad,
        conv_bias_grad[0],
        select_weight_grad,
        step_weight_grad,
        step_bias_grad[0],
        decay_log_grad,
        skip_gain_grad[0],
        out_weight_grad,
    )


def solution(mesh):
    placed = (
        P("wide", "narrow"),
        P(),
        P(None, None, "narrow"),
        P(None, "narrow"),
        P("narrow"),
        P(None, "narrow"),
        P(None, "narrow"),
        P("narrow"),
        P(None, "narrow"),
        P("narrow"),
        P("narrow", None),
        P("wide"),
        P("wide", "narrow"),
    )
    return jax.shard_map(
        local,
        mesh=mesh,
        in_specs=placed,
        out_specs=(
            P("wide", "narrow"),
            P("wide", "narrow"),
            P(),
            P(None, None, "narrow"),
            P(None, "narrow"),
            P("narrow"),
            P(None, "narrow"),
            P(None, "narrow"),
            P("narrow"),
            P(None, "narrow"),
            P("narrow"),
            P("narrow", None),
        ),
        check_vma=False,
    )
```

```python
import functools

import jax
import jax.numpy as jnp
from jax import lax
from jax.experimental import pallas as pl
from jax.experimental.pallas import tpu as pltpu
from jax.sharding import PartitionSpec as P

epsilon = 1e-05
log2e = 1.4426950408889634
reset_step = 1e30
lanes = 128
halo = 16
body_rows = 32
scan_width = 512
vmem_bytes = 56 * 1024 * 1024
tiny_cost = pl.CostEstimate(flops=1, bytes_accessed=1, transcendentals=0)
f32 = jnp.float32
bf16 = jnp.bfloat16
contract_first = (((0,), (0,)), ((), ()))
contract_last = (((1,), (1,)), ((), ()))


def passed_along(array, axis, by):
    peers = lax.axis_size(axis)
    pairs = [(i, i + by) for i in range(peers) if 0 <= i + by < peers]
    return lax.ppermute(array, axis, pairs)


def swapped(array, axis, bit):
    peers = lax.axis_size(axis)
    return lax.ppermute(array, axis, [(i, i ^ bit) for i in range(peers)])


def wide_bits():
    bit, bits = 1, []
    while bit < lax.axis_size("wide"):
        bits.append(bit)
        bit *= 2
    return bits


def to_next_both(array):
    count, sides = lax.axis_size("wide"), lax.axis_size("narrow")
    pairs = [
        (i * sides + k, (i + 1) * sides + (sides - 1 - k))
        for i in range(count - 1)
        for k in range(sides)
    ]
    return passed_along(array, "wide", 1), lax.ppermute(array, ("wide", "narrow"), pairs)


def is_upper(bit):
    return (lax.axis_index("wide") & bit) != 0


def group_bits(size):
    bits, bit = [], 4
    while bit < lax.axis_size("wide"):
        bits.append(bit)
        bit *= 2
    return [tuple(bits[k : k + size]) for k in range(0, len(bits), size)]


def flips(bits):
    return [sum(b for k, b in enumerate(bits) if n >> k & 1) for n in range(2 ** len(bits))]


def scattered(piece, bits):
    rows = piece.shape[0] // 2 ** len(bits)
    here = sum(is_upper(b).astype(jnp.int32) << k for k, b in enumerate(bits))

    def block(n):
        return lax.dynamic_slice_in_dim(piece, (here ^ n) * rows, rows, 0)

    total = block(0).astype(f32)
    for n, flip in enumerate(flips(bits)):
        if n > 0:
            total = total + swapped(block(n).astype(bf16), "wide", flip).astype(f32)
    return total


def gathered(held, bits, *waits):
    blocks = [held] + [swapped(held, "wide", flip) for flip in flips(bits)[1:]]
    if waits:
        blocks[1] = after(blocks[1], *waits)
    for bit in bits:
        upper = is_upper(bit)
        blocks = [
            jnp.concatenate([jnp.where(upper, b, a), jnp.where(upper, a, b)])
            for a, b in zip(blocks[0::2], blocks[1::2])
        ]
    return blocks[0]


def early_bits():
    bits, bit = [], 2
    while bit < lax.axis_size("wide"):
        bits.append(bit)
        bit *= 2
    return list(zip(bits, bits[1:] + bits[:1]))


def early_upper(bits):
    place = lax.axis_index("wide")
    return jnp.where(place & 1 == 0, place & bits[0] != 0, place & bits[1] != 0).astype(jnp.int32)[None]


def early_swapped(array, bits):
    peers = lax.axis_size("wide")
    return lax.ppermute(array, "wide", [(i, i ^ bits[i % 2]) for i in range(peers)])


def quarter_of_four(array):
    width = array.shape[1] // 4
    here = lax.axis_index("wide") & 3

    def quarter(n):
        return lax.dynamic_slice_in_dim(array, (here ^ n) * width, width, 1)

    return [quarter(0)] + [swapped(quarter(n), "wide", n) for n in (2, 1, 3)]


def silu_slope(values):
    logistic = jax.nn.sigmoid(values)
    return logistic * (1.0 + values * (1.0 - logistic))


def softplus(values):
    return jnp.maximum(values, 0.0) + jnp.log1p(jnp.exp(-jnp.abs(values)))


def column_spec(rows, start=0):
    return pl.BlockSpec((rows, scan_width), lambda j: (0, start + j))


def part_spec(part, rows, start=0):
    return pl.BlockSpec((None, rows, scan_width), lambda j: (part, 0, start + j))


def whole_spec(rows, width):
    return pl.BlockSpec((rows, width), lambda j: (0, 0))


def call(kernel, name, width, in_specs, out_specs, out_shape, scratch, *operands):
    return pl.pallas_call(
        kernel,
        grid=(width // scan_width,),
        in_specs=in_specs,
        out_specs=out_specs,
        out_shape=out_shape,
        scratch_shapes=scratch,
        compiler_params=pltpu.CompilerParams(vmem_limit_bytes=vmem_bytes),
        cost_estimate=tiny_cost,
        name=name,
    )(*operands)


def conv_kernel(
    inner_ref,
    conv_weight_ref,
    conv_bias_ref,
    select_ref,
    mask_ref,
    convolved_ref,
    act_ref,
    selected_ref,
    inner,
):
    rows = act_ref.shape[0]
    taps = conv_weight_ref.shape[0]
    inner[:halo, :] = inner_ref[rows:, :].astype(f32)
    inner[halo:, :] = inner_ref[:rows, :].astype(f32)
    total = conv_bias_ref[...] + conv_weight_ref[taps - 1 :, :] * inner[halo:, :]
    for lag in range(1, taps):
        earlier = inner[pl.ds(halo - lag, rows), :] * mask_ref[:, lag : lag + 1]
        total = total + conv_weight_ref[taps - 1 - lag : taps - lag, :] * earlier
    convolved_ref[...] = total
    act = (total * jax.nn.sigmoid(total)).astype(bf16)
    act_ref[...] = act
    part = lax.dot_general(select_ref[...], act, contract_last, preferred_element_type=f32)

    @pl.when(pl.program_id(0) == 0)
    def _():
        selected_ref[...] = part

    @pl.when(pl.program_id(0) > 0)
    def _():
        selected_ref[...] += part


def convolve(projected, conv_weight, conv_bias, select_weight, masks):
    parts, extended, width = projected.shape
    rows = extended - halo
    taps = conv_weight.shape[0]
    columns = select_weight.shape[0]
    return call(
        conv_kernel,
        "convolve",
        width,
        [
            part_spec(0, extended),
            column_spec(taps),
            column_spec(1),
            column_spec(columns),
            whole_spec(rows, masks.shape[1]),
        ],
        [column_spec(rows), column_spec(rows), whole_spec(columns, rows)],
        [
            jax.ShapeDtypeStruct((rows, width), f32),
            jax.ShapeDtypeStruct((rows, width), bf16),
            jax.ShapeDtypeStruct((columns, rows), f32),
        ],
        [pltpu.VMEM((extended, scan_width), f32)],
        projected,
        conv_weight,
        conv_bias,
        select_weight,
        masks,
    )


def coef_columns(coef, block):
    per_tile = lanes // body_rows
    start = pl.multiple_of((block // per_tile) * lanes, lanes)
    tile = coef[:, pl.ds(start, lanes)]
    back = body_rows * lax.rem(block, per_tile)
    return pltpu.roll(tile, lax.rem(lanes - back, lanes), 1)


def ends_kernel(
    selected_ref,
    other_ref,
    step_weight_ref,
    step_bias_ref,
    act_ref,
    gate_ref,
    gated_grad_ref,
    mask_ref,
    decay_log_ref,
    step_pre_ref,
    step_ref,
    ends_ref,
    coef,
    held_step,
    drive,
    scan_grad,
):
    rows = act_ref.shape[0]
    count = decay_log_ref.shape[0]
    rank = step_weight_ref.shape[0]
    decay2 = -jnp.exp(decay_log_ref[...]) * log2e
    selected = selected_ref[...] + other_ref[...]
    coef[...] = selected[rank:, :]
    step_low = selected[:rank, :].astype(bf16)
    step_pre = step_bias_ref[...] + lax.dot_general(
        step_low, step_weight_ref[...], contract_first, preferred_element_type=f32
    )
    step_pre_ref[...] = step_pre
    step = softplus(step_pre)
    step_ref[...] = step
    held_step[...] = jnp.where(mask_ref[:, 1:2] > 0.0, step, reset_step)
    drive[...] = step * act_ref[...].astype(f32)
    gate = gate_ref[...].astype(f32)
    scan_grad[...] = gated_grad_ref[...] * (gate * jax.nn.sigmoid(gate))
    zero = jnp.zeros(decay2.shape, f32)

    def body(block, carried):
        state, product, adjoint = carried
        columns = coef_columns(coef, block)
        for i in range(body_rows):
            row = pl.ds(block * body_rows + i, 1)
            factor = jnp.exp2(held_step[row, :] * decay2)
            state = factor * state + columns[:count, i : i + 1] * drive[row, :]
            product = factor * product
            adjoint = adjoint + product * (columns[count:, i : i + 1] * scan_grad[row, :])
        return state, product, adjoint

    state, product, adjoint = lax.fori_loop(0, rows // body_rows, body, (zero, zero + 1.0, zero))
    ends_ref[:count, :] = state
    ends_ref[count : 2 * count, :] = adjoint
    total = jnp.sum(held_step[...], axis=0, keepdims=True)
    ends_ref[2 * count :, :] = jnp.broadcast_to(total, (8, total.shape[1]))


def scan_ends(
    selected, other, step_weight, step_bias, act, projected, gated_grad, masks, decay_log
):
    rows, width = act.shape
    count = decay_log.shape[0]
    columns = selected.shape[0]
    rank = step_weight.shape[0]
    return call(
        ends_kernel,
        "scan_ends",
        width,
        [
            whole_spec(columns, rows),
            whole_spec(columns, rows),
            column_spec(rank),
            column_spec(1),
            column_spec(rows),
            part_spec(1, rows),
            column_spec(rows),
            whole_spec(rows, masks.shape[1]),
            column_spec(count),
        ],
        [column_spec(rows), column_spec(rows), column_spec(2 * count + 8)],
        [
            jax.ShapeDtypeStruct((rows, width), f32),
            jax.ShapeDtypeStruct((rows, width), f32),
            jax.ShapeDtypeStruct((2 * count + 8, width), f32),
        ],
        [pltpu.VMEM((2 * count, rows), f32)] + [pltpu.VMEM((rows, scan_width), f32)] * 3,
        selected,
        other,
        step_weight,
        step_bias,
        act,
        projected,
        gated_grad,
        masks,
        decay_log,
    )


def lane_tiles(values):
    return [values[:, k : k + lanes] for k in range(0, values.shape[1], lanes)]


def tree_sum(parts):
    while len(parts) > 1:
        odd = parts[len(parts) // 2 * 2 :]
        parts = [a + b for a, b in zip(parts[0::2], parts[1::2])] + odd
    return parts[0]


def keep_halves(scratch, i, values):
    for k, tile in enumerate(lane_tiles(values)):
        at = (k * body_rows + i) * 8
        scratch[at : at + 8, :] = tile[:8] + tile[8:]


def put_state_sums(scratch, out_ref, block):
    for group in range(body_rows // 8):
        row = pl.ds(pl.multiple_of(block * body_rows + group * 8, 8), 8)
        for k in range(out_ref.shape[1] // lanes):
            at = (k * body_rows + group * 8) * 8
            total = tree_sum([scratch[pl.ds(at + n, 8, stride=8), :] for n in range(8)])
            out_ref[row, k * lanes : (k + 1) * lanes] = total


def lane_sums(values):
    ones = jnp.ones((8, lanes), bf16)
    high = values.astype(bf16)
    low = (values - high.astype(f32)).astype(bf16)
    total = lax.dot_general(ones, high, contract_last, preferred_element_type=f32)
    total += lax.dot_general(ones, low, contract_last, preferred_element_type=f32)
    return total[:1, :]


def at_token(t, count):
    return pl.ds(pl.multiple_of(t * count, count), count)


def forward_kernel(
    selected_ref,
    other_ref,
    step_ref,
    act_ref,
    gate_ref,
    gated_grad_ref,
    mask_ref,
    decay_log_ref,
    passed_ref,
    entering_ref,
    skip_ref,
    gated_ref,
    gate_grad_ref,
    entry_ref,
    coef,
    held_step,
    drive,
    scanned,
    halves,
):
    rows = step_ref.shape[0]
    count = decay_log_ref.shape[0]
    rank = selected_ref.shape[0] - 2 * count
    decay = -jnp.exp(decay_log_ref[...])
    decay2 = decay * log2e
    before_steps = passed_ref[2 * count : 2 * count + 1, :]
    entry = passed_ref[:count, :] + through(decay, before_steps) * entering_ref[...]
    entry_ref[...] = entry
    coef[...] = selected_ref[rank:, :] + other_ref[rank:, :]
    act = act_ref[...].astype(f32)
    held_step[...] = jnp.where(mask_ref[:, 1:2] > 0.0, step_ref[...], reset_step)
    drive[...] = step_ref[...] * act

    def forward(block, state):
        columns = coef_columns(coef, block)
        for i in range(body_rows):
            row = pl.ds(block * body_rows + i, 1)
            factor = jnp.exp2(held_step[row, :] * decay2)
            state = factor * state + columns[:count, i : i + 1] * drive[row, :]
            keep_halves(halves, i, columns[count:, i : i + 1] * state)
        put_state_sums(halves, scanned, block)
        return state

    lax.fori_loop(0, rows // body_rows, forward, entry)
    gate = gate_ref[...].astype(f32)
    logistic = jax.nn.sigmoid(gate)
    total = scanned[...] + skip_ref[...] * act
    gated_ref[...] = (total * (gate * logistic)).astype(bf16)
    slope = logistic * (1.0 + gate * (1.0 - logistic))
    gate_grad_ref[...] = (gated_grad_ref[...] * total * slope).astype(bf16)


def scan_forward(
    selected, other, step, act, projected, gated_grad, masks, decay_log, passed, entering, skip_gain
):
    rows, width = step.shape
    count = decay_log.shape[0]
    columns = selected.shape[0]
    return call(
        forward_kernel,
        "scan_forward",
        width,
        [
            whole_spec(columns, rows),
            whole_spec(columns, rows),
            column_spec(rows),
            column_spec(rows),
            part_spec(1, rows),
            column_spec(rows),
            whole_spec(rows, masks.shape[1]),
            column_spec(count),
            column_spec(2 * count + 8),
            column_spec(count),
            column_spec(1),
        ],
        [column_spec(rows), column_spec(rows), column_spec(count)],
        [
            jax.ShapeDtypeStruct((rows, width), bf16),
            jax.ShapeDtypeStruct((rows, width), bf16),
            jax.ShapeDtypeStruct((count, width), f32),
        ],
        [pltpu.VMEM((2 * count, rows), f32)]
        + [pltpu.VMEM((rows, scan_width), f32)] * 3
        + [pltpu.VMEM((8 * body_rows * (scan_width // lanes), lanes), f32)],
        selected,
        other,
        step,
        act,
        projected,
        gated_grad,
        masks,
        decay_log,
        passed,
        entering,
        skip_gain,
    )


def backward_kernel(
    selected_ref,
    other_ref,
    step_pre_ref,
    step_ref,
    act_ref,
    gate_ref,
    gated_grad_ref,
    mask_ref,
    decay_log_ref,
    entry_ref,
    passed_ref,
    returning_ref,
    skip_ref,
    step_weight_ref,
    first_wait,
    second_wait,
    act_grad_ref,
    select_grad_ref,
    small_ref,
    coef,
    held_step,
    drive,
    scan_grad,
    weighted,
    held_sum,
    states,
    factors,
    halves,
    more_halves,
    in_sum,
    read_sum,
):
    rows = step_ref.shape[0]
    count = decay_log_ref.shape[0]
    rank = step_weight_ref.shape[0]
    blocks = rows // body_rows
    decay = -jnp.exp(decay_log_ref[...])
    decay2 = decay * log2e
    after_steps = passed_ref[2 * count + 1 : 2 * count + 2, :]
    tail = passed_ref[count : 2 * count, :] + through(decay, after_steps) * returning_ref[...]
    selected = selected_ref[...] + other_ref[...]
    coef[...] = selected[rank:, :]
    step_low = selected[:rank, :].astype(bf16)
    step = step_ref[...]
    act = act_ref[...].astype(f32)
    held_step[...] = jnp.where(mask_ref[:, 1:2] > 0.0, step, reset_step)
    drive[...] = step * act
    gate = gate_ref[...].astype(f32)
    grads = gated_grad_ref[...] * (gate * jax.nn.sigmoid(gate))
    scan_grad[...] = grads
    small_ref[rank + count : rank + count + 1, :] = jnp.sum(grads * act, axis=0, keepdims=True)
    states[:count, :] = entry_ref[...]

    @pl.when(pl.program_id(0) == 0)
    def _():
        in_sum[...] = jnp.zeros(in_sum.shape, f32)
        read_sum[...] = jnp.zeros(read_sum.shape, f32)
        select_grad_ref[...] = jnp.zeros(select_grad_ref.shape, f32)

    def forward(block, state):
        columns = coef_columns(coef, block)
        for i in range(body_rows):
            t = block * body_rows + i
            row = pl.ds(t, 1)
            factor = jnp.exp2(held_step[row, :] * decay2)
            state = factor * state + columns[:count, i : i + 1] * drive[row, :]
            factors[at_token(t, count), :] = factor
            states[at_token(t + 1, count), :] = state
        return state

    lax.fori_loop(0, blocks, forward, entry_ref[...])

    def backward(k, carried):
        adjoint, decay_grad = carried
        block = blocks - 1 - k
        columns = coef_columns(coef, block)
        for i in range(body_rows - 1, -1, -1):
            t = block * body_rows + i
            row = pl.ds(t, 1)
            here = at_token(t, count)
            grad = scan_grad[row, :]
            summed = columns[count:, i : i + 1] * grad + adjoint
            read_sum[here, :] += tree_sum(lane_tiles(grad * states[at_token(t + 1, count), :]))
            in_sum[here, :] += tree_sum(lane_tiles(summed * drive[row, :]))
            keep_halves(halves, i, summed * columns[:count, i : i + 1])
            adjoint = factors[here, :] * summed
            held = adjoint * states[here, :]
            decay_grad = decay_grad + held * step_ref[row, :]
            keep_halves(more_halves, i, held * decay)
        put_state_sums(halves, weighted, block)
        put_state_sums(more_halves, held_sum, block)
        return adjoint, decay_grad

    ignored, decay_grad = lax.fori_loop(
        0, blocks, backward, (tail, jnp.zeros(decay.shape, f32))
    )
    act_grad_ref[...] = step * weighted[...] + skip_ref[...] * scan_grad[...]
    step_grad = act * weighted[...] + held_sum[...]
    pre_grad = (step_grad * jax.nn.sigmoid(step_pre_ref[...])).astype(bf16)
    small_ref[:rank, :] = jnp.dot(step_low, pre_grad, preferred_element_type=f32)
    small_ref[rank : rank + count, :] = decay_grad * decay
    bias_grad = jnp.sum(pre_grad.astype(f32), axis=0, keepdims=True)
    small_ref[rank + count + 1 : rank + count + 2, :] = bias_grad
    select_grad_ref[:rank, :] += lax.dot_general(
        step_weight_ref[...], pre_grad, contract_last, preferred_element_type=f32
    )

    @pl.when(pl.program_id(0) == pl.num_programs(0) - 1)
    def _():
        for n in range(count):
            at = pl.ds(n, rows, stride=count)
            select_grad_ref[rank + n : rank + n + 1, :] = lane_sums(in_sum[at, :])
            select_grad_ref[rank + count + n : rank + count + n + 1, :] = lane_sums(read_sum[at, :])


def scan_backward(
    selected,
    other,
    step_pre,
    step,
    act,
    projected,
    gated_grad,
    masks,
    decay_log,
    entry,
    passed,
    returning,
    skip_gain,
    step_weight,
    waits,
):
    rows, width = step.shape
    count = decay_log.shape[0]
    columns = selected.shape[0]
    rank = step_weight.shape[0]
    half_rows = 8 * body_rows * (scan_width // lanes)
    small = rank + count + 2
    return call(
        backward_kernel,
        "scan_backward",
        width,
        [
            whole_spec(columns, rows),
            whole_spec(columns, rows),
            column_spec(rows),
            column_spec(rows),
            column_spec(rows),
            part_spec(1, rows),
            column_spec(rows),
            whole_spec(rows, masks.shape[1]),
            column_spec(count),
            column_spec(count),
            column_spec(2 * count + 8),
            column_spec(count),
            column_spec(1),
            column_spec(rank),
        ]
        + [pl.BlockSpec(memory_space=pl.ANY)] * 2,
        [column_spec(rows), whole_spec(columns, rows), column_spec(small)],
        [
            jax.ShapeDtypeStruct((rows, width), f32),
            jax.ShapeDtypeStruct((columns, rows), f32),
            jax.ShapeDtypeStruct((small, width), f32),
        ],
        [pltpu.VMEM((2 * count, rows), f32)]
        + [pltpu.VMEM((rows, scan_width), f32)] * 5
        + [
            pltpu.VMEM(((rows + 1) * count, scan_width), f32),
            pltpu.VMEM((rows * count, scan_width), f32),
            pltpu.VMEM((half_rows, lanes), f32),
            pltpu.VMEM((half_rows, lanes), f32),
            pltpu.VMEM((rows * count, lanes), f32),
            pltpu.VMEM((rows * count, lanes), f32),
        ],
        selected,
        other,
        step_pre,
        step,
        act,
        projected,
        gated_grad,
        masks,
        decay_log,
        entry,
        passed,
        returning,
        skip_gain,
        step_weight,
        *waits,
    )


def conv_grad_kernel(
    select_grad_ref,
    other_ref,
    select_ref,
    act_grad_ref,
    convolved_ref,
    act_ref,
    inner_ref,
    conv_weight_ref,
    mask_ref,
    *rest,
):
    inner_grad_ref, before_ref, last_ref, small_ref, inner, shifted = rest[-6:]
    rows = act_ref.shape[0]
    taps = conv_weight_ref.shape[0]
    columns = select_ref.shape[0]
    select_grad = (select_grad_ref[...] + other_ref[...]).astype(bf16)
    total = act_grad_ref[...] + lax.dot_general(
        select_grad, select_ref[...], contract_first, preferred_element_type=f32
    )
    conv_grad = total * silu_slope(convolved_ref[...])
    small_ref[:columns, :] = jnp.dot(select_grad, act_ref[...], preferred_element_type=f32)
    inner[:halo, :] = inner_ref[rows:, :].astype(f32)
    inner[halo:, :] = inner_ref[:rows, :].astype(f32)
    edges = jnp.zeros((8, conv_grad.shape[1]), f32)
    shifted[:8, :] = edges
    shifted[rows + 8 :, :] = edges
    out = conv_weight_ref[taps - 1 :, :] * conv_grad
    before = edges
    small_ref[columns + taps - 1 : columns + taps, :] = jnp.sum(
        conv_grad * inner[halo:, :], axis=0, keepdims=True
    )
    for lag in range(1, taps):
        masked = conv_grad * mask_ref[:, lag : lag + 1]
        at = taps - 1 - lag
        small_ref[columns + at : columns + at + 1, :] = jnp.sum(
            masked * inner[pl.ds(halo - lag, rows), :], axis=0, keepdims=True
        )
        shifted[8 : rows + 8, :] = masked
        weight = conv_weight_ref[at : at + 1, :]
        out = out + weight * shifted[pl.ds(8 + lag, rows), :]
        before = before + weight * shifted[pl.ds(lag, 8), :]
    small_ref[columns + taps : columns + taps + 1, :] = jnp.sum(conv_grad, axis=0, keepdims=True)
    inner_grad_ref[...] = out.astype(bf16)
    before_ref[...] = before
    last_ref[...] = out[rows - 8 :, :]


def convolve_grad(
    select_grad, other, select_weight, act_grad, convolved, act, projected, conv_weight, masks, waits
):
    rows, width = act.shape
    extended = rows + halo
    columns = select_weight.shape[0]
    taps = conv_weight.shape[0]
    small = columns + taps + 1
    return call(
        conv_grad_kernel,
        "convolve_grad",
        width,
        [
            whole_spec(columns, rows),
            whole_spec(columns, rows),
            column_spec(columns),
            column_spec(rows),
            column_spec(rows),
            column_spec(rows),
            part_spec(0, extended),
            column_spec(taps),
            whole_spec(rows, masks.shape[1]),
        ]
        + [pl.BlockSpec(memory_space=pl.ANY)] * len(waits),
        [column_spec(rows), column_spec(8), column_spec(8), column_spec(small)],
        [
            jax.ShapeDtypeStruct((rows, width), bf16),
            jax.ShapeDtypeStruct((8, width), f32),
            jax.ShapeDtypeStruct((8, width), f32),
            jax.ShapeDtypeStruct((small, width), f32),
        ],
        [pltpu.VMEM((extended, scan_width), f32), pltpu.VMEM((rows + 16, scan_width), f32)],
        select_grad,
        other,
        select_weight,
        act_grad,
        convolved,
        act,
        projected,
        conv_weight,
        masks,
        *waits,
    )


def normalize_kernel(
    own_ref,
    other_ref,
    edge_ref,
    other_edge_ref,
    gain_ref,
    ids_ref,
    whole_ref,
    extended_ref,
    normed_ref,
    inverse_ref,
    mask_ref,
    rows_ref,
):
    rows, half = own_ref.shape
    ids = ids_ref[...].astype(f32)
    place = lax.broadcasted_iota(jnp.int32, ids.shape, 1)
    same = []
    for lag in range(8):
        earlier = jnp.where(place < lag, ids[:, :1], pltpu.roll(ids, lag, 1)) if lag else ids
        same.append(jnp.where(earlier == ids, 1.0, 0.0))
    spare = jnp.zeros((lanes - 8, rows), f32)
    mask_ref[...] = jnp.concatenate(same + [spare]).T
    right = lax.axis_index("narrow") == 1
    for at, own, other in ((0, own_ref, other_ref), (rows, edge_ref, other_edge_ref)):
        end = at + own.shape[0]
        rows_ref[at:end, :half] = jnp.where(right, other[...], own[...])
        rows_ref[at:end, half:] = jnp.where(right, own[...], other[...])
    whole_ref[...] = rows_ref[:rows, :]
    whole = rows_ref[...].astype(f32)
    inverse = lax.rsqrt(jnp.mean(whole * whole, axis=1, keepdims=True) + epsilon)
    normed = (whole * inverse * gain_ref[...]).astype(bf16)
    extended_ref[...] = normed
    normed_ref[...] = normed[:rows]
    inverse_ref[...] = inverse[:rows]


def normalized(own, other, edge, other_edge, gain, ids):
    rows, half = own.shape
    extended = rows + edge.shape[0]
    return pl.pallas_call(
        normalize_kernel,
        out_shape=[
            jax.ShapeDtypeStruct((rows, 2 * half), bf16),
            jax.ShapeDtypeStruct((extended, 2 * half), bf16),
            jax.ShapeDtypeStruct((rows, 2 * half), bf16),
            jax.ShapeDtypeStruct((rows, 1), f32),
            jax.ShapeDtypeStruct((rows, lanes), f32),
        ],
        scratch_shapes=[pltpu.VMEM((extended, 2 * half), bf16)],
        cost_estimate=tiny_cost,
        name="normalized",
    )(own, other, edge, other_edge, gain, ids)


def after(array, *waits):
    anywhere = pl.BlockSpec(memory_space=pl.ANY)
    return pl.pallas_call(
        lambda *refs: None,
        in_specs=[anywhere] * (1 + len(waits)),
        out_specs=anywhere,
        out_shape=jax.ShapeDtypeStruct(array.shape, array.dtype),
        input_output_aliases={0: 0},
        cost_estimate=tiny_cost,
        name="after",
    )(array, *waits)


def patch_kernel(ids_ref, rows_ref, last_ref, next_ref, *rest):
    count = ids_ref.shape[0]
    place = lax.broadcasted_iota(jnp.int32, (8, 1), 0)
    same = jnp.zeros((8, 1), f32)
    for lag in range(8):
        here = jnp.where(ids_ref[count - 1 - lag] == ids_ref[count - 1], 1.0, 0.0)
        same = same + jnp.where(place == 7 - lag, here, 0.0)
    total = last_ref[...] + next_ref[...] * same
    rows = rows_ref[...].astype(f32)
    rest[-1][...] = jnp.concatenate([rows[: halo - 8], total]).astype(bf16)


def patched(ids, grads, last, following, *waits):
    rows, width = grads.shape
    block = pl.BlockSpec((halo, width), lambda j: (rows // halo - 1, 0))
    edge = pl.BlockSpec((8, width), lambda j: (0, 0))
    return pl.pallas_call(
        patch_kernel,
        grid=(1,),
        in_specs=[pl.BlockSpec(memory_space=pltpu.SMEM), block, edge, edge]
        + [pl.BlockSpec(memory_space=pl.ANY)] * len(waits),
        out_specs=block,
        out_shape=jax.ShapeDtypeStruct((rows, width), bf16),
        input_output_aliases={1: 0},
        cost_estimate=tiny_cost,
        name="patched",
    )(ids, grads, last, following, *waits)


def edge_kernel(ids_ref, tokens_ref, out_ref):
    rows = ids_ref.shape[0]
    taps = 4
    out_ref[...] = tokens_ref[...]
    place = lax.broadcasted_iota(jnp.int32, (halo, 1), 0)
    same = jnp.zeros((halo, 1), f32)
    for lag in range(taps):
        here = jnp.where(ids_ref[rows - 1 - lag] == ids_ref[rows - 1], 1.0, 0.0)
        same = same + jnp.where(place == halo - 1 - lag, here, 0.0)
    out_ref[...] = (tokens_ref[...].astype(f32) * same).astype(bf16)


def edge_rows_of(ids, tokens):
    rows, width = tokens.shape
    return pl.pallas_call(
        edge_kernel,
        grid=(1,),
        in_specs=[
            pl.BlockSpec(memory_space=pltpu.SMEM),
            pl.BlockSpec((halo, width), lambda j: (rows // halo - 1, 0)),
        ],
        out_specs=pl.BlockSpec((halo, width), lambda j: (0, 0)),
        out_shape=jax.ShapeDtypeStruct((halo, width), bf16),
        cost_estimate=tiny_cost,
        name="edge_rows",
    )(ids, tokens)


block_rows, used_rows = 16, 12


def small_kernel(place_ref, scan_ref, conv_ref, wait_ref, keep_ref, *rest):
    *sends_refs, rows, blocks = rest
    rows[...] = jnp.zeros(rows.shape, f32)
    rows[: scan_ref.shape[0], :] = scan_ref[...]
    rows[scan_ref.shape[0] : scan_ref.shape[0] + conv_ref.shape[0], :] = conv_ref[...]
    blocks[...] = jnp.zeros(blocks.shape, f32)
    for n in range(16):
        blocks[n * block_rows : n * block_rows + used_rows, :] = rows[
            n * used_rows : (n + 1) * used_rows, :
        ]
    quarter = keep_ref.shape[0]
    for n in range(4):
        start = pl.multiple_of((place_ref[0] ^ n) * quarter, quarter)
        block = blocks[pl.ds(start, quarter), :]
        if n == 0:
            keep_ref[...] = block
        else:
            sends_refs[n - 1][...] = block.astype(bf16)


def small_quarters(place, scan_small, conv_small, wait):
    width = scan_small.shape[1]
    return pl.pallas_call(
        small_kernel,
        in_specs=[pl.BlockSpec(memory_space=pltpu.SMEM)]
        + [pl.BlockSpec(memory_space=pltpu.VMEM)] * 2
        + [pl.BlockSpec(memory_space=pl.ANY)],
        out_shape=[jax.ShapeDtypeStruct((4 * block_rows, width), f32)]
        + [jax.ShapeDtypeStruct((4 * block_rows, width), bf16)] * 3,
        scratch_shapes=[
            pltpu.VMEM((16 * used_rows, width), f32),
            pltpu.VMEM((16 * block_rows, width), f32),
        ],
        cost_estimate=tiny_cost,
        name="small_quarters",
    )(place, scan_small, conv_small, wait)


def quarter_kernel(
    place_ref,
    own_ref,
    near_ref,
    far_ref,
    last_ref,
    normed_0,
    normed_1,
    normed_2,
    normed_3,
    small_ref,
    first_ref,
    second_ref,
    third_ref,
    *rest,
):
    keep_ref, *sends_refs, piece, small = rest[-6:]
    total = None
    grads = (own_ref, near_ref, far_ref, last_ref)
    for left, right in zip((normed_0, normed_1, normed_2, normed_3), grads):
        part = lax.dot_general(left[...], right[...], contract_first, preferred_element_type=f32)
        total = part if total is None else total + part
    piece[...] = total
    small[...] = small_ref[...] + sum(
        ref[...].astype(f32) for ref in (first_ref, second_ref, third_ref)
    )
    rows, spare = piece.shape[0] // 4, small.shape[0] // 4
    for n in range(4):
        block = place_ref[0] ^ n
        inner_rows = piece[pl.ds(pl.multiple_of(block * rows, rows), rows), :]
        small_rows = small[pl.ds(pl.multiple_of(block * spare, spare), spare), :]
        if n == 0:
            keep_ref[:rows, :] = inner_rows
            keep_ref[rows:, :] = small_rows
        else:
            sends_refs[n - 1][:rows, :] = inner_rows.astype(bf16)
            sends_refs[n - 1][rows:, :] = small_rows.astype(bf16)


def inner_quarter(place, own, near, far, last, normed, smalls, waits):
    width = own.shape[1]
    quarter = normed[0].shape[1]
    spare = smalls[0].shape[0]
    rows = (quarter + spare) // 4
    return pl.pallas_call(
        quarter_kernel,
        in_specs=[pl.BlockSpec(memory_space=pltpu.SMEM)]
        + [pl.BlockSpec(memory_space=pltpu.VMEM)] * 12
        + [pl.BlockSpec(memory_space=pl.ANY)] * len(waits),
        out_shape=[jax.ShapeDtypeStruct((rows, width), f32)]
        + [jax.ShapeDtypeStruct((rows, width), bf16)] * 3,
        scratch_shapes=[pltpu.VMEM((quarter, width), f32), pltpu.VMEM((spare, width), f32)],
        compiler_params=pltpu.CompilerParams(vmem_limit_bytes=vmem_bytes),
        cost_estimate=tiny_cost,
        name="inner_quarter",
    )(place, own, near, far, last, *normed, *smalls, *waits)


def join_kernel(place_ref, own_gate, other_gate, first_ref, second_ref, *rest, small_rows):
    at_end = 2 + len(small_rows) if small_rows else 0
    out_ref = rest[-1 - at_end]
    step = pl.program_id(0)
    rows = out_ref.shape[0] // 2
    second_core = place_ref[0] & 1 == 1
    out_ref[:, 1, :] = jnp.where(second_core, own_gate[...], other_gate[...]).astype(f32)

    def put(ref):
        for n in range(2):
            at = n * (rows + block_rows)
            out_ref[n * rows : (n + 1) * rows, 0, :] = ref[at : at + rows, :].astype(f32)

    @pl.when(step < 2)
    def _():
        put(first_ref)

    @pl.when(step >= 2)
    def _():
        put(second_ref)

    if not small_rows:
        return
    *row_refs, gain_ref, blocks = rest[-at_end:]

    @pl.when(step == 3)
    def _():
        for flip, ref in enumerate(rest[:4]):
            for n in range(4):
                at = ((place_ref[0] ^ flip) * 4 + n) * block_rows
                taken = ref[(n + 1) * rows + n * block_rows : (n + 1) * (rows + block_rows), :]
                blocks[pl.ds(pl.multiple_of(at, block_rows), block_rows), :] = taken.astype(f32)
        for ref, start in zip(row_refs, small_rows):
            for row in range(ref.shape[0]):
                at = (start + row) // used_rows * block_rows + (start + row) % used_rows
                ref[row : row + 1, :] = blocks[at : at + 1, :]
        gain_ref[...] = sum(
            blocks[n * block_rows + used_rows : n * block_rows + used_rows + 1, :] for n in range(16)
        )


def joined(place, flip, gates, first, second, before, waits, held=(), small_rows=(), small_counts=()):
    depth, width = gates[0].shape
    quarter = depth // 4
    block = quarter // 2
    piece = first.shape[0] // 2

    def target(j, place):
        return 2 * (place[0] ^ (flip + j // 2)) + lax.rem(j, 2)

    vmem = pl.BlockSpec(memory_space=pltpu.VMEM)
    untouched = [*before, *waits]
    return pl.pallas_call(
        functools.partial(join_kernel, small_rows=small_rows),
        grid_spec=pltpu.PrefetchScalarGridSpec(
            num_scalar_prefetch=1,
            grid=(4,),
            in_specs=[
                pl.BlockSpec((block, width), lambda j, place: (target(j, place), 0)),
                pl.BlockSpec((block, width), lambda j, place: (target(j, place), 0)),
                pl.BlockSpec((piece, width), lambda j, place: (jnp.minimum(j, 1), 0)),
                pl.BlockSpec((piece, width), lambda j, place: (jnp.maximum(j - 2, 0), 0)),
            ]
            + [vmem] * len(held)
            + [pl.BlockSpec(memory_space=pl.ANY)] * len(untouched),
            out_specs=[pl.BlockSpec((block, 2, width), lambda j, place: (target(j, place), 0, 0))]
            + [pl.BlockSpec((rows, width), lambda j, place: (0, 0)) for rows in small_counts],
            scratch_shapes=[pltpu.VMEM((16 * block_rows, width), f32)] if small_rows else [],
        ),
        out_shape=[jax.ShapeDtypeStruct((depth, 2, width), f32)]
        + [jax.ShapeDtypeStruct((rows, width), f32) for rows in small_counts],
        input_output_aliases={5 + len(held) + k: k for k in range(len(before))},
        compiler_params=pltpu.CompilerParams(vmem_limit_bytes=vmem_bytes),
        cost_estimate=tiny_cost,
        name="joined",
    )(place, *gates, first, second, *held, *untouched)


def small_call(kernel, name, out_shape, scalars, arrays, waits, scratch=()):
    return pl.pallas_call(
        functools.partial(kernel, waits=len(waits)),
        in_specs=[pl.BlockSpec(memory_space=pltpu.SMEM)] * len(scalars)
        + [pl.BlockSpec(memory_space=pltpu.VMEM)] * len(arrays)
        + [pl.BlockSpec(memory_space=pl.ANY)] * len(waits),
        out_shape=out_shape,
        scratch_shapes=scratch,
        compiler_params=pltpu.CompilerParams(vmem_limit_bytes=vmem_bytes),
        cost_estimate=tiny_cost,
        name=name,
    )(*scalars, *arrays, *waits)


def product_half(left, right, half):
    size = left.shape[1] // 2
    return lax.dot_general(
        left[:, half * size : (half + 1) * size],
        right[...],
        contract_first,
        preferred_element_type=f32,
    )


def early_send_kernel(core_ref, gated_ref, cot_ref, normed_ref, gate_grad_ref, out_ref, *, waits):
    size = out_ref.shape[0] // 2
    for core, left, right in ((1, gated_ref, cot_ref), (0, normed_ref, gate_grad_ref)):

        @pl.when(core_ref[0] == core)
        def _():
            for half in range(2):
                rows = slice(half * size, (half + 1) * size)
                out_ref[rows, :] = product_half(left, right, half).astype(bf16)


def early_first_kernel(
    core_ref,
    upper_ref,
    gated_ref,
    cot_ref,
    normed_ref,
    gate_grad_ref,
    arrived_ref,
    *rest,
    waits,
):
    keep_ref, send_ref = rest[waits:]
    size = keep_ref.shape[0]
    for core, left, right in ((0, gated_ref, cot_ref), (1, normed_ref, gate_grad_ref)):
        for half in range(2):
            for mine in range(2):

                @pl.when((core_ref[0] == core) & ((upper_ref[0] == half) == (mine == 1)))
                def _():
                    rows = slice(half * size, (half + 1) * size)
                    total = product_half(left, right, half) + arrived_ref[rows, :].astype(f32)
                    if mine:
                        keep_ref[...] = total
                    else:
                        send_ref[...] = total.astype(bf16)


def fold_kernel(upper_ref, keep_ref, arrived_ref, *rest, waits):
    out_ref, send_ref = rest[waits:]
    size = out_ref.shape[0]
    mine = pl.ds(pl.multiple_of(upper_ref[0] * size, size), size)
    other = pl.ds(pl.multiple_of((1 - upper_ref[0]) * size, size), size)
    out_ref[...] = keep_ref[mine, :] + arrived_ref[mine, :].astype(f32)
    send_ref[...] = (keep_ref[other, :] + arrived_ref[other, :].astype(f32)).astype(bf16)


def folded(keep, arrived, bits, *waits):
    rows, width = keep.shape
    kinds = [jax.ShapeDtypeStruct((rows // 2, width), kind) for kind in (f32, bf16)]
    return small_call(fold_kernel, "folded", kinds, [early_upper(bits)], [keep, arrived], waits)


def settle_kernel(keep_ref, arrived_ref, *rest, waits):
    rest[waits][...] = (keep_ref[...] + arrived_ref[...].astype(f32)).astype(bf16)


def settled(keep, arrived, *waits):
    kind = jax.ShapeDtypeStruct(keep.shape, bf16)
    return small_call(settle_kernel, "settled", kind, [], [keep, arrived], waits)


def unfold_kernel(upper_ref, held_ref, arrived_ref, *rest, waits):
    out_ref = rest[waits]
    size = held_ref.shape[0]
    out_ref[pl.ds(pl.multiple_of(upper_ref[0] * size, size), size), :] = held_ref[...]
    out_ref[pl.ds(pl.multiple_of((1 - upper_ref[0]) * size, size), size), :] = arrived_ref[...]


def unfolded(held, arrived, bits, *waits):
    rows, width = held.shape
    kind = jax.ShapeDtypeStruct((2 * rows, width), bf16)
    return small_call(
        unfold_kernel, "unfolded", kind, [early_upper(bits)], [held, arrived], waits
    )


def widen_kernel(place_ref, own_ref, other_ref, out_ref):
    out_ref[...] = jnp.where(place_ref[0] & 1 == 1, other_ref[...], own_ref[...]).astype(f32)


def widened(place, own, other):
    rows, width = own.shape
    block = pl.BlockSpec((rows // 4, width), lambda j: (j, 0))
    return pl.pallas_call(
        widen_kernel,
        grid=(4,),
        in_specs=[pl.BlockSpec(memory_space=pltpu.SMEM), block, block],
        out_specs=block,
        out_shape=jax.ShapeDtypeStruct((rows, width), f32),
        cost_estimate=tiny_cost,
        name="widened",
    )(place, own, other)


def through(decay, total):
    return jnp.exp(decay * total)


def round_kernel(second_ref, decay_log_ref, own_ref, other_ref, passed_ref, new_passed_ref, *ends_refs):
    count = decay_log_ref.shape[0]
    decay = -jnp.exp(decay_log_ref[...])
    second = second_ref[0] > 0

    def split(ref):
        return ref[:count], ref[count : 2 * count], ref[2 * count : 2 * count + 1]

    own, other = split(own_ref), split(other_ref)
    early = [jnp.where(second, b, a) for a, b in zip(own, other)]
    late = [jnp.where(second, a, b) for a, b in zip(own, other)]
    state = late[0] + through(decay, late[2]) * early[0]
    adjoint = early[1] + through(decay, early[2]) * late[1]
    if len(ends_refs) == 2:
        ends_refs[0][...] = state
        ends_refs[1][...] = adjoint
    else:
        ends_refs[0][:count, :] = state
        ends_refs[0][count : 2 * count, :] = adjoint
        ends_refs[0][2 * count :, :] = jnp.broadcast_to(early[2] + late[2], (8, decay.shape[1]))
    before, after = passed_ref[:count], passed_ref[count : 2 * count]
    before_steps = passed_ref[2 * count : 2 * count + 1]
    after_steps = passed_ref[2 * count + 1 : 2 * count + 2]
    new_passed_ref[:count, :] = before + jnp.where(second, through(decay, before_steps) * other[0], 0.0)
    new_passed_ref[count : 2 * count, :] = after + jnp.where(
        second, 0.0, through(decay, after_steps) * other[1]
    )
    new_passed_ref[2 * count : 2 * count + 1, :] = before_steps + jnp.where(second, other[2], 0.0)
    new_passed_ref[2 * count + 1 : 2 * count + 2, :] = after_steps + jnp.where(second, 0.0, other[2])


def carried(ends, decay_log):
    count, width = decay_log.shape
    place = lax.axis_index("wide").astype(jnp.int32)
    passed = jnp.zeros((2 * count + 8, width), f32)
    packed = ends
    vmem = pl.BlockSpec(memory_space=pltpu.VMEM)
    for k, kinds in enumerate(([ends], [decay_log, decay_log])):
        passed, *out = pl.pallas_call(
            round_kernel,
            in_specs=[pl.BlockSpec(memory_space=pltpu.SMEM)] + [vmem] * 4,
            out_shape=[jax.ShapeDtypeStruct(kind.shape, f32) for kind in [passed] + kinds],
            cost_estimate=tiny_cost,
            name="carry_round",
        )((place >> k & 1)[None], decay_log, packed, swapped(packed, "wide", 2**k), passed)
        packed = out[0]
    from_before = passed_along(out[0], "wide", 4)
    from_after = passed_along(out[1], "wide", -4)
    return passed, from_before, from_after


def local(
    tokens,
    norm_gain,
    in_weight,
    conv_weight,
    conv_bias,
    select_weight,
    step_weight,
    step_bias,
    decay_log,
    skip_gain,
    out_weight,
    segment_ids,
    cotangent,
):
    rows, features = tokens.shape
    taps = conv_weight.shape[0]
    columns = select_weight.shape[0]
    rank = step_weight.shape[0]
    count = decay_log.shape[0]
    right_half = lax.axis_index("narrow") == 1

    def both_halves(own, other):
        return jnp.concatenate(
            [jnp.where(right_half, other, own), jnp.where(right_half, own, other)], axis=1
        )

    other_tokens = swapped(tokens, "narrow", 1)
    other_cot = swapped(cotangent, "narrow", 1)
    edge, other_edge = to_next_both(edge_rows_of(segment_ids, tokens))

    whole_low, normed_ext, normed, inverse, masks = normalized(
        tokens, other_tokens, edge, other_edge, norm_gain[None], segment_ids[None]
    )
    projected = jnp.einsum(
        "td,dce->cte", normed_ext, in_weight, preferred_element_type=f32
    ).astype(bf16)
    convolved, act, selected = convolve(
        projected, conv_weight, conv_bias[None], select_weight, masks
    )
    other_selected = swapped(selected, "narrow", 1)
    cot_whole = both_halves(cotangent, other_cot)
    gated_grad = lax.dot_general(
        cot_whole, out_weight, contract_last, preferred_element_type=f32
    )
    step_pre, step, ends = scan_ends(
        selected,
        other_selected,
        step_weight,
        step_bias[None],
        act,
        projected,
        gated_grad,
        masks,
        decay_log,
    )
    passed, entering, returning = carried(ends, decay_log)
    gated, gate_grad, entry = scan_forward(
        selected,
        other_selected,
        step,
        act,
        projected,
        gated_grad,
        masks,
        decay_log,
        passed,
        entering,
        skip_gain[None],
    )
    wide_place = lax.axis_index("wide").astype(jnp.int32)
    four_place = (wide_place & 3)[None]
    first_bits, *more_bits = group_bits(2)
    whole = whole_low.astype(f32)

    def narrow_halves(array):
        low, high = array[:, :features], array[:, features:]
        return jnp.where(right_half, high, low), jnp.where(right_half, low, high)

    steps = early_bits()
    core = (wide_place & 1)[None]
    factors = [gated, cot_whole, normed, gate_grad]
    size, depth = out_weight.shape[0], cot_whole.shape[1]
    send = small_call(
        early_send_kernel, "early_send", jax.ShapeDtypeStruct((size, depth), bf16), [core], factors, []
    )
    arrived = swapped(send, "wide", 1)
    out_part = jnp.dot(gated, out_weight, preferred_element_type=f32)
    out_mine, out_other = narrow_halves(out_part)
    early, send = small_call(
        early_first_kernel,
        "early_first",
        [jax.ShapeDtypeStruct((size // 2, depth), kind) for kind in (f32, bf16)],
        [core, early_upper(steps[0])],
        [*factors, arrived],
        [out_other, returning],
    )
    arrived = early_swapped(send, steps[0])
    out_theirs = swapped(out_other, "narrow", 1)
    act_grad, select_grad, scan_small = scan_backward(
        selected,
        other_selected,
        step_pre,
        step,
        act,
        projected,
        gated_grad,
        masks,
        decay_log,
        entry,
        passed,
        returning,
        skip_gain[None],
        step_weight,
        [send, out_other],
    )
    layer_out = (tokens.astype(f32) + (out_mine + out_theirs)).astype(bf16)
    normed_four = quarter_of_four(after(normed, select_grad))
    inner_main, before, last, conv_small = convolve_grad(
        select_grad,
        swapped(select_grad, "narrow", 1),
        select_weight,
        act_grad,
        convolved,
        act,
        projected,
        conv_weight,
        masks,
        [out_theirs],
    )
    following = passed_along(before, "wide", -1)
    early, send = folded(early, arrived, steps[1], conv_small)
    arrived = early_swapped(send, steps[1])
    inner_grad = patched(segment_ids, inner_main, last, following, send, *normed_four)
    near = swapped(inner_grad, "wide", 2)
    far = swapped(inner_grad, "wide", 1)
    keep, *sends = small_quarters(four_place, scan_small, conv_small, inner_grad)
    smalls = [keep] + [swapped(sends[n - 1], "wide", n) for n in (1, 2, 3)]
    normed_part = jnp.einsum(
        "cte,dce->td", jnp.stack([inner_grad, gate_grad]), in_weight, preferred_element_type=f32
    )
    gain_part = jnp.sum(normed_part * whole * inverse, axis=0, keepdims=True)
    row_part = jnp.sum(normed_part * norm_gain * whole, axis=1)[None]
    gain_sum = gain_part + swapped(gain_part, "narrow", 1)
    for bit in (bit for bits in more_bits for bit in bits):
        gain_sum = gain_sum + swapped(gain_sum, "wide", bit)
    for bits in steps[2:]:
        early, send = folded(early, arrived, bits, gain_part, *sends)
        arrived = early_swapped(send, bits)
    normed_mine, normed_other = narrow_halves(normed_part)
    row_theirs = swapped(row_part, "narrow", 1)
    normed_theirs = swapped(normed_other, "narrow", 1)
    near = after(near, send, gain_sum, row_theirs, *smalls[1:])
    last = swapped(near, "wide", 1)
    early = settled(early, arrived, near)
    back = early_swapped(early, steps[-1])
    keep, *sends = inner_quarter(
        (wide_place >> 2 & 3)[None],
        inner_grad,
        near,
        far,
        last,
        normed_four,
        smalls,
        [early],
    )
    for bits, following_bits in zip(steps[:1:-1], steps[-2:0:-1]):
        early = unfolded(early, back, bits, keep)
        back = early_swapped(early, following_bits)
    row_sum = (row_part + row_theirs).reshape(rows, 1)
    gain_mine = jnp.where(right_half, norm_gain[features:], norm_gain[:features])
    whole_grad = inverse * (gain_mine * (normed_mine + normed_theirs)) - tokens.astype(f32) * (
        inverse * inverse * inverse
    ) * (row_sum / (2 * features))
    tokens_grad = (whole_grad + cotangent.astype(f32)).astype(bf16)
    arrived = [swapped(sends[n - 1], "wide", flips(first_bits)[n]) for n in (1, 2, 3)]
    arrived[0] = after(arrived[0], early, normed_theirs)
    held = keep + sum(a.astype(f32) for a in arrived)
    for bits in more_bits:
        held = scattered(held, bits)
    held = held.astype(bf16)
    for bits in reversed(more_bits):
        held = gathered(held, bits)
    spare = jnp.broadcast_to(gain_sum, (block_rows - used_rows, gain_sum.shape[1]))
    held = jnp.concatenate([held[: held.shape[0] - spare.shape[0]], spare.astype(bf16)])
    early = unfolded(early, back, steps[1], held)
    back = early_swapped(early, steps[0])
    held = gathered(held, first_bits, early)
    core = swapped(held, "wide", 1)
    early = unfolded(early, back, steps[0], core)
    core_early = swapped(early, "wide", 1)
    out_weight_grad = widened(four_place, early, core_early)
    gates = (early, core_early)
    (begun,) = joined(four_place, 0, gates, held, core, (), (out_weight_grad,))
    near = after(swapped(held, "wide", 2), begun)
    far = swapped(near, "wide", 1)
    conv_at = rank + count + 2
    (
        in_weight_grad,
        step_weight_grad,
        decay_log_grad,
        skip_gain_grad,
        step_bias_grad,
        select_weight_grad,
        conv_weight_grad,
        conv_bias_grad,
        norm_gain_grad,
    ) = joined(
        four_place,
        2,
        gates,
        near,
        far,
        (begun,),
        (),
        (held, core, near, far),
        (0, rank, rank + count, rank + count + 1, conv_at, conv_at + columns, conv_at + columns + taps),
        (rank, count, 1, 1, columns, taps, 1, 1),
    )
    return (
        layer_out,
        tokens_grad,
        norm_gain_grad[0],
        in_weight_grad,
        conv_weight_grad,
        conv_bias_grad[0],
        select_weight_grad,
        step_weight_grad,
        step_bias_grad[0],
        decay_log_grad,
        skip_gain_grad[0],
        out_weight_grad,
    )


def solution(mesh):
    placed = (
        P("wide", "narrow"),
        P(),
        P(None, None, "narrow"),
        P(None, "narrow"),
        P("narrow"),
        P(None, "narrow"),
        P(None, "narrow"),
        P("narrow"),
        P(None, "narrow"),
        P("narrow"),
        P("narrow", None),
        P("wide"),
        P("wide", "narrow"),
    )
    return jax.shard_map(
        local,
        mesh=mesh,
        in_specs=placed,
        out_specs=(
            P("wide", "narrow"),
            P("wide", "narrow"),
            P(),
            P(None, None, "narrow"),
            P(None, "narrow"),
            P("narrow"),
            P(None, "narrow"),
            P(None, "narrow"),
            P("narrow"),
            P(None, "narrow"),
            P("narrow"),
            P("narrow", None),
        ),
        check_vma=False,
    )
```

```python
import functools

import jax
import jax.numpy as jnp
from jax import lax
from jax.experimental import pallas as pl
from jax.experimental.pallas import tpu as pltpu
from jax.sharding import PartitionSpec as P

epsilon = 1e-05
log2e = 1.4426950408889634
reset_step = 1e30
lanes = 128
halo = 16
body_rows = 32
scan_width = 512
vmem_bytes = 56 * 1024 * 1024
tiny_cost = pl.CostEstimate(flops=1, bytes_accessed=1, transcendentals=0)
f32 = jnp.float32
bf16 = jnp.bfloat16
contract_first = (((0,), (0,)), ((), ()))
contract_last = (((1,), (1,)), ((), ()))


def passed_along(array, axis, by):
    peers = lax.axis_size(axis)
    pairs = [(i, i + by) for i in range(peers) if 0 <= i + by < peers]
    return lax.ppermute(array, axis, pairs)


def swapped(array, axis, bit):
    peers = lax.axis_size(axis)
    return lax.ppermute(array, axis, [(i, i ^ bit) for i in range(peers)])


def wide_bits():
    bit, bits = 1, []
    while bit < lax.axis_size("wide"):
        bits.append(bit)
        bit *= 2
    return bits


def to_next_both(array):
    count, sides = lax.axis_size("wide"), lax.axis_size("narrow")
    pairs = [
        (i * sides + k, (i + 1) * sides + (sides - 1 - k))
        for i in range(count - 1)
        for k in range(sides)
    ]
    return passed_along(array, "wide", 1), lax.ppermute(array, ("wide", "narrow"), pairs)


def is_upper(bit):
    return (lax.axis_index("wide") & bit) != 0


def group_bits(size):
    bits, bit = [], 4
    while bit < lax.axis_size("wide"):
        bits.append(bit)
        bit *= 2
    return [tuple(bits[k : k + size]) for k in range(0, len(bits), size)]


def flips(bits):
    return [sum(b for k, b in enumerate(bits) if n >> k & 1) for n in range(2 ** len(bits))]


def scattered(piece, bits):
    rows = piece.shape[0] // 2 ** len(bits)
    here = sum(is_upper(b).astype(jnp.int32) << k for k, b in enumerate(bits))

    def block(n):
        return lax.dynamic_slice_in_dim(piece, (here ^ n) * rows, rows, 0)

    total = block(0).astype(f32)
    for n, flip in enumerate(flips(bits)):
        if n > 0:
            total = total + swapped(block(n).astype(bf16), "wide", flip).astype(f32)
    return total


def gathered(held, bits, *waits):
    blocks = [held] + [swapped(held, "wide", flip) for flip in flips(bits)[1:]]
    if waits:
        blocks[1] = after(blocks[1], *waits)
    for bit in bits:
        upper = is_upper(bit)
        blocks = [
            jnp.concatenate([jnp.where(upper, b, a), jnp.where(upper, a, b)])
            for a, b in zip(blocks[0::2], blocks[1::2])
        ]
    return blocks[0]


def early_bits():
    bits, bit = [], 2
    while bit < lax.axis_size("wide"):
        bits.append(bit)
        bit *= 2
    return list(zip(bits, bits[1:] + bits[:1]))


def early_upper(bits):
    place = lax.axis_index("wide")
    return jnp.where(place & 1 == 0, place & bits[0] != 0, place & bits[1] != 0).astype(jnp.int32)[None]


def early_swapped(array, bits):
    peers = lax.axis_size("wide")
    return lax.ppermute(array, "wide", [(i, i ^ bits[i % 2]) for i in range(peers)])


def quarter_of_four(array):
    width = array.shape[1] // 4
    here = lax.axis_index("wide") & 3

    def quarter(n):
        return lax.dynamic_slice_in_dim(array, (here ^ n) * width, width, 1)

    return [quarter(0)] + [swapped(quarter(n), "wide", n) for n in (2, 1, 3)]


def silu_slope(values):
    logistic = jax.nn.sigmoid(values)
    return logistic * (1.0 + values * (1.0 - logistic))


def softplus(values):
    return jnp.maximum(values, 0.0) + jnp.log1p(jnp.exp(-jnp.abs(values)))


def column_spec(rows, start=0):
    return pl.BlockSpec((rows, scan_width), lambda j: (0, start + j))


def part_spec(part, rows, start=0):
    return pl.BlockSpec((None, rows, scan_width), lambda j: (part, 0, start + j))


def whole_spec(rows, width):
    return pl.BlockSpec((rows, width), lambda j: (0, 0))


def call(kernel, name, width, in_specs, out_specs, out_shape, scratch, *operands):
    return pl.pallas_call(
        kernel,
        grid=(width // scan_width,),
        in_specs=in_specs,
        out_specs=out_specs,
        out_shape=out_shape,
        scratch_shapes=scratch,
        compiler_params=pltpu.CompilerParams(vmem_limit_bytes=vmem_bytes),
        cost_estimate=tiny_cost,
        name=name,
    )(*operands)


def conv_kernel(
    inner_ref,
    conv_weight_ref,
    conv_bias_ref,
    select_ref,
    mask_ref,
    convolved_ref,
    act_ref,
    selected_ref,
    inner,
):
    rows = act_ref.shape[0]
    taps = conv_weight_ref.shape[0]
    inner[:halo, :] = inner_ref[rows:, :].astype(f32)
    inner[halo:, :] = inner_ref[:rows, :].astype(f32)
    total = conv_bias_ref[...] + conv_weight_ref[taps - 1 :, :] * inner[halo:, :]
    for lag in range(1, taps):
        earlier = inner[pl.ds(halo - lag, rows), :] * mask_ref[:, lag : lag + 1]
        total = total + conv_weight_ref[taps - 1 - lag : taps - lag, :] * earlier
    convolved_ref[...] = total
    act = (total * jax.nn.sigmoid(total)).astype(bf16)
    act_ref[...] = act
    part = lax.dot_general(select_ref[...], act, contract_last, preferred_element_type=f32)

    @pl.when(pl.program_id(0) == 0)
    def _():
        selected_ref[...] = part

    @pl.when(pl.program_id(0) > 0)
    def _():
        selected_ref[...] += part


def convolve(projected, conv_weight, conv_bias, select_weight, masks):
    parts, extended, width = projected.shape
    rows = extended - halo
    taps = conv_weight.shape[0]
    columns = select_weight.shape[0]
    return call(
        conv_kernel,
        "convolve",
        width,
        [
            part_spec(0, extended),
            column_spec(taps),
            column_spec(1),
            column_spec(columns),
            whole_spec(rows, masks.shape[1]),
        ],
        [column_spec(rows), column_spec(rows), whole_spec(columns, rows)],
        [
            jax.ShapeDtypeStruct((rows, width), f32),
            jax.ShapeDtypeStruct((rows, width), bf16),
            jax.ShapeDtypeStruct((columns, rows), f32),
        ],
        [pltpu.VMEM((extended, scan_width), f32)],
        projected,
        conv_weight,
        conv_bias,
        select_weight,
        masks,
    )


def coef_columns(coef, block):
    per_tile = lanes // body_rows
    start = pl.multiple_of((block // per_tile) * lanes, lanes)
    tile = coef[:, pl.ds(start, lanes)]
    back = body_rows * lax.rem(block, per_tile)
    return pltpu.roll(tile, lax.rem(lanes - back, lanes), 1)


def ends_kernel(
    selected_ref,
    other_ref,
    step_weight_ref,
    step_bias_ref,
    act_ref,
    gate_ref,
    gated_grad_ref,
    mask_ref,
    decay_log_ref,
    step_pre_ref,
    step_ref,
    ends_ref,
    coef,
    held_step,
    drive,
    scan_grad,
):
    rows = act_ref.shape[0]
    count = decay_log_ref.shape[0]
    rank = step_weight_ref.shape[0]
    decay2 = -jnp.exp(decay_log_ref[...]) * log2e
    selected = selected_ref[...] + other_ref[...]
    coef[...] = selected[rank:, :]
    step_low = selected[:rank, :].astype(bf16)
    step_pre = step_bias_ref[...] + lax.dot_general(
        step_low, step_weight_ref[...], contract_first, preferred_element_type=f32
    )
    step_pre_ref[...] = step_pre
    step = softplus(step_pre)
    step_ref[...] = step
    held_step[...] = jnp.where(mask_ref[:, 1:2] > 0.0, step, reset_step)
    drive[...] = step * act_ref[...].astype(f32)
    gate = gate_ref[...].astype(f32)
    scan_grad[...] = gated_grad_ref[...] * (gate * jax.nn.sigmoid(gate))
    zero = jnp.zeros(decay2.shape, f32)

    def body(block, carried):
        state, product, adjoint = carried
        columns = coef_columns(coef, block)
        for i in range(body_rows):
            row = pl.ds(block * body_rows + i, 1)
            factor = jnp.exp2(held_step[row, :] * decay2)
            state = factor * state + columns[:count, i : i + 1] * drive[row, :]
            product = factor * product
            adjoint = adjoint + product * (columns[count:, i : i + 1] * scan_grad[row, :])
        return state, product, adjoint

    state, product, adjoint = lax.fori_loop(0, rows // body_rows, body, (zero, zero + 1.0, zero))
    ends_ref[:count, :] = state
    ends_ref[count : 2 * count, :] = adjoint
    total = jnp.sum(held_step[...], axis=0, keepdims=True)
    ends_ref[2 * count :, :] = jnp.broadcast_to(total, (8, total.shape[1]))


def scan_ends(
    selected, other, step_weight, step_bias, act, projected, gated_grad, masks, decay_log
):
    rows, width = act.shape
    count = decay_log.shape[0]
    columns = selected.shape[0]
    rank = step_weight.shape[0]
    return call(
        ends_kernel,
        "scan_ends",
        width,
        [
            whole_spec(columns, rows),
            whole_spec(columns, rows),
            column_spec(rank),
            column_spec(1),
            column_spec(rows),
            part_spec(1, rows),
            column_spec(rows),
            whole_spec(rows, masks.shape[1]),
            column_spec(count),
        ],
        [column_spec(rows), column_spec(rows), column_spec(2 * count + 8)],
        [
            jax.ShapeDtypeStruct((rows, width), f32),
            jax.ShapeDtypeStruct((rows, width), f32),
            jax.ShapeDtypeStruct((2 * count + 8, width), f32),
        ],
        [pltpu.VMEM((2 * count, rows), f32)] + [pltpu.VMEM((rows, scan_width), f32)] * 3,
        selected,
        other,
        step_weight,
        step_bias,
        act,
        projected,
        gated_grad,
        masks,
        decay_log,
    )


def lane_tiles(values):
    return [values[:, k : k + lanes] for k in range(0, values.shape[1], lanes)]


def tree_sum(parts):
    while len(parts) > 1:
        odd = parts[len(parts) // 2 * 2 :]
        parts = [a + b for a, b in zip(parts[0::2], parts[1::2])] + odd
    return parts[0]


def keep_halves(scratch, i, values):
    for k, tile in enumerate(lane_tiles(values)):
        at = (k * body_rows + i) * 8
        scratch[at : at + 8, :] = tile[:8] + tile[8:]


def put_state_sums(scratch, out_ref, block):
    for group in range(body_rows // 8):
        row = pl.ds(pl.multiple_of(block * body_rows + group * 8, 8), 8)
        for k in range(out_ref.shape[1] // lanes):
            at = (k * body_rows + group * 8) * 8
            total = tree_sum([scratch[pl.ds(at + n, 8, stride=8), :] for n in range(8)])
            out_ref[row, k * lanes : (k + 1) * lanes] = total


def lane_sums(values):
    ones = jnp.ones((8, lanes), bf16)
    high = values.astype(bf16)
    low = (values - high.astype(f32)).astype(bf16)
    total = lax.dot_general(ones, high, contract_last, preferred_element_type=f32)
    total += lax.dot_general(ones, low, contract_last, preferred_element_type=f32)
    return total[:1, :]


def at_token(t, count):
    return pl.ds(pl.multiple_of(t * count, count), count)


def forward_kernel(
    selected_ref,
    other_ref,
    step_ref,
    act_ref,
    gate_ref,
    gated_grad_ref,
    mask_ref,
    decay_log_ref,
    passed_ref,
    entering_ref,
    skip_ref,
    gated_ref,
    gate_grad_ref,
    entry_ref,
    coef,
    held_step,
    drive,
    scanned,
    halves,
):
    rows = step_ref.shape[0]
    count = decay_log_ref.shape[0]
    rank = selected_ref.shape[0] - 2 * count
    decay = -jnp.exp(decay_log_ref[...])
    decay2 = decay * log2e
    before_steps = passed_ref[2 * count : 2 * count + 1, :]
    entry = passed_ref[:count, :] + through(decay, before_steps) * entering_ref[...]
    entry_ref[...] = entry
    coef[...] = selected_ref[rank:, :] + other_ref[rank:, :]
    act = act_ref[...].astype(f32)
    held_step[...] = jnp.where(mask_ref[:, 1:2] > 0.0, step_ref[...], reset_step)
    drive[...] = step_ref[...] * act

    def forward(block, state):
        columns = coef_columns(coef, block)
        for i in range(body_rows):
            row = pl.ds(block * body_rows + i, 1)
            factor = jnp.exp2(held_step[row, :] * decay2)
            state = factor * state + columns[:count, i : i + 1] * drive[row, :]
            keep_halves(halves, i, columns[count:, i : i + 1] * state)
        put_state_sums(halves, scanned, block)
        return state

    lax.fori_loop(0, rows // body_rows, forward, entry)
    gate = gate_ref[...].astype(f32)
    logistic = jax.nn.sigmoid(gate)
    total = scanned[...] + skip_ref[...] * act
    gated_ref[...] = (total * (gate * logistic)).astype(bf16)
    slope = logistic * (1.0 + gate * (1.0 - logistic))
    gate_grad_ref[...] = (gated_grad_ref[...] * total * slope).astype(bf16)


def scan_forward(
    selected, other, step, act, projected, gated_grad, masks, decay_log, passed, entering, skip_gain
):
    rows, width = step.shape
    count = decay_log.shape[0]
    columns = selected.shape[0]
    return call(
        forward_kernel,
        "scan_forward",
        width,
        [
            whole_spec(columns, rows),
            whole_spec(columns, rows),
            column_spec(rows),
            column_spec(rows),
            part_spec(1, rows),
            column_spec(rows),
            whole_spec(rows, masks.shape[1]),
            column_spec(count),
            column_spec(2 * count + 8),
            column_spec(count),
            column_spec(1),
        ],
        [column_spec(rows), column_spec(rows), column_spec(count)],
        [
            jax.ShapeDtypeStruct((rows, width), bf16),
            jax.ShapeDtypeStruct((rows, width), bf16),
            jax.ShapeDtypeStruct((count, width), f32),
        ],
        [pltpu.VMEM((2 * count, rows), f32)]
        + [pltpu.VMEM((rows, scan_width), f32)] * 3
        + [pltpu.VMEM((8 * body_rows * (scan_width // lanes), lanes), f32)],
        selected,
        other,
        step,
        act,
        projected,
        gated_grad,
        masks,
        decay_log,
        passed,
        entering,
        skip_gain,
    )


def backward_kernel(
    selected_ref,
    other_ref,
    step_pre_ref,
    step_ref,
    act_ref,
    gate_ref,
    gated_grad_ref,
    mask_ref,
    decay_log_ref,
    entry_ref,
    passed_ref,
    returning_ref,
    skip_ref,
    step_weight_ref,
    earlier_ref,
    first_wait,
    second_wait,
    act_grad_ref,
    select_grad_ref,
    small_ref,
    coef,
    held_step,
    drive,
    scan_grad,
    weighted,
    held_sum,
    states,
    factors,
    halves,
    more_halves,
    in_sum,
    read_sum,
):
    rows = step_ref.shape[0]
    count = decay_log_ref.shape[0]
    rank = step_weight_ref.shape[0]
    blocks = rows // body_rows
    decay = -jnp.exp(decay_log_ref[...])
    decay2 = decay * log2e
    after_steps = passed_ref[2 * count + 1 : 2 * count + 2, :]
    tail = passed_ref[count : 2 * count, :] + through(decay, after_steps) * returning_ref[...]
    selected = selected_ref[...] + other_ref[...]
    coef[...] = selected[rank:, :]
    step_low = selected[:rank, :].astype(bf16)
    step = step_ref[...]
    act = act_ref[...].astype(f32)
    held_step[...] = jnp.where(mask_ref[:, 1:2] > 0.0, step, reset_step)
    drive[...] = step * act
    gate = gate_ref[...].astype(f32)
    grads = gated_grad_ref[...] * (gate * jax.nn.sigmoid(gate))
    scan_grad[...] = grads
    small_ref[rank + count : rank + count + 1, :] = jnp.sum(grads * act, axis=0, keepdims=True)
    states[:count, :] = entry_ref[...]

    def forward(block, state):
        columns = coef_columns(coef, block)
        for i in range(body_rows):
            t = block * body_rows + i
            row = pl.ds(t, 1)
            factor = jnp.exp2(held_step[row, :] * decay2)
            state = factor * state + columns[:count, i : i + 1] * drive[row, :]
            factors[at_token(t, count), :] = factor
            states[at_token(t + 1, count), :] = state
        return state

    lax.fori_loop(0, blocks, forward, entry_ref[...])

    def backward(k, carried):
        adjoint, decay_grad = carried
        block = blocks - 1 - k
        columns = coef_columns(coef, block)
        for i in range(body_rows - 1, -1, -1):
            t = block * body_rows + i
            row = pl.ds(t, 1)
            here = at_token(t, count)
            grad = scan_grad[row, :]
            summed = columns[count:, i : i + 1] * grad + adjoint
            read_sum[here, :] = tree_sum(lane_tiles(grad * states[at_token(t + 1, count), :]))
            in_sum[here, :] = tree_sum(lane_tiles(summed * drive[row, :]))
            keep_halves(halves, i, summed * columns[:count, i : i + 1])
            adjoint = factors[here, :] * summed
            held = adjoint * states[here, :]
            decay_grad = decay_grad + held * step_ref[row, :]
            keep_halves(more_halves, i, held * decay)
        put_state_sums(halves, weighted, block)
        put_state_sums(more_halves, held_sum, block)
        return adjoint, decay_grad

    ignored, decay_grad = lax.fori_loop(
        0, blocks, backward, (tail, jnp.zeros(decay.shape, f32))
    )
    act_grad_ref[...] = step * weighted[...] + skip_ref[...] * scan_grad[...]
    step_grad = act * weighted[...] + held_sum[...]
    pre_grad = (step_grad * jax.nn.sigmoid(step_pre_ref[...])).astype(bf16)
    small_ref[:rank, :] = jnp.dot(step_low, pre_grad, preferred_element_type=f32)
    small_ref[rank : rank + count, :] = decay_grad * decay
    bias_grad = jnp.sum(pre_grad.astype(f32), axis=0, keepdims=True)
    small_ref[rank + count + 1 : rank + count + 2, :] = bias_grad
    select_grad_ref[:rank, :] = earlier_ref[:rank, :] + lax.dot_general(
        step_weight_ref[...], pre_grad, contract_last, preferred_element_type=f32
    )
    for n in range(count):
        at = pl.ds(n, rows, stride=count)
        for sums, start in ((in_sum, rank), (read_sum, rank + count)):
            row = slice(start + n, start + n + 1)
            select_grad_ref[row, :] = earlier_ref[row, :] + lane_sums(sums[at, :])


def scan_backward(
    part,
    selected,
    other,
    step_pre,
    step,
    act,
    projected,
    gated_grad,
    masks,
    decay_log,
    entry,
    passed,
    returning,
    skip_gain,
    step_weight,
    earlier,
    waits,
):
    rows, width = step.shape[0], scan_width
    count = decay_log.shape[0]
    columns = selected.shape[0]
    rank = step_weight.shape[0]
    half_rows = 8 * body_rows * (scan_width // lanes)
    small = rank + count + 2
    return call(
        backward_kernel,
        "scan_backward",
        width,
        [
            whole_spec(columns, rows),
            whole_spec(columns, rows),
            column_spec(rows, part),
            column_spec(rows, part),
            column_spec(rows, part),
            part_spec(1, rows, part),
            column_spec(rows, part),
            whole_spec(rows, masks.shape[1]),
            column_spec(count, part),
            column_spec(count, part),
            column_spec(2 * count + 8, part),
            column_spec(count, part),
            column_spec(1, part),
            column_spec(rank, part),
            whole_spec(columns, rows),
        ]
        + [pl.BlockSpec(memory_space=pl.ANY)] * 2,
        [column_spec(rows), whole_spec(columns, rows), column_spec(small)],
        [
            jax.ShapeDtypeStruct((rows, width), f32),
            jax.ShapeDtypeStruct((columns, rows), f32),
            jax.ShapeDtypeStruct((small, width), f32),
        ],
        [pltpu.VMEM((2 * count, rows), f32)]
        + [pltpu.VMEM((rows, scan_width), f32)] * 5
        + [
            pltpu.VMEM(((rows + 1) * count, scan_width), f32),
            pltpu.VMEM((rows * count, scan_width), f32),
            pltpu.VMEM((half_rows, lanes), f32),
            pltpu.VMEM((half_rows, lanes), f32),
            pltpu.VMEM((rows * count, lanes), f32),
            pltpu.VMEM((rows * count, lanes), f32),
        ],
        selected,
        other,
        step_pre,
        step,
        act,
        projected,
        gated_grad,
        masks,
        decay_log,
        entry,
        passed,
        returning,
        skip_gain,
        step_weight,
        earlier,
        *waits,
    )


def conv_grad_kernel(
    select_grad_ref,
    other_ref,
    select_ref,
    first_act_grad,
    second_act_grad,
    convolved_ref,
    act_ref,
    inner_ref,
    conv_weight_ref,
    mask_ref,
    *rest,
):
    inner_grad_ref, before_ref, last_ref, small_ref, inner, shifted = rest[-6:]
    rows = act_ref.shape[0]
    taps = conv_weight_ref.shape[0]
    columns = select_ref.shape[0]
    select_grad = (select_grad_ref[...] + other_ref[...]).astype(bf16)
    act_grad = jnp.where(pl.program_id(0) == 0, first_act_grad[...], second_act_grad[...])
    total = act_grad + lax.dot_general(
        select_grad, select_ref[...], contract_first, preferred_element_type=f32
    )
    conv_grad = total * silu_slope(convolved_ref[...])
    small_ref[:columns, :] = jnp.dot(select_grad, act_ref[...], preferred_element_type=f32)
    inner[:halo, :] = inner_ref[rows:, :].astype(f32)
    inner[halo:, :] = inner_ref[:rows, :].astype(f32)
    edges = jnp.zeros((8, conv_grad.shape[1]), f32)
    shifted[:8, :] = edges
    shifted[rows + 8 :, :] = edges
    out = conv_weight_ref[taps - 1 :, :] * conv_grad
    before = edges
    small_ref[columns + taps - 1 : columns + taps, :] = jnp.sum(
        conv_grad * inner[halo:, :], axis=0, keepdims=True
    )
    for lag in range(1, taps):
        masked = conv_grad * mask_ref[:, lag : lag + 1]
        at = taps - 1 - lag
        small_ref[columns + at : columns + at + 1, :] = jnp.sum(
            masked * inner[pl.ds(halo - lag, rows), :], axis=0, keepdims=True
        )
        shifted[8 : rows + 8, :] = masked
        weight = conv_weight_ref[at : at + 1, :]
        out = out + weight * shifted[pl.ds(8 + lag, rows), :]
        before = before + weight * shifted[pl.ds(lag, 8), :]
    small_ref[columns + taps : columns + taps + 1, :] = jnp.sum(conv_grad, axis=0, keepdims=True)
    inner_grad_ref[...] = out.astype(bf16)
    before_ref[...] = before
    last_ref[...] = out[rows - 8 :, :]


def convolve_grad(
    select_grad, other, select_weight, act_grads, convolved, act, projected, conv_weight, masks, waits
):
    rows, width = act.shape
    extended = rows + halo
    columns = select_weight.shape[0]
    taps = conv_weight.shape[0]
    small = columns + taps + 1
    return call(
        conv_grad_kernel,
        "convolve_grad",
        width,
        [
            whole_spec(columns, rows),
            whole_spec(columns, rows),
            column_spec(columns),
            whole_spec(rows, scan_width),
            whole_spec(rows, scan_width),
            column_spec(rows),
            column_spec(rows),
            part_spec(0, extended),
            column_spec(taps),
            whole_spec(rows, masks.shape[1]),
        ]
        + [pl.BlockSpec(memory_space=pl.ANY)] * len(waits),
        [column_spec(rows), column_spec(8), column_spec(8), column_spec(small)],
        [
            jax.ShapeDtypeStruct((rows, width), bf16),
            jax.ShapeDtypeStruct((8, width), f32),
            jax.ShapeDtypeStruct((8, width), f32),
            jax.ShapeDtypeStruct((small, width), f32),
        ],
        [pltpu.VMEM((extended, scan_width), f32), pltpu.VMEM((rows + 16, scan_width), f32)],
        select_grad,
        other,
        select_weight,
        *act_grads,
        convolved,
        act,
        projected,
        conv_weight,
        masks,
        *waits,
    )


def normalize_kernel(
    own_ref,
    other_ref,
    edge_ref,
    other_edge_ref,
    gain_ref,
    ids_ref,
    whole_ref,
    extended_ref,
    normed_ref,
    inverse_ref,
    mask_ref,
    rows_ref,
):
    rows, half = own_ref.shape
    ids = ids_ref[...].astype(f32)
    place = lax.broadcasted_iota(jnp.int32, ids.shape, 1)
    same = []
    for lag in range(8):
        earlier = jnp.where(place < lag, ids[:, :1], pltpu.roll(ids, lag, 1)) if lag else ids
        same.append(jnp.where(earlier == ids, 1.0, 0.0))
    spare = jnp.zeros((lanes - 8, rows), f32)
    mask_ref[...] = jnp.concatenate(same + [spare]).T
    right = lax.axis_index("narrow") == 1
    for at, own, other in ((0, own_ref, other_ref), (rows, edge_ref, other_edge_ref)):
        end = at + own.shape[0]
        rows_ref[at:end, :half] = jnp.where(right, other[...], own[...])
        rows_ref[at:end, half:] = jnp.where(right, own[...], other[...])
    whole_ref[...] = rows_ref[:rows, :]
    whole = rows_ref[...].astype(f32)
    inverse = lax.rsqrt(jnp.mean(whole * whole, axis=1, keepdims=True) + epsilon)
    normed = (whole * inverse * gain_ref[...]).astype(bf16)
    extended_ref[...] = normed
    normed_ref[...] = normed[:rows]
    inverse_ref[...] = inverse[:rows]


def normalized(own, other, edge, other_edge, gain, ids):
    rows, half = own.shape
    extended = rows + edge.shape[0]
    return pl.pallas_call(
        normalize_kernel,
        out_shape=[
            jax.ShapeDtypeStruct((rows, 2 * half), bf16),
            jax.ShapeDtypeStruct((extended, 2 * half), bf16),
            jax.ShapeDtypeStruct((rows, 2 * half), bf16),
            jax.ShapeDtypeStruct((rows, 1), f32),
            jax.ShapeDtypeStruct((rows, lanes), f32),
        ],
        scratch_shapes=[pltpu.VMEM((extended, 2 * half), bf16)],
        cost_estimate=tiny_cost,
        name="normalized",
    )(own, other, edge, other_edge, gain, ids)


def after(array, *waits):
    anywhere = pl.BlockSpec(memory_space=pl.ANY)
    return pl.pallas_call(
        lambda *refs: None,
        in_specs=[anywhere] * (1 + len(waits)),
        out_specs=anywhere,
        out_shape=jax.ShapeDtypeStruct(array.shape, array.dtype),
        input_output_aliases={0: 0},
        cost_estimate=tiny_cost,
        name="after",
    )(array, *waits)


def patch_kernel(ids_ref, rows_ref, last_ref, next_ref, *rest):
    count = ids_ref.shape[0]
    place = lax.broadcasted_iota(jnp.int32, (8, 1), 0)
    same = jnp.zeros((8, 1), f32)
    for lag in range(8):
        here = jnp.where(ids_ref[count - 1 - lag] == ids_ref[count - 1], 1.0, 0.0)
        same = same + jnp.where(place == 7 - lag, here, 0.0)
    total = last_ref[...] + next_ref[...] * same
    rows = rows_ref[...].astype(f32)
    rest[-1][...] = jnp.concatenate([rows[: halo - 8], total]).astype(bf16)


def patched(ids, grads, last, following, *waits):
    rows, width = grads.shape
    block = pl.BlockSpec((halo, width), lambda j: (rows // halo - 1, 0))
    edge = pl.BlockSpec((8, width), lambda j: (0, 0))
    return pl.pallas_call(
        patch_kernel,
        grid=(1,),
        in_specs=[pl.BlockSpec(memory_space=pltpu.SMEM), block, edge, edge]
        + [pl.BlockSpec(memory_space=pl.ANY)] * len(waits),
        out_specs=block,
        out_shape=jax.ShapeDtypeStruct((rows, width), bf16),
        input_output_aliases={1: 0},
        cost_estimate=tiny_cost,
        name="patched",
    )(ids, grads, last, following, *waits)


def edge_kernel(ids_ref, tokens_ref, out_ref):
    rows = ids_ref.shape[0]
    taps = 4
    out_ref[...] = tokens_ref[...]
    place = lax.broadcasted_iota(jnp.int32, (halo, 1), 0)
    same = jnp.zeros((halo, 1), f32)
    for lag in range(taps):
        here = jnp.where(ids_ref[rows - 1 - lag] == ids_ref[rows - 1], 1.0, 0.0)
        same = same + jnp.where(place == halo - 1 - lag, here, 0.0)
    out_ref[...] = (tokens_ref[...].astype(f32) * same).astype(bf16)


def edge_rows_of(ids, tokens):
    rows, width = tokens.shape
    return pl.pallas_call(
        edge_kernel,
        grid=(1,),
        in_specs=[
            pl.BlockSpec(memory_space=pltpu.SMEM),
            pl.BlockSpec((halo, width), lambda j: (rows // halo - 1, 0)),
        ],
        out_specs=pl.BlockSpec((halo, width), lambda j: (0, 0)),
        out_shape=jax.ShapeDtypeStruct((halo, width), bf16),
        cost_estimate=tiny_cost,
        name="edge_rows",
    )(ids, tokens)


block_rows, used_rows = 16, 12


def small_kernel(place_ref, first_scan, second_scan, conv_ref, wait_ref, keep_ref, *rest):
    *sends_refs, rows, blocks = rest
    rows[...] = jnp.zeros(rows.shape, f32)
    count = first_scan.shape[0]
    rows[:count, :scan_width] = first_scan[...]
    rows[:count, scan_width:] = second_scan[...]
    rows[count : count + conv_ref.shape[0], :] = conv_ref[...]
    blocks[...] = jnp.zeros(blocks.shape, f32)
    for n in range(16):
        blocks[n * block_rows : n * block_rows + used_rows, :] = rows[
            n * used_rows : (n + 1) * used_rows, :
        ]
    quarter = keep_ref.shape[0]
    for n in range(4):
        start = pl.multiple_of((place_ref[0] ^ n) * quarter, quarter)
        block = blocks[pl.ds(start, quarter), :]
        if n == 0:
            keep_ref[...] = block
        else:
            sends_refs[n - 1][...] = block.astype(bf16)


def small_quarters(place, scan_smalls, conv_small, wait):
    width = conv_small.shape[1]
    return pl.pallas_call(
        small_kernel,
        in_specs=[pl.BlockSpec(memory_space=pltpu.SMEM)]
        + [pl.BlockSpec(memory_space=pltpu.VMEM)] * 3
        + [pl.BlockSpec(memory_space=pl.ANY)],
        out_shape=[jax.ShapeDtypeStruct((4 * block_rows, width), f32)]
        + [jax.ShapeDtypeStruct((4 * block_rows, width), bf16)] * 3,
        scratch_shapes=[
            pltpu.VMEM((16 * used_rows, width), f32),
            pltpu.VMEM((16 * block_rows, width), f32),
        ],
        cost_estimate=tiny_cost,
        name="small_quarters",
    )(place, *scan_smalls, conv_small, wait)


def quarter_kernel(
    place_ref,
    own_ref,
    near_ref,
    far_ref,
    last_ref,
    normed_0,
    normed_1,
    normed_2,
    normed_3,
    small_ref,
    first_ref,
    second_ref,
    third_ref,
    *rest,
):
    keep_ref, *sends_refs, piece, small = rest[-6:]
    total = None
    grads = (own_ref, near_ref, far_ref, last_ref)
    for left, right in zip((normed_0, normed_1, normed_2, normed_3), grads):
        part = lax.dot_general(left[...], right[...], contract_first, preferred_element_type=f32)
        total = part if total is None else total + part
    piece[...] = total
    small[...] = small_ref[...] + sum(
        ref[...].astype(f32) for ref in (first_ref, second_ref, third_ref)
    )
    rows, spare = piece.shape[0] // 4, small.shape[0] // 4
    for n in range(4):
        block = place_ref[0] ^ n
        inner_rows = piece[pl.ds(pl.multiple_of(block * rows, rows), rows), :]
        small_rows = small[pl.ds(pl.multiple_of(block * spare, spare), spare), :]
        if n == 0:
            keep_ref[:rows, :] = inner_rows
            keep_ref[rows:, :] = small_rows
        else:
            sends_refs[n - 1][:rows, :] = inner_rows.astype(bf16)
            sends_refs[n - 1][rows:, :] = small_rows.astype(bf16)


def inner_quarter(place, own, near, far, last, normed, smalls, waits):
    width = own.shape[1]
    quarter = normed[0].shape[1]
    spare = smalls[0].shape[0]
    rows = (quarter + spare) // 4
    return pl.pallas_call(
        quarter_kernel,
        in_specs=[pl.BlockSpec(memory_space=pltpu.SMEM)]
        + [pl.BlockSpec(memory_space=pltpu.VMEM)] * 12
        + [pl.BlockSpec(memory_space=pl.ANY)] * len(waits),
        out_shape=[jax.ShapeDtypeStruct((rows, width), f32)]
        + [jax.ShapeDtypeStruct((rows, width), bf16)] * 3,
        scratch_shapes=[pltpu.VMEM((quarter, width), f32), pltpu.VMEM((spare, width), f32)],
        compiler_params=pltpu.CompilerParams(vmem_limit_bytes=vmem_bytes),
        cost_estimate=tiny_cost,
        name="inner_quarter",
    )(place, own, near, far, last, *normed, *smalls, *waits)


def join_kernel(place_ref, own_gate, other_gate, first_ref, second_ref, *rest, small_rows):
    at_end = 2 + len(small_rows) if small_rows else 0
    out_ref = rest[-1 - at_end]
    step = pl.program_id(0)
    rows = out_ref.shape[0] // 2
    second_core = place_ref[0] & 1 == 1
    out_ref[:, 1, :] = jnp.where(second_core, own_gate[...], other_gate[...]).astype(f32)

    def put(ref):
        for n in range(2):
            at = n * (rows + block_rows)
            out_ref[n * rows : (n + 1) * rows, 0, :] = ref[at : at + rows, :].astype(f32)

    @pl.when(step < 2)
    def _():
        put(first_ref)

    @pl.when(step >= 2)
    def _():
        put(second_ref)

    if not small_rows:
        return
    *row_refs, gain_ref, blocks = rest[-at_end:]

    @pl.when(step == 3)
    def _():
        for flip, ref in enumerate(rest[:4]):
            for n in range(4):
                at = ((place_ref[0] ^ flip) * 4 + n) * block_rows
                taken = ref[(n + 1) * rows + n * block_rows : (n + 1) * (rows + block_rows), :]
                blocks[pl.ds(pl.multiple_of(at, block_rows), block_rows), :] = taken.astype(f32)
        for ref, start in zip(row_refs, small_rows):
            for row in range(ref.shape[0]):
                at = (start + row) // used_rows * block_rows + (start + row) % used_rows
                ref[row : row + 1, :] = blocks[at : at + 1, :]
        gain_ref[...] = sum(
            blocks[n * block_rows + used_rows : n * block_rows + used_rows + 1, :] for n in range(16)
        )


def joined(place, flip, gates, first, second, before, waits, held=(), small_rows=(), small_counts=()):
    depth, width = gates[0].shape
    quarter = depth // 4
    block = quarter // 2
    piece = first.shape[0] // 2

    def target(j, place):
        return 2 * (place[0] ^ (flip + j // 2)) + lax.rem(j, 2)

    vmem = pl.BlockSpec(memory_space=pltpu.VMEM)
    untouched = [*before, *waits]
    return pl.pallas_call(
        functools.partial(join_kernel, small_rows=small_rows),
        grid_spec=pltpu.PrefetchScalarGridSpec(
            num_scalar_prefetch=1,
            grid=(4,),
            in_specs=[
                pl.BlockSpec((block, width), lambda j, place: (target(j, place), 0)),
                pl.BlockSpec((block, width), lambda j, place: (target(j, place), 0)),
                pl.BlockSpec((piece, width), lambda j, place: (jnp.minimum(j, 1), 0)),
                pl.BlockSpec((piece, width), lambda j, place: (jnp.maximum(j - 2, 0), 0)),
            ]
            + [vmem] * len(held)
            + [pl.BlockSpec(memory_space=pl.ANY)] * len(untouched),
            out_specs=[pl.BlockSpec((block, 2, width), lambda j, place: (target(j, place), 0, 0))]
            + [pl.BlockSpec((rows, width), lambda j, place: (0, 0)) for rows in small_counts],
            scratch_shapes=[pltpu.VMEM((16 * block_rows, width), f32)] if small_rows else [],
        ),
        out_shape=[jax.ShapeDtypeStruct((depth, 2, width), f32)]
        + [jax.ShapeDtypeStruct((rows, width), f32) for rows in small_counts],
        input_output_aliases={5 + len(held) + k: k for k in range(len(before))},
        compiler_params=pltpu.CompilerParams(vmem_limit_bytes=vmem_bytes),
        cost_estimate=tiny_cost,
        name="joined",
    )(place, *gates, first, second, *held, *untouched)


def small_call(kernel, name, out_shape, scalars, arrays, waits, scratch=()):
    return pl.pallas_call(
        functools.partial(kernel, waits=len(waits)),
        in_specs=[pl.BlockSpec(memory_space=pltpu.SMEM)] * len(scalars)
        + [pl.BlockSpec(memory_space=pltpu.VMEM)] * len(arrays)
        + [pl.BlockSpec(memory_space=pl.ANY)] * len(waits),
        out_shape=out_shape,
        scratch_shapes=scratch,
        compiler_params=pltpu.CompilerParams(vmem_limit_bytes=vmem_bytes),
        cost_estimate=tiny_cost,
        name=name,
    )(*scalars, *arrays, *waits)


def product_half(left, right, half):
    size = left.shape[1] // 2
    return lax.dot_general(
        left[:, half * size : (half + 1) * size],
        right[...],
        contract_first,
        preferred_element_type=f32,
    )


def early_send_kernel(core_ref, gated_ref, cot_ref, normed_ref, gate_grad_ref, *rest, waits):
    out_ref = rest[waits]
    size = out_ref.shape[0] // 2
    for core, left, right in ((1, gated_ref, cot_ref), (0, normed_ref, gate_grad_ref)):

        @pl.when(core_ref[0] == core)
        def _():
            for half in range(2):
                rows = slice(half * size, (half + 1) * size)
                out_ref[rows, :] = product_half(left, right, half).astype(bf16)


def early_first_kernel(
    core_ref,
    upper_ref,
    gated_ref,
    cot_ref,
    normed_ref,
    gate_grad_ref,
    arrived_ref,
    *rest,
    waits,
):
    keep_ref, send_ref = rest[waits:]
    size = keep_ref.shape[0]
    for core, left, right in ((0, gated_ref, cot_ref), (1, normed_ref, gate_grad_ref)):
        for half in range(2):
            for mine in range(2):

                @pl.when((core_ref[0] == core) & ((upper_ref[0] == half) == (mine == 1)))
                def _():
                    rows = slice(half * size, (half + 1) * size)
                    total = product_half(left, right, half) + arrived_ref[rows, :].astype(f32)
                    if mine:
                        keep_ref[...] = total
                    else:
                        send_ref[...] = total.astype(bf16)


def fold_kernel(upper_ref, keep_ref, arrived_ref, *rest, waits):
    out_ref, send_ref = rest[waits:]
    size = out_ref.shape[0]
    mine = pl.ds(pl.multiple_of(upper_ref[0] * size, size), size)
    other = pl.ds(pl.multiple_of((1 - upper_ref[0]) * size, size), size)
    out_ref[...] = keep_ref[mine, :] + arrived_ref[mine, :].astype(f32)
    send_ref[...] = (keep_ref[other, :] + arrived_ref[other, :].astype(f32)).astype(bf16)


def folded(keep, arrived, bits, *waits):
    rows, width = keep.shape
    kinds = [jax.ShapeDtypeStruct((rows // 2, width), kind) for kind in (f32, bf16)]
    return small_call(fold_kernel, "folded", kinds, [early_upper(bits)], [keep, arrived], waits)


def settle_kernel(keep_ref, arrived_ref, *rest, waits):
    rest[waits][...] = (keep_ref[...] + arrived_ref[...].astype(f32)).astype(bf16)


def settled(keep, arrived, *waits):
    kind = jax.ShapeDtypeStruct(keep.shape, bf16)
    return small_call(settle_kernel, "settled", kind, [], [keep, arrived], waits)


def unfold_kernel(upper_ref, held_ref, arrived_ref, *rest, waits):
    out_ref = rest[waits]
    size = held_ref.shape[0]
    out_ref[pl.ds(pl.multiple_of(upper_ref[0] * size, size), size), :] = held_ref[...]
    out_ref[pl.ds(pl.multiple_of((1 - upper_ref[0]) * size, size), size), :] = arrived_ref[...]


def unfolded(held, arrived, bits, *waits):
    rows, width = held.shape
    kind = jax.ShapeDtypeStruct((2 * rows, width), bf16)
    return small_call(
        unfold_kernel, "unfolded", kind, [early_upper(bits)], [held, arrived], waits
    )


def widen_kernel(place_ref, own_ref, other_ref, wait_ref, out_ref):
    out_ref[...] = jnp.where(place_ref[0] & 1 == 1, other_ref[...], own_ref[...]).astype(f32)


def widened(place, own, other, wait):
    rows, width = own.shape
    block = pl.BlockSpec((rows // 4, width), lambda j: (j, 0))
    return pl.pallas_call(
        widen_kernel,
        grid=(4,),
        in_specs=[pl.BlockSpec(memory_space=pltpu.SMEM), block, block]
        + [pl.BlockSpec(memory_space=pl.ANY)],
        out_specs=block,
        out_shape=jax.ShapeDtypeStruct((rows, width), f32),
        cost_estimate=tiny_cost,
        name="widened",
    )(place, own, other, wait)


def through(decay, total):
    return jnp.exp(decay * total)


def round_kernel(second_ref, decay_log_ref, own_ref, other_ref, passed_ref, new_passed_ref, *ends_refs):
    count = decay_log_ref.shape[0]
    decay = -jnp.exp(decay_log_ref[...])
    second = second_ref[0] > 0

    def split(ref):
        return ref[:count], ref[count : 2 * count], ref[2 * count : 2 * count + 1]

    own, other = split(own_ref), split(other_ref)
    early = [jnp.where(second, b, a) for a, b in zip(own, other)]
    late = [jnp.where(second, a, b) for a, b in zip(own, other)]
    state = late[0] + through(decay, late[2]) * early[0]
    adjoint = early[1] + through(decay, early[2]) * late[1]
    if len(ends_refs) == 2:
        ends_refs[0][...] = state
        ends_refs[1][...] = adjoint
    else:
        ends_refs[0][:count, :] = state
        ends_refs[0][count : 2 * count, :] = adjoint
        ends_refs[0][2 * count :, :] = jnp.broadcast_to(early[2] + late[2], (8, decay.shape[1]))
    before, after = passed_ref[:count], passed_ref[count : 2 * count]
    before_steps = passed_ref[2 * count : 2 * count + 1]
    after_steps = passed_ref[2 * count + 1 : 2 * count + 2]
    new_passed_ref[:count, :] = before + jnp.where(second, through(decay, before_steps) * other[0], 0.0)
    new_passed_ref[count : 2 * count, :] = after + jnp.where(
        second, 0.0, through(decay, after_steps) * other[1]
    )
    new_passed_ref[2 * count : 2 * count + 1, :] = before_steps + jnp.where(second, other[2], 0.0)
    new_passed_ref[2 * count + 1 : 2 * count + 2, :] = after_steps + jnp.where(second, 0.0, other[2])


def carried(ends, decay_log):
    count, width = decay_log.shape
    place = lax.axis_index("wide").astype(jnp.int32)
    passed = jnp.zeros((2 * count + 8, width), f32)
    packed = ends
    vmem = pl.BlockSpec(memory_space=pltpu.VMEM)
    for k, kinds in enumerate(([ends], [decay_log, decay_log])):
        passed, *out = pl.pallas_call(
            round_kernel,
            in_specs=[pl.BlockSpec(memory_space=pltpu.SMEM)] + [vmem] * 4,
            out_shape=[jax.ShapeDtypeStruct(kind.shape, f32) for kind in [passed] + kinds],
            cost_estimate=tiny_cost,
            name="carry_round",
        )((place >> k & 1)[None], decay_log, packed, swapped(packed, "wide", 2**k), passed)
        packed = out[0]
    from_before = passed_along(out[0], "wide", 4)
    from_after = passed_along(out[1], "wide", -4)
    return passed, from_before, from_after


def local(
    tokens,
    norm_gain,
    in_weight,
    conv_weight,
    conv_bias,
    select_weight,
    step_weight,
    step_bias,
    decay_log,
    skip_gain,
    out_weight,
    segment_ids,
    cotangent,
):
    rows, features = tokens.shape
    taps = conv_weight.shape[0]
    columns = select_weight.shape[0]
    rank = step_weight.shape[0]
    count = decay_log.shape[0]
    right_half = lax.axis_index("narrow") == 1

    def both_halves(own, other):
        return jnp.concatenate(
            [jnp.where(right_half, other, own), jnp.where(right_half, own, other)], axis=1
        )

    other_tokens = swapped(tokens, "narrow", 1)
    other_cot = swapped(cotangent, "narrow", 1)
    edge, other_edge = to_next_both(edge_rows_of(segment_ids, tokens))

    whole_low, normed_ext, normed, inverse, masks = normalized(
        tokens, other_tokens, edge, other_edge, norm_gain[None], segment_ids[None]
    )
    projected = jnp.einsum(
        "td,dce->cte", normed_ext, in_weight, preferred_element_type=f32
    ).astype(bf16)
    convolved, act, selected = convolve(
        projected, conv_weight, conv_bias[None], select_weight, masks
    )
    other_selected = swapped(selected, "narrow", 1)
    cot_whole = both_halves(cotangent, other_cot)
    gated_grad = lax.dot_general(
        cot_whole, out_weight, contract_last, preferred_element_type=f32
    )
    step_pre, step, ends = scan_ends(
        selected,
        other_selected,
        step_weight,
        step_bias[None],
        act,
        projected,
        gated_grad,
        masks,
        decay_log,
    )
    passed, entering, returning = carried(ends, decay_log)
    gated, gate_grad, entry = scan_forward(
        selected,
        other_selected,
        step,
        act,
        projected,
        gated_grad,
        masks,
        decay_log,
        passed,
        entering,
        skip_gain[None],
    )
    wide_place = lax.axis_index("wide").astype(jnp.int32)
    four_place = (wide_place & 3)[None]
    first_bits, *more_bits = group_bits(2)
    whole = whole_low.astype(f32)

    def narrow_halves(array):
        low, high = array[:, :features], array[:, features:]
        return jnp.where(right_half, high, low), jnp.where(right_half, low, high)

    steps = early_bits()
    core = (wide_place & 1)[None]
    factors = [gated, cot_whole, normed, gate_grad]
    size, depth = out_weight.shape[0], cot_whole.shape[1]
    send = small_call(
        early_send_kernel,
        "early_send",
        jax.ShapeDtypeStruct((size, depth), bf16),
        [core],
        factors,
        [returning],
    )
    arrived = swapped(send, "wide", 1)
    out_part = jnp.dot(gated, out_weight, preferred_element_type=f32)
    out_mine, out_other = narrow_halves(out_part)
    early, send = small_call(
        early_first_kernel,
        "early_first",
        [jax.ShapeDtypeStruct((size // 2, depth), kind) for kind in (f32, bf16)],
        [core, early_upper(steps[0])],
        [*factors, arrived],
        [out_other],
    )
    arrived = early_swapped(send, steps[0])
    out_theirs = swapped(out_other, "narrow", 1)
    select_grad = jnp.zeros(selected.shape, f32)
    waits, act_grads, scan_smalls = [send, out_other], [], []
    for part in range(2):
        act_grad, select_grad, scan_small = scan_backward(
            part,
            selected,
            other_selected,
            step_pre,
            step,
            act,
            projected,
            gated_grad,
            masks,
            decay_log,
            entry,
            passed,
            returning,
            skip_gain[None],
            step_weight,
            select_grad,
            waits,
        )
        act_grads.append(act_grad)
        scan_smalls.append(scan_small)
        if part == 0:
            early, send = folded(early, arrived, steps[1], select_grad)
            arrived = early_swapped(send, steps[1])
            waits = [send, out_other]
    layer_out = (tokens.astype(f32) + (out_mine + out_theirs)).astype(bf16)
    normed_four = quarter_of_four(after(normed, select_grad))
    inner_main, before, last, conv_small = convolve_grad(
        select_grad,
        swapped(select_grad, "narrow", 1),
        select_weight,
        act_grads,
        convolved,
        act,
        projected,
        conv_weight,
        masks,
        [out_theirs],
    )
    following = passed_along(before, "wide", -1)
    for bits in steps[2:]:
        early, send = folded(early, arrived, bits, conv_small, *normed_four)
        arrived = early_swapped(send, bits)
    inner_grad = patched(segment_ids, inner_main, last, following, send)
    near = swapped(inner_grad, "wide", 2)
    far = swapped(inner_grad, "wide", 1)
    keep, *sends = small_quarters(four_place, scan_smalls, conv_small, inner_grad)
    smalls = [keep] + [swapped(sends[n - 1], "wide", n) for n in (1, 2, 3)]
    normed_part = jnp.einsum(
        "cte,dce->td", jnp.stack([inner_grad, gate_grad]), in_weight, preferred_element_type=f32
    )
    gain_part = jnp.sum(normed_part * whole * inverse, axis=0, keepdims=True)
    row_part = jnp.sum(normed_part * norm_gain * whole, axis=1)[None]
    gain_sum = gain_part + swapped(gain_part, "narrow", 1)
    for bit in (bit for bits in more_bits for bit in bits):
        gain_sum = gain_sum + swapped(gain_sum, "wide", bit)
    early = settled(early, arrived, gain_part, *sends)
    for bits in steps[:1:-1]:
        back = early_swapped(early, bits)
        early = unfolded(early, back, bits, *smalls[1:])
    back = early_swapped(early, steps[1])
    normed_mine, normed_other = narrow_halves(normed_part)
    row_theirs = swapped(row_part, "narrow", 1)
    normed_theirs = swapped(normed_other, "narrow", 1)
    near = after(near, early, gain_sum, row_theirs, *smalls[1:])
    last = swapped(near, "wide", 1)
    keep, *sends = inner_quarter(
        (wide_place >> 2 & 3)[None],
        inner_grad,
        near,
        far,
        last,
        normed_four,
        smalls,
        [],
    )
    row_sum = (row_part + row_theirs).reshape(rows, 1)
    gain_mine = jnp.where(right_half, norm_gain[features:], norm_gain[:features])
    whole_grad = inverse * (gain_mine * (normed_mine + normed_theirs)) - tokens.astype(f32) * (
        inverse * inverse * inverse
    ) * (row_sum / (2 * features))
    tokens_grad = (whole_grad + cotangent.astype(f32)).astype(bf16)
    arrived = [swapped(sends[n - 1], "wide", flips(first_bits)[n]) for n in (1, 2, 3)]
    arrived[0] = after(arrived[0], normed_theirs)
    held = keep + sum(a.astype(f32) for a in arrived)
    for bits in more_bits:
        held = scattered(held, bits)
    held = held.astype(bf16)
    for bits in reversed(more_bits):
        held = gathered(held, bits)
    spare = jnp.broadcast_to(gain_sum, (block_rows - used_rows, gain_sum.shape[1]))
    held = jnp.concatenate([held[: held.shape[0] - spare.shape[0]], spare.astype(bf16)])
    early = unfolded(early, back, steps[1], held)
    early = unfolded(early, early_swapped(early, steps[0]), steps[0])
    held = gathered(held, first_bits, early)
    core_early = swapped(early, "wide", 1)
    core = swapped(held, "wide", 1)
    out_weight_grad = widened(four_place, early, core_early, core)
    gates = (early, core_early)
    (begun,) = joined(
        four_place, 0, gates, held, core, (), (layer_out, tokens_grad, out_weight_grad)
    )
    near = after(swapped(held, "wide", 2), begun)
    far = swapped(near, "wide", 1)
    conv_at = rank + count + 2
    (
        in_weight_grad,
        step_weight_grad,
        decay_log_grad,
        skip_gain_grad,
        step_bias_grad,
        select_weight_grad,
        conv_weight_grad,
        conv_bias_grad,
        norm_gain_grad,
    ) = joined(
        four_place,
        2,
        gates,
        near,
        far,
        (begun,),
        (),
        (held, core, near, far),
        (0, rank, rank + count, rank + count + 1, conv_at, conv_at + columns, conv_at + columns + taps),
        (rank, count, 1, 1, columns, taps, 1, 1),
    )
    return (
        layer_out,
        tokens_grad,
        norm_gain_grad[0],
        in_weight_grad,
        conv_weight_grad,
        conv_bias_grad[0],
        select_weight_grad,
        step_weight_grad,
        step_bias_grad[0],
        decay_log_grad,
        skip_gain_grad[0],
        out_weight_grad,
    )


def solution(mesh):
    placed = (
        P("wide", "narrow"),
        P(),
        P(None, None, "narrow"),
        P(None, "narrow"),
        P("narrow"),
        P(None, "narrow"),
        P(None, "narrow"),
        P("narrow"),
        P(None, "narrow"),
        P("narrow"),
        P("narrow", None),
        P("wide"),
        P("wide", "narrow"),
    )
    return jax.shard_map(
        local,
        mesh=mesh,
        in_specs=placed,
        out_specs=(
            P("wide", "narrow"),
            P("wide", "narrow"),
            P(),
            P(None, None, "narrow"),
            P(None, "narrow"),
            P("narrow"),
            P(None, "narrow"),
            P(None, "narrow"),
            P("narrow"),
            P(None, "narrow"),
            P("narrow"),
            P("narrow", None),
        ),
        check_vma=False,
    )
```

```python
import functools

import jax
import jax.numpy as jnp
from jax import lax
from jax.experimental import pallas as pl
from jax.experimental.pallas import tpu as pltpu
from jax.sharding import PartitionSpec as P

epsilon = 1e-05
log2e = 1.4426950408889634
reset_step = 1e30
lanes = 128
halo = 16
body_rows = 32
scan_width = 512
vmem_bytes = 56 * 1024 * 1024
tiny_cost = pl.CostEstimate(flops=1, bytes_accessed=1, transcendentals=0)
f32 = jnp.float32
bf16 = jnp.bfloat16
contract_first = (((0,), (0,)), ((), ()))
contract_last = (((1,), (1,)), ((), ()))


def passed_along(array, axis, by):
    peers = lax.axis_size(axis)
    pairs = [(i, i + by) for i in range(peers) if 0 <= i + by < peers]
    return lax.ppermute(array, axis, pairs)


def swapped(array, axis, bit):
    peers = lax.axis_size(axis)
    return lax.ppermute(array, axis, [(i, i ^ bit) for i in range(peers)])


def wide_bits():
    bit, bits = 1, []
    while bit < lax.axis_size("wide"):
        bits.append(bit)
        bit *= 2
    return bits


def to_next_both(array):
    count, sides = lax.axis_size("wide"), lax.axis_size("narrow")
    pairs = [
        (i * sides + k, (i + 1) * sides + (sides - 1 - k))
        for i in range(count - 1)
        for k in range(sides)
    ]
    return passed_along(array, "wide", 1), lax.ppermute(array, ("wide", "narrow"), pairs)


def is_upper(bit):
    return (lax.axis_index("wide") & bit) != 0


def group_bits(size):
    bits, bit = [], 4
    while bit < lax.axis_size("wide"):
        bits.append(bit)
        bit *= 2
    return [tuple(bits[k : k + size]) for k in range(0, len(bits), size)]


def flips(bits):
    return [sum(b for k, b in enumerate(bits) if n >> k & 1) for n in range(2 ** len(bits))]


def scattered(piece, bits):
    rows = piece.shape[0] // 2 ** len(bits)
    here = sum(is_upper(b).astype(jnp.int32) << k for k, b in enumerate(bits))

    def block(n):
        return lax.dynamic_slice_in_dim(piece, (here ^ n) * rows, rows, 0)

    total = block(0).astype(f32)
    for n, flip in enumerate(flips(bits)):
        if n > 0:
            total = total + swapped(block(n).astype(bf16), "wide", flip).astype(f32)
    return total


def gathered(held, bits, *waits):
    blocks = [held] + [swapped(held, "wide", flip) for flip in flips(bits)[1:]]
    if waits:
        blocks[1] = after(blocks[1], *waits)
    for bit in bits:
        upper = is_upper(bit)
        blocks = [
            jnp.concatenate([jnp.where(upper, b, a), jnp.where(upper, a, b)])
            for a, b in zip(blocks[0::2], blocks[1::2])
        ]
    return blocks[0]


def early_bits():
    bits, bit = [], 2
    while bit < lax.axis_size("wide"):
        bits.append(bit)
        bit *= 2
    return list(zip(bits, bits[1:] + bits[:1]))


def early_upper(bits):
    place = lax.axis_index("wide")
    return jnp.where(place & 1 == 0, place & bits[0] != 0, place & bits[1] != 0).astype(jnp.int32)[None]


def early_swapped(array, bits):
    peers = lax.axis_size("wide")
    return lax.ppermute(array, "wide", [(i, i ^ bits[i % 2]) for i in range(peers)])


def quarter_of_four(array):
    width = array.shape[1] // 4
    here = lax.axis_index("wide") & 3

    def quarter(n):
        return lax.dynamic_slice_in_dim(array, (here ^ n) * width, width, 1)

    return [quarter(0)] + [swapped(quarter(n), "wide", n) for n in (2, 1, 3)]


def silu_slope(values):
    logistic = jax.nn.sigmoid(values)
    return logistic * (1.0 + values * (1.0 - logistic))


def softplus(values):
    return jnp.maximum(values, 0.0) + jnp.log1p(jnp.exp(-jnp.abs(values)))


def column_spec(rows, start=0):
    return pl.BlockSpec((rows, scan_width), lambda j: (0, start + j))


def part_spec(part, rows, start=0):
    return pl.BlockSpec((None, rows, scan_width), lambda j: (part, 0, start + j))


def whole_spec(rows, width):
    return pl.BlockSpec((rows, width), lambda j: (0, 0))


def call(kernel, name, width, in_specs, out_specs, out_shape, scratch, *operands):
    return pl.pallas_call(
        kernel,
        grid=(width // scan_width,),
        in_specs=in_specs,
        out_specs=out_specs,
        out_shape=out_shape,
        scratch_shapes=scratch,
        compiler_params=pltpu.CompilerParams(vmem_limit_bytes=vmem_bytes),
        cost_estimate=tiny_cost,
        name=name,
    )(*operands)


def conv_kernel(
    inner_ref,
    conv_weight_ref,
    conv_bias_ref,
    select_ref,
    mask_ref,
    convolved_ref,
    act_ref,
    selected_ref,
    inner,
):
    rows = act_ref.shape[0]
    taps = conv_weight_ref.shape[0]
    inner[:halo, :] = inner_ref[rows:, :].astype(f32)
    inner[halo:, :] = inner_ref[:rows, :].astype(f32)
    total = conv_bias_ref[...] + conv_weight_ref[taps - 1 :, :] * inner[halo:, :]
    for lag in range(1, taps):
        earlier = inner[pl.ds(halo - lag, rows), :] * mask_ref[:, lag : lag + 1]
        total = total + conv_weight_ref[taps - 1 - lag : taps - lag, :] * earlier
    convolved_ref[...] = total
    act = (total * jax.nn.sigmoid(total)).astype(bf16)
    act_ref[...] = act
    part = lax.dot_general(select_ref[...], act, contract_last, preferred_element_type=f32)

    @pl.when(pl.program_id(0) == 0)
    def _():
        selected_ref[...] = part

    @pl.when(pl.program_id(0) > 0)
    def _():
        selected_ref[...] += part


def convolve(projected, conv_weight, conv_bias, select_weight, masks):
    parts, extended, width = projected.shape
    rows = extended - halo
    taps = conv_weight.shape[0]
    columns = select_weight.shape[0]
    return call(
        conv_kernel,
        "convolve",
        width,
        [
            part_spec(0, extended),
            column_spec(taps),
            column_spec(1),
            column_spec(columns),
            whole_spec(rows, masks.shape[1]),
        ],
        [column_spec(rows), column_spec(rows), whole_spec(columns, rows)],
        [
            jax.ShapeDtypeStruct((rows, width), f32),
            jax.ShapeDtypeStruct((rows, width), bf16),
            jax.ShapeDtypeStruct((columns, rows), f32),
        ],
        [pltpu.VMEM((extended, scan_width), f32)],
        projected,
        conv_weight,
        conv_bias,
        select_weight,
        masks,
    )


def coef_columns(coef, block):
    per_tile = lanes // body_rows
    start = pl.multiple_of((block // per_tile) * lanes, lanes)
    tile = coef[:, pl.ds(start, lanes)]
    back = body_rows * lax.rem(block, per_tile)
    return pltpu.roll(tile, lax.rem(lanes - back, lanes), 1)


def ends_kernel(
    selected_ref,
    other_ref,
    step_weight_ref,
    step_bias_ref,
    act_ref,
    gate_ref,
    gated_grad_ref,
    mask_ref,
    decay_log_ref,
    step_pre_ref,
    step_ref,
    ends_ref,
    coef,
    held_step,
    drive,
    scan_grad,
):
    rows = act_ref.shape[0]
    count = decay_log_ref.shape[0]
    rank = step_weight_ref.shape[0]
    decay2 = -jnp.exp(decay_log_ref[...]) * log2e
    selected = selected_ref[...] + other_ref[...]
    coef[...] = selected[rank:, :]
    step_low = selected[:rank, :].astype(bf16)
    step_pre = step_bias_ref[...] + lax.dot_general(
        step_low, step_weight_ref[...], contract_first, preferred_element_type=f32
    )
    step_pre_ref[...] = step_pre
    step = softplus(step_pre)
    step_ref[...] = step
    held_step[...] = jnp.where(mask_ref[:, 1:2] > 0.0, step, reset_step)
    drive[...] = step * act_ref[...].astype(f32)
    gate = gate_ref[...].astype(f32)
    scan_grad[...] = gated_grad_ref[...] * (gate * jax.nn.sigmoid(gate))
    zero = jnp.zeros(decay2.shape, f32)

    def body(block, carried):
        state, product, adjoint = carried
        columns = coef_columns(coef, block)
        for i in range(body_rows):
            row = pl.ds(block * body_rows + i, 1)
            factor = jnp.exp2(held_step[row, :] * decay2)
            state = factor * state + columns[:count, i : i + 1] * drive[row, :]
            product = factor * product
            adjoint = adjoint + product * (columns[count:, i : i + 1] * scan_grad[row, :])
        return state, product, adjoint

    state, product, adjoint = lax.fori_loop(0, rows // body_rows, body, (zero, zero + 1.0, zero))
    ends_ref[:count, :] = state
    ends_ref[count : 2 * count, :] = adjoint
    total = jnp.sum(held_step[...], axis=0, keepdims=True)
    ends_ref[2 * count :, :] = jnp.broadcast_to(total, (8, total.shape[1]))


def scan_ends(
    selected, other, step_weight, step_bias, act, projected, gated_grad, masks, decay_log
):
    rows, width = act.shape
    count = decay_log.shape[0]
    columns = selected.shape[0]
    rank = step_weight.shape[0]
    return call(
        ends_kernel,
        "scan_ends",
        width,
        [
            whole_spec(columns, rows),
            whole_spec(columns, rows),
            column_spec(rank),
            column_spec(1),
            column_spec(rows),
            part_spec(1, rows),
            column_spec(rows),
            whole_spec(rows, masks.shape[1]),
            column_spec(count),
        ],
        [column_spec(rows), column_spec(rows), column_spec(2 * count + 8)],
        [
            jax.ShapeDtypeStruct((rows, width), f32),
            jax.ShapeDtypeStruct((rows, width), f32),
            jax.ShapeDtypeStruct((2 * count + 8, width), f32),
        ],
        [pltpu.VMEM((2 * count, rows), f32)] + [pltpu.VMEM((rows, scan_width), f32)] * 3,
        selected,
        other,
        step_weight,
        step_bias,
        act,
        projected,
        gated_grad,
        masks,
        decay_log,
    )


def lane_tiles(values):
    return [values[:, k : k + lanes] for k in range(0, values.shape[1], lanes)]


def tree_sum(parts):
    while len(parts) > 1:
        odd = parts[len(parts) // 2 * 2 :]
        parts = [a + b for a, b in zip(parts[0::2], parts[1::2])] + odd
    return parts[0]


def keep_halves(scratch, i, values):
    for k, tile in enumerate(lane_tiles(values)):
        at = (k * body_rows + i) * 8
        scratch[at : at + 8, :] = tile[:8] + tile[8:]


def put_state_sums(scratch, out_ref, block):
    for group in range(body_rows // 8):
        row = pl.ds(pl.multiple_of(block * body_rows + group * 8, 8), 8)
        for k in range(out_ref.shape[1] // lanes):
            at = (k * body_rows + group * 8) * 8
            total = tree_sum([scratch[pl.ds(at + n, 8, stride=8), :] for n in range(8)])
            out_ref[row, k * lanes : (k + 1) * lanes] = total


def lane_sums(values):
    ones = jnp.ones((8, lanes), bf16)
    high = values.astype(bf16)
    low = (values - high.astype(f32)).astype(bf16)
    total = lax.dot_general(ones, high, contract_last, preferred_element_type=f32)
    total += lax.dot_general(ones, low, contract_last, preferred_element_type=f32)
    return total[:1, :]


def at_token(t, count):
    return pl.ds(pl.multiple_of(t * count, count), count)


def forward_kernel(
    selected_ref,
    other_ref,
    step_ref,
    act_ref,
    gate_ref,
    gated_grad_ref,
    mask_ref,
    decay_log_ref,
    passed_ref,
    entering_ref,
    skip_ref,
    gated_ref,
    gate_grad_ref,
    entry_ref,
    coef,
    held_step,
    drive,
    scanned,
    halves,
):
    rows = step_ref.shape[0]
    count = decay_log_ref.shape[0]
    rank = selected_ref.shape[0] - 2 * count
    decay = -jnp.exp(decay_log_ref[...])
    decay2 = decay * log2e
    before_steps = passed_ref[2 * count : 2 * count + 1, :]
    entry = passed_ref[:count, :] + through(decay, before_steps) * entering_ref[...]
    entry_ref[...] = entry
    coef[...] = selected_ref[rank:, :] + other_ref[rank:, :]
    act = act_ref[...].astype(f32)
    held_step[...] = jnp.where(mask_ref[:, 1:2] > 0.0, step_ref[...], reset_step)
    drive[...] = step_ref[...] * act

    def forward(block, state):
        columns = coef_columns(coef, block)
        for i in range(body_rows):
            row = pl.ds(block * body_rows + i, 1)
            factor = jnp.exp2(held_step[row, :] * decay2)
            state = factor * state + columns[:count, i : i + 1] * drive[row, :]
            keep_halves(halves, i, columns[count:, i : i + 1] * state)
        put_state_sums(halves, scanned, block)
        return state

    lax.fori_loop(0, rows // body_rows, forward, entry)
    gate = gate_ref[...].astype(f32)
    logistic = jax.nn.sigmoid(gate)
    total = scanned[...] + skip_ref[...] * act
    gated_ref[...] = (total * (gate * logistic)).astype(bf16)
    slope = logistic * (1.0 + gate * (1.0 - logistic))
    gate_grad_ref[...] = (gated_grad_ref[...] * total * slope).astype(bf16)


def scan_forward(
    selected, other, step, act, projected, gated_grad, masks, decay_log, passed, entering, skip_gain
):
    rows, width = step.shape
    count = decay_log.shape[0]
    columns = selected.shape[0]
    return call(
        forward_kernel,
        "scan_forward",
        width,
        [
            whole_spec(columns, rows),
            whole_spec(columns, rows),
            column_spec(rows),
            column_spec(rows),
            part_spec(1, rows),
            column_spec(rows),
            whole_spec(rows, masks.shape[1]),
            column_spec(count),
            column_spec(2 * count + 8),
            column_spec(count),
            column_spec(1),
        ],
        [column_spec(rows), column_spec(rows), column_spec(count)],
        [
            jax.ShapeDtypeStruct((rows, width), bf16),
            jax.ShapeDtypeStruct((rows, width), bf16),
            jax.ShapeDtypeStruct((count, width), f32),
        ],
        [pltpu.VMEM((2 * count, rows), f32)]
        + [pltpu.VMEM((rows, scan_width), f32)] * 3
        + [pltpu.VMEM((8 * body_rows * (scan_width // lanes), lanes), f32)],
        selected,
        other,
        step,
        act,
        projected,
        gated_grad,
        masks,
        decay_log,
        passed,
        entering,
        skip_gain,
    )


def backward_kernel(
    selected_ref,
    other_ref,
    step_pre_ref,
    step_ref,
    act_ref,
    gate_ref,
    gated_grad_ref,
    mask_ref,
    decay_log_ref,
    entry_ref,
    passed_ref,
    returning_ref,
    skip_ref,
    step_weight_ref,
    earlier_ref,
    first_wait,
    second_wait,
    act_grad_ref,
    select_grad_ref,
    small_ref,
    coef,
    held_step,
    drive,
    scan_grad,
    weighted,
    held_sum,
    states,
    factors,
    halves,
    more_halves,
    in_sum,
    read_sum,
):
    rows = step_ref.shape[0]
    count = decay_log_ref.shape[0]
    rank = step_weight_ref.shape[0]
    blocks = rows // body_rows
    decay = -jnp.exp(decay_log_ref[...])
    decay2 = decay * log2e
    after_steps = passed_ref[2 * count + 1 : 2 * count + 2, :]
    tail = passed_ref[count : 2 * count, :] + through(decay, after_steps) * returning_ref[...]
    selected = selected_ref[...] + other_ref[...]
    coef[...] = selected[rank:, :]
    step_low = selected[:rank, :].astype(bf16)
    step = step_ref[...]
    act = act_ref[...].astype(f32)
    held_step[...] = jnp.where(mask_ref[:, 1:2] > 0.0, step, reset_step)
    drive[...] = step * act
    gate = gate_ref[...].astype(f32)
    grads = gated_grad_ref[...] * (gate * jax.nn.sigmoid(gate))
    scan_grad[...] = grads
    small_ref[rank + count : rank + count + 1, :] = jnp.sum(grads * act, axis=0, keepdims=True)
    states[:count, :] = entry_ref[...]

    def forward(block, state):
        columns = coef_columns(coef, block)
        for i in range(body_rows):
            t = block * body_rows + i
            row = pl.ds(t, 1)
            factor = jnp.exp2(held_step[row, :] * decay2)
            state = factor * state + columns[:count, i : i + 1] * drive[row, :]
            factors[at_token(t, count), :] = factor
            states[at_token(t + 1, count), :] = state
        return state

    lax.fori_loop(0, blocks, forward, entry_ref[...])

    def backward(k, carried):
        adjoint, decay_grad = carried
        block = blocks - 1 - k
        columns = coef_columns(coef, block)
        for i in range(body_rows - 1, -1, -1):
            t = block * body_rows + i
            row = pl.ds(t, 1)
            here = at_token(t, count)
            grad = scan_grad[row, :]
            summed = columns[count:, i : i + 1] * grad + adjoint
            read_sum[here, :] = tree_sum(lane_tiles(grad * states[at_token(t + 1, count), :]))
            in_sum[here, :] = tree_sum(lane_tiles(summed * drive[row, :]))
            keep_halves(halves, i, summed * columns[:count, i : i + 1])
            adjoint = factors[here, :] * summed
            held = adjoint * states[here, :]
            decay_grad = decay_grad + held * step_ref[row, :]
            keep_halves(more_halves, i, held * decay)
        put_state_sums(halves, weighted, block)
        put_state_sums(more_halves, held_sum, block)
        return adjoint, decay_grad

    ignored, decay_grad = lax.fori_loop(
        0, blocks, backward, (tail, jnp.zeros(decay.shape, f32))
    )
    act_grad_ref[...] = step * weighted[...] + skip_ref[...] * scan_grad[...]
    step_grad = act * weighted[...] + held_sum[...]
    pre_grad = (step_grad * jax.nn.sigmoid(step_pre_ref[...])).astype(bf16)
    small_ref[:rank, :] = jnp.dot(step_low, pre_grad, preferred_element_type=f32)
    small_ref[rank : rank + count, :] = decay_grad * decay
    bias_grad = jnp.sum(pre_grad.astype(f32), axis=0, keepdims=True)
    small_ref[rank + count + 1 : rank + count + 2, :] = bias_grad
    select_grad_ref[:rank, :] = earlier_ref[:rank, :] + lax.dot_general(
        step_weight_ref[...], pre_grad, contract_last, preferred_element_type=f32
    )
    for n in range(count):
        at = pl.ds(n, rows, stride=count)
        for sums, start in ((in_sum, rank), (read_sum, rank + count)):
            row = slice(start + n, start + n + 1)
            select_grad_ref[row, :] = earlier_ref[row, :] + lane_sums(sums[at, :])


def scan_backward(
    part,
    selected,
    other,
    step_pre,
    step,
    act,
    projected,
    gated_grad,
    masks,
    decay_log,
    entry,
    passed,
    returning,
    skip_gain,
    step_weight,
    earlier,
    waits,
):
    rows, width = step.shape[0], scan_width
    count = decay_log.shape[0]
    columns = selected.shape[0]
    rank = step_weight.shape[0]
    half_rows = 8 * body_rows * (scan_width // lanes)
    small = rank + count + 2
    return call(
        backward_kernel,
        "scan_backward",
        width,
        [
            whole_spec(columns, rows),
            whole_spec(columns, rows),
            column_spec(rows, part),
            column_spec(rows, part),
            column_spec(rows, part),
            part_spec(1, rows, part),
            column_spec(rows, part),
            whole_spec(rows, masks.shape[1]),
            column_spec(count, part),
            column_spec(count, part),
            column_spec(2 * count + 8, part),
            column_spec(count, part),
            column_spec(1, part),
            column_spec(rank, part),
            whole_spec(columns, rows),
        ]
        + [pl.BlockSpec(memory_space=pl.ANY)] * 2,
        [column_spec(rows), whole_spec(columns, rows), column_spec(small)],
        [
            jax.ShapeDtypeStruct((rows, width), f32),
            jax.ShapeDtypeStruct((columns, rows), f32),
            jax.ShapeDtypeStruct((small, width), f32),
        ],
        [pltpu.VMEM((2 * count, rows), f32)]
        + [pltpu.VMEM((rows, scan_width), f32)] * 5
        + [
            pltpu.VMEM(((rows + 1) * count, scan_width), f32),
            pltpu.VMEM((rows * count, scan_width), f32),
            pltpu.VMEM((half_rows, lanes), f32),
            pltpu.VMEM((half_rows, lanes), f32),
            pltpu.VMEM((rows * count, lanes), f32),
            pltpu.VMEM((rows * count, lanes), f32),
        ],
        selected,
        other,
        step_pre,
        step,
        act,
        projected,
        gated_grad,
        masks,
        decay_log,
        entry,
        passed,
        returning,
        skip_gain,
        step_weight,
        earlier,
        *waits,
    )


def conv_grad_kernel(
    select_grad_ref,
    other_ref,
    select_ref,
    first_act_grad,
    second_act_grad,
    convolved_ref,
    act_ref,
    inner_ref,
    conv_weight_ref,
    mask_ref,
    *rest,
):
    inner_grad_ref, before_ref, last_ref, small_ref, inner, shifted = rest[-6:]
    rows = act_ref.shape[0]
    taps = conv_weight_ref.shape[0]
    columns = select_ref.shape[0]
    select_grad = (select_grad_ref[...] + other_ref[...]).astype(bf16)
    act_grad = jnp.where(pl.program_id(0) == 0, first_act_grad[...], second_act_grad[...])
    total = act_grad + lax.dot_general(
        select_grad, select_ref[...], contract_first, preferred_element_type=f32
    )
    conv_grad = total * silu_slope(convolved_ref[...])
    small_ref[:columns, :] = jnp.dot(select_grad, act_ref[...], preferred_element_type=f32)
    inner[:halo, :] = inner_ref[rows:, :].astype(f32)
    inner[halo:, :] = inner_ref[:rows, :].astype(f32)
    edges = jnp.zeros((8, conv_grad.shape[1]), f32)
    shifted[:8, :] = edges
    shifted[rows + 8 :, :] = edges
    out = conv_weight_ref[taps - 1 :, :] * conv_grad
    before = edges
    small_ref[columns + taps - 1 : columns + taps, :] = jnp.sum(
        conv_grad * inner[halo:, :], axis=0, keepdims=True
    )
    for lag in range(1, taps):
        masked = conv_grad * mask_ref[:, lag : lag + 1]
        at = taps - 1 - lag
        small_ref[columns + at : columns + at + 1, :] = jnp.sum(
            masked * inner[pl.ds(halo - lag, rows), :], axis=0, keepdims=True
        )
        shifted[8 : rows + 8, :] = masked
        weight = conv_weight_ref[at : at + 1, :]
        out = out + weight * shifted[pl.ds(8 + lag, rows), :]
        before = before + weight * shifted[pl.ds(lag, 8), :]
    small_ref[columns + taps : columns + taps + 1, :] = jnp.sum(conv_grad, axis=0, keepdims=True)
    inner_grad_ref[...] = out.astype(bf16)
    before_ref[...] = before
    last_ref[...] = out[rows - 8 :, :]


def convolve_grad(
    select_grad, other, select_weight, act_grads, convolved, act, projected, conv_weight, masks, waits
):
    rows, width = act.shape
    extended = rows + halo
    columns = select_weight.shape[0]
    taps = conv_weight.shape[0]
    small = columns + taps + 1
    return call(
        conv_grad_kernel,
        "convolve_grad",
        width,
        [
            whole_spec(columns, rows),
            whole_spec(columns, rows),
            column_spec(columns),
            whole_spec(rows, scan_width),
            whole_spec(rows, scan_width),
            column_spec(rows),
            column_spec(rows),
            part_spec(0, extended),
            column_spec(taps),
            whole_spec(rows, masks.shape[1]),
        ]
        + [pl.BlockSpec(memory_space=pl.ANY)] * len(waits),
        [column_spec(rows), column_spec(8), column_spec(8), column_spec(small)],
        [
            jax.ShapeDtypeStruct((rows, width), bf16),
            jax.ShapeDtypeStruct((8, width), f32),
            jax.ShapeDtypeStruct((8, width), f32),
            jax.ShapeDtypeStruct((small, width), f32),
        ],
        [pltpu.VMEM((extended, scan_width), f32), pltpu.VMEM((rows + 16, scan_width), f32)],
        select_grad,
        other,
        select_weight,
        *act_grads,
        convolved,
        act,
        projected,
        conv_weight,
        masks,
        *waits,
    )


def normalize_kernel(
    own_ref,
    other_ref,
    edge_ref,
    other_edge_ref,
    gain_ref,
    ids_ref,
    whole_ref,
    extended_ref,
    normed_ref,
    inverse_ref,
    mask_ref,
    rows_ref,
):
    rows, half = own_ref.shape
    ids = ids_ref[...].astype(f32)
    place = lax.broadcasted_iota(jnp.int32, ids.shape, 1)
    same = []
    for lag in range(8):
        earlier = jnp.where(place < lag, ids[:, :1], pltpu.roll(ids, lag, 1)) if lag else ids
        same.append(jnp.where(earlier == ids, 1.0, 0.0))
    spare = jnp.zeros((lanes - 8, rows), f32)
    mask_ref[...] = jnp.concatenate(same + [spare]).T
    right = lax.axis_index("narrow") == 1
    for at, own, other in ((0, own_ref, other_ref), (rows, edge_ref, other_edge_ref)):
        end = at + own.shape[0]
        rows_ref[at:end, :half] = jnp.where(right, other[...], own[...])
        rows_ref[at:end, half:] = jnp.where(right, own[...], other[...])
    whole_ref[...] = rows_ref[:rows, :]
    whole = rows_ref[...].astype(f32)
    inverse = lax.rsqrt(jnp.mean(whole * whole, axis=1, keepdims=True) + epsilon)
    normed = (whole * inverse * gain_ref[...]).astype(bf16)
    extended_ref[...] = normed
    normed_ref[...] = normed[:rows]
    inverse_ref[...] = inverse[:rows]


def normalized(own, other, edge, other_edge, gain, ids):
    rows, half = own.shape
    extended = rows + edge.shape[0]
    return pl.pallas_call(
        normalize_kernel,
        out_shape=[
            jax.ShapeDtypeStruct((rows, 2 * half), bf16),
            jax.ShapeDtypeStruct((extended, 2 * half), bf16),
            jax.ShapeDtypeStruct((rows, 2 * half), bf16),
            jax.ShapeDtypeStruct((rows, 1), f32),
            jax.ShapeDtypeStruct((rows, lanes), f32),
        ],
        scratch_shapes=[pltpu.VMEM((extended, 2 * half), bf16)],
        cost_estimate=tiny_cost,
        name="normalized",
    )(own, other, edge, other_edge, gain, ids)


def after(array, *waits):
    anywhere = pl.BlockSpec(memory_space=pl.ANY)
    return pl.pallas_call(
        lambda *refs: None,
        in_specs=[anywhere] * (1 + len(waits)),
        out_specs=anywhere,
        out_shape=jax.ShapeDtypeStruct(array.shape, array.dtype),
        input_output_aliases={0: 0},
        cost_estimate=tiny_cost,
        name="after",
    )(array, *waits)


def patch_kernel(ids_ref, rows_ref, last_ref, next_ref, *rest):
    count = ids_ref.shape[0]
    place = lax.broadcasted_iota(jnp.int32, (8, 1), 0)
    same = jnp.zeros((8, 1), f32)
    for lag in range(8):
        here = jnp.where(ids_ref[count - 1 - lag] == ids_ref[count - 1], 1.0, 0.0)
        same = same + jnp.where(place == 7 - lag, here, 0.0)
    total = last_ref[...] + next_ref[...] * same
    rows = rows_ref[...].astype(f32)
    rest[-1][...] = jnp.concatenate([rows[: halo - 8], total]).astype(bf16)


def patched(ids, grads, last, following, *waits):
    rows, width = grads.shape
    block = pl.BlockSpec((halo, width), lambda j: (rows // halo - 1, 0))
    edge = pl.BlockSpec((8, width), lambda j: (0, 0))
    return pl.pallas_call(
        patch_kernel,
        grid=(1,),
        in_specs=[pl.BlockSpec(memory_space=pltpu.SMEM), block, edge, edge]
        + [pl.BlockSpec(memory_space=pl.ANY)] * len(waits),
        out_specs=block,
        out_shape=jax.ShapeDtypeStruct((rows, width), bf16),
        input_output_aliases={1: 0},
        cost_estimate=tiny_cost,
        name="patched",
    )(ids, grads, last, following, *waits)


def edge_kernel(ids_ref, tokens_ref, out_ref):
    rows = ids_ref.shape[0]
    taps = 4
    out_ref[...] = tokens_ref[...]
    place = lax.broadcasted_iota(jnp.int32, (halo, 1), 0)
    same = jnp.zeros((halo, 1), f32)
    for lag in range(taps):
        here = jnp.where(ids_ref[rows - 1 - lag] == ids_ref[rows - 1], 1.0, 0.0)
        same = same + jnp.where(place == halo - 1 - lag, here, 0.0)
    out_ref[...] = (tokens_ref[...].astype(f32) * same).astype(bf16)


def edge_rows_of(ids, tokens):
    rows, width = tokens.shape
    return pl.pallas_call(
        edge_kernel,
        grid=(1,),
        in_specs=[
            pl.BlockSpec(memory_space=pltpu.SMEM),
            pl.BlockSpec((halo, width), lambda j: (rows // halo - 1, 0)),
        ],
        out_specs=pl.BlockSpec((halo, width), lambda j: (0, 0)),
        out_shape=jax.ShapeDtypeStruct((halo, width), bf16),
        cost_estimate=tiny_cost,
        name="edge_rows",
    )(ids, tokens)


block_rows, used_rows = 16, 12


def small_kernel(place_ref, first_scan, second_scan, conv_ref, wait_ref, keep_ref, *rest):
    *sends_refs, rows, blocks = rest
    rows[...] = jnp.zeros(rows.shape, f32)
    count = first_scan.shape[0]
    rows[:count, :scan_width] = first_scan[...]
    rows[:count, scan_width:] = second_scan[...]
    rows[count : count + conv_ref.shape[0], :] = conv_ref[...]
    blocks[...] = jnp.zeros(blocks.shape, f32)
    for n in range(16):
        blocks[n * block_rows : n * block_rows + used_rows, :] = rows[
            n * used_rows : (n + 1) * used_rows, :
        ]
    quarter = keep_ref.shape[0]
    for n in range(4):
        start = pl.multiple_of((place_ref[0] ^ n) * quarter, quarter)
        block = blocks[pl.ds(start, quarter), :]
        if n == 0:
            keep_ref[...] = block
        else:
            sends_refs[n - 1][...] = block.astype(bf16)


def small_quarters(place, scan_smalls, conv_small, wait):
    width = conv_small.shape[1]
    return pl.pallas_call(
        small_kernel,
        in_specs=[pl.BlockSpec(memory_space=pltpu.SMEM)]
        + [pl.BlockSpec(memory_space=pltpu.VMEM)] * 3
        + [pl.BlockSpec(memory_space=pl.ANY)],
        out_shape=[jax.ShapeDtypeStruct((4 * block_rows, width), f32)]
        + [jax.ShapeDtypeStruct((4 * block_rows, width), bf16)] * 3,
        scratch_shapes=[
            pltpu.VMEM((16 * used_rows, width), f32),
            pltpu.VMEM((16 * block_rows, width), f32),
        ],
        cost_estimate=tiny_cost,
        name="small_quarters",
    )(place, *scan_smalls, conv_small, wait)


def quarter_kernel(
    place_ref,
    own_ref,
    near_ref,
    far_ref,
    normed_0,
    normed_1,
    normed_2,
    normed_3,
    small_ref,
    first_ref,
    second_ref,
    third_ref,
    *rest,
):
    keep_ref, *sends_refs, piece, small = rest[-6:]
    total = None
    tokens = own_ref.shape[0]
    grads = (own_ref[...], near_ref[...], far_ref[:tokens, :], far_ref[tokens:, :])
    for left, right in zip((normed_0, normed_1, normed_2, normed_3), grads):
        part = lax.dot_general(left[...], right, contract_first, preferred_element_type=f32)
        total = part if total is None else total + part
    piece[...] = total
    small[...] = small_ref[...] + sum(
        ref[...].astype(f32) for ref in (first_ref, second_ref, third_ref)
    )
    rows, spare = piece.shape[0] // 4, small.shape[0] // 4
    for n in range(4):
        block = place_ref[0] ^ n
        inner_rows = piece[pl.ds(pl.multiple_of(block * rows, rows), rows), :]
        small_rows = small[pl.ds(pl.multiple_of(block * spare, spare), spare), :]
        if n == 0:
            keep_ref[:rows, :] = inner_rows
            keep_ref[rows:, :] = small_rows
        else:
            sends_refs[n - 1][:rows, :] = inner_rows.astype(bf16)
            sends_refs[n - 1][rows:, :] = small_rows.astype(bf16)


def inner_quarter(place, own, near, far, normed, smalls, waits):
    width = own.shape[1]
    quarter = normed[0].shape[1]
    spare = smalls[0].shape[0]
    rows = (quarter + spare) // 4
    return pl.pallas_call(
        quarter_kernel,
        in_specs=[pl.BlockSpec(memory_space=pltpu.SMEM)]
        + [pl.BlockSpec(memory_space=pltpu.VMEM)] * 11
        + [pl.BlockSpec(memory_space=pl.ANY)] * len(waits),
        out_shape=[jax.ShapeDtypeStruct((rows, width), f32)]
        + [jax.ShapeDtypeStruct((rows, width), bf16)] * 3,
        scratch_shapes=[pltpu.VMEM((quarter, width), f32), pltpu.VMEM((spare, width), f32)],
        compiler_params=pltpu.CompilerParams(vmem_limit_bytes=vmem_bytes),
        cost_estimate=tiny_cost,
        name="inner_quarter",
    )(place, own, near, far, *normed, *smalls, *waits)


def join_kernel(place_ref, own_gate, other_gate, first_ref, second_ref, *rest, small_rows):
    at_end = 2 + len(small_rows) if small_rows else 0
    out_ref = rest[-1 - at_end]
    step = pl.program_id(0)
    rows = out_ref.shape[0] // 2
    second_core = place_ref[0] & 1 == 1
    out_ref[:, 1, :] = jnp.where(second_core, own_gate[...], other_gate[...]).astype(f32)

    def put(ref):
        for n in range(2):
            at = n * (rows + block_rows)
            out_ref[n * rows : (n + 1) * rows, 0, :] = ref[at : at + rows, :].astype(f32)

    @pl.when(step < 2)
    def _():
        put(first_ref)

    @pl.when(step >= 2)
    def _():
        put(second_ref)

    if not small_rows:
        return
    *row_refs, gain_ref, blocks = rest[-at_end:]

    @pl.when(step == 3)
    def _():
        for flip, ref in enumerate(rest[:4]):
            for n in range(4):
                at = ((place_ref[0] ^ flip) * 4 + n) * block_rows
                taken = ref[(n + 1) * rows + n * block_rows : (n + 1) * (rows + block_rows), :]
                blocks[pl.ds(pl.multiple_of(at, block_rows), block_rows), :] = taken.astype(f32)
        for ref, start in zip(row_refs, small_rows):
            for row in range(ref.shape[0]):
                at = (start + row) // used_rows * block_rows + (start + row) % used_rows
                ref[row : row + 1, :] = blocks[at : at + 1, :]
        gain_ref[...] = sum(
            blocks[n * block_rows + used_rows : n * block_rows + used_rows + 1, :] for n in range(16)
        )


def joined(place, flip, gates, first, second, before, waits, held=(), small_rows=(), small_counts=()):
    depth, width = gates[0].shape
    quarter = depth // 4
    block = quarter // 2
    piece = first.shape[0] // 2

    def target(j, place):
        return 2 * (place[0] ^ (flip + j // 2)) + lax.rem(j, 2)

    vmem = pl.BlockSpec(memory_space=pltpu.VMEM)
    untouched = [*before, *waits]
    return pl.pallas_call(
        functools.partial(join_kernel, small_rows=small_rows),
        grid_spec=pltpu.PrefetchScalarGridSpec(
            num_scalar_prefetch=1,
            grid=(4,),
            in_specs=[
                pl.BlockSpec((block, width), lambda j, place: (target(j, place), 0)),
                pl.BlockSpec((block, width), lambda j, place: (target(j, place), 0)),
                pl.BlockSpec((piece, width), lambda j, place: (jnp.minimum(j, 1), 0)),
                pl.BlockSpec((piece, width), lambda j, place: (jnp.maximum(j - 2, 0), 0)),
            ]
            + [vmem] * len(held)
            + [pl.BlockSpec(memory_space=pl.ANY)] * len(untouched),
            out_specs=[pl.BlockSpec((block, 2, width), lambda j, place: (target(j, place), 0, 0))]
            + [pl.BlockSpec((rows, width), lambda j, place: (0, 0)) for rows in small_counts],
            scratch_shapes=[pltpu.VMEM((16 * block_rows, width), f32)] if small_rows else [],
        ),
        out_shape=[jax.ShapeDtypeStruct((depth, 2, width), f32)]
        + [jax.ShapeDtypeStruct((rows, width), f32) for rows in small_counts],
        input_output_aliases={5 + len(held) + k: k for k in range(len(before))},
        compiler_params=pltpu.CompilerParams(vmem_limit_bytes=vmem_bytes),
        cost_estimate=tiny_cost,
        name="joined",
    )(place, *gates, first, second, *held, *untouched)


def small_call(kernel, name, out_shape, scalars, arrays, waits, scratch=()):
    return pl.pallas_call(
        functools.partial(kernel, waits=len(waits)),
        in_specs=[pl.BlockSpec(memory_space=pltpu.SMEM)] * len(scalars)
        + [pl.BlockSpec(memory_space=pltpu.VMEM)] * len(arrays)
        + [pl.BlockSpec(memory_space=pl.ANY)] * len(waits),
        out_shape=out_shape,
        scratch_shapes=scratch,
        compiler_params=pltpu.CompilerParams(vmem_limit_bytes=vmem_bytes),
        cost_estimate=tiny_cost,
        name=name,
    )(*scalars, *arrays, *waits)


def product_half(left, right, half):
    size = left.shape[1] // 2
    return lax.dot_general(
        left[:, half * size : (half + 1) * size],
        right[...],
        contract_first,
        preferred_element_type=f32,
    )


def early_send_kernel(core_ref, gated_ref, cot_ref, normed_ref, gate_grad_ref, *rest, waits):
    out_ref = rest[waits]
    size = out_ref.shape[0] // 2
    for core, left, right in ((1, gated_ref, cot_ref), (0, normed_ref, gate_grad_ref)):

        @pl.when(core_ref[0] == core)
        def _():
            for half in range(2):
                rows = slice(half * size, (half + 1) * size)
                out_ref[rows, :] = product_half(left, right, half).astype(bf16)


def early_first_kernel(
    core_ref,
    upper_ref,
    gated_ref,
    cot_ref,
    normed_ref,
    gate_grad_ref,
    arrived_ref,
    *rest,
    waits,
):
    keep_ref, send_ref = rest[waits:]
    size = keep_ref.shape[0]
    for core, left, right in ((0, gated_ref, cot_ref), (1, normed_ref, gate_grad_ref)):
        for half in range(2):
            for mine in range(2):

                @pl.when((core_ref[0] == core) & ((upper_ref[0] == half) == (mine == 1)))
                def _():
                    rows = slice(half * size, (half + 1) * size)
                    total = product_half(left, right, half) + arrived_ref[rows, :].astype(f32)
                    if mine:
                        keep_ref[...] = total
                    else:
                        send_ref[...] = total.astype(bf16)


def fold_kernel(upper_ref, keep_ref, arrived_ref, *rest, waits):
    out_ref, send_ref = rest[waits:]
    size = out_ref.shape[0]
    mine = pl.ds(pl.multiple_of(upper_ref[0] * size, size), size)
    other = pl.ds(pl.multiple_of((1 - upper_ref[0]) * size, size), size)
    out_ref[...] = keep_ref[mine, :] + arrived_ref[mine, :].astype(f32)
    send_ref[...] = (keep_ref[other, :] + arrived_ref[other, :].astype(f32)).astype(bf16)


def folded(keep, arrived, bits, *waits):
    rows, width = keep.shape
    kinds = [jax.ShapeDtypeStruct((rows // 2, width), kind) for kind in (f32, bf16)]
    return small_call(fold_kernel, "folded", kinds, [early_upper(bits)], [keep, arrived], waits)


def settle_kernel(keep_ref, arrived_ref, *rest, waits):
    rest[waits][...] = (keep_ref[...] + arrived_ref[...].astype(f32)).astype(bf16)


def settled(keep, arrived, *waits):
    kind = jax.ShapeDtypeStruct(keep.shape, bf16)
    return small_call(settle_kernel, "settled", kind, [], [keep, arrived], waits)


def unfold_kernel(upper_ref, held_ref, arrived_ref, *rest, waits):
    out_ref = rest[waits]
    size = held_ref.shape[0]
    out_ref[pl.ds(pl.multiple_of(upper_ref[0] * size, size), size), :] = held_ref[...]
    out_ref[pl.ds(pl.multiple_of((1 - upper_ref[0]) * size, size), size), :] = arrived_ref[...]


def unfolded(held, arrived, bits, *waits):
    rows, width = held.shape
    kind = jax.ShapeDtypeStruct((2 * rows, width), bf16)
    return small_call(
        unfold_kernel, "unfolded", kind, [early_upper(bits)], [held, arrived], waits
    )


def widen_kernel(place_ref, own_ref, other_ref, wait_ref, out_ref):
    out_ref[...] = jnp.where(place_ref[0] & 1 == 1, other_ref[...], own_ref[...]).astype(f32)


def widened(place, own, other, wait):
    rows, width = own.shape
    block = pl.BlockSpec((rows // 4, width), lambda j: (j, 0))
    return pl.pallas_call(
        widen_kernel,
        grid=(4,),
        in_specs=[pl.BlockSpec(memory_space=pltpu.SMEM), block, block]
        + [pl.BlockSpec(memory_space=pl.ANY)],
        out_specs=block,
        out_shape=jax.ShapeDtypeStruct((rows, width), f32),
        cost_estimate=tiny_cost,
        name="widened",
    )(place, own, other, wait)


def through(decay, total):
    return jnp.exp(decay * total)


def round_kernel(second_ref, decay_log_ref, own_ref, other_ref, passed_ref, new_passed_ref, *ends_refs):
    count = decay_log_ref.shape[0]
    decay = -jnp.exp(decay_log_ref[...])
    second = second_ref[0] > 0

    def split(ref):
        return ref[:count], ref[count : 2 * count], ref[2 * count : 2 * count + 1]

    own, other = split(own_ref), split(other_ref)
    early = [jnp.where(second, b, a) for a, b in zip(own, other)]
    late = [jnp.where(second, a, b) for a, b in zip(own, other)]
    state = late[0] + through(decay, late[2]) * early[0]
    adjoint = early[1] + through(decay, early[2]) * late[1]
    if len(ends_refs) == 2:
        ends_refs[0][...] = state
        ends_refs[1][...] = adjoint
    else:
        ends_refs[0][:count, :] = state
        ends_refs[0][count : 2 * count, :] = adjoint
        ends_refs[0][2 * count :, :] = jnp.broadcast_to(early[2] + late[2], (8, decay.shape[1]))
    before, after = passed_ref[:count], passed_ref[count : 2 * count]
    before_steps = passed_ref[2 * count : 2 * count + 1]
    after_steps = passed_ref[2 * count + 1 : 2 * count + 2]
    new_passed_ref[:count, :] = before + jnp.where(second, through(decay, before_steps) * other[0], 0.0)
    new_passed_ref[count : 2 * count, :] = after + jnp.where(
        second, 0.0, through(decay, after_steps) * other[1]
    )
    new_passed_ref[2 * count : 2 * count + 1, :] = before_steps + jnp.where(second, other[2], 0.0)
    new_passed_ref[2 * count + 1 : 2 * count + 2, :] = after_steps + jnp.where(second, 0.0, other[2])


def carried(ends, decay_log):
    count, width = decay_log.shape
    place = lax.axis_index("wide").astype(jnp.int32)
    passed = jnp.zeros((2 * count + 8, width), f32)
    packed = ends
    vmem = pl.BlockSpec(memory_space=pltpu.VMEM)
    for k, kinds in enumerate(([ends], [decay_log, decay_log])):
        passed, *out = pl.pallas_call(
            round_kernel,
            in_specs=[pl.BlockSpec(memory_space=pltpu.SMEM)] + [vmem] * 4,
            out_shape=[jax.ShapeDtypeStruct(kind.shape, f32) for kind in [passed] + kinds],
            cost_estimate=tiny_cost,
            name="carry_round",
        )((place >> k & 1)[None], decay_log, packed, swapped(packed, "wide", 2**k), passed)
        packed = out[0]
    from_before = passed_along(out[0], "wide", 4)
    from_after = passed_along(out[1], "wide", -4)
    return passed, from_before, from_after


def local(
    tokens,
    norm_gain,
    in_weight,
    conv_weight,
    conv_bias,
    select_weight,
    step_weight,
    step_bias,
    decay_log,
    skip_gain,
    out_weight,
    segment_ids,
    cotangent,
):
    rows, features = tokens.shape
    taps = conv_weight.shape[0]
    columns = select_weight.shape[0]
    rank = step_weight.shape[0]
    count = decay_log.shape[0]
    right_half = lax.axis_index("narrow") == 1

    def both_halves(own, other):
        return jnp.concatenate(
            [jnp.where(right_half, other, own), jnp.where(right_half, own, other)], axis=1
        )

    other_tokens = swapped(tokens, "narrow", 1)
    other_cot = swapped(cotangent, "narrow", 1)
    edge, other_edge = to_next_both(edge_rows_of(segment_ids, tokens))

    whole_low, normed_ext, normed, inverse, masks = normalized(
        tokens, other_tokens, edge, other_edge, norm_gain[None], segment_ids[None]
    )
    projected = jnp.einsum(
        "td,dce->cte", normed_ext, in_weight, preferred_element_type=f32
    ).astype(bf16)
    convolved, act, selected = convolve(
        projected, conv_weight, conv_bias[None], select_weight, masks
    )
    other_selected = swapped(selected, "narrow", 1)
    cot_whole = both_halves(cotangent, other_cot)
    gated_grad = lax.dot_general(
        cot_whole, out_weight, contract_last, preferred_element_type=f32
    )
    step_pre, step, ends = scan_ends(
        selected,
        other_selected,
        step_weight,
        step_bias[None],
        act,
        projected,
        gated_grad,
        masks,
        decay_log,
    )
    passed, entering, returning = carried(ends, decay_log)
    gated, gate_grad, entry = scan_forward(
        selected,
        other_selected,
        step,
        act,
        projected,
        gated_grad,
        masks,
        decay_log,
        passed,
        entering,
        skip_gain[None],
    )
    wide_place = lax.axis_index("wide").astype(jnp.int32)
    four_place = (wide_place & 3)[None]
    first_bits, *more_bits = group_bits(2)
    whole = whole_low.astype(f32)

    def narrow_halves(array):
        low, high = array[:, :features], array[:, features:]
        return jnp.where(right_half, high, low), jnp.where(right_half, low, high)

    steps = early_bits()
    core = (wide_place & 1)[None]
    factors = [gated, cot_whole, normed, gate_grad]
    size, depth = out_weight.shape[0], cot_whole.shape[1]
    send = small_call(
        early_send_kernel,
        "early_send",
        jax.ShapeDtypeStruct((size, depth), bf16),
        [core],
        factors,
        [returning],
    )
    arrived = swapped(send, "wide", 1)
    out_part = jnp.dot(gated, out_weight, preferred_element_type=f32)
    out_mine, out_other = narrow_halves(out_part)
    early, send = small_call(
        early_first_kernel,
        "early_first",
        [jax.ShapeDtypeStruct((size // 2, depth), kind) for kind in (f32, bf16)],
        [core, early_upper(steps[0])],
        [*factors, arrived],
        [out_other],
    )
    arrived = early_swapped(send, steps[0])
    out_theirs = swapped(out_other, "narrow", 1)
    select_grad = jnp.zeros(selected.shape, f32)
    waits, act_grads, scan_smalls = [send, out_other], [], []
    for part in range(2):
        act_grad, select_grad, scan_small = scan_backward(
            part,
            selected,
            other_selected,
            step_pre,
            step,
            act,
            projected,
            gated_grad,
            masks,
            decay_log,
            entry,
            passed,
            returning,
            skip_gain[None],
            step_weight,
            select_grad,
            waits,
        )
        act_grads.append(act_grad)
        scan_smalls.append(scan_small)
        if part == 0:
            early, send = folded(early, arrived, steps[1], select_grad)
            arrived = early_swapped(send, steps[1])
            waits = [send, out_other]
    layer_out = (tokens.astype(f32) + (out_mine + out_theirs)).astype(bf16)
    normed_four = quarter_of_four(after(normed, select_grad))
    inner_main, before, last, conv_small = convolve_grad(
        select_grad,
        swapped(select_grad, "narrow", 1),
        select_weight,
        act_grads,
        convolved,
        act,
        projected,
        conv_weight,
        masks,
        [out_theirs],
    )
    following = passed_along(before, "wide", -1)
    for bits in steps[2:]:
        early, send = folded(early, arrived, bits, conv_small, *normed_four)
        arrived = early_swapped(send, bits)
    inner_grad = patched(segment_ids, inner_main, last, following, send)
    near = swapped(inner_grad, "wide", 2)
    early = settled(early, arrived, inner_grad)
    keep, *sends = small_quarters(four_place, scan_smalls, conv_small, early)
    smalls = [keep] + [swapped(sends[n - 1], "wide", n) for n in (1, 2, 3)]
    normed_part = jnp.einsum(
        "cte,dce->td", jnp.stack([inner_grad, gate_grad]), in_weight, preferred_element_type=f32
    )
    gain_part = jnp.sum(normed_part * whole * inverse, axis=0, keepdims=True)
    row_part = jnp.sum(normed_part * norm_gain * whole, axis=1)[None]
    gain_sum = gain_part + swapped(gain_part, "narrow", 1)
    for bit in (bit for bits in more_bits for bit in bits):
        gain_sum = gain_sum + swapped(gain_sum, "wide", bit)
    near = after(near, gain_part, *smalls[1:])
    far = swapped(jnp.concatenate([inner_grad, near]), "wide", 1)
    normed_mine, normed_other = narrow_halves(normed_part)
    row_theirs = swapped(row_part, "narrow", 1)
    normed_theirs = swapped(normed_other, "narrow", 1)
    keep, *sends = inner_quarter(
        (wide_place >> 2 & 3)[None],
        inner_grad,
        near,
        far,
        normed_four,
        smalls,
        [gain_sum, row_theirs],
    )
    for bits in steps[:1:-1]:
        early = unfolded(early, early_swapped(early, bits), bits, keep)
    back = early_swapped(early, steps[1])
    row_sum = (row_part + row_theirs).reshape(rows, 1)
    gain_mine = jnp.where(right_half, norm_gain[features:], norm_gain[:features])
    whole_grad = inverse * (gain_mine * (normed_mine + normed_theirs)) - tokens.astype(f32) * (
        inverse * inverse * inverse
    ) * (row_sum / (2 * features))
    tokens_grad = (whole_grad + cotangent.astype(f32)).astype(bf16)
    arrived = [swapped(sends[n - 1], "wide", flips(first_bits)[n]) for n in (1, 2, 3)]
    arrived[0] = after(arrived[0], normed_theirs, early)
    held = keep + sum(a.astype(f32) for a in arrived)
    for bits in more_bits:
        held = scattered(held, bits)
    held = held.astype(bf16)
    for bits in reversed(more_bits):
        held = gathered(held, bits)
    spare = jnp.broadcast_to(gain_sum, (block_rows - used_rows, gain_sum.shape[1]))
    held = jnp.concatenate([held[: held.shape[0] - spare.shape[0]], spare.astype(bf16)])
    early = unfolded(early, back, steps[1], held)
    back = early_swapped(early, steps[0])
    held = gathered(held, first_bits, early)
    core = swapped(held, "wide", 1)
    early = unfolded(early, back, steps[0], core)
    core_early = swapped(early, "wide", 1)
    out_weight_grad = widened(four_place, early, core_early, core)
    gates = (early, core_early)
    (begun,) = joined(
        four_place, 0, gates, held, core, (), (layer_out, tokens_grad, out_weight_grad)
    )
    near = after(swapped(held, "wide", 2), begun)
    far = swapped(near, "wide", 1)
    conv_at = rank + count + 2
    (
        in_weight_grad,
        step_weight_grad,
        decay_log_grad,
        skip_gain_grad,
        step_bias_grad,
        select_weight_grad,
        conv_weight_grad,
        conv_bias_grad,
        norm_gain_grad,
    ) = joined(
        four_place,
        2,
        gates,
        near,
        far,
        (begun,),
        (),
        (held, core, near, far),
        (0, rank, rank + count, rank + count + 1, conv_at, conv_at + columns, conv_at + columns + taps),
        (rank, count, 1, 1, columns, taps, 1, 1),
    )
    return (
        layer_out,
        tokens_grad,
        norm_gain_grad[0],
        in_weight_grad,
        conv_weight_grad,
        conv_bias_grad[0],
        select_weight_grad,
        step_weight_grad,
        step_bias_grad[0],
        decay_log_grad,
        skip_gain_grad[0],
        out_weight_grad,
    )


def solution(mesh):
    placed = (
        P("wide", "narrow"),
        P(),
        P(None, None, "narrow"),
        P(None, "narrow"),
        P("narrow"),
        P(None, "narrow"),
        P(None, "narrow"),
        P("narrow"),
        P(None, "narrow"),
        P("narrow"),
        P("narrow", None),
        P("wide"),
        P("wide", "narrow"),
    )
    return jax.shard_map(
        local,
        mesh=mesh,
        in_specs=placed,
        out_specs=(
            P("wide", "narrow"),
            P("wide", "narrow"),
            P(),
            P(None, None, "narrow"),
            P(None, "narrow"),
            P("narrow"),
            P(None, "narrow"),
            P(None, "narrow"),
            P("narrow"),
            P(None, "narrow"),
            P("narrow"),
            P("narrow", None),
        ),
        check_vma=False,
    )
```

```python
import functools

import jax
import jax.numpy as jnp
from jax import lax
from jax.experimental import pallas as pl
from jax.experimental.pallas import tpu as pltpu
from jax.sharding import PartitionSpec as P

epsilon = 1e-05
log2e = 1.4426950408889634
reset_step = 1e30
lanes = 128
halo = 16
body_rows = 32
scan_width = 512
vmem_bytes = 56 * 1024 * 1024
tiny_cost = pl.CostEstimate(flops=1, bytes_accessed=1, transcendentals=0)
f32 = jnp.float32
bf16 = jnp.bfloat16
contract_first = (((0,), (0,)), ((), ()))
contract_last = (((1,), (1,)), ((), ()))


def passed_along(array, axis, by):
    peers = lax.axis_size(axis)
    pairs = [(i, i + by) for i in range(peers) if 0 <= i + by < peers]
    return lax.ppermute(array, axis, pairs)


def swapped(array, axis, bit):
    peers = lax.axis_size(axis)
    return lax.ppermute(array, axis, [(i, i ^ bit) for i in range(peers)])


def wide_bits():
    bit, bits = 1, []
    while bit < lax.axis_size("wide"):
        bits.append(bit)
        bit *= 2
    return bits


def to_next_both(array):
    count, sides = lax.axis_size("wide"), lax.axis_size("narrow")
    pairs = [
        (i * sides + k, (i + 1) * sides + (sides - 1 - k))
        for i in range(count - 1)
        for k in range(sides)
    ]
    return passed_along(array, "wide", 1), lax.ppermute(array, ("wide", "narrow"), pairs)


def is_upper(bit):
    return (lax.axis_index("wide") & bit) != 0


def group_bits(size):
    bits, bit = [], 4
    while bit < lax.axis_size("wide"):
        bits.append(bit)
        bit *= 2
    return [tuple(bits[k : k + size]) for k in range(0, len(bits), size)]


def flips(bits):
    return [sum(b for k, b in enumerate(bits) if n >> k & 1) for n in range(2 ** len(bits))]


def scattered(piece, bits):
    rows = piece.shape[0] // 2 ** len(bits)
    here = sum(is_upper(b).astype(jnp.int32) << k for k, b in enumerate(bits))

    def block(n):
        return lax.dynamic_slice_in_dim(piece, (here ^ n) * rows, rows, 0)

    total = block(0).astype(f32)
    for n, flip in enumerate(flips(bits)):
        if n > 0:
            total = total + swapped(block(n).astype(bf16), "wide", flip).astype(f32)
    return total


def gathered(held, bits):
    blocks = [held] + [swapped(held, "wide", flip) for flip in flips(bits)[1:]]
    for bit in bits:
        upper = is_upper(bit)
        blocks = [
            jnp.concatenate([jnp.where(upper, b, a), jnp.where(upper, a, b)])
            for a, b in zip(blocks[0::2], blocks[1::2])
        ]
    return blocks[0]


def quarter_of_four(array):
    width = array.shape[1] // 4
    here = lax.axis_index("wide") & 3

    def quarter(n):
        return lax.dynamic_slice_in_dim(array, (here ^ n) * width, width, 1)

    return [quarter(0)] + [swapped(quarter(n), "wide", n) for n in (2, 1, 3)]


def silu_slope(values):
    logistic = jax.nn.sigmoid(values)
    return logistic * (1.0 + values * (1.0 - logistic))


def softplus(values):
    return jnp.maximum(values, 0.0) + jnp.log1p(jnp.exp(-jnp.abs(values)))


def column_spec(rows, start=0):
    return pl.BlockSpec((rows, scan_width), lambda j: (0, start + j))


def part_spec(part, rows, start=0):
    return pl.BlockSpec((None, rows, scan_width), lambda j: (part, 0, start + j))


def whole_spec(rows, width):
    return pl.BlockSpec((rows, width), lambda j: (0, 0))


def call(kernel, name, width, in_specs, out_specs, out_shape, scratch, *operands):
    return pl.pallas_call(
        kernel,
        grid=(width // scan_width,),
        in_specs=in_specs,
        out_specs=out_specs,
        out_shape=out_shape,
        scratch_shapes=scratch,
        compiler_params=pltpu.CompilerParams(vmem_limit_bytes=vmem_bytes),
        cost_estimate=tiny_cost,
        name=name,
    )(*operands)


def conv_kernel(
    inner_ref,
    conv_weight_ref,
    conv_bias_ref,
    select_ref,
    mask_ref,
    convolved_ref,
    act_ref,
    selected_ref,
    inner,
):
    rows = act_ref.shape[0]
    taps = conv_weight_ref.shape[0]
    inner[:halo, :] = inner_ref[rows:, :].astype(f32)
    inner[halo:, :] = inner_ref[:rows, :].astype(f32)
    total = conv_bias_ref[...] + conv_weight_ref[taps - 1 :, :] * inner[halo:, :]
    for lag in range(1, taps):
        earlier = inner[pl.ds(halo - lag, rows), :] * mask_ref[:, lag : lag + 1]
        total = total + conv_weight_ref[taps - 1 - lag : taps - lag, :] * earlier
    convolved_ref[...] = total
    act = (total * jax.nn.sigmoid(total)).astype(bf16)
    act_ref[...] = act
    part = lax.dot_general(select_ref[...], act, contract_last, preferred_element_type=f32)

    @pl.when(pl.program_id(0) == 0)
    def _():
        selected_ref[...] = part

    @pl.when(pl.program_id(0) > 0)
    def _():
        selected_ref[...] += part


def convolve(projected, conv_weight, conv_bias, select_weight, masks):
    parts, extended, width = projected.shape
    rows = extended - halo
    taps = conv_weight.shape[0]
    columns = select_weight.shape[0]
    return call(
        conv_kernel,
        "convolve",
        width,
        [
            part_spec(0, extended),
            column_spec(taps),
            column_spec(1),
            column_spec(columns),
            whole_spec(rows, masks.shape[1]),
        ],
        [column_spec(rows), column_spec(rows), whole_spec(columns, rows)],
        [
            jax.ShapeDtypeStruct((rows, width), f32),
            jax.ShapeDtypeStruct((rows, width), bf16),
            jax.ShapeDtypeStruct((columns, rows), f32),
        ],
        [pltpu.VMEM((extended, scan_width), f32)],
        projected,
        conv_weight,
        conv_bias,
        select_weight,
        masks,
    )


def coef_columns(coef, block):
    per_tile = lanes // body_rows
    start = pl.multiple_of((block // per_tile) * lanes, lanes)
    tile = coef[:, pl.ds(start, lanes)]
    back = body_rows * lax.rem(block, per_tile)
    return pltpu.roll(tile, lax.rem(lanes - back, lanes), 1)


def ends_kernel(
    selected_ref,
    other_ref,
    step_weight_ref,
    step_bias_ref,
    act_ref,
    gate_ref,
    gated_grad_ref,
    mask_ref,
    decay_log_ref,
    step_pre_ref,
    step_ref,
    ends_ref,
    coef,
    held_step,
    drive,
    scan_grad,
):
    rows = act_ref.shape[0]
    count = decay_log_ref.shape[0]
    rank = step_weight_ref.shape[0]
    decay2 = -jnp.exp(decay_log_ref[...]) * log2e
    selected = selected_ref[...] + other_ref[...]
    coef[...] = selected[rank:, :]
    step_low = selected[:rank, :].astype(bf16)
    step_pre = step_bias_ref[...] + lax.dot_general(
        step_low, step_weight_ref[...], contract_first, preferred_element_type=f32
    )
    step_pre_ref[...] = step_pre
    step = softplus(step_pre)
    step_ref[...] = step
    held_step[...] = jnp.where(mask_ref[:, 1:2] > 0.0, step, reset_step)
    drive[...] = step * act_ref[...].astype(f32)
    gate = gate_ref[...].astype(f32)
    scan_grad[...] = gated_grad_ref[...] * (gate * jax.nn.sigmoid(gate))
    zero = jnp.zeros(decay2.shape, f32)

    def body(block, carried):
        state, product, adjoint = carried
        columns = coef_columns(coef, block)
        for i in range(body_rows):
            row = pl.ds(block * body_rows + i, 1)
            factor = jnp.exp2(held_step[row, :] * decay2)
            state = factor * state + columns[:count, i : i + 1] * drive[row, :]
            product = factor * product
            adjoint = adjoint + product * (columns[count:, i : i + 1] * scan_grad[row, :])
        return state, product, adjoint

    state, product, adjoint = lax.fori_loop(0, rows // body_rows, body, (zero, zero + 1.0, zero))
    ends_ref[:count, :] = state
    ends_ref[count : 2 * count, :] = adjoint
    total = jnp.sum(held_step[...], axis=0, keepdims=True)
    ends_ref[2 * count :, :] = jnp.broadcast_to(total, (8, total.shape[1]))


def scan_ends(
    selected, other, step_weight, step_bias, act, projected, gated_grad, masks, decay_log
):
    rows, width = act.shape
    count = decay_log.shape[0]
    columns = selected.shape[0]
    rank = step_weight.shape[0]
    return call(
        ends_kernel,
        "scan_ends",
        width,
        [
            whole_spec(columns, rows),
            whole_spec(columns, rows),
            column_spec(rank),
            column_spec(1),
            column_spec(rows),
            part_spec(1, rows),
            column_spec(rows),
            whole_spec(rows, masks.shape[1]),
            column_spec(count),
        ],
        [column_spec(rows), column_spec(rows), column_spec(2 * count + 8)],
        [
            jax.ShapeDtypeStruct((rows, width), f32),
            jax.ShapeDtypeStruct((rows, width), f32),
            jax.ShapeDtypeStruct((2 * count + 8, width), f32),
        ],
        [pltpu.VMEM((2 * count, rows), f32)] + [pltpu.VMEM((rows, scan_width), f32)] * 3,
        selected,
        other,
        step_weight,
        step_bias,
        act,
        projected,
        gated_grad,
        masks,
        decay_log,
    )


def lane_tiles(values):
    return [values[:, k : k + lanes] for k in range(0, values.shape[1], lanes)]


def tree_sum(parts):
    while len(parts) > 1:
        odd = parts[len(parts) // 2 * 2 :]
        parts = [a + b for a, b in zip(parts[0::2], parts[1::2])] + odd
    return parts[0]


def keep_halves(scratch, i, values):
    for k, tile in enumerate(lane_tiles(values)):
        at = (k * body_rows + i) * 8
        scratch[at : at + 8, :] = tile[:8] + tile[8:]


def put_state_sums(scratch, out_ref, block):
    for group in range(body_rows // 8):
        row = pl.ds(pl.multiple_of(block * body_rows + group * 8, 8), 8)
        for k in range(out_ref.shape[1] // lanes):
            at = (k * body_rows + group * 8) * 8
            total = tree_sum([scratch[pl.ds(at + n, 8, stride=8), :] for n in range(8)])
            out_ref[row, k * lanes : (k + 1) * lanes] = total


def lane_sums(values):
    ones = jnp.ones((8, lanes), bf16)
    high = values.astype(bf16)
    low = (values - high.astype(f32)).astype(bf16)
    total = lax.dot_general(ones, high, contract_last, preferred_element_type=f32)
    total += lax.dot_general(ones, low, contract_last, preferred_element_type=f32)
    return total[:1, :]


def at_token(t, count):
    return pl.ds(pl.multiple_of(t * count, count), count)


def forward_kernel(
    selected_ref,
    other_ref,
    step_ref,
    act_ref,
    gate_ref,
    gated_grad_ref,
    mask_ref,
    decay_log_ref,
    passed_ref,
    entering_ref,
    skip_ref,
    gated_ref,
    gate_grad_ref,
    entry_ref,
    coef,
    held_step,
    drive,
    scanned,
    halves,
):
    rows = step_ref.shape[0]
    count = decay_log_ref.shape[0]
    rank = selected_ref.shape[0] - 2 * count
    decay = -jnp.exp(decay_log_ref[...])
    decay2 = decay * log2e
    before_steps = passed_ref[2 * count : 2 * count + 1, :]
    entry = passed_ref[:count, :] + through(decay, before_steps) * entering_ref[...]
    entry_ref[...] = entry
    coef[...] = selected_ref[rank:, :] + other_ref[rank:, :]
    act = act_ref[...].astype(f32)
    held_step[...] = jnp.where(mask_ref[:, 1:2] > 0.0, step_ref[...], reset_step)
    drive[...] = step_ref[...] * act

    def forward(block, state):
        columns = coef_columns(coef, block)
        for i in range(body_rows):
            row = pl.ds(block * body_rows + i, 1)
            factor = jnp.exp2(held_step[row, :] * decay2)
            state = factor * state + columns[:count, i : i + 1] * drive[row, :]
            keep_halves(halves, i, columns[count:, i : i + 1] * state)
        put_state_sums(halves, scanned, block)
        return state

    lax.fori_loop(0, rows // body_rows, forward, entry)
    gate = gate_ref[...].astype(f32)
    logistic = jax.nn.sigmoid(gate)
    total = scanned[...] + skip_ref[...] * act
    gated_ref[...] = (total * (gate * logistic)).astype(bf16)
    slope = logistic * (1.0 + gate * (1.0 - logistic))
    gate_grad_ref[...] = (gated_grad_ref[...] * total * slope).astype(bf16)


def scan_forward(
    selected, other, step, act, projected, gated_grad, masks, decay_log, passed, entering, skip_gain
):
    rows, width = step.shape
    count = decay_log.shape[0]
    columns = selected.shape[0]
    return call(
        forward_kernel,
        "scan_forward",
        width,
        [
            whole_spec(columns, rows),
            whole_spec(columns, rows),
            column_spec(rows),
            column_spec(rows),
            part_spec(1, rows),
            column_spec(rows),
            whole_spec(rows, masks.shape[1]),
            column_spec(count),
            column_spec(2 * count + 8),
            column_spec(count),
            column_spec(1),
        ],
        [column_spec(rows), column_spec(rows), column_spec(count)],
        [
            jax.ShapeDtypeStruct((rows, width), bf16),
            jax.ShapeDtypeStruct((rows, width), bf16),
            jax.ShapeDtypeStruct((count, width), f32),
        ],
        [pltpu.VMEM((2 * count, rows), f32)]
        + [pltpu.VMEM((rows, scan_width), f32)] * 3
        + [pltpu.VMEM((8 * body_rows * (scan_width // lanes), lanes), f32)],
        selected,
        other,
        step,
        act,
        projected,
        gated_grad,
        masks,
        decay_log,
        passed,
        entering,
        skip_gain,
    )


def backward_kernel(
    selected_ref,
    other_ref,
    step_pre_ref,
    step_ref,
    act_ref,
    gate_ref,
    gated_grad_ref,
    mask_ref,
    decay_log_ref,
    entry_ref,
    passed_ref,
    returning_ref,
    skip_ref,
    step_weight_ref,
    act_grad_ref,
    select_grad_ref,
    small_ref,
    coef,
    held_step,
    drive,
    scan_grad,
    weighted,
    held_sum,
    states,
    factors,
    halves,
    more_halves,
    in_sum,
    read_sum,
):
    rows = step_ref.shape[0]
    count = decay_log_ref.shape[0]
    rank = step_weight_ref.shape[0]
    blocks = rows // body_rows
    decay = -jnp.exp(decay_log_ref[...])
    decay2 = decay * log2e
    after_steps = passed_ref[2 * count + 1 : 2 * count + 2, :]
    tail = passed_ref[count : 2 * count, :] + through(decay, after_steps) * returning_ref[...]
    selected = selected_ref[...] + other_ref[...]
    coef[...] = selected[rank:, :]
    step_low = selected[:rank, :].astype(bf16)
    step = step_ref[...]
    act = act_ref[...].astype(f32)
    held_step[...] = jnp.where(mask_ref[:, 1:2] > 0.0, step, reset_step)
    drive[...] = step * act
    gate = gate_ref[...].astype(f32)
    grads = gated_grad_ref[...] * (gate * jax.nn.sigmoid(gate))
    scan_grad[...] = grads
    small_ref[rank + count : rank + count + 1, :] = jnp.sum(grads * act, axis=0, keepdims=True)
    states[:count, :] = entry_ref[...]

    @pl.when(pl.program_id(0) == 0)
    def _():
        in_sum[...] = jnp.zeros(in_sum.shape, f32)
        read_sum[...] = jnp.zeros(read_sum.shape, f32)
        select_grad_ref[...] = jnp.zeros(select_grad_ref.shape, f32)

    def forward(block, state):
        columns = coef_columns(coef, block)
        for i in range(body_rows):
            t = block * body_rows + i
            row = pl.ds(t, 1)
            factor = jnp.exp2(held_step[row, :] * decay2)
            state = factor * state + columns[:count, i : i + 1] * drive[row, :]
            factors[at_token(t, count), :] = factor
            states[at_token(t + 1, count), :] = state
        return state

    lax.fori_loop(0, blocks, forward, entry_ref[...])

    def backward(k, carried):
        adjoint, decay_grad = carried
        block = blocks - 1 - k
        columns = coef_columns(coef, block)
        for i in range(body_rows - 1, -1, -1):
            t = block * body_rows + i
            row = pl.ds(t, 1)
            here = at_token(t, count)
            grad = scan_grad[row, :]
            summed = columns[count:, i : i + 1] * grad + adjoint
            read_sum[here, :] += tree_sum(lane_tiles(grad * states[at_token(t + 1, count), :]))
            in_sum[here, :] += tree_sum(lane_tiles(summed * drive[row, :]))
            keep_halves(halves, i, summed * columns[:count, i : i + 1])
            adjoint = factors[here, :] * summed
            held = adjoint * states[here, :]
            decay_grad = decay_grad + held * step_ref[row, :]
            keep_halves(more_halves, i, held * decay)
        put_state_sums(halves, weighted, block)
        put_state_sums(more_halves, held_sum, block)
        return adjoint, decay_grad

    ignored, decay_grad = lax.fori_loop(
        0, blocks, backward, (tail, jnp.zeros(decay.shape, f32))
    )
    act_grad_ref[...] = step * weighted[...] + skip_ref[...] * scan_grad[...]
    step_grad = act * weighted[...] + held_sum[...]
    pre_grad = (step_grad * jax.nn.sigmoid(step_pre_ref[...])).astype(bf16)
    small_ref[:rank, :] = jnp.dot(step_low, pre_grad, preferred_element_type=f32)
    small_ref[rank : rank + count, :] = decay_grad * decay
    bias_grad = jnp.sum(pre_grad.astype(f32), axis=0, keepdims=True)
    small_ref[rank + count + 1 : rank + count + 2, :] = bias_grad
    select_grad_ref[:rank, :] += lax.dot_general(
        step_weight_ref[...], pre_grad, contract_last, preferred_element_type=f32
    )

    @pl.when(pl.program_id(0) == pl.num_programs(0) - 1)
    def _():
        for n in range(count):
            at = pl.ds(n, rows, stride=count)
            select_grad_ref[rank + n : rank + n + 1, :] = lane_sums(in_sum[at, :])
            select_grad_ref[rank + count + n : rank + count + n + 1, :] = lane_sums(read_sum[at, :])


def scan_backward(
    selected,
    other,
    step_pre,
    step,
    act,
    projected,
    gated_grad,
    masks,
    decay_log,
    entry,
    passed,
    returning,
    skip_gain,
    step_weight,
):
    rows, width = step.shape
    count = decay_log.shape[0]
    columns = selected.shape[0]
    rank = step_weight.shape[0]
    half_rows = 8 * body_rows * (scan_width // lanes)
    small = rank + count + 2
    return call(
        backward_kernel,
        "scan_backward",
        width,
        [
            whole_spec(columns, rows),
            whole_spec(columns, rows),
            column_spec(rows),
            column_spec(rows),
            column_spec(rows),
            part_spec(1, rows),
            column_spec(rows),
            whole_spec(rows, masks.shape[1]),
            column_spec(count),
            column_spec(count),
            column_spec(2 * count + 8),
            column_spec(count),
            column_spec(1),
            column_spec(rank),
        ],
        [column_spec(rows), whole_spec(columns, rows), column_spec(small)],
        [
            jax.ShapeDtypeStruct((rows, width), f32),
            jax.ShapeDtypeStruct((columns, rows), f32),
            jax.ShapeDtypeStruct((small, width), f32),
        ],
        [pltpu.VMEM((2 * count, rows), f32)]
        + [pltpu.VMEM((rows, scan_width), f32)] * 5
        + [
            pltpu.VMEM(((rows + 1) * count, scan_width), f32),
            pltpu.VMEM((rows * count, scan_width), f32),
            pltpu.VMEM((half_rows, lanes), f32),
            pltpu.VMEM((half_rows, lanes), f32),
            pltpu.VMEM((rows * count, lanes), f32),
            pltpu.VMEM((rows * count, lanes), f32),
        ],
        selected,
        other,
        step_pre,
        step,
        act,
        projected,
        gated_grad,
        masks,
        decay_log,
        entry,
        passed,
        returning,
        skip_gain,
        step_weight,
    )


def conv_grad_kernel(
    select_grad_ref,
    other_ref,
    select_ref,
    act_grad_ref,
    convolved_ref,
    act_ref,
    inner_ref,
    conv_weight_ref,
    mask_ref,
    *rest,
):
    inner_grad_ref, before_ref, last_ref, small_ref, inner, shifted = rest[-6:]
    rows = act_ref.shape[0]
    taps = conv_weight_ref.shape[0]
    columns = select_ref.shape[0]
    select_grad = (select_grad_ref[...] + other_ref[...]).astype(bf16)
    total = act_grad_ref[...] + lax.dot_general(
        select_grad, select_ref[...], contract_first, preferred_element_type=f32
    )
    conv_grad = total * silu_slope(convolved_ref[...])
    small_ref[:columns, :] = jnp.dot(select_grad, act_ref[...], preferred_element_type=f32)
    inner[:halo, :] = inner_ref[rows:, :].astype(f32)
    inner[halo:, :] = inner_ref[:rows, :].astype(f32)
    edges = jnp.zeros((8, conv_grad.shape[1]), f32)
    shifted[:8, :] = edges
    shifted[rows + 8 :, :] = edges
    out = conv_weight_ref[taps - 1 :, :] * conv_grad
    before = edges
    small_ref[columns + taps - 1 : columns + taps, :] = jnp.sum(
        conv_grad * inner[halo:, :], axis=0, keepdims=True
    )
    for lag in range(1, taps):
        masked = conv_grad * mask_ref[:, lag : lag + 1]
        at = taps - 1 - lag
        small_ref[columns + at : columns + at + 1, :] = jnp.sum(
            masked * inner[pl.ds(halo - lag, rows), :], axis=0, keepdims=True
        )
        shifted[8 : rows + 8, :] = masked
        weight = conv_weight_ref[at : at + 1, :]
        out = out + weight * shifted[pl.ds(8 + lag, rows), :]
        before = before + weight * shifted[pl.ds(lag, 8), :]
    small_ref[columns + taps : columns + taps + 1, :] = jnp.sum(conv_grad, axis=0, keepdims=True)
    inner_grad_ref[...] = out.astype(bf16)
    before_ref[...] = before
    last_ref[...] = out[rows - 8 :, :]


def convolve_grad(
    select_grad, other, select_weight, act_grad, convolved, act, projected, conv_weight, masks, waits
):
    rows, width = act.shape
    extended = rows + halo
    columns = select_weight.shape[0]
    taps = conv_weight.shape[0]
    small = columns + taps + 1
    return call(
        conv_grad_kernel,
        "convolve_grad",
        width,
        [
            whole_spec(columns, rows),
            whole_spec(columns, rows),
            column_spec(columns),
            column_spec(rows),
            column_spec(rows),
            column_spec(rows),
            part_spec(0, extended),
            column_spec(taps),
            whole_spec(rows, masks.shape[1]),
        ]
        + [pl.BlockSpec(memory_space=pl.ANY)] * len(waits),
        [column_spec(rows), column_spec(8), column_spec(8), column_spec(small)],
        [
            jax.ShapeDtypeStruct((rows, width), bf16),
            jax.ShapeDtypeStruct((8, width), f32),
            jax.ShapeDtypeStruct((8, width), f32),
            jax.ShapeDtypeStruct((small, width), f32),
        ],
        [pltpu.VMEM((extended, scan_width), f32), pltpu.VMEM((rows + 16, scan_width), f32)],
        select_grad,
        other,
        select_weight,
        act_grad,
        convolved,
        act,
        projected,
        conv_weight,
        masks,
        *waits,
    )


def normalize_kernel(
    own_ref,
    other_ref,
    edge_ref,
    other_edge_ref,
    gain_ref,
    ids_ref,
    whole_ref,
    extended_ref,
    normed_ref,
    inverse_ref,
    mask_ref,
    rows_ref,
):
    rows, half = own_ref.shape
    ids = ids_ref[...].astype(f32)
    place = lax.broadcasted_iota(jnp.int32, ids.shape, 1)
    same = []
    for lag in range(8):
        earlier = jnp.where(place < lag, ids[:, :1], pltpu.roll(ids, lag, 1)) if lag else ids
        same.append(jnp.where(earlier == ids, 1.0, 0.0))
    spare = jnp.zeros((lanes - 8, rows), f32)
    mask_ref[...] = jnp.concatenate(same + [spare]).T
    right = lax.axis_index("narrow") == 1
    for at, own, other in ((0, own_ref, other_ref), (rows, edge_ref, other_edge_ref)):
        end = at + own.shape[0]
        rows_ref[at:end, :half] = jnp.where(right, other[...], own[...])
        rows_ref[at:end, half:] = jnp.where(right, own[...], other[...])
    whole_ref[...] = rows_ref[:rows, :]
    whole = rows_ref[...].astype(f32)
    inverse = lax.rsqrt(jnp.mean(whole * whole, axis=1, keepdims=True) + epsilon)
    normed = (whole * inverse * gain_ref[...]).astype(bf16)
    extended_ref[...] = normed
    normed_ref[...] = normed[:rows]
    inverse_ref[...] = inverse[:rows]


def normalized(own, other, edge, other_edge, gain, ids):
    rows, half = own.shape
    extended = rows + edge.shape[0]
    return pl.pallas_call(
        normalize_kernel,
        out_shape=[
            jax.ShapeDtypeStruct((rows, 2 * half), bf16),
            jax.ShapeDtypeStruct((extended, 2 * half), bf16),
            jax.ShapeDtypeStruct((rows, 2 * half), bf16),
            jax.ShapeDtypeStruct((rows, 1), f32),
            jax.ShapeDtypeStruct((rows, lanes), f32),
        ],
        scratch_shapes=[pltpu.VMEM((extended, 2 * half), bf16)],
        cost_estimate=tiny_cost,
        name="normalized",
    )(own, other, edge, other_edge, gain, ids)


def after(array, *waits):
    anywhere = pl.BlockSpec(memory_space=pl.ANY)
    return pl.pallas_call(
        lambda *refs: None,
        in_specs=[anywhere] * (1 + len(waits)),
        out_specs=anywhere,
        out_shape=jax.ShapeDtypeStruct(array.shape, array.dtype),
        input_output_aliases={0: 0},
        cost_estimate=tiny_cost,
        name="after",
    )(array, *waits)


def patch_kernel(ids_ref, rows_ref, last_ref, next_ref, *rest):
    count = ids_ref.shape[0]
    place = lax.broadcasted_iota(jnp.int32, (8, 1), 0)
    same = jnp.zeros((8, 1), f32)
    for lag in range(8):
        here = jnp.where(ids_ref[count - 1 - lag] == ids_ref[count - 1], 1.0, 0.0)
        same = same + jnp.where(place == 7 - lag, here, 0.0)
    total = last_ref[...] + next_ref[...] * same
    rows = rows_ref[...].astype(f32)
    rest[-1][...] = jnp.concatenate([rows[: halo - 8], total]).astype(bf16)


def patched(ids, grads, last, following, *waits):
    rows, width = grads.shape
    block = pl.BlockSpec((halo, width), lambda j: (rows // halo - 1, 0))
    edge = pl.BlockSpec((8, width), lambda j: (0, 0))
    return pl.pallas_call(
        patch_kernel,
        grid=(1,),
        in_specs=[pl.BlockSpec(memory_space=pltpu.SMEM), block, edge, edge]
        + [pl.BlockSpec(memory_space=pl.ANY)] * len(waits),
        out_specs=block,
        out_shape=jax.ShapeDtypeStruct((rows, width), bf16),
        input_output_aliases={1: 0},
        cost_estimate=tiny_cost,
        name="patched",
    )(ids, grads, last, following, *waits)


def edge_kernel(ids_ref, tokens_ref, out_ref):
    rows = ids_ref.shape[0]
    taps = 4
    out_ref[...] = tokens_ref[...]
    place = lax.broadcasted_iota(jnp.int32, (halo, 1), 0)
    same = jnp.zeros((halo, 1), f32)
    for lag in range(taps):
        here = jnp.where(ids_ref[rows - 1 - lag] == ids_ref[rows - 1], 1.0, 0.0)
        same = same + jnp.where(place == halo - 1 - lag, here, 0.0)
    out_ref[...] = (tokens_ref[...].astype(f32) * same).astype(bf16)


def edge_rows_of(ids, tokens):
    rows, width = tokens.shape
    return pl.pallas_call(
        edge_kernel,
        grid=(1,),
        in_specs=[
            pl.BlockSpec(memory_space=pltpu.SMEM),
            pl.BlockSpec((halo, width), lambda j: (rows // halo - 1, 0)),
        ],
        out_specs=pl.BlockSpec((halo, width), lambda j: (0, 0)),
        out_shape=jax.ShapeDtypeStruct((halo, width), bf16),
        cost_estimate=tiny_cost,
        name="edge_rows",
    )(ids, tokens)


block_rows, used_rows = 16, 12


def small_kernel(place_ref, scan_ref, conv_ref, wait_ref, keep_ref, *rest):
    *sends_refs, rows, blocks = rest
    rows[...] = jnp.zeros(rows.shape, f32)
    rows[: scan_ref.shape[0], :] = scan_ref[...]
    rows[scan_ref.shape[0] : scan_ref.shape[0] + conv_ref.shape[0], :] = conv_ref[...]
    blocks[...] = jnp.zeros(blocks.shape, f32)
    for n in range(16):
        blocks[n * block_rows : n * block_rows + used_rows, :] = rows[
            n * used_rows : (n + 1) * used_rows, :
        ]
    quarter = keep_ref.shape[0]
    for n in range(4):
        start = pl.multiple_of((place_ref[0] ^ n) * quarter, quarter)
        block = blocks[pl.ds(start, quarter), :]
        if n == 0:
            keep_ref[...] = block
        else:
            sends_refs[n - 1][...] = block.astype(bf16)


def small_quarters(place, scan_small, conv_small, wait):
    width = scan_small.shape[1]
    return pl.pallas_call(
        small_kernel,
        in_specs=[pl.BlockSpec(memory_space=pltpu.SMEM)]
        + [pl.BlockSpec(memory_space=pltpu.VMEM)] * 2
        + [pl.BlockSpec(memory_space=pl.ANY)],
        out_shape=[jax.ShapeDtypeStruct((4 * block_rows, width), f32)]
        + [jax.ShapeDtypeStruct((4 * block_rows, width), bf16)] * 3,
        scratch_shapes=[
            pltpu.VMEM((16 * used_rows, width), f32),
            pltpu.VMEM((16 * block_rows, width), f32),
        ],
        cost_estimate=tiny_cost,
        name="small_quarters",
    )(place, scan_small, conv_small, wait)


def quarter_kernel(
    place_ref,
    own_ref,
    near_ref,
    far_ref,
    normed_0,
    normed_1,
    normed_2,
    normed_3,
    small_ref,
    first_ref,
    second_ref,
    third_ref,
    *rest,
):
    keep_ref, *sends_refs, piece, small = rest[-6:]
    total = None
    tokens = own_ref.shape[0]
    grads = (own_ref[...], near_ref[...], far_ref[:tokens, :], far_ref[tokens:, :])
    for left, right in zip((normed_0, normed_1, normed_2, normed_3), grads):
        part = lax.dot_general(left[...], right, contract_first, preferred_element_type=f32)
        total = part if total is None else total + part
    piece[...] = total
    small[...] = small_ref[...] + sum(
        ref[...].astype(f32) for ref in (first_ref, second_ref, third_ref)
    )
    rows, spare = piece.shape[0] // 4, small.shape[0] // 4
    for n in range(4):
        block = place_ref[0] ^ n
        inner_rows = piece[pl.ds(pl.multiple_of(block * rows, rows), rows), :]
        small_rows = small[pl.ds(pl.multiple_of(block * spare, spare), spare), :]
        if n == 0:
            keep_ref[:rows, :] = inner_rows
            keep_ref[rows:, :] = small_rows
        else:
            sends_refs[n - 1][:rows, :] = inner_rows.astype(bf16)
            sends_refs[n - 1][rows:, :] = small_rows.astype(bf16)


def inner_quarter(place, own, near, far, normed, smalls, waits):
    width = own.shape[1]
    quarter = normed[0].shape[1]
    spare = smalls[0].shape[0]
    rows = (quarter + spare) // 4
    return pl.pallas_call(
        quarter_kernel,
        in_specs=[pl.BlockSpec(memory_space=pltpu.SMEM)]
        + [pl.BlockSpec(memory_space=pltpu.VMEM)] * 11
        + [pl.BlockSpec(memory_space=pl.ANY)] * len(waits),
        out_shape=[jax.ShapeDtypeStruct((rows, width), f32)]
        + [jax.ShapeDtypeStruct((rows, width), bf16)] * 3,
        scratch_shapes=[pltpu.VMEM((quarter, width), f32), pltpu.VMEM((spare, width), f32)],
        compiler_params=pltpu.CompilerParams(vmem_limit_bytes=vmem_bytes),
        cost_estimate=tiny_cost,
        name="inner_quarter",
    )(place, own, near, far, *normed, *smalls, *waits)


def join_kernel(place_ref, gate_ref, first_ref, second_ref, *rest, small_rows):
    at_end = 2 + len(small_rows) if small_rows else 0
    out_ref = rest[-1 - at_end]
    step = pl.program_id(0)
    rows = out_ref.shape[0] // 2
    out_ref[:, 1, :] = gate_ref[...].astype(f32)

    def put(ref):
        for n in range(2):
            at = n * (rows + block_rows)
            out_ref[n * rows : (n + 1) * rows, 0, :] = ref[at : at + rows, :].astype(f32)

    @pl.when(step < 2)
    def _():
        put(first_ref)

    @pl.when(step >= 2)
    def _():
        put(second_ref)

    if not small_rows:
        return
    *row_refs, gain_ref, blocks = rest[-at_end:]

    @pl.when(step == 3)
    def _():
        for flip, ref in enumerate(rest[:4]):
            for n in range(4):
                at = ((place_ref[0] ^ flip) * 4 + n) * block_rows
                taken = ref[(n + 1) * rows + n * block_rows : (n + 1) * (rows + block_rows), :]
                blocks[pl.ds(pl.multiple_of(at, block_rows), block_rows), :] = taken.astype(f32)
        for ref, start in zip(row_refs, small_rows):
            for row in range(ref.shape[0]):
                at = (start + row) // used_rows * block_rows + (start + row) % used_rows
                ref[row : row + 1, :] = blocks[at : at + 1, :]
        gain_ref[...] = sum(
            blocks[n * block_rows + used_rows : n * block_rows + used_rows + 1, :] for n in range(16)
        )


def joined(place, flip, gate, first, second, before, waits, held=(), small_rows=(), small_counts=()):
    depth, width = gate.shape
    quarter = depth // 4
    block = quarter // 2
    piece = first.shape[0] // 2

    def target(j, place):
        return 2 * (place[0] ^ (flip + j // 2)) + lax.rem(j, 2)

    vmem = pl.BlockSpec(memory_space=pltpu.VMEM)
    untouched = [*before, *waits]
    return pl.pallas_call(
        functools.partial(join_kernel, small_rows=small_rows),
        grid_spec=pltpu.PrefetchScalarGridSpec(
            num_scalar_prefetch=1,
            grid=(4,),
            in_specs=[
                pl.BlockSpec((block, width), lambda j, place: (target(j, place), 0)),
                pl.BlockSpec((piece, width), lambda j, place: (jnp.minimum(j, 1), 0)),
                pl.BlockSpec((piece, width), lambda j, place: (jnp.maximum(j - 2, 0), 0)),
            ]
            + [vmem] * len(held)
            + [pl.BlockSpec(memory_space=pl.ANY)] * len(untouched),
            out_specs=[pl.BlockSpec((block, 2, width), lambda j, place: (target(j, place), 0, 0))]
            + [pl.BlockSpec((rows, width), lambda j, place: (0, 0)) for rows in small_counts],
            scratch_shapes=[pltpu.VMEM((16 * block_rows, width), f32)] if small_rows else [],
        ),
        out_shape=[jax.ShapeDtypeStruct((depth, 2, width), f32)]
        + [jax.ShapeDtypeStruct((rows, width), f32) for rows in small_counts],
        input_output_aliases={4 + len(held) + k: k for k in range(len(before))},
        compiler_params=pltpu.CompilerParams(vmem_limit_bytes=vmem_bytes),
        cost_estimate=tiny_cost,
        name="joined",
    )(place, gate, first, second, *held, *untouched)


def through(decay, total):
    return jnp.exp(decay * total)


def round_kernel(second_ref, decay_log_ref, own_ref, other_ref, passed_ref, new_passed_ref, *ends_refs):
    count = decay_log_ref.shape[0]
    decay = -jnp.exp(decay_log_ref[...])
    second = second_ref[0] > 0

    def split(ref):
        return ref[:count], ref[count : 2 * count], ref[2 * count : 2 * count + 1]

    own, other = split(own_ref), split(other_ref)
    early = [jnp.where(second, b, a) for a, b in zip(own, other)]
    late = [jnp.where(second, a, b) for a, b in zip(own, other)]
    state = late[0] + through(decay, late[2]) * early[0]
    adjoint = early[1] + through(decay, early[2]) * late[1]
    if len(ends_refs) == 2:
        ends_refs[0][...] = state
        ends_refs[1][...] = adjoint
    else:
        ends_refs[0][:count, :] = state
        ends_refs[0][count : 2 * count, :] = adjoint
        ends_refs[0][2 * count :, :] = jnp.broadcast_to(early[2] + late[2], (8, decay.shape[1]))
    before, after = passed_ref[:count], passed_ref[count : 2 * count]
    before_steps = passed_ref[2 * count : 2 * count + 1]
    after_steps = passed_ref[2 * count + 1 : 2 * count + 2]
    new_passed_ref[:count, :] = before + jnp.where(second, through(decay, before_steps) * other[0], 0.0)
    new_passed_ref[count : 2 * count, :] = after + jnp.where(
        second, 0.0, through(decay, after_steps) * other[1]
    )
    new_passed_ref[2 * count : 2 * count + 1, :] = before_steps + jnp.where(second, other[2], 0.0)
    new_passed_ref[2 * count + 1 : 2 * count + 2, :] = after_steps + jnp.where(second, 0.0, other[2])


def carried(ends, decay_log):
    count, width = decay_log.shape
    place = lax.axis_index("wide").astype(jnp.int32)
    passed = jnp.zeros((2 * count + 8, width), f32)
    packed = ends
    vmem = pl.BlockSpec(memory_space=pltpu.VMEM)
    for k, kinds in enumerate(([ends], [decay_log, decay_log])):
        passed, *out = pl.pallas_call(
            round_kernel,
            in_specs=[pl.BlockSpec(memory_space=pltpu.SMEM)] + [vmem] * 4,
            out_shape=[jax.ShapeDtypeStruct(kind.shape, f32) for kind in [passed] + kinds],
            cost_estimate=tiny_cost,
            name="carry_round",
        )((place >> k & 1)[None], decay_log, packed, swapped(packed, "wide", 2**k), passed)
        packed = out[0]
    from_before = passed_along(out[0], "wide", 4)
    from_after = passed_along(out[1], "wide", -4)
    return passed, from_before, from_after


def local(
    tokens,
    norm_gain,
    in_weight,
    conv_weight,
    conv_bias,
    select_weight,
    step_weight,
    step_bias,
    decay_log,
    skip_gain,
    out_weight,
    segment_ids,
    cotangent,
):
    rows, features = tokens.shape
    taps = conv_weight.shape[0]
    columns = select_weight.shape[0]
    rank = step_weight.shape[0]
    count = decay_log.shape[0]
    right_half = lax.axis_index("narrow") == 1

    def both_halves(own, other):
        return jnp.concatenate(
            [jnp.where(right_half, other, own), jnp.where(right_half, own, other)], axis=1
        )

    other_tokens = swapped(tokens, "narrow", 1)
    other_cot = swapped(cotangent, "narrow", 1)
    edge, other_edge = to_next_both(edge_rows_of(segment_ids, tokens))

    whole_low, normed_ext, normed, inverse, masks = normalized(
        tokens, other_tokens, edge, other_edge, norm_gain[None], segment_ids[None]
    )
    projected = jnp.einsum(
        "td,dce->cte", normed_ext, in_weight, preferred_element_type=f32
    ).astype(bf16)
    convolved, act, selected = convolve(
        projected, conv_weight, conv_bias[None], select_weight, masks
    )
    other_selected = swapped(selected, "narrow", 1)
    cot_whole = both_halves(cotangent, other_cot)
    gated_grad = lax.dot_general(
        cot_whole, out_weight, contract_last, preferred_element_type=f32
    )
    step_pre, step, ends = scan_ends(
        selected,
        other_selected,
        step_weight,
        step_bias[None],
        act,
        projected,
        gated_grad,
        masks,
        decay_log,
    )
    passed, entering, returning = carried(ends, decay_log)
    gated, gate_grad, entry = scan_forward(
        selected,
        other_selected,
        step,
        act,
        projected,
        gated_grad,
        masks,
        decay_log,
        passed,
        entering,
        skip_gain[None],
    )
    gated = after(gated, returning)
    products = (
        lax.dot_general(gated, cot_whole, contract_first, preferred_element_type=f32).astype(bf16),
        lax.dot_general(normed, gate_grad, contract_first, preferred_element_type=f32).astype(bf16),
    )
    out_sum, gate_sum = lax.psum(products, "wide")
    wide_place = lax.axis_index("wide").astype(jnp.int32)
    four_place = (wide_place & 3)[None]

    def narrow_halves(array):
        low, high = array[:, :features], array[:, features:]
        return jnp.where(right_half, high, low), jnp.where(right_half, low, high)

    def after_forward(products):
        whole = whole_low.astype(f32)
        act_grad, select_grad, scan_small = scan_backward(
            selected,
            other_selected,
            step_pre,
            step,
            act,
            projected,
            gated_grad,
            masks,
            decay_log,
            entry,
            passed,
            returning,
            skip_gain[None],
            step_weight,
        )
        normed_four = quarter_of_four(after(normed, select_grad))
        inner_main, before, last, conv_small = convolve_grad(
            select_grad,
            swapped(select_grad, "narrow", 1),
            select_weight,
            act_grad,
            convolved,
            act,
            projected,
            conv_weight,
            masks,
            [],
        )
        following = passed_along(before, "wide", -1)
        inner_grad = patched(segment_ids, inner_main, last, following, *normed_four)
        near = swapped(inner_grad, "wide", 2)
        keep, *sends = small_quarters(four_place, scan_small, conv_small, inner_grad)
        smalls = [keep] + [swapped(sends[n - 1], "wide", n) for n in (1, 2, 3)]
        normed_part = jnp.einsum(
            "cte,dce->td", jnp.stack([inner_grad, gate_grad]), in_weight, preferred_element_type=f32
        )
        gain_part = jnp.sum(normed_part * whole * inverse, axis=0, keepdims=True)
        row_part = jnp.sum(normed_part * norm_gain * whole, axis=1)[None]
        near = after(near, gain_part, *smalls[1:])
        far = swapped(jnp.concatenate([inner_grad, near]), "wide", 1)
        first_bits, *more_bits = group_bits(2)
        gain_sum = gain_part + swapped(gain_part, "narrow", 1)
        for bit in (bit for bits in more_bits for bit in bits):
            gain_sum = gain_sum + swapped(gain_sum, "wide", bit)
        row_theirs = swapped(row_part, "narrow", 1)
        keep, *sends = inner_quarter(
            (wide_place >> 2 & 3)[None],
            inner_grad,
            near,
            far,
            normed_four,
            smalls,
            [gain_sum, row_theirs],
        )
        normed_mine, normed_other = narrow_halves(normed_part)
        normed_theirs = swapped(after(normed_other, keep), "narrow", 1)
        out_part = jnp.dot(gated, out_weight, preferred_element_type=f32)
        out_mine, out_other = narrow_halves(out_part)
        out_theirs = swapped(after(out_other, keep), "narrow", 1)
        layer_out = (tokens.astype(f32) + (out_mine + out_theirs)).astype(bf16)
        row_sum = (row_part + row_theirs).reshape(rows, 1)
        gain_mine = jnp.where(right_half, norm_gain[features:], norm_gain[:features])
        whole_grad = inverse * (gain_mine * (normed_mine + normed_theirs)) - tokens.astype(f32) * (
            inverse * inverse * inverse
        ) * (row_sum / (2 * features))
        tokens_grad = (whole_grad + cotangent.astype(f32)).astype(bf16)
        held = keep
        for n, flip in enumerate(flips(first_bits)[1:]):
            held = held + swapped(sends[n], "wide", flip).astype(f32)
        for bits in more_bits:
            held = scattered(held, bits)
        held = held.astype(bf16)
        for bits in reversed(more_bits):
            held = gathered(held, bits)
        spare = jnp.broadcast_to(gain_sum, (block_rows - used_rows, gain_sum.shape[1]))
        held = jnp.concatenate([held[: held.shape[0] - spare.shape[0]], spare.astype(bf16)])
        held = gathered(held, first_bits)
        return held, layer_out, tokens_grad

    kinds = jax.eval_shape(after_forward, products)
    held, layer_out, tokens_grad = lax.cond(
        segment_ids[0] >= 0,
        after_forward,
        lambda pair: jax.tree.map(lambda kind: jnp.zeros(kind.shape, kind.dtype), kinds),
        products,
    )

    out_weight_grad = out_sum.astype(f32)
    core = swapped(held, "wide", 1)
    (begun,) = joined(four_place, 0, gate_sum, held, core, (), (out_weight_grad,))
    near = after(swapped(held, "wide", 2), begun)
    far = swapped(near, "wide", 1)
    conv_at = rank + count + 2
    (
        in_weight_grad,
        step_weight_grad,
        decay_log_grad,
        skip_gain_grad,
        step_bias_grad,
        select_weight_grad,
        conv_weight_grad,
        conv_bias_grad,
        norm_gain_grad,
    ) = joined(
        four_place,
        2,
        gate_sum,
        near,
        far,
        (begun,),
        (),
        (held, core, near, far),
        (0, rank, rank + count, rank + count + 1, conv_at, conv_at + columns, conv_at + columns + taps),
        (rank, count, 1, 1, columns, taps, 1, 1),
    )
    return (
        layer_out,
        tokens_grad,
        norm_gain_grad[0],
        in_weight_grad,
        conv_weight_grad,
        conv_bias_grad[0],
        select_weight_grad,
        step_weight_grad,
        step_bias_grad[0],
        decay_log_grad,
        skip_gain_grad[0],
        out_weight_grad,
    )


def solution(mesh):
    placed = (
        P("wide", "narrow"),
        P(),
        P(None, None, "narrow"),
        P(None, "narrow"),
        P("narrow"),
        P(None, "narrow"),
        P(None, "narrow"),
        P("narrow"),
        P(None, "narrow"),
        P("narrow"),
        P("narrow", None),
        P("wide"),
        P("wide", "narrow"),
    )
    return jax.shard_map(
        local,
        mesh=mesh,
        in_specs=placed,
        out_specs=(
            P("wide", "narrow"),
            P("wide", "narrow"),
            P(),
            P(None, None, "narrow"),
            P(None, "narrow"),
            P("narrow"),
            P(None, "narrow"),
            P(None, "narrow"),
            P("narrow"),
            P(None, "narrow"),
            P("narrow"),
            P("narrow", None),
        ),
        check_vma=False,
    )
```

```python
import functools

import jax
import jax.numpy as jnp
from jax import lax
from jax.experimental import pallas as pl
from jax.experimental.pallas import tpu as pltpu
from jax.sharding import PartitionSpec as P

epsilon = 1e-05
log2e = 1.4426950408889634
reset_step = 1e30
lanes = 128
halo = 16
body_rows = 32
scan_width = 512
vmem_bytes = 56 * 1024 * 1024
tiny_cost = pl.CostEstimate(flops=1, bytes_accessed=1, transcendentals=0)
f32 = jnp.float32
bf16 = jnp.bfloat16
contract_first = (((0,), (0,)), ((), ()))
contract_last = (((1,), (1,)), ((), ()))


def passed_along(array, axis, by):
    peers = lax.axis_size(axis)
    pairs = [(i, i + by) for i in range(peers) if 0 <= i + by < peers]
    return lax.ppermute(array, axis, pairs)


def swapped(array, axis, bit):
    peers = lax.axis_size(axis)
    return lax.ppermute(array, axis, [(i, i ^ bit) for i in range(peers)])


def wide_bits():
    bit, bits = 1, []
    while bit < lax.axis_size("wide"):
        bits.append(bit)
        bit *= 2
    return bits


def to_next_both(array):
    count, sides = lax.axis_size("wide"), lax.axis_size("narrow")
    pairs = [
        (i * sides + k, (i + 1) * sides + (sides - 1 - k))
        for i in range(count - 1)
        for k in range(sides)
    ]
    return passed_along(array, "wide", 1), lax.ppermute(array, ("wide", "narrow"), pairs)


def is_upper(bit):
    return (lax.axis_index("wide") & bit) != 0


def group_bits(size):
    bits, bit = [], 4
    while bit < lax.axis_size("wide"):
        bits.append(bit)
        bit *= 2
    return [tuple(bits[k : k + size]) for k in range(0, len(bits), size)]


def flips(bits):
    return [sum(b for k, b in enumerate(bits) if n >> k & 1) for n in range(2 ** len(bits))]


def scattered(piece, bits):
    rows = piece.shape[0] // 2 ** len(bits)
    here = sum(is_upper(b).astype(jnp.int32) << k for k, b in enumerate(bits))

    def block(n):
        return lax.dynamic_slice_in_dim(piece, (here ^ n) * rows, rows, 0)

    total = block(0).astype(f32)
    for n, flip in enumerate(flips(bits)):
        if n > 0:
            total = total + swapped(block(n).astype(bf16), "wide", flip).astype(f32)
    return total


def gathered(held, bits):
    blocks = [held] + [swapped(held, "wide", flip) for flip in flips(bits)[1:]]
    for bit in bits:
        upper = is_upper(bit)
        blocks = [
            jnp.concatenate([jnp.where(upper, b, a), jnp.where(upper, a, b)])
            for a, b in zip(blocks[0::2], blocks[1::2])
        ]
    return blocks[0]


def quarter_of_four(array):
    width = array.shape[1] // 4
    here = lax.axis_index("wide") & 3

    def quarter(n):
        return lax.dynamic_slice_in_dim(array, (here ^ n) * width, width, 1)

    return [quarter(0)] + [swapped(quarter(n), "wide", n) for n in (2, 1, 3)]


def silu_slope(values):
    logistic = jax.nn.sigmoid(values)
    return logistic * (1.0 + values * (1.0 - logistic))


def softplus(values):
    return jnp.maximum(values, 0.0) + jnp.log1p(jnp.exp(-jnp.abs(values)))


def column_spec(rows, start=0):
    return pl.BlockSpec((rows, scan_width), lambda j: (0, start + j))


def part_spec(part, rows, start=0):
    return pl.BlockSpec((None, rows, scan_width), lambda j: (part, 0, start + j))


def whole_spec(rows, width):
    return pl.BlockSpec((rows, width), lambda j: (0, 0))


def call(kernel, name, width, in_specs, out_specs, out_shape, scratch, *operands):
    return pl.pallas_call(
        kernel,
        grid=(width // scan_width,),
        in_specs=in_specs,
        out_specs=out_specs,
        out_shape=out_shape,
        scratch_shapes=scratch,
        compiler_params=pltpu.CompilerParams(vmem_limit_bytes=vmem_bytes),
        cost_estimate=tiny_cost,
        name=name,
    )(*operands)


def conv_kernel(
    inner_ref,
    conv_weight_ref,
    conv_bias_ref,
    select_ref,
    mask_ref,
    convolved_ref,
    act_ref,
    selected_ref,
    inner,
):
    rows = act_ref.shape[0]
    taps = conv_weight_ref.shape[0]
    inner[:halo, :] = inner_ref[rows:, :].astype(f32)
    inner[halo:, :] = inner_ref[:rows, :].astype(f32)
    total = conv_bias_ref[...] + conv_weight_ref[taps - 1 :, :] * inner[halo:, :]
    for lag in range(1, taps):
        earlier = inner[pl.ds(halo - lag, rows), :] * mask_ref[:, lag : lag + 1]
        total = total + conv_weight_ref[taps - 1 - lag : taps - lag, :] * earlier
    convolved_ref[...] = total
    act = (total * jax.nn.sigmoid(total)).astype(bf16)
    act_ref[...] = act
    part = lax.dot_general(select_ref[...], act, contract_last, preferred_element_type=f32)

    @pl.when(pl.program_id(0) == 0)
    def _():
        selected_ref[...] = part

    @pl.when(pl.program_id(0) > 0)
    def _():
        selected_ref[...] += part


def convolve(projected, conv_weight, conv_bias, select_weight, masks):
    parts, extended, width = projected.shape
    rows = extended - halo
    taps = conv_weight.shape[0]
    columns = select_weight.shape[0]
    return call(
        conv_kernel,
        "convolve",
        width,
        [
            part_spec(0, extended),
            column_spec(taps),
            column_spec(1),
            column_spec(columns),
            whole_spec(rows, masks.shape[1]),
        ],
        [column_spec(rows), column_spec(rows), whole_spec(columns, rows)],
        [
            jax.ShapeDtypeStruct((rows, width), f32),
            jax.ShapeDtypeStruct((rows, width), bf16),
            jax.ShapeDtypeStruct((columns, rows), f32),
        ],
        [pltpu.VMEM((extended, scan_width), f32)],
        projected,
        conv_weight,
        conv_bias,
        select_weight,
        masks,
    )


def coef_columns(coef, block):
    per_tile = lanes // body_rows
    start = pl.multiple_of((block // per_tile) * lanes, lanes)
    tile = coef[:, pl.ds(start, lanes)]
    back = body_rows * lax.rem(block, per_tile)
    return pltpu.roll(tile, lax.rem(lanes - back, lanes), 1)


def ends_kernel(
    selected_ref,
    other_ref,
    step_weight_ref,
    step_bias_ref,
    act_ref,
    gate_ref,
    gated_grad_ref,
    mask_ref,
    decay_log_ref,
    step_pre_ref,
    step_ref,
    ends_ref,
    coef,
    held_step,
    drive,
    scan_grad,
):
    rows = act_ref.shape[0]
    count = decay_log_ref.shape[0]
    rank = step_weight_ref.shape[0]
    decay2 = -jnp.exp(decay_log_ref[...]) * log2e
    selected = selected_ref[...] + other_ref[...]
    coef[...] = selected[rank:, :]
    step_low = selected[:rank, :].astype(bf16)
    step_pre = step_bias_ref[...] + lax.dot_general(
        step_low, step_weight_ref[...], contract_first, preferred_element_type=f32
    )
    step_pre_ref[...] = step_pre
    step = softplus(step_pre)
    step_ref[...] = step
    held_step[...] = jnp.where(mask_ref[:, 1:2] > 0.0, step, reset_step)
    drive[...] = step * act_ref[...].astype(f32)
    gate = gate_ref[...].astype(f32)
    scan_grad[...] = gated_grad_ref[...] * (gate * jax.nn.sigmoid(gate))
    zero = jnp.zeros(decay2.shape, f32)

    def body(block, carried):
        state, product, adjoint = carried
        columns = coef_columns(coef, block)
        for i in range(body_rows):
            row = pl.ds(block * body_rows + i, 1)
            factor = jnp.exp2(held_step[row, :] * decay2)
            state = factor * state + columns[:count, i : i + 1] * drive[row, :]
            product = factor * product
            adjoint = adjoint + product * (columns[count:, i : i + 1] * scan_grad[row, :])
        return state, product, adjoint

    state, product, adjoint = lax.fori_loop(0, rows // body_rows, body, (zero, zero + 1.0, zero))
    ends_ref[:count, :] = state
    ends_ref[count : 2 * count, :] = adjoint
    total = jnp.sum(held_step[...], axis=0, keepdims=True)
    ends_ref[2 * count :, :] = jnp.broadcast_to(total, (8, total.shape[1]))


def scan_ends(
    selected, other, step_weight, step_bias, act, projected, gated_grad, masks, decay_log
):
    rows, width = act.shape
    count = decay_log.shape[0]
    columns = selected.shape[0]
    rank = step_weight.shape[0]
    return call(
        ends_kernel,
        "scan_ends",
        width,
        [
            whole_spec(columns, rows),
            whole_spec(columns, rows),
            column_spec(rank),
            column_spec(1),
            column_spec(rows),
            part_spec(1, rows),
            column_spec(rows),
            whole_spec(rows, masks.shape[1]),
            column_spec(count),
        ],
        [column_spec(rows), column_spec(rows), column_spec(2 * count + 8)],
        [
            jax.ShapeDtypeStruct((rows, width), f32),
            jax.ShapeDtypeStruct((rows, width), f32),
            jax.ShapeDtypeStruct((2 * count + 8, width), f32),
        ],
        [pltpu.VMEM((2 * count, rows), f32)] + [pltpu.VMEM((rows, scan_width), f32)] * 3,
        selected,
        other,
        step_weight,
        step_bias,
        act,
        projected,
        gated_grad,
        masks,
        decay_log,
    )


def lane_tiles(values):
    return [values[:, k : k + lanes] for k in range(0, values.shape[1], lanes)]


def tree_sum(parts):
    while len(parts) > 1:
        odd = parts[len(parts) // 2 * 2 :]
        parts = [a + b for a, b in zip(parts[0::2], parts[1::2])] + odd
    return parts[0]


def keep_halves(scratch, i, values):
    for k, tile in enumerate(lane_tiles(values)):
        at = (k * body_rows + i) * 8
        scratch[at : at + 8, :] = tile[:8] + tile[8:]


def put_state_sums(scratch, out_ref, block):
    for group in range(body_rows // 8):
        row = pl.ds(pl.multiple_of(block * body_rows + group * 8, 8), 8)
        for k in range(out_ref.shape[1] // lanes):
            at = (k * body_rows + group * 8) * 8
            total = tree_sum([scratch[pl.ds(at + n, 8, stride=8), :] for n in range(8)])
            out_ref[row, k * lanes : (k + 1) * lanes] = total


def lane_sums(values):
    ones = jnp.ones((8, lanes), bf16)
    high = values.astype(bf16)
    low = (values - high.astype(f32)).astype(bf16)
    total = lax.dot_general(ones, high, contract_last, preferred_element_type=f32)
    total += lax.dot_general(ones, low, contract_last, preferred_element_type=f32)
    return total[:1, :]


def at_token(t, count):
    return pl.ds(pl.multiple_of(t * count, count), count)


def forward_kernel(
    selected_ref,
    other_ref,
    step_ref,
    act_ref,
    gate_ref,
    gated_grad_ref,
    mask_ref,
    decay_log_ref,
    passed_ref,
    entering_ref,
    skip_ref,
    gated_ref,
    gate_grad_ref,
    entry_ref,
    coef,
    held_step,
    drive,
    scanned,
    halves,
):
    rows = step_ref.shape[0]
    count = decay_log_ref.shape[0]
    rank = selected_ref.shape[0] - 2 * count
    decay = -jnp.exp(decay_log_ref[...])
    decay2 = decay * log2e
    before_steps = passed_ref[2 * count : 2 * count + 1, :]
    entry = passed_ref[:count, :] + through(decay, before_steps) * entering_ref[...]
    entry_ref[...] = entry
    coef[...] = selected_ref[rank:, :] + other_ref[rank:, :]
    act = act_ref[...].astype(f32)
    held_step[...] = jnp.where(mask_ref[:, 1:2] > 0.0, step_ref[...], reset_step)
    drive[...] = step_ref[...] * act

    def forward(block, state):
        columns = coef_columns(coef, block)
        for i in range(body_rows):
            row = pl.ds(block * body_rows + i, 1)
            factor = jnp.exp2(held_step[row, :] * decay2)
            state = factor * state + columns[:count, i : i + 1] * drive[row, :]
            keep_halves(halves, i, columns[count:, i : i + 1] * state)
        put_state_sums(halves, scanned, block)
        return state

    lax.fori_loop(0, rows // body_rows, forward, entry)
    gate = gate_ref[...].astype(f32)
    logistic = jax.nn.sigmoid(gate)
    total = scanned[...] + skip_ref[...] * act
    gated_ref[...] = (total * (gate * logistic)).astype(bf16)
    slope = logistic * (1.0 + gate * (1.0 - logistic))
    gate_grad_ref[...] = (gated_grad_ref[...] * total * slope).astype(bf16)


def scan_forward(
    selected, other, step, act, projected, gated_grad, masks, decay_log, passed, entering, skip_gain
):
    rows, width = step.shape
    count = decay_log.shape[0]
    columns = selected.shape[0]
    return call(
        forward_kernel,
        "scan_forward",
        width,
        [
            whole_spec(columns, rows),
            whole_spec(columns, rows),
            column_spec(rows),
            column_spec(rows),
            part_spec(1, rows),
            column_spec(rows),
            whole_spec(rows, masks.shape[1]),
            column_spec(count),
            column_spec(2 * count + 8),
            column_spec(count),
            column_spec(1),
        ],
        [column_spec(rows), column_spec(rows), column_spec(count)],
        [
            jax.ShapeDtypeStruct((rows, width), bf16),
            jax.ShapeDtypeStruct((rows, width), bf16),
            jax.ShapeDtypeStruct((count, width), f32),
        ],
        [pltpu.VMEM((2 * count, rows), f32)]
        + [pltpu.VMEM((rows, scan_width), f32)] * 3
        + [pltpu.VMEM((8 * body_rows * (scan_width // lanes), lanes), f32)],
        selected,
        other,
        step,
        act,
        projected,
        gated_grad,
        masks,
        decay_log,
        passed,
        entering,
        skip_gain,
    )


def backward_kernel(
    selected_ref,
    other_ref,
    step_pre_ref,
    step_ref,
    act_ref,
    gate_ref,
    gated_grad_ref,
    mask_ref,
    decay_log_ref,
    entry_ref,
    passed_ref,
    returning_ref,
    skip_ref,
    step_weight_ref,
    act_grad_ref,
    select_grad_ref,
    small_ref,
    coef,
    held_step,
    drive,
    scan_grad,
    weighted,
    held_sum,
    states,
    factors,
    halves,
    more_halves,
    in_sum,
    read_sum,
):
    rows = step_ref.shape[0]
    count = decay_log_ref.shape[0]
    rank = step_weight_ref.shape[0]
    blocks = rows // body_rows
    decay = -jnp.exp(decay_log_ref[...])
    decay2 = decay * log2e
    after_steps = passed_ref[2 * count + 1 : 2 * count + 2, :]
    tail = passed_ref[count : 2 * count, :] + through(decay, after_steps) * returning_ref[...]
    selected = selected_ref[...] + other_ref[...]
    coef[...] = selected[rank:, :]
    step_low = selected[:rank, :].astype(bf16)
    step = step_ref[...]
    act = act_ref[...].astype(f32)
    held_step[...] = jnp.where(mask_ref[:, 1:2] > 0.0, step, reset_step)
    drive[...] = step * act
    gate = gate_ref[...].astype(f32)
    grads = gated_grad_ref[...] * (gate * jax.nn.sigmoid(gate))
    scan_grad[...] = grads
    small_ref[rank + count : rank + count + 1, :] = jnp.sum(grads * act, axis=0, keepdims=True)
    states[:count, :] = entry_ref[...]

    @pl.when(pl.program_id(0) == 0)
    def _():
        in_sum[...] = jnp.zeros(in_sum.shape, f32)
        read_sum[...] = jnp.zeros(read_sum.shape, f32)
        select_grad_ref[...] = jnp.zeros(select_grad_ref.shape, f32)

    def forward(block, state):
        columns = coef_columns(coef, block)
        for i in range(body_rows):
            t = block * body_rows + i
            row = pl.ds(t, 1)
            factor = jnp.exp2(held_step[row, :] * decay2)
            state = factor * state + columns[:count, i : i + 1] * drive[row, :]
            factors[at_token(t, count), :] = factor
            states[at_token(t + 1, count), :] = state
        return state

    lax.fori_loop(0, blocks, forward, entry_ref[...])

    def backward(k, carried):
        adjoint, decay_grad = carried
        block = blocks - 1 - k
        columns = coef_columns(coef, block)
        for i in range(body_rows - 1, -1, -1):
            t = block * body_rows + i
            row = pl.ds(t, 1)
            here = at_token(t, count)
            grad = scan_grad[row, :]
            summed = columns[count:, i : i + 1] * grad + adjoint
            read_sum[here, :] += tree_sum(lane_tiles(grad * states[at_token(t + 1, count), :]))
            in_sum[here, :] += tree_sum(lane_tiles(summed * drive[row, :]))
            keep_halves(halves, i, summed * columns[:count, i : i + 1])
            adjoint = factors[here, :] * summed
            held = adjoint * states[here, :]
            decay_grad = decay_grad + held * step_ref[row, :]
            keep_halves(more_halves, i, held * decay)
        put_state_sums(halves, weighted, block)
        put_state_sums(more_halves, held_sum, block)
        return adjoint, decay_grad

    ignored, decay_grad = lax.fori_loop(
        0, blocks, backward, (tail, jnp.zeros(decay.shape, f32))
    )
    act_grad_ref[...] = step * weighted[...] + skip_ref[...] * scan_grad[...]
    step_grad = act * weighted[...] + held_sum[...]
    pre_grad = (step_grad * jax.nn.sigmoid(step_pre_ref[...])).astype(bf16)
    small_ref[:rank, :] = jnp.dot(step_low, pre_grad, preferred_element_type=f32)
    small_ref[rank : rank + count, :] = decay_grad * decay
    bias_grad = jnp.sum(pre_grad.astype(f32), axis=0, keepdims=True)
    small_ref[rank + count + 1 : rank + count + 2, :] = bias_grad
    select_grad_ref[:rank, :] += lax.dot_general(
        step_weight_ref[...], pre_grad, contract_last, preferred_element_type=f32
    )

    @pl.when(pl.program_id(0) == pl.num_programs(0) - 1)
    def _():
        for n in range(count):
            at = pl.ds(n, rows, stride=count)
            select_grad_ref[rank + n : rank + n + 1, :] = lane_sums(in_sum[at, :])
            select_grad_ref[rank + count + n : rank + count + n + 1, :] = lane_sums(read_sum[at, :])


def scan_backward(
    selected,
    other,
    step_pre,
    step,
    act,
    projected,
    gated_grad,
    masks,
    decay_log,
    entry,
    passed,
    returning,
    skip_gain,
    step_weight,
):
    rows, width = step.shape
    count = decay_log.shape[0]
    columns = selected.shape[0]
    rank = step_weight.shape[0]
    half_rows = 8 * body_rows * (scan_width // lanes)
    small = rank + count + 2
    return call(
        backward_kernel,
        "scan_backward",
        width,
        [
            whole_spec(columns, rows),
            whole_spec(columns, rows),
            column_spec(rows),
            column_spec(rows),
            column_spec(rows),
            part_spec(1, rows),
            column_spec(rows),
            whole_spec(rows, masks.shape[1]),
            column_spec(count),
            column_spec(count),
            column_spec(2 * count + 8),
            column_spec(count),
            column_spec(1),
            column_spec(rank),
        ],
        [column_spec(rows), whole_spec(columns, rows), column_spec(small)],
        [
            jax.ShapeDtypeStruct((rows, width), f32),
            jax.ShapeDtypeStruct((columns, rows), f32),
            jax.ShapeDtypeStruct((small, width), f32),
        ],
        [pltpu.VMEM((2 * count, rows), f32)]
        + [pltpu.VMEM((rows, scan_width), f32)] * 5
        + [
            pltpu.VMEM(((rows + 1) * count, scan_width), f32),
            pltpu.VMEM((rows * count, scan_width), f32),
            pltpu.VMEM((half_rows, lanes), f32),
            pltpu.VMEM((half_rows, lanes), f32),
            pltpu.VMEM((rows * count, lanes), f32),
            pltpu.VMEM((rows * count, lanes), f32),
        ],
        selected,
        other,
        step_pre,
        step,
        act,
        projected,
        gated_grad,
        masks,
        decay_log,
        entry,
        passed,
        returning,
        skip_gain,
        step_weight,
    )


def conv_grad_kernel(
    select_grad_ref,
    other_ref,
    select_ref,
    act_grad_ref,
    convolved_ref,
    act_ref,
    inner_ref,
    conv_weight_ref,
    mask_ref,
    *rest,
):
    inner_grad_ref, before_ref, last_ref, small_ref, inner, shifted = rest[-6:]
    rows = act_ref.shape[0]
    taps = conv_weight_ref.shape[0]
    columns = select_ref.shape[0]
    select_grad = (select_grad_ref[...] + other_ref[...]).astype(bf16)
    total = act_grad_ref[...] + lax.dot_general(
        select_grad, select_ref[...], contract_first, preferred_element_type=f32
    )
    conv_grad = total * silu_slope(convolved_ref[...])
    small_ref[:columns, :] = jnp.dot(select_grad, act_ref[...], preferred_element_type=f32)
    inner[:halo, :] = inner_ref[rows:, :].astype(f32)
    inner[halo:, :] = inner_ref[:rows, :].astype(f32)
    edges = jnp.zeros((8, conv_grad.shape[1]), f32)
    shifted[:8, :] = edges
    shifted[rows + 8 :, :] = edges
    out = conv_weight_ref[taps - 1 :, :] * conv_grad
    before = edges
    small_ref[columns + taps - 1 : columns + taps, :] = jnp.sum(
        conv_grad * inner[halo:, :], axis=0, keepdims=True
    )
    for lag in range(1, taps):
        masked = conv_grad * mask_ref[:, lag : lag + 1]
        at = taps - 1 - lag
        small_ref[columns + at : columns + at + 1, :] = jnp.sum(
            masked * inner[pl.ds(halo - lag, rows), :], axis=0, keepdims=True
        )
        shifted[8 : rows + 8, :] = masked
        weight = conv_weight_ref[at : at + 1, :]
        out = out + weight * shifted[pl.ds(8 + lag, rows), :]
        before = before + weight * shifted[pl.ds(lag, 8), :]
    small_ref[columns + taps : columns + taps + 1, :] = jnp.sum(conv_grad, axis=0, keepdims=True)
    inner_grad_ref[...] = out.astype(bf16)
    before_ref[...] = before
    last_ref[...] = out[rows - 8 :, :]


def convolve_grad(
    select_grad, other, select_weight, act_grad, convolved, act, projected, conv_weight, masks, waits
):
    rows, width = act.shape
    extended = rows + halo
    columns = select_weight.shape[0]
    taps = conv_weight.shape[0]
    small = columns + taps + 1
    return call(
        conv_grad_kernel,
        "convolve_grad",
        width,
        [
            whole_spec(columns, rows),
            whole_spec(columns, rows),
            column_spec(columns),
            column_spec(rows),
            column_spec(rows),
            column_spec(rows),
            part_spec(0, extended),
            column_spec(taps),
            whole_spec(rows, masks.shape[1]),
        ]
        + [pl.BlockSpec(memory_space=pl.ANY)] * len(waits),
        [column_spec(rows), column_spec(8), column_spec(8), column_spec(small)],
        [
            jax.ShapeDtypeStruct((rows, width), bf16),
            jax.ShapeDtypeStruct((8, width), f32),
            jax.ShapeDtypeStruct((8, width), f32),
            jax.ShapeDtypeStruct((small, width), f32),
        ],
        [pltpu.VMEM((extended, scan_width), f32), pltpu.VMEM((rows + 16, scan_width), f32)],
        select_grad,
        other,
        select_weight,
        act_grad,
        convolved,
        act,
        projected,
        conv_weight,
        masks,
        *waits,
    )


def normalize_kernel(
    own_ref,
    other_ref,
    edge_ref,
    other_edge_ref,
    gain_ref,
    ids_ref,
    whole_ref,
    extended_ref,
    normed_ref,
    inverse_ref,
    mask_ref,
    rows_ref,
):
    rows, half = own_ref.shape
    ids = ids_ref[...].astype(f32)
    place = lax.broadcasted_iota(jnp.int32, ids.shape, 1)
    same = []
    for lag in range(8):
        earlier = jnp.where(place < lag, ids[:, :1], pltpu.roll(ids, lag, 1)) if lag else ids
        same.append(jnp.where(earlier == ids, 1.0, 0.0))
    spare = jnp.zeros((lanes - 8, rows), f32)
    mask_ref[...] = jnp.concatenate(same + [spare]).T
    right = lax.axis_index("narrow") == 1
    for at, own, other in ((0, own_ref, other_ref), (rows, edge_ref, other_edge_ref)):
        end = at + own.shape[0]
        rows_ref[at:end, :half] = jnp.where(right, other[...], own[...])
        rows_ref[at:end, half:] = jnp.where(right, own[...], other[...])
    whole_ref[...] = rows_ref[:rows, :]
    whole = rows_ref[...].astype(f32)
    inverse = lax.rsqrt(jnp.mean(whole * whole, axis=1, keepdims=True) + epsilon)
    normed = (whole * inverse * gain_ref[...]).astype(bf16)
    extended_ref[...] = normed
    normed_ref[...] = normed[:rows]
    inverse_ref[...] = inverse[:rows]


def normalized(own, other, edge, other_edge, gain, ids):
    rows, half = own.shape
    extended = rows + edge.shape[0]
    return pl.pallas_call(
        normalize_kernel,
        out_shape=[
            jax.ShapeDtypeStruct((rows, 2 * half), bf16),
            jax.ShapeDtypeStruct((extended, 2 * half), bf16),
            jax.ShapeDtypeStruct((rows, 2 * half), bf16),
            jax.ShapeDtypeStruct((rows, 1), f32),
            jax.ShapeDtypeStruct((rows, lanes), f32),
        ],
        scratch_shapes=[pltpu.VMEM((extended, 2 * half), bf16)],
        cost_estimate=tiny_cost,
        name="normalized",
    )(own, other, edge, other_edge, gain, ids)


def after(array, *waits):
    anywhere = pl.BlockSpec(memory_space=pl.ANY)
    return pl.pallas_call(
        lambda *refs: None,
        in_specs=[anywhere] * (1 + len(waits)),
        out_specs=anywhere,
        out_shape=jax.ShapeDtypeStruct(array.shape, array.dtype),
        input_output_aliases={0: 0},
        cost_estimate=tiny_cost,
        name="after",
    )(array, *waits)


def patch_kernel(ids_ref, rows_ref, last_ref, next_ref, *rest):
    count = ids_ref.shape[0]
    place = lax.broadcasted_iota(jnp.int32, (8, 1), 0)
    same = jnp.zeros((8, 1), f32)
    for lag in range(8):
        here = jnp.where(ids_ref[count - 1 - lag] == ids_ref[count - 1], 1.0, 0.0)
        same = same + jnp.where(place == 7 - lag, here, 0.0)
    total = last_ref[...] + next_ref[...] * same
    rows = rows_ref[...].astype(f32)
    rest[-1][...] = jnp.concatenate([rows[: halo - 8], total]).astype(bf16)


def patched(ids, grads, last, following, *waits):
    rows, width = grads.shape
    block = pl.BlockSpec((halo, width), lambda j: (rows // halo - 1, 0))
    edge = pl.BlockSpec((8, width), lambda j: (0, 0))
    return pl.pallas_call(
        patch_kernel,
        grid=(1,),
        in_specs=[pl.BlockSpec(memory_space=pltpu.SMEM), block, edge, edge]
        + [pl.BlockSpec(memory_space=pl.ANY)] * len(waits),
        out_specs=block,
        out_shape=jax.ShapeDtypeStruct((rows, width), bf16),
        input_output_aliases={1: 0},
        cost_estimate=tiny_cost,
        name="patched",
    )(ids, grads, last, following, *waits)


def edge_kernel(ids_ref, tokens_ref, out_ref):
    rows = ids_ref.shape[0]
    taps = 4
    out_ref[...] = tokens_ref[...]
    place = lax.broadcasted_iota(jnp.int32, (halo, 1), 0)
    same = jnp.zeros((halo, 1), f32)
    for lag in range(taps):
        here = jnp.where(ids_ref[rows - 1 - lag] == ids_ref[rows - 1], 1.0, 0.0)
        same = same + jnp.where(place == halo - 1 - lag, here, 0.0)
    out_ref[...] = (tokens_ref[...].astype(f32) * same).astype(bf16)


def edge_rows_of(ids, tokens):
    rows, width = tokens.shape
    return pl.pallas_call(
        edge_kernel,
        grid=(1,),
        in_specs=[
            pl.BlockSpec(memory_space=pltpu.SMEM),
            pl.BlockSpec((halo, width), lambda j: (rows // halo - 1, 0)),
        ],
        out_specs=pl.BlockSpec((halo, width), lambda j: (0, 0)),
        out_shape=jax.ShapeDtypeStruct((halo, width), bf16),
        cost_estimate=tiny_cost,
        name="edge_rows",
    )(ids, tokens)


block_rows, used_rows = 16, 12


def small_kernel(core_ref, scan_ref, conv_ref, wait_ref, keep_ref, send_ref, rows, blocks):
    rows[...] = jnp.zeros(rows.shape, f32)
    rows[: scan_ref.shape[0], :] = scan_ref[...]
    rows[scan_ref.shape[0] : scan_ref.shape[0] + conv_ref.shape[0], :] = conv_ref[...]
    blocks[...] = jnp.zeros(blocks.shape, f32)
    for n in range(16):
        blocks[n * block_rows : n * block_rows + used_rows, :] = rows[
            n * used_rows : (n + 1) * used_rows, :
        ]
    half = keep_ref.shape[0]
    mine = pl.ds(pl.multiple_of(core_ref[0] * half, half), half)
    other = pl.ds(pl.multiple_of((1 - core_ref[0]) * half, half), half)
    keep_ref[...] = blocks[mine, :]
    send_ref[...] = blocks[other, :].astype(bf16)


def small_halves(core, scan_small, conv_small, wait):
    width = scan_small.shape[1]
    return pl.pallas_call(
        small_kernel,
        in_specs=[pl.BlockSpec(memory_space=pltpu.SMEM)]
        + [pl.BlockSpec(memory_space=pltpu.VMEM)] * 2
        + [pl.BlockSpec(memory_space=pl.ANY)],
        out_shape=[jax.ShapeDtypeStruct((8 * block_rows, width), kind) for kind in (f32, bf16)],
        scratch_shapes=[
            pltpu.VMEM((16 * used_rows, width), f32),
            pltpu.VMEM((16 * block_rows, width), f32),
        ],
        cost_estimate=tiny_cost,
        name="small_halves",
    )(core, scan_small, conv_small, wait)


def fold_kernel(upper_ref, keep_ref, arrived_ref, out_ref, send_ref):
    size = out_ref.shape[0]
    mine = pl.ds(pl.multiple_of(upper_ref[0] * size, size), size)
    other = pl.ds(pl.multiple_of((1 - upper_ref[0]) * size, size), size)
    out_ref[...] = keep_ref[mine, :] + arrived_ref[mine, :].astype(f32)
    send_ref[...] = (keep_ref[other, :] + arrived_ref[other, :].astype(f32)).astype(bf16)


def folded(upper, keep, arrived):
    rows, width = keep.shape
    return pl.pallas_call(
        fold_kernel,
        in_specs=[pl.BlockSpec(memory_space=pltpu.SMEM)]
        + [pl.BlockSpec(memory_space=pltpu.VMEM)] * 2,
        out_shape=[jax.ShapeDtypeStruct((rows // 2, width), kind) for kind in (f32, bf16)],
        cost_estimate=tiny_cost,
        name="folded",
    )(upper, keep, arrived)


def quarter_kernel(
    place_ref,
    own_ref,
    near_ref,
    far_ref,
    normed_0,
    normed_1,
    normed_2,
    normed_3,
    small_ref,
    arrived_ref,
    *rest,
):
    keep_ref, *sends_refs, piece, small = rest[-6:]
    total = None
    tokens = own_ref.shape[0]
    grads = (own_ref[...], near_ref[...], far_ref[:tokens, :], far_ref[tokens:, :])
    for left, right in zip((normed_0, normed_1, normed_2, normed_3), grads):
        part = lax.dot_general(left[...], right, contract_first, preferred_element_type=f32)
        total = part if total is None else total + part
    piece[...] = total
    small[...] = small_ref[...] + arrived_ref[...].astype(f32)
    rows, spare = piece.shape[0] // 4, small.shape[0] // 4
    for n in range(4):
        block = place_ref[0] ^ n
        inner_rows = piece[pl.ds(pl.multiple_of(block * rows, rows), rows), :]
        small_rows = small[pl.ds(pl.multiple_of(block * spare, spare), spare), :]
        if n == 0:
            keep_ref[:rows, :] = inner_rows
            keep_ref[rows:, :] = small_rows
        else:
            sends_refs[n - 1][:rows, :] = inner_rows.astype(bf16)
            sends_refs[n - 1][rows:, :] = small_rows.astype(bf16)


def inner_quarter(place, own, near, far, normed, smalls, waits):
    width = own.shape[1]
    quarter = normed[0].shape[1]
    spare = smalls[0].shape[0]
    rows = (quarter + spare) // 4
    return pl.pallas_call(
        quarter_kernel,
        in_specs=[pl.BlockSpec(memory_space=pltpu.SMEM)]
        + [pl.BlockSpec(memory_space=pltpu.VMEM)] * 9
        + [pl.BlockSpec(memory_space=pl.ANY)] * len(waits),
        out_shape=[jax.ShapeDtypeStruct((rows, width), f32)]
        + [jax.ShapeDtypeStruct((rows, width), bf16)] * 3,
        scratch_shapes=[pltpu.VMEM((quarter, width), f32), pltpu.VMEM((spare, width), f32)],
        compiler_params=pltpu.CompilerParams(vmem_limit_bytes=vmem_bytes),
        cost_estimate=tiny_cost,
        name="inner_quarter",
    )(place, own, near, far, *normed, *smalls, *waits)


def put_quarter(out_ref, gate_ref, inner_ref):
    rows = out_ref.shape[0] // 4
    out_ref[:, 1, :] = gate_ref[...].astype(f32)
    for n in range(4):
        at = n * (rows + block_rows)
        out_ref[n * rows : (n + 1) * rows, 0, :] = inner_ref[at : at + rows, :].astype(f32)


def first_join_kernel(place_ref, gate_ref, first_ref, second_ref, low_ref, out_ref, wide_ref):
    wide_ref[...] = low_ref[...].astype(f32)

    @pl.when(pl.program_id(0) == 0)
    def _():
        put_quarter(out_ref, gate_ref, first_ref)

    @pl.when(pl.program_id(0) == 1)
    def _():
        put_quarter(out_ref, gate_ref, second_ref)


def last_join_kernel(place_ref, gate_ref, first_ref, second_ref, *rest, small_rows):
    held = rest[:4]
    out_ref, *row_refs, gain_ref, blocks = rest[5:]

    @pl.when(pl.program_id(0) == 0)
    def _():
        put_quarter(out_ref, gate_ref, first_ref)

    @pl.when(pl.program_id(0) == 1)
    def _():
        put_quarter(out_ref, gate_ref, second_ref)
        rows = out_ref.shape[0] // 4
        for flip, ref in enumerate(held):
            number = place_ref[0] ^ flip
            number = (number & 1) * 2 + number // 2
            for n in range(4):
                at = (number * 4 + n) * block_rows
                taken = ref[(n + 1) * rows + n * block_rows : (n + 1) * (rows + block_rows), :]
                blocks[pl.ds(pl.multiple_of(at, block_rows), block_rows), :] = taken.astype(f32)
        for ref, start in zip(row_refs, small_rows):
            for row in range(ref.shape[0]):
                at = (start + row) // used_rows * block_rows + (start + row) % used_rows
                ref[row : row + 1, :] = blocks[at : at + 1, :]
        gain_ref[...] = sum(
            blocks[n * block_rows + used_rows : n * block_rows + used_rows + 1, :] for n in range(16)
        )


def joined(kernel, place, flip, gate, first, second, specs, operands, out_specs, out_shape, scratch, aliases):
    depth, width = gate.shape
    quarter = depth // 4

    def target(j, place):
        return place[0] ^ (flip + j)

    whole = pl.BlockSpec(first.shape, lambda j, place: (0, 0))
    return pl.pallas_call(
        kernel,
        grid_spec=pltpu.PrefetchScalarGridSpec(
            num_scalar_prefetch=1,
            grid=(2,),
            in_specs=[
                pl.BlockSpec((quarter, width), lambda j, place: (target(j, place), 0)),
                whole,
                whole,
            ]
            + specs,
            out_specs=[
                pl.BlockSpec((quarter, 2, width), lambda j, place: (target(j, place), 0, 0))
            ]
            + out_specs,
            scratch_shapes=scratch,
        ),
        out_shape=[jax.ShapeDtypeStruct((depth, 2, width), f32)] + out_shape,
        input_output_aliases=aliases,
        compiler_params=pltpu.CompilerParams(vmem_limit_bytes=vmem_bytes),
        cost_estimate=tiny_cost,
        name="joined",
    )(place, gate, first, second, *operands)


def joined_first(place, gate, first, second, low):
    rows, width = low.shape
    half = pl.BlockSpec((rows // 2, width), lambda j, place: (j, 0))
    kind = jax.ShapeDtypeStruct((rows, width), f32)
    return joined(
        first_join_kernel, place, 0, gate, first, second, [half], [low], [half], [kind], [], {}
    )


def joined_last(place, gate, held, begun, small_rows, small_counts):
    width = gate.shape[1]
    whole = pl.BlockSpec(held[0].shape, lambda j, place: (0, 0))
    return joined(
        functools.partial(last_join_kernel, small_rows=small_rows),
        place,
        2,
        gate,
        held[2],
        held[3],
        [whole] * 4 + [pl.BlockSpec(memory_space=pl.ANY)],
        [*held, begun],
        [pl.BlockSpec((rows, width), lambda j, place: (0, 0)) for rows in small_counts],
        [jax.ShapeDtypeStruct((rows, width), f32) for rows in small_counts],
        [pltpu.VMEM((16 * block_rows, width), f32)],
        {8: 0},
    )


def through(decay, total):
    return jnp.exp(decay * total)


def round_kernel(second_ref, decay_log_ref, own_ref, other_ref, *rest, first):
    count, width = decay_log_ref.shape
    new_passed_ref, *ends_refs = rest if first else rest[1:]
    decay = -jnp.exp(decay_log_ref[...])
    second = second_ref[0] > 0

    def split(ref):
        return ref[:count], ref[count : 2 * count], ref[2 * count : 2 * count + 1]

    own, other = split(own_ref), split(other_ref)
    early = [jnp.where(second, b, a) for a, b in zip(own, other)]
    late = [jnp.where(second, a, b) for a, b in zip(own, other)]
    state = late[0] + through(decay, late[2]) * early[0]
    adjoint = early[1] + through(decay, early[2]) * late[1]
    if len(ends_refs) == 2:
        ends_refs[0][...] = state
        ends_refs[1][...] = adjoint
    else:
        ends_refs[0][:count, :] = state
        ends_refs[0][count : 2 * count, :] = adjoint
        ends_refs[0][2 * count :, :] = jnp.broadcast_to(early[2] + late[2], (8, decay.shape[1]))
    if first:
        before = after = jnp.zeros((count, width), f32)
        before_steps = after_steps = jnp.zeros((1, width), f32)
    else:
        before, after = rest[0][:count], rest[0][count : 2 * count]
        before_steps = rest[0][2 * count : 2 * count + 1]
        after_steps = rest[0][2 * count + 1 : 2 * count + 2]
    new_passed_ref[:count, :] = before + jnp.where(second, through(decay, before_steps) * other[0], 0.0)
    new_passed_ref[count : 2 * count, :] = after + jnp.where(
        second, 0.0, through(decay, after_steps) * other[1]
    )
    new_passed_ref[2 * count : 2 * count + 1, :] = before_steps + jnp.where(second, other[2], 0.0)
    new_passed_ref[2 * count + 1 : 2 * count + 2, :] = after_steps + jnp.where(second, 0.0, other[2])


def carried(ends, decay_log):
    count, width = decay_log.shape
    place = lax.axis_index("wide").astype(jnp.int32)
    state = jax.ShapeDtypeStruct((count, width), f32)
    passed_kind = jax.ShapeDtypeStruct((2 * count + 8, width), f32)
    packed, passed = ends, []
    vmem = pl.BlockSpec(memory_space=pltpu.VMEM)
    for k, kinds in enumerate(([jax.ShapeDtypeStruct(ends.shape, f32)], [state, state])):
        new_passed, *out = pl.pallas_call(
            functools.partial(round_kernel, first=k == 0),
            in_specs=[pl.BlockSpec(memory_space=pltpu.SMEM)] + [vmem] * (3 + k),
            out_shape=[passed_kind] + kinds,
            cost_estimate=tiny_cost,
            name="carry_round",
        )((place >> k & 1)[None], decay_log, packed, swapped(packed, "wide", 2**k), *passed)
        packed, passed = out[0], [new_passed]
    from_before = passed_along(out[0], "wide", 4)
    from_after = passed_along(out[1], "wide", -4)
    return passed[0], from_before, from_after


def local(
    tokens,
    norm_gain,
    in_weight,
    conv_weight,
    conv_bias,
    select_weight,
    step_weight,
    step_bias,
    decay_log,
    skip_gain,
    out_weight,
    segment_ids,
    cotangent,
):
    rows, features = tokens.shape
    taps = conv_weight.shape[0]
    columns = select_weight.shape[0]
    rank = step_weight.shape[0]
    count = decay_log.shape[0]
    right_half = lax.axis_index("narrow") == 1

    def both_halves(own, other):
        return jnp.concatenate(
            [jnp.where(right_half, other, own), jnp.where(right_half, own, other)], axis=1
        )

    other_tokens = swapped(tokens, "narrow", 1)
    other_cot = swapped(cotangent, "narrow", 1)
    edge, other_edge = to_next_both(edge_rows_of(segment_ids, tokens))

    whole_low, normed_ext, normed, inverse, masks = normalized(
        tokens, other_tokens, edge, other_edge, norm_gain[None], segment_ids[None]
    )
    projected = jnp.einsum(
        "td,dce->cte", normed_ext, in_weight, preferred_element_type=f32
    ).astype(bf16)
    convolved, act, selected = convolve(
        projected, conv_weight, conv_bias[None], select_weight, masks
    )
    other_selected = swapped(selected, "narrow", 1)
    cot_whole = both_halves(cotangent, other_cot)
    gated_grad = lax.dot_general(
        cot_whole, out_weight, contract_last, preferred_element_type=f32
    )
    step_pre, step, ends = scan_ends(
        selected,
        other_selected,
        step_weight,
        step_bias[None],
        act,
        projected,
        gated_grad,
        masks,
        decay_log,
    )
    passed, entering, returning = carried(ends, decay_log)
    gated, gate_grad, entry = scan_forward(
        selected,
        other_selected,
        step,
        act,
        projected,
        gated_grad,
        masks,
        decay_log,
        passed,
        entering,
        skip_gain[None],
    )
    gated = after(gated, returning)
    products = (
        lax.dot_general(gated, cot_whole, contract_first, preferred_element_type=f32).astype(bf16),
        lax.dot_general(normed, gate_grad, contract_first, preferred_element_type=f32).astype(bf16),
    )
    out_sum, gate_sum = lax.psum(products, "wide")
    wide_place = lax.axis_index("wide").astype(jnp.int32)
    four_place = (wide_place & 3)[None]

    def narrow_halves(array):
        low, high = array[:, :features], array[:, features:]
        return jnp.where(right_half, high, low), jnp.where(right_half, low, high)

    def after_forward(products):
        whole = whole_low.astype(f32)
        act_grad, select_grad, scan_small = scan_backward(
            selected,
            other_selected,
            step_pre,
            step,
            act,
            projected,
            gated_grad,
            masks,
            decay_log,
            entry,
            passed,
            returning,
            skip_gain[None],
            step_weight,
        )
        normed_four = quarter_of_four(after(normed, select_grad))
        inner_main, before, last, conv_small = convolve_grad(
            select_grad,
            swapped(select_grad, "narrow", 1),
            select_weight,
            act_grad,
            convolved,
            act,
            projected,
            conv_weight,
            masks,
            [],
        )
        following = passed_along(before, "wide", -1)
        inner_grad = patched(segment_ids, inner_main, last, following, *normed_four)
        near = swapped(inner_grad, "wide", 2)
        keep, send = small_halves(wide_place[None] & 1, scan_small, conv_small, inner_grad)
        keep, send = folded((wide_place >> 1 & 1)[None], keep, swapped(send, "wide", 1))
        smalls = [keep, swapped(send, "wide", 2)]
        normed_part = jnp.einsum(
            "cte,dce->td", jnp.stack([inner_grad, gate_grad]), in_weight, preferred_element_type=f32
        )
        gain_part = jnp.sum(normed_part * whole * inverse, axis=0, keepdims=True)
        row_part = jnp.sum(normed_part * norm_gain * whole, axis=1)[None]
        first_bits, *more_bits = group_bits(2)
        gain_sum = gain_part + swapped(gain_part, "narrow", 1)
        for bit in (bit for bits in more_bits for bit in bits):
            gain_sum = gain_sum + swapped(gain_sum, "wide", bit)
        row_theirs = swapped(row_part, "narrow", 1)
        near = after(near, gain_sum, row_theirs, smalls[1])
        far = swapped(jnp.concatenate([inner_grad, near]), "wide", 1)
        keep, *sends = inner_quarter(
            (wide_place >> 2 & 3)[None],
            inner_grad,
            near,
            far,
            normed_four,
            smalls,
            [],
        )
        normed_mine, normed_other = narrow_halves(normed_part)
        normed_theirs = swapped(after(normed_other, keep), "narrow", 1)
        out_part = jnp.dot(after(gated, keep), out_weight, preferred_element_type=f32)
        out_mine, out_other = narrow_halves(out_part)
        out_theirs = swapped(out_other, "narrow", 1)
        layer_out = (tokens.astype(f32) + (out_mine + out_theirs)).astype(bf16)
        row_sum = (row_part + row_theirs).reshape(rows, 1)
        gain_mine = jnp.where(right_half, norm_gain[features:], norm_gain[:features])
        whole_grad = inverse * (gain_mine * (normed_mine + normed_theirs)) - tokens.astype(f32) * (
            inverse * inverse * inverse
        ) * (row_sum / (2 * features))
        tokens_grad = (whole_grad + cotangent.astype(f32)).astype(bf16)
        held = keep
        for n, flip in enumerate(flips(first_bits)[1:]):
            held = held + swapped(sends[n], "wide", flip).astype(f32)
        for bits in more_bits:
            held = scattered(held, bits)
        held = held.astype(bf16)
        for bits in reversed(more_bits):
            held = gathered(held, bits)
        spare = jnp.broadcast_to(gain_sum, (block_rows - used_rows, gain_sum.shape[1]))
        held = jnp.concatenate([held[: held.shape[0] - spare.shape[0]], spare.astype(bf16)])
        held = gathered(held, first_bits)
        return held, layer_out, tokens_grad

    kinds = jax.eval_shape(after_forward, products)
    held, layer_out, tokens_grad = lax.cond(
        wide_place >= 0,
        after_forward,
        lambda pair: jax.tree.map(lambda kind: jnp.zeros(kind.shape, kind.dtype), kinds),
        products,
    )

    core = swapped(held, "wide", 1)
    begun, out_weight_grad = joined_first(four_place, gate_sum, held, core, out_sum)
    near = after(swapped(held, "wide", 2), begun)
    far = swapped(near, "wide", 1)
    conv_at = rank + count + 2
    (
        in_weight_grad,
        step_weight_grad,
        decay_log_grad,
        skip_gain_grad,
        step_bias_grad,
        select_weight_grad,
        conv_weight_grad,
        conv_bias_grad,
        norm_gain_grad,
    ) = joined_last(
        four_place,
        gate_sum,
        (held, core, near, far),
        begun,
        (0, rank, rank + count, rank + count + 1, conv_at, conv_at + columns, conv_at + columns + taps),
        (rank, count, 1, 1, columns, taps, 1, 1),
    )
    return (
        layer_out,
        tokens_grad,
        norm_gain_grad[0],
        in_weight_grad,
        conv_weight_grad,
        conv_bias_grad[0],
        select_weight_grad,
        step_weight_grad,
        step_bias_grad[0],
        decay_log_grad,
        skip_gain_grad[0],
        out_weight_grad,
    )


def solution(mesh):
    placed = (
        P("wide", "narrow"),
        P(),
        P(None, None, "narrow"),
        P(None, "narrow"),
        P("narrow"),
        P(None, "narrow"),
        P(None, "narrow"),
        P("narrow"),
        P(None, "narrow"),
        P("narrow"),
        P("narrow", None),
        P("wide"),
        P("wide", "narrow"),
    )
    return jax.shard_map(
        local,
        mesh=mesh,
        in_specs=placed,
        out_specs=(
            P("wide", "narrow"),
            P("wide", "narrow"),
            P(),
            P(None, None, "narrow"),
            P(None, "narrow"),
            P("narrow"),
            P(None, "narrow"),
            P(None, "narrow"),
            P("narrow"),
            P(None, "narrow"),
            P("narrow"),
            P("narrow", None),
        ),
        check_vma=False,
    )
```

```python
import functools

import jax
import jax.numpy as jnp
from jax import lax
from jax.experimental import pallas as pl
from jax.experimental.pallas import tpu as pltpu
from jax.sharding import PartitionSpec as P

epsilon = 1e-05
log2e = 1.4426950408889634
reset_step = 1e30
lanes = 128
halo = 16
body_rows = 32
scan_width = 512
vmem_bytes = 56 * 1024 * 1024
tiny_cost = pl.CostEstimate(flops=1, bytes_accessed=1, transcendentals=0)
f32 = jnp.float32
bf16 = jnp.bfloat16
contract_first = (((0,), (0,)), ((), ()))
contract_last = (((1,), (1,)), ((), ()))


def passed_along(array, axis, by):
    peers = lax.axis_size(axis)
    pairs = [(i, i + by) for i in range(peers) if 0 <= i + by < peers]
    return lax.ppermute(array, axis, pairs)


def swapped(array, axis, bit):
    peers = lax.axis_size(axis)
    return lax.ppermute(array, axis, [(i, i ^ bit) for i in range(peers)])


def wide_bits():
    bit, bits = 1, []
    while bit < lax.axis_size("wide"):
        bits.append(bit)
        bit *= 2
    return bits


def to_next_both(array):
    count, sides = lax.axis_size("wide"), lax.axis_size("narrow")
    pairs = [
        (i * sides + k, (i + 1) * sides + (sides - 1 - k))
        for i in range(count - 1)
        for k in range(sides)
    ]
    return passed_along(array, "wide", 1), lax.ppermute(array, ("wide", "narrow"), pairs)


def is_upper(bit):
    return (lax.axis_index("wide") & bit) != 0


def group_bits(size):
    bits, bit = [], 4
    while bit < lax.axis_size("wide"):
        bits.append(bit)
        bit *= 2
    return [tuple(bits[k : k + size]) for k in range(0, len(bits), size)]


def flips(bits):
    return [sum(b for k, b in enumerate(bits) if n >> k & 1) for n in range(2 ** len(bits))]


def scattered(piece, bits):
    rows = piece.shape[0] // 2 ** len(bits)
    here = sum(is_upper(b).astype(jnp.int32) << k for k, b in enumerate(bits))

    def block(n):
        return lax.dynamic_slice_in_dim(piece, (here ^ n) * rows, rows, 0)

    total = block(0).astype(f32)
    for n, flip in enumerate(flips(bits)):
        if n > 0:
            total = total + swapped(block(n).astype(bf16), "wide", flip).astype(f32)
    return total


def gathered(held, bits):
    blocks = [held] + [swapped(held, "wide", flip) for flip in flips(bits)[1:]]
    for bit in bits:
        upper = is_upper(bit)
        blocks = [
            jnp.concatenate([jnp.where(upper, b, a), jnp.where(upper, a, b)])
            for a, b in zip(blocks[0::2], blocks[1::2])
        ]
    return blocks[0]


def quarter_of_four(array):
    width = array.shape[1] // 4
    here = lax.axis_index("wide") & 3

    def quarter(n):
        return lax.dynamic_slice_in_dim(array, (here ^ n) * width, width, 1)

    return [quarter(0)] + [swapped(quarter(n), "wide", n) for n in (2, 1, 3)]


def silu_slope(values):
    logistic = jax.nn.sigmoid(values)
    return logistic * (1.0 + values * (1.0 - logistic))


def softplus(values):
    return jnp.maximum(values, 0.0) + jnp.log1p(jnp.exp(-jnp.abs(values)))


def column_spec(rows, start=0):
    return pl.BlockSpec((rows, scan_width), lambda j: (0, start + j))


def part_spec(part, rows, start=0):
    return pl.BlockSpec((None, rows, scan_width), lambda j: (part, 0, start + j))


def whole_spec(rows, width):
    return pl.BlockSpec((rows, width), lambda j: (0, 0))


def call(kernel, name, width, in_specs, out_specs, out_shape, scratch, *operands):
    return pl.pallas_call(
        kernel,
        grid=(width // scan_width,),
        in_specs=in_specs,
        out_specs=out_specs,
        out_shape=out_shape,
        scratch_shapes=scratch,
        compiler_params=pltpu.CompilerParams(vmem_limit_bytes=vmem_bytes),
        cost_estimate=tiny_cost,
        name=name,
    )(*operands)


def conv_kernel(
    inner_ref,
    conv_weight_ref,
    conv_bias_ref,
    select_ref,
    mask_ref,
    convolved_ref,
    act_ref,
    selected_ref,
    inner,
):
    rows = act_ref.shape[0]
    taps = conv_weight_ref.shape[0]
    inner[:halo, :] = inner_ref[rows:, :].astype(f32)
    inner[halo:, :] = inner_ref[:rows, :].astype(f32)
    total = conv_bias_ref[...] + conv_weight_ref[taps - 1 :, :] * inner[halo:, :]
    for lag in range(1, taps):
        earlier = inner[pl.ds(halo - lag, rows), :] * mask_ref[:, lag : lag + 1]
        total = total + conv_weight_ref[taps - 1 - lag : taps - lag, :] * earlier
    convolved_ref[...] = total
    act = (total * jax.nn.sigmoid(total)).astype(bf16)
    act_ref[...] = act
    part = lax.dot_general(select_ref[...], act, contract_last, preferred_element_type=f32)

    @pl.when(pl.program_id(0) == 0)
    def _():
        selected_ref[...] = part

    @pl.when(pl.program_id(0) > 0)
    def _():
        selected_ref[...] += part


def convolve(projected, conv_weight, conv_bias, select_weight, masks):
    parts, extended, width = projected.shape
    rows = extended - halo
    taps = conv_weight.shape[0]
    columns = select_weight.shape[0]
    return call(
        conv_kernel,
        "convolve",
        width,
        [
            part_spec(0, extended),
            column_spec(taps),
            column_spec(1),
            column_spec(columns),
            whole_spec(rows, masks.shape[1]),
        ],
        [column_spec(rows), column_spec(rows), whole_spec(columns, rows)],
        [
            jax.ShapeDtypeStruct((rows, width), f32),
            jax.ShapeDtypeStruct((rows, width), bf16),
            jax.ShapeDtypeStruct((columns, rows), f32),
        ],
        [pltpu.VMEM((extended, scan_width), f32)],
        projected,
        conv_weight,
        conv_bias,
        select_weight,
        masks,
    )


def coef_columns(coef, block):
    per_tile = lanes // body_rows
    start = pl.multiple_of((block // per_tile) * lanes, lanes)
    tile = coef[:, pl.ds(start, lanes)]
    back = body_rows * lax.rem(block, per_tile)
    return pltpu.roll(tile, lax.rem(lanes - back, lanes), 1)


def ends_kernel(
    selected_ref,
    other_ref,
    step_weight_ref,
    step_bias_ref,
    act_ref,
    gate_ref,
    gated_grad_ref,
    mask_ref,
    decay_log_ref,
    step_pre_ref,
    step_ref,
    ends_ref,
    coef,
    held_step,
    drive,
    scan_grad,
):
    rows = act_ref.shape[0]
    count = decay_log_ref.shape[0]
    rank = step_weight_ref.shape[0]
    decay2 = -jnp.exp(decay_log_ref[...]) * log2e
    selected = selected_ref[...] + other_ref[...]
    coef[...] = selected[rank:, :]
    step_low = selected[:rank, :].astype(bf16)
    step_pre = step_bias_ref[...] + lax.dot_general(
        step_low, step_weight_ref[...], contract_first, preferred_element_type=f32
    )
    step_pre_ref[...] = step_pre
    step = softplus(step_pre)
    step_ref[...] = step
    held_step[...] = jnp.where(mask_ref[:, 1:2] > 0.0, step, reset_step)
    drive[...] = step * act_ref[...].astype(f32)
    gate = gate_ref[...].astype(f32)
    scan_grad[...] = gated_grad_ref[...] * (gate * jax.nn.sigmoid(gate))
    zero = jnp.zeros(decay2.shape, f32)

    def body(block, carried):
        state, product, adjoint = carried
        columns = coef_columns(coef, block)
        for i in range(body_rows):
            row = pl.ds(block * body_rows + i, 1)
            factor = jnp.exp2(held_step[row, :] * decay2)
            state = factor * state + columns[:count, i : i + 1] * drive[row, :]
            product = factor * product
            adjoint = adjoint + product * (columns[count:, i : i + 1] * scan_grad[row, :])
        return state, product, adjoint

    state, product, adjoint = lax.fori_loop(0, rows // body_rows, body, (zero, zero + 1.0, zero))
    ends_ref[:count, :] = state
    ends_ref[count : 2 * count, :] = adjoint
    total = jnp.sum(held_step[...], axis=0, keepdims=True)
    ends_ref[2 * count :, :] = jnp.broadcast_to(total, (8, total.shape[1]))


def scan_ends(
    selected, other, step_weight, step_bias, act, projected, gated_grad, masks, decay_log
):
    rows, width = act.shape
    count = decay_log.shape[0]
    columns = selected.shape[0]
    rank = step_weight.shape[0]
    return call(
        ends_kernel,
        "scan_ends",
        width,
        [
            whole_spec(columns, rows),
            whole_spec(columns, rows),
            column_spec(rank),
            column_spec(1),
            column_spec(rows),
            part_spec(1, rows),
            column_spec(rows),
            whole_spec(rows, masks.shape[1]),
            column_spec(count),
        ],
        [column_spec(rows), column_spec(rows), column_spec(2 * count + 8)],
        [
            jax.ShapeDtypeStruct((rows, width), f32),
            jax.ShapeDtypeStruct((rows, width), f32),
            jax.ShapeDtypeStruct((2 * count + 8, width), f32),
        ],
        [pltpu.VMEM((2 * count, rows), f32)] + [pltpu.VMEM((rows, scan_width), f32)] * 3,
        selected,
        other,
        step_weight,
        step_bias,
        act,
        projected,
        gated_grad,
        masks,
        decay_log,
    )


def lane_tiles(values):
    return [values[:, k : k + lanes] for k in range(0, values.shape[1], lanes)]


def tree_sum(parts):
    while len(parts) > 1:
        odd = parts[len(parts) // 2 * 2 :]
        parts = [a + b for a, b in zip(parts[0::2], parts[1::2])] + odd
    return parts[0]


def keep_halves(scratch, i, values):
    for k, tile in enumerate(lane_tiles(values)):
        at = (k * body_rows + i) * 8
        scratch[at : at + 8, :] = tile[:8] + tile[8:]


def put_state_sums(scratch, out_ref, block):
    for group in range(body_rows // 8):
        row = pl.ds(pl.multiple_of(block * body_rows + group * 8, 8), 8)
        for k in range(out_ref.shape[1] // lanes):
            at = (k * body_rows + group * 8) * 8
            total = tree_sum([scratch[pl.ds(at + n, 8, stride=8), :] for n in range(8)])
            out_ref[row, k * lanes : (k + 1) * lanes] = total


def lane_sums(values):
    ones = jnp.ones((8, lanes), bf16)
    high = values.astype(bf16)
    low = (values - high.astype(f32)).astype(bf16)
    total = lax.dot_general(ones, high, contract_last, preferred_element_type=f32)
    total += lax.dot_general(ones, low, contract_last, preferred_element_type=f32)
    return total[:1, :]


def at_token(t, count):
    return pl.ds(pl.multiple_of(t * count, count), count)


def forward_kernel(
    selected_ref,
    other_ref,
    step_ref,
    act_ref,
    gate_ref,
    gated_grad_ref,
    mask_ref,
    decay_log_ref,
    passed_ref,
    entering_ref,
    skip_ref,
    gated_ref,
    gate_grad_ref,
    entry_ref,
    coef,
    held_step,
    drive,
    scanned,
    halves,
):
    rows = step_ref.shape[0]
    count = decay_log_ref.shape[0]
    rank = selected_ref.shape[0] - 2 * count
    decay = -jnp.exp(decay_log_ref[...])
    decay2 = decay * log2e
    before_steps = passed_ref[2 * count : 2 * count + 1, :]
    entry = passed_ref[:count, :] + through(decay, before_steps) * entering_ref[...]
    entry_ref[...] = entry
    coef[...] = selected_ref[rank:, :] + other_ref[rank:, :]
    act = act_ref[...].astype(f32)
    held_step[...] = jnp.where(mask_ref[:, 1:2] > 0.0, step_ref[...], reset_step)
    drive[...] = step_ref[...] * act

    def forward(block, state):
        columns = coef_columns(coef, block)
        for i in range(body_rows):
            row = pl.ds(block * body_rows + i, 1)
            factor = jnp.exp2(held_step[row, :] * decay2)
            state = factor * state + columns[:count, i : i + 1] * drive[row, :]
            keep_halves(halves, i, columns[count:, i : i + 1] * state)
        put_state_sums(halves, scanned, block)
        return state

    lax.fori_loop(0, rows // body_rows, forward, entry)
    gate = gate_ref[...].astype(f32)
    logistic = jax.nn.sigmoid(gate)
    total = scanned[...] + skip_ref[...] * act
    gated_ref[...] = (total * (gate * logistic)).astype(bf16)
    slope = logistic * (1.0 + gate * (1.0 - logistic))
    gate_grad_ref[...] = (gated_grad_ref[...] * total * slope).astype(bf16)


def scan_forward(
    selected, other, step, act, projected, gated_grad, masks, decay_log, passed, entering, skip_gain
):
    rows, width = step.shape
    count = decay_log.shape[0]
    columns = selected.shape[0]
    return call(
        forward_kernel,
        "scan_forward",
        width,
        [
            whole_spec(columns, rows),
            whole_spec(columns, rows),
            column_spec(rows),
            column_spec(rows),
            part_spec(1, rows),
            column_spec(rows),
            whole_spec(rows, masks.shape[1]),
            column_spec(count),
            column_spec(2 * count + 8),
            column_spec(count),
            column_spec(1),
        ],
        [column_spec(rows), column_spec(rows), column_spec(count)],
        [
            jax.ShapeDtypeStruct((rows, width), bf16),
            jax.ShapeDtypeStruct((rows, width), bf16),
            jax.ShapeDtypeStruct((count, width), f32),
        ],
        [pltpu.VMEM((2 * count, rows), f32)]
        + [pltpu.VMEM((rows, scan_width), f32)] * 3
        + [pltpu.VMEM((8 * body_rows * (scan_width // lanes), lanes), f32)],
        selected,
        other,
        step,
        act,
        projected,
        gated_grad,
        masks,
        decay_log,
        passed,
        entering,
        skip_gain,
    )


def backward_kernel(
    selected_ref,
    other_ref,
    step_pre_ref,
    step_ref,
    act_ref,
    gate_ref,
    gated_grad_ref,
    mask_ref,
    decay_log_ref,
    entry_ref,
    passed_ref,
    returning_ref,
    skip_ref,
    step_weight_ref,
    act_grad_ref,
    select_grad_ref,
    small_ref,
    coef,
    held_step,
    drive,
    scan_grad,
    weighted,
    held_sum,
    states,
    factors,
    halves,
    more_halves,
    in_sum,
    read_sum,
):
    rows = step_ref.shape[0]
    count = decay_log_ref.shape[0]
    rank = step_weight_ref.shape[0]
    blocks = rows // body_rows
    decay = -jnp.exp(decay_log_ref[...])
    decay2 = decay * log2e
    after_steps = passed_ref[2 * count + 1 : 2 * count + 2, :]
    tail = passed_ref[count : 2 * count, :] + through(decay, after_steps) * returning_ref[...]
    selected = selected_ref[...] + other_ref[...]
    coef[...] = selected[rank:, :]
    step_low = selected[:rank, :].astype(bf16)
    step = step_ref[...]
    act = act_ref[...].astype(f32)
    held_step[...] = jnp.where(mask_ref[:, 1:2] > 0.0, step, reset_step)
    drive[...] = step * act
    gate = gate_ref[...].astype(f32)
    grads = gated_grad_ref[...] * (gate * jax.nn.sigmoid(gate))
    scan_grad[...] = grads
    small_ref[rank + count : rank + count + 1, :] = jnp.sum(grads * act, axis=0, keepdims=True)
    states[:count, :] = entry_ref[...]

    @pl.when(pl.program_id(0) == 0)
    def _():
        in_sum[...] = jnp.zeros(in_sum.shape, f32)
        read_sum[...] = jnp.zeros(read_sum.shape, f32)
        select_grad_ref[...] = jnp.zeros(select_grad_ref.shape, f32)

    def forward(block, state):
        columns = coef_columns(coef, block)
        for i in range(body_rows):
            t = block * body_rows + i
            row = pl.ds(t, 1)
            factor = jnp.exp2(held_step[row, :] * decay2)
            state = factor * state + columns[:count, i : i + 1] * drive[row, :]
            factors[at_token(t, count), :] = factor
            states[at_token(t + 1, count), :] = state
        return state

    lax.fori_loop(0, blocks, forward, entry_ref[...])

    def backward(k, carried):
        adjoint, decay_grad = carried
        block = blocks - 1 - k
        columns = coef_columns(coef, block)
        for i in range(body_rows - 1, -1, -1):
            t = block * body_rows + i
            row = pl.ds(t, 1)
            here = at_token(t, count)
            grad = scan_grad[row, :]
            summed = columns[count:, i : i + 1] * grad + adjoint
            read_sum[here, :] += tree_sum(lane_tiles(grad * states[at_token(t + 1, count), :]))
            in_sum[here, :] += tree_sum(lane_tiles(summed * drive[row, :]))
            keep_halves(halves, i, summed * columns[:count, i : i + 1])
            adjoint = factors[here, :] * summed
            held = adjoint * states[here, :]
            decay_grad = decay_grad + held * step_ref[row, :]
            keep_halves(more_halves, i, held * decay)
        put_state_sums(halves, weighted, block)
        put_state_sums(more_halves, held_sum, block)
        return adjoint, decay_grad

    ignored, decay_grad = lax.fori_loop(
        0, blocks, backward, (tail, jnp.zeros(decay.shape, f32))
    )
    act_grad_ref[...] = step * weighted[...] + skip_ref[...] * scan_grad[...]
    step_grad = act * weighted[...] + held_sum[...]
    pre_grad = (step_grad * jax.nn.sigmoid(step_pre_ref[...])).astype(bf16)
    small_ref[:rank, :] = jnp.dot(step_low, pre_grad, preferred_element_type=f32)
    small_ref[rank : rank + count, :] = decay_grad * decay
    bias_grad = jnp.sum(pre_grad.astype(f32), axis=0, keepdims=True)
    small_ref[rank + count + 1 : rank + count + 2, :] = bias_grad
    select_grad_ref[:rank, :] += lax.dot_general(
        step_weight_ref[...], pre_grad, contract_last, preferred_element_type=f32
    )

    @pl.when(pl.program_id(0) == pl.num_programs(0) - 1)
    def _():
        for n in range(count):
            at = pl.ds(n, rows, stride=count)
            select_grad_ref[rank + n : rank + n + 1, :] = lane_sums(in_sum[at, :])
            select_grad_ref[rank + count + n : rank + count + n + 1, :] = lane_sums(read_sum[at, :])


def scan_backward(
    selected,
    other,
    step_pre,
    step,
    act,
    projected,
    gated_grad,
    masks,
    decay_log,
    entry,
    passed,
    returning,
    skip_gain,
    step_weight,
):
    rows, width = step.shape
    count = decay_log.shape[0]
    columns = selected.shape[0]
    rank = step_weight.shape[0]
    half_rows = 8 * body_rows * (scan_width // lanes)
    small = rank + count + 2
    return call(
        backward_kernel,
        "scan_backward",
        width,
        [
            whole_spec(columns, rows),
            whole_spec(columns, rows),
            column_spec(rows),
            column_spec(rows),
            column_spec(rows),
            part_spec(1, rows),
            column_spec(rows),
            whole_spec(rows, masks.shape[1]),
            column_spec(count),
            column_spec(count),
            column_spec(2 * count + 8),
            column_spec(count),
            column_spec(1),
            column_spec(rank),
        ],
        [column_spec(rows), whole_spec(columns, rows), column_spec(small)],
        [
            jax.ShapeDtypeStruct((rows, width), f32),
            jax.ShapeDtypeStruct((columns, rows), f32),
            jax.ShapeDtypeStruct((small, width), f32),
        ],
        [pltpu.VMEM((2 * count, rows), f32)]
        + [pltpu.VMEM((rows, scan_width), f32)] * 5
        + [
            pltpu.VMEM(((rows + 1) * count, scan_width), f32),
            pltpu.VMEM((rows * count, scan_width), f32),
            pltpu.VMEM((half_rows, lanes), f32),
            pltpu.VMEM((half_rows, lanes), f32),
            pltpu.VMEM((rows * count, lanes), f32),
            pltpu.VMEM((rows * count, lanes), f32),
        ],
        selected,
        other,
        step_pre,
        step,
        act,
        projected,
        gated_grad,
        masks,
        decay_log,
        entry,
        passed,
        returning,
        skip_gain,
        step_weight,
    )


def conv_grad_kernel(
    select_grad_ref,
    other_ref,
    select_ref,
    act_grad_ref,
    convolved_ref,
    act_ref,
    inner_ref,
    conv_weight_ref,
    mask_ref,
    *rest,
):
    inner_grad_ref, before_ref, last_ref, small_ref, inner, shifted = rest[-6:]
    rows = act_ref.shape[0]
    taps = conv_weight_ref.shape[0]
    columns = select_ref.shape[0]
    select_grad = (select_grad_ref[...] + other_ref[...]).astype(bf16)
    total = act_grad_ref[...] + lax.dot_general(
        select_grad, select_ref[...], contract_first, preferred_element_type=f32
    )
    conv_grad = total * silu_slope(convolved_ref[...])
    small_ref[:columns, :] = jnp.dot(select_grad, act_ref[...], preferred_element_type=f32)
    inner[:halo, :] = inner_ref[rows:, :].astype(f32)
    inner[halo:, :] = inner_ref[:rows, :].astype(f32)
    edges = jnp.zeros((8, conv_grad.shape[1]), f32)
    shifted[:8, :] = edges
    shifted[rows + 8 :, :] = edges
    out = conv_weight_ref[taps - 1 :, :] * conv_grad
    before = edges
    small_ref[columns + taps - 1 : columns + taps, :] = jnp.sum(
        conv_grad * inner[halo:, :], axis=0, keepdims=True
    )
    for lag in range(1, taps):
        masked = conv_grad * mask_ref[:, lag : lag + 1]
        at = taps - 1 - lag
        small_ref[columns + at : columns + at + 1, :] = jnp.sum(
            masked * inner[pl.ds(halo - lag, rows), :], axis=0, keepdims=True
        )
        shifted[8 : rows + 8, :] = masked
        weight = conv_weight_ref[at : at + 1, :]
        out = out + weight * shifted[pl.ds(8 + lag, rows), :]
        before = before + weight * shifted[pl.ds(lag, 8), :]
    small_ref[columns + taps : columns + taps + 1, :] = jnp.sum(conv_grad, axis=0, keepdims=True)
    inner_grad_ref[...] = out.astype(bf16)
    before_ref[...] = before
    last_ref[...] = out[rows - 8 :, :]


def convolve_grad(
    select_grad, other, select_weight, act_grad, convolved, act, projected, conv_weight, masks, waits
):
    rows, width = act.shape
    extended = rows + halo
    columns = select_weight.shape[0]
    taps = conv_weight.shape[0]
    small = columns + taps + 1
    return call(
        conv_grad_kernel,
        "convolve_grad",
        width,
        [
            whole_spec(columns, rows),
            whole_spec(columns, rows),
            column_spec(columns),
            column_spec(rows),
            column_spec(rows),
            column_spec(rows),
            part_spec(0, extended),
            column_spec(taps),
            whole_spec(rows, masks.shape[1]),
        ]
        + [pl.BlockSpec(memory_space=pl.ANY)] * len(waits),
        [column_spec(rows), column_spec(8), column_spec(8), column_spec(small)],
        [
            jax.ShapeDtypeStruct((rows, width), bf16),
            jax.ShapeDtypeStruct((8, width), f32),
            jax.ShapeDtypeStruct((8, width), f32),
            jax.ShapeDtypeStruct((small, width), f32),
        ],
        [pltpu.VMEM((extended, scan_width), f32), pltpu.VMEM((rows + 16, scan_width), f32)],
        select_grad,
        other,
        select_weight,
        act_grad,
        convolved,
        act,
        projected,
        conv_weight,
        masks,
        *waits,
    )


def normalize_kernel(
    own_ref,
    other_ref,
    edge_ref,
    other_edge_ref,
    gain_ref,
    ids_ref,
    whole_ref,
    extended_ref,
    normed_ref,
    inverse_ref,
    mask_ref,
    rows_ref,
):
    rows, half = own_ref.shape
    ids = ids_ref[...].astype(f32)
    place = lax.broadcasted_iota(jnp.int32, ids.shape, 1)
    same = []
    for lag in range(8):
        earlier = jnp.where(place < lag, ids[:, :1], pltpu.roll(ids, lag, 1)) if lag else ids
        same.append(jnp.where(earlier == ids, 1.0, 0.0))
    spare = jnp.zeros((lanes - 8, rows), f32)
    mask_ref[...] = jnp.concatenate(same + [spare]).T
    right = lax.axis_index("narrow") == 1
    for at, own, other in ((0, own_ref, other_ref), (rows, edge_ref, other_edge_ref)):
        end = at + own.shape[0]
        rows_ref[at:end, :half] = jnp.where(right, other[...], own[...])
        rows_ref[at:end, half:] = jnp.where(right, own[...], other[...])
    whole_ref[...] = rows_ref[:rows, :]
    whole = rows_ref[...].astype(f32)
    inverse = lax.rsqrt(jnp.mean(whole * whole, axis=1, keepdims=True) + epsilon)
    normed = (whole * inverse * gain_ref[...]).astype(bf16)
    extended_ref[...] = normed
    normed_ref[...] = normed[:rows]
    inverse_ref[...] = inverse[:rows]


def normalized(own, other, edge, other_edge, gain, ids):
    rows, half = own.shape
    extended = rows + edge.shape[0]
    return pl.pallas_call(
        normalize_kernel,
        out_shape=[
            jax.ShapeDtypeStruct((rows, 2 * half), bf16),
            jax.ShapeDtypeStruct((extended, 2 * half), bf16),
            jax.ShapeDtypeStruct((rows, 2 * half), bf16),
            jax.ShapeDtypeStruct((rows, 1), f32),
            jax.ShapeDtypeStruct((rows, lanes), f32),
        ],
        scratch_shapes=[pltpu.VMEM((extended, 2 * half), bf16)],
        cost_estimate=tiny_cost,
        name="normalized",
    )(own, other, edge, other_edge, gain, ids)


def after(array, *waits):
    anywhere = pl.BlockSpec(memory_space=pl.ANY)
    return pl.pallas_call(
        lambda *refs: None,
        in_specs=[anywhere] * (1 + len(waits)),
        out_specs=anywhere,
        out_shape=jax.ShapeDtypeStruct(array.shape, array.dtype),
        input_output_aliases={0: 0},
        cost_estimate=tiny_cost,
        name="after",
    )(array, *waits)


def patch_kernel(ids_ref, rows_ref, last_ref, next_ref, *rest):
    count = ids_ref.shape[0]
    place = lax.broadcasted_iota(jnp.int32, (8, 1), 0)
    same = jnp.zeros((8, 1), f32)
    for lag in range(8):
        here = jnp.where(ids_ref[count - 1 - lag] == ids_ref[count - 1], 1.0, 0.0)
        same = same + jnp.where(place == 7 - lag, here, 0.0)
    total = last_ref[...] + next_ref[...] * same
    rows = rows_ref[...].astype(f32)
    rest[-1][...] = jnp.concatenate([rows[: halo - 8], total]).astype(bf16)


def patched(ids, grads, last, following, *waits):
    rows, width = grads.shape
    block = pl.BlockSpec((halo, width), lambda j: (rows // halo - 1, 0))
    edge = pl.BlockSpec((8, width), lambda j: (0, 0))
    return pl.pallas_call(
        patch_kernel,
        grid=(1,),
        in_specs=[pl.BlockSpec(memory_space=pltpu.SMEM), block, edge, edge]
        + [pl.BlockSpec(memory_space=pl.ANY)] * len(waits),
        out_specs=block,
        out_shape=jax.ShapeDtypeStruct((rows, width), bf16),
        input_output_aliases={1: 0},
        cost_estimate=tiny_cost,
        name="patched",
    )(ids, grads, last, following, *waits)


def edge_kernel(ids_ref, tokens_ref, out_ref):
    rows = ids_ref.shape[0]
    taps = 4
    out_ref[...] = tokens_ref[...]
    place = lax.broadcasted_iota(jnp.int32, (halo, 1), 0)
    same = jnp.zeros((halo, 1), f32)
    for lag in range(taps):
        here = jnp.where(ids_ref[rows - 1 - lag] == ids_ref[rows - 1], 1.0, 0.0)
        same = same + jnp.where(place == halo - 1 - lag, here, 0.0)
    out_ref[...] = (tokens_ref[...].astype(f32) * same).astype(bf16)


def edge_rows_of(ids, tokens):
    rows, width = tokens.shape
    return pl.pallas_call(
        edge_kernel,
        grid=(1,),
        in_specs=[
            pl.BlockSpec(memory_space=pltpu.SMEM),
            pl.BlockSpec((halo, width), lambda j: (rows // halo - 1, 0)),
        ],
        out_specs=pl.BlockSpec((halo, width), lambda j: (0, 0)),
        out_shape=jax.ShapeDtypeStruct((halo, width), bf16),
        cost_estimate=tiny_cost,
        name="edge_rows",
    )(ids, tokens)


block_rows, used_rows = 16, 12


def small_kernel(core_ref, scan_ref, conv_ref, wait_ref, keep_ref, send_ref, rows, blocks):
    rows[...] = jnp.zeros(rows.shape, f32)
    rows[: scan_ref.shape[0], :] = scan_ref[...]
    rows[scan_ref.shape[0] : scan_ref.shape[0] + conv_ref.shape[0], :] = conv_ref[...]
    blocks[...] = jnp.zeros(blocks.shape, f32)
    for n in range(16):
        blocks[n * block_rows : n * block_rows + used_rows, :] = rows[
            n * used_rows : (n + 1) * used_rows, :
        ]
    half = keep_ref.shape[0]
    mine = pl.ds(pl.multiple_of(core_ref[0] * half, half), half)
    other = pl.ds(pl.multiple_of((1 - core_ref[0]) * half, half), half)
    keep_ref[...] = blocks[mine, :]
    send_ref[...] = blocks[other, :].astype(bf16)


def small_halves(core, scan_small, conv_small, wait):
    width = scan_small.shape[1]
    return pl.pallas_call(
        small_kernel,
        in_specs=[pl.BlockSpec(memory_space=pltpu.SMEM)]
        + [pl.BlockSpec(memory_space=pltpu.VMEM)] * 2
        + [pl.BlockSpec(memory_space=pl.ANY)],
        out_shape=[jax.ShapeDtypeStruct((8 * block_rows, width), kind) for kind in (f32, bf16)],
        scratch_shapes=[
            pltpu.VMEM((16 * used_rows, width), f32),
            pltpu.VMEM((16 * block_rows, width), f32),
        ],
        cost_estimate=tiny_cost,
        name="small_halves",
    )(core, scan_small, conv_small, wait)


def fold_kernel(upper_ref, keep_ref, arrived_ref, out_ref, send_ref):
    size = out_ref.shape[0]
    mine = pl.ds(pl.multiple_of(upper_ref[0] * size, size), size)
    other = pl.ds(pl.multiple_of((1 - upper_ref[0]) * size, size), size)
    out_ref[...] = keep_ref[mine, :] + arrived_ref[mine, :].astype(f32)
    send_ref[...] = (keep_ref[other, :] + arrived_ref[other, :].astype(f32)).astype(bf16)


def folded(upper, keep, arrived):
    rows, width = keep.shape
    return pl.pallas_call(
        fold_kernel,
        in_specs=[pl.BlockSpec(memory_space=pltpu.SMEM)]
        + [pl.BlockSpec(memory_space=pltpu.VMEM)] * 2,
        out_shape=[jax.ShapeDtypeStruct((rows // 2, width), kind) for kind in (f32, bf16)],
        cost_estimate=tiny_cost,
        name="folded",
    )(upper, keep, arrived)


def quarter_kernel(
    place_ref,
    own_ref,
    near_ref,
    far_ref,
    normed_0,
    normed_1,
    normed_2,
    normed_3,
    small_ref,
    arrived_ref,
    *rest,
):
    keep_ref, *sends_refs, piece, small = rest[-6:]
    total = None
    tokens = own_ref.shape[0]
    grads = (own_ref[...], near_ref[...], far_ref[:tokens, :], far_ref[tokens:, :])
    for left, right in zip((normed_0, normed_1, normed_2, normed_3), grads):
        part = lax.dot_general(left[...], right, contract_first, preferred_element_type=f32)
        total = part if total is None else total + part
    piece[...] = total
    small[...] = small_ref[...] + arrived_ref[...].astype(f32)
    rows, spare = piece.shape[0] // 4, small.shape[0] // 4
    for n in range(4):
        block = place_ref[0] ^ n
        inner_rows = piece[pl.ds(pl.multiple_of(block * rows, rows), rows), :]
        small_rows = small[pl.ds(pl.multiple_of(block * spare, spare), spare), :]
        if n == 0:
            keep_ref[:rows, :] = inner_rows
            keep_ref[rows:, :] = small_rows
        else:
            sends_refs[n - 1][:rows, :] = inner_rows.astype(bf16)
            sends_refs[n - 1][rows:, :] = small_rows.astype(bf16)


def inner_quarter(place, own, near, far, normed, smalls, waits):
    width = own.shape[1]
    quarter = normed[0].shape[1]
    spare = smalls[0].shape[0]
    rows = (quarter + spare) // 4
    return pl.pallas_call(
        quarter_kernel,
        in_specs=[pl.BlockSpec(memory_space=pltpu.SMEM)]
        + [pl.BlockSpec(memory_space=pltpu.VMEM)] * 9
        + [pl.BlockSpec(memory_space=pl.ANY)] * len(waits),
        out_shape=[jax.ShapeDtypeStruct((rows, width), f32)]
        + [jax.ShapeDtypeStruct((rows, width), bf16)] * 3,
        scratch_shapes=[pltpu.VMEM((quarter, width), f32), pltpu.VMEM((spare, width), f32)],
        compiler_params=pltpu.CompilerParams(vmem_limit_bytes=vmem_bytes),
        cost_estimate=tiny_cost,
        name="inner_quarter",
    )(place, own, near, far, *normed, *smalls, *waits)


def put_quarter(out_ref, gate_ref, inner_ref):
    rows = out_ref.shape[0] // 4
    out_ref[:, 1, :] = gate_ref[...].astype(f32)
    for n in range(4):
        at = n * (rows + block_rows)
        out_ref[n * rows : (n + 1) * rows, 0, :] = inner_ref[at : at + rows, :].astype(f32)


def first_join_kernel(place_ref, gate_ref, first_ref, second_ref, low_ref, out_ref, wide_ref):
    wide_ref[...] = low_ref[...].astype(f32)

    @pl.when(pl.program_id(0) == 0)
    def _():
        put_quarter(out_ref, gate_ref, first_ref)

    @pl.when(pl.program_id(0) == 1)
    def _():
        put_quarter(out_ref, gate_ref, second_ref)


def last_join_kernel(place_ref, gate_ref, first_ref, second_ref, *rest, small_rows):
    held = rest[:4]
    out_ref, *row_refs, gain_ref, blocks = rest[5:]

    @pl.when(pl.program_id(0) == 0)
    def _():
        put_quarter(out_ref, gate_ref, first_ref)

    @pl.when(pl.program_id(0) == 1)
    def _():
        put_quarter(out_ref, gate_ref, second_ref)
        rows = out_ref.shape[0] // 4
        for flip, ref in enumerate(held):
            number = place_ref[0] ^ flip
            number = (number & 1) * 2 + number // 2
            for n in range(4):
                at = (number * 4 + n) * block_rows
                taken = ref[(n + 1) * rows + n * block_rows : (n + 1) * (rows + block_rows), :]
                blocks[pl.ds(pl.multiple_of(at, block_rows), block_rows), :] = taken.astype(f32)
        for ref, start in zip(row_refs, small_rows):
            for row in range(ref.shape[0]):
                at = (start + row) // used_rows * block_rows + (start + row) % used_rows
                ref[row : row + 1, :] = blocks[at : at + 1, :]
        gain_ref[...] = sum(
            blocks[n * block_rows + used_rows : n * block_rows + used_rows + 1, :] for n in range(16)
        )


def joined(kernel, place, flip, gate, first, second, specs, operands, out_specs, out_shape, scratch, aliases):
    depth, width = gate.shape
    quarter = depth // 4

    def target(j, place):
        return place[0] ^ (flip + j)

    whole = pl.BlockSpec(first.shape, lambda j, place: (0, 0))
    return pl.pallas_call(
        kernel,
        grid_spec=pltpu.PrefetchScalarGridSpec(
            num_scalar_prefetch=1,
            grid=(2,),
            in_specs=[
                pl.BlockSpec((quarter, width), lambda j, place: (target(j, place), 0)),
                whole,
                whole,
            ]
            + specs,
            out_specs=[
                pl.BlockSpec((quarter, 2, width), lambda j, place: (target(j, place), 0, 0))
            ]
            + out_specs,
            scratch_shapes=scratch,
        ),
        out_shape=[jax.ShapeDtypeStruct((depth, 2, width), f32)] + out_shape,
        input_output_aliases=aliases,
        compiler_params=pltpu.CompilerParams(vmem_limit_bytes=vmem_bytes),
        cost_estimate=tiny_cost,
        name="joined",
    )(place, gate, first, second, *operands)


def joined_first(place, gate, first, second, low):
    rows, width = low.shape
    half = pl.BlockSpec((rows // 2, width), lambda j, place: (j, 0))
    kind = jax.ShapeDtypeStruct((rows, width), f32)
    return joined(
        first_join_kernel, place, 0, gate, first, second, [half], [low], [half], [kind], [], {}
    )


def joined_last(place, gate, held, begun, small_rows, small_counts):
    width = gate.shape[1]
    whole = pl.BlockSpec(held[0].shape, lambda j, place: (0, 0))
    return joined(
        functools.partial(last_join_kernel, small_rows=small_rows),
        place,
        2,
        gate,
        held[2],
        held[3],
        [whole] * 4 + [pl.BlockSpec(memory_space=pl.ANY)],
        [*held, begun],
        [pl.BlockSpec((rows, width), lambda j, place: (0, 0)) for rows in small_counts],
        [jax.ShapeDtypeStruct((rows, width), f32) for rows in small_counts],
        [pltpu.VMEM((16 * block_rows, width), f32)],
        {8: 0},
    )


def through(decay, total):
    return jnp.exp(decay * total)


def round_kernel(second_ref, decay_log_ref, own_ref, other_ref, *rest, first):
    count, width = decay_log_ref.shape
    new_passed_ref, *ends_refs = rest if first else rest[1:]
    decay = -jnp.exp(decay_log_ref[...])
    second = second_ref[0] > 0

    def split(ref):
        return ref[:count], ref[count : 2 * count], ref[2 * count : 2 * count + 1]

    own, other = split(own_ref), split(other_ref)
    early = [jnp.where(second, b, a) for a, b in zip(own, other)]
    late = [jnp.where(second, a, b) for a, b in zip(own, other)]
    state = late[0] + through(decay, late[2]) * early[0]
    adjoint = early[1] + through(decay, early[2]) * late[1]
    if len(ends_refs) == 2:
        ends_refs[0][...] = state
        ends_refs[1][...] = adjoint
    else:
        ends_refs[0][:count, :] = state
        ends_refs[0][count : 2 * count, :] = adjoint
        ends_refs[0][2 * count :, :] = jnp.broadcast_to(early[2] + late[2], (8, decay.shape[1]))
    if first:
        before = after = jnp.zeros((count, width), f32)
        before_steps = after_steps = jnp.zeros((1, width), f32)
    else:
        before, after = rest[0][:count], rest[0][count : 2 * count]
        before_steps = rest[0][2 * count : 2 * count + 1]
        after_steps = rest[0][2 * count + 1 : 2 * count + 2]
    new_passed_ref[:count, :] = before + jnp.where(second, through(decay, before_steps) * other[0], 0.0)
    new_passed_ref[count : 2 * count, :] = after + jnp.where(
        second, 0.0, through(decay, after_steps) * other[1]
    )
    new_passed_ref[2 * count : 2 * count + 1, :] = before_steps + jnp.where(second, other[2], 0.0)
    new_passed_ref[2 * count + 1 : 2 * count + 2, :] = after_steps + jnp.where(second, 0.0, other[2])


def carried(ends, decay_log):
    count, width = decay_log.shape
    place = lax.axis_index("wide").astype(jnp.int32)
    state = jax.ShapeDtypeStruct((count, width), f32)
    passed_kind = jax.ShapeDtypeStruct((2 * count + 8, width), f32)
    packed, passed = ends, []
    vmem = pl.BlockSpec(memory_space=pltpu.VMEM)
    for k, kinds in enumerate(([jax.ShapeDtypeStruct(ends.shape, f32)], [state, state])):
        new_passed, *out = pl.pallas_call(
            functools.partial(round_kernel, first=k == 0),
            in_specs=[pl.BlockSpec(memory_space=pltpu.SMEM)] + [vmem] * (3 + k),
            out_shape=[passed_kind] + kinds,
            cost_estimate=tiny_cost,
            name="carry_round",
        )((place >> k & 1)[None], decay_log, packed, swapped(packed, "wide", 2**k), *passed)
        packed, passed = out[0], [new_passed]
    from_before = passed_along(out[0], "wide", 4)
    from_after = passed_along(out[1], "wide", -4)
    return passed[0], from_before, from_after


def local(
    tokens,
    norm_gain,
    in_weight,
    conv_weight,
    conv_bias,
    select_weight,
    step_weight,
    step_bias,
    decay_log,
    skip_gain,
    out_weight,
    segment_ids,
    cotangent,
):
    rows, features = tokens.shape
    taps = conv_weight.shape[0]
    columns = select_weight.shape[0]
    rank = step_weight.shape[0]
    count = decay_log.shape[0]
    right_half = lax.axis_index("narrow") == 1

    def both_halves(own, other):
        return jnp.concatenate(
            [jnp.where(right_half, other, own), jnp.where(right_half, own, other)], axis=1
        )

    other_tokens = swapped(tokens, "narrow", 1)
    other_cot = swapped(cotangent, "narrow", 1)
    edge, other_edge = to_next_both(edge_rows_of(segment_ids, tokens))

    whole_low, normed_ext, normed, inverse, masks = normalized(
        tokens, other_tokens, edge, other_edge, norm_gain[None], segment_ids[None]
    )
    projected = jnp.einsum(
        "td,dce->cte", normed_ext, in_weight, preferred_element_type=f32
    ).astype(bf16)
    convolved, act, selected = convolve(
        projected, conv_weight, conv_bias[None], select_weight, masks
    )
    other_selected = swapped(selected, "narrow", 1)
    cot_whole = both_halves(cotangent, other_cot)
    gated_grad = lax.dot_general(
        cot_whole, out_weight, contract_last, preferred_element_type=f32
    )
    step_pre, step, ends = scan_ends(
        selected,
        other_selected,
        step_weight,
        step_bias[None],
        act,
        projected,
        gated_grad,
        masks,
        decay_log,
    )
    passed, entering, returning = carried(ends, decay_log)
    gated, gate_grad, entry = scan_forward(
        selected,
        other_selected,
        step,
        act,
        projected,
        gated_grad,
        masks,
        decay_log,
        passed,
        entering,
        skip_gain[None],
    )
    gated = after(gated, returning)
    products = (
        lax.dot_general(gated, cot_whole, contract_first, preferred_element_type=f32).astype(bf16),
        lax.dot_general(normed, gate_grad, contract_first, preferred_element_type=f32).astype(bf16),
    )
    out_sum, gate_sum = lax.psum(products, "wide")
    wide_place = lax.axis_index("wide").astype(jnp.int32)
    four_place = (wide_place & 3)[None]

    def narrow_halves(array):
        low, high = array[:, :features], array[:, features:]
        return jnp.where(right_half, high, low), jnp.where(right_half, low, high)

    def after_forward(products):
        whole = whole_low.astype(f32)
        act_grad, select_grad, scan_small = scan_backward(
            selected,
            other_selected,
            step_pre,
            step,
            act,
            projected,
            gated_grad,
            masks,
            decay_log,
            entry,
            passed,
            returning,
            skip_gain[None],
            step_weight,
        )
        normed_four = quarter_of_four(after(normed, select_grad))
        inner_main, before, last, conv_small = convolve_grad(
            select_grad,
            swapped(select_grad, "narrow", 1),
            select_weight,
            act_grad,
            convolved,
            act,
            projected,
            conv_weight,
            masks,
            [],
        )
        following = passed_along(before, "wide", -1)
        inner_grad = patched(segment_ids, inner_main, last, following, *normed_four)
        near = swapped(inner_grad, "wide", 2)
        keep, send = small_halves(wide_place[None] & 1, scan_small, conv_small, inner_grad)
        keep, send = folded((wide_place >> 1 & 1)[None], keep, swapped(send, "wide", 1))
        smalls = [keep, swapped(send, "wide", 2)]
        normed_part = jnp.einsum(
            "cte,dce->td", jnp.stack([inner_grad, gate_grad]), in_weight, preferred_element_type=f32
        )
        gain_part = jnp.sum(normed_part * whole * inverse, axis=0, keepdims=True)
        row_part = jnp.sum(normed_part * norm_gain * whole, axis=1)[None]
        first_bits, *more_bits = group_bits(2)
        gain_sum = gain_part + swapped(gain_part, "narrow", 1)
        for bit in (bit for bits in more_bits for bit in bits):
            gain_sum = gain_sum + swapped(gain_sum, "wide", bit)
        row_theirs = swapped(row_part, "narrow", 1)
        near = after(near, gain_sum, row_theirs, smalls[1])
        far = swapped(jnp.concatenate([inner_grad, near]), "wide", 1)
        keep, *sends = inner_quarter(
            (wide_place >> 2 & 3)[None],
            inner_grad,
            near,
            far,
            normed_four,
            smalls,
            [],
        )
        row_sum = (row_part + row_theirs).reshape(rows, 1)
        out_part = jnp.dot(after(gated, keep), out_weight, preferred_element_type=f32)
        held = keep
        for n, flip in enumerate(flips(first_bits)[1:]):
            held = held + swapped(sends[n], "wide", flip).astype(f32)
        for bits in more_bits:
            held = scattered(held, bits)
        held = held.astype(bf16)
        for bits in reversed(more_bits):
            held = gathered(held, bits)
        spare = jnp.broadcast_to(gain_sum, (block_rows - used_rows, gain_sum.shape[1]))
        held = jnp.concatenate([held[: held.shape[0] - spare.shape[0]], spare.astype(bf16)])
        held = gathered(held, first_bits)
        return held, row_sum, *narrow_halves(normed_part), *narrow_halves(out_part)

    kinds = jax.eval_shape(after_forward, products)
    held, row_sum, normed_mine, normed_other, out_mine, out_other = lax.cond(
        wide_place >= 0,
        after_forward,
        lambda pair: jax.tree.map(lambda kind: jnp.zeros(kind.shape, kind.dtype), kinds),
        products,
    )

    core = swapped(held, "wide", 1)
    begun, out_weight_grad = joined_first(four_place, gate_sum, held, core, out_sum)
    near = swapped(held, "wide", 2)
    far = swapped(near, "wide", 1)
    layer_out = (tokens.astype(f32) + (out_mine + swapped(out_other, "narrow", 1))).astype(bf16)
    gain_mine = jnp.where(right_half, norm_gain[features:], norm_gain[:features])
    normed_grad = normed_mine + swapped(normed_other, "narrow", 1)
    whole_grad = inverse * (gain_mine * normed_grad) - tokens.astype(f32) * (
        inverse * inverse * inverse
    ) * (row_sum / (2 * features))
    tokens_grad = (whole_grad + cotangent.astype(f32)).astype(bf16)
    conv_at = rank + count + 2
    (
        in_weight_grad,
        step_weight_grad,
        decay_log_grad,
        skip_gain_grad,
        step_bias_grad,
        select_weight_grad,
        conv_weight_grad,
        conv_bias_grad,
        norm_gain_grad,
    ) = joined_last(
        four_place,
        gate_sum,
        (held, core, near, far),
        begun,
        (0, rank, rank + count, rank + count + 1, conv_at, conv_at + columns, conv_at + columns + taps),
        (rank, count, 1, 1, columns, taps, 1, 1),
    )
    return (
        layer_out,
        tokens_grad,
        norm_gain_grad[0],
        in_weight_grad,
        conv_weight_grad,
        conv_bias_grad[0],
        select_weight_grad,
        step_weight_grad,
        step_bias_grad[0],
        decay_log_grad,
        skip_gain_grad[0],
        out_weight_grad,
    )


def solution(mesh):
    placed = (
        P("wide", "narrow"),
        P(),
        P(None, None, "narrow"),
        P(None, "narrow"),
        P("narrow"),
        P(None, "narrow"),
        P(None, "narrow"),
        P("narrow"),
        P(None, "narrow"),
        P("narrow"),
        P("narrow", None),
        P("wide"),
        P("wide", "narrow"),
    )
    return jax.shard_map(
        local,
        mesh=mesh,
        in_specs=placed,
        out_specs=(
            P("wide", "narrow"),
            P("wide", "narrow"),
            P(),
            P(None, None, "narrow"),
            P(None, "narrow"),
            P("narrow"),
            P(None, "narrow"),
            P(None, "narrow"),
            P("narrow"),
            P(None, "narrow"),
            P("narrow"),
            P("narrow", None),
        ),
        check_vma=False,
    )
```

```python
import functools

import jax
import jax.numpy as jnp
from jax import lax
from jax.experimental import pallas as pl
from jax.experimental.pallas import tpu as pltpu
from jax.sharding import PartitionSpec as P

epsilon = 1e-05
log2e = 1.4426950408889634
reset_step = 1e30
lanes = 128
halo = 16
body_rows = 32
scan_width = 512
vmem_bytes = 56 * 1024 * 1024
tiny_cost = pl.CostEstimate(flops=1, bytes_accessed=1, transcendentals=0)
f32 = jnp.float32
bf16 = jnp.bfloat16
contract_first = (((0,), (0,)), ((), ()))
contract_last = (((1,), (1,)), ((), ()))


def passed_along(array, axis, by):
    peers = lax.axis_size(axis)
    pairs = [(i, i + by) for i in range(peers) if 0 <= i + by < peers]
    return lax.ppermute(array, axis, pairs)


def swapped(array, axis, bit):
    peers = lax.axis_size(axis)
    return lax.ppermute(array, axis, [(i, i ^ bit) for i in range(peers)])


def wide_bits():
    bit, bits = 1, []
    while bit < lax.axis_size("wide"):
        bits.append(bit)
        bit *= 2
    return bits


def to_next_both(array):
    count, sides = lax.axis_size("wide"), lax.axis_size("narrow")
    pairs = [
        (i * sides + k, (i + 1) * sides + (sides - 1 - k))
        for i in range(count - 1)
        for k in range(sides)
    ]
    return passed_along(array, "wide", 1), lax.ppermute(array, ("wide", "narrow"), pairs)


def is_upper(bit):
    return (lax.axis_index("wide") & bit) != 0


def group_bits(size):
    bits, bit = [], 4
    while bit < lax.axis_size("wide"):
        bits.append(bit)
        bit *= 2
    return [tuple(bits[k : k + size]) for k in range(0, len(bits), size)]


def flips(bits):
    return [sum(b for k, b in enumerate(bits) if n >> k & 1) for n in range(2 ** len(bits))]


def scattered(piece, bits):
    rows = piece.shape[0] // 2 ** len(bits)
    here = sum(is_upper(b).astype(jnp.int32) << k for k, b in enumerate(bits))

    def block(n):
        return lax.dynamic_slice_in_dim(piece, (here ^ n) * rows, rows, 0)

    total = block(0).astype(f32)
    for n, flip in enumerate(flips(bits)):
        if n > 0:
            total = total + swapped(block(n).astype(bf16), "wide", flip).astype(f32)
    return total


def gathered(held, bits):
    blocks = [held] + [swapped(held, "wide", flip) for flip in flips(bits)[1:]]
    for bit in bits:
        upper = is_upper(bit)
        blocks = [
            jnp.concatenate([jnp.where(upper, b, a), jnp.where(upper, a, b)])
            for a, b in zip(blocks[0::2], blocks[1::2])
        ]
    return blocks[0]


def quarter_of_four(array):
    width = array.shape[1] // 4
    here = lax.axis_index("wide") & 3

    def quarter(n):
        return lax.dynamic_slice_in_dim(array, (here ^ n) * width, width, 1)

    return [quarter(0)] + [swapped(quarter(n), "wide", n) for n in (2, 1, 3)]


def silu_slope(values):
    logistic = jax.nn.sigmoid(values)
    return logistic * (1.0 + values * (1.0 - logistic))


def softplus(values):
    return jnp.maximum(values, 0.0) + jnp.log1p(jnp.exp(-jnp.abs(values)))


def column_spec(rows, start=0):
    return pl.BlockSpec((rows, scan_width), lambda j: (0, start + j))


def part_spec(part, rows, start=0):
    return pl.BlockSpec((None, rows, scan_width), lambda j: (part, 0, start + j))


def whole_spec(rows, width):
    return pl.BlockSpec((rows, width), lambda j: (0, 0))


def call(kernel, name, width, in_specs, out_specs, out_shape, scratch, *operands):
    return pl.pallas_call(
        kernel,
        grid=(width // scan_width,),
        in_specs=in_specs,
        out_specs=out_specs,
        out_shape=out_shape,
        scratch_shapes=scratch,
        compiler_params=pltpu.CompilerParams(vmem_limit_bytes=vmem_bytes),
        cost_estimate=tiny_cost,
        name=name,
    )(*operands)


def conv_kernel(
    inner_ref,
    conv_weight_ref,
    conv_bias_ref,
    select_ref,
    mask_ref,
    convolved_ref,
    act_ref,
    selected_ref,
    inner,
):
    rows = act_ref.shape[0]
    taps = conv_weight_ref.shape[0]
    inner[:halo, :] = inner_ref[rows:, :].astype(f32)
    inner[halo:, :] = inner_ref[:rows, :].astype(f32)
    total = conv_bias_ref[...] + conv_weight_ref[taps - 1 :, :] * inner[halo:, :]
    for lag in range(1, taps):
        earlier = inner[pl.ds(halo - lag, rows), :] * mask_ref[:, lag : lag + 1]
        total = total + conv_weight_ref[taps - 1 - lag : taps - lag, :] * earlier
    convolved_ref[...] = total
    act = (total * jax.nn.sigmoid(total)).astype(bf16)
    act_ref[...] = act
    part = lax.dot_general(select_ref[...], act, contract_last, preferred_element_type=f32)

    @pl.when(pl.program_id(0) == 0)
    def _():
        selected_ref[...] = part

    @pl.when(pl.program_id(0) > 0)
    def _():
        selected_ref[...] += part


def convolve(projected, conv_weight, conv_bias, select_weight, masks):
    parts, extended, width = projected.shape
    rows = extended - halo
    taps = conv_weight.shape[0]
    columns = select_weight.shape[0]
    return call(
        conv_kernel,
        "convolve",
        width,
        [
            part_spec(0, extended),
            column_spec(taps),
            column_spec(1),
            column_spec(columns),
            whole_spec(rows, masks.shape[1]),
        ],
        [column_spec(rows), column_spec(rows), whole_spec(columns, rows)],
        [
            jax.ShapeDtypeStruct((rows, width), f32),
            jax.ShapeDtypeStruct((rows, width), bf16),
            jax.ShapeDtypeStruct((columns, rows), f32),
        ],
        [pltpu.VMEM((extended, scan_width), f32)],
        projected,
        conv_weight,
        conv_bias,
        select_weight,
        masks,
    )


def coef_columns(coef, block):
    per_tile = lanes // body_rows
    start = pl.multiple_of((block // per_tile) * lanes, lanes)
    tile = coef[:, pl.ds(start, lanes)]
    back = body_rows * lax.rem(block, per_tile)
    return pltpu.roll(tile, lax.rem(lanes - back, lanes), 1)


def put_ends(ends_ref, state, adjoint, total):
    count, width = state.shape
    ends_ref[:count, :] = state.astype(bf16)
    ends_ref[count : 2 * count, :] = adjoint.astype(bf16)
    high = total.astype(bf16).astype(f32)
    upper = lax.broadcasted_iota(jnp.int32, (16, width), 0) < 8
    ends_ref[2 * count :, :] = jnp.where(upper, high, total - high).astype(bf16)


def get_ends(ends_ref, count):
    total = ends_ref[2 * count :].astype(f32)
    return (
        ends_ref[:count].astype(f32),
        ends_ref[count : 2 * count].astype(f32),
        total[:1] + total[8:9],
    )


def ends_kernel(
    selected_ref,
    other_ref,
    step_weight_ref,
    step_bias_ref,
    act_ref,
    gate_ref,
    gated_grad_ref,
    mask_ref,
    decay_log_ref,
    step_pre_ref,
    step_ref,
    ends_ref,
    coef,
    held_step,
    drive,
    scan_grad,
):
    rows = act_ref.shape[0]
    count = decay_log_ref.shape[0]
    rank = step_weight_ref.shape[0]
    decay2 = -jnp.exp(decay_log_ref[...]) * log2e
    selected = selected_ref[...] + other_ref[...]
    coef[...] = selected[rank:, :]
    step_low = selected[:rank, :].astype(bf16)
    step_pre = step_bias_ref[...] + lax.dot_general(
        step_low, step_weight_ref[...], contract_first, preferred_element_type=f32
    )
    step_pre_ref[...] = step_pre
    step = softplus(step_pre)
    step_ref[...] = step
    held_step[...] = jnp.where(mask_ref[:, 1:2] > 0.0, step, reset_step)
    drive[...] = step * act_ref[...].astype(f32)
    gate = gate_ref[...].astype(f32)
    scan_grad[...] = gated_grad_ref[...] * (gate * jax.nn.sigmoid(gate))
    zero = jnp.zeros(decay2.shape, f32)

    def body(block, carried):
        state, product, adjoint = carried
        columns = coef_columns(coef, block)
        for i in range(body_rows):
            row = pl.ds(block * body_rows + i, 1)
            factor = jnp.exp2(held_step[row, :] * decay2)
            state = factor * state + columns[:count, i : i + 1] * drive[row, :]
            product = factor * product
            adjoint = adjoint + product * (columns[count:, i : i + 1] * scan_grad[row, :])
        return state, product, adjoint

    state, product, adjoint = lax.fori_loop(0, rows // body_rows, body, (zero, zero + 1.0, zero))
    put_ends(ends_ref, state, adjoint, jnp.sum(held_step[...], axis=0, keepdims=True))


def scan_ends(
    selected, other, step_weight, step_bias, act, projected, gated_grad, masks, decay_log
):
    rows, width = act.shape
    count = decay_log.shape[0]
    columns = selected.shape[0]
    rank = step_weight.shape[0]
    return call(
        ends_kernel,
        "scan_ends",
        width,
        [
            whole_spec(columns, rows),
            whole_spec(columns, rows),
            column_spec(rank),
            column_spec(1),
            column_spec(rows),
            part_spec(1, rows),
            column_spec(rows),
            whole_spec(rows, masks.shape[1]),
            column_spec(count),
        ],
        [column_spec(rows), column_spec(rows), column_spec(2 * count + 16)],
        [
            jax.ShapeDtypeStruct((rows, width), f32),
            jax.ShapeDtypeStruct((rows, width), f32),
            jax.ShapeDtypeStruct((2 * count + 16, width), bf16),
        ],
        [pltpu.VMEM((2 * count, rows), f32)] + [pltpu.VMEM((rows, scan_width), f32)] * 3,
        selected,
        other,
        step_weight,
        step_bias,
        act,
        projected,
        gated_grad,
        masks,
        decay_log,
    )


def lane_tiles(values):
    return [values[:, k : k + lanes] for k in range(0, values.shape[1], lanes)]


def tree_sum(parts):
    while len(parts) > 1:
        odd = parts[len(parts) // 2 * 2 :]
        parts = [a + b for a, b in zip(parts[0::2], parts[1::2])] + odd
    return parts[0]


def keep_halves(scratch, i, values):
    for k, tile in enumerate(lane_tiles(values)):
        at = (k * body_rows + i) * 8
        scratch[at : at + 8, :] = tile[:8] + tile[8:]


def put_state_sums(scratch, out_ref, block):
    for group in range(body_rows // 8):
        row = pl.ds(pl.multiple_of(block * body_rows + group * 8, 8), 8)
        for k in range(out_ref.shape[1] // lanes):
            at = (k * body_rows + group * 8) * 8
            total = tree_sum([scratch[pl.ds(at + n, 8, stride=8), :] for n in range(8)])
            out_ref[row, k * lanes : (k + 1) * lanes] = total


def lane_sums(values):
    ones = jnp.ones((8, lanes), bf16)
    high = values.astype(bf16)
    low = (values - high.astype(f32)).astype(bf16)
    total = lax.dot_general(ones, high, contract_last, preferred_element_type=f32)
    total += lax.dot_general(ones, low, contract_last, preferred_element_type=f32)
    return total[:1, :]


def at_token(t, count):
    return pl.ds(pl.multiple_of(t * count, count), count)


def forward_kernel(
    selected_ref,
    other_ref,
    step_ref,
    act_ref,
    gate_ref,
    gated_grad_ref,
    mask_ref,
    decay_log_ref,
    passed_ref,
    entering_ref,
    skip_ref,
    gated_ref,
    gate_grad_ref,
    entry_ref,
    coef,
    held_step,
    drive,
    scanned,
    halves,
):
    rows = step_ref.shape[0]
    count = decay_log_ref.shape[0]
    rank = selected_ref.shape[0] - 2 * count
    decay = -jnp.exp(decay_log_ref[...])
    decay2 = decay * log2e
    before_steps = passed_ref[2 * count : 2 * count + 1, :]
    entry = passed_ref[:count, :] + through(decay, before_steps) * entering_ref[...].astype(f32)
    entry_ref[...] = entry
    coef[...] = selected_ref[rank:, :] + other_ref[rank:, :]
    act = act_ref[...].astype(f32)
    held_step[...] = jnp.where(mask_ref[:, 1:2] > 0.0, step_ref[...], reset_step)
    drive[...] = step_ref[...] * act

    def forward(block, state):
        columns = coef_columns(coef, block)
        for i in range(body_rows):
            row = pl.ds(block * body_rows + i, 1)
            factor = jnp.exp2(held_step[row, :] * decay2)
            state = factor * state + columns[:count, i : i + 1] * drive[row, :]
            keep_halves(halves, i, columns[count:, i : i + 1] * state)
        put_state_sums(halves, scanned, block)
        return state

    lax.fori_loop(0, rows // body_rows, forward, entry)
    gate = gate_ref[...].astype(f32)
    logistic = jax.nn.sigmoid(gate)
    total = scanned[...] + skip_ref[...] * act
    gated_ref[...] = (total * (gate * logistic)).astype(bf16)
    slope = logistic * (1.0 + gate * (1.0 - logistic))
    gate_grad_ref[...] = (gated_grad_ref[...] * total * slope).astype(bf16)


def scan_forward(
    selected, other, step, act, projected, gated_grad, masks, decay_log, passed, entering, skip_gain
):
    rows, width = step.shape
    count = decay_log.shape[0]
    columns = selected.shape[0]
    return call(
        forward_kernel,
        "scan_forward",
        width,
        [
            whole_spec(columns, rows),
            whole_spec(columns, rows),
            column_spec(rows),
            column_spec(rows),
            part_spec(1, rows),
            column_spec(rows),
            whole_spec(rows, masks.shape[1]),
            column_spec(count),
            column_spec(2 * count + 8),
            column_spec(count),
            column_spec(1),
        ],
        [column_spec(rows), column_spec(rows), column_spec(count)],
        [
            jax.ShapeDtypeStruct((rows, width), bf16),
            jax.ShapeDtypeStruct((rows, width), bf16),
            jax.ShapeDtypeStruct((count, width), f32),
        ],
        [pltpu.VMEM((2 * count, rows), f32)]
        + [pltpu.VMEM((rows, scan_width), f32)] * 3
        + [pltpu.VMEM((8 * body_rows * (scan_width // lanes), lanes), f32)],
        selected,
        other,
        step,
        act,
        projected,
        gated_grad,
        masks,
        decay_log,
        passed,
        entering,
        skip_gain,
    )


def backward_kernel(
    selected_ref,
    other_ref,
    step_pre_ref,
    step_ref,
    act_ref,
    gate_ref,
    gated_grad_ref,
    mask_ref,
    decay_log_ref,
    entry_ref,
    passed_ref,
    returning_ref,
    skip_ref,
    step_weight_ref,
    act_grad_ref,
    select_grad_ref,
    small_ref,
    coef,
    held_step,
    drive,
    scan_grad,
    weighted,
    held_sum,
    states,
    factors,
    halves,
    more_halves,
    in_sum,
    read_sum,
):
    rows = step_ref.shape[0]
    count = decay_log_ref.shape[0]
    rank = step_weight_ref.shape[0]
    blocks = rows // body_rows
    decay = -jnp.exp(decay_log_ref[...])
    decay2 = decay * log2e
    after_steps = passed_ref[2 * count + 1 : 2 * count + 2, :]
    tail = passed_ref[count : 2 * count, :] + through(decay, after_steps) * returning_ref[...].astype(f32)
    selected = selected_ref[...] + other_ref[...]
    coef[...] = selected[rank:, :]
    step_low = selected[:rank, :].astype(bf16)
    step = step_ref[...]
    act = act_ref[...].astype(f32)
    held_step[...] = jnp.where(mask_ref[:, 1:2] > 0.0, step, reset_step)
    drive[...] = step * act
    gate = gate_ref[...].astype(f32)
    grads = gated_grad_ref[...] * (gate * jax.nn.sigmoid(gate))
    scan_grad[...] = grads
    small_ref[rank + count : rank + count + 1, :] = jnp.sum(grads * act, axis=0, keepdims=True)
    states[:count, :] = entry_ref[...]

    @pl.when(pl.program_id(0) == 0)
    def _():
        in_sum[...] = jnp.zeros(in_sum.shape, f32)
        read_sum[...] = jnp.zeros(read_sum.shape, f32)
        select_grad_ref[...] = jnp.zeros(select_grad_ref.shape, f32)

    def forward(block, state):
        columns = coef_columns(coef, block)
        for i in range(body_rows):
            t = block * body_rows + i
            row = pl.ds(t, 1)
            factor = jnp.exp2(held_step[row, :] * decay2)
            state = factor * state + columns[:count, i : i + 1] * drive[row, :]
            factors[at_token(t, count), :] = factor
            states[at_token(t + 1, count), :] = state
        return state

    lax.fori_loop(0, blocks, forward, entry_ref[...])

    def backward(k, carried):
        adjoint, decay_grad = carried
        block = blocks - 1 - k
        columns = coef_columns(coef, block)
        for i in range(body_rows - 1, -1, -1):
            t = block * body_rows + i
            row = pl.ds(t, 1)
            here = at_token(t, count)
            grad = scan_grad[row, :]
            summed = columns[count:, i : i + 1] * grad + adjoint
            read_sum[here, :] += tree_sum(lane_tiles(grad * states[at_token(t + 1, count), :]))
            in_sum[here, :] += tree_sum(lane_tiles(summed * drive[row, :]))
            keep_halves(halves, i, summed * columns[:count, i : i + 1])
            adjoint = factors[here, :] * summed
            held = adjoint * states[here, :]
            decay_grad = decay_grad + held * step_ref[row, :]
            keep_halves(more_halves, i, held * decay)
        put_state_sums(halves, weighted, block)
        put_state_sums(more_halves, held_sum, block)
        return adjoint, decay_grad

    ignored, decay_grad = lax.fori_loop(
        0, blocks, backward, (tail, jnp.zeros(decay.shape, f32))
    )
    act_grad_ref[...] = step * weighted[...] + skip_ref[...] * scan_grad[...]
    step_grad = act * weighted[...] + held_sum[...]
    pre_grad = (step_grad * jax.nn.sigmoid(step_pre_ref[...])).astype(bf16)
    small_ref[:rank, :] = jnp.dot(step_low, pre_grad, preferred_element_type=f32)
    small_ref[rank : rank + count, :] = decay_grad * decay
    bias_grad = jnp.sum(pre_grad.astype(f32), axis=0, keepdims=True)
    small_ref[rank + count + 1 : rank + count + 2, :] = bias_grad
    select_grad_ref[:rank, :] += lax.dot_general(
        step_weight_ref[...], pre_grad, contract_last, preferred_element_type=f32
    )

    @pl.when(pl.program_id(0) == pl.num_programs(0) - 1)
    def _():
        for n in range(count):
            at = pl.ds(n, rows, stride=count)
            select_grad_ref[rank + n : rank + n + 1, :] = lane_sums(in_sum[at, :])
            select_grad_ref[rank + count + n : rank + count + n + 1, :] = lane_sums(read_sum[at, :])


def scan_backward(
    selected,
    other,
    step_pre,
    step,
    act,
    projected,
    gated_grad,
    masks,
    decay_log,
    entry,
    passed,
    returning,
    skip_gain,
    step_weight,
):
    rows, width = step.shape
    count = decay_log.shape[0]
    columns = selected.shape[0]
    rank = step_weight.shape[0]
    half_rows = 8 * body_rows * (scan_width // lanes)
    small = rank + count + 2
    return call(
        backward_kernel,
        "scan_backward",
        width,
        [
            whole_spec(columns, rows),
            whole_spec(columns, rows),
            column_spec(rows),
            column_spec(rows),
            column_spec(rows),
            part_spec(1, rows),
            column_spec(rows),
            whole_spec(rows, masks.shape[1]),
            column_spec(count),
            column_spec(count),
            column_spec(2 * count + 8),
            column_spec(count),
            column_spec(1),
            column_spec(rank),
        ],
        [column_spec(rows), whole_spec(columns, rows), column_spec(small)],
        [
            jax.ShapeDtypeStruct((rows, width), f32),
            jax.ShapeDtypeStruct((columns, rows), f32),
            jax.ShapeDtypeStruct((small, width), f32),
        ],
        [pltpu.VMEM((2 * count, rows), f32)]
        + [pltpu.VMEM((rows, scan_width), f32)] * 5
        + [
            pltpu.VMEM(((rows + 1) * count, scan_width), f32),
            pltpu.VMEM((rows * count, scan_width), f32),
            pltpu.VMEM((half_rows, lanes), f32),
            pltpu.VMEM((half_rows, lanes), f32),
            pltpu.VMEM((rows * count, lanes), f32),
            pltpu.VMEM((rows * count, lanes), f32),
        ],
        selected,
        other,
        step_pre,
        step,
        act,
        projected,
        gated_grad,
        masks,
        decay_log,
        entry,
        passed,
        returning,
        skip_gain,
        step_weight,
    )


def conv_grad_kernel(
    select_grad_ref,
    other_ref,
    select_ref,
    act_grad_ref,
    convolved_ref,
    act_ref,
    inner_ref,
    conv_weight_ref,
    mask_ref,
    *rest,
):
    inner_grad_ref, before_ref, last_ref, small_ref, inner, shifted = rest[-6:]
    rows = act_ref.shape[0]
    taps = conv_weight_ref.shape[0]
    columns = select_ref.shape[0]
    select_grad = (select_grad_ref[...] + other_ref[...]).astype(bf16)
    total = act_grad_ref[...] + lax.dot_general(
        select_grad, select_ref[...], contract_first, preferred_element_type=f32
    )
    conv_grad = total * silu_slope(convolved_ref[...])
    small_ref[:columns, :] = jnp.dot(select_grad, act_ref[...], preferred_element_type=f32)
    inner[:halo, :] = inner_ref[rows:, :].astype(f32)
    inner[halo:, :] = inner_ref[:rows, :].astype(f32)
    edges = jnp.zeros((8, conv_grad.shape[1]), f32)
    shifted[:8, :] = edges
    shifted[rows + 8 :, :] = edges
    out = conv_weight_ref[taps - 1 :, :] * conv_grad
    before = edges
    small_ref[columns + taps - 1 : columns + taps, :] = jnp.sum(
        conv_grad * inner[halo:, :], axis=0, keepdims=True
    )
    for lag in range(1, taps):
        masked = conv_grad * mask_ref[:, lag : lag + 1]
        at = taps - 1 - lag
        small_ref[columns + at : columns + at + 1, :] = jnp.sum(
            masked * inner[pl.ds(halo - lag, rows), :], axis=0, keepdims=True
        )
        shifted[8 : rows + 8, :] = masked
        weight = conv_weight_ref[at : at + 1, :]
        out = out + weight * shifted[pl.ds(8 + lag, rows), :]
        before = before + weight * shifted[pl.ds(lag, 8), :]
    small_ref[columns + taps : columns + taps + 1, :] = jnp.sum(conv_grad, axis=0, keepdims=True)
    inner_grad_ref[...] = out.astype(bf16)
    before_ref[...] = before
    last_ref[...] = out[rows - 8 :, :]


def convolve_grad(
    select_grad, other, select_weight, act_grad, convolved, act, projected, conv_weight, masks, waits
):
    rows, width = act.shape
    extended = rows + halo
    columns = select_weight.shape[0]
    taps = conv_weight.shape[0]
    small = columns + taps + 1
    return call(
        conv_grad_kernel,
        "convolve_grad",
        width,
        [
            whole_spec(columns, rows),
            whole_spec(columns, rows),
            column_spec(columns),
            column_spec(rows),
            column_spec(rows),
            column_spec(rows),
            part_spec(0, extended),
            column_spec(taps),
            whole_spec(rows, masks.shape[1]),
        ]
        + [pl.BlockSpec(memory_space=pl.ANY)] * len(waits),
        [column_spec(rows), column_spec(8), column_spec(8), column_spec(small)],
        [
            jax.ShapeDtypeStruct((rows, width), bf16),
            jax.ShapeDtypeStruct((8, width), f32),
            jax.ShapeDtypeStruct((8, width), f32),
            jax.ShapeDtypeStruct((small, width), f32),
        ],
        [pltpu.VMEM((extended, scan_width), f32), pltpu.VMEM((rows + 16, scan_width), f32)],
        select_grad,
        other,
        select_weight,
        act_grad,
        convolved,
        act,
        projected,
        conv_weight,
        masks,
        *waits,
    )


def normalize_kernel(
    own_ref,
    other_ref,
    edge_ref,
    other_edge_ref,
    gain_ref,
    ids_ref,
    whole_ref,
    extended_ref,
    normed_ref,
    inverse_ref,
    mask_ref,
    rows_ref,
):
    rows, half = own_ref.shape
    ids = ids_ref[...].astype(f32)
    place = lax.broadcasted_iota(jnp.int32, ids.shape, 1)
    same = []
    for lag in range(8):
        earlier = jnp.where(place < lag, ids[:, :1], pltpu.roll(ids, lag, 1)) if lag else ids
        same.append(jnp.where(earlier == ids, 1.0, 0.0))
    spare = jnp.zeros((lanes - 8, rows), f32)
    mask_ref[...] = jnp.concatenate(same + [spare]).T
    right = lax.axis_index("narrow") == 1
    for at, own, other in ((0, own_ref, other_ref), (rows, edge_ref, other_edge_ref)):
        end = at + own.shape[0]
        rows_ref[at:end, :half] = jnp.where(right, other[...], own[...])
        rows_ref[at:end, half:] = jnp.where(right, own[...], other[...])
    whole_ref[...] = rows_ref[:rows, :]
    whole = rows_ref[...].astype(f32)
    inverse = lax.rsqrt(jnp.mean(whole * whole, axis=1, keepdims=True) + epsilon)
    normed = (whole * inverse * gain_ref[...]).astype(bf16)
    extended_ref[...] = normed
    normed_ref[...] = normed[:rows]
    inverse_ref[...] = inverse[:rows]


def normalized(own, other, edge, other_edge, gain, ids):
    rows, half = own.shape
    extended = rows + edge.shape[0]
    return pl.pallas_call(
        normalize_kernel,
        out_shape=[
            jax.ShapeDtypeStruct((rows, 2 * half), bf16),
            jax.ShapeDtypeStruct((extended, 2 * half), bf16),
            jax.ShapeDtypeStruct((rows, 2 * half), bf16),
            jax.ShapeDtypeStruct((rows, 1), f32),
            jax.ShapeDtypeStruct((rows, lanes), f32),
        ],
        scratch_shapes=[pltpu.VMEM((extended, 2 * half), bf16)],
        cost_estimate=tiny_cost,
        name="normalized",
    )(own, other, edge, other_edge, gain, ids)


def after(array, *waits):
    anywhere = pl.BlockSpec(memory_space=pl.ANY)
    return pl.pallas_call(
        lambda *refs: None,
        in_specs=[anywhere] * (1 + len(waits)),
        out_specs=anywhere,
        out_shape=jax.ShapeDtypeStruct(array.shape, array.dtype),
        input_output_aliases={0: 0},
        cost_estimate=tiny_cost,
        name="after",
    )(array, *waits)


def patch_kernel(ids_ref, rows_ref, last_ref, next_ref, *rest):
    count = ids_ref.shape[0]
    place = lax.broadcasted_iota(jnp.int32, (8, 1), 0)
    same = jnp.zeros((8, 1), f32)
    for lag in range(8):
        here = jnp.where(ids_ref[count - 1 - lag] == ids_ref[count - 1], 1.0, 0.0)
        same = same + jnp.where(place == 7 - lag, here, 0.0)
    total = last_ref[...] + next_ref[...] * same
    rows = rows_ref[...].astype(f32)
    rest[-1][...] = jnp.concatenate([rows[: halo - 8], total]).astype(bf16)


def patched(ids, grads, last, following, *waits):
    rows, width = grads.shape
    block = pl.BlockSpec((halo, width), lambda j: (rows // halo - 1, 0))
    edge = pl.BlockSpec((8, width), lambda j: (0, 0))
    return pl.pallas_call(
        patch_kernel,
        grid=(1,),
        in_specs=[pl.BlockSpec(memory_space=pltpu.SMEM), block, edge, edge]
        + [pl.BlockSpec(memory_space=pl.ANY)] * len(waits),
        out_specs=block,
        out_shape=jax.ShapeDtypeStruct((rows, width), bf16),
        input_output_aliases={1: 0},
        cost_estimate=tiny_cost,
        name="patched",
    )(ids, grads, last, following, *waits)


def edge_kernel(ids_ref, tokens_ref, out_ref):
    rows = ids_ref.shape[0]
    taps = 4
    out_ref[...] = tokens_ref[...]
    place = lax.broadcasted_iota(jnp.int32, (halo, 1), 0)
    same = jnp.zeros((halo, 1), f32)
    for lag in range(taps):
        here = jnp.where(ids_ref[rows - 1 - lag] == ids_ref[rows - 1], 1.0, 0.0)
        same = same + jnp.where(place == halo - 1 - lag, here, 0.0)
    out_ref[...] = (tokens_ref[...].astype(f32) * same).astype(bf16)


def edge_rows_of(ids, tokens):
    rows, width = tokens.shape
    return pl.pallas_call(
        edge_kernel,
        grid=(1,),
        in_specs=[
            pl.BlockSpec(memory_space=pltpu.SMEM),
            pl.BlockSpec((halo, width), lambda j: (rows // halo - 1, 0)),
        ],
        out_specs=pl.BlockSpec((halo, width), lambda j: (0, 0)),
        out_shape=jax.ShapeDtypeStruct((halo, width), bf16),
        cost_estimate=tiny_cost,
        name="edge_rows",
    )(ids, tokens)


block_rows, used_rows = 16, 12


def small_kernel(core_ref, scan_ref, conv_ref, wait_ref, keep_ref, send_ref, rows, blocks):
    rows[...] = jnp.zeros(rows.shape, f32)
    rows[: scan_ref.shape[0], :] = scan_ref[...]
    rows[scan_ref.shape[0] : scan_ref.shape[0] + conv_ref.shape[0], :] = conv_ref[...]
    blocks[...] = jnp.zeros(blocks.shape, f32)
    for n in range(16):
        blocks[n * block_rows : n * block_rows + used_rows, :] = rows[
            n * used_rows : (n + 1) * used_rows, :
        ]
    half = keep_ref.shape[0]
    mine = pl.ds(pl.multiple_of(core_ref[0] * half, half), half)
    other = pl.ds(pl.multiple_of((1 - core_ref[0]) * half, half), half)
    keep_ref[...] = blocks[mine, :]
    send_ref[...] = blocks[other, :].astype(bf16)


def small_halves(core, scan_small, conv_small, wait):
    width = scan_small.shape[1]
    return pl.pallas_call(
        small_kernel,
        in_specs=[pl.BlockSpec(memory_space=pltpu.SMEM)]
        + [pl.BlockSpec(memory_space=pltpu.VMEM)] * 2
        + [pl.BlockSpec(memory_space=pl.ANY)],
        out_shape=[jax.ShapeDtypeStruct((8 * block_rows, width), kind) for kind in (f32, bf16)],
        scratch_shapes=[
            pltpu.VMEM((16 * used_rows, width), f32),
            pltpu.VMEM((16 * block_rows, width), f32),
        ],
        cost_estimate=tiny_cost,
        name="small_halves",
    )(core, scan_small, conv_small, wait)


def fold_kernel(upper_ref, keep_ref, arrived_ref, out_ref, send_ref):
    size = out_ref.shape[0]
    mine = pl.ds(pl.multiple_of(upper_ref[0] * size, size), size)
    other = pl.ds(pl.multiple_of((1 - upper_ref[0]) * size, size), size)
    out_ref[...] = keep_ref[mine, :] + arrived_ref[mine, :].astype(f32)
    send_ref[...] = (keep_ref[other, :] + arrived_ref[other, :].astype(f32)).astype(bf16)


def folded(upper, keep, arrived):
    rows, width = keep.shape
    return pl.pallas_call(
        fold_kernel,
        in_specs=[pl.BlockSpec(memory_space=pltpu.SMEM)]
        + [pl.BlockSpec(memory_space=pltpu.VMEM)] * 2,
        out_shape=[jax.ShapeDtypeStruct((rows // 2, width), kind) for kind in (f32, bf16)],
        cost_estimate=tiny_cost,
        name="folded",
    )(upper, keep, arrived)


def quarter_kernel(
    place_ref,
    own_ref,
    near_ref,
    far_ref,
    normed_0,
    normed_1,
    normed_2,
    normed_3,
    small_ref,
    arrived_ref,
    *rest,
):
    keep_ref, *sends_refs, piece, small = rest[-6:]
    total = None
    tokens = own_ref.shape[0]
    grads = (own_ref[...], near_ref[...], far_ref[:tokens, :], far_ref[tokens:, :])
    for left, right in zip((normed_0, normed_1, normed_2, normed_3), grads):
        part = lax.dot_general(left[...], right, contract_first, preferred_element_type=f32)
        total = part if total is None else total + part
    piece[...] = total
    small[...] = small_ref[...] + arrived_ref[...].astype(f32)
    rows, spare = piece.shape[0] // 4, small.shape[0] // 4
    for n in range(4):
        block = place_ref[0] ^ n
        inner_rows = piece[pl.ds(pl.multiple_of(block * rows, rows), rows), :]
        small_rows = small[pl.ds(pl.multiple_of(block * spare, spare), spare), :]
        if n == 0:
            keep_ref[:rows, :] = inner_rows
            keep_ref[rows:, :] = small_rows
        else:
            sends_refs[n - 1][:rows, :] = inner_rows.astype(bf16)
            sends_refs[n - 1][rows:, :] = small_rows.astype(bf16)


def inner_quarter(place, own, near, far, normed, smalls, waits):
    width = own.shape[1]
    quarter = normed[0].shape[1]
    spare = smalls[0].shape[0]
    rows = (quarter + spare) // 4
    return pl.pallas_call(
        quarter_kernel,
        in_specs=[pl.BlockSpec(memory_space=pltpu.SMEM)]
        + [pl.BlockSpec(memory_space=pltpu.VMEM)] * 9
        + [pl.BlockSpec(memory_space=pl.ANY)] * len(waits),
        out_shape=[jax.ShapeDtypeStruct((rows, width), f32)]
        + [jax.ShapeDtypeStruct((rows, width), bf16)] * 3,
        scratch_shapes=[pltpu.VMEM((quarter, width), f32), pltpu.VMEM((spare, width), f32)],
        compiler_params=pltpu.CompilerParams(vmem_limit_bytes=vmem_bytes),
        cost_estimate=tiny_cost,
        name="inner_quarter",
    )(place, own, near, far, *normed, *smalls, *waits)


def put_quarter(out_ref, gate_ref, inner_ref):
    rows = out_ref.shape[0] // 4
    out_ref[:, 1, :] = gate_ref[...].astype(f32)
    for n in range(4):
        at = n * (rows + block_rows)
        out_ref[n * rows : (n + 1) * rows, 0, :] = inner_ref[at : at + rows, :].astype(f32)


def first_join_kernel(place_ref, gate_ref, first_ref, second_ref, low_ref, out_ref, wide_ref):
    wide_ref[...] = low_ref[...].astype(f32)

    @pl.when(pl.program_id(0) == 0)
    def _():
        put_quarter(out_ref, gate_ref, first_ref)

    @pl.when(pl.program_id(0) == 1)
    def _():
        put_quarter(out_ref, gate_ref, second_ref)


def last_join_kernel(place_ref, gate_ref, first_ref, second_ref, *rest, small_rows):
    held = rest[:4]
    out_ref, *row_refs, gain_ref, blocks = rest[5:]

    @pl.when(pl.program_id(0) == 0)
    def _():
        put_quarter(out_ref, gate_ref, first_ref)

    @pl.when(pl.program_id(0) == 1)
    def _():
        put_quarter(out_ref, gate_ref, second_ref)
        rows = out_ref.shape[0] // 4
        for flip, ref in enumerate(held):
            number = place_ref[0] ^ flip
            number = (number & 1) * 2 + number // 2
            for n in range(4):
                at = (number * 4 + n) * block_rows
                taken = ref[(n + 1) * rows + n * block_rows : (n + 1) * (rows + block_rows), :]
                blocks[pl.ds(pl.multiple_of(at, block_rows), block_rows), :] = taken.astype(f32)
        for ref, start in zip(row_refs, small_rows):
            for row in range(ref.shape[0]):
                at = (start + row) // used_rows * block_rows + (start + row) % used_rows
                ref[row : row + 1, :] = blocks[at : at + 1, :]
        gain_ref[...] = sum(
            blocks[n * block_rows + used_rows : n * block_rows + used_rows + 1, :] for n in range(16)
        )


def joined(kernel, place, flip, gate, first, second, specs, operands, out_specs, out_shape, scratch, aliases):
    depth, width = gate.shape
    quarter = depth // 4

    def target(j, place):
        return place[0] ^ (flip + j)

    whole = pl.BlockSpec(first.shape, lambda j, place: (0, 0))
    return pl.pallas_call(
        kernel,
        grid_spec=pltpu.PrefetchScalarGridSpec(
            num_scalar_prefetch=1,
            grid=(2,),
            in_specs=[
                pl.BlockSpec((quarter, width), lambda j, place: (target(j, place), 0)),
                whole,
                whole,
            ]
            + specs,
            out_specs=[
                pl.BlockSpec((quarter, 2, width), lambda j, place: (target(j, place), 0, 0))
            ]
            + out_specs,
            scratch_shapes=scratch,
        ),
        out_shape=[jax.ShapeDtypeStruct((depth, 2, width), f32)] + out_shape,
        input_output_aliases=aliases,
        compiler_params=pltpu.CompilerParams(vmem_limit_bytes=vmem_bytes),
        cost_estimate=tiny_cost,
        name="joined",
    )(place, gate, first, second, *operands)


def joined_first(place, gate, first, second, low):
    rows, width = low.shape
    half = pl.BlockSpec((rows // 2, width), lambda j, place: (j, 0))
    kind = jax.ShapeDtypeStruct((rows, width), f32)
    return joined(
        first_join_kernel, place, 0, gate, first, second, [half], [low], [half], [kind], [], {}
    )


def joined_last(place, gate, held, begun, small_rows, small_counts):
    width = gate.shape[1]
    whole = pl.BlockSpec(held[0].shape, lambda j, place: (0, 0))
    return joined(
        functools.partial(last_join_kernel, small_rows=small_rows),
        place,
        2,
        gate,
        held[2],
        held[3],
        [whole] * 4 + [pl.BlockSpec(memory_space=pl.ANY)],
        [*held, begun],
        [pl.BlockSpec((rows, width), lambda j, place: (0, 0)) for rows in small_counts],
        [jax.ShapeDtypeStruct((rows, width), f32) for rows in small_counts],
        [pltpu.VMEM((16 * block_rows, width), f32)],
        {8: 0},
    )


def through(decay, total):
    return jnp.exp(decay * total)


def round_kernel(second_ref, decay_log_ref, own_ref, other_ref, *rest, first):
    count, width = decay_log_ref.shape
    new_passed_ref, *ends_refs = rest if first else rest[1:]
    decay = -jnp.exp(decay_log_ref[...])
    second = second_ref[0] > 0
    own, other = get_ends(own_ref, count), get_ends(other_ref, count)
    early = [jnp.where(second, b, a) for a, b in zip(own, other)]
    late = [jnp.where(second, a, b) for a, b in zip(own, other)]
    state = late[0] + through(decay, late[2]) * early[0]
    adjoint = early[1] + through(decay, early[2]) * late[1]
    if len(ends_refs) == 2:
        ends_refs[0][...] = state.astype(bf16)
        ends_refs[1][...] = adjoint.astype(bf16)
    else:
        put_ends(ends_refs[0], state, adjoint, early[2] + late[2])
    if first:
        before = after = jnp.zeros((count, width), f32)
        before_steps = after_steps = jnp.zeros((1, width), f32)
    else:
        before, after = rest[0][:count], rest[0][count : 2 * count]
        before_steps = rest[0][2 * count : 2 * count + 1]
        after_steps = rest[0][2 * count + 1 : 2 * count + 2]
    new_passed_ref[:count, :] = before + jnp.where(second, through(decay, before_steps) * other[0], 0.0)
    new_passed_ref[count : 2 * count, :] = after + jnp.where(
        second, 0.0, through(decay, after_steps) * other[1]
    )
    new_passed_ref[2 * count : 2 * count + 1, :] = before_steps + jnp.where(second, other[2], 0.0)
    new_passed_ref[2 * count + 1 : 2 * count + 2, :] = after_steps + jnp.where(second, 0.0, other[2])


def carried(ends, decay_log):
    count, width = decay_log.shape
    place = lax.axis_index("wide").astype(jnp.int32)
    state = jax.ShapeDtypeStruct((count, width), bf16)
    passed_kind = jax.ShapeDtypeStruct((2 * count + 8, width), f32)
    packed, passed = ends, []
    vmem = pl.BlockSpec(memory_space=pltpu.VMEM)
    for k, kinds in enumerate(([jax.ShapeDtypeStruct(ends.shape, bf16)], [state, state])):
        new_passed, *out = pl.pallas_call(
            functools.partial(round_kernel, first=k == 0),
            in_specs=[pl.BlockSpec(memory_space=pltpu.SMEM)] + [vmem] * (3 + k),
            out_shape=[passed_kind] + kinds,
            cost_estimate=tiny_cost,
            name="carry_round",
        )((place >> k & 1)[None], decay_log, packed, swapped(packed, "wide", 2**k), *passed)
        packed, passed = out[0], [new_passed]
    from_before = passed_along(out[0], "wide", 4)
    from_after = passed_along(out[1], "wide", -4)
    return passed[0], from_before, from_after


def local(
    tokens,
    norm_gain,
    in_weight,
    conv_weight,
    conv_bias,
    select_weight,
    step_weight,
    step_bias,
    decay_log,
    skip_gain,
    out_weight,
    segment_ids,
    cotangent,
):
    rows, features = tokens.shape
    taps = conv_weight.shape[0]
    columns = select_weight.shape[0]
    rank = step_weight.shape[0]
    count = decay_log.shape[0]
    right_half = lax.axis_index("narrow") == 1

    def both_halves(own, other):
        return jnp.concatenate(
            [jnp.where(right_half, other, own), jnp.where(right_half, own, other)], axis=1
        )

    other_tokens = swapped(tokens, "narrow", 1)
    other_cot = swapped(cotangent, "narrow", 1)
    edge, other_edge = to_next_both(edge_rows_of(segment_ids, tokens))

    whole_low, normed_ext, normed, inverse, masks = normalized(
        tokens, other_tokens, edge, other_edge, norm_gain[None], segment_ids[None]
    )
    projected = jnp.einsum(
        "td,dce->cte", normed_ext, in_weight, preferred_element_type=f32
    ).astype(bf16)
    convolved, act, selected = convolve(
        projected, conv_weight, conv_bias[None], select_weight, masks
    )
    other_selected = swapped(selected, "narrow", 1)
    cot_whole = both_halves(cotangent, other_cot)
    gated_grad = lax.dot_general(
        cot_whole, out_weight, contract_last, preferred_element_type=f32
    )
    step_pre, step, ends = scan_ends(
        selected,
        other_selected,
        step_weight,
        step_bias[None],
        act,
        projected,
        gated_grad,
        masks,
        decay_log,
    )
    passed, entering, returning = carried(ends, decay_log)
    gated, gate_grad, entry = scan_forward(
        selected,
        other_selected,
        step,
        act,
        projected,
        gated_grad,
        masks,
        decay_log,
        passed,
        entering,
        skip_gain[None],
    )
    gated = after(gated, returning)
    products = (
        lax.dot_general(gated, cot_whole, contract_first, preferred_element_type=f32).astype(bf16),
        lax.dot_general(normed, gate_grad, contract_first, preferred_element_type=f32).astype(bf16),
    )
    out_sum, gate_sum = lax.psum(products, "wide")
    wide_place = lax.axis_index("wide").astype(jnp.int32)
    four_place = (wide_place & 3)[None]

    def narrow_halves(array):
        low, high = array[:, :features], array[:, features:]
        return jnp.where(right_half, high, low), jnp.where(right_half, low, high)

    def after_forward(products):
        whole = whole_low.astype(f32)
        act_grad, select_grad, scan_small = scan_backward(
            selected,
            other_selected,
            step_pre,
            step,
            act,
            projected,
            gated_grad,
            masks,
            decay_log,
            entry,
            passed,
            returning,
            skip_gain[None],
            step_weight,
        )
        normed_four = quarter_of_four(after(normed, select_grad))
        inner_main, before, last, conv_small = convolve_grad(
            select_grad,
            swapped(select_grad, "narrow", 1),
            select_weight,
            act_grad,
            convolved,
            act,
            projected,
            conv_weight,
            masks,
            [],
        )
        following = passed_along(before, "wide", -1)
        inner_grad = patched(segment_ids, inner_main, last, following, *normed_four)
        near = swapped(inner_grad, "wide", 2)
        keep, send = small_halves(wide_place[None] & 1, scan_small, conv_small, inner_grad)
        keep, send = folded((wide_place >> 1 & 1)[None], keep, swapped(send, "wide", 1))
        smalls = [keep, swapped(send, "wide", 2)]
        normed_part = jnp.einsum(
            "cte,dce->td", jnp.stack([inner_grad, gate_grad]), in_weight, preferred_element_type=f32
        )
        gain_part = jnp.sum(normed_part * whole * inverse, axis=0, keepdims=True)
        row_part = jnp.sum(normed_part * norm_gain * whole, axis=1)[None]
        first_bits, *more_bits = group_bits(2)
        gain_sum = gain_part + swapped(gain_part, "narrow", 1)
        for bit in (bit for bits in more_bits for bit in bits):
            gain_sum = gain_sum + swapped(gain_sum, "wide", bit)
        row_theirs = swapped(row_part, "narrow", 1)
        near = after(near, gain_sum, row_theirs, smalls[1])
        far = swapped(jnp.concatenate([inner_grad, near]), "wide", 1)
        keep, *sends = inner_quarter(
            (wide_place >> 2 & 3)[None],
            inner_grad,
            near,
            far,
            normed_four,
            smalls,
            [],
        )
        normed_mine, normed_other = narrow_halves(normed_part)
        normed_theirs = swapped(after(normed_other, keep), "narrow", 1)
        out_part = jnp.dot(after(gated, keep), out_weight, preferred_element_type=f32)
        out_mine, out_other = narrow_halves(out_part)
        out_theirs = swapped(out_other, "narrow", 1)
        layer_out = (tokens.astype(f32) + (out_mine + out_theirs)).astype(bf16)
        row_sum = (row_part + row_theirs).reshape(rows, 1)
        gain_mine = jnp.where(right_half, norm_gain[features:], norm_gain[:features])
        whole_grad = inverse * (gain_mine * (normed_mine + normed_theirs)) - tokens.astype(f32) * (
            inverse * inverse * inverse
        ) * (row_sum / (2 * features))
        tokens_grad = (whole_grad + cotangent.astype(f32)).astype(bf16)
        held = keep
        for n, flip in enumerate(flips(first_bits)[1:]):
            held = held + swapped(sends[n], "wide", flip).astype(f32)
        for bits in more_bits:
            held = scattered(held, bits)
        held = held.astype(bf16)
        for bits in reversed(more_bits):
            held = gathered(held, bits)
        spare = jnp.broadcast_to(gain_sum, (block_rows - used_rows, gain_sum.shape[1]))
        held = jnp.concatenate([held[: held.shape[0] - spare.shape[0]], spare.astype(bf16)])
        held = gathered(held, first_bits)
        return held, layer_out, tokens_grad

    kinds = jax.eval_shape(after_forward, products)
    held, layer_out, tokens_grad = lax.cond(
        wide_place >= 0,
        after_forward,
        lambda pair: jax.tree.map(lambda kind: jnp.zeros(kind.shape, kind.dtype), kinds),
        products,
    )

    core = swapped(held, "wide", 1)
    begun, out_weight_grad = joined_first(four_place, gate_sum, held, core, out_sum)
    near = swapped(held, "wide", 2)
    far = swapped(near, "wide", 1)
    conv_at = rank + count + 2
    (
        in_weight_grad,
        step_weight_grad,
        decay_log_grad,
        skip_gain_grad,
        step_bias_grad,
        select_weight_grad,
        conv_weight_grad,
        conv_bias_grad,
        norm_gain_grad,
    ) = joined_last(
        four_place,
        gate_sum,
        (held, core, near, far),
        begun,
        (0, rank, rank + count, rank + count + 1, conv_at, conv_at + columns, conv_at + columns + taps),
        (rank, count, 1, 1, columns, taps, 1, 1),
    )
    return (
        layer_out,
        tokens_grad,
        norm_gain_grad[0],
        in_weight_grad,
        conv_weight_grad,
        conv_bias_grad[0],
        select_weight_grad,
        step_weight_grad,
        step_bias_grad[0],
        decay_log_grad,
        skip_gain_grad[0],
        out_weight_grad,
    )


def solution(mesh):
    placed = (
        P("wide", "narrow"),
        P(),
        P(None, None, "narrow"),
        P(None, "narrow"),
        P("narrow"),
        P(None, "narrow"),
        P(None, "narrow"),
        P("narrow"),
        P(None, "narrow"),
        P("narrow"),
        P("narrow", None),
        P("wide"),
        P("wide", "narrow"),
    )
    return jax.shard_map(
        local,
        mesh=mesh,
        in_specs=placed,
        out_specs=(
            P("wide", "narrow"),
            P("wide", "narrow"),
            P(),
            P(None, None, "narrow"),
            P(None, "narrow"),
            P("narrow"),
            P(None, "narrow"),
            P(None, "narrow"),
            P("narrow"),
            P(None, "narrow"),
            P("narrow"),
            P("narrow", None),
        ),
        check_vma=False,
    )
```

```python
import functools

import jax
import jax.numpy as jnp
from jax import lax
from jax.experimental import pallas as pl
from jax.experimental.pallas import tpu as pltpu
from jax.sharding import PartitionSpec as P

epsilon = 1e-05
log2e = 1.4426950408889634
reset_step = 1e30
lanes = 128
halo = 16
body_rows = 32
scan_width = 512
vmem_bytes = 56 * 1024 * 1024
tiny_cost = pl.CostEstimate(flops=1, bytes_accessed=1, transcendentals=0)
f32 = jnp.float32
bf16 = jnp.bfloat16
contract_first = (((0,), (0,)), ((), ()))
contract_last = (((1,), (1,)), ((), ()))


def passed_along(array, axis, by):
    peers = lax.axis_size(axis)
    pairs = [(i, i + by) for i in range(peers) if 0 <= i + by < peers]
    return lax.ppermute(array, axis, pairs)


def swapped(array, axis, bit):
    peers = lax.axis_size(axis)
    return lax.ppermute(array, axis, [(i, i ^ bit) for i in range(peers)])


def wide_bits():
    bit, bits = 1, []
    while bit < lax.axis_size("wide"):
        bits.append(bit)
        bit *= 2
    return bits


def to_next_both(array):
    count, sides = lax.axis_size("wide"), lax.axis_size("narrow")
    pairs = [
        (i * sides + k, (i + 1) * sides + (sides - 1 - k))
        for i in range(count - 1)
        for k in range(sides)
    ]
    return passed_along(array, "wide", 1), lax.ppermute(array, ("wide", "narrow"), pairs)


def is_upper(bit):
    return (lax.axis_index("wide") & bit) != 0


def group_bits(size):
    bits, bit = [], 4
    while bit < lax.axis_size("wide"):
        bits.append(bit)
        bit *= 2
    return [tuple(bits[k : k + size]) for k in range(0, len(bits), size)]


def flips(bits):
    return [sum(b for k, b in enumerate(bits) if n >> k & 1) for n in range(2 ** len(bits))]


def scattered(piece, bits):
    rows = piece.shape[0] // 2 ** len(bits)
    here = sum(is_upper(b).astype(jnp.int32) << k for k, b in enumerate(bits))

    def block(n):
        return lax.dynamic_slice_in_dim(piece, (here ^ n) * rows, rows, 0)

    total = block(0).astype(f32)
    for n, flip in enumerate(flips(bits)):
        if n > 0:
            total = total + swapped(block(n).astype(bf16), "wide", flip).astype(f32)
    return total


def gathered(held, bits):
    blocks = [held] + [swapped(held, "wide", flip) for flip in flips(bits)[1:]]
    for bit in bits:
        upper = is_upper(bit)
        blocks = [
            jnp.concatenate([jnp.where(upper, b, a), jnp.where(upper, a, b)])
            for a, b in zip(blocks[0::2], blocks[1::2])
        ]
    return blocks[0]


def quarter_of_four(array):
    width = array.shape[1] // 4
    here = lax.axis_index("wide") & 3

    def quarter(n):
        return lax.dynamic_slice_in_dim(array, (here ^ n) * width, width, 1)

    return [quarter(0)] + [swapped(quarter(n), "wide", n) for n in (2, 1, 3)]


def silu_slope(values):
    logistic = jax.nn.sigmoid(values)
    return logistic * (1.0 + values * (1.0 - logistic))


def softplus(values):
    return jnp.maximum(values, 0.0) + jnp.log1p(jnp.exp(-jnp.abs(values)))


def column_spec(rows, start=0):
    return pl.BlockSpec((rows, scan_width), lambda j: (0, start + j))


def part_spec(part, rows, start=0):
    return pl.BlockSpec((None, rows, scan_width), lambda j: (part, 0, start + j))


def whole_spec(rows, width):
    return pl.BlockSpec((rows, width), lambda j: (0, 0))


def call(kernel, name, width, in_specs, out_specs, out_shape, scratch, *operands):
    return pl.pallas_call(
        kernel,
        grid=(width // scan_width,),
        in_specs=in_specs,
        out_specs=out_specs,
        out_shape=out_shape,
        scratch_shapes=scratch,
        compiler_params=pltpu.CompilerParams(vmem_limit_bytes=vmem_bytes),
        cost_estimate=tiny_cost,
        name=name,
    )(*operands)


def conv_kernel(
    inner_ref,
    conv_weight_ref,
    conv_bias_ref,
    select_ref,
    mask_ref,
    convolved_ref,
    act_ref,
    selected_ref,
    inner,
):
    rows = act_ref.shape[0]
    taps = conv_weight_ref.shape[0]
    inner[:halo, :] = inner_ref[rows:, :].astype(f32)
    inner[halo:, :] = inner_ref[:rows, :].astype(f32)
    total = conv_bias_ref[...] + conv_weight_ref[taps - 1 :, :] * inner[halo:, :]
    for lag in range(1, taps):
        earlier = inner[pl.ds(halo - lag, rows), :] * mask_ref[:, lag : lag + 1]
        total = total + conv_weight_ref[taps - 1 - lag : taps - lag, :] * earlier
    convolved_ref[...] = total
    act = (total * jax.nn.sigmoid(total)).astype(bf16)
    act_ref[...] = act
    part = lax.dot_general(select_ref[...], act, contract_last, preferred_element_type=f32)

    @pl.when(pl.program_id(0) == 0)
    def _():
        selected_ref[...] = part

    @pl.when(pl.program_id(0) > 0)
    def _():
        selected_ref[...] += part


def convolve(projected, conv_weight, conv_bias, select_weight, masks):
    parts, extended, width = projected.shape
    rows = extended - halo
    taps = conv_weight.shape[0]
    columns = select_weight.shape[0]
    return call(
        conv_kernel,
        "convolve",
        width,
        [
            part_spec(0, extended),
            column_spec(taps),
            column_spec(1),
            column_spec(columns),
            whole_spec(rows, masks.shape[1]),
        ],
        [column_spec(rows), column_spec(rows), whole_spec(columns, rows)],
        [
            jax.ShapeDtypeStruct((rows, width), f32),
            jax.ShapeDtypeStruct((rows, width), bf16),
            jax.ShapeDtypeStruct((columns, rows), f32),
        ],
        [pltpu.VMEM((extended, scan_width), f32)],
        projected,
        conv_weight,
        conv_bias,
        select_weight,
        masks,
    )


def coef_columns(coef, block):
    per_tile = lanes // body_rows
    start = pl.multiple_of((block // per_tile) * lanes, lanes)
    tile = coef[:, pl.ds(start, lanes)]
    back = body_rows * lax.rem(block, per_tile)
    return pltpu.roll(tile, lax.rem(lanes - back, lanes), 1)


def put_ends(ends_ref, state, adjoint, total):
    count, width = state.shape
    ends_ref[:count, :] = state.astype(bf16)
    ends_ref[count : 2 * count, :] = adjoint.astype(bf16)
    high = total.astype(bf16).astype(f32)
    upper = lax.broadcasted_iota(jnp.int32, (16, width), 0) < 8
    ends_ref[2 * count :, :] = jnp.where(upper, high, total - high).astype(bf16)


def get_ends(ends_ref, count):
    total = ends_ref[2 * count :].astype(f32)
    return (
        ends_ref[:count].astype(f32),
        ends_ref[count : 2 * count].astype(f32),
        total[:1] + total[8:9],
    )


def ends_kernel(
    selected_ref,
    other_ref,
    step_weight_ref,
    step_bias_ref,
    act_ref,
    gate_ref,
    gated_grad_ref,
    mask_ref,
    decay_log_ref,
    step_pre_ref,
    step_ref,
    ends_ref,
    coef,
    held_step,
    drive,
    scan_grad,
):
    rows = act_ref.shape[0]
    count = decay_log_ref.shape[0]
    rank = step_weight_ref.shape[0]
    decay2 = -jnp.exp(decay_log_ref[...]) * log2e
    selected = selected_ref[...] + other_ref[...]
    coef[...] = selected[rank:, :]
    step_low = selected[:rank, :].astype(bf16)
    step_pre = step_bias_ref[...] + lax.dot_general(
        step_low, step_weight_ref[...], contract_first, preferred_element_type=f32
    )
    step_pre_ref[...] = step_pre
    step = softplus(step_pre)
    step_ref[...] = step
    held_step[...] = jnp.where(mask_ref[:, 1:2] > 0.0, step, reset_step)
    drive[...] = step * act_ref[...].astype(f32)
    gate = gate_ref[...].astype(f32)
    scan_grad[...] = gated_grad_ref[...] * (gate * jax.nn.sigmoid(gate))
    zero = jnp.zeros(decay2.shape, f32)

    def body(block, carried):
        state, product, adjoint = carried
        columns = coef_columns(coef, block)
        for i in range(body_rows):
            row = pl.ds(block * body_rows + i, 1)
            factor = jnp.exp2(held_step[row, :] * decay2)
            state = factor * state + columns[:count, i : i + 1] * drive[row, :]
            product = factor * product
            adjoint = adjoint + product * (columns[count:, i : i + 1] * scan_grad[row, :])
        return state, product, adjoint

    state, product, adjoint = lax.fori_loop(0, rows // body_rows, body, (zero, zero + 1.0, zero))
    put_ends(ends_ref, state, adjoint, jnp.sum(held_step[...], axis=0, keepdims=True))


def scan_ends(
    selected, other, step_weight, step_bias, act, projected, gated_grad, masks, decay_log
):
    rows, width = act.shape
    count = decay_log.shape[0]
    columns = selected.shape[0]
    rank = step_weight.shape[0]
    return call(
        ends_kernel,
        "scan_ends",
        width,
        [
            whole_spec(columns, rows),
            whole_spec(columns, rows),
            column_spec(rank),
            column_spec(1),
            column_spec(rows),
            part_spec(1, rows),
            column_spec(rows),
            whole_spec(rows, masks.shape[1]),
            column_spec(count),
        ],
        [column_spec(rows), column_spec(rows), column_spec(2 * count + 16)],
        [
            jax.ShapeDtypeStruct((rows, width), f32),
            jax.ShapeDtypeStruct((rows, width), f32),
            jax.ShapeDtypeStruct((2 * count + 16, width), bf16),
        ],
        [pltpu.VMEM((2 * count, rows), f32)] + [pltpu.VMEM((rows, scan_width), f32)] * 3,
        selected,
        other,
        step_weight,
        step_bias,
        act,
        projected,
        gated_grad,
        masks,
        decay_log,
    )


def lane_tiles(values):
    return [values[:, k : k + lanes] for k in range(0, values.shape[1], lanes)]


def tree_sum(parts):
    while len(parts) > 1:
        odd = parts[len(parts) // 2 * 2 :]
        parts = [a + b for a, b in zip(parts[0::2], parts[1::2])] + odd
    return parts[0]


def keep_halves(scratch, i, values):
    for k, tile in enumerate(lane_tiles(values)):
        at = (k * body_rows + i) * 8
        scratch[at : at + 8, :] = tile[:8] + tile[8:]


def put_state_sums(scratch, out_ref, block):
    for group in range(body_rows // 8):
        row = pl.ds(pl.multiple_of(block * body_rows + group * 8, 8), 8)
        for k in range(out_ref.shape[1] // lanes):
            at = (k * body_rows + group * 8) * 8
            total = tree_sum([scratch[pl.ds(at + n, 8, stride=8), :] for n in range(8)])
            out_ref[row, k * lanes : (k + 1) * lanes] = total


def lane_sums(values):
    ones = jnp.ones((8, lanes), bf16)
    high = values.astype(bf16)
    low = (values - high.astype(f32)).astype(bf16)
    total = lax.dot_general(ones, high, contract_last, preferred_element_type=f32)
    total += lax.dot_general(ones, low, contract_last, preferred_element_type=f32)
    return total[:1, :]


def at_token(t, count):
    return pl.ds(pl.multiple_of(t * count, count), count)


def forward_kernel(
    selected_ref,
    other_ref,
    step_ref,
    act_ref,
    gate_ref,
    gated_grad_ref,
    mask_ref,
    decay_log_ref,
    passed_ref,
    entering_ref,
    skip_ref,
    cot_ref,
    normed_ref,
    gated_ref,
    gate_grad_ref,
    out_product_ref,
    gate_product_ref,
    entry_ref,
    coef,
    held_step,
    drive,
    scanned,
    halves,
):
    rows = step_ref.shape[0]
    count = decay_log_ref.shape[0]
    rank = selected_ref.shape[0] - 2 * count
    decay = -jnp.exp(decay_log_ref[...])
    decay2 = decay * log2e
    before_steps = passed_ref[2 * count : 2 * count + 1, :]
    entry = passed_ref[:count, :] + through(decay, before_steps) * entering_ref[...].astype(f32)
    entry_ref[...] = entry
    coef[...] = selected_ref[rank:, :] + other_ref[rank:, :]
    act = act_ref[...].astype(f32)
    held_step[...] = jnp.where(mask_ref[:, 1:2] > 0.0, step_ref[...], reset_step)
    drive[...] = step_ref[...] * act

    def forward(block, state):
        columns = coef_columns(coef, block)
        for i in range(body_rows):
            row = pl.ds(block * body_rows + i, 1)
            factor = jnp.exp2(held_step[row, :] * decay2)
            state = factor * state + columns[:count, i : i + 1] * drive[row, :]
            keep_halves(halves, i, columns[count:, i : i + 1] * state)
        put_state_sums(halves, scanned, block)
        return state

    lax.fori_loop(0, rows // body_rows, forward, entry)
    gate = gate_ref[...].astype(f32)
    logistic = jax.nn.sigmoid(gate)
    total = scanned[...] + skip_ref[...] * act
    gated = (total * (gate * logistic)).astype(bf16)
    gated_ref[...] = gated
    out_product_ref[...] = lax.dot_general(
        gated, cot_ref[...], contract_first, preferred_element_type=f32
    ).astype(bf16)
    slope = logistic * (1.0 + gate * (1.0 - logistic))
    gate_grad = (gated_grad_ref[...] * total * slope).astype(bf16)
    gate_grad_ref[...] = gate_grad
    gate_product_ref[...] = lax.dot_general(
        normed_ref[...], gate_grad, contract_first, preferred_element_type=f32
    ).astype(bf16)


def scan_forward(
    selected,
    other,
    step,
    act,
    projected,
    gated_grad,
    masks,
    decay_log,
    passed,
    entering,
    skip_gain,
    cot,
    normed,
):
    rows, width = step.shape
    count = decay_log.shape[0]
    columns = selected.shape[0]
    return call(
        forward_kernel,
        "scan_forward",
        width,
        [
            whole_spec(columns, rows),
            whole_spec(columns, rows),
            column_spec(rows),
            column_spec(rows),
            part_spec(1, rows),
            column_spec(rows),
            whole_spec(rows, masks.shape[1]),
            column_spec(count),
            column_spec(2 * count + 8),
            column_spec(count),
            column_spec(1),
            whole_spec(*cot.shape),
            whole_spec(*normed.shape),
        ],
        [
            column_spec(rows),
            column_spec(rows),
            pl.BlockSpec((scan_width, cot.shape[1]), lambda j: (j, 0)),
            column_spec(normed.shape[1]),
            column_spec(count),
        ],
        [
            jax.ShapeDtypeStruct((rows, width), bf16),
            jax.ShapeDtypeStruct((rows, width), bf16),
            jax.ShapeDtypeStruct((width, cot.shape[1]), bf16),
            jax.ShapeDtypeStruct((normed.shape[1], width), bf16),
            jax.ShapeDtypeStruct((count, width), f32),
        ],
        [pltpu.VMEM((2 * count, rows), f32)]
        + [pltpu.VMEM((rows, scan_width), f32)] * 3
        + [pltpu.VMEM((8 * body_rows * (scan_width // lanes), lanes), f32)],
        selected,
        other,
        step,
        act,
        projected,
        gated_grad,
        masks,
        decay_log,
        passed,
        entering,
        skip_gain,
        cot,
        normed,
    )


def backward_kernel(
    selected_ref,
    other_ref,
    step_pre_ref,
    step_ref,
    act_ref,
    gate_ref,
    gated_grad_ref,
    mask_ref,
    decay_log_ref,
    entry_ref,
    passed_ref,
    returning_ref,
    skip_ref,
    step_weight_ref,
    act_grad_ref,
    select_grad_ref,
    small_ref,
    coef,
    held_step,
    drive,
    scan_grad,
    weighted,
    held_sum,
    states,
    factors,
    halves,
    more_halves,
    in_sum,
    read_sum,
):
    rows = step_ref.shape[0]
    count = decay_log_ref.shape[0]
    rank = step_weight_ref.shape[0]
    blocks = rows // body_rows
    decay = -jnp.exp(decay_log_ref[...])
    decay2 = decay * log2e
    after_steps = passed_ref[2 * count + 1 : 2 * count + 2, :]
    tail = passed_ref[count : 2 * count, :] + through(decay, after_steps) * returning_ref[...].astype(f32)
    selected = selected_ref[...] + other_ref[...]
    coef[...] = selected[rank:, :]
    step_low = selected[:rank, :].astype(bf16)
    step = step_ref[...]
    act = act_ref[...].astype(f32)
    held_step[...] = jnp.where(mask_ref[:, 1:2] > 0.0, step, reset_step)
    drive[...] = step * act
    gate = gate_ref[...].astype(f32)
    grads = gated_grad_ref[...] * (gate * jax.nn.sigmoid(gate))
    scan_grad[...] = grads
    small_ref[rank + count : rank + count + 1, :] = jnp.sum(grads * act, axis=0, keepdims=True)
    states[:count, :] = entry_ref[...]

    @pl.when(pl.program_id(0) == 0)
    def _():
        in_sum[...] = jnp.zeros(in_sum.shape, f32)
        read_sum[...] = jnp.zeros(read_sum.shape, f32)
        select_grad_ref[...] = jnp.zeros(select_grad_ref.shape, f32)

    def forward(block, state):
        columns = coef_columns(coef, block)
        for i in range(body_rows):
            t = block * body_rows + i
            row = pl.ds(t, 1)
            factor = jnp.exp2(held_step[row, :] * decay2)
            state = factor * state + columns[:count, i : i + 1] * drive[row, :]
            factors[at_token(t, count), :] = factor
            states[at_token(t + 1, count), :] = state
        return state

    lax.fori_loop(0, blocks, forward, entry_ref[...])

    def backward(k, carried):
        adjoint, decay_grad = carried
        block = blocks - 1 - k
        columns = coef_columns(coef, block)
        for i in range(body_rows - 1, -1, -1):
            t = block * body_rows + i
            row = pl.ds(t, 1)
            here = at_token(t, count)
            grad = scan_grad[row, :]
            summed = columns[count:, i : i + 1] * grad + adjoint
            read_sum[here, :] += tree_sum(lane_tiles(grad * states[at_token(t + 1, count), :]))
            in_sum[here, :] += tree_sum(lane_tiles(summed * drive[row, :]))
            keep_halves(halves, i, summed * columns[:count, i : i + 1])
            adjoint = factors[here, :] * summed
            held = adjoint * states[here, :]
            decay_grad = decay_grad + held * step_ref[row, :]
            keep_halves(more_halves, i, held * decay)
        put_state_sums(halves, weighted, block)
        put_state_sums(more_halves, held_sum, block)
        return adjoint, decay_grad

    ignored, decay_grad = lax.fori_loop(
        0, blocks, backward, (tail, jnp.zeros(decay.shape, f32))
    )
    act_grad_ref[...] = step * weighted[...] + skip_ref[...] * scan_grad[...]
    step_grad = act * weighted[...] + held_sum[...]
    pre_grad = (step_grad * jax.nn.sigmoid(step_pre_ref[...])).astype(bf16)
    small_ref[:rank, :] = jnp.dot(step_low, pre_grad, preferred_element_type=f32)
    small_ref[rank : rank + count, :] = decay_grad * decay
    bias_grad = jnp.sum(pre_grad.astype(f32), axis=0, keepdims=True)
    small_ref[rank + count + 1 : rank + count + 2, :] = bias_grad
    select_grad_ref[:rank, :] += lax.dot_general(
        step_weight_ref[...], pre_grad, contract_last, preferred_element_type=f32
    )

    @pl.when(pl.program_id(0) == pl.num_programs(0) - 1)
    def _():
        for n in range(count):
            at = pl.ds(n, rows, stride=count)
            select_grad_ref[rank + n : rank + n + 1, :] = lane_sums(in_sum[at, :])
            select_grad_ref[rank + count + n : rank + count + n + 1, :] = lane_sums(read_sum[at, :])


def scan_backward(
    selected,
    other,
    step_pre,
    step,
    act,
    projected,
    gated_grad,
    masks,
    decay_log,
    entry,
    passed,
    returning,
    skip_gain,
    step_weight,
):
    rows, width = step.shape
    count = decay_log.shape[0]
    columns = selected.shape[0]
    rank = step_weight.shape[0]
    half_rows = 8 * body_rows * (scan_width // lanes)
    small = rank + count + 2
    return call(
        backward_kernel,
        "scan_backward",
        width,
        [
            whole_spec(columns, rows),
            whole_spec(columns, rows),
            column_spec(rows),
            column_spec(rows),
            column_spec(rows),
            part_spec(1, rows),
            column_spec(rows),
            whole_spec(rows, masks.shape[1]),
            column_spec(count),
            column_spec(count),
            column_spec(2 * count + 8),
            column_spec(count),
            column_spec(1),
            column_spec(rank),
        ],
        [column_spec(rows), whole_spec(columns, rows), column_spec(small)],
        [
            jax.ShapeDtypeStruct((rows, width), f32),
            jax.ShapeDtypeStruct((columns, rows), f32),
            jax.ShapeDtypeStruct((small, width), f32),
        ],
        [pltpu.VMEM((2 * count, rows), f32)]
        + [pltpu.VMEM((rows, scan_width), f32)] * 5
        + [
            pltpu.VMEM(((rows + 1) * count, scan_width), f32),
            pltpu.VMEM((rows * count, scan_width), f32),
            pltpu.VMEM((half_rows, lanes), f32),
            pltpu.VMEM((half_rows, lanes), f32),
            pltpu.VMEM((rows * count, lanes), f32),
            pltpu.VMEM((rows * count, lanes), f32),
        ],
        selected,
        other,
        step_pre,
        step,
        act,
        projected,
        gated_grad,
        masks,
        decay_log,
        entry,
        passed,
        returning,
        skip_gain,
        step_weight,
    )


def conv_grad_kernel(
    select_grad_ref,
    other_ref,
    select_ref,
    act_grad_ref,
    convolved_ref,
    act_ref,
    inner_ref,
    conv_weight_ref,
    mask_ref,
    *rest,
):
    inner_grad_ref, before_ref, last_ref, small_ref, inner, shifted = rest[-6:]
    rows = act_ref.shape[0]
    taps = conv_weight_ref.shape[0]
    columns = select_ref.shape[0]
    select_grad = (select_grad_ref[...] + other_ref[...]).astype(bf16)
    total = act_grad_ref[...] + lax.dot_general(
        select_grad, select_ref[...], contract_first, preferred_element_type=f32
    )
    conv_grad = total * silu_slope(convolved_ref[...])
    small_ref[:columns, :] = jnp.dot(select_grad, act_ref[...], preferred_element_type=f32)
    inner[:halo, :] = inner_ref[rows:, :].astype(f32)
    inner[halo:, :] = inner_ref[:rows, :].astype(f32)
    edges = jnp.zeros((8, conv_grad.shape[1]), f32)
    shifted[:8, :] = edges
    shifted[rows + 8 :, :] = edges
    out = conv_weight_ref[taps - 1 :, :] * conv_grad
    before = edges
    small_ref[columns + taps - 1 : columns + taps, :] = jnp.sum(
        conv_grad * inner[halo:, :], axis=0, keepdims=True
    )
    for lag in range(1, taps):
        masked = conv_grad * mask_ref[:, lag : lag + 1]
        at = taps - 1 - lag
        small_ref[columns + at : columns + at + 1, :] = jnp.sum(
            masked * inner[pl.ds(halo - lag, rows), :], axis=0, keepdims=True
        )
        shifted[8 : rows + 8, :] = masked
        weight = conv_weight_ref[at : at + 1, :]
        out = out + weight * shifted[pl.ds(8 + lag, rows), :]
        before = before + weight * shifted[pl.ds(lag, 8), :]
    small_ref[columns + taps : columns + taps + 1, :] = jnp.sum(conv_grad, axis=0, keepdims=True)
    inner_grad_ref[...] = out.astype(bf16)
    before_ref[...] = before
    last_ref[...] = out[rows - 8 :, :]


def convolve_grad(
    select_grad, other, select_weight, act_grad, convolved, act, projected, conv_weight, masks, waits
):
    rows, width = act.shape
    extended = rows + halo
    columns = select_weight.shape[0]
    taps = conv_weight.shape[0]
    small = columns + taps + 1
    return call(
        conv_grad_kernel,
        "convolve_grad",
        width,
        [
            whole_spec(columns, rows),
            whole_spec(columns, rows),
            column_spec(columns),
            column_spec(rows),
            column_spec(rows),
            column_spec(rows),
            part_spec(0, extended),
            column_spec(taps),
            whole_spec(rows, masks.shape[1]),
        ]
        + [pl.BlockSpec(memory_space=pl.ANY)] * len(waits),
        [column_spec(rows), column_spec(8), column_spec(8), column_spec(small)],
        [
            jax.ShapeDtypeStruct((rows, width), bf16),
            jax.ShapeDtypeStruct((8, width), f32),
            jax.ShapeDtypeStruct((8, width), f32),
            jax.ShapeDtypeStruct((small, width), f32),
        ],
        [pltpu.VMEM((extended, scan_width), f32), pltpu.VMEM((rows + 16, scan_width), f32)],
        select_grad,
        other,
        select_weight,
        act_grad,
        convolved,
        act,
        projected,
        conv_weight,
        masks,
        *waits,
    )


def normalize_kernel(
    own_ref,
    other_ref,
    edge_ref,
    other_edge_ref,
    gain_ref,
    ids_ref,
    whole_ref,
    extended_ref,
    normed_ref,
    inverse_ref,
    mask_ref,
    rows_ref,
):
    rows, half = own_ref.shape
    ids = ids_ref[...].astype(f32)
    place = lax.broadcasted_iota(jnp.int32, ids.shape, 1)
    same = []
    for lag in range(8):
        earlier = jnp.where(place < lag, ids[:, :1], pltpu.roll(ids, lag, 1)) if lag else ids
        same.append(jnp.where(earlier == ids, 1.0, 0.0))
    spare = jnp.zeros((lanes - 8, rows), f32)
    mask_ref[...] = jnp.concatenate(same + [spare]).T
    right = lax.axis_index("narrow") == 1
    for at, own, other in ((0, own_ref, other_ref), (rows, edge_ref, other_edge_ref)):
        end = at + own.shape[0]
        rows_ref[at:end, :half] = jnp.where(right, other[...], own[...])
        rows_ref[at:end, half:] = jnp.where(right, own[...], other[...])
    whole_ref[...] = rows_ref[:rows, :]
    whole = rows_ref[...].astype(f32)
    inverse = lax.rsqrt(jnp.mean(whole * whole, axis=1, keepdims=True) + epsilon)
    normed = (whole * inverse * gain_ref[...]).astype(bf16)
    extended_ref[...] = normed
    normed_ref[...] = normed[:rows]
    inverse_ref[...] = inverse[:rows]


def normalized(own, other, edge, other_edge, gain, ids):
    rows, half = own.shape
    extended = rows + edge.shape[0]
    return pl.pallas_call(
        normalize_kernel,
        out_shape=[
            jax.ShapeDtypeStruct((rows, 2 * half), bf16),
            jax.ShapeDtypeStruct((extended, 2 * half), bf16),
            jax.ShapeDtypeStruct((rows, 2 * half), bf16),
            jax.ShapeDtypeStruct((rows, 1), f32),
            jax.ShapeDtypeStruct((rows, lanes), f32),
        ],
        scratch_shapes=[pltpu.VMEM((extended, 2 * half), bf16)],
        cost_estimate=tiny_cost,
        name="normalized",
    )(own, other, edge, other_edge, gain, ids)


def after(array, *waits):
    anywhere = pl.BlockSpec(memory_space=pl.ANY)
    return pl.pallas_call(
        lambda *refs: None,
        in_specs=[anywhere] * (1 + len(waits)),
        out_specs=anywhere,
        out_shape=jax.ShapeDtypeStruct(array.shape, array.dtype),
        input_output_aliases={0: 0},
        cost_estimate=tiny_cost,
        name="after",
    )(array, *waits)


def patch_kernel(ids_ref, rows_ref, last_ref, next_ref, *rest):
    count = ids_ref.shape[0]
    place = lax.broadcasted_iota(jnp.int32, (8, 1), 0)
    same = jnp.zeros((8, 1), f32)
    for lag in range(8):
        here = jnp.where(ids_ref[count - 1 - lag] == ids_ref[count - 1], 1.0, 0.0)
        same = same + jnp.where(place == 7 - lag, here, 0.0)
    total = last_ref[...] + next_ref[...] * same
    rows = rows_ref[...].astype(f32)
    rest[-1][...] = jnp.concatenate([rows[: halo - 8], total]).astype(bf16)


def patched(ids, grads, last, following, *waits):
    rows, width = grads.shape
    block = pl.BlockSpec((halo, width), lambda j: (rows // halo - 1, 0))
    edge = pl.BlockSpec((8, width), lambda j: (0, 0))
    return pl.pallas_call(
        patch_kernel,
        grid=(1,),
        in_specs=[pl.BlockSpec(memory_space=pltpu.SMEM), block, edge, edge]
        + [pl.BlockSpec(memory_space=pl.ANY)] * len(waits),
        out_specs=block,
        out_shape=jax.ShapeDtypeStruct((rows, width), bf16),
        input_output_aliases={1: 0},
        cost_estimate=tiny_cost,
        name="patched",
    )(ids, grads, last, following, *waits)


def edge_kernel(ids_ref, tokens_ref, out_ref):
    rows = ids_ref.shape[0]
    taps = 4
    out_ref[...] = tokens_ref[...]
    place = lax.broadcasted_iota(jnp.int32, (halo, 1), 0)
    same = jnp.zeros((halo, 1), f32)
    for lag in range(taps):
        here = jnp.where(ids_ref[rows - 1 - lag] == ids_ref[rows - 1], 1.0, 0.0)
        same = same + jnp.where(place == halo - 1 - lag, here, 0.0)
    out_ref[...] = (tokens_ref[...].astype(f32) * same).astype(bf16)


def edge_rows_of(ids, tokens):
    rows, width = tokens.shape
    return pl.pallas_call(
        edge_kernel,
        grid=(1,),
        in_specs=[
            pl.BlockSpec(memory_space=pltpu.SMEM),
            pl.BlockSpec((halo, width), lambda j: (rows // halo - 1, 0)),
        ],
        out_specs=pl.BlockSpec((halo, width), lambda j: (0, 0)),
        out_shape=jax.ShapeDtypeStruct((halo, width), bf16),
        cost_estimate=tiny_cost,
        name="edge_rows",
    )(ids, tokens)


block_rows, used_rows = 16, 12


def small_kernel(core_ref, scan_ref, conv_ref, wait_ref, keep_ref, send_ref, rows, blocks):
    rows[...] = jnp.zeros(rows.shape, f32)
    rows[: scan_ref.shape[0], :] = scan_ref[...]
    rows[scan_ref.shape[0] : scan_ref.shape[0] + conv_ref.shape[0], :] = conv_ref[...]
    blocks[...] = jnp.zeros(blocks.shape, f32)
    for n in range(16):
        blocks[n * block_rows : n * block_rows + used_rows, :] = rows[
            n * used_rows : (n + 1) * used_rows, :
        ]
    half = keep_ref.shape[0]
    mine = pl.ds(pl.multiple_of(core_ref[0] * half, half), half)
    other = pl.ds(pl.multiple_of((1 - core_ref[0]) * half, half), half)
    keep_ref[...] = blocks[mine, :]
    send_ref[...] = blocks[other, :].astype(bf16)


def small_halves(core, scan_small, conv_small, wait):
    width = scan_small.shape[1]
    return pl.pallas_call(
        small_kernel,
        in_specs=[pl.BlockSpec(memory_space=pltpu.SMEM)]
        + [pl.BlockSpec(memory_space=pltpu.VMEM)] * 2
        + [pl.BlockSpec(memory_space=pl.ANY)],
        out_shape=[jax.ShapeDtypeStruct((8 * block_rows, width), kind) for kind in (f32, bf16)],
        scratch_shapes=[
            pltpu.VMEM((16 * used_rows, width), f32),
            pltpu.VMEM((16 * block_rows, width), f32),
        ],
        cost_estimate=tiny_cost,
        name="small_halves",
    )(core, scan_small, conv_small, wait)


def fold_kernel(upper_ref, keep_ref, arrived_ref, out_ref, send_ref):
    size = out_ref.shape[0]
    mine = pl.ds(pl.multiple_of(upper_ref[0] * size, size), size)
    other = pl.ds(pl.multiple_of((1 - upper_ref[0]) * size, size), size)
    out_ref[...] = keep_ref[mine, :] + arrived_ref[mine, :].astype(f32)
    send_ref[...] = (keep_ref[other, :] + arrived_ref[other, :].astype(f32)).astype(bf16)


def folded(upper, keep, arrived):
    rows, width = keep.shape
    return pl.pallas_call(
        fold_kernel,
        in_specs=[pl.BlockSpec(memory_space=pltpu.SMEM)]
        + [pl.BlockSpec(memory_space=pltpu.VMEM)] * 2,
        out_shape=[jax.ShapeDtypeStruct((rows // 2, width), kind) for kind in (f32, bf16)],
        cost_estimate=tiny_cost,
        name="folded",
    )(upper, keep, arrived)


def quarter_kernel(
    place_ref,
    own_ref,
    near_ref,
    far_ref,
    normed_0,
    normed_1,
    normed_2,
    normed_3,
    small_ref,
    arrived_ref,
    *rest,
):
    keep_ref, *sends_refs, piece, small = rest[-6:]
    total = None
    tokens = own_ref.shape[0]
    grads = (own_ref[...], near_ref[...], far_ref[:tokens, :], far_ref[tokens:, :])
    for left, right in zip((normed_0, normed_1, normed_2, normed_3), grads):
        part = lax.dot_general(left[...], right, contract_first, preferred_element_type=f32)
        total = part if total is None else total + part
    piece[...] = total
    small[...] = small_ref[...] + arrived_ref[...].astype(f32)
    rows, spare = piece.shape[0] // 4, small.shape[0] // 4
    for n in range(4):
        block = place_ref[0] ^ n
        inner_rows = piece[pl.ds(pl.multiple_of(block * rows, rows), rows), :]
        small_rows = small[pl.ds(pl.multiple_of(block * spare, spare), spare), :]
        if n == 0:
            keep_ref[:rows, :] = inner_rows
            keep_ref[rows:, :] = small_rows
        else:
            sends_refs[n - 1][:rows, :] = inner_rows.astype(bf16)
            sends_refs[n - 1][rows:, :] = small_rows.astype(bf16)


def inner_quarter(place, own, near, far, normed, smalls, waits):
    width = own.shape[1]
    quarter = normed[0].shape[1]
    spare = smalls[0].shape[0]
    rows = (quarter + spare) // 4
    return pl.pallas_call(
        quarter_kernel,
        in_specs=[pl.BlockSpec(memory_space=pltpu.SMEM)]
        + [pl.BlockSpec(memory_space=pltpu.VMEM)] * 9
        + [pl.BlockSpec(memory_space=pl.ANY)] * len(waits),
        out_shape=[jax.ShapeDtypeStruct((rows, width), f32)]
        + [jax.ShapeDtypeStruct((rows, width), bf16)] * 3,
        scratch_shapes=[pltpu.VMEM((quarter, width), f32), pltpu.VMEM((spare, width), f32)],
        compiler_params=pltpu.CompilerParams(vmem_limit_bytes=vmem_bytes),
        cost_estimate=tiny_cost,
        name="inner_quarter",
    )(place, own, near, far, *normed, *smalls, *waits)


def put_quarter(out_ref, gate_ref, inner_ref):
    rows = out_ref.shape[0] // 4
    out_ref[:, 1, :] = gate_ref[...].astype(f32)
    for n in range(4):
        at = n * (rows + block_rows)
        out_ref[n * rows : (n + 1) * rows, 0, :] = inner_ref[at : at + rows, :].astype(f32)


def first_join_kernel(place_ref, gate_ref, first_ref, second_ref, low_ref, out_ref, wide_ref):
    wide_ref[...] = low_ref[...].astype(f32)

    @pl.when(pl.program_id(0) == 0)
    def _():
        put_quarter(out_ref, gate_ref, first_ref)

    @pl.when(pl.program_id(0) == 1)
    def _():
        put_quarter(out_ref, gate_ref, second_ref)


def last_join_kernel(place_ref, gate_ref, first_ref, second_ref, *rest, small_rows):
    held = rest[:4]
    out_ref, *row_refs, gain_ref, blocks = rest[5:]

    @pl.when(pl.program_id(0) == 0)
    def _():
        put_quarter(out_ref, gate_ref, first_ref)

    @pl.when(pl.program_id(0) == 1)
    def _():
        put_quarter(out_ref, gate_ref, second_ref)
        rows = out_ref.shape[0] // 4
        for flip, ref in enumerate(held):
            number = place_ref[0] ^ flip
            number = (number & 1) * 2 + number // 2
            for n in range(4):
                at = (number * 4 + n) * block_rows
                taken = ref[(n + 1) * rows + n * block_rows : (n + 1) * (rows + block_rows), :]
                blocks[pl.ds(pl.multiple_of(at, block_rows), block_rows), :] = taken.astype(f32)
        for ref, start in zip(row_refs, small_rows):
            for row in range(ref.shape[0]):
                at = (start + row) // used_rows * block_rows + (start + row) % used_rows
                ref[row : row + 1, :] = blocks[at : at + 1, :]
        gain_ref[...] = sum(
            blocks[n * block_rows + used_rows : n * block_rows + used_rows + 1, :] for n in range(16)
        )


def joined(kernel, place, flip, gate, first, second, specs, operands, out_specs, out_shape, scratch, aliases):
    depth, width = gate.shape
    quarter = depth // 4

    def target(j, place):
        return place[0] ^ (flip + j)

    whole = pl.BlockSpec(first.shape, lambda j, place: (0, 0))
    return pl.pallas_call(
        kernel,
        grid_spec=pltpu.PrefetchScalarGridSpec(
            num_scalar_prefetch=1,
            grid=(2,),
            in_specs=[
                pl.BlockSpec((quarter, width), lambda j, place: (target(j, place), 0)),
                whole,
                whole,
            ]
            + specs,
            out_specs=[
                pl.BlockSpec((quarter, 2, width), lambda j, place: (target(j, place), 0, 0))
            ]
            + out_specs,
            scratch_shapes=scratch,
        ),
        out_shape=[jax.ShapeDtypeStruct((depth, 2, width), f32)] + out_shape,
        input_output_aliases=aliases,
        compiler_params=pltpu.CompilerParams(vmem_limit_bytes=vmem_bytes),
        cost_estimate=tiny_cost,
        name="joined",
    )(place, gate, first, second, *operands)


def joined_first(place, gate, first, second, low):
    rows, width = low.shape
    half = pl.BlockSpec((rows // 2, width), lambda j, place: (j, 0))
    kind = jax.ShapeDtypeStruct((rows, width), f32)
    return joined(
        first_join_kernel, place, 0, gate, first, second, [half], [low], [half], [kind], [], {}
    )


def joined_last(place, gate, held, begun, small_rows, small_counts):
    width = gate.shape[1]
    whole = pl.BlockSpec(held[0].shape, lambda j, place: (0, 0))
    return joined(
        functools.partial(last_join_kernel, small_rows=small_rows),
        place,
        2,
        gate,
        held[2],
        held[3],
        [whole] * 4 + [pl.BlockSpec(memory_space=pl.ANY)],
        [*held, begun],
        [pl.BlockSpec((rows, width), lambda j, place: (0, 0)) for rows in small_counts],
        [jax.ShapeDtypeStruct((rows, width), f32) for rows in small_counts],
        [pltpu.VMEM((16 * block_rows, width), f32)],
        {8: 0},
    )


def through(decay, total):
    return jnp.exp(decay * total)


def round_kernel(second_ref, decay_log_ref, own_ref, other_ref, *rest, first):
    count, width = decay_log_ref.shape
    new_passed_ref, *ends_refs = rest if first else rest[1:]
    decay = -jnp.exp(decay_log_ref[...])
    second = second_ref[0] > 0
    own, other = get_ends(own_ref, count), get_ends(other_ref, count)
    early = [jnp.where(second, b, a) for a, b in zip(own, other)]
    late = [jnp.where(second, a, b) for a, b in zip(own, other)]
    state = late[0] + through(decay, late[2]) * early[0]
    adjoint = early[1] + through(decay, early[2]) * late[1]
    if len(ends_refs) == 2:
        ends_refs[0][...] = state.astype(bf16)
        ends_refs[1][...] = adjoint.astype(bf16)
    else:
        put_ends(ends_refs[0], state, adjoint, early[2] + late[2])
    if first:
        before = after = jnp.zeros((count, width), f32)
        before_steps = after_steps = jnp.zeros((1, width), f32)
    else:
        before, after = rest[0][:count], rest[0][count : 2 * count]
        before_steps = rest[0][2 * count : 2 * count + 1]
        after_steps = rest[0][2 * count + 1 : 2 * count + 2]
    new_passed_ref[:count, :] = before + jnp.where(second, through(decay, before_steps) * other[0], 0.0)
    new_passed_ref[count : 2 * count, :] = after + jnp.where(
        second, 0.0, through(decay, after_steps) * other[1]
    )
    new_passed_ref[2 * count : 2 * count + 1, :] = before_steps + jnp.where(second, other[2], 0.0)
    new_passed_ref[2 * count + 1 : 2 * count + 2, :] = after_steps + jnp.where(second, 0.0, other[2])


def carried(ends, decay_log):
    count, width = decay_log.shape
    place = lax.axis_index("wide").astype(jnp.int32)
    state = jax.ShapeDtypeStruct((count, width), bf16)
    passed_kind = jax.ShapeDtypeStruct((2 * count + 8, width), f32)
    packed, passed = ends, []
    vmem = pl.BlockSpec(memory_space=pltpu.VMEM)
    for k, kinds in enumerate(([jax.ShapeDtypeStruct(ends.shape, bf16)], [state, state])):
        new_passed, *out = pl.pallas_call(
            functools.partial(round_kernel, first=k == 0),
            in_specs=[pl.BlockSpec(memory_space=pltpu.SMEM)] + [vmem] * (3 + k),
            out_shape=[passed_kind] + kinds,
            cost_estimate=tiny_cost,
            name="carry_round",
        )((place >> k & 1)[None], decay_log, packed, swapped(packed, "wide", 2**k), *passed)
        packed, passed = out[0], [new_passed]
    from_before = passed_along(out[0], "wide", 4)
    from_after = passed_along(out[1], "wide", -4)
    return passed[0], from_before, from_after


def local(
    tokens,
    norm_gain,
    in_weight,
    conv_weight,
    conv_bias,
    select_weight,
    step_weight,
    step_bias,
    decay_log,
    skip_gain,
    out_weight,
    segment_ids,
    cotangent,
):
    rows, features = tokens.shape
    taps = conv_weight.shape[0]
    columns = select_weight.shape[0]
    rank = step_weight.shape[0]
    count = decay_log.shape[0]
    right_half = lax.axis_index("narrow") == 1

    def both_halves(own, other):
        return jnp.concatenate(
            [jnp.where(right_half, other, own), jnp.where(right_half, own, other)], axis=1
        )

    other_tokens = swapped(tokens, "narrow", 1)
    other_cot = swapped(cotangent, "narrow", 1)
    edge, other_edge = to_next_both(edge_rows_of(segment_ids, tokens))

    whole_low, normed_ext, normed, inverse, masks = normalized(
        tokens, other_tokens, edge, other_edge, norm_gain[None], segment_ids[None]
    )
    projected = jnp.einsum(
        "td,dce->cte", normed_ext, in_weight, preferred_element_type=f32
    ).astype(bf16)
    convolved, act, selected = convolve(
        projected, conv_weight, conv_bias[None], select_weight, masks
    )
    other_selected = swapped(selected, "narrow", 1)
    cot_whole = both_halves(cotangent, other_cot)
    gated_grad = lax.dot_general(
        cot_whole, out_weight, contract_last, preferred_element_type=f32
    )
    step_pre, step, ends = scan_ends(
        selected,
        other_selected,
        step_weight,
        step_bias[None],
        act,
        projected,
        gated_grad,
        masks,
        decay_log,
    )
    passed, entering, returning = carried(ends, decay_log)
    gated, gate_grad, out_product, gate_product, entry = scan_forward(
        selected,
        other_selected,
        step,
        act,
        projected,
        gated_grad,
        masks,
        decay_log,
        passed,
        entering,
        skip_gain[None],
        cot_whole,
        normed,
    )
    products = (after(out_product, returning), gate_product)
    out_sum, gate_sum = lax.psum(products, "wide")
    wide_place = lax.axis_index("wide").astype(jnp.int32)
    four_place = (wide_place & 3)[None]

    def narrow_halves(array):
        low, high = array[:, :features], array[:, features:]
        return jnp.where(right_half, high, low), jnp.where(right_half, low, high)

    def after_forward(products):
        whole = whole_low.astype(f32)
        act_grad, select_grad, scan_small = scan_backward(
            selected,
            other_selected,
            step_pre,
            step,
            act,
            projected,
            gated_grad,
            masks,
            decay_log,
            entry,
            passed,
            returning,
            skip_gain[None],
            step_weight,
        )
        normed_four = quarter_of_four(after(normed, select_grad))
        inner_main, before, last, conv_small = convolve_grad(
            select_grad,
            swapped(select_grad, "narrow", 1),
            select_weight,
            act_grad,
            convolved,
            act,
            projected,
            conv_weight,
            masks,
            [],
        )
        following = passed_along(before, "wide", -1)
        inner_grad = patched(segment_ids, inner_main, last, following, *normed_four)
        near = swapped(inner_grad, "wide", 2)
        keep, send = small_halves(wide_place[None] & 1, scan_small, conv_small, inner_grad)
        keep, send = folded((wide_place >> 1 & 1)[None], keep, swapped(send, "wide", 1))
        smalls = [keep, swapped(send, "wide", 2)]
        normed_part = jnp.einsum(
            "cte,dce->td", jnp.stack([inner_grad, gate_grad]), in_weight, preferred_element_type=f32
        )
        gain_part = jnp.sum(normed_part * whole * inverse, axis=0, keepdims=True)
        row_part = jnp.sum(normed_part * norm_gain * whole, axis=1)[None]
        first_bits, *more_bits = group_bits(2)
        gain_sum = gain_part + swapped(gain_part, "narrow", 1)
        for bit in (bit for bits in more_bits for bit in bits):
            gain_sum = gain_sum + swapped(gain_sum, "wide", bit)
        row_theirs = swapped(row_part, "narrow", 1)
        near = after(near, gain_sum, row_theirs, smalls[1])
        far = swapped(jnp.concatenate([inner_grad, near]), "wide", 1)
        keep, *sends = inner_quarter(
            (wide_place >> 2 & 3)[None],
            inner_grad,
            near,
            far,
            normed_four,
            smalls,
            [],
        )
        normed_mine, normed_other = narrow_halves(normed_part)
        normed_theirs = swapped(after(normed_other, keep), "narrow", 1)
        out_part = jnp.dot(after(gated, keep), out_weight, preferred_element_type=f32)
        out_mine, out_other = narrow_halves(out_part)
        out_theirs = swapped(out_other, "narrow", 1)
        layer_out = (tokens.astype(f32) + (out_mine + out_theirs)).astype(bf16)
        row_sum = (row_part + row_theirs).reshape(rows, 1)
        gain_mine = jnp.where(right_half, norm_gain[features:], norm_gain[:features])
        whole_grad = inverse * (gain_mine * (normed_mine + normed_theirs)) - tokens.astype(f32) * (
            inverse * inverse * inverse
        ) * (row_sum / (2 * features))
        tokens_grad = (whole_grad + cotangent.astype(f32)).astype(bf16)
        held = keep
        for n, flip in enumerate(flips(first_bits)[1:]):
            held = held + swapped(sends[n], "wide", flip).astype(f32)
        for bits in more_bits:
            held = scattered(held, bits)
        held = held.astype(bf16)
        for bits in reversed(more_bits):
            held = gathered(held, bits)
        spare = jnp.broadcast_to(gain_sum, (block_rows - used_rows, gain_sum.shape[1]))
        held = jnp.concatenate([held[: held.shape[0] - spare.shape[0]], spare.astype(bf16)])
        held = gathered(held, first_bits)
        return held, layer_out, tokens_grad

    kinds = jax.eval_shape(after_forward, products)
    held, layer_out, tokens_grad = lax.cond(
        wide_place >= 0,
        after_forward,
        lambda pair: jax.tree.map(lambda kind: jnp.zeros(kind.shape, kind.dtype), kinds),
        products,
    )

    core = swapped(held, "wide", 1)
    begun, out_weight_grad = joined_first(four_place, gate_sum, held, core, out_sum)
    near = swapped(held, "wide", 2)
    far = swapped(near, "wide", 1)
    conv_at = rank + count + 2
    (
        in_weight_grad,
        step_weight_grad,
        decay_log_grad,
        skip_gain_grad,
        step_bias_grad,
        select_weight_grad,
        conv_weight_grad,
        conv_bias_grad,
        norm_gain_grad,
    ) = joined_last(
        four_place,
        gate_sum,
        (held, core, near, far),
        begun,
        (0, rank, rank + count, rank + count + 1, conv_at, conv_at + columns, conv_at + columns + taps),
        (rank, count, 1, 1, columns, taps, 1, 1),
    )
    return (
        layer_out,
        tokens_grad,
        norm_gain_grad[0],
        in_weight_grad,
        conv_weight_grad,
        conv_bias_grad[0],
        select_weight_grad,
        step_weight_grad,
        step_bias_grad[0],
        decay_log_grad,
        skip_gain_grad[0],
        out_weight_grad,
    )


def solution(mesh):
    placed = (
        P("wide", "narrow"),
        P(),
        P(None, None, "narrow"),
        P(None, "narrow"),
        P("narrow"),
        P(None, "narrow"),
        P(None, "narrow"),
        P("narrow"),
        P(None, "narrow"),
        P("narrow"),
        P("narrow", None),
        P("wide"),
        P("wide", "narrow"),
    )
    return jax.shard_map(
        local,
        mesh=mesh,
        in_specs=placed,
        out_specs=(
            P("wide", "narrow"),
            P("wide", "narrow"),
            P(),
            P(None, None, "narrow"),
            P(None, "narrow"),
            P("narrow"),
            P(None, "narrow"),
            P(None, "narrow"),
            P("narrow"),
            P(None, "narrow"),
            P("narrow"),
            P("narrow", None),
        ),
        check_vma=False,
    )
```

```python
import functools

import jax
import jax.numpy as jnp
from jax import lax
from jax.experimental import pallas as pl
from jax.experimental.pallas import tpu as pltpu
from jax.sharding import PartitionSpec as P

epsilon = 1e-05
log2e = 1.4426950408889634
reset_step = 1e30
lanes = 128
halo = 16
body_rows = 32
scan_width = 512
vmem_bytes = 56 * 1024 * 1024
tiny_cost = pl.CostEstimate(flops=1, bytes_accessed=1, transcendentals=0)
f32 = jnp.float32
bf16 = jnp.bfloat16
contract_first = (((0,), (0,)), ((), ()))
contract_last = (((1,), (1,)), ((), ()))


def passed_along(array, axis, by):
    peers = lax.axis_size(axis)
    pairs = [(i, i + by) for i in range(peers) if 0 <= i + by < peers]
    return lax.ppermute(array, axis, pairs)


def swapped(array, axis, bit):
    peers = lax.axis_size(axis)
    return lax.ppermute(array, axis, [(i, i ^ bit) for i in range(peers)])


def wide_bits():
    bit, bits = 1, []
    while bit < lax.axis_size("wide"):
        bits.append(bit)
        bit *= 2
    return bits


def to_next_both(array):
    count, sides = lax.axis_size("wide"), lax.axis_size("narrow")
    pairs = [
        (i * sides + k, (i + 1) * sides + (sides - 1 - k))
        for i in range(count - 1)
        for k in range(sides)
    ]
    return passed_along(array, "wide", 1), lax.ppermute(array, ("wide", "narrow"), pairs)


def is_upper(bit):
    return (lax.axis_index("wide") & bit) != 0


def group_bits(size):
    bits, bit = [], 4
    while bit < lax.axis_size("wide"):
        bits.append(bit)
        bit *= 2
    return [tuple(bits[k : k + size]) for k in range(0, len(bits), size)]


def flips(bits):
    return [sum(b for k, b in enumerate(bits) if n >> k & 1) for n in range(2 ** len(bits))]


def scattered(piece, bits):
    rows = piece.shape[0] // 2 ** len(bits)
    here = sum(is_upper(b).astype(jnp.int32) << k for k, b in enumerate(bits))

    def block(n):
        return lax.dynamic_slice_in_dim(piece, (here ^ n) * rows, rows, 0)

    total = block(0).astype(f32)
    for n, flip in enumerate(flips(bits)):
        if n > 0:
            total = total + swapped(block(n).astype(bf16), "wide", flip).astype(f32)
    return total


def gathered(held, bits):
    blocks = [held] + [swapped(held, "wide", flip) for flip in flips(bits)[1:]]
    for bit in bits:
        upper = is_upper(bit)
        blocks = [
            jnp.concatenate([jnp.where(upper, b, a), jnp.where(upper, a, b)])
            for a, b in zip(blocks[0::2], blocks[1::2])
        ]
    return blocks[0]


def quarter_of_four(array):
    width = array.shape[1] // 4
    here = lax.axis_index("wide") & 3

    def quarter(n):
        return lax.dynamic_slice_in_dim(array, (here ^ n) * width, width, 1)

    return [quarter(0)] + [swapped(quarter(n), "wide", n) for n in (2, 1, 3)]


def silu_slope(values):
    logistic = jax.nn.sigmoid(values)
    return logistic * (1.0 + values * (1.0 - logistic))


def softplus(values):
    return jnp.maximum(values, 0.0) + jnp.log1p(jnp.exp(-jnp.abs(values)))


def column_spec(rows, start=0):
    return pl.BlockSpec((rows, scan_width), lambda j: (0, start + j))


def part_spec(part, rows, start=0):
    return pl.BlockSpec((None, rows, scan_width), lambda j: (part, 0, start + j))


def whole_spec(rows, width):
    return pl.BlockSpec((rows, width), lambda j: (0, 0))


def call(kernel, name, width, in_specs, out_specs, out_shape, scratch, *operands):
    return pl.pallas_call(
        kernel,
        grid=(width // scan_width,),
        in_specs=in_specs,
        out_specs=out_specs,
        out_shape=out_shape,
        scratch_shapes=scratch,
        compiler_params=pltpu.CompilerParams(vmem_limit_bytes=vmem_bytes),
        cost_estimate=tiny_cost,
        name=name,
    )(*operands)


def conv_kernel(
    inner_ref,
    conv_weight_ref,
    conv_bias_ref,
    select_ref,
    mask_ref,
    cot_ref,
    other_cot_ref,
    convolved_ref,
    act_ref,
    selected_ref,
    whole_cot_ref,
    inner,
):
    rows = act_ref.shape[0]
    taps = conv_weight_ref.shape[0]
    inner[:halo, :] = inner_ref[rows:, :].astype(f32)
    inner[halo:, :] = inner_ref[:rows, :].astype(f32)
    total = conv_bias_ref[...] + conv_weight_ref[taps - 1 :, :] * inner[halo:, :]
    for lag in range(1, taps):
        earlier = inner[pl.ds(halo - lag, rows), :] * mask_ref[:, lag : lag + 1]
        total = total + conv_weight_ref[taps - 1 - lag : taps - lag, :] * earlier
    convolved_ref[...] = total
    act = (total * jax.nn.sigmoid(total)).astype(bf16)
    act_ref[...] = act
    part = lax.dot_general(select_ref[...], act, contract_last, preferred_element_type=f32)

    @pl.when(pl.program_id(0) == 0)
    def _():
        selected_ref[...] = part
        half = cot_ref.shape[1]
        right = lax.axis_index("narrow") == 1
        whole_cot_ref[:, :half] = jnp.where(right, other_cot_ref[...], cot_ref[...])
        whole_cot_ref[:, half:] = jnp.where(right, cot_ref[...], other_cot_ref[...])

    @pl.when(pl.program_id(0) > 0)
    def _():
        selected_ref[...] += part


def convolve(projected, conv_weight, conv_bias, select_weight, masks, cot, other_cot):
    parts, extended, width = projected.shape
    rows = extended - halo
    taps = conv_weight.shape[0]
    columns = select_weight.shape[0]
    return call(
        conv_kernel,
        "convolve",
        width,
        [
            part_spec(0, extended),
            column_spec(taps),
            column_spec(1),
            column_spec(columns),
            whole_spec(rows, masks.shape[1]),
            whole_spec(*cot.shape),
            whole_spec(*cot.shape),
        ],
        [
            column_spec(rows),
            column_spec(rows),
            whole_spec(columns, rows),
            whole_spec(rows, 2 * cot.shape[1]),
        ],
        [
            jax.ShapeDtypeStruct((rows, width), f32),
            jax.ShapeDtypeStruct((rows, width), bf16),
            jax.ShapeDtypeStruct((columns, rows), f32),
            jax.ShapeDtypeStruct((rows, 2 * cot.shape[1]), bf16),
        ],
        [pltpu.VMEM((extended, scan_width), f32)],
        projected,
        conv_weight,
        conv_bias,
        select_weight,
        masks,
        cot,
        other_cot,
    )


def coef_columns(coef, block):
    per_tile = lanes // body_rows
    start = pl.multiple_of((block // per_tile) * lanes, lanes)
    tile = coef[:, pl.ds(start, lanes)]
    back = body_rows * lax.rem(block, per_tile)
    return pltpu.roll(tile, lax.rem(lanes - back, lanes), 1)


def put_ends(ends_ref, state, adjoint, total):
    count, width = state.shape
    ends_ref[:count, :] = state.astype(bf16)
    ends_ref[count : 2 * count, :] = adjoint.astype(bf16)
    high = total.astype(bf16).astype(f32)
    upper = lax.broadcasted_iota(jnp.int32, (16, width), 0) < 8
    ends_ref[2 * count :, :] = jnp.where(upper, high, total - high).astype(bf16)


def get_ends(ends_ref, count):
    total = ends_ref[2 * count :].astype(f32)
    return (
        ends_ref[:count].astype(f32),
        ends_ref[count : 2 * count].astype(f32),
        total[:1] + total[8:9],
    )


def ends_kernel(
    selected_ref,
    other_ref,
    step_weight_ref,
    step_bias_ref,
    act_ref,
    gate_ref,
    gated_grad_ref,
    mask_ref,
    decay_log_ref,
    step_pre_ref,
    step_ref,
    ends_ref,
    coef,
    held_step,
    drive,
    scan_grad,
):
    rows = act_ref.shape[0]
    count = decay_log_ref.shape[0]
    rank = step_weight_ref.shape[0]
    decay2 = -jnp.exp(decay_log_ref[...]) * log2e
    selected = selected_ref[...] + other_ref[...]
    coef[...] = selected[rank:, :]
    step_low = selected[:rank, :].astype(bf16)
    step_pre = step_bias_ref[...] + lax.dot_general(
        step_low, step_weight_ref[...], contract_first, preferred_element_type=f32
    )
    step_pre_ref[...] = step_pre
    step = softplus(step_pre)
    step_ref[...] = step
    held_step[...] = jnp.where(mask_ref[:, 1:2] > 0.0, step, reset_step)
    drive[...] = step * act_ref[...].astype(f32)
    gate = gate_ref[...].astype(f32)
    scan_grad[...] = gated_grad_ref[...] * (gate * jax.nn.sigmoid(gate))
    zero = jnp.zeros(decay2.shape, f32)

    def body(block, carried):
        state, product, adjoint = carried
        columns = coef_columns(coef, block)
        for i in range(body_rows):
            row = pl.ds(block * body_rows + i, 1)
            factor = jnp.exp2(held_step[row, :] * decay2)
            state = factor * state + columns[:count, i : i + 1] * drive[row, :]
            product = factor * product
            adjoint = adjoint + product * (columns[count:, i : i + 1] * scan_grad[row, :])
        return state, product, adjoint

    state, product, adjoint = lax.fori_loop(0, rows // body_rows, body, (zero, zero + 1.0, zero))
    put_ends(ends_ref, state, adjoint, jnp.sum(held_step[...], axis=0, keepdims=True))


def scan_ends(
    selected, other, step_weight, step_bias, act, projected, gated_grad, masks, decay_log
):
    rows, width = act.shape
    count = decay_log.shape[0]
    columns = selected.shape[0]
    rank = step_weight.shape[0]
    return call(
        ends_kernel,
        "scan_ends",
        width,
        [
            whole_spec(columns, rows),
            whole_spec(columns, rows),
            column_spec(rank),
            column_spec(1),
            column_spec(rows),
            part_spec(1, rows),
            column_spec(rows),
            whole_spec(rows, masks.shape[1]),
            column_spec(count),
        ],
        [column_spec(rows), column_spec(rows), column_spec(2 * count + 16)],
        [
            jax.ShapeDtypeStruct((rows, width), f32),
            jax.ShapeDtypeStruct((rows, width), f32),
            jax.ShapeDtypeStruct((2 * count + 16, width), bf16),
        ],
        [pltpu.VMEM((2 * count, rows), f32)] + [pltpu.VMEM((rows, scan_width), f32)] * 3,
        selected,
        other,
        step_weight,
        step_bias,
        act,
        projected,
        gated_grad,
        masks,
        decay_log,
    )


def lane_tiles(values):
    return [values[:, k : k + lanes] for k in range(0, values.shape[1], lanes)]


def tree_sum(parts):
    while len(parts) > 1:
        odd = parts[len(parts) // 2 * 2 :]
        parts = [a + b for a, b in zip(parts[0::2], parts[1::2])] + odd
    return parts[0]


def keep_halves(scratch, i, values):
    for k, tile in enumerate(lane_tiles(values)):
        at = (k * body_rows + i) * 8
        scratch[at : at + 8, :] = tile[:8] + tile[8:]


def put_state_sums(scratch, out_ref, block):
    for group in range(body_rows // 8):
        row = pl.ds(pl.multiple_of(block * body_rows + group * 8, 8), 8)
        for k in range(out_ref.shape[1] // lanes):
            at = (k * body_rows + group * 8) * 8
            total = tree_sum([scratch[pl.ds(at + n, 8, stride=8), :] for n in range(8)])
            out_ref[row, k * lanes : (k + 1) * lanes] = total


def lane_sums(values):
    ones = jnp.ones((8, lanes), bf16)
    high = values.astype(bf16)
    low = (values - high.astype(f32)).astype(bf16)
    total = lax.dot_general(ones, high, contract_last, preferred_element_type=f32)
    total += lax.dot_general(ones, low, contract_last, preferred_element_type=f32)
    return total[:1, :]


def at_token(t, count):
    return pl.ds(pl.multiple_of(t * count, count), count)


def forward_kernel(
    selected_ref,
    other_ref,
    step_ref,
    act_ref,
    gate_ref,
    gated_grad_ref,
    mask_ref,
    decay_log_ref,
    passed_ref,
    entering_ref,
    skip_ref,
    cot_ref,
    normed_ref,
    gated_ref,
    gate_grad_ref,
    out_product_ref,
    gate_product_ref,
    entry_ref,
    coef,
    held_step,
    drive,
    scanned,
    halves,
):
    rows = step_ref.shape[0]
    count = decay_log_ref.shape[0]
    rank = selected_ref.shape[0] - 2 * count
    decay = -jnp.exp(decay_log_ref[...])
    decay2 = decay * log2e
    before_steps = passed_ref[2 * count : 2 * count + 1, :]
    entry = passed_ref[:count, :] + through(decay, before_steps) * entering_ref[...].astype(f32)
    entry_ref[...] = entry
    coef[...] = selected_ref[rank:, :] + other_ref[rank:, :]
    act = act_ref[...].astype(f32)
    held_step[...] = jnp.where(mask_ref[:, 1:2] > 0.0, step_ref[...], reset_step)
    drive[...] = step_ref[...] * act

    def forward(block, state):
        columns = coef_columns(coef, block)
        for i in range(body_rows):
            row = pl.ds(block * body_rows + i, 1)
            factor = jnp.exp2(held_step[row, :] * decay2)
            state = factor * state + columns[:count, i : i + 1] * drive[row, :]
            keep_halves(halves, i, columns[count:, i : i + 1] * state)
        put_state_sums(halves, scanned, block)
        return state

    lax.fori_loop(0, rows // body_rows, forward, entry)
    gate = gate_ref[...].astype(f32)
    logistic = jax.nn.sigmoid(gate)
    total = scanned[...] + skip_ref[...] * act
    gated = (total * (gate * logistic)).astype(bf16)
    gated_ref[...] = gated
    out_product_ref[...] = lax.dot_general(
        gated, cot_ref[...], contract_first, preferred_element_type=f32
    ).astype(bf16)
    slope = logistic * (1.0 + gate * (1.0 - logistic))
    gate_grad = (gated_grad_ref[...] * total * slope).astype(bf16)
    gate_grad_ref[...] = gate_grad
    gate_product_ref[...] = lax.dot_general(
        normed_ref[...], gate_grad, contract_first, preferred_element_type=f32
    ).astype(bf16)


def scan_forward(
    selected,
    other,
    step,
    act,
    projected,
    gated_grad,
    masks,
    decay_log,
    passed,
    entering,
    skip_gain,
    cot,
    normed,
):
    rows, width = step.shape
    count = decay_log.shape[0]
    columns = selected.shape[0]
    return call(
        forward_kernel,
        "scan_forward",
        width,
        [
            whole_spec(columns, rows),
            whole_spec(columns, rows),
            column_spec(rows),
            column_spec(rows),
            part_spec(1, rows),
            column_spec(rows),
            whole_spec(rows, masks.shape[1]),
            column_spec(count),
            column_spec(2 * count + 8),
            column_spec(count),
            column_spec(1),
            whole_spec(*cot.shape),
            whole_spec(*normed.shape),
        ],
        [
            column_spec(rows),
            column_spec(rows),
            pl.BlockSpec((scan_width, cot.shape[1]), lambda j: (j, 0)),
            column_spec(normed.shape[1]),
            column_spec(count),
        ],
        [
            jax.ShapeDtypeStruct((rows, width), bf16),
            jax.ShapeDtypeStruct((rows, width), bf16),
            jax.ShapeDtypeStruct((width, cot.shape[1]), bf16),
            jax.ShapeDtypeStruct((normed.shape[1], width), bf16),
            jax.ShapeDtypeStruct((count, width), f32),
        ],
        [pltpu.VMEM((2 * count, rows), f32)]
        + [pltpu.VMEM((rows, scan_width), f32)] * 3
        + [pltpu.VMEM((8 * body_rows * (scan_width // lanes), lanes), f32)],
        selected,
        other,
        step,
        act,
        projected,
        gated_grad,
        masks,
        decay_log,
        passed,
        entering,
        skip_gain,
        cot,
        normed,
    )


def backward_kernel(
    selected_ref,
    other_ref,
    step_pre_ref,
    step_ref,
    act_ref,
    gate_ref,
    gated_grad_ref,
    mask_ref,
    decay_log_ref,
    entry_ref,
    passed_ref,
    returning_ref,
    skip_ref,
    step_weight_ref,
    act_grad_ref,
    select_grad_ref,
    small_ref,
    coef,
    held_step,
    drive,
    scan_grad,
    weighted,
    held_sum,
    states,
    factors,
    halves,
    more_halves,
    in_sum,
    read_sum,
):
    rows = step_ref.shape[0]
    count = decay_log_ref.shape[0]
    rank = step_weight_ref.shape[0]
    blocks = rows // body_rows
    decay = -jnp.exp(decay_log_ref[...])
    decay2 = decay * log2e
    after_steps = passed_ref[2 * count + 1 : 2 * count + 2, :]
    tail = passed_ref[count : 2 * count, :] + through(decay, after_steps) * returning_ref[...].astype(f32)
    selected = selected_ref[...] + other_ref[...]
    coef[...] = selected[rank:, :]
    step_low = selected[:rank, :].astype(bf16)
    step = step_ref[...]
    act = act_ref[...].astype(f32)
    held_step[...] = jnp.where(mask_ref[:, 1:2] > 0.0, step, reset_step)
    drive[...] = step * act
    gate = gate_ref[...].astype(f32)
    grads = gated_grad_ref[...] * (gate * jax.nn.sigmoid(gate))
    scan_grad[...] = grads
    small_ref[rank + count : rank + count + 1, :] = jnp.sum(grads * act, axis=0, keepdims=True)
    states[:count, :] = entry_ref[...]

    @pl.when(pl.program_id(0) == 0)
    def _():
        in_sum[...] = jnp.zeros(in_sum.shape, f32)
        read_sum[...] = jnp.zeros(read_sum.shape, f32)
        select_grad_ref[...] = jnp.zeros(select_grad_ref.shape, f32)

    def forward(block, state):
        columns = coef_columns(coef, block)
        for i in range(body_rows):
            t = block * body_rows + i
            row = pl.ds(t, 1)
            factor = jnp.exp2(held_step[row, :] * decay2)
            state = factor * state + columns[:count, i : i + 1] * drive[row, :]
            factors[at_token(t, count), :] = factor
            states[at_token(t + 1, count), :] = state
        return state

    lax.fori_loop(0, blocks, forward, entry_ref[...])

    def backward(k, carried):
        adjoint, decay_grad = carried
        block = blocks - 1 - k
        columns = coef_columns(coef, block)
        for i in range(body_rows - 1, -1, -1):
            t = block * body_rows + i
            row = pl.ds(t, 1)
            here = at_token(t, count)
            grad = scan_grad[row, :]
            summed = columns[count:, i : i + 1] * grad + adjoint
            read_sum[here, :] += tree_sum(lane_tiles(grad * states[at_token(t + 1, count), :]))
            in_sum[here, :] += tree_sum(lane_tiles(summed * drive[row, :]))
            keep_halves(halves, i, summed * columns[:count, i : i + 1])
            adjoint = factors[here, :] * summed
            held = adjoint * states[here, :]
            decay_grad = decay_grad + held * step_ref[row, :]
            keep_halves(more_halves, i, held * decay)
        put_state_sums(halves, weighted, block)
        put_state_sums(more_halves, held_sum, block)
        return adjoint, decay_grad

    ignored, decay_grad = lax.fori_loop(
        0, blocks, backward, (tail, jnp.zeros(decay.shape, f32))
    )
    act_grad_ref[...] = step * weighted[...] + skip_ref[...] * scan_grad[...]
    step_grad = act * weighted[...] + held_sum[...]
    pre_grad = (step_grad * jax.nn.sigmoid(step_pre_ref[...])).astype(bf16)
    small_ref[:rank, :] = jnp.dot(step_low, pre_grad, preferred_element_type=f32)
    small_ref[rank : rank + count, :] = decay_grad * decay
    bias_grad = jnp.sum(pre_grad.astype(f32), axis=0, keepdims=True)
    small_ref[rank + count + 1 : rank + count + 2, :] = bias_grad
    select_grad_ref[:rank, :] += lax.dot_general(
        step_weight_ref[...], pre_grad, contract_last, preferred_element_type=f32
    )

    @pl.when(pl.program_id(0) == pl.num_programs(0) - 1)
    def _():
        for n in range(count):
            at = pl.ds(n, rows, stride=count)
            select_grad_ref[rank + n : rank + n + 1, :] = lane_sums(in_sum[at, :])
            select_grad_ref[rank + count + n : rank + count + n + 1, :] = lane_sums(read_sum[at, :])


def scan_backward(
    selected,
    other,
    step_pre,
    step,
    act,
    projected,
    gated_grad,
    masks,
    decay_log,
    entry,
    passed,
    returning,
    skip_gain,
    step_weight,
):
    rows, width = step.shape
    count = decay_log.shape[0]
    columns = selected.shape[0]
    rank = step_weight.shape[0]
    half_rows = 8 * body_rows * (scan_width // lanes)
    small = rank + count + 2
    return call(
        backward_kernel,
        "scan_backward",
        width,
        [
            whole_spec(columns, rows),
            whole_spec(columns, rows),
            column_spec(rows),
            column_spec(rows),
            column_spec(rows),
            part_spec(1, rows),
            column_spec(rows),
            whole_spec(rows, masks.shape[1]),
            column_spec(count),
            column_spec(count),
            column_spec(2 * count + 8),
            column_spec(count),
            column_spec(1),
            column_spec(rank),
        ],
        [column_spec(rows), whole_spec(columns, rows), column_spec(small)],
        [
            jax.ShapeDtypeStruct((rows, width), f32),
            jax.ShapeDtypeStruct((columns, rows), f32),
            jax.ShapeDtypeStruct((small, width), f32),
        ],
        [pltpu.VMEM((2 * count, rows), f32)]
        + [pltpu.VMEM((rows, scan_width), f32)] * 5
        + [
            pltpu.VMEM(((rows + 1) * count, scan_width), f32),
            pltpu.VMEM((rows * count, scan_width), f32),
            pltpu.VMEM((half_rows, lanes), f32),
            pltpu.VMEM((half_rows, lanes), f32),
            pltpu.VMEM((rows * count, lanes), f32),
            pltpu.VMEM((rows * count, lanes), f32),
        ],
        selected,
        other,
        step_pre,
        step,
        act,
        projected,
        gated_grad,
        masks,
        decay_log,
        entry,
        passed,
        returning,
        skip_gain,
        step_weight,
    )


def conv_grad_kernel(
    select_grad_ref,
    other_ref,
    select_ref,
    act_grad_ref,
    convolved_ref,
    act_ref,
    inner_ref,
    conv_weight_ref,
    mask_ref,
    *rest,
):
    inner_grad_ref, before_ref, last_ref, small_ref, inner, shifted = rest[-6:]
    rows = act_ref.shape[0]
    taps = conv_weight_ref.shape[0]
    columns = select_ref.shape[0]
    select_grad = (select_grad_ref[...] + other_ref[...]).astype(bf16)
    total = act_grad_ref[...] + lax.dot_general(
        select_grad, select_ref[...], contract_first, preferred_element_type=f32
    )
    conv_grad = total * silu_slope(convolved_ref[...])
    small_ref[:columns, :] = jnp.dot(select_grad, act_ref[...], preferred_element_type=f32)
    inner[:halo, :] = inner_ref[rows:, :].astype(f32)
    inner[halo:, :] = inner_ref[:rows, :].astype(f32)
    edges = jnp.zeros((8, conv_grad.shape[1]), f32)
    shifted[:8, :] = edges
    shifted[rows + 8 :, :] = edges
    out = conv_weight_ref[taps - 1 :, :] * conv_grad
    before = edges
    small_ref[columns + taps - 1 : columns + taps, :] = jnp.sum(
        conv_grad * inner[halo:, :], axis=0, keepdims=True
    )
    for lag in range(1, taps):
        masked = conv_grad * mask_ref[:, lag : lag + 1]
        at = taps - 1 - lag
        small_ref[columns + at : columns + at + 1, :] = jnp.sum(
            masked * inner[pl.ds(halo - lag, rows), :], axis=0, keepdims=True
        )
        shifted[8 : rows + 8, :] = masked
        weight = conv_weight_ref[at : at + 1, :]
        out = out + weight * shifted[pl.ds(8 + lag, rows), :]
        before = before + weight * shifted[pl.ds(lag, 8), :]
    small_ref[columns + taps : columns + taps + 1, :] = jnp.sum(conv_grad, axis=0, keepdims=True)
    inner_grad_ref[...] = out.astype(bf16)
    before_ref[...] = before
    last_ref[...] = out[rows - 8 :, :]


def convolve_grad(
    select_grad, other, select_weight, act_grad, convolved, act, projected, conv_weight, masks, waits
):
    rows, width = act.shape
    extended = rows + halo
    columns = select_weight.shape[0]
    taps = conv_weight.shape[0]
    small = columns + taps + 1
    return call(
        conv_grad_kernel,
        "convolve_grad",
        width,
        [
            whole_spec(columns, rows),
            whole_spec(columns, rows),
            column_spec(columns),
            column_spec(rows),
            column_spec(rows),
            column_spec(rows),
            part_spec(0, extended),
            column_spec(taps),
            whole_spec(rows, masks.shape[1]),
        ]
        + [pl.BlockSpec(memory_space=pl.ANY)] * len(waits),
        [column_spec(rows), column_spec(8), column_spec(8), column_spec(small)],
        [
            jax.ShapeDtypeStruct((rows, width), bf16),
            jax.ShapeDtypeStruct((8, width), f32),
            jax.ShapeDtypeStruct((8, width), f32),
            jax.ShapeDtypeStruct((small, width), f32),
        ],
        [pltpu.VMEM((extended, scan_width), f32), pltpu.VMEM((rows + 16, scan_width), f32)],
        select_grad,
        other,
        select_weight,
        act_grad,
        convolved,
        act,
        projected,
        conv_weight,
        masks,
        *waits,
    )


def normalize_kernel(
    own_ref,
    other_ref,
    edge_ref,
    other_edge_ref,
    gain_ref,
    ids_ref,
    whole_ref,
    extended_ref,
    normed_ref,
    inverse_ref,
    mask_ref,
    rows_ref,
):
    rows, half = own_ref.shape
    ids = ids_ref[...].astype(f32)
    place = lax.broadcasted_iota(jnp.int32, ids.shape, 1)
    same = []
    for lag in range(8):
        earlier = jnp.where(place < lag, ids[:, :1], pltpu.roll(ids, lag, 1)) if lag else ids
        same.append(jnp.where(earlier == ids, 1.0, 0.0))
    spare = jnp.zeros((lanes - 8, rows), f32)
    mask_ref[...] = jnp.concatenate(same + [spare]).T
    right = lax.axis_index("narrow") == 1
    for at, own, other in ((0, own_ref, other_ref), (rows, edge_ref, other_edge_ref)):
        end = at + own.shape[0]
        rows_ref[at:end, :half] = jnp.where(right, other[...], own[...])
        rows_ref[at:end, half:] = jnp.where(right, own[...], other[...])
    whole_ref[...] = rows_ref[:rows, :]
    whole = rows_ref[...].astype(f32)
    inverse = lax.rsqrt(jnp.mean(whole * whole, axis=1, keepdims=True) + epsilon)
    normed = (whole * inverse * gain_ref[...]).astype(bf16)
    extended_ref[...] = normed
    normed_ref[...] = normed[:rows]
    inverse_ref[...] = inverse[:rows]


def normalized(own, other, edge, other_edge, gain, ids):
    rows, half = own.shape
    extended = rows + edge.shape[0]
    return pl.pallas_call(
        normalize_kernel,
        out_shape=[
            jax.ShapeDtypeStruct((rows, 2 * half), bf16),
            jax.ShapeDtypeStruct((extended, 2 * half), bf16),
            jax.ShapeDtypeStruct((rows, 2 * half), bf16),
            jax.ShapeDtypeStruct((rows, 1), f32),
            jax.ShapeDtypeStruct((rows, lanes), f32),
        ],
        scratch_shapes=[pltpu.VMEM((extended, 2 * half), bf16)],
        cost_estimate=tiny_cost,
        name="normalized",
    )(own, other, edge, other_edge, gain, ids)


def after(array, *waits):
    anywhere = pl.BlockSpec(memory_space=pl.ANY)
    return pl.pallas_call(
        lambda *refs: None,
        in_specs=[anywhere] * (1 + len(waits)),
        out_specs=anywhere,
        out_shape=jax.ShapeDtypeStruct(array.shape, array.dtype),
        input_output_aliases={0: 0},
        cost_estimate=tiny_cost,
        name="after",
    )(array, *waits)


def patch_kernel(ids_ref, rows_ref, last_ref, next_ref, *rest):
    count = ids_ref.shape[0]
    place = lax.broadcasted_iota(jnp.int32, (8, 1), 0)
    same = jnp.zeros((8, 1), f32)
    for lag in range(8):
        here = jnp.where(ids_ref[count - 1 - lag] == ids_ref[count - 1], 1.0, 0.0)
        same = same + jnp.where(place == 7 - lag, here, 0.0)
    total = last_ref[...] + next_ref[...] * same
    rows = rows_ref[...].astype(f32)
    rest[-1][...] = jnp.concatenate([rows[: halo - 8], total]).astype(bf16)


def patched(ids, grads, last, following, *waits):
    rows, width = grads.shape
    block = pl.BlockSpec((halo, width), lambda j: (rows // halo - 1, 0))
    edge = pl.BlockSpec((8, width), lambda j: (0, 0))
    return pl.pallas_call(
        patch_kernel,
        grid=(1,),
        in_specs=[pl.BlockSpec(memory_space=pltpu.SMEM), block, edge, edge]
        + [pl.BlockSpec(memory_space=pl.ANY)] * len(waits),
        out_specs=block,
        out_shape=jax.ShapeDtypeStruct((rows, width), bf16),
        input_output_aliases={1: 0},
        cost_estimate=tiny_cost,
        name="patched",
    )(ids, grads, last, following, *waits)


def edge_kernel(ids_ref, tokens_ref, out_ref):
    rows = ids_ref.shape[0]
    taps = 4
    out_ref[...] = tokens_ref[...]
    place = lax.broadcasted_iota(jnp.int32, (halo, 1), 0)
    same = jnp.zeros((halo, 1), f32)
    for lag in range(taps):
        here = jnp.where(ids_ref[rows - 1 - lag] == ids_ref[rows - 1], 1.0, 0.0)
        same = same + jnp.where(place == halo - 1 - lag, here, 0.0)
    out_ref[...] = (tokens_ref[...].astype(f32) * same).astype(bf16)


def edge_rows_of(ids, tokens):
    rows, width = tokens.shape
    return pl.pallas_call(
        edge_kernel,
        grid=(1,),
        in_specs=[
            pl.BlockSpec(memory_space=pltpu.SMEM),
            pl.BlockSpec((halo, width), lambda j: (rows // halo - 1, 0)),
        ],
        out_specs=pl.BlockSpec((halo, width), lambda j: (0, 0)),
        out_shape=jax.ShapeDtypeStruct((halo, width), bf16),
        cost_estimate=tiny_cost,
        name="edge_rows",
    )(ids, tokens)


block_rows, used_rows = 16, 12


def small_kernel(core_ref, scan_ref, conv_ref, wait_ref, keep_ref, send_ref, rows, blocks):
    rows[...] = jnp.zeros(rows.shape, f32)
    rows[: scan_ref.shape[0], :] = scan_ref[...]
    rows[scan_ref.shape[0] : scan_ref.shape[0] + conv_ref.shape[0], :] = conv_ref[...]
    blocks[...] = jnp.zeros(blocks.shape, f32)
    for n in range(16):
        blocks[n * block_rows : n * block_rows + used_rows, :] = rows[
            n * used_rows : (n + 1) * used_rows, :
        ]
    half = keep_ref.shape[0]
    mine = pl.ds(pl.multiple_of(core_ref[0] * half, half), half)
    other = pl.ds(pl.multiple_of((1 - core_ref[0]) * half, half), half)
    keep_ref[...] = blocks[mine, :]
    send_ref[...] = blocks[other, :].astype(bf16)


def small_halves(core, scan_small, conv_small, wait):
    width = scan_small.shape[1]
    return pl.pallas_call(
        small_kernel,
        in_specs=[pl.BlockSpec(memory_space=pltpu.SMEM)]
        + [pl.BlockSpec(memory_space=pltpu.VMEM)] * 2
        + [pl.BlockSpec(memory_space=pl.ANY)],
        out_shape=[jax.ShapeDtypeStruct((8 * block_rows, width), kind) for kind in (f32, bf16)],
        scratch_shapes=[
            pltpu.VMEM((16 * used_rows, width), f32),
            pltpu.VMEM((16 * block_rows, width), f32),
        ],
        cost_estimate=tiny_cost,
        name="small_halves",
    )(core, scan_small, conv_small, wait)


def fold_kernel(upper_ref, keep_ref, arrived_ref, out_ref, send_ref):
    size = out_ref.shape[0]
    mine = pl.ds(pl.multiple_of(upper_ref[0] * size, size), size)
    other = pl.ds(pl.multiple_of((1 - upper_ref[0]) * size, size), size)
    out_ref[...] = keep_ref[mine, :] + arrived_ref[mine, :].astype(f32)
    send_ref[...] = (keep_ref[other, :] + arrived_ref[other, :].astype(f32)).astype(bf16)


def folded(upper, keep, arrived):
    rows, width = keep.shape
    return pl.pallas_call(
        fold_kernel,
        in_specs=[pl.BlockSpec(memory_space=pltpu.SMEM)]
        + [pl.BlockSpec(memory_space=pltpu.VMEM)] * 2,
        out_shape=[jax.ShapeDtypeStruct((rows // 2, width), kind) for kind in (f32, bf16)],
        cost_estimate=tiny_cost,
        name="folded",
    )(upper, keep, arrived)


def quarter_kernel(
    place_ref,
    own_ref,
    near_ref,
    far_ref,
    normed_0,
    normed_1,
    normed_2,
    normed_3,
    small_ref,
    arrived_ref,
    *rest,
):
    keep_ref, *sends_refs, piece, small = rest[-6:]
    total = None
    tokens = own_ref.shape[0]
    grads = (own_ref[...], near_ref[...], far_ref[:tokens, :], far_ref[tokens:, :])
    for left, right in zip((normed_0, normed_1, normed_2, normed_3), grads):
        part = lax.dot_general(left[...], right, contract_first, preferred_element_type=f32)
        total = part if total is None else total + part
    piece[...] = total
    small[...] = small_ref[...] + arrived_ref[...].astype(f32)
    rows, spare = piece.shape[0] // 4, small.shape[0] // 4
    for n in range(4):
        block = place_ref[0] ^ n
        inner_rows = piece[pl.ds(pl.multiple_of(block * rows, rows), rows), :]
        small_rows = small[pl.ds(pl.multiple_of(block * spare, spare), spare), :]
        if n == 0:
            keep_ref[:rows, :] = inner_rows
            keep_ref[rows:, :] = small_rows
        else:
            sends_refs[n - 1][:rows, :] = inner_rows.astype(bf16)
            sends_refs[n - 1][rows:, :] = small_rows.astype(bf16)


def inner_quarter(place, own, near, far, normed, smalls, waits):
    width = own.shape[1]
    quarter = normed[0].shape[1]
    spare = smalls[0].shape[0]
    rows = (quarter + spare) // 4
    return pl.pallas_call(
        quarter_kernel,
        in_specs=[pl.BlockSpec(memory_space=pltpu.SMEM)]
        + [pl.BlockSpec(memory_space=pltpu.VMEM)] * 9
        + [pl.BlockSpec(memory_space=pl.ANY)] * len(waits),
        out_shape=[jax.ShapeDtypeStruct((rows, width), f32)]
        + [jax.ShapeDtypeStruct((rows, width), bf16)] * 3,
        scratch_shapes=[pltpu.VMEM((quarter, width), f32), pltpu.VMEM((spare, width), f32)],
        compiler_params=pltpu.CompilerParams(vmem_limit_bytes=vmem_bytes),
        cost_estimate=tiny_cost,
        name="inner_quarter",
    )(place, own, near, far, *normed, *smalls, *waits)


def put_quarter(out_ref, gate_ref, inner_ref):
    rows = out_ref.shape[0] // 4
    out_ref[:, 1, :] = gate_ref[...].astype(f32)
    for n in range(4):
        at = n * (rows + block_rows)
        out_ref[n * rows : (n + 1) * rows, 0, :] = inner_ref[at : at + rows, :].astype(f32)


def join_kernel(place_ref, gate_ref, low_ref, *rest, small_rows):
    held = rest[:4]
    out_ref, wide_ref, *row_refs, gain_ref, blocks = rest[4:]
    wide_ref[...] = low_ref[...].astype(f32)
    rows = out_ref.shape[0] // 4
    for flip, ref in enumerate(held):

        @pl.when(pl.program_id(0) == flip)
        def _():
            put_quarter(out_ref, gate_ref, ref)
            number = place_ref[0] ^ flip
            number = (number & 1) * 2 + number // 2
            for n in range(4):
                at = (number * 4 + n) * block_rows
                taken = ref[(n + 1) * rows + n * block_rows : (n + 1) * (rows + block_rows), :]
                blocks[pl.ds(pl.multiple_of(at, block_rows), block_rows), :] = taken.astype(f32)

    @pl.when(pl.program_id(0) == 3)
    def _():
        for ref, start in zip(row_refs, small_rows):
            for row in range(ref.shape[0]):
                at = (start + row) // used_rows * block_rows + (start + row) % used_rows
                ref[row : row + 1, :] = blocks[at : at + 1, :]
        gain_ref[...] = sum(
            blocks[n * block_rows + used_rows : n * block_rows + used_rows + 1, :] for n in range(16)
        )


def joined(place, gate, low, held, small_rows, small_counts):
    depth, width = gate.shape
    quarter = depth // 4
    whole = pl.BlockSpec(held[0].shape, lambda j, place: (0, 0))
    part = pl.BlockSpec((quarter, width), lambda j, place: (j, 0))
    return pl.pallas_call(
        functools.partial(join_kernel, small_rows=small_rows),
        grid_spec=pltpu.PrefetchScalarGridSpec(
            num_scalar_prefetch=1,
            grid=(4,),
            in_specs=[pl.BlockSpec((quarter, width), lambda j, place: (place[0] ^ j, 0)), part]
            + [whole] * 4,
            out_specs=[
                pl.BlockSpec((quarter, 2, width), lambda j, place: (place[0] ^ j, 0, 0)),
                part,
            ]
            + [pl.BlockSpec((rows, width), lambda j, place: (0, 0)) for rows in small_counts],
            scratch_shapes=[pltpu.VMEM((16 * block_rows, width), f32)],
        ),
        out_shape=[
            jax.ShapeDtypeStruct((depth, 2, width), f32),
            jax.ShapeDtypeStruct(low.shape, f32),
        ]
        + [jax.ShapeDtypeStruct((rows, width), f32) for rows in small_counts],
        compiler_params=pltpu.CompilerParams(vmem_limit_bytes=vmem_bytes),
        cost_estimate=tiny_cost,
        name="joined",
    )(place, gate, low, *held)


def through(decay, total):
    return jnp.exp(decay * total)


def round_kernel(second_ref, decay_log_ref, own_ref, other_ref, *rest, first):
    count, width = decay_log_ref.shape
    new_passed_ref, *ends_refs = rest if first else rest[1:]
    decay = -jnp.exp(decay_log_ref[...])
    second = second_ref[0] > 0
    own, other = get_ends(own_ref, count), get_ends(other_ref, count)
    early = [jnp.where(second, b, a) for a, b in zip(own, other)]
    late = [jnp.where(second, a, b) for a, b in zip(own, other)]
    state = late[0] + through(decay, late[2]) * early[0]
    adjoint = early[1] + through(decay, early[2]) * late[1]
    if len(ends_refs) == 2:
        ends_refs[0][...] = state.astype(bf16)
        ends_refs[1][...] = adjoint.astype(bf16)
    else:
        put_ends(ends_refs[0], state, adjoint, early[2] + late[2])
    if first:
        before = after = jnp.zeros((count, width), f32)
        before_steps = after_steps = jnp.zeros((1, width), f32)
    else:
        before, after = rest[0][:count], rest[0][count : 2 * count]
        before_steps = rest[0][2 * count : 2 * count + 1]
        after_steps = rest[0][2 * count + 1 : 2 * count + 2]
    new_passed_ref[:count, :] = before + jnp.where(second, through(decay, before_steps) * other[0], 0.0)
    new_passed_ref[count : 2 * count, :] = after + jnp.where(
        second, 0.0, through(decay, after_steps) * other[1]
    )
    new_passed_ref[2 * count : 2 * count + 1, :] = before_steps + jnp.where(second, other[2], 0.0)
    new_passed_ref[2 * count + 1 : 2 * count + 2, :] = after_steps + jnp.where(second, 0.0, other[2])


def carried(ends, decay_log):
    count, width = decay_log.shape
    place = lax.axis_index("wide").astype(jnp.int32)
    state = jax.ShapeDtypeStruct((count, width), bf16)
    passed_kind = jax.ShapeDtypeStruct((2 * count + 8, width), f32)
    packed, passed = ends, []
    vmem = pl.BlockSpec(memory_space=pltpu.VMEM)
    for k, kinds in enumerate(([jax.ShapeDtypeStruct(ends.shape, bf16)], [state, state])):
        new_passed, *out = pl.pallas_call(
            functools.partial(round_kernel, first=k == 0),
            in_specs=[pl.BlockSpec(memory_space=pltpu.SMEM)] + [vmem] * (3 + k),
            out_shape=[passed_kind] + kinds,
            cost_estimate=tiny_cost,
            name="carry_round",
        )((place >> k & 1)[None], decay_log, packed, swapped(packed, "wide", 2**k), *passed)
        packed, passed = out[0], [new_passed]
    from_before = passed_along(out[0], "wide", 4)
    from_after = passed_along(out[1], "wide", -4)
    return passed[0], from_before, from_after


def local(
    tokens,
    norm_gain,
    in_weight,
    conv_weight,
    conv_bias,
    select_weight,
    step_weight,
    step_bias,
    decay_log,
    skip_gain,
    out_weight,
    segment_ids,
    cotangent,
):
    rows, features = tokens.shape
    taps = conv_weight.shape[0]
    columns = select_weight.shape[0]
    rank = step_weight.shape[0]
    count = decay_log.shape[0]
    right_half = lax.axis_index("narrow") == 1

    other_tokens = swapped(tokens, "narrow", 1)
    other_cot = swapped(cotangent, "narrow", 1)
    edge, other_edge = to_next_both(edge_rows_of(segment_ids, tokens))

    whole_low, normed_ext, normed, inverse, masks = normalized(
        tokens, other_tokens, edge, other_edge, norm_gain[None], segment_ids[None]
    )
    projected = jnp.einsum(
        "td,dce->cte", normed_ext, in_weight, preferred_element_type=f32
    ).astype(bf16)
    convolved, act, selected, cot_whole = convolve(
        projected, conv_weight, conv_bias[None], select_weight, masks, cotangent, other_cot
    )
    other_selected = swapped(selected, "narrow", 1)
    gated_grad = lax.dot_general(
        cot_whole, out_weight, contract_last, preferred_element_type=f32
    )
    step_pre, step, ends = scan_ends(
        selected,
        other_selected,
        step_weight,
        step_bias[None],
        act,
        projected,
        gated_grad,
        masks,
        decay_log,
    )
    passed, entering, returning = carried(ends, decay_log)
    gated, gate_grad, out_product, gate_product, entry = scan_forward(
        selected,
        other_selected,
        step,
        act,
        projected,
        gated_grad,
        masks,
        decay_log,
        passed,
        entering,
        skip_gain[None],
        cot_whole,
        normed,
    )
    products = (after(out_product, returning), gate_product)
    out_sum, gate_sum = lax.psum(products, "wide")
    wide_place = lax.axis_index("wide").astype(jnp.int32)
    four_place = (wide_place & 3)[None]

    def narrow_halves(array):
        low, high = array[:, :features], array[:, features:]
        return jnp.where(right_half, high, low), jnp.where(right_half, low, high)

    def after_forward(products):
        whole = whole_low.astype(f32)
        act_grad, select_grad, scan_small = scan_backward(
            selected,
            other_selected,
            step_pre,
            step,
            act,
            projected,
            gated_grad,
            masks,
            decay_log,
            entry,
            passed,
            returning,
            skip_gain[None],
            step_weight,
        )
        normed_four = quarter_of_four(after(normed, select_grad))
        inner_main, before, last, conv_small = convolve_grad(
            select_grad,
            swapped(select_grad, "narrow", 1),
            select_weight,
            act_grad,
            convolved,
            act,
            projected,
            conv_weight,
            masks,
            [],
        )
        following = passed_along(before, "wide", -1)
        inner_grad = patched(segment_ids, inner_main, last, following, *normed_four)
        near = swapped(inner_grad, "wide", 2)
        keep, send = small_halves(wide_place[None] & 1, scan_small, conv_small, inner_grad)
        keep, send = folded((wide_place >> 1 & 1)[None], keep, swapped(send, "wide", 1))
        smalls = [keep, swapped(send, "wide", 2)]
        normed_part = jnp.einsum(
            "cte,dce->td", jnp.stack([inner_grad, gate_grad]), in_weight, preferred_element_type=f32
        )
        inverse_then = after(inverse, send)
        gain_part = jnp.sum(normed_part * whole * inverse_then, axis=0, keepdims=True)
        row_part = jnp.sum(normed_part * norm_gain * whole, axis=1)[None]
        first_bits, *more_bits = group_bits(2)
        gain_sum = gain_part + swapped(gain_part, "narrow", 1)
        for bit in (bit for bits in more_bits for bit in bits):
            gain_sum = gain_sum + swapped(gain_sum, "wide", bit)
        row_theirs = swapped(row_part, "narrow", 1)
        near = after(near, gain_part, smalls[1])
        far = swapped(jnp.concatenate([inner_grad, near]), "wide", 1)
        keep, *sends = inner_quarter(
            (wide_place >> 2 & 3)[None],
            inner_grad,
            near,
            far,
            normed_four,
            smalls,
            [],
        )
        normed_mine, normed_other = narrow_halves(normed_part)
        normed_theirs = swapped(after(normed_other, keep), "narrow", 1)
        out_part = jnp.dot(after(gated, keep), out_weight, preferred_element_type=f32)
        out_mine, out_other = narrow_halves(out_part)
        out_theirs = swapped(out_other, "narrow", 1)
        layer_out = (tokens.astype(f32) + (out_mine + out_theirs)).astype(bf16)
        row_sum = (row_part + row_theirs).reshape(rows, 1)
        gain_mine = jnp.where(right_half, norm_gain[features:], norm_gain[:features])
        whole_grad = inverse * (gain_mine * (normed_mine + normed_theirs)) - tokens.astype(f32) * (
            inverse * inverse * inverse
        ) * (row_sum / (2 * features))
        tokens_grad = (whole_grad + cotangent.astype(f32)).astype(bf16)
        held = keep
        for n, flip in enumerate(flips(first_bits)[1:]):
            held = held + swapped(sends[n], "wide", flip).astype(f32)
        for bits in more_bits:
            held = scattered(held, bits)
        held = held.astype(bf16)
        for bits in reversed(more_bits):
            held = gathered(held, bits)
        spare = jnp.broadcast_to(gain_sum, (block_rows - used_rows, gain_sum.shape[1]))
        held = jnp.concatenate([held[: held.shape[0] - spare.shape[0]], spare.astype(bf16)])
        held = gathered(held, first_bits)
        return held, layer_out, tokens_grad

    kinds = jax.eval_shape(after_forward, products)
    held, layer_out, tokens_grad = lax.cond(
        wide_place >= 0,
        after_forward,
        lambda pair: jax.tree.map(lambda kind: jnp.zeros(kind.shape, kind.dtype), kinds),
        products,
    )

    core = swapped(held, "wide", 1)
    near = swapped(held, "wide", 2)
    far = swapped(near, "wide", 1)
    conv_at = rank + count + 2
    (
        in_weight_grad,
        out_weight_grad,
        step_weight_grad,
        decay_log_grad,
        skip_gain_grad,
        step_bias_grad,
        select_weight_grad,
        conv_weight_grad,
        conv_bias_grad,
        norm_gain_grad,
    ) = joined(
        four_place,
        gate_sum,
        out_sum,
        (held, core, near, far),
        (0, rank, rank + count, rank + count + 1, conv_at, conv_at + columns, conv_at + columns + taps),
        (rank, count, 1, 1, columns, taps, 1, 1),
    )
    return (
        layer_out,
        tokens_grad,
        norm_gain_grad[0],
        in_weight_grad,
        conv_weight_grad,
        conv_bias_grad[0],
        select_weight_grad,
        step_weight_grad,
        step_bias_grad[0],
        decay_log_grad,
        skip_gain_grad[0],
        out_weight_grad,
    )


def solution(mesh):
    placed = (
        P("wide", "narrow"),
        P(),
        P(None, None, "narrow"),
        P(None, "narrow"),
        P("narrow"),
        P(None, "narrow"),
        P(None, "narrow"),
        P("narrow"),
        P(None, "narrow"),
        P("narrow"),
        P("narrow", None),
        P("wide"),
        P("wide", "narrow"),
    )
    return jax.shard_map(
        local,
        mesh=mesh,
        in_specs=placed,
        out_specs=(
            P("wide", "narrow"),
            P("wide", "narrow"),
            P(),
            P(None, None, "narrow"),
            P(None, "narrow"),
            P("narrow"),
            P(None, "narrow"),
            P(None, "narrow"),
            P("narrow"),
            P(None, "narrow"),
            P("narrow"),
            P("narrow", None),
        ),
        check_vma=False,
    )
```

```python
import functools

import jax
import jax.numpy as jnp
from jax import lax
from jax.experimental import pallas as pl
from jax.experimental.pallas import tpu as pltpu
from jax.sharding import PartitionSpec as P

epsilon = 1e-05
log2e = 1.4426950408889634
reset_step = 1e30
lanes = 128
halo = 16
body_rows = 32
scan_width = 512
vmem_bytes = 56 * 1024 * 1024
tiny_cost = pl.CostEstimate(flops=1, bytes_accessed=1, transcendentals=0)
f32 = jnp.float32
bf16 = jnp.bfloat16
contract_first = (((0,), (0,)), ((), ()))
contract_last = (((1,), (1,)), ((), ()))


def passed_along(array, axis, by):
    peers = lax.axis_size(axis)
    pairs = [(i, i + by) for i in range(peers) if 0 <= i + by < peers]
    return lax.ppermute(array, axis, pairs)


def swapped(array, axis, bit):
    peers = lax.axis_size(axis)
    return lax.ppermute(array, axis, [(i, i ^ bit) for i in range(peers)])


def wide_bits():
    bit, bits = 1, []
    while bit < lax.axis_size("wide"):
        bits.append(bit)
        bit *= 2
    return bits


def to_next_both(array):
    count, sides = lax.axis_size("wide"), lax.axis_size("narrow")
    pairs = [
        (i * sides + k, (i + 1) * sides + (sides - 1 - k))
        for i in range(count - 1)
        for k in range(sides)
    ]
    return passed_along(array, "wide", 1), lax.ppermute(array, ("wide", "narrow"), pairs)


def is_upper(bit):
    return (lax.axis_index("wide") & bit) != 0


def group_bits(size):
    bits, bit = [], 4
    while bit < lax.axis_size("wide"):
        bits.append(bit)
        bit *= 2
    return [tuple(bits[k : k + size]) for k in range(0, len(bits), size)]


def flips(bits):
    return [sum(b for k, b in enumerate(bits) if n >> k & 1) for n in range(2 ** len(bits))]


def scattered(piece, bits):
    rows = piece.shape[0] // 2 ** len(bits)
    here = sum(is_upper(b).astype(jnp.int32) << k for k, b in enumerate(bits))

    def block(n):
        return lax.dynamic_slice_in_dim(piece, (here ^ n) * rows, rows, 0)

    total = block(0).astype(f32)
    for n, flip in enumerate(flips(bits)):
        if n > 0:
            total = total + swapped(block(n).astype(bf16), "wide", flip).astype(f32)
    return total


def gathered(held, bits):
    blocks = [held] + [swapped(held, "wide", flip) for flip in flips(bits)[1:]]
    for bit in bits:
        upper = is_upper(bit)
        blocks = [
            jnp.concatenate([jnp.where(upper, b, a), jnp.where(upper, a, b)])
            for a, b in zip(blocks[0::2], blocks[1::2])
        ]
    return blocks[0]


def core_columns(rows):
    width = rows.shape[1] // 2
    upper = is_upper(1).astype(jnp.int32)
    return (
        lax.dynamic_slice_in_dim(rows, upper * width, width, 1),
        lax.dynamic_slice_in_dim(rows, (1 - upper) * width, width, 1),
    )


def silu_slope(values):
    logistic = jax.nn.sigmoid(values)
    return logistic * (1.0 + values * (1.0 - logistic))


def softplus(values):
    return jnp.maximum(values, 0.0) + jnp.log1p(jnp.exp(-jnp.abs(values)))


def column_spec(rows, start=0):
    return pl.BlockSpec((rows, scan_width), lambda j: (0, start + j))


def part_spec(part, rows, start=0):
    return pl.BlockSpec((None, rows, scan_width), lambda j: (part, 0, start + j))


def whole_spec(rows, width):
    return pl.BlockSpec((rows, width), lambda j: (0, 0))


def call(kernel, name, width, in_specs, out_specs, out_shape, scratch, *operands):
    return pl.pallas_call(
        kernel,
        grid=(width // scan_width,),
        in_specs=in_specs,
        out_specs=out_specs,
        out_shape=out_shape,
        scratch_shapes=scratch,
        compiler_params=pltpu.CompilerParams(vmem_limit_bytes=vmem_bytes),
        cost_estimate=tiny_cost,
        name=name,
    )(*operands)


def conv_kernel(
    inner_ref,
    conv_weight_ref,
    conv_bias_ref,
    select_ref,
    mask_ref,
    convolved_ref,
    act_ref,
    selected_ref,
    inner,
):
    rows = act_ref.shape[0]
    taps = conv_weight_ref.shape[0]
    inner[:halo, :] = inner_ref[rows:, :].astype(f32)
    inner[halo:, :] = inner_ref[:rows, :].astype(f32)
    total = conv_bias_ref[...] + conv_weight_ref[taps - 1 :, :] * inner[halo:, :]
    for lag in range(1, taps):
        earlier = inner[pl.ds(halo - lag, rows), :] * mask_ref[:, lag : lag + 1]
        total = total + conv_weight_ref[taps - 1 - lag : taps - lag, :] * earlier
    convolved_ref[...] = total
    act = (total * jax.nn.sigmoid(total)).astype(bf16)
    act_ref[...] = act
    part = lax.dot_general(select_ref[...], act, contract_last, preferred_element_type=f32)

    @pl.when(pl.program_id(0) == 0)
    def _():
        selected_ref[...] = part

    @pl.when(pl.program_id(0) > 0)
    def _():
        selected_ref[...] += part


def convolve(projected, conv_weight, conv_bias, select_weight, masks):
    parts, extended, width = projected.shape
    rows = extended - halo
    taps = conv_weight.shape[0]
    columns = select_weight.shape[0]
    return call(
        conv_kernel,
        "convolve",
        width,
        [
            part_spec(0, extended),
            column_spec(taps),
            column_spec(1),
            column_spec(columns),
            whole_spec(rows, masks.shape[1]),
        ],
        [column_spec(rows), column_spec(rows), whole_spec(columns, rows)],
        [
            jax.ShapeDtypeStruct((rows, width), f32),
            jax.ShapeDtypeStruct((rows, width), bf16),
            jax.ShapeDtypeStruct((columns, rows), f32),
        ],
        [pltpu.VMEM((extended, scan_width), f32)],
        projected,
        conv_weight,
        conv_bias,
        select_weight,
        masks,
    )


def coef_columns(coef, block):
    per_tile = lanes // body_rows
    start = pl.multiple_of((block // per_tile) * lanes, lanes)
    tile = coef[:, pl.ds(start, lanes)]
    back = body_rows * lax.rem(block, per_tile)
    return pltpu.roll(tile, lax.rem(lanes - back, lanes), 1)


def put_ends(ends_ref, state, adjoint, total):
    count, width = state.shape
    ends_ref[:count, :] = state.astype(bf16)
    ends_ref[count : 2 * count, :] = adjoint.astype(bf16)
    high = total.astype(bf16).astype(f32)
    upper = lax.broadcasted_iota(jnp.int32, (16, width), 0) < 8
    ends_ref[2 * count :, :] = jnp.where(upper, high, total - high).astype(bf16)


def get_ends(ends_ref, count):
    total = ends_ref[2 * count :].astype(f32)
    return (
        ends_ref[:count].astype(f32),
        ends_ref[count : 2 * count].astype(f32),
        total[:1] + total[8:9],
    )


def ends_kernel(
    selected_ref,
    other_ref,
    step_weight_ref,
    step_bias_ref,
    act_ref,
    gate_ref,
    gated_grad_ref,
    mask_ref,
    decay_log_ref,
    step_pre_ref,
    step_ref,
    ends_ref,
    coef,
    held_step,
    drive,
    scan_grad,
):
    rows = act_ref.shape[0]
    count = decay_log_ref.shape[0]
    rank = step_weight_ref.shape[0]
    decay2 = -jnp.exp(decay_log_ref[...]) * log2e
    selected = selected_ref[...] + other_ref[...]
    coef[...] = selected[rank:, :]
    step_low = selected[:rank, :].astype(bf16)
    step_pre = step_bias_ref[...] + lax.dot_general(
        step_low, step_weight_ref[...], contract_first, preferred_element_type=f32
    )
    step_pre_ref[...] = step_pre
    step = softplus(step_pre)
    step_ref[...] = step
    held_step[...] = jnp.where(mask_ref[:, 1:2] > 0.0, step, reset_step)
    drive[...] = step * act_ref[...].astype(f32)
    gate = gate_ref[...].astype(f32)
    scan_grad[...] = gated_grad_ref[...] * (gate * jax.nn.sigmoid(gate))
    zero = jnp.zeros(decay2.shape, f32)

    def body(block, carried):
        state, product, adjoint = carried
        columns = coef_columns(coef, block)
        for i in range(body_rows):
            row = pl.ds(block * body_rows + i, 1)
            factor = jnp.exp2(held_step[row, :] * decay2)
            state = factor * state + columns[:count, i : i + 1] * drive[row, :]
            product = factor * product
            adjoint = adjoint + product * (columns[count:, i : i + 1] * scan_grad[row, :])
        return state, product, adjoint

    state, product, adjoint = lax.fori_loop(0, rows // body_rows, body, (zero, zero + 1.0, zero))
    put_ends(ends_ref, state, adjoint, jnp.sum(held_step[...], axis=0, keepdims=True))


def scan_ends(
    selected, other, step_weight, step_bias, act, projected, gated_grad, masks, decay_log
):
    rows, width = act.shape
    count = decay_log.shape[0]
    columns = selected.shape[0]
    rank = step_weight.shape[0]
    return call(
        ends_kernel,
        "scan_ends",
        width,
        [
            whole_spec(columns, rows),
            whole_spec(columns, rows),
            column_spec(rank),
            column_spec(1),
            column_spec(rows),
            part_spec(1, rows),
            column_spec(rows),
            whole_spec(rows, masks.shape[1]),
            column_spec(count),
        ],
        [column_spec(rows), column_spec(rows), column_spec(2 * count + 16)],
        [
            jax.ShapeDtypeStruct((rows, width), f32),
            jax.ShapeDtypeStruct((rows, width), f32),
            jax.ShapeDtypeStruct((2 * count + 16, width), bf16),
        ],
        [pltpu.VMEM((2 * count, rows), f32)] + [pltpu.VMEM((rows, scan_width), f32)] * 3,
        selected,
        other,
        step_weight,
        step_bias,
        act,
        projected,
        gated_grad,
        masks,
        decay_log,
    )


def lane_tiles(values):
    return [values[:, k : k + lanes] for k in range(0, values.shape[1], lanes)]


def tree_sum(parts):
    while len(parts) > 1:
        odd = parts[len(parts) // 2 * 2 :]
        parts = [a + b for a, b in zip(parts[0::2], parts[1::2])] + odd
    return parts[0]


def keep_halves(scratch, i, values):
    for k, tile in enumerate(lane_tiles(values)):
        at = (k * body_rows + i) * 8
        scratch[at : at + 8, :] = tile[:8] + tile[8:]


def put_state_sums(scratch, out_ref, block):
    for group in range(body_rows // 8):
        row = pl.ds(pl.multiple_of(block * body_rows + group * 8, 8), 8)
        for k in range(out_ref.shape[1] // lanes):
            at = (k * body_rows + group * 8) * 8
            total = tree_sum([scratch[pl.ds(at + n, 8, stride=8), :] for n in range(8)])
            out_ref[row, k * lanes : (k + 1) * lanes] = total


def lane_sums(values):
    ones = jnp.ones((8, lanes), bf16)
    high = values.astype(bf16)
    low = (values - high.astype(f32)).astype(bf16)
    total = lax.dot_general(ones, high, contract_last, preferred_element_type=f32)
    total += lax.dot_general(ones, low, contract_last, preferred_element_type=f32)
    return total[:1, :]


def at_token(t, count):
    return pl.ds(pl.multiple_of(t * count, count), count)


def forward_kernel(
    selected_ref,
    other_ref,
    step_ref,
    act_ref,
    gate_ref,
    gated_grad_ref,
    mask_ref,
    decay_log_ref,
    passed_ref,
    entering_ref,
    skip_ref,
    cot_ref,
    normed_ref,
    gated_ref,
    gate_grad_ref,
    out_product_ref,
    gate_product_ref,
    entry_ref,
    coef,
    held_step,
    drive,
    scanned,
    halves,
):
    rows = step_ref.shape[0]
    count = decay_log_ref.shape[0]
    rank = selected_ref.shape[0] - 2 * count
    decay = -jnp.exp(decay_log_ref[...])
    decay2 = decay * log2e
    before_steps = passed_ref[2 * count : 2 * count + 1, :]
    entry = passed_ref[:count, :] + through(decay, before_steps) * entering_ref[...].astype(f32)
    entry_ref[...] = entry
    coef[...] = selected_ref[rank:, :] + other_ref[rank:, :]
    act = act_ref[...].astype(f32)
    held_step[...] = jnp.where(mask_ref[:, 1:2] > 0.0, step_ref[...], reset_step)
    drive[...] = step_ref[...] * act

    def forward(block, state):
        columns = coef_columns(coef, block)
        for i in range(body_rows):
            row = pl.ds(block * body_rows + i, 1)
            factor = jnp.exp2(held_step[row, :] * decay2)
            state = factor * state + columns[:count, i : i + 1] * drive[row, :]
            keep_halves(halves, i, columns[count:, i : i + 1] * state)
        put_state_sums(halves, scanned, block)
        return state

    lax.fori_loop(0, rows // body_rows, forward, entry)
    gate = gate_ref[...].astype(f32)
    logistic = jax.nn.sigmoid(gate)
    total = scanned[...] + skip_ref[...] * act
    gated = (total * (gate * logistic)).astype(bf16)
    gated_ref[...] = gated
    out_product_ref[...] = lax.dot_general(
        gated, cot_ref[...], contract_first, preferred_element_type=f32
    ).astype(bf16)
    slope = logistic * (1.0 + gate * (1.0 - logistic))
    gate_grad = (gated_grad_ref[...] * total * slope).astype(bf16)
    gate_grad_ref[...] = gate_grad
    gate_product_ref[...] = lax.dot_general(
        normed_ref[...], gate_grad, contract_first, preferred_element_type=f32
    ).astype(bf16)


def scan_forward(
    selected,
    other,
    step,
    act,
    projected,
    gated_grad,
    masks,
    decay_log,
    passed,
    entering,
    skip_gain,
    cot,
    normed,
):
    rows, width = step.shape
    count = decay_log.shape[0]
    columns = selected.shape[0]
    return call(
        forward_kernel,
        "scan_forward",
        width,
        [
            whole_spec(columns, rows),
            whole_spec(columns, rows),
            column_spec(rows),
            column_spec(rows),
            part_spec(1, rows),
            column_spec(rows),
            whole_spec(rows, masks.shape[1]),
            column_spec(count),
            column_spec(2 * count + 8),
            column_spec(count),
            column_spec(1),
            whole_spec(*cot.shape),
            whole_spec(*normed.shape),
        ],
        [
            column_spec(rows),
            column_spec(rows),
            pl.BlockSpec((scan_width, cot.shape[1]), lambda j: (j, 0)),
            column_spec(normed.shape[1]),
            column_spec(count),
        ],
        [
            jax.ShapeDtypeStruct((rows, width), bf16),
            jax.ShapeDtypeStruct((rows, width), bf16),
            jax.ShapeDtypeStruct((width, cot.shape[1]), bf16),
            jax.ShapeDtypeStruct((normed.shape[1], width), bf16),
            jax.ShapeDtypeStruct((count, width), f32),
        ],
        [pltpu.VMEM((2 * count, rows), f32)]
        + [pltpu.VMEM((rows, scan_width), f32)] * 3
        + [pltpu.VMEM((8 * body_rows * (scan_width // lanes), lanes), f32)],
        selected,
        other,
        step,
        act,
        projected,
        gated_grad,
        masks,
        decay_log,
        passed,
        entering,
        skip_gain,
        cot,
        normed,
    )


def backward_kernel(
    selected_ref,
    other_ref,
    step_pre_ref,
    step_ref,
    act_ref,
    gate_ref,
    gated_grad_ref,
    mask_ref,
    decay_log_ref,
    entry_ref,
    passed_ref,
    returning_ref,
    skip_ref,
    step_weight_ref,
    act_grad_ref,
    select_grad_ref,
    small_ref,
    coef,
    held_step,
    drive,
    scan_grad,
    weighted,
    held_sum,
    states,
    factors,
    halves,
    more_halves,
    in_sum,
    read_sum,
):
    rows = step_ref.shape[0]
    count = decay_log_ref.shape[0]
    rank = step_weight_ref.shape[0]
    blocks = rows // body_rows
    decay = -jnp.exp(decay_log_ref[...])
    decay2 = decay * log2e
    after_steps = passed_ref[2 * count + 1 : 2 * count + 2, :]
    tail = passed_ref[count : 2 * count, :] + through(decay, after_steps) * returning_ref[...].astype(f32)
    selected = selected_ref[...] + other_ref[...]
    coef[...] = selected[rank:, :]
    step_low = selected[:rank, :].astype(bf16)
    step = step_ref[...]
    act = act_ref[...].astype(f32)
    held_step[...] = jnp.where(mask_ref[:, 1:2] > 0.0, step, reset_step)
    drive[...] = step * act
    gate = gate_ref[...].astype(f32)
    grads = gated_grad_ref[...] * (gate * jax.nn.sigmoid(gate))
    scan_grad[...] = grads
    small_ref[rank + count : rank + count + 1, :] = jnp.sum(grads * act, axis=0, keepdims=True)
    states[:count, :] = entry_ref[...]

    @pl.when(pl.program_id(0) == 0)
    def _():
        in_sum[...] = jnp.zeros(in_sum.shape, f32)
        read_sum[...] = jnp.zeros(read_sum.shape, f32)
        select_grad_ref[...] = jnp.zeros(select_grad_ref.shape, f32)

    def forward(block, state):
        columns = coef_columns(coef, block)
        for i in range(body_rows):
            t = block * body_rows + i
            row = pl.ds(t, 1)
            factor = jnp.exp2(held_step[row, :] * decay2)
            state = factor * state + columns[:count, i : i + 1] * drive[row, :]
            factors[at_token(t, count), :] = factor
            states[at_token(t + 1, count), :] = state
        return state

    lax.fori_loop(0, blocks, forward, entry_ref[...])

    def backward(k, carried):
        adjoint, decay_grad = carried
        block = blocks - 1 - k
        columns = coef_columns(coef, block)
        for i in range(body_rows - 1, -1, -1):
            t = block * body_rows + i
            row = pl.ds(t, 1)
            here = at_token(t, count)
            grad = scan_grad[row, :]
            summed = columns[count:, i : i + 1] * grad + adjoint
            read_sum[here, :] += tree_sum(lane_tiles(grad * states[at_token(t + 1, count), :]))
            in_sum[here, :] += tree_sum(lane_tiles(summed * drive[row, :]))
            keep_halves(halves, i, summed * columns[:count, i : i + 1])
            adjoint = factors[here, :] * summed
            held = adjoint * states[here, :]
            decay_grad = decay_grad + held * step_ref[row, :]
            keep_halves(more_halves, i, held * decay)
        put_state_sums(halves, weighted, block)
        put_state_sums(more_halves, held_sum, block)
        return adjoint, decay_grad

    ignored, decay_grad = lax.fori_loop(
        0, blocks, backward, (tail, jnp.zeros(decay.shape, f32))
    )
    act_grad_ref[...] = step * weighted[...] + skip_ref[...] * scan_grad[...]
    step_grad = act * weighted[...] + held_sum[...]
    pre_grad = (step_grad * jax.nn.sigmoid(step_pre_ref[...])).astype(bf16)
    small_ref[:rank, :] = jnp.dot(step_low, pre_grad, preferred_element_type=f32)
    small_ref[rank : rank + count, :] = decay_grad * decay
    bias_grad = jnp.sum(pre_grad.astype(f32), axis=0, keepdims=True)
    small_ref[rank + count + 1 : rank + count + 2, :] = bias_grad
    select_grad_ref[:rank, :] += lax.dot_general(
        step_weight_ref[...], pre_grad, contract_last, preferred_element_type=f32
    )

    @pl.when(pl.program_id(0) == pl.num_programs(0) - 1)
    def _():
        for n in range(count):
            at = pl.ds(n, rows, stride=count)
            select_grad_ref[rank + n : rank + n + 1, :] = lane_sums(in_sum[at, :])
            select_grad_ref[rank + count + n : rank + count + n + 1, :] = lane_sums(read_sum[at, :])


def scan_backward(
    selected,
    other,
    step_pre,
    step,
    act,
    projected,
    gated_grad,
    masks,
    decay_log,
    entry,
    passed,
    returning,
    skip_gain,
    step_weight,
):
    rows, width = step.shape
    count = decay_log.shape[0]
    columns = selected.shape[0]
    rank = step_weight.shape[0]
    half_rows = 8 * body_rows * (scan_width // lanes)
    small = rank + count + 2
    return call(
        backward_kernel,
        "scan_backward",
        width,
        [
            whole_spec(columns, rows),
            whole_spec(columns, rows),
            column_spec(rows),
            column_spec(rows),
            column_spec(rows),
            part_spec(1, rows),
            column_spec(rows),
            whole_spec(rows, masks.shape[1]),
            column_spec(count),
            column_spec(count),
            column_spec(2 * count + 8),
            column_spec(count),
            column_spec(1),
            column_spec(rank),
        ],
        [column_spec(rows), whole_spec(columns, rows), column_spec(small)],
        [
            jax.ShapeDtypeStruct((rows, width), f32),
            jax.ShapeDtypeStruct((columns, rows), f32),
            jax.ShapeDtypeStruct((small, width), f32),
        ],
        [pltpu.VMEM((2 * count, rows), f32)]
        + [pltpu.VMEM((rows, scan_width), f32)] * 5
        + [
            pltpu.VMEM(((rows + 1) * count, scan_width), f32),
            pltpu.VMEM((rows * count, scan_width), f32),
            pltpu.VMEM((half_rows, lanes), f32),
            pltpu.VMEM((half_rows, lanes), f32),
            pltpu.VMEM((rows * count, lanes), f32),
            pltpu.VMEM((rows * count, lanes), f32),
        ],
        selected,
        other,
        step_pre,
        step,
        act,
        projected,
        gated_grad,
        masks,
        decay_log,
        entry,
        passed,
        returning,
        skip_gain,
        step_weight,
    )


def conv_grad_kernel(
    select_grad_ref,
    other_ref,
    select_ref,
    act_grad_ref,
    convolved_ref,
    act_ref,
    inner_ref,
    conv_weight_ref,
    mask_ref,
    *rest,
):
    inner_grad_ref, before_ref, last_ref, small_ref, inner, shifted = rest[-6:]
    rows = act_ref.shape[0]
    taps = conv_weight_ref.shape[0]
    columns = select_ref.shape[0]
    select_grad = (select_grad_ref[...] + other_ref[...]).astype(bf16)
    total = act_grad_ref[...] + lax.dot_general(
        select_grad, select_ref[...], contract_first, preferred_element_type=f32
    )
    conv_grad = total * silu_slope(convolved_ref[...])
    small_ref[:columns, :] = jnp.dot(select_grad, act_ref[...], preferred_element_type=f32)
    inner[:halo, :] = inner_ref[rows:, :].astype(f32)
    inner[halo:, :] = inner_ref[:rows, :].astype(f32)
    edges = jnp.zeros((8, conv_grad.shape[1]), f32)
    shifted[:8, :] = edges
    shifted[rows + 8 :, :] = edges
    out = conv_weight_ref[taps - 1 :, :] * conv_grad
    before = edges
    small_ref[columns + taps - 1 : columns + taps, :] = jnp.sum(
        conv_grad * inner[halo:, :], axis=0, keepdims=True
    )
    for lag in range(1, taps):
        masked = conv_grad * mask_ref[:, lag : lag + 1]
        at = taps - 1 - lag
        small_ref[columns + at : columns + at + 1, :] = jnp.sum(
            masked * inner[pl.ds(halo - lag, rows), :], axis=0, keepdims=True
        )
        shifted[8 : rows + 8, :] = masked
        weight = conv_weight_ref[at : at + 1, :]
        out = out + weight * shifted[pl.ds(8 + lag, rows), :]
        before = before + weight * shifted[pl.ds(lag, 8), :]
    small_ref[columns + taps : columns + taps + 1, :] = jnp.sum(conv_grad, axis=0, keepdims=True)
    inner_grad_ref[...] = out.astype(bf16)
    before_ref[...] = before
    last_ref[...] = out[rows - halo :, :]


def convolve_grad(
    select_grad, other, select_weight, act_grad, convolved, act, projected, conv_weight, masks, waits
):
    rows, width = act.shape
    extended = rows + halo
    columns = select_weight.shape[0]
    taps = conv_weight.shape[0]
    small = columns + taps + 1
    return call(
        conv_grad_kernel,
        "convolve_grad",
        width,
        [
            whole_spec(columns, rows),
            whole_spec(columns, rows),
            column_spec(columns),
            column_spec(rows),
            column_spec(rows),
            column_spec(rows),
            part_spec(0, extended),
            column_spec(taps),
            whole_spec(rows, masks.shape[1]),
        ]
        + [pl.BlockSpec(memory_space=pl.ANY)] * len(waits),
        [column_spec(rows), column_spec(8), column_spec(halo), column_spec(small)],
        [
            jax.ShapeDtypeStruct((rows, width), bf16),
            jax.ShapeDtypeStruct((8, width), f32),
            jax.ShapeDtypeStruct((halo, width), f32),
            jax.ShapeDtypeStruct((small, width), f32),
        ],
        [pltpu.VMEM((extended, scan_width), f32), pltpu.VMEM((rows + 16, scan_width), f32)],
        select_grad,
        other,
        select_weight,
        act_grad,
        convolved,
        act,
        projected,
        conv_weight,
        masks,
        *waits,
    )


def normalize_kernel(
    own_ref,
    other_ref,
    edge_ref,
    other_edge_ref,
    gain_ref,
    ids_ref,
    whole_ref,
    extended_ref,
    normed_ref,
    chip_ref,
    other_chip_ref,
    inverse_ref,
    mask_ref,
    rows_ref,
):
    rows, half = own_ref.shape
    ids = ids_ref[...].astype(f32)
    place = lax.broadcasted_iota(jnp.int32, ids.shape, 1)
    same = []
    for lag in range(8):
        earlier = jnp.where(place < lag, ids[:, :1], pltpu.roll(ids, lag, 1)) if lag else ids
        same.append(jnp.where(earlier == ids, 1.0, 0.0))
    spare = jnp.zeros((lanes - 8, rows), f32)
    mask_ref[...] = jnp.concatenate(same + [spare]).T
    right = lax.axis_index("narrow") == 1
    for at, own, other in ((0, own_ref, other_ref), (rows, edge_ref, other_edge_ref)):
        end = at + own.shape[0]
        rows_ref[at:end, :half] = jnp.where(right, other[...], own[...])
        rows_ref[at:end, half:] = jnp.where(right, own[...], other[...])
    whole_ref[...] = rows_ref[:rows, :]
    whole = rows_ref[...].astype(f32)
    inverse = lax.rsqrt(jnp.mean(whole * whole, axis=1, keepdims=True) + epsilon)
    normed = (whole * inverse * gain_ref[...]).astype(bf16)
    extended_ref[...] = normed
    normed_ref[...] = normed[:rows]
    upper = lax.axis_index("wide") & 2 != 0
    low, high = normed[:rows, :half], normed[:rows, half:]
    chip_ref[...] = jnp.where(upper, high, low)
    other_chip_ref[...] = jnp.where(upper, low, high)
    inverse_ref[...] = inverse[:rows]


def normalized(own, other, edge, other_edge, gain, ids):
    rows, half = own.shape
    extended = rows + edge.shape[0]
    return pl.pallas_call(
        normalize_kernel,
        out_shape=[
            jax.ShapeDtypeStruct((rows, 2 * half), bf16),
            jax.ShapeDtypeStruct((extended, 2 * half), bf16),
            jax.ShapeDtypeStruct((rows, 2 * half), bf16),
            jax.ShapeDtypeStruct((rows, half), bf16),
            jax.ShapeDtypeStruct((rows, half), bf16),
            jax.ShapeDtypeStruct((rows, 1), f32),
            jax.ShapeDtypeStruct((rows, lanes), f32),
        ],
        scratch_shapes=[pltpu.VMEM((extended, 2 * half), bf16)],
        cost_estimate=tiny_cost,
        name="normalized",
    )(own, other, edge, other_edge, gain, ids)


def after(array, *waits):
    anywhere = pl.BlockSpec(memory_space=pl.ANY)
    return pl.pallas_call(
        lambda *refs: None,
        in_specs=[anywhere] * (1 + len(waits)),
        out_specs=anywhere,
        out_shape=jax.ShapeDtypeStruct(array.shape, array.dtype),
        input_output_aliases={0: 0},
        cost_estimate=tiny_cost,
        name="after",
    )(array, *waits)


def patch_kernel(ids_ref, last_ref, next_ref, wait_ref, out_ref):
    count = ids_ref.shape[0]
    place = lax.broadcasted_iota(jnp.int32, (8, 1), 0)
    same = jnp.zeros((8, 1), f32)
    for lag in range(8):
        here = jnp.where(ids_ref[count - 1 - lag] == ids_ref[count - 1], 1.0, 0.0)
        same = same + jnp.where(place == 7 - lag, here, 0.0)
    last = last_ref[...]
    out_ref[...] = jnp.concatenate([last[:8], last[8:] + next_ref[...] * same]).astype(bf16)


def patched(ids, last, following, wait):
    vmem = pl.BlockSpec(memory_space=pltpu.VMEM)
    return pl.pallas_call(
        patch_kernel,
        in_specs=[
            pl.BlockSpec(memory_space=pltpu.SMEM),
            vmem,
            vmem,
            pl.BlockSpec(memory_space=pl.ANY),
        ],
        out_shape=jax.ShapeDtypeStruct(last.shape, bf16),
        cost_estimate=tiny_cost,
        name="patched",
    )(ids, last, following, wait)


def edge_kernel(ids_ref, tokens_ref, out_ref):
    rows = ids_ref.shape[0]
    taps = 4
    out_ref[...] = tokens_ref[...]
    place = lax.broadcasted_iota(jnp.int32, (halo, 1), 0)
    same = jnp.zeros((halo, 1), f32)
    for lag in range(taps):
        here = jnp.where(ids_ref[rows - 1 - lag] == ids_ref[rows - 1], 1.0, 0.0)
        same = same + jnp.where(place == halo - 1 - lag, here, 0.0)
    out_ref[...] = (tokens_ref[...].astype(f32) * same).astype(bf16)


def edge_rows_of(ids, tokens):
    rows, width = tokens.shape
    return pl.pallas_call(
        edge_kernel,
        grid=(1,),
        in_specs=[
            pl.BlockSpec(memory_space=pltpu.SMEM),
            pl.BlockSpec((halo, width), lambda j: (rows // halo - 1, 0)),
        ],
        out_specs=pl.BlockSpec((halo, width), lambda j: (0, 0)),
        out_shape=jax.ShapeDtypeStruct((halo, width), bf16),
        cost_estimate=tiny_cost,
        name="edge_rows",
    )(ids, tokens)


block_rows, used_rows = 16, 12


def small_kernel(core_ref, scan_ref, conv_ref, wait_ref, keep_ref, send_ref, rows, blocks):
    rows[...] = jnp.zeros(rows.shape, f32)
    rows[: scan_ref.shape[0], :] = scan_ref[...]
    rows[scan_ref.shape[0] : scan_ref.shape[0] + conv_ref.shape[0], :] = conv_ref[...]
    blocks[...] = jnp.zeros(blocks.shape, f32)
    for n in range(16):
        blocks[n * block_rows : n * block_rows + used_rows, :] = rows[
            n * used_rows : (n + 1) * used_rows, :
        ]
    half = keep_ref.shape[0]
    mine = pl.ds(pl.multiple_of(core_ref[0] * half, half), half)
    other = pl.ds(pl.multiple_of((1 - core_ref[0]) * half, half), half)
    keep_ref[...] = blocks[mine, :]
    send_ref[...] = blocks[other, :].astype(bf16)


def small_halves(core, scan_small, conv_small, wait):
    width = scan_small.shape[1]
    return pl.pallas_call(
        small_kernel,
        in_specs=[pl.BlockSpec(memory_space=pltpu.SMEM)]
        + [pl.BlockSpec(memory_space=pltpu.VMEM)] * 2
        + [pl.BlockSpec(memory_space=pl.ANY)],
        out_shape=[jax.ShapeDtypeStruct((8 * block_rows, width), kind) for kind in (f32, bf16)],
        scratch_shapes=[
            pltpu.VMEM((16 * used_rows, width), f32),
            pltpu.VMEM((16 * block_rows, width), f32),
        ],
        cost_estimate=tiny_cost,
        name="small_halves",
    )(core, scan_small, conv_small, wait)


def fold_kernel(upper_ref, keep_ref, arrived_ref, out_ref, send_ref):
    size = out_ref.shape[0]
    mine = pl.ds(pl.multiple_of(upper_ref[0] * size, size), size)
    other = pl.ds(pl.multiple_of((1 - upper_ref[0]) * size, size), size)
    out_ref[...] = keep_ref[mine, :] + arrived_ref[mine, :].astype(f32)
    send_ref[...] = (keep_ref[other, :] + arrived_ref[other, :].astype(f32)).astype(bf16)


def folded(upper, keep, arrived):
    rows, width = keep.shape
    return pl.pallas_call(
        fold_kernel,
        in_specs=[pl.BlockSpec(memory_space=pltpu.SMEM)]
        + [pl.BlockSpec(memory_space=pltpu.VMEM)] * 2,
        out_shape=[jax.ShapeDtypeStruct((rows // 2, width), kind) for kind in (f32, bf16)],
        cost_estimate=tiny_cost,
        name="folded",
    )(upper, keep, arrived)


def quarter_kernel(
    place_ref, ours_ref, far_ref, normed_ref, far_normed_ref, small_ref, arrived_ref, *rest
):
    keep_ref, *sends_refs, piece, small = rest[-6:]
    piece[...] = lax.dot_general(
        normed_ref[...], ours_ref[...], contract_first, preferred_element_type=f32
    ) + lax.dot_general(
        far_normed_ref[...], far_ref[...], contract_first, preferred_element_type=f32
    )
    small[...] = small_ref[...] + arrived_ref[: small.shape[0], :].astype(f32)
    rows, spare = piece.shape[0] // 4, small.shape[0] // 4
    for n in range(4):
        block = place_ref[0] ^ n
        inner_rows = piece[pl.ds(pl.multiple_of(block * rows, rows), rows), :]
        small_rows = small[pl.ds(pl.multiple_of(block * spare, spare), spare), :]
        if n == 0:
            keep_ref[:rows, :] = inner_rows
            keep_ref[rows:, :] = small_rows
        else:
            sends_refs[n - 1][:rows, :] = inner_rows.astype(bf16)
            sends_refs[n - 1][rows:, :] = small_rows.astype(bf16)


def inner_quarter(place, ours, far, normed, far_normed, smalls):
    width = ours.shape[1]
    quarter = normed.shape[1]
    spare = smalls[0].shape[0]
    rows = (quarter + spare) // 4
    return pl.pallas_call(
        quarter_kernel,
        in_specs=[pl.BlockSpec(memory_space=pltpu.SMEM)]
        + [pl.BlockSpec(memory_space=pltpu.VMEM)] * 6,
        out_shape=[jax.ShapeDtypeStruct((rows, width), f32)]
        + [jax.ShapeDtypeStruct((rows, width), bf16)] * 3,
        scratch_shapes=[pltpu.VMEM((quarter, width), f32), pltpu.VMEM((spare, width), f32)],
        compiler_params=pltpu.CompilerParams(vmem_limit_bytes=vmem_bytes),
        cost_estimate=tiny_cost,
        name="inner_quarter",
    )(place, ours, far, normed, far_normed, *smalls)


def put_quarter(out_ref, gate_ref, inner_ref):
    rows = out_ref.shape[0] // 4
    out_ref[:, 1, :] = gate_ref[...].astype(f32)
    for n in range(4):
        at = n * (rows + block_rows)
        out_ref[n * rows : (n + 1) * rows, 0, :] = inner_ref[at : at + rows, :].astype(f32)


def join_kernel(place_ref, gate_ref, low_ref, *rest, small_rows):
    held = rest[:4]
    out_ref, wide_ref, *row_refs, gain_ref, blocks = rest[4:]
    wide_ref[...] = low_ref[...].astype(f32)
    rows = out_ref.shape[0] // 4
    for flip, ref in enumerate(held):

        @pl.when(pl.program_id(0) == flip)
        def _():
            put_quarter(out_ref, gate_ref, ref)
            number = place_ref[0] ^ flip
            number = (number & 1) * 2 + number // 2
            for n in range(4):
                at = (number * 4 + n) * block_rows
                taken = ref[(n + 1) * rows + n * block_rows : (n + 1) * (rows + block_rows), :]
                blocks[pl.ds(pl.multiple_of(at, block_rows), block_rows), :] = taken.astype(f32)

    @pl.when(pl.program_id(0) == 3)
    def _():
        for ref, start in zip(row_refs, small_rows):
            for row in range(ref.shape[0]):
                at = (start + row) // used_rows * block_rows + (start + row) % used_rows
                ref[row : row + 1, :] = blocks[at : at + 1, :]
        gain_ref[...] = sum(
            blocks[n * block_rows + used_rows : n * block_rows + used_rows + 1, :] for n in range(16)
        )


def joined(place, gate, low, held, small_rows, small_counts):
    depth, width = gate.shape
    quarter = depth // 4
    whole = pl.BlockSpec(held[0].shape, lambda j, place: (0, 0))
    part = pl.BlockSpec((quarter, width), lambda j, place: (j, 0))
    return pl.pallas_call(
        functools.partial(join_kernel, small_rows=small_rows),
        grid_spec=pltpu.PrefetchScalarGridSpec(
            num_scalar_prefetch=1,
            grid=(4,),
            in_specs=[pl.BlockSpec((quarter, width), lambda j, place: (place[0] ^ j, 0)), part]
            + [whole] * 4,
            out_specs=[
                pl.BlockSpec((quarter, 2, width), lambda j, place: (place[0] ^ j, 0, 0)),
                part,
            ]
            + [pl.BlockSpec((rows, width), lambda j, place: (0, 0)) for rows in small_counts],
            scratch_shapes=[pltpu.VMEM((16 * block_rows, width), f32)],
        ),
        out_shape=[
            jax.ShapeDtypeStruct((depth, 2, width), f32),
            jax.ShapeDtypeStruct(low.shape, f32),
        ]
        + [jax.ShapeDtypeStruct((rows, width), f32) for rows in small_counts],
        compiler_params=pltpu.CompilerParams(vmem_limit_bytes=vmem_bytes),
        cost_estimate=tiny_cost,
        name="joined",
    )(place, gate, low, *held)


def through(decay, total):
    return jnp.exp(decay * total)


def round_kernel(second_ref, decay_log_ref, own_ref, other_ref, *rest, first):
    count, width = decay_log_ref.shape
    new_passed_ref, *ends_refs = rest if first else rest[1:]
    decay = -jnp.exp(decay_log_ref[...])
    second = second_ref[0] > 0
    own, other = get_ends(own_ref, count), get_ends(other_ref, count)
    early = [jnp.where(second, b, a) for a, b in zip(own, other)]
    late = [jnp.where(second, a, b) for a, b in zip(own, other)]
    state = late[0] + through(decay, late[2]) * early[0]
    adjoint = early[1] + through(decay, early[2]) * late[1]
    if len(ends_refs) == 2:
        ends_refs[0][...] = state.astype(bf16)
        ends_refs[1][...] = adjoint.astype(bf16)
    else:
        put_ends(ends_refs[0], state, adjoint, early[2] + late[2])
    if first:
        before = after = jnp.zeros((count, width), f32)
        before_steps = after_steps = jnp.zeros((1, width), f32)
    else:
        before, after = rest[0][:count], rest[0][count : 2 * count]
        before_steps = rest[0][2 * count : 2 * count + 1]
        after_steps = rest[0][2 * count + 1 : 2 * count + 2]
    new_passed_ref[:count, :] = before + jnp.where(second, through(decay, before_steps) * other[0], 0.0)
    new_passed_ref[count : 2 * count, :] = after + jnp.where(
        second, 0.0, through(decay, after_steps) * other[1]
    )
    new_passed_ref[2 * count : 2 * count + 1, :] = before_steps + jnp.where(second, other[2], 0.0)
    new_passed_ref[2 * count + 1 : 2 * count + 2, :] = after_steps + jnp.where(second, 0.0, other[2])


def carried(ends, decay_log):
    count, width = decay_log.shape
    place = lax.axis_index("wide").astype(jnp.int32)
    state = jax.ShapeDtypeStruct((count, width), bf16)
    passed_kind = jax.ShapeDtypeStruct((2 * count + 8, width), f32)
    packed, passed = ends, []
    vmem = pl.BlockSpec(memory_space=pltpu.VMEM)
    for k, kinds in enumerate(([jax.ShapeDtypeStruct(ends.shape, bf16)], [state, state])):
        new_passed, *out = pl.pallas_call(
            functools.partial(round_kernel, first=k == 0),
            in_specs=[pl.BlockSpec(memory_space=pltpu.SMEM)] + [vmem] * (3 + k),
            out_shape=[passed_kind] + kinds,
            cost_estimate=tiny_cost,
            name="carry_round",
        )((place >> k & 1)[None], decay_log, packed, swapped(packed, "wide", 2**k), *passed)
        packed, passed = out[0], [new_passed]
    from_before = passed_along(out[0], "wide", 4)
    from_after = passed_along(out[1], "wide", -4)
    return passed[0], from_before, from_after


def local(
    tokens,
    norm_gain,
    in_weight,
    conv_weight,
    conv_bias,
    select_weight,
    step_weight,
    step_bias,
    decay_log,
    skip_gain,
    out_weight,
    segment_ids,
    cotangent,
):
    rows, features = tokens.shape
    taps = conv_weight.shape[0]
    columns = select_weight.shape[0]
    rank = step_weight.shape[0]
    count = decay_log.shape[0]
    right_half = lax.axis_index("narrow") == 1

    def both_halves(own, other):
        return jnp.concatenate(
            [jnp.where(right_half, other, own), jnp.where(right_half, own, other)], axis=1
        )

    other_tokens = swapped(tokens, "narrow", 1)
    other_cot = swapped(cotangent, "narrow", 1)
    edge, other_edge = to_next_both(edge_rows_of(segment_ids, tokens))

    whole_low, normed_ext, normed, normed_chip, normed_other_chip, inverse, masks = normalized(
        tokens, other_tokens, edge, other_edge, norm_gain[None], segment_ids[None]
    )
    projected = jnp.einsum(
        "td,dce->cte", normed_ext, in_weight, preferred_element_type=f32
    ).astype(bf16)
    convolved, act, selected = convolve(
        projected, conv_weight, conv_bias[None], select_weight, masks
    )
    other_selected = swapped(selected, "narrow", 1)
    cot_whole = both_halves(cotangent, other_cot)
    gated_grad = lax.dot_general(
        cot_whole, out_weight, contract_last, preferred_element_type=f32
    )
    step_pre, step, ends = scan_ends(
        selected,
        other_selected,
        step_weight,
        step_bias[None],
        act,
        projected,
        gated_grad,
        masks,
        decay_log,
    )
    passed, entering, returning = carried(ends, decay_log)
    gated, gate_grad, out_product, gate_product, entry = scan_forward(
        selected,
        other_selected,
        step,
        act,
        projected,
        gated_grad,
        masks,
        decay_log,
        passed,
        entering,
        skip_gain[None],
        cot_whole,
        normed,
    )
    products = (after(out_product, returning), gate_product)
    out_sum, gate_sum = lax.psum(products, "wide")
    wide_place = lax.axis_index("wide").astype(jnp.int32)
    four_place = (wide_place & 3)[None]

    def narrow_halves(array):
        low, high = array[:, :features], array[:, features:]
        return jnp.where(right_half, high, low), jnp.where(right_half, low, high)

    def after_forward(products):
        whole = whole_low.astype(f32)
        act_grad, select_grad, scan_small = scan_backward(
            selected,
            other_selected,
            step_pre,
            step,
            act,
            projected,
            gated_grad,
            masks,
            decay_log,
            entry,
            passed,
            returning,
            skip_gain[None],
            step_weight,
        )
        normed_near = swapped(normed_other_chip, "wide", 2)
        inner_main, before, last, conv_small = convolve_grad(
            select_grad,
            swapped(select_grad, "narrow", 1),
            select_weight,
            act_grad,
            convolved,
            act,
            projected,
            conv_weight,
            masks,
            [],
        )
        near = swapped(inner_main, "wide", 2)
        following = passed_along(before, "wide", -1)
        last_rows = patched(segment_ids, last, following, normed_near)
        inner_grad = jnp.concatenate([inner_main[: rows - halo], last_rows])
        normed_own, normed_send = core_columns(jnp.concatenate([normed_chip, normed_near]))
        normed_far = swapped(normed_send, "wide", 1)
        keep, send = small_halves(wide_place[None] & 1, scan_small, conv_small, last_rows)
        keep, send = folded((wide_place >> 1 & 1)[None], keep, swapped(send, "wide", 1))
        arrived = swapped(jnp.concatenate([send, last_rows]), "wide", 2)
        normed_part = jnp.einsum(
            "cte,dce->td", jnp.stack([inner_grad, gate_grad]), in_weight, preferred_element_type=f32
        )
        gain_part = jnp.sum(normed_part * whole * inverse, axis=0, keepdims=True)
        row_part = jnp.sum(normed_part * norm_gain * whole, axis=1)[None]
        first_bits, *more_bits = group_bits(2)
        narrow_sums = jnp.concatenate([gain_part, row_part], axis=1)
        narrow_sums = narrow_sums + swapped(narrow_sums, "narrow", 1)
        gain_sum = narrow_sums[:, : 2 * features]
        for bit in (bit for bits in more_bits for bit in bits):
            gain_sum = gain_sum + swapped(gain_sum, "wide", bit)
        arrived = after(arrived, narrow_sums, normed_far)
        ours = jnp.concatenate([inner_grad, near[: rows - halo], arrived[-halo:]])
        far = swapped(ours, "wide", 1)
        keep, *sends = inner_quarter(
            (wide_place >> 2 & 3)[None],
            ours,
            far,
            normed_own,
            normed_far,
            (keep, arrived),
        )
        normed_mine, normed_other = narrow_halves(normed_part)
        normed_theirs = swapped(after(normed_other, keep), "narrow", 1)
        out_part = jnp.dot(after(gated, keep), out_weight, preferred_element_type=f32)
        out_mine, out_other = narrow_halves(out_part)
        out_theirs = swapped(out_other, "narrow", 1)
        layer_out = (tokens.astype(f32) + (out_mine + out_theirs)).astype(bf16)
        row_sum = narrow_sums[:, 2 * features :].reshape(rows, 1)
        gain_mine = jnp.where(right_half, norm_gain[features:], norm_gain[:features])
        whole_grad = inverse * (gain_mine * (normed_mine + normed_theirs)) - tokens.astype(f32) * (
            inverse * inverse * inverse
        ) * (row_sum / (2 * features))
        tokens_grad = (whole_grad + cotangent.astype(f32)).astype(bf16)
        held = keep
        for n, flip in enumerate(flips(first_bits)[1:]):
            held = held + swapped(sends[n], "wide", flip).astype(f32)
        for bits in more_bits:
            held = scattered(held, bits)
        held = held.astype(bf16)
        for bits in reversed(more_bits):
            held = gathered(held, bits)
        spare = jnp.broadcast_to(gain_sum, (block_rows - used_rows, gain_sum.shape[1]))
        held = jnp.concatenate([held[: held.shape[0] - spare.shape[0]], spare.astype(bf16)])
        held = gathered(held, first_bits)
        return held, layer_out, tokens_grad

    kinds = jax.eval_shape(after_forward, products)
    held, layer_out, tokens_grad = lax.cond(
        wide_place >= 0,
        after_forward,
        lambda pair: jax.tree.map(lambda kind: jnp.zeros(kind.shape, kind.dtype), kinds),
        products,
    )

    core = swapped(held, "wide", 1)
    near = swapped(held, "wide", 2)
    far = swapped(near, "wide", 1)
    conv_at = rank + count + 2
    (
        in_weight_grad,
        out_weight_grad,
        step_weight_grad,
        decay_log_grad,
        skip_gain_grad,
        step_bias_grad,
        select_weight_grad,
        conv_weight_grad,
        conv_bias_grad,
        norm_gain_grad,
    ) = joined(
        four_place,
        gate_sum,
        out_sum,
        (held, core, near, far),
        (0, rank, rank + count, rank + count + 1, conv_at, conv_at + columns, conv_at + columns + taps),
        (rank, count, 1, 1, columns, taps, 1, 1),
    )
    return (
        layer_out,
        tokens_grad,
        norm_gain_grad[0],
        in_weight_grad,
        conv_weight_grad,
        conv_bias_grad[0],
        select_weight_grad,
        step_weight_grad,
        step_bias_grad[0],
        decay_log_grad,
        skip_gain_grad[0],
        out_weight_grad,
    )


def solution(mesh):
    placed = (
        P("wide", "narrow"),
        P(),
        P(None, None, "narrow"),
        P(None, "narrow"),
        P("narrow"),
        P(None, "narrow"),
        P(None, "narrow"),
        P("narrow"),
        P(None, "narrow"),
        P("narrow"),
        P("narrow", None),
        P("wide"),
        P("wide", "narrow"),
    )
    return jax.shard_map(
        local,
        mesh=mesh,
        in_specs=placed,
        out_specs=(
            P("wide", "narrow"),
            P("wide", "narrow"),
            P(),
            P(None, None, "narrow"),
            P(None, "narrow"),
            P("narrow"),
            P(None, "narrow"),
            P(None, "narrow"),
            P("narrow"),
            P(None, "narrow"),
            P("narrow"),
            P("narrow", None),
        ),
        check_vma=False,
    )
```

```python
import functools

import jax
import jax.numpy as jnp
from jax import lax
from jax.experimental import pallas as pl
from jax.experimental.pallas import tpu as pltpu
from jax.sharding import PartitionSpec as P

epsilon = 1e-05
log2e = 1.4426950408889634
reset_step = 1e30
lanes = 128
halo = 16
body_rows = 32
scan_width = 512
vmem_bytes = 56 * 1024 * 1024
tiny_cost = pl.CostEstimate(flops=1, bytes_accessed=1, transcendentals=0)
f32 = jnp.float32
bf16 = jnp.bfloat16
contract_first = (((0,), (0,)), ((), ()))
contract_last = (((1,), (1,)), ((), ()))


def passed_along(array, axis, by):
    peers = lax.axis_size(axis)
    pairs = [(i, i + by) for i in range(peers) if 0 <= i + by < peers]
    return lax.ppermute(array, axis, pairs)


def swapped(array, axis, bit):
    peers = lax.axis_size(axis)
    return lax.ppermute(array, axis, [(i, i ^ bit) for i in range(peers)])


def wide_bits():
    bit, bits = 1, []
    while bit < lax.axis_size("wide"):
        bits.append(bit)
        bit *= 2
    return bits


def to_next_both(array):
    count, sides = lax.axis_size("wide"), lax.axis_size("narrow")
    pairs = [
        (i * sides + k, (i + 1) * sides + (sides - 1 - k))
        for i in range(count - 1)
        for k in range(sides)
    ]
    return passed_along(array, "wide", 1), lax.ppermute(array, ("wide", "narrow"), pairs)


def is_upper(bit):
    return (lax.axis_index("wide") & bit) != 0


def group_bits(size):
    bits, bit = [], 4
    while bit < lax.axis_size("wide"):
        bits.append(bit)
        bit *= 2
    return [tuple(bits[k : k + size]) for k in range(0, len(bits), size)]


def flips(bits):
    return [sum(b for k, b in enumerate(bits) if n >> k & 1) for n in range(2 ** len(bits))]


def scattered(piece, bits):
    rows = piece.shape[0] // 2 ** len(bits)
    here = sum(is_upper(b).astype(jnp.int32) << k for k, b in enumerate(bits))

    def block(n):
        return lax.dynamic_slice_in_dim(piece, (here ^ n) * rows, rows, 0)

    total = block(0).astype(f32)
    for n, flip in enumerate(flips(bits)):
        if n > 0:
            total = total + swapped(block(n).astype(bf16), "wide", flip).astype(f32)
    return total


def gathered(held, bits):
    blocks = [held] + [swapped(held, "wide", flip) for flip in flips(bits)[1:]]
    for bit in bits:
        upper = is_upper(bit)
        blocks = [
            jnp.concatenate([jnp.where(upper, b, a), jnp.where(upper, a, b)])
            for a, b in zip(blocks[0::2], blocks[1::2])
        ]
    return blocks[0]


def quarter_of_four(array):
    width = array.shape[1] // 4
    here = lax.axis_index("wide") & 3

    def quarter(n):
        return lax.dynamic_slice_in_dim(array, (here ^ n) * width, width, 1)

    return [quarter(0)] + [swapped(quarter(n), "wide", n) for n in (2, 1, 3)]


def silu_slope(values):
    logistic = jax.nn.sigmoid(values)
    return logistic * (1.0 + values * (1.0 - logistic))


def softplus(values):
    return jnp.maximum(values, 0.0) + jnp.log1p(jnp.exp(-jnp.abs(values)))


def column_spec(rows, start=0):
    return pl.BlockSpec((rows, scan_width), lambda j: (0, start + j))


def part_spec(part, rows, start=0):
    return pl.BlockSpec((None, rows, scan_width), lambda j: (part, 0, start + j))


def whole_spec(rows, width):
    return pl.BlockSpec((rows, width), lambda j: (0, 0))


def call(kernel, name, width, in_specs, out_specs, out_shape, scratch, *operands):
    return pl.pallas_call(
        kernel,
        grid=(width // scan_width,),
        in_specs=in_specs,
        out_specs=out_specs,
        out_shape=out_shape,
        scratch_shapes=scratch,
        compiler_params=pltpu.CompilerParams(vmem_limit_bytes=vmem_bytes),
        cost_estimate=tiny_cost,
        name=name,
    )(*operands)


def conv_kernel(
    inner_ref,
    conv_weight_ref,
    conv_bias_ref,
    select_ref,
    mask_ref,
    convolved_ref,
    act_ref,
    selected_ref,
    inner,
):
    rows = act_ref.shape[0]
    taps = conv_weight_ref.shape[0]
    inner[:halo, :] = inner_ref[rows:, :].astype(f32)
    inner[halo:, :] = inner_ref[:rows, :].astype(f32)
    total = conv_bias_ref[...] + conv_weight_ref[taps - 1 :, :] * inner[halo:, :]
    for lag in range(1, taps):
        earlier = inner[pl.ds(halo - lag, rows), :] * mask_ref[:, lag : lag + 1]
        total = total + conv_weight_ref[taps - 1 - lag : taps - lag, :] * earlier
    convolved_ref[...] = total
    act = (total * jax.nn.sigmoid(total)).astype(bf16)
    act_ref[...] = act
    part = lax.dot_general(select_ref[...], act, contract_last, preferred_element_type=f32)

    @pl.when(pl.program_id(0) == 0)
    def _():
        selected_ref[...] = part

    @pl.when(pl.program_id(0) > 0)
    def _():
        selected_ref[...] += part


def convolve(projected, conv_weight, conv_bias, select_weight, masks):
    parts, extended, width = projected.shape
    rows = extended - halo
    taps = conv_weight.shape[0]
    columns = select_weight.shape[0]
    return call(
        conv_kernel,
        "convolve",
        width,
        [
            part_spec(0, extended),
            column_spec(taps),
            column_spec(1),
            column_spec(columns),
            whole_spec(rows, masks.shape[1]),
        ],
        [column_spec(rows), column_spec(rows), whole_spec(columns, rows)],
        [
            jax.ShapeDtypeStruct((rows, width), f32),
            jax.ShapeDtypeStruct((rows, width), bf16),
            jax.ShapeDtypeStruct((columns, rows), f32),
        ],
        [pltpu.VMEM((extended, scan_width), f32)],
        projected,
        conv_weight,
        conv_bias,
        select_weight,
        masks,
    )


def coef_columns(coef, block):
    per_tile = lanes // body_rows
    start = pl.multiple_of((block // per_tile) * lanes, lanes)
    tile = coef[:, pl.ds(start, lanes)]
    back = body_rows * lax.rem(block, per_tile)
    return pltpu.roll(tile, lax.rem(lanes - back, lanes), 1)


def put_ends(ends_ref, state, adjoint, total):
    count, width = state.shape
    ends_ref[:count, :] = state.astype(bf16)
    ends_ref[count : 2 * count, :] = adjoint.astype(bf16)
    high = total.astype(bf16).astype(f32)
    upper = lax.broadcasted_iota(jnp.int32, (16, width), 0) < 8
    ends_ref[2 * count :, :] = jnp.where(upper, high, total - high).astype(bf16)


def get_ends(ends_ref, count):
    total = ends_ref[2 * count :].astype(f32)
    return (
        ends_ref[:count].astype(f32),
        ends_ref[count : 2 * count].astype(f32),
        total[:1] + total[8:9],
    )


def ends_kernel(
    selected_ref,
    other_ref,
    step_weight_ref,
    step_bias_ref,
    act_ref,
    gate_ref,
    gated_grad_ref,
    mask_ref,
    decay_log_ref,
    step_pre_ref,
    step_ref,
    ends_ref,
    coef,
    held_step,
    drive,
    scan_grad,
):
    rows = act_ref.shape[0]
    count = decay_log_ref.shape[0]
    rank = step_weight_ref.shape[0]
    decay2 = -jnp.exp(decay_log_ref[...]) * log2e
    selected = selected_ref[...] + other_ref[...]
    coef[...] = selected[rank:, :]
    step_low = selected[:rank, :].astype(bf16)
    step_pre = step_bias_ref[...] + lax.dot_general(
        step_low, step_weight_ref[...], contract_first, preferred_element_type=f32
    )
    step_pre_ref[...] = step_pre
    step = softplus(step_pre)
    step_ref[...] = step
    held_step[...] = jnp.where(mask_ref[:, 1:2] > 0.0, step, reset_step)
    drive[...] = step * act_ref[...].astype(f32)
    gate = gate_ref[...].astype(f32)
    scan_grad[...] = gated_grad_ref[...] * (gate * jax.nn.sigmoid(gate))
    zero = jnp.zeros(decay2.shape, f32)

    def body(block, carried):
        state, product, adjoint = carried
        columns = coef_columns(coef, block)
        for i in range(body_rows):
            row = pl.ds(block * body_rows + i, 1)
            factor = jnp.exp2(held_step[row, :] * decay2)
            state = factor * state + columns[:count, i : i + 1] * drive[row, :]
            product = factor * product
            adjoint = adjoint + product * (columns[count:, i : i + 1] * scan_grad[row, :])
        return state, product, adjoint

    state, product, adjoint = lax.fori_loop(0, rows // body_rows, body, (zero, zero + 1.0, zero))
    put_ends(ends_ref, state, adjoint, jnp.sum(held_step[...], axis=0, keepdims=True))


def scan_ends(
    selected, other, step_weight, step_bias, act, projected, gated_grad, masks, decay_log
):
    rows, width = act.shape
    count = decay_log.shape[0]
    columns = selected.shape[0]
    rank = step_weight.shape[0]
    return call(
        ends_kernel,
        "scan_ends",
        width,
        [
            whole_spec(columns, rows),
            whole_spec(columns, rows),
            column_spec(rank),
            column_spec(1),
            column_spec(rows),
            part_spec(1, rows),
            column_spec(rows),
            whole_spec(rows, masks.shape[1]),
            column_spec(count),
        ],
        [column_spec(rows), column_spec(rows), column_spec(2 * count + 16)],
        [
            jax.ShapeDtypeStruct((rows, width), f32),
            jax.ShapeDtypeStruct((rows, width), f32),
            jax.ShapeDtypeStruct((2 * count + 16, width), bf16),
        ],
        [pltpu.VMEM((2 * count, rows), f32)] + [pltpu.VMEM((rows, scan_width), f32)] * 3,
        selected,
        other,
        step_weight,
        step_bias,
        act,
        projected,
        gated_grad,
        masks,
        decay_log,
    )


def lane_tiles(values):
    return [values[:, k : k + lanes] for k in range(0, values.shape[1], lanes)]


def tree_sum(parts):
    while len(parts) > 1:
        odd = parts[len(parts) // 2 * 2 :]
        parts = [a + b for a, b in zip(parts[0::2], parts[1::2])] + odd
    return parts[0]


def keep_halves(scratch, i, values):
    for k, tile in enumerate(lane_tiles(values)):
        at = (k * body_rows + i) * 8
        scratch[at : at + 8, :] = tile[:8] + tile[8:]


def put_state_sums(scratch, out_ref, block):
    for group in range(body_rows // 8):
        row = pl.ds(pl.multiple_of(block * body_rows + group * 8, 8), 8)
        for k in range(out_ref.shape[1] // lanes):
            at = (k * body_rows + group * 8) * 8
            total = tree_sum([scratch[pl.ds(at + n, 8, stride=8), :] for n in range(8)])
            out_ref[row, k * lanes : (k + 1) * lanes] = total


def lane_sums(values):
    ones = jnp.ones((8, lanes), bf16)
    high = values.astype(bf16)
    low = (values - high.astype(f32)).astype(bf16)
    total = lax.dot_general(ones, high, contract_last, preferred_element_type=f32)
    total += lax.dot_general(ones, low, contract_last, preferred_element_type=f32)
    return total[:1, :]


def at_token(t, count):
    return pl.ds(pl.multiple_of(t * count, count), count)


def forward_kernel(
    selected_ref,
    other_ref,
    step_ref,
    act_ref,
    gate_ref,
    gated_grad_ref,
    mask_ref,
    decay_log_ref,
    passed_ref,
    entering_ref,
    skip_ref,
    cot_ref,
    normed_ref,
    gated_ref,
    gate_grad_ref,
    out_product_ref,
    gate_product_ref,
    entry_ref,
    coef,
    held_step,
    drive,
    scanned,
    halves,
):
    rows = step_ref.shape[0]
    count = decay_log_ref.shape[0]
    rank = selected_ref.shape[0] - 2 * count
    decay = -jnp.exp(decay_log_ref[...])
    decay2 = decay * log2e
    before_steps = passed_ref[2 * count : 2 * count + 1, :]
    entry = passed_ref[:count, :] + through(decay, before_steps) * entering_ref[...].astype(f32)
    entry_ref[...] = entry
    coef[...] = selected_ref[rank:, :] + other_ref[rank:, :]
    act = act_ref[...].astype(f32)
    held_step[...] = jnp.where(mask_ref[:, 1:2] > 0.0, step_ref[...], reset_step)
    drive[...] = step_ref[...] * act

    def forward(block, state):
        columns = coef_columns(coef, block)
        for i in range(body_rows):
            row = pl.ds(block * body_rows + i, 1)
            factor = jnp.exp2(held_step[row, :] * decay2)
            state = factor * state + columns[:count, i : i + 1] * drive[row, :]
            keep_halves(halves, i, columns[count:, i : i + 1] * state)
        put_state_sums(halves, scanned, block)
        return state

    lax.fori_loop(0, rows // body_rows, forward, entry)
    gate = gate_ref[...].astype(f32)
    logistic = jax.nn.sigmoid(gate)
    total = scanned[...] + skip_ref[...] * act
    gated = (total * (gate * logistic)).astype(bf16)
    gated_ref[...] = gated
    out_product_ref[...] = lax.dot_general(
        gated, cot_ref[...], contract_first, preferred_element_type=f32
    ).astype(bf16)
    slope = logistic * (1.0 + gate * (1.0 - logistic))
    gate_grad = (gated_grad_ref[...] * total * slope).astype(bf16)
    gate_grad_ref[...] = gate_grad
    gate_product_ref[...] = lax.dot_general(
        normed_ref[...], gate_grad, contract_first, preferred_element_type=f32
    ).astype(bf16)


def scan_forward(
    selected,
    other,
    step,
    act,
    projected,
    gated_grad,
    masks,
    decay_log,
    passed,
    entering,
    skip_gain,
    cot,
    normed,
):
    rows, width = step.shape
    count = decay_log.shape[0]
    columns = selected.shape[0]
    return call(
        forward_kernel,
        "scan_forward",
        width,
        [
            whole_spec(columns, rows),
            whole_spec(columns, rows),
            column_spec(rows),
            column_spec(rows),
            part_spec(1, rows),
            column_spec(rows),
            whole_spec(rows, masks.shape[1]),
            column_spec(count),
            column_spec(2 * count + 8),
            column_spec(count),
            column_spec(1),
            whole_spec(*cot.shape),
            whole_spec(*normed.shape),
        ],
        [
            column_spec(rows),
            column_spec(rows),
            pl.BlockSpec((scan_width, cot.shape[1]), lambda j: (j, 0)),
            column_spec(normed.shape[1]),
            column_spec(count),
        ],
        [
            jax.ShapeDtypeStruct((rows, width), bf16),
            jax.ShapeDtypeStruct((rows, width), bf16),
            jax.ShapeDtypeStruct((width, cot.shape[1]), bf16),
            jax.ShapeDtypeStruct((normed.shape[1], width), bf16),
            jax.ShapeDtypeStruct((count, width), f32),
        ],
        [pltpu.VMEM((2 * count, rows), f32)]
        + [pltpu.VMEM((rows, scan_width), f32)] * 3
        + [pltpu.VMEM((8 * body_rows * (scan_width // lanes), lanes), f32)],
        selected,
        other,
        step,
        act,
        projected,
        gated_grad,
        masks,
        decay_log,
        passed,
        entering,
        skip_gain,
        cot,
        normed,
    )


def backward_kernel(
    selected_ref,
    other_ref,
    step_pre_ref,
    step_ref,
    act_ref,
    gate_ref,
    gated_grad_ref,
    mask_ref,
    decay_log_ref,
    entry_ref,
    passed_ref,
    returning_ref,
    skip_ref,
    step_weight_ref,
    act_grad_ref,
    select_grad_ref,
    small_ref,
    coef,
    held_step,
    drive,
    scan_grad,
    weighted,
    held_sum,
    states,
    factors,
    halves,
    more_halves,
    in_sum,
    read_sum,
):
    rows = step_ref.shape[0]
    count = decay_log_ref.shape[0]
    rank = step_weight_ref.shape[0]
    blocks = rows // body_rows
    decay = -jnp.exp(decay_log_ref[...])
    decay2 = decay * log2e
    after_steps = passed_ref[2 * count + 1 : 2 * count + 2, :]
    tail = passed_ref[count : 2 * count, :] + through(decay, after_steps) * returning_ref[...].astype(f32)
    selected = selected_ref[...] + other_ref[...]
    coef[...] = selected[rank:, :]
    step_low = selected[:rank, :].astype(bf16)
    step = step_ref[...]
    act = act_ref[...].astype(f32)
    held_step[...] = jnp.where(mask_ref[:, 1:2] > 0.0, step, reset_step)
    drive[...] = step * act
    gate = gate_ref[...].astype(f32)
    grads = gated_grad_ref[...] * (gate * jax.nn.sigmoid(gate))
    scan_grad[...] = grads
    small_ref[rank + count : rank + count + 1, :] = jnp.sum(grads * act, axis=0, keepdims=True)
    states[:count, :] = entry_ref[...]

    @pl.when(pl.program_id(0) == 0)
    def _():
        in_sum[...] = jnp.zeros(in_sum.shape, f32)
        read_sum[...] = jnp.zeros(read_sum.shape, f32)
        select_grad_ref[...] = jnp.zeros(select_grad_ref.shape, f32)

    def forward(block, state):
        columns = coef_columns(coef, block)
        for i in range(body_rows):
            t = block * body_rows + i
            row = pl.ds(t, 1)
            factor = jnp.exp2(held_step[row, :] * decay2)
            state = factor * state + columns[:count, i : i + 1] * drive[row, :]
            factors[at_token(t, count), :] = factor
            states[at_token(t + 1, count), :] = state
        return state

    lax.fori_loop(0, blocks, forward, entry_ref[...])

    def backward(k, carried):
        adjoint, decay_grad = carried
        block = blocks - 1 - k
        columns = coef_columns(coef, block)
        for i in range(body_rows - 1, -1, -1):
            t = block * body_rows + i
            row = pl.ds(t, 1)
            here = at_token(t, count)
            grad = scan_grad[row, :]
            summed = columns[count:, i : i + 1] * grad + adjoint
            read_sum[here, :] += tree_sum(lane_tiles(grad * states[at_token(t + 1, count), :]))
            in_sum[here, :] += tree_sum(lane_tiles(summed * drive[row, :]))
            keep_halves(halves, i, summed * columns[:count, i : i + 1])
            adjoint = factors[here, :] * summed
            held = adjoint * states[here, :]
            decay_grad = decay_grad + held * step_ref[row, :]
            keep_halves(more_halves, i, held * decay)
        put_state_sums(halves, weighted, block)
        put_state_sums(more_halves, held_sum, block)
        return adjoint, decay_grad

    ignored, decay_grad = lax.fori_loop(
        0, blocks, backward, (tail, jnp.zeros(decay.shape, f32))
    )
    act_grad_ref[...] = step * weighted[...] + skip_ref[...] * scan_grad[...]
    step_grad = act * weighted[...] + held_sum[...]
    pre_grad = (step_grad * jax.nn.sigmoid(step_pre_ref[...])).astype(bf16)
    small_ref[:rank, :] = jnp.dot(step_low, pre_grad, preferred_element_type=f32)
    small_ref[rank : rank + count, :] = decay_grad * decay
    bias_grad = jnp.sum(pre_grad.astype(f32), axis=0, keepdims=True)
    small_ref[rank + count + 1 : rank + count + 2, :] = bias_grad
    select_grad_ref[:rank, :] += lax.dot_general(
        step_weight_ref[...], pre_grad, contract_last, preferred_element_type=f32
    )

    @pl.when(pl.program_id(0) == pl.num_programs(0) - 1)
    def _():
        for n in range(count):
            at = pl.ds(n, rows, stride=count)
            select_grad_ref[rank + n : rank + n + 1, :] = lane_sums(in_sum[at, :])
            select_grad_ref[rank + count + n : rank + count + n + 1, :] = lane_sums(read_sum[at, :])


def scan_backward(
    selected,
    other,
    step_pre,
    step,
    act,
    projected,
    gated_grad,
    masks,
    decay_log,
    entry,
    passed,
    returning,
    skip_gain,
    step_weight,
):
    rows, width = step.shape
    count = decay_log.shape[0]
    columns = selected.shape[0]
    rank = step_weight.shape[0]
    half_rows = 8 * body_rows * (scan_width // lanes)
    small = rank + count + 2
    return call(
        backward_kernel,
        "scan_backward",
        width,
        [
            whole_spec(columns, rows),
            whole_spec(columns, rows),
            column_spec(rows),
            column_spec(rows),
            column_spec(rows),
            part_spec(1, rows),
            column_spec(rows),
            whole_spec(rows, masks.shape[1]),
            column_spec(count),
            column_spec(count),
            column_spec(2 * count + 8),
            column_spec(count),
            column_spec(1),
            column_spec(rank),
        ],
        [column_spec(rows), whole_spec(columns, rows), column_spec(small)],
        [
            jax.ShapeDtypeStruct((rows, width), f32),
            jax.ShapeDtypeStruct((columns, rows), f32),
            jax.ShapeDtypeStruct((small, width), f32),
        ],
        [pltpu.VMEM((2 * count, rows), f32)]
        + [pltpu.VMEM((rows, scan_width), f32)] * 5
        + [
            pltpu.VMEM(((rows + 1) * count, scan_width), f32),
            pltpu.VMEM((rows * count, scan_width), f32),
            pltpu.VMEM((half_rows, lanes), f32),
            pltpu.VMEM((half_rows, lanes), f32),
            pltpu.VMEM((rows * count, lanes), f32),
            pltpu.VMEM((rows * count, lanes), f32),
        ],
        selected,
        other,
        step_pre,
        step,
        act,
        projected,
        gated_grad,
        masks,
        decay_log,
        entry,
        passed,
        returning,
        skip_gain,
        step_weight,
    )


def conv_grad_kernel(
    select_grad_ref,
    other_ref,
    select_ref,
    act_grad_ref,
    convolved_ref,
    act_ref,
    inner_ref,
    conv_weight_ref,
    mask_ref,
    *rest,
):
    inner_grad_ref, before_ref, last_ref, small_ref, inner, shifted = rest[-6:]
    rows = act_ref.shape[0]
    taps = conv_weight_ref.shape[0]
    columns = select_ref.shape[0]
    select_grad = (select_grad_ref[...] + other_ref[...]).astype(bf16)
    total = act_grad_ref[...] + lax.dot_general(
        select_grad, select_ref[...], contract_first, preferred_element_type=f32
    )
    conv_grad = total * silu_slope(convolved_ref[...])
    small_ref[:columns, :] = jnp.dot(select_grad, act_ref[...], preferred_element_type=f32)
    inner[:halo, :] = inner_ref[rows:, :].astype(f32)
    inner[halo:, :] = inner_ref[:rows, :].astype(f32)
    edges = jnp.zeros((8, conv_grad.shape[1]), f32)
    shifted[:8, :] = edges
    shifted[rows + 8 :, :] = edges
    out = conv_weight_ref[taps - 1 :, :] * conv_grad
    before = edges
    small_ref[columns + taps - 1 : columns + taps, :] = jnp.sum(
        conv_grad * inner[halo:, :], axis=0, keepdims=True
    )
    for lag in range(1, taps):
        masked = conv_grad * mask_ref[:, lag : lag + 1]
        at = taps - 1 - lag
        small_ref[columns + at : columns + at + 1, :] = jnp.sum(
            masked * inner[pl.ds(halo - lag, rows), :], axis=0, keepdims=True
        )
        shifted[8 : rows + 8, :] = masked
        weight = conv_weight_ref[at : at + 1, :]
        out = out + weight * shifted[pl.ds(8 + lag, rows), :]
        before = before + weight * shifted[pl.ds(lag, 8), :]
    small_ref[columns + taps : columns + taps + 1, :] = jnp.sum(conv_grad, axis=0, keepdims=True)
    inner_grad_ref[...] = out.astype(bf16)
    before_ref[...] = before
    last_ref[...] = out[rows - 8 :, :]


def convolve_grad(
    select_grad, other, select_weight, act_grad, convolved, act, projected, conv_weight, masks, waits
):
    rows, width = act.shape
    extended = rows + halo
    columns = select_weight.shape[0]
    taps = conv_weight.shape[0]
    small = columns + taps + 1
    return call(
        conv_grad_kernel,
        "convolve_grad",
        width,
        [
            whole_spec(columns, rows),
            whole_spec(columns, rows),
            column_spec(columns),
            column_spec(rows),
            column_spec(rows),
            column_spec(rows),
            part_spec(0, extended),
            column_spec(taps),
            whole_spec(rows, masks.shape[1]),
        ]
        + [pl.BlockSpec(memory_space=pl.ANY)] * len(waits),
        [column_spec(rows), column_spec(8), column_spec(8), column_spec(small)],
        [
            jax.ShapeDtypeStruct((rows, width), bf16),
            jax.ShapeDtypeStruct((8, width), f32),
            jax.ShapeDtypeStruct((8, width), f32),
            jax.ShapeDtypeStruct((small, width), f32),
        ],
        [pltpu.VMEM((extended, scan_width), f32), pltpu.VMEM((rows + 16, scan_width), f32)],
        select_grad,
        other,
        select_weight,
        act_grad,
        convolved,
        act,
        projected,
        conv_weight,
        masks,
        *waits,
    )


def normalize_kernel(
    own_ref,
    other_ref,
    edge_ref,
    other_edge_ref,
    gain_ref,
    ids_ref,
    whole_ref,
    extended_ref,
    normed_ref,
    inverse_ref,
    mask_ref,
    rows_ref,
):
    rows, half = own_ref.shape
    ids = ids_ref[...].astype(f32)
    place = lax.broadcasted_iota(jnp.int32, ids.shape, 1)
    same = []
    for lag in range(8):
        earlier = jnp.where(place < lag, ids[:, :1], pltpu.roll(ids, lag, 1)) if lag else ids
        same.append(jnp.where(earlier == ids, 1.0, 0.0))
    spare = jnp.zeros((lanes - 8, rows), f32)
    mask_ref[...] = jnp.concatenate(same + [spare]).T
    right = lax.axis_index("narrow") == 1
    for at, own, other in ((0, own_ref, other_ref), (rows, edge_ref, other_edge_ref)):
        end = at + own.shape[0]
        rows_ref[at:end, :half] = jnp.where(right, other[...], own[...])
        rows_ref[at:end, half:] = jnp.where(right, own[...], other[...])
    whole_ref[...] = rows_ref[:rows, :]
    whole = rows_ref[...].astype(f32)
    inverse = lax.rsqrt(jnp.mean(whole * whole, axis=1, keepdims=True) + epsilon)
    normed = (whole * inverse * gain_ref[...]).astype(bf16)
    extended_ref[...] = normed
    normed_ref[...] = normed[:rows]
    inverse_ref[...] = inverse[:rows]


def normalized(own, other, edge, other_edge, gain, ids):
    rows, half = own.shape
    extended = rows + edge.shape[0]
    return pl.pallas_call(
        normalize_kernel,
        out_shape=[
            jax.ShapeDtypeStruct((rows, 2 * half), bf16),
            jax.ShapeDtypeStruct((extended, 2 * half), bf16),
            jax.ShapeDtypeStruct((rows, 2 * half), bf16),
            jax.ShapeDtypeStruct((rows, 1), f32),
            jax.ShapeDtypeStruct((rows, lanes), f32),
        ],
        scratch_shapes=[pltpu.VMEM((extended, 2 * half), bf16)],
        cost_estimate=tiny_cost,
        name="normalized",
    )(own, other, edge, other_edge, gain, ids)


def after(array, *waits):
    anywhere = pl.BlockSpec(memory_space=pl.ANY)
    return pl.pallas_call(
        lambda *refs: None,
        in_specs=[anywhere] * (1 + len(waits)),
        out_specs=anywhere,
        out_shape=jax.ShapeDtypeStruct(array.shape, array.dtype),
        input_output_aliases={0: 0},
        cost_estimate=tiny_cost,
        name="after",
    )(array, *waits)


def patch_kernel(ids_ref, rows_ref, last_ref, next_ref, *rest):
    count = ids_ref.shape[0]
    place = lax.broadcasted_iota(jnp.int32, (8, 1), 0)
    same = jnp.zeros((8, 1), f32)
    for lag in range(8):
        here = jnp.where(ids_ref[count - 1 - lag] == ids_ref[count - 1], 1.0, 0.0)
        same = same + jnp.where(place == 7 - lag, here, 0.0)
    total = last_ref[...] + next_ref[...] * same
    rows = rows_ref[...].astype(f32)
    rest[-1][...] = jnp.concatenate([rows[: halo - 8], total]).astype(bf16)


def patched(ids, grads, last, following, *waits):
    rows, width = grads.shape
    block = pl.BlockSpec((halo, width), lambda j: (rows // halo - 1, 0))
    edge = pl.BlockSpec((8, width), lambda j: (0, 0))
    return pl.pallas_call(
        patch_kernel,
        grid=(1,),
        in_specs=[pl.BlockSpec(memory_space=pltpu.SMEM), block, edge, edge]
        + [pl.BlockSpec(memory_space=pl.ANY)] * len(waits),
        out_specs=block,
        out_shape=jax.ShapeDtypeStruct((rows, width), bf16),
        input_output_aliases={1: 0},
        cost_estimate=tiny_cost,
        name="patched",
    )(ids, grads, last, following, *waits)


def edge_kernel(ids_ref, tokens_ref, out_ref):
    rows = ids_ref.shape[0]
    taps = 4
    out_ref[...] = tokens_ref[...]
    place = lax.broadcasted_iota(jnp.int32, (halo, 1), 0)
    same = jnp.zeros((halo, 1), f32)
    for lag in range(taps):
        here = jnp.where(ids_ref[rows - 1 - lag] == ids_ref[rows - 1], 1.0, 0.0)
        same = same + jnp.where(place == halo - 1 - lag, here, 0.0)
    out_ref[...] = (tokens_ref[...].astype(f32) * same).astype(bf16)


def edge_rows_of(ids, tokens):
    rows, width = tokens.shape
    return pl.pallas_call(
        edge_kernel,
        grid=(1,),
        in_specs=[
            pl.BlockSpec(memory_space=pltpu.SMEM),
            pl.BlockSpec((halo, width), lambda j: (rows // halo - 1, 0)),
        ],
        out_specs=pl.BlockSpec((halo, width), lambda j: (0, 0)),
        out_shape=jax.ShapeDtypeStruct((halo, width), bf16),
        cost_estimate=tiny_cost,
        name="edge_rows",
    )(ids, tokens)


block_rows, used_rows = 16, 12


def small_kernel(core_ref, scan_ref, conv_ref, wait_ref, keep_ref, send_ref, rows, blocks):
    rows[...] = jnp.zeros(rows.shape, f32)
    rows[: scan_ref.shape[0], :] = scan_ref[...]
    rows[scan_ref.shape[0] : scan_ref.shape[0] + conv_ref.shape[0], :] = conv_ref[...]
    blocks[...] = jnp.zeros(blocks.shape, f32)
    for n in range(16):
        blocks[n * block_rows : n * block_rows + used_rows, :] = rows[
            n * used_rows : (n + 1) * used_rows, :
        ]
    half = keep_ref.shape[0]
    mine = pl.ds(pl.multiple_of(core_ref[0] * half, half), half)
    other = pl.ds(pl.multiple_of((1 - core_ref[0]) * half, half), half)
    keep_ref[...] = blocks[mine, :]
    send_ref[...] = blocks[other, :].astype(bf16)


def small_halves(core, scan_small, conv_small, wait):
    width = scan_small.shape[1]
    return pl.pallas_call(
        small_kernel,
        in_specs=[pl.BlockSpec(memory_space=pltpu.SMEM)]
        + [pl.BlockSpec(memory_space=pltpu.VMEM)] * 2
        + [pl.BlockSpec(memory_space=pl.ANY)],
        out_shape=[jax.ShapeDtypeStruct((8 * block_rows, width), kind) for kind in (f32, bf16)],
        scratch_shapes=[
            pltpu.VMEM((16 * used_rows, width), f32),
            pltpu.VMEM((16 * block_rows, width), f32),
        ],
        cost_estimate=tiny_cost,
        name="small_halves",
    )(core, scan_small, conv_small, wait)


def fold_kernel(upper_ref, keep_ref, arrived_ref, out_ref, send_ref):
    size = out_ref.shape[0]
    mine = pl.ds(pl.multiple_of(upper_ref[0] * size, size), size)
    other = pl.ds(pl.multiple_of((1 - upper_ref[0]) * size, size), size)
    out_ref[...] = keep_ref[mine, :] + arrived_ref[mine, :].astype(f32)
    send_ref[...] = (keep_ref[other, :] + arrived_ref[other, :].astype(f32)).astype(bf16)


def folded(upper, keep, arrived):
    rows, width = keep.shape
    return pl.pallas_call(
        fold_kernel,
        in_specs=[pl.BlockSpec(memory_space=pltpu.SMEM)]
        + [pl.BlockSpec(memory_space=pltpu.VMEM)] * 2,
        out_shape=[jax.ShapeDtypeStruct((rows // 2, width), kind) for kind in (f32, bf16)],
        cost_estimate=tiny_cost,
        name="folded",
    )(upper, keep, arrived)


def quarter_kernel(
    place_ref,
    own_ref,
    near_ref,
    far_ref,
    normed_0,
    normed_1,
    normed_2,
    normed_3,
    small_ref,
    arrived_ref,
    *rest,
):
    keep_ref, *sends_refs, piece, small = rest[-6:]
    total = None
    tokens = own_ref.shape[0]
    grads = (own_ref[...], near_ref[...], far_ref[:tokens, :], far_ref[tokens:, :])
    for left, right in zip((normed_0, normed_1, normed_2, normed_3), grads):
        part = lax.dot_general(left[...], right, contract_first, preferred_element_type=f32)
        total = part if total is None else total + part
    piece[...] = total
    small[...] = small_ref[...] + arrived_ref[...].astype(f32)
    rows, spare = piece.shape[0] // 4, small.shape[0] // 4
    for n in range(4):
        block = place_ref[0] ^ n
        inner_rows = piece[pl.ds(pl.multiple_of(block * rows, rows), rows), :]
        small_rows = small[pl.ds(pl.multiple_of(block * spare, spare), spare), :]
        if n == 0:
            keep_ref[:rows, :] = inner_rows
            keep_ref[rows:, :] = small_rows
        else:
            sends_refs[n - 1][:rows, :] = inner_rows.astype(bf16)
            sends_refs[n - 1][rows:, :] = small_rows.astype(bf16)


def inner_quarter(place, own, near, far, normed, smalls, waits):
    width = own.shape[1]
    quarter = normed[0].shape[1]
    spare = smalls[0].shape[0]
    rows = (quarter + spare) // 4
    return pl.pallas_call(
        quarter_kernel,
        in_specs=[pl.BlockSpec(memory_space=pltpu.SMEM)]
        + [pl.BlockSpec(memory_space=pltpu.VMEM)] * 9
        + [pl.BlockSpec(memory_space=pl.ANY)] * len(waits),
        out_shape=[jax.ShapeDtypeStruct((rows, width), f32)]
        + [jax.ShapeDtypeStruct((rows, width), bf16)] * 3,
        scratch_shapes=[pltpu.VMEM((quarter, width), f32), pltpu.VMEM((spare, width), f32)],
        compiler_params=pltpu.CompilerParams(vmem_limit_bytes=vmem_bytes),
        cost_estimate=tiny_cost,
        name="inner_quarter",
    )(place, own, near, far, *normed, *smalls, *waits)


def put_quarter(out_ref, gate_ref, inner_ref):
    rows = out_ref.shape[0] // 4
    out_ref[:, 1, :] = gate_ref[...].astype(f32)
    for n in range(4):
        at = n * (rows + block_rows)
        out_ref[n * rows : (n + 1) * rows, 0, :] = inner_ref[at : at + rows, :].astype(f32)


def join_kernel(place_ref, gate_ref, low_ref, *rest, small_rows):
    held = rest[:4]
    out_ref, wide_ref, *row_refs, gain_ref, blocks = rest[4:]
    wide_ref[...] = low_ref[...].astype(f32)
    rows = out_ref.shape[0] // 4
    for flip, ref in enumerate(held):

        @pl.when(pl.program_id(0) == flip)
        def _():
            put_quarter(out_ref, gate_ref, ref)
            number = place_ref[0] ^ flip
            number = (number & 1) * 2 + number // 2
            for n in range(4):
                at = (number * 4 + n) * block_rows
                taken = ref[(n + 1) * rows + n * block_rows : (n + 1) * (rows + block_rows), :]
                blocks[pl.ds(pl.multiple_of(at, block_rows), block_rows), :] = taken.astype(f32)

    @pl.when(pl.program_id(0) == 3)
    def _():
        for ref, start in zip(row_refs, small_rows):
            for row in range(ref.shape[0]):
                at = (start + row) // used_rows * block_rows + (start + row) % used_rows
                ref[row : row + 1, :] = blocks[at : at + 1, :]
        gain_ref[...] = sum(
            blocks[n * block_rows + used_rows : n * block_rows + used_rows + 1, :] for n in range(16)
        )


def joined(place, gate, low, held, small_rows, small_counts):
    depth, width = gate.shape
    quarter = depth // 4
    whole = pl.BlockSpec(held[0].shape, lambda j, place: (0, 0))
    part = pl.BlockSpec((quarter, width), lambda j, place: (j, 0))
    return pl.pallas_call(
        functools.partial(join_kernel, small_rows=small_rows),
        grid_spec=pltpu.PrefetchScalarGridSpec(
            num_scalar_prefetch=1,
            grid=(4,),
            in_specs=[pl.BlockSpec((quarter, width), lambda j, place: (place[0] ^ j, 0)), part]
            + [whole] * 4,
            out_specs=[
                pl.BlockSpec((quarter, 2, width), lambda j, place: (place[0] ^ j, 0, 0)),
                part,
            ]
            + [pl.BlockSpec((rows, width), lambda j, place: (0, 0)) for rows in small_counts],
            scratch_shapes=[pltpu.VMEM((16 * block_rows, width), f32)],
        ),
        out_shape=[
            jax.ShapeDtypeStruct((depth, 2, width), f32),
            jax.ShapeDtypeStruct(low.shape, f32),
        ]
        + [jax.ShapeDtypeStruct((rows, width), f32) for rows in small_counts],
        compiler_params=pltpu.CompilerParams(vmem_limit_bytes=vmem_bytes),
        cost_estimate=tiny_cost,
        name="joined",
    )(place, gate, low, *held)


def through(decay, total):
    return jnp.exp(decay * total)


def round_kernel(second_ref, decay_log_ref, own_ref, other_ref, *rest, first):
    count, width = decay_log_ref.shape
    new_passed_ref, *ends_refs = rest if first else rest[1:]
    decay = -jnp.exp(decay_log_ref[...])
    second = second_ref[0] > 0
    own, other = get_ends(own_ref, count), get_ends(other_ref, count)
    early = [jnp.where(second, b, a) for a, b in zip(own, other)]
    late = [jnp.where(second, a, b) for a, b in zip(own, other)]
    state = late[0] + through(decay, late[2]) * early[0]
    adjoint = early[1] + through(decay, early[2]) * late[1]
    if len(ends_refs) == 2:
        ends_refs[0][...] = state.astype(bf16)
        ends_refs[1][...] = adjoint.astype(bf16)
    else:
        put_ends(ends_refs[0], state, adjoint, early[2] + late[2])
    if first:
        before = after = jnp.zeros((count, width), f32)
        before_steps = after_steps = jnp.zeros((1, width), f32)
    else:
        before, after = rest[0][:count], rest[0][count : 2 * count]
        before_steps = rest[0][2 * count : 2 * count + 1]
        after_steps = rest[0][2 * count + 1 : 2 * count + 2]
    new_passed_ref[:count, :] = before + jnp.where(second, through(decay, before_steps) * other[0], 0.0)
    new_passed_ref[count : 2 * count, :] = after + jnp.where(
        second, 0.0, through(decay, after_steps) * other[1]
    )
    new_passed_ref[2 * count : 2 * count + 1, :] = before_steps + jnp.where(second, other[2], 0.0)
    new_passed_ref[2 * count + 1 : 2 * count + 2, :] = after_steps + jnp.where(second, 0.0, other[2])


def carried(ends, decay_log):
    count, width = decay_log.shape
    place = lax.axis_index("wide").astype(jnp.int32)
    state = jax.ShapeDtypeStruct((count, width), bf16)
    passed_kind = jax.ShapeDtypeStruct((2 * count + 8, width), f32)
    packed, passed = ends, []
    vmem = pl.BlockSpec(memory_space=pltpu.VMEM)
    for k, kinds in enumerate(([jax.ShapeDtypeStruct(ends.shape, bf16)], [state, state])):
        new_passed, *out = pl.pallas_call(
            functools.partial(round_kernel, first=k == 0),
            in_specs=[pl.BlockSpec(memory_space=pltpu.SMEM)] + [vmem] * (3 + k),
            out_shape=[passed_kind] + kinds,
            cost_estimate=tiny_cost,
            name="carry_round",
        )((place >> k & 1)[None], decay_log, packed, swapped(packed, "wide", 2**k), *passed)
        packed, passed = out[0], [new_passed]
    from_before = passed_along(out[0], "wide", 4)
    from_after = passed_along(out[1], "wide", -4)
    return passed[0], from_before, from_after


def local(
    tokens,
    norm_gain,
    in_weight,
    conv_weight,
    conv_bias,
    select_weight,
    step_weight,
    step_bias,
    decay_log,
    skip_gain,
    out_weight,
    segment_ids,
    cotangent,
):
    rows, features = tokens.shape
    taps = conv_weight.shape[0]
    columns = select_weight.shape[0]
    rank = step_weight.shape[0]
    count = decay_log.shape[0]
    right_half = lax.axis_index("narrow") == 1

    def both_halves(own, other):
        return jnp.concatenate(
            [jnp.where(right_half, other, own), jnp.where(right_half, own, other)], axis=1
        )

    other_tokens = swapped(tokens, "narrow", 1)
    other_cot = swapped(cotangent, "narrow", 1)
    edge, other_edge = to_next_both(edge_rows_of(segment_ids, tokens))

    whole_low, normed_ext, normed, inverse, masks = normalized(
        tokens, other_tokens, edge, other_edge, norm_gain[None], segment_ids[None]
    )
    projected = jnp.einsum(
        "td,dce->cte", normed_ext, in_weight, preferred_element_type=f32
    ).astype(bf16)
    convolved, act, selected = convolve(
        projected, conv_weight, conv_bias[None], select_weight, masks
    )
    other_selected = swapped(selected, "narrow", 1)
    cot_whole = both_halves(cotangent, other_cot)
    gated_grad = lax.dot_general(
        cot_whole, out_weight, contract_last, preferred_element_type=f32
    )
    step_pre, step, ends = scan_ends(
        selected,
        other_selected,
        step_weight,
        step_bias[None],
        act,
        projected,
        gated_grad,
        masks,
        decay_log,
    )
    passed, entering, returning = carried(ends, decay_log)
    gated, gate_grad, out_product, gate_product, entry = scan_forward(
        selected,
        other_selected,
        step,
        act,
        projected,
        gated_grad,
        masks,
        decay_log,
        passed,
        entering,
        skip_gain[None],
        cot_whole,
        normed,
    )
    products = (after(out_product, returning), gate_product)
    out_sum, gate_sum = lax.psum(products, "wide")
    wide_place = lax.axis_index("wide").astype(jnp.int32)
    four_place = (wide_place & 3)[None]

    def narrow_halves(array):
        low, high = array[:, :features], array[:, features:]
        return jnp.where(right_half, high, low), jnp.where(right_half, low, high)

    def after_forward(products):
        whole = whole_low.astype(f32)
        act_grad, select_grad, scan_small = scan_backward(
            selected,
            other_selected,
            step_pre,
            step,
            act,
            projected,
            gated_grad,
            masks,
            decay_log,
            entry,
            passed,
            returning,
            skip_gain[None],
            step_weight,
        )
        normed_four = quarter_of_four(after(normed, select_grad))
        inner_main, before, last, conv_small = convolve_grad(
            select_grad,
            swapped(select_grad, "narrow", 1),
            select_weight,
            act_grad,
            convolved,
            act,
            projected,
            conv_weight,
            masks,
            [],
        )
        following = passed_along(before, "wide", -1)
        inner_grad = patched(segment_ids, inner_main, last, following, *normed_four)
        near = swapped(inner_grad, "wide", 2)
        keep, send = small_halves(wide_place[None] & 1, scan_small, conv_small, inner_grad)
        keep, send = folded((wide_place >> 1 & 1)[None], keep, swapped(send, "wide", 1))
        smalls = [keep, swapped(send, "wide", 2)]
        normed_part = jnp.einsum(
            "cte,dce->td", jnp.stack([inner_grad, gate_grad]), in_weight, preferred_element_type=f32
        )
        gain_part = jnp.sum(normed_part * whole * inverse, axis=0, keepdims=True)
        row_part = jnp.sum(normed_part * norm_gain * whole, axis=1)[None]
        first_bits, *more_bits = group_bits(2)
        narrow_sums = jnp.concatenate([gain_part, row_part], axis=1)
        narrow_sums = narrow_sums + swapped(narrow_sums, "narrow", 1)
        gain_sum = narrow_sums[:, : 2 * features]
        for bit in (bit for bits in more_bits for bit in bits):
            gain_sum = gain_sum + swapped(gain_sum, "wide", bit)
        normed_mine, normed_other = narrow_halves(normed_part)
        normed_theirs = swapped(normed_other, "narrow", 1)
        near = after(near, narrow_sums, smalls[1], normed_theirs)
        far = swapped(jnp.concatenate([inner_grad, near]), "wide", 1)
        keep, *sends = inner_quarter(
            (wide_place >> 2 & 3)[None],
            inner_grad,
            near,
            far,
            normed_four,
            smalls,
            [],
        )
        out_part = jnp.dot(after(gated, keep), out_weight, preferred_element_type=f32)
        out_mine, out_other = narrow_halves(out_part)
        out_theirs = swapped(out_other, "narrow", 1)
        layer_out = (tokens.astype(f32) + (out_mine + out_theirs)).astype(bf16)
        row_sum = narrow_sums[:, 2 * features :].reshape(rows, 1)
        gain_mine = jnp.where(right_half, norm_gain[features:], norm_gain[:features])
        whole_grad = inverse * (gain_mine * (normed_mine + normed_theirs)) - tokens.astype(f32) * (
            inverse * inverse * inverse
        ) * (row_sum / (2 * features))
        tokens_grad = (whole_grad + cotangent.astype(f32)).astype(bf16)
        held = keep
        for n, flip in enumerate(flips(first_bits)[1:]):
            held = held + swapped(sends[n], "wide", flip).astype(f32)
        for bits in more_bits:
            held = scattered(held, bits)
        held = held.astype(bf16)
        for bits in reversed(more_bits):
            held = gathered(held, bits)
        spare = jnp.broadcast_to(gain_sum, (block_rows - used_rows, gain_sum.shape[1]))
        held = jnp.concatenate([held[: held.shape[0] - spare.shape[0]], spare.astype(bf16)])
        held = gathered(held, first_bits)
        return held, layer_out, tokens_grad

    kinds = jax.eval_shape(after_forward, products)
    held, layer_out, tokens_grad = lax.cond(
        wide_place >= 0,
        after_forward,
        lambda pair: jax.tree.map(lambda kind: jnp.zeros(kind.shape, kind.dtype), kinds),
        products,
    )

    core = swapped(held, "wide", 1)
    near = swapped(held, "wide", 2)
    far = swapped(near, "wide", 1)
    conv_at = rank + count + 2
    (
        in_weight_grad,
        out_weight_grad,
        step_weight_grad,
        decay_log_grad,
        skip_gain_grad,
        step_bias_grad,
        select_weight_grad,
        conv_weight_grad,
        conv_bias_grad,
        norm_gain_grad,
    ) = joined(
        four_place,
        gate_sum,
        out_sum,
        (held, core, near, far),
        (0, rank, rank + count, rank + count + 1, conv_at, conv_at + columns, conv_at + columns + taps),
        (rank, count, 1, 1, columns, taps, 1, 1),
    )
    return (
        layer_out,
        tokens_grad,
        norm_gain_grad[0],
        in_weight_grad,
        conv_weight_grad,
        conv_bias_grad[0],
        select_weight_grad,
        step_weight_grad,
        step_bias_grad[0],
        decay_log_grad,
        skip_gain_grad[0],
        out_weight_grad,
    )


def solution(mesh):
    placed = (
        P("wide", "narrow"),
        P(),
        P(None, None, "narrow"),
        P(None, "narrow"),
        P("narrow"),
        P(None, "narrow"),
        P(None, "narrow"),
        P("narrow"),
        P(None, "narrow"),
        P("narrow"),
        P("narrow", None),
        P("wide"),
        P("wide", "narrow"),
    )
    return jax.shard_map(
        local,
        mesh=mesh,
        in_specs=placed,
        out_specs=(
            P("wide", "narrow"),
            P("wide", "narrow"),
            P(),
            P(None, None, "narrow"),
            P(None, "narrow"),
            P("narrow"),
            P(None, "narrow"),
            P(None, "narrow"),
            P("narrow"),
            P(None, "narrow"),
            P("narrow"),
            P("narrow", None),
        ),
        check_vma=False,
    )
```

```python
import functools

import jax
import jax.numpy as jnp
from jax import lax
from jax.experimental import pallas as pl
from jax.experimental.pallas import tpu as pltpu
from jax.sharding import PartitionSpec as P

epsilon = 1e-05
log2e = 1.4426950408889634
reset_step = 1e30
lanes = 128
halo = 16
body_rows = 32
scan_width = 512
vmem_bytes = 56 * 1024 * 1024
tiny_cost = pl.CostEstimate(flops=1, bytes_accessed=1, transcendentals=0)
f32 = jnp.float32
bf16 = jnp.bfloat16
contract_first = (((0,), (0,)), ((), ()))
contract_last = (((1,), (1,)), ((), ()))


def passed_along(array, axis, by):
    peers = lax.axis_size(axis)
    pairs = [(i, i + by) for i in range(peers) if 0 <= i + by < peers]
    return lax.ppermute(array, axis, pairs)


def swapped(array, axis, bit):
    peers = lax.axis_size(axis)
    return lax.ppermute(array, axis, [(i, i ^ bit) for i in range(peers)])


def wide_bits():
    bit, bits = 1, []
    while bit < lax.axis_size("wide"):
        bits.append(bit)
        bit *= 2
    return bits


def to_next_both(array):
    count, sides = lax.axis_size("wide"), lax.axis_size("narrow")
    pairs = [
        (i * sides + k, (i + 1) * sides + (sides - 1 - k))
        for i in range(count - 1)
        for k in range(sides)
    ]
    return passed_along(array, "wide", 1), lax.ppermute(array, ("wide", "narrow"), pairs)


def is_upper(bit):
    return (lax.axis_index("wide") & bit) != 0


def group_bits(size):
    bits, bit = [], 4
    while bit < lax.axis_size("wide"):
        bits.append(bit)
        bit *= 2
    return [tuple(bits[k : k + size][::-1]) for k in range(0, len(bits), size)]


def flips(bits):
    return [sum(b for k, b in enumerate(bits) if n >> k & 1) for n in range(2 ** len(bits))]


def scattered(piece, bits):
    rows = piece.shape[0] // 2 ** len(bits)
    here = sum(is_upper(b).astype(jnp.int32) << k for k, b in enumerate(bits))

    def block(n):
        return lax.dynamic_slice_in_dim(piece, (here ^ n) * rows, rows, 0)

    total = block(0).astype(f32)
    for n, flip in enumerate(flips(bits)):
        if n > 0:
            total = total + swapped(block(n).astype(bf16), "wide", flip).astype(f32)
    return total


def gathered(held, bits):
    blocks = [held] + [swapped(held, "wide", flip) for flip in flips(bits)[1:]]
    for bit in bits:
        upper = is_upper(bit)
        blocks = [
            jnp.concatenate([jnp.where(upper, b, a), jnp.where(upper, a, b)])
            for a, b in zip(blocks[0::2], blocks[1::2])
        ]
    return blocks[0]


def quarter_of_four(array):
    width = array.shape[1] // 4
    here = lax.axis_index("wide") & 3

    def quarter(n):
        return lax.dynamic_slice_in_dim(array, (here ^ n) * width, width, 1)

    return [quarter(0)] + [swapped(quarter(n), "wide", n) for n in (2, 1, 3)]


def silu_slope(values):
    logistic = jax.nn.sigmoid(values)
    return logistic * (1.0 + values * (1.0 - logistic))


def softplus(values):
    return jnp.maximum(values, 0.0) + jnp.log1p(jnp.exp(-jnp.abs(values)))


def column_spec(rows, start=0):
    return pl.BlockSpec((rows, scan_width), lambda j: (0, start + j))


def part_spec(part, rows, start=0):
    return pl.BlockSpec((None, rows, scan_width), lambda j: (part, 0, start + j))


def whole_spec(rows, width):
    return pl.BlockSpec((rows, width), lambda j: (0, 0))


def call(kernel, name, width, in_specs, out_specs, out_shape, scratch, *operands):
    return pl.pallas_call(
        kernel,
        grid=(width // scan_width,),
        in_specs=in_specs,
        out_specs=out_specs,
        out_shape=out_shape,
        scratch_shapes=scratch,
        compiler_params=pltpu.CompilerParams(vmem_limit_bytes=vmem_bytes),
        cost_estimate=tiny_cost,
        name=name,
    )(*operands)


def conv_kernel(
    inner_ref,
    conv_weight_ref,
    conv_bias_ref,
    select_ref,
    mask_ref,
    convolved_ref,
    act_ref,
    selected_ref,
    inner,
):
    rows = act_ref.shape[0]
    taps = conv_weight_ref.shape[0]
    inner[:halo, :] = inner_ref[rows:, :].astype(f32)
    inner[halo:, :] = inner_ref[:rows, :].astype(f32)
    total = conv_bias_ref[...] + conv_weight_ref[taps - 1 :, :] * inner[halo:, :]
    for lag in range(1, taps):
        earlier = inner[pl.ds(halo - lag, rows), :] * mask_ref[:, lag : lag + 1]
        total = total + conv_weight_ref[taps - 1 - lag : taps - lag, :] * earlier
    convolved_ref[...] = total
    act = (total * jax.nn.sigmoid(total)).astype(bf16)
    act_ref[...] = act
    part = lax.dot_general(select_ref[...], act, contract_last, preferred_element_type=f32)

    @pl.when(pl.program_id(0) == 0)
    def _():
        selected_ref[...] = part

    @pl.when(pl.program_id(0) > 0)
    def _():
        selected_ref[...] += part


def convolve(projected, conv_weight, conv_bias, select_weight, masks):
    parts, extended, width = projected.shape
    rows = extended - halo
    taps = conv_weight.shape[0]
    columns = select_weight.shape[0]
    return call(
        conv_kernel,
        "convolve",
        width,
        [
            part_spec(0, extended),
            column_spec(taps),
            column_spec(1),
            column_spec(columns),
            whole_spec(rows, masks.shape[1]),
        ],
        [column_spec(rows), column_spec(rows), whole_spec(columns, rows)],
        [
            jax.ShapeDtypeStruct((rows, width), f32),
            jax.ShapeDtypeStruct((rows, width), bf16),
            jax.ShapeDtypeStruct((columns, rows), f32),
        ],
        [pltpu.VMEM((extended, scan_width), f32)],
        projected,
        conv_weight,
        conv_bias,
        select_weight,
        masks,
    )


def coef_columns(coef, block):
    per_tile = lanes // body_rows
    start = pl.multiple_of((block // per_tile) * lanes, lanes)
    tile = coef[:, pl.ds(start, lanes)]
    back = body_rows * lax.rem(block, per_tile)
    return pltpu.roll(tile, lax.rem(lanes - back, lanes), 1)


def put_ends(ends_ref, state, adjoint, total):
    count, width = state.shape
    ends_ref[:count, :] = state.astype(bf16)
    ends_ref[count : 2 * count, :] = adjoint.astype(bf16)
    high = total.astype(bf16).astype(f32)
    upper = lax.broadcasted_iota(jnp.int32, (16, width), 0) < 8
    ends_ref[2 * count :, :] = jnp.where(upper, high, total - high).astype(bf16)


def get_ends(ends_ref, count):
    total = ends_ref[2 * count :].astype(f32)
    return (
        ends_ref[:count].astype(f32),
        ends_ref[count : 2 * count].astype(f32),
        total[:1] + total[8:9],
    )


def ends_kernel(
    selected_ref,
    other_ref,
    step_weight_ref,
    step_bias_ref,
    act_ref,
    gate_ref,
    gated_grad_ref,
    mask_ref,
    decay_log_ref,
    step_pre_ref,
    step_ref,
    ends_ref,
    coef,
    held_step,
    drive,
    scan_grad,
):
    rows = act_ref.shape[0]
    count = decay_log_ref.shape[0]
    rank = step_weight_ref.shape[0]
    decay2 = -jnp.exp(decay_log_ref[...]) * log2e
    selected = selected_ref[...] + other_ref[...]
    coef[...] = selected[rank:, :]
    step_low = selected[:rank, :].astype(bf16)
    step_pre = step_bias_ref[...] + lax.dot_general(
        step_low, step_weight_ref[...], contract_first, preferred_element_type=f32
    )
    step_pre_ref[...] = step_pre
    step = softplus(step_pre)
    step_ref[...] = step
    held_step[...] = jnp.where(mask_ref[:, 1:2] > 0.0, step, reset_step)
    drive[...] = step * act_ref[...].astype(f32)
    gate = gate_ref[...].astype(f32)
    scan_grad[...] = gated_grad_ref[...] * (gate * jax.nn.sigmoid(gate))
    zero = jnp.zeros(decay2.shape, f32)

    def body(block, carried):
        state, product, adjoint = carried
        columns = coef_columns(coef, block)
        for i in range(body_rows):
            row = pl.ds(block * body_rows + i, 1)
            factor = jnp.exp2(held_step[row, :] * decay2)
            state = factor * state + columns[:count, i : i + 1] * drive[row, :]
            product = factor * product
            adjoint = adjoint + product * (columns[count:, i : i + 1] * scan_grad[row, :])
        return state, product, adjoint

    state, product, adjoint = lax.fori_loop(0, rows // body_rows, body, (zero, zero + 1.0, zero))
    put_ends(ends_ref, state, adjoint, jnp.sum(held_step[...], axis=0, keepdims=True))


def scan_ends(
    selected, other, step_weight, step_bias, act, projected, gated_grad, masks, decay_log
):
    rows, width = act.shape
    count = decay_log.shape[0]
    columns = selected.shape[0]
    rank = step_weight.shape[0]
    return call(
        ends_kernel,
        "scan_ends",
        width,
        [
            whole_spec(columns, rows),
            whole_spec(columns, rows),
            column_spec(rank),
            column_spec(1),
            column_spec(rows),
            part_spec(1, rows),
            column_spec(rows),
            whole_spec(rows, masks.shape[1]),
            column_spec(count),
        ],
        [column_spec(rows), column_spec(rows), column_spec(2 * count + 16)],
        [
            jax.ShapeDtypeStruct((rows, width), f32),
            jax.ShapeDtypeStruct((rows, width), f32),
            jax.ShapeDtypeStruct((2 * count + 16, width), bf16),
        ],
        [pltpu.VMEM((2 * count, rows), f32)] + [pltpu.VMEM((rows, scan_width), f32)] * 3,
        selected,
        other,
        step_weight,
        step_bias,
        act,
        projected,
        gated_grad,
        masks,
        decay_log,
    )


def lane_tiles(values):
    return [values[:, k : k + lanes] for k in range(0, values.shape[1], lanes)]


def tree_sum(parts):
    while len(parts) > 1:
        odd = parts[len(parts) // 2 * 2 :]
        parts = [a + b for a, b in zip(parts[0::2], parts[1::2])] + odd
    return parts[0]


def keep_halves(scratch, i, values):
    for k, tile in enumerate(lane_tiles(values)):
        at = (k * body_rows + i) * 8
        scratch[at : at + 8, :] = tile[:8] + tile[8:]


def put_state_sums(scratch, out_ref, block):
    for group in range(body_rows // 8):
        row = pl.ds(pl.multiple_of(block * body_rows + group * 8, 8), 8)
        for k in range(out_ref.shape[1] // lanes):
            at = (k * body_rows + group * 8) * 8
            total = tree_sum([scratch[pl.ds(at + n, 8, stride=8), :] for n in range(8)])
            out_ref[row, k * lanes : (k + 1) * lanes] = total


def lane_sums(values):
    ones = jnp.ones((8, lanes), bf16)
    high = values.astype(bf16)
    low = (values - high.astype(f32)).astype(bf16)
    total = lax.dot_general(ones, high, contract_last, preferred_element_type=f32)
    total += lax.dot_general(ones, low, contract_last, preferred_element_type=f32)
    return total[:1, :]


def at_token(t, count):
    return pl.ds(pl.multiple_of(t * count, count), count)


def forward_kernel(
    selected_ref,
    other_ref,
    step_ref,
    act_ref,
    gate_ref,
    gated_grad_ref,
    mask_ref,
    decay_log_ref,
    passed_ref,
    entering_ref,
    skip_ref,
    cot_ref,
    normed_ref,
    gated_ref,
    gate_grad_ref,
    out_product_ref,
    gate_product_ref,
    entry_ref,
    coef,
    held_step,
    drive,
    scanned,
    halves,
):
    rows = step_ref.shape[0]
    count = decay_log_ref.shape[0]
    rank = selected_ref.shape[0] - 2 * count
    decay = -jnp.exp(decay_log_ref[...])
    decay2 = decay * log2e
    before_steps = passed_ref[2 * count : 2 * count + 1, :]
    entry = passed_ref[:count, :] + through(decay, before_steps) * entering_ref[...].astype(f32)
    entry_ref[...] = entry
    coef[...] = selected_ref[rank:, :] + other_ref[rank:, :]
    act = act_ref[...].astype(f32)
    held_step[...] = jnp.where(mask_ref[:, 1:2] > 0.0, step_ref[...], reset_step)
    drive[...] = step_ref[...] * act

    def forward(block, state):
        columns = coef_columns(coef, block)
        for i in range(body_rows):
            row = pl.ds(block * body_rows + i, 1)
            factor = jnp.exp2(held_step[row, :] * decay2)
            state = factor * state + columns[:count, i : i + 1] * drive[row, :]
            keep_halves(halves, i, columns[count:, i : i + 1] * state)
        put_state_sums(halves, scanned, block)
        return state

    lax.fori_loop(0, rows // body_rows, forward, entry)
    gate = gate_ref[...].astype(f32)
    logistic = jax.nn.sigmoid(gate)
    total = scanned[...] + skip_ref[...] * act
    gated = (total * (gate * logistic)).astype(bf16)
    gated_ref[...] = gated
    out_product_ref[...] = lax.dot_general(
        gated, cot_ref[...], contract_first, preferred_element_type=f32
    ).astype(bf16)
    slope = logistic * (1.0 + gate * (1.0 - logistic))
    gate_grad = (gated_grad_ref[...] * total * slope).astype(bf16)
    gate_grad_ref[...] = gate_grad
    gate_product_ref[...] = lax.dot_general(
        normed_ref[...], gate_grad, contract_first, preferred_element_type=f32
    ).astype(bf16)


def scan_forward(
    selected,
    other,
    step,
    act,
    projected,
    gated_grad,
    masks,
    decay_log,
    passed,
    entering,
    skip_gain,
    cot,
    normed,
):
    rows, width = step.shape
    count = decay_log.shape[0]
    columns = selected.shape[0]
    return call(
        forward_kernel,
        "scan_forward",
        width,
        [
            whole_spec(columns, rows),
            whole_spec(columns, rows),
            column_spec(rows),
            column_spec(rows),
            part_spec(1, rows),
            column_spec(rows),
            whole_spec(rows, masks.shape[1]),
            column_spec(count),
            column_spec(2 * count + 8),
            column_spec(count),
            column_spec(1),
            whole_spec(*cot.shape),
            whole_spec(*normed.shape),
        ],
        [
            column_spec(rows),
            column_spec(rows),
            pl.BlockSpec((scan_width, cot.shape[1]), lambda j: (j, 0)),
            column_spec(normed.shape[1]),
            column_spec(count),
        ],
        [
            jax.ShapeDtypeStruct((rows, width), bf16),
            jax.ShapeDtypeStruct((rows, width), bf16),
            jax.ShapeDtypeStruct((width, cot.shape[1]), bf16),
            jax.ShapeDtypeStruct((normed.shape[1], width), bf16),
            jax.ShapeDtypeStruct((count, width), f32),
        ],
        [pltpu.VMEM((2 * count, rows), f32)]
        + [pltpu.VMEM((rows, scan_width), f32)] * 3
        + [pltpu.VMEM((8 * body_rows * (scan_width // lanes), lanes), f32)],
        selected,
        other,
        step,
        act,
        projected,
        gated_grad,
        masks,
        decay_log,
        passed,
        entering,
        skip_gain,
        cot,
        normed,
    )


def backward_kernel(
    selected_ref,
    other_ref,
    step_pre_ref,
    step_ref,
    act_ref,
    gate_ref,
    gated_grad_ref,
    mask_ref,
    decay_log_ref,
    entry_ref,
    passed_ref,
    returning_ref,
    skip_ref,
    step_weight_ref,
    act_grad_ref,
    select_grad_ref,
    small_ref,
    coef,
    held_step,
    drive,
    scan_grad,
    weighted,
    held_sum,
    states,
    factors,
    halves,
    more_halves,
    in_sum,
    read_sum,
):
    rows = step_ref.shape[0]
    count = decay_log_ref.shape[0]
    rank = step_weight_ref.shape[0]
    blocks = rows // body_rows
    decay = -jnp.exp(decay_log_ref[...])
    decay2 = decay * log2e
    after_steps = passed_ref[2 * count + 1 : 2 * count + 2, :]
    tail = passed_ref[count : 2 * count, :] + through(decay, after_steps) * returning_ref[...].astype(f32)
    selected = selected_ref[...] + other_ref[...]
    coef[...] = selected[rank:, :]
    step_low = selected[:rank, :].astype(bf16)
    step = step_ref[...]
    act = act_ref[...].astype(f32)
    held_step[...] = jnp.where(mask_ref[:, 1:2] > 0.0, step, reset_step)
    drive[...] = step * act
    gate = gate_ref[...].astype(f32)
    grads = gated_grad_ref[...] * (gate * jax.nn.sigmoid(gate))
    scan_grad[...] = grads
    small_ref[rank + count : rank + count + 1, :] = jnp.sum(grads * act, axis=0, keepdims=True)
    states[:count, :] = entry_ref[...]

    @pl.when(pl.program_id(0) == 0)
    def _():
        in_sum[...] = jnp.zeros(in_sum.shape, f32)
        read_sum[...] = jnp.zeros(read_sum.shape, f32)
        select_grad_ref[...] = jnp.zeros(select_grad_ref.shape, f32)

    def forward(block, state):
        columns = coef_columns(coef, block)
        for i in range(body_rows):
            t = block * body_rows + i
            row = pl.ds(t, 1)
            factor = jnp.exp2(held_step[row, :] * decay2)
            state = factor * state + columns[:count, i : i + 1] * drive[row, :]
            factors[at_token(t, count), :] = factor
            states[at_token(t + 1, count), :] = state
        return state

    lax.fori_loop(0, blocks, forward, entry_ref[...])

    def backward(k, carried):
        adjoint, decay_grad = carried
        block = blocks - 1 - k
        columns = coef_columns(coef, block)
        for i in range(body_rows - 1, -1, -1):
            t = block * body_rows + i
            row = pl.ds(t, 1)
            here = at_token(t, count)
            grad = scan_grad[row, :]
            summed = columns[count:, i : i + 1] * grad + adjoint
            read_sum[here, :] += tree_sum(lane_tiles(grad * states[at_token(t + 1, count), :]))
            in_sum[here, :] += tree_sum(lane_tiles(summed * drive[row, :]))
            keep_halves(halves, i, summed * columns[:count, i : i + 1])
            adjoint = factors[here, :] * summed
            held = adjoint * states[here, :]
            decay_grad = decay_grad + held * step_ref[row, :]
            keep_halves(more_halves, i, held * decay)
        put_state_sums(halves, weighted, block)
        put_state_sums(more_halves, held_sum, block)
        return adjoint, decay_grad

    ignored, decay_grad = lax.fori_loop(
        0, blocks, backward, (tail, jnp.zeros(decay.shape, f32))
    )
    act_grad_ref[...] = step * weighted[...] + skip_ref[...] * scan_grad[...]
    step_grad = act * weighted[...] + held_sum[...]
    pre_grad = (step_grad * jax.nn.sigmoid(step_pre_ref[...])).astype(bf16)
    small_ref[:rank, :] = jnp.dot(step_low, pre_grad, preferred_element_type=f32)
    small_ref[rank : rank + count, :] = decay_grad * decay
    bias_grad = jnp.sum(pre_grad.astype(f32), axis=0, keepdims=True)
    small_ref[rank + count + 1 : rank + count + 2, :] = bias_grad
    select_grad_ref[:rank, :] += lax.dot_general(
        step_weight_ref[...], pre_grad, contract_last, preferred_element_type=f32
    )

    @pl.when(pl.program_id(0) == pl.num_programs(0) - 1)
    def _():
        for n in range(count):
            at = pl.ds(n, rows, stride=count)
            select_grad_ref[rank + n : rank + n + 1, :] = lane_sums(in_sum[at, :])
            select_grad_ref[rank + count + n : rank + count + n + 1, :] = lane_sums(read_sum[at, :])


def scan_backward(
    selected,
    other,
    step_pre,
    step,
    act,
    projected,
    gated_grad,
    masks,
    decay_log,
    entry,
    passed,
    returning,
    skip_gain,
    step_weight,
):
    rows, width = step.shape
    count = decay_log.shape[0]
    columns = selected.shape[0]
    rank = step_weight.shape[0]
    half_rows = 8 * body_rows * (scan_width // lanes)
    small = rank + count + 2
    return call(
        backward_kernel,
        "scan_backward",
        width,
        [
            whole_spec(columns, rows),
            whole_spec(columns, rows),
            column_spec(rows),
            column_spec(rows),
            column_spec(rows),
            part_spec(1, rows),
            column_spec(rows),
            whole_spec(rows, masks.shape[1]),
            column_spec(count),
            column_spec(count),
            column_spec(2 * count + 8),
            column_spec(count),
            column_spec(1),
            column_spec(rank),
        ],
        [column_spec(rows), whole_spec(columns, rows), column_spec(small)],
        [
            jax.ShapeDtypeStruct((rows, width), f32),
            jax.ShapeDtypeStruct((columns, rows), f32),
            jax.ShapeDtypeStruct((small, width), f32),
        ],
        [pltpu.VMEM((2 * count, rows), f32)]
        + [pltpu.VMEM((rows, scan_width), f32)] * 5
        + [
            pltpu.VMEM(((rows + 1) * count, scan_width), f32),
            pltpu.VMEM((rows * count, scan_width), f32),
            pltpu.VMEM((half_rows, lanes), f32),
            pltpu.VMEM((half_rows, lanes), f32),
            pltpu.VMEM((rows * count, lanes), f32),
            pltpu.VMEM((rows * count, lanes), f32),
        ],
        selected,
        other,
        step_pre,
        step,
        act,
        projected,
        gated_grad,
        masks,
        decay_log,
        entry,
        passed,
        returning,
        skip_gain,
        step_weight,
    )


def conv_grad_kernel(
    select_grad_ref,
    other_ref,
    select_ref,
    act_grad_ref,
    convolved_ref,
    act_ref,
    inner_ref,
    conv_weight_ref,
    mask_ref,
    *rest,
):
    inner_grad_ref, before_ref, last_ref, small_ref, inner, shifted = rest[-6:]
    rows = act_ref.shape[0]
    taps = conv_weight_ref.shape[0]
    columns = select_ref.shape[0]
    select_grad = (select_grad_ref[...] + other_ref[...]).astype(bf16)
    total = act_grad_ref[...] + lax.dot_general(
        select_grad, select_ref[...], contract_first, preferred_element_type=f32
    )
    conv_grad = total * silu_slope(convolved_ref[...])
    small_ref[:columns, :] = jnp.dot(select_grad, act_ref[...], preferred_element_type=f32)
    inner[:halo, :] = inner_ref[rows:, :].astype(f32)
    inner[halo:, :] = inner_ref[:rows, :].astype(f32)
    edges = jnp.zeros((8, conv_grad.shape[1]), f32)
    shifted[:8, :] = edges
    shifted[rows + 8 :, :] = edges
    out = conv_weight_ref[taps - 1 :, :] * conv_grad
    before = edges
    small_ref[columns + taps - 1 : columns + taps, :] = jnp.sum(
        conv_grad * inner[halo:, :], axis=0, keepdims=True
    )
    for lag in range(1, taps):
        masked = conv_grad * mask_ref[:, lag : lag + 1]
        at = taps - 1 - lag
        small_ref[columns + at : columns + at + 1, :] = jnp.sum(
            masked * inner[pl.ds(halo - lag, rows), :], axis=0, keepdims=True
        )
        shifted[8 : rows + 8, :] = masked
        weight = conv_weight_ref[at : at + 1, :]
        out = out + weight * shifted[pl.ds(8 + lag, rows), :]
        before = before + weight * shifted[pl.ds(lag, 8), :]
    small_ref[columns + taps : columns + taps + 1, :] = jnp.sum(conv_grad, axis=0, keepdims=True)
    inner_grad_ref[...] = out.astype(bf16)
    before_ref[...] = before
    last_ref[...] = out[rows - 8 :, :]


def convolve_grad(
    select_grad, other, select_weight, act_grad, convolved, act, projected, conv_weight, masks, waits
):
    rows, width = act.shape
    extended = rows + halo
    columns = select_weight.shape[0]
    taps = conv_weight.shape[0]
    small = columns + taps + 1
    return call(
        conv_grad_kernel,
        "convolve_grad",
        width,
        [
            whole_spec(columns, rows),
            whole_spec(columns, rows),
            column_spec(columns),
            column_spec(rows),
            column_spec(rows),
            column_spec(rows),
            part_spec(0, extended),
            column_spec(taps),
            whole_spec(rows, masks.shape[1]),
        ]
        + [pl.BlockSpec(memory_space=pl.ANY)] * len(waits),
        [column_spec(rows), column_spec(8), column_spec(8), column_spec(small)],
        [
            jax.ShapeDtypeStruct((rows, width), bf16),
            jax.ShapeDtypeStruct((8, width), f32),
            jax.ShapeDtypeStruct((8, width), f32),
            jax.ShapeDtypeStruct((small, width), f32),
        ],
        [pltpu.VMEM((extended, scan_width), f32), pltpu.VMEM((rows + 16, scan_width), f32)],
        select_grad,
        other,
        select_weight,
        act_grad,
        convolved,
        act,
        projected,
        conv_weight,
        masks,
        *waits,
    )


def normalize_kernel(
    own_ref,
    other_ref,
    edge_ref,
    other_edge_ref,
    gain_ref,
    ids_ref,
    whole_ref,
    extended_ref,
    normed_ref,
    inverse_ref,
    mask_ref,
    rows_ref,
):
    rows, half = own_ref.shape
    ids = ids_ref[...].astype(f32)
    place = lax.broadcasted_iota(jnp.int32, ids.shape, 1)
    same = []
    for lag in range(8):
        earlier = jnp.where(place < lag, ids[:, :1], pltpu.roll(ids, lag, 1)) if lag else ids
        same.append(jnp.where(earlier == ids, 1.0, 0.0))
    spare = jnp.zeros((lanes - 8, rows), f32)
    mask_ref[...] = jnp.concatenate(same + [spare]).T
    right = lax.axis_index("narrow") == 1
    for at, own, other in ((0, own_ref, other_ref), (rows, edge_ref, other_edge_ref)):
        end = at + own.shape[0]
        rows_ref[at:end, :half] = jnp.where(right, other[...], own[...])
        rows_ref[at:end, half:] = jnp.where(right, own[...], other[...])
    whole_ref[...] = rows_ref[:rows, :]
    whole = rows_ref[...].astype(f32)
    inverse = lax.rsqrt(jnp.mean(whole * whole, axis=1, keepdims=True) + epsilon)
    normed = (whole * inverse * gain_ref[...]).astype(bf16)
    extended_ref[...] = normed
    normed_ref[...] = normed[:rows]
    inverse_ref[...] = inverse[:rows]


def normalized(own, other, edge, other_edge, gain, ids):
    rows, half = own.shape
    extended = rows + edge.shape[0]
    return pl.pallas_call(
        normalize_kernel,
        out_shape=[
            jax.ShapeDtypeStruct((rows, 2 * half), bf16),
            jax.ShapeDtypeStruct((extended, 2 * half), bf16),
            jax.ShapeDtypeStruct((rows, 2 * half), bf16),
            jax.ShapeDtypeStruct((rows, 1), f32),
            jax.ShapeDtypeStruct((rows, lanes), f32),
        ],
        scratch_shapes=[pltpu.VMEM((extended, 2 * half), bf16)],
        cost_estimate=tiny_cost,
        name="normalized",
    )(own, other, edge, other_edge, gain, ids)


def after(array, *waits):
    anywhere = pl.BlockSpec(memory_space=pl.ANY)
    return pl.pallas_call(
        lambda *refs: None,
        in_specs=[anywhere] * (1 + len(waits)),
        out_specs=anywhere,
        out_shape=jax.ShapeDtypeStruct(array.shape, array.dtype),
        input_output_aliases={0: 0},
        cost_estimate=tiny_cost,
        name="after",
    )(array, *waits)


def patch_kernel(ids_ref, rows_ref, last_ref, next_ref, *rest):
    count = ids_ref.shape[0]
    place = lax.broadcasted_iota(jnp.int32, (8, 1), 0)
    same = jnp.zeros((8, 1), f32)
    for lag in range(8):
        here = jnp.where(ids_ref[count - 1 - lag] == ids_ref[count - 1], 1.0, 0.0)
        same = same + jnp.where(place == 7 - lag, here, 0.0)
    total = last_ref[...] + next_ref[...] * same
    rows = rows_ref[...].astype(f32)
    rest[-1][...] = jnp.concatenate([rows[: halo - 8], total]).astype(bf16)


def patched(ids, grads, last, following, *waits):
    rows, width = grads.shape
    block = pl.BlockSpec((halo, width), lambda j: (rows // halo - 1, 0))
    edge = pl.BlockSpec((8, width), lambda j: (0, 0))
    return pl.pallas_call(
        patch_kernel,
        grid=(1,),
        in_specs=[pl.BlockSpec(memory_space=pltpu.SMEM), block, edge, edge]
        + [pl.BlockSpec(memory_space=pl.ANY)] * len(waits),
        out_specs=block,
        out_shape=jax.ShapeDtypeStruct((rows, width), bf16),
        input_output_aliases={1: 0},
        cost_estimate=tiny_cost,
        name="patched",
    )(ids, grads, last, following, *waits)


def edge_kernel(ids_ref, tokens_ref, out_ref):
    rows = ids_ref.shape[0]
    taps = 4
    out_ref[...] = tokens_ref[...]
    place = lax.broadcasted_iota(jnp.int32, (halo, 1), 0)
    same = jnp.zeros((halo, 1), f32)
    for lag in range(taps):
        here = jnp.where(ids_ref[rows - 1 - lag] == ids_ref[rows - 1], 1.0, 0.0)
        same = same + jnp.where(place == halo - 1 - lag, here, 0.0)
    out_ref[...] = (tokens_ref[...].astype(f32) * same).astype(bf16)


def edge_rows_of(ids, tokens):
    rows, width = tokens.shape
    return pl.pallas_call(
        edge_kernel,
        grid=(1,),
        in_specs=[
            pl.BlockSpec(memory_space=pltpu.SMEM),
            pl.BlockSpec((halo, width), lambda j: (rows // halo - 1, 0)),
        ],
        out_specs=pl.BlockSpec((halo, width), lambda j: (0, 0)),
        out_shape=jax.ShapeDtypeStruct((halo, width), bf16),
        cost_estimate=tiny_cost,
        name="edge_rows",
    )(ids, tokens)


block_rows, used_rows = 16, 12


def small_kernel(core_ref, scan_ref, conv_ref, wait_ref, keep_ref, send_ref, rows, blocks):
    rows[...] = jnp.zeros(rows.shape, f32)
    rows[: scan_ref.shape[0], :] = scan_ref[...]
    rows[scan_ref.shape[0] : scan_ref.shape[0] + conv_ref.shape[0], :] = conv_ref[...]
    blocks[...] = jnp.zeros(blocks.shape, f32)
    for n in range(16):
        blocks[n * block_rows : n * block_rows + used_rows, :] = rows[
            n * used_rows : (n + 1) * used_rows, :
        ]
    half = keep_ref.shape[0]
    mine = pl.ds(pl.multiple_of(core_ref[0] * half, half), half)
    other = pl.ds(pl.multiple_of((1 - core_ref[0]) * half, half), half)
    keep_ref[...] = blocks[mine, :]
    send_ref[...] = blocks[other, :].astype(bf16)


def small_halves(core, scan_small, conv_small, wait):
    width = scan_small.shape[1]
    return pl.pallas_call(
        small_kernel,
        in_specs=[pl.BlockSpec(memory_space=pltpu.SMEM)]
        + [pl.BlockSpec(memory_space=pltpu.VMEM)] * 2
        + [pl.BlockSpec(memory_space=pl.ANY)],
        out_shape=[jax.ShapeDtypeStruct((8 * block_rows, width), kind) for kind in (f32, bf16)],
        scratch_shapes=[
            pltpu.VMEM((16 * used_rows, width), f32),
            pltpu.VMEM((16 * block_rows, width), f32),
        ],
        cost_estimate=tiny_cost,
        name="small_halves",
    )(core, scan_small, conv_small, wait)


def fold_kernel(upper_ref, keep_ref, arrived_ref, out_ref, send_ref):
    size = out_ref.shape[0]
    mine = pl.ds(pl.multiple_of(upper_ref[0] * size, size), size)
    other = pl.ds(pl.multiple_of((1 - upper_ref[0]) * size, size), size)
    out_ref[...] = keep_ref[mine, :] + arrived_ref[mine, :].astype(f32)
    send_ref[...] = (keep_ref[other, :] + arrived_ref[other, :].astype(f32)).astype(bf16)


def folded(upper, keep, arrived):
    rows, width = keep.shape
    return pl.pallas_call(
        fold_kernel,
        in_specs=[pl.BlockSpec(memory_space=pltpu.SMEM)]
        + [pl.BlockSpec(memory_space=pltpu.VMEM)] * 2,
        out_shape=[jax.ShapeDtypeStruct((rows // 2, width), kind) for kind in (f32, bf16)],
        cost_estimate=tiny_cost,
        name="folded",
    )(upper, keep, arrived)


def quarter_kernel(
    place_ref,
    own_ref,
    near_ref,
    far_ref,
    normed_0,
    normed_1,
    normed_2,
    normed_3,
    small_ref,
    arrived_ref,
    *rest,
):
    keep_ref, *sends_refs, piece, small = rest[-6:]
    total = None
    tokens = own_ref.shape[0]
    grads = (own_ref[...], near_ref[...], far_ref[:tokens, :], far_ref[tokens:, :])
    for left, right in zip((normed_0, normed_1, normed_2, normed_3), grads):
        part = lax.dot_general(left[...], right, contract_first, preferred_element_type=f32)
        total = part if total is None else total + part
    piece[...] = total
    small[...] = small_ref[...] + arrived_ref[...].astype(f32)
    rows, spare = piece.shape[0] // 4, small.shape[0] // 4
    for n in range(4):
        block = place_ref[0] ^ n
        inner_rows = piece[pl.ds(pl.multiple_of(block * rows, rows), rows), :]
        small_rows = small[pl.ds(pl.multiple_of(block * spare, spare), spare), :]
        if n == 0:
            keep_ref[:rows, :] = inner_rows
            keep_ref[rows:, :] = small_rows
        else:
            sends_refs[n - 1][:rows, :] = inner_rows.astype(bf16)
            sends_refs[n - 1][rows:, :] = small_rows.astype(bf16)


def inner_quarter(place, own, near, far, normed, smalls, waits):
    width = own.shape[1]
    quarter = normed[0].shape[1]
    spare = smalls[0].shape[0]
    rows = (quarter + spare) // 4
    return pl.pallas_call(
        quarter_kernel,
        in_specs=[pl.BlockSpec(memory_space=pltpu.SMEM)]
        + [pl.BlockSpec(memory_space=pltpu.VMEM)] * 9
        + [pl.BlockSpec(memory_space=pl.ANY)] * len(waits),
        out_shape=[jax.ShapeDtypeStruct((rows, width), f32)]
        + [jax.ShapeDtypeStruct((rows, width), bf16)] * 3,
        scratch_shapes=[pltpu.VMEM((quarter, width), f32), pltpu.VMEM((spare, width), f32)],
        compiler_params=pltpu.CompilerParams(vmem_limit_bytes=vmem_bytes),
        cost_estimate=tiny_cost,
        name="inner_quarter",
    )(place, own, near, far, *normed, *smalls, *waits)


def put_quarter(out_ref, gate_ref, inner_ref):
    rows = out_ref.shape[0] // 4
    out_ref[:, 1, :] = gate_ref[...].astype(f32)
    for n in range(4):
        at = n * (rows + block_rows)
        out_ref[n * rows : (n + 1) * rows, 0, :] = inner_ref[at : at + rows, :].astype(f32)


def join_kernel(place_ref, gate_ref, low_ref, *rest, small_rows):
    held = rest[:4]
    out_ref, wide_ref, *row_refs, gain_ref, blocks = rest[4:]
    wide_ref[...] = low_ref[...].astype(f32)
    rows = out_ref.shape[0] // 4
    for flip, ref in enumerate(held):

        @pl.when(pl.program_id(0) == flip)
        def _():
            put_quarter(out_ref, gate_ref, ref)
            number = place_ref[0] ^ flip
            number = (number & 1) * 2 + number // 2
            for n in range(4):
                at = (number * 4 + n) * block_rows
                taken = ref[(n + 1) * rows + n * block_rows : (n + 1) * (rows + block_rows), :]
                blocks[pl.ds(pl.multiple_of(at, block_rows), block_rows), :] = taken.astype(f32)

    @pl.when(pl.program_id(0) == 3)
    def _():
        for ref, start in zip(row_refs, small_rows):
            for row in range(ref.shape[0]):
                at = (start + row) // used_rows * block_rows + (start + row) % used_rows
                ref[row : row + 1, :] = blocks[at : at + 1, :]
        gain_ref[...] = sum(
            blocks[n * block_rows + used_rows : n * block_rows + used_rows + 1, :] for n in range(16)
        )


def joined(place, gate, low, held, small_rows, small_counts):
    depth, width = gate.shape
    quarter = depth // 4
    whole = pl.BlockSpec(held[0].shape, lambda j, place: (0, 0))
    part = pl.BlockSpec((quarter, width), lambda j, place: (j, 0))
    return pl.pallas_call(
        functools.partial(join_kernel, small_rows=small_rows),
        grid_spec=pltpu.PrefetchScalarGridSpec(
            num_scalar_prefetch=1,
            grid=(4,),
            in_specs=[pl.BlockSpec((quarter, width), lambda j, place: (place[0] ^ j, 0)), part]
            + [whole] * 4,
            out_specs=[
                pl.BlockSpec((quarter, 2, width), lambda j, place: (place[0] ^ j, 0, 0)),
                part,
            ]
            + [pl.BlockSpec((rows, width), lambda j, place: (0, 0)) for rows in small_counts],
            scratch_shapes=[pltpu.VMEM((16 * block_rows, width), f32)],
        ),
        out_shape=[
            jax.ShapeDtypeStruct((depth, 2, width), f32),
            jax.ShapeDtypeStruct(low.shape, f32),
        ]
        + [jax.ShapeDtypeStruct((rows, width), f32) for rows in small_counts],
        compiler_params=pltpu.CompilerParams(vmem_limit_bytes=vmem_bytes),
        cost_estimate=tiny_cost,
        name="joined",
    )(place, gate, low, *held)


def through(decay, total):
    return jnp.exp(decay * total)


def round_kernel(second_ref, decay_log_ref, own_ref, other_ref, *rest, first):
    count, width = decay_log_ref.shape
    new_passed_ref, *ends_refs = rest if first else rest[1:]
    decay = -jnp.exp(decay_log_ref[...])
    second = second_ref[0] > 0
    own, other = get_ends(own_ref, count), get_ends(other_ref, count)
    early = [jnp.where(second, b, a) for a, b in zip(own, other)]
    late = [jnp.where(second, a, b) for a, b in zip(own, other)]
    state = late[0] + through(decay, late[2]) * early[0]
    adjoint = early[1] + through(decay, early[2]) * late[1]
    if len(ends_refs) == 2:
        ends_refs[0][...] = state.astype(bf16)
        ends_refs[1][...] = adjoint.astype(bf16)
    else:
        put_ends(ends_refs[0], state, adjoint, early[2] + late[2])
    if first:
        before = after = jnp.zeros((count, width), f32)
        before_steps = after_steps = jnp.zeros((1, width), f32)
    else:
        before, after = rest[0][:count], rest[0][count : 2 * count]
        before_steps = rest[0][2 * count : 2 * count + 1]
        after_steps = rest[0][2 * count + 1 : 2 * count + 2]
    new_passed_ref[:count, :] = before + jnp.where(second, through(decay, before_steps) * other[0], 0.0)
    new_passed_ref[count : 2 * count, :] = after + jnp.where(
        second, 0.0, through(decay, after_steps) * other[1]
    )
    new_passed_ref[2 * count : 2 * count + 1, :] = before_steps + jnp.where(second, other[2], 0.0)
    new_passed_ref[2 * count + 1 : 2 * count + 2, :] = after_steps + jnp.where(second, 0.0, other[2])


def carried(ends, decay_log):
    count, width = decay_log.shape
    place = lax.axis_index("wide").astype(jnp.int32)
    state = jax.ShapeDtypeStruct((count, width), bf16)
    passed_kind = jax.ShapeDtypeStruct((2 * count + 8, width), f32)
    packed, passed = ends, []
    vmem = pl.BlockSpec(memory_space=pltpu.VMEM)
    for k, kinds in enumerate(([jax.ShapeDtypeStruct(ends.shape, bf16)], [state, state])):
        new_passed, *out = pl.pallas_call(
            functools.partial(round_kernel, first=k == 0),
            in_specs=[pl.BlockSpec(memory_space=pltpu.SMEM)] + [vmem] * (3 + k),
            out_shape=[passed_kind] + kinds,
            cost_estimate=tiny_cost,
            name="carry_round",
        )((place >> k & 1)[None], decay_log, packed, swapped(packed, "wide", 2**k), *passed)
        packed, passed = out[0], [new_passed]
    from_before = passed_along(out[0], "wide", 4)
    from_after = passed_along(out[1], "wide", -4)
    return passed[0], from_before, from_after


def local(
    tokens,
    norm_gain,
    in_weight,
    conv_weight,
    conv_bias,
    select_weight,
    step_weight,
    step_bias,
    decay_log,
    skip_gain,
    out_weight,
    segment_ids,
    cotangent,
):
    rows, features = tokens.shape
    taps = conv_weight.shape[0]
    columns = select_weight.shape[0]
    rank = step_weight.shape[0]
    count = decay_log.shape[0]
    right_half = lax.axis_index("narrow") == 1

    def both_halves(own, other):
        return jnp.concatenate(
            [jnp.where(right_half, other, own), jnp.where(right_half, own, other)], axis=1
        )

    other_tokens = swapped(tokens, "narrow", 1)
    other_cot = swapped(cotangent, "narrow", 1)
    edge, other_edge = to_next_both(edge_rows_of(segment_ids, tokens))

    whole_low, normed_ext, normed, inverse, masks = normalized(
        tokens, other_tokens, edge, other_edge, norm_gain[None], segment_ids[None]
    )
    projected = jnp.einsum(
        "td,dce->cte", normed_ext, in_weight, preferred_element_type=f32
    ).astype(bf16)
    convolved, act, selected = convolve(
        projected, conv_weight, conv_bias[None], select_weight, masks
    )
    other_selected = swapped(selected, "narrow", 1)
    cot_whole = both_halves(cotangent, other_cot)
    gated_grad = lax.dot_general(
        cot_whole, out_weight, contract_last, preferred_element_type=f32
    )
    step_pre, step, ends = scan_ends(
        selected,
        other_selected,
        step_weight,
        step_bias[None],
        act,
        projected,
        gated_grad,
        masks,
        decay_log,
    )
    passed, entering, returning = carried(ends, decay_log)
    gated, gate_grad, out_product, gate_product, entry = scan_forward(
        selected,
        other_selected,
        step,
        act,
        projected,
        gated_grad,
        masks,
        decay_log,
        passed,
        entering,
        skip_gain[None],
        cot_whole,
        normed,
    )
    products = (after(out_product, returning), gate_product)
    out_sum, gate_sum = lax.psum(products, "wide")
    wide_place = lax.axis_index("wide").astype(jnp.int32)
    four_place = (wide_place & 3)[None]

    def narrow_halves(array):
        low, high = array[:, :features], array[:, features:]
        return jnp.where(right_half, high, low), jnp.where(right_half, low, high)

    def after_forward(products):
        whole = whole_low.astype(f32)
        act_grad, select_grad, scan_small = scan_backward(
            selected,
            other_selected,
            step_pre,
            step,
            act,
            projected,
            gated_grad,
            masks,
            decay_log,
            entry,
            passed,
            returning,
            skip_gain[None],
            step_weight,
        )
        normed_four = quarter_of_four(after(normed, select_grad))
        inner_main, before, last, conv_small = convolve_grad(
            select_grad,
            swapped(select_grad, "narrow", 1),
            select_weight,
            act_grad,
            convolved,
            act,
            projected,
            conv_weight,
            masks,
            [],
        )
        following = passed_along(before, "wide", -1)
        inner_grad = patched(segment_ids, inner_main, last, following, *normed_four)
        near = swapped(inner_grad, "wide", 2)
        keep, send = small_halves(wide_place[None] & 1, scan_small, conv_small, inner_grad)
        keep, send = folded((wide_place >> 1 & 1)[None], keep, swapped(send, "wide", 1))
        smalls = [keep, swapped(send, "wide", 2)]
        normed_part = jnp.einsum(
            "cte,dce->td", jnp.stack([inner_grad, gate_grad]), in_weight, preferred_element_type=f32
        )
        gain_part = jnp.sum(normed_part * whole * inverse, axis=0, keepdims=True)
        row_part = jnp.sum(normed_part * norm_gain * whole, axis=1)[None]
        first_bits, *more_bits = group_bits(2)
        gain_sum = gain_part + swapped(gain_part, "narrow", 1)
        for bit in (bit for bits in more_bits for bit in bits):
            gain_sum = gain_sum + swapped(gain_sum, "wide", bit)
        row_theirs = swapped(row_part, "narrow", 1)
        near = after(near, gain_sum, row_theirs, smalls[1])
        far = swapped(jnp.concatenate([inner_grad, near]), "wide", 1)
        keep, *sends = inner_quarter(
            ((wide_place >> 3 & 1) + 2 * (wide_place >> 2 & 1))[None],
            inner_grad,
            near,
            far,
            normed_four,
            smalls,
            [],
        )
        normed_mine, normed_other = narrow_halves(normed_part)
        normed_theirs = swapped(after(normed_other, keep), "narrow", 1)
        out_part = jnp.dot(after(gated, keep), out_weight, preferred_element_type=f32)
        out_mine, out_other = narrow_halves(out_part)
        out_theirs = swapped(out_other, "narrow", 1)
        layer_out = (tokens.astype(f32) + (out_mine + out_theirs)).astype(bf16)
        row_sum = (row_part + row_theirs).reshape(rows, 1)
        gain_mine = jnp.where(right_half, norm_gain[features:], norm_gain[:features])
        whole_grad = inverse * (gain_mine * (normed_mine + normed_theirs)) - tokens.astype(f32) * (
            inverse * inverse * inverse
        ) * (row_sum / (2 * features))
        tokens_grad = (whole_grad + cotangent.astype(f32)).astype(bf16)
        held = keep
        for n, flip in enumerate(flips(first_bits)[1:]):
            held = held + swapped(sends[n], "wide", flip).astype(f32)
        for bits in more_bits:
            held = scattered(held, bits)
        held = held.astype(bf16)
        for bits in reversed(more_bits):
            held = gathered(held, bits)
        spare = jnp.broadcast_to(gain_sum, (block_rows - used_rows, gain_sum.shape[1]))
        held = jnp.concatenate([held[: held.shape[0] - spare.shape[0]], spare.astype(bf16)])
        for bit in first_bits:
            held = gathered(held, (bit,))
        return held, layer_out, tokens_grad

    kinds = jax.eval_shape(after_forward, products)
    held, layer_out, tokens_grad = lax.cond(
        wide_place >= 0,
        after_forward,
        lambda pair: jax.tree.map(lambda kind: jnp.zeros(kind.shape, kind.dtype), kinds),
        products,
    )

    core = swapped(held, "wide", 1)
    near = swapped(held, "wide", 2)
    far = swapped(near, "wide", 1)
    conv_at = rank + count + 2
    (
        in_weight_grad,
        out_weight_grad,
        step_weight_grad,
        decay_log_grad,
        skip_gain_grad,
        step_bias_grad,
        select_weight_grad,
        conv_weight_grad,
        conv_bias_grad,
        norm_gain_grad,
    ) = joined(
        four_place,
        gate_sum,
        out_sum,
        (held, core, near, far),
        (0, rank, rank + count, rank + count + 1, conv_at, conv_at + columns, conv_at + columns + taps),
        (rank, count, 1, 1, columns, taps, 1, 1),
    )
    return (
        layer_out,
        tokens_grad,
        norm_gain_grad[0],
        in_weight_grad,
        conv_weight_grad,
        conv_bias_grad[0],
        select_weight_grad,
        step_weight_grad,
        step_bias_grad[0],
        decay_log_grad,
        skip_gain_grad[0],
        out_weight_grad,
    )


def solution(mesh):
    placed = (
        P("wide", "narrow"),
        P(),
        P(None, None, "narrow"),
        P(None, "narrow"),
        P("narrow"),
        P(None, "narrow"),
        P(None, "narrow"),
        P("narrow"),
        P(None, "narrow"),
        P("narrow"),
        P("narrow", None),
        P("wide"),
        P("wide", "narrow"),
    )
    return jax.shard_map(
        local,
        mesh=mesh,
        in_specs=placed,
        out_specs=(
            P("wide", "narrow"),
            P("wide", "narrow"),
            P(),
            P(None, None, "narrow"),
            P(None, "narrow"),
            P("narrow"),
            P(None, "narrow"),
            P(None, "narrow"),
            P("narrow"),
            P(None, "narrow"),
            P("narrow"),
            P("narrow", None),
        ),
        check_vma=False,
    )
```

```python
import functools

import jax
import jax.numpy as jnp
from jax import lax
from jax.experimental import pallas as pl
from jax.experimental.pallas import tpu as pltpu
from jax.sharding import PartitionSpec as P

epsilon = 1e-05
log2e = 1.4426950408889634
reset_step = 1e30
lanes = 128
halo = 16
body_rows = 64
scan_width = 512
vmem_bytes = 56 * 1024 * 1024
tiny_cost = pl.CostEstimate(flops=1, bytes_accessed=1, transcendentals=0)
f32 = jnp.float32
bf16 = jnp.bfloat16
contract_first = (((0,), (0,)), ((), ()))
contract_last = (((1,), (1,)), ((), ()))


def passed_along(array, axis, by):
    peers = lax.axis_size(axis)
    pairs = [(i, i + by) for i in range(peers) if 0 <= i + by < peers]
    return lax.ppermute(array, axis, pairs)


def swapped(array, axis, bit):
    peers = lax.axis_size(axis)
    return lax.ppermute(array, axis, [(i, i ^ bit) for i in range(peers)])


def wide_bits():
    bit, bits = 1, []
    while bit < lax.axis_size("wide"):
        bits.append(bit)
        bit *= 2
    return bits


def to_next_both(array):
    count, sides = lax.axis_size("wide"), lax.axis_size("narrow")
    pairs = [
        (i * sides + k, (i + 1) * sides + (sides - 1 - k))
        for i in range(count - 1)
        for k in range(sides)
    ]
    return passed_along(array, "wide", 1), lax.ppermute(array, ("wide", "narrow"), pairs)


def is_upper(bit):
    return (lax.axis_index("wide") & bit) != 0


def group_bits(size):
    bits, bit = [], 4
    while bit < lax.axis_size("wide"):
        bits.append(bit)
        bit *= 2
    return [tuple(bits[k : k + size]) for k in range(0, len(bits), size)]


def flips(bits):
    return [sum(b for k, b in enumerate(bits) if n >> k & 1) for n in range(2 ** len(bits))]


def scattered(piece, bits):
    rows = piece.shape[0] // 2 ** len(bits)
    here = sum(is_upper(b).astype(jnp.int32) << k for k, b in enumerate(bits))

    def block(n):
        return lax.dynamic_slice_in_dim(piece, (here ^ n) * rows, rows, 0)

    total = block(0).astype(f32)
    for n, flip in enumerate(flips(bits)):
        if n > 0:
            total = total + swapped(block(n).astype(bf16), "wide", flip).astype(f32)
    return total


def gathered(held, bits):
    blocks = [held] + [swapped(held, "wide", flip) for flip in flips(bits)[1:]]
    for bit in bits:
        upper = is_upper(bit)
        blocks = [
            jnp.concatenate([jnp.where(upper, b, a), jnp.where(upper, a, b)])
            for a, b in zip(blocks[0::2], blocks[1::2])
        ]
    return blocks[0]


def quarter_of_four(array):
    width = array.shape[1] // 4
    here = lax.axis_index("wide") & 3

    def quarter(n):
        return lax.dynamic_slice_in_dim(array, (here ^ n) * width, width, 1)

    return [quarter(0)] + [swapped(quarter(n), "wide", n) for n in (2, 1, 3)]


def silu_slope(values):
    logistic = jax.nn.sigmoid(values)
    return logistic * (1.0 + values * (1.0 - logistic))


def softplus(values):
    return jnp.maximum(values, 0.0) + jnp.log1p(jnp.exp(-jnp.abs(values)))


def column_spec(rows, start=0):
    return pl.BlockSpec((rows, scan_width), lambda j: (0, start + j))


def part_spec(part, rows, start=0):
    return pl.BlockSpec((None, rows, scan_width), lambda j: (part, 0, start + j))


def whole_spec(rows, width):
    return pl.BlockSpec((rows, width), lambda j: (0, 0))


def call(kernel, name, width, in_specs, out_specs, out_shape, scratch, *operands):
    return pl.pallas_call(
        kernel,
        grid=(width // scan_width,),
        in_specs=in_specs,
        out_specs=out_specs,
        out_shape=out_shape,
        scratch_shapes=scratch,
        compiler_params=pltpu.CompilerParams(vmem_limit_bytes=vmem_bytes),
        cost_estimate=tiny_cost,
        name=name,
    )(*operands)


def conv_kernel(
    inner_ref,
    conv_weight_ref,
    conv_bias_ref,
    select_ref,
    mask_ref,
    convolved_ref,
    act_ref,
    selected_ref,
    inner,
):
    rows = act_ref.shape[0]
    taps = conv_weight_ref.shape[0]
    inner[:halo, :] = inner_ref[rows:, :].astype(f32)
    inner[halo:, :] = inner_ref[:rows, :].astype(f32)
    total = conv_bias_ref[...] + conv_weight_ref[taps - 1 :, :] * inner[halo:, :]
    for lag in range(1, taps):
        earlier = inner[pl.ds(halo - lag, rows), :] * mask_ref[:, lag : lag + 1]
        total = total + conv_weight_ref[taps - 1 - lag : taps - lag, :] * earlier
    convolved_ref[...] = total
    act = (total * jax.nn.sigmoid(total)).astype(bf16)
    act_ref[...] = act
    part = lax.dot_general(select_ref[...], act, contract_last, preferred_element_type=f32)

    @pl.when(pl.program_id(0) == 0)
    def _():
        selected_ref[...] = part

    @pl.when(pl.program_id(0) > 0)
    def _():
        selected_ref[...] += part


def convolve(projected, conv_weight, conv_bias, select_weight, masks):
    parts, extended, width = projected.shape
    rows = extended - halo
    taps = conv_weight.shape[0]
    columns = select_weight.shape[0]
    return call(
        conv_kernel,
        "convolve",
        width,
        [
            part_spec(0, extended),
            column_spec(taps),
            column_spec(1),
            column_spec(columns),
            whole_spec(rows, masks.shape[1]),
        ],
        [column_spec(rows), column_spec(rows), whole_spec(columns, rows)],
        [
            jax.ShapeDtypeStruct((rows, width), f32),
            jax.ShapeDtypeStruct((rows, width), bf16),
            jax.ShapeDtypeStruct((columns, rows), f32),
        ],
        [pltpu.VMEM((extended, scan_width), f32)],
        projected,
        conv_weight,
        conv_bias,
        select_weight,
        masks,
    )


def coef_columns(coef, block):
    per_tile = lanes // body_rows
    start = pl.multiple_of((block // per_tile) * lanes, lanes)
    tile = coef[:, pl.ds(start, lanes)]
    back = body_rows * lax.rem(block, per_tile)
    return pltpu.roll(tile, lax.rem(lanes - back, lanes), 1)


def put_ends(ends_ref, state, adjoint, total):
    count, width = state.shape
    ends_ref[:count, :] = state.astype(bf16)
    ends_ref[count : 2 * count, :] = adjoint.astype(bf16)
    high = total.astype(bf16).astype(f32)
    upper = lax.broadcasted_iota(jnp.int32, (16, width), 0) < 8
    ends_ref[2 * count :, :] = jnp.where(upper, high, total - high).astype(bf16)


def get_ends(ends_ref, count):
    total = ends_ref[2 * count :].astype(f32)
    return (
        ends_ref[:count].astype(f32),
        ends_ref[count : 2 * count].astype(f32),
        total[:1] + total[8:9],
    )


def ends_kernel(
    selected_ref,
    other_ref,
    step_weight_ref,
    step_bias_ref,
    act_ref,
    gate_ref,
    gated_grad_ref,
    mask_ref,
    decay_log_ref,
    step_pre_ref,
    step_ref,
    ends_ref,
    coef,
    held_step,
    drive,
    scan_grad,
):
    rows = act_ref.shape[0]
    count = decay_log_ref.shape[0]
    rank = step_weight_ref.shape[0]
    decay2 = -jnp.exp(decay_log_ref[...]) * log2e
    selected = selected_ref[...] + other_ref[...]
    coef[...] = selected[rank:, :]
    step_low = selected[:rank, :].astype(bf16)
    step_pre = step_bias_ref[...] + lax.dot_general(
        step_low, step_weight_ref[...], contract_first, preferred_element_type=f32
    )
    step_pre_ref[...] = step_pre
    step = softplus(step_pre)
    step_ref[...] = step
    held_step[...] = jnp.where(mask_ref[:, 1:2] > 0.0, step, reset_step)
    drive[...] = step * act_ref[...].astype(f32)
    gate = gate_ref[...].astype(f32)
    scan_grad[...] = gated_grad_ref[...] * (gate * jax.nn.sigmoid(gate))
    zero = jnp.zeros(decay2.shape, f32)

    def body(block, carried):
        state, product, adjoint = carried
        columns = coef_columns(coef, block)
        for i in range(body_rows):
            row = pl.ds(block * body_rows + i, 1)
            factor = jnp.exp2(held_step[row, :] * decay2)
            state = factor * state + columns[:count, i : i + 1] * drive[row, :]
            product = factor * product
            adjoint = adjoint + product * (columns[count:, i : i + 1] * scan_grad[row, :])
        return state, product, adjoint

    state, product, adjoint = lax.fori_loop(0, rows // body_rows, body, (zero, zero + 1.0, zero))
    put_ends(ends_ref, state, adjoint, jnp.sum(held_step[...], axis=0, keepdims=True))


def scan_ends(
    selected, other, step_weight, step_bias, act, projected, gated_grad, masks, decay_log
):
    rows, width = act.shape
    count = decay_log.shape[0]
    columns = selected.shape[0]
    rank = step_weight.shape[0]
    return call(
        ends_kernel,
        "scan_ends",
        width,
        [
            whole_spec(columns, rows),
            whole_spec(columns, rows),
            column_spec(rank),
            column_spec(1),
            column_spec(rows),
            part_spec(1, rows),
            column_spec(rows),
            whole_spec(rows, masks.shape[1]),
            column_spec(count),
        ],
        [column_spec(rows), column_spec(rows), column_spec(2 * count + 16)],
        [
            jax.ShapeDtypeStruct((rows, width), f32),
            jax.ShapeDtypeStruct((rows, width), f32),
            jax.ShapeDtypeStruct((2 * count + 16, width), bf16),
        ],
        [pltpu.VMEM((2 * count, rows), f32)] + [pltpu.VMEM((rows, scan_width), f32)] * 3,
        selected,
        other,
        step_weight,
        step_bias,
        act,
        projected,
        gated_grad,
        masks,
        decay_log,
    )


def lane_tiles(values):
    return [values[:, k : k + lanes] for k in range(0, values.shape[1], lanes)]


def tree_sum(parts):
    while len(parts) > 1:
        odd = parts[len(parts) // 2 * 2 :]
        parts = [a + b for a, b in zip(parts[0::2], parts[1::2])] + odd
    return parts[0]


def keep_halves(scratch, i, values):
    for k, tile in enumerate(lane_tiles(values)):
        at = (k * body_rows + i) * 8
        scratch[at : at + 8, :] = tile[:8] + tile[8:]


def put_state_sums(scratch, out_ref, block):
    for group in range(body_rows // 8):
        row = pl.ds(pl.multiple_of(block * body_rows + group * 8, 8), 8)
        for k in range(out_ref.shape[1] // lanes):
            at = (k * body_rows + group * 8) * 8
            total = tree_sum([scratch[pl.ds(at + n, 8, stride=8), :] for n in range(8)])
            out_ref[row, k * lanes : (k + 1) * lanes] = total


def lane_sums(values):
    ones = jnp.ones((8, lanes), bf16)
    high = values.astype(bf16)
    low = (values - high.astype(f32)).astype(bf16)
    total = lax.dot_general(ones, high, contract_last, preferred_element_type=f32)
    total += lax.dot_general(ones, low, contract_last, preferred_element_type=f32)
    return total[:1, :]


def at_token(t, count):
    return pl.ds(pl.multiple_of(t * count, count), count)


def forward_kernel(
    selected_ref,
    other_ref,
    step_ref,
    act_ref,
    gate_ref,
    gated_grad_ref,
    mask_ref,
    decay_log_ref,
    passed_ref,
    entering_ref,
    skip_ref,
    cot_ref,
    normed_ref,
    gated_ref,
    gate_grad_ref,
    out_product_ref,
    gate_product_ref,
    entry_ref,
    coef,
    held_step,
    drive,
    scanned,
    halves,
):
    rows = step_ref.shape[0]
    count = decay_log_ref.shape[0]
    rank = selected_ref.shape[0] - 2 * count
    decay = -jnp.exp(decay_log_ref[...])
    decay2 = decay * log2e
    before_steps = passed_ref[2 * count : 2 * count + 1, :]
    entry = passed_ref[:count, :] + through(decay, before_steps) * entering_ref[...].astype(f32)
    entry_ref[...] = entry
    coef[...] = selected_ref[rank:, :] + other_ref[rank:, :]
    act = act_ref[...].astype(f32)
    held_step[...] = jnp.where(mask_ref[:, 1:2] > 0.0, step_ref[...], reset_step)
    drive[...] = step_ref[...] * act

    def forward(block, state):
        columns = coef_columns(coef, block)
        for i in range(body_rows):
            row = pl.ds(block * body_rows + i, 1)
            factor = jnp.exp2(held_step[row, :] * decay2)
            state = factor * state + columns[:count, i : i + 1] * drive[row, :]
            keep_halves(halves, i, columns[count:, i : i + 1] * state)
        put_state_sums(halves, scanned, block)
        return state

    lax.fori_loop(0, rows // body_rows, forward, entry)
    gate = gate_ref[...].astype(f32)
    logistic = jax.nn.sigmoid(gate)
    total = scanned[...] + skip_ref[...] * act
    gated = (total * (gate * logistic)).astype(bf16)
    gated_ref[...] = gated
    out_product_ref[...] = lax.dot_general(
        gated, cot_ref[...], contract_first, preferred_element_type=f32
    ).astype(bf16)
    slope = logistic * (1.0 + gate * (1.0 - logistic))
    gate_grad = (gated_grad_ref[...] * total * slope).astype(bf16)
    gate_grad_ref[...] = gate_grad
    gate_product_ref[...] = lax.dot_general(
        normed_ref[...], gate_grad, contract_first, preferred_element_type=f32
    ).astype(bf16)


def scan_forward(
    selected,
    other,
    step,
    act,
    projected,
    gated_grad,
    masks,
    decay_log,
    passed,
    entering,
    skip_gain,
    cot,
    normed,
):
    rows, width = step.shape
    count = decay_log.shape[0]
    columns = selected.shape[0]
    return call(
        forward_kernel,
        "scan_forward",
        width,
        [
            whole_spec(columns, rows),
            whole_spec(columns, rows),
            column_spec(rows),
            column_spec(rows),
            part_spec(1, rows),
            column_spec(rows),
            whole_spec(rows, masks.shape[1]),
            column_spec(count),
            column_spec(2 * count + 8),
            column_spec(count),
            column_spec(1),
            whole_spec(*cot.shape),
            whole_spec(*normed.shape),
        ],
        [
            column_spec(rows),
            column_spec(rows),
            pl.BlockSpec((scan_width, cot.shape[1]), lambda j: (j, 0)),
            column_spec(normed.shape[1]),
            column_spec(count),
        ],
        [
            jax.ShapeDtypeStruct((rows, width), bf16),
            jax.ShapeDtypeStruct((rows, width), bf16),
            jax.ShapeDtypeStruct((width, cot.shape[1]), bf16),
            jax.ShapeDtypeStruct((normed.shape[1], width), bf16),
            jax.ShapeDtypeStruct((count, width), f32),
        ],
        [pltpu.VMEM((2 * count, rows), f32)]
        + [pltpu.VMEM((rows, scan_width), f32)] * 3
        + [pltpu.VMEM((8 * body_rows * (scan_width // lanes), lanes), f32)],
        selected,
        other,
        step,
        act,
        projected,
        gated_grad,
        masks,
        decay_log,
        passed,
        entering,
        skip_gain,
        cot,
        normed,
    )


def backward_kernel(
    selected_ref,
    other_ref,
    step_pre_ref,
    step_ref,
    act_ref,
    gate_ref,
    gated_grad_ref,
    mask_ref,
    decay_log_ref,
    entry_ref,
    passed_ref,
    returning_ref,
    skip_ref,
    step_weight_ref,
    act_grad_ref,
    select_grad_ref,
    small_ref,
    coef,
    held_step,
    drive,
    scan_grad,
    weighted,
    held_sum,
    states,
    factors,
    halves,
    more_halves,
    in_sum,
    read_sum,
):
    rows = step_ref.shape[0]
    count = decay_log_ref.shape[0]
    rank = step_weight_ref.shape[0]
    blocks = rows // body_rows
    decay = -jnp.exp(decay_log_ref[...])
    decay2 = decay * log2e
    after_steps = passed_ref[2 * count + 1 : 2 * count + 2, :]
    tail = passed_ref[count : 2 * count, :] + through(decay, after_steps) * returning_ref[...].astype(f32)
    selected = selected_ref[...] + other_ref[...]
    coef[...] = selected[rank:, :]
    step_low = selected[:rank, :].astype(bf16)
    step = step_ref[...]
    act = act_ref[...].astype(f32)
    held_step[...] = jnp.where(mask_ref[:, 1:2] > 0.0, step, reset_step)
    drive[...] = step * act
    gate = gate_ref[...].astype(f32)
    grads = gated_grad_ref[...] * (gate * jax.nn.sigmoid(gate))
    scan_grad[...] = grads
    small_ref[rank + count : rank + count + 1, :] = jnp.sum(grads * act, axis=0, keepdims=True)
    states[:count, :] = entry_ref[...]

    @pl.when(pl.program_id(0) == 0)
    def _():
        in_sum[...] = jnp.zeros(in_sum.shape, f32)
        read_sum[...] = jnp.zeros(read_sum.shape, f32)
        select_grad_ref[...] = jnp.zeros(select_grad_ref.shape, f32)

    def forward(block, state):
        columns = coef_columns(coef, block)
        for i in range(body_rows):
            t = block * body_rows + i
            row = pl.ds(t, 1)
            factor = jnp.exp2(held_step[row, :] * decay2)
            state = factor * state + columns[:count, i : i + 1] * drive[row, :]
            factors[at_token(t, count), :] = factor
            states[at_token(t + 1, count), :] = state
        return state

    lax.fori_loop(0, blocks, forward, entry_ref[...])

    def backward(k, carried):
        adjoint, decay_grad = carried
        block = blocks - 1 - k
        columns = coef_columns(coef, block)
        for i in range(body_rows - 1, -1, -1):
            t = block * body_rows + i
            row = pl.ds(t, 1)
            here = at_token(t, count)
            grad = scan_grad[row, :]
            summed = columns[count:, i : i + 1] * grad + adjoint
            read_sum[here, :] += tree_sum(lane_tiles(grad * states[at_token(t + 1, count), :]))
            in_sum[here, :] += tree_sum(lane_tiles(summed * drive[row, :]))
            keep_halves(halves, i, summed * columns[:count, i : i + 1])
            adjoint = factors[here, :] * summed
            held = adjoint * states[here, :]
            decay_grad = decay_grad + held * step_ref[row, :]
            keep_halves(more_halves, i, held * decay)
        put_state_sums(halves, weighted, block)
        put_state_sums(more_halves, held_sum, block)
        return adjoint, decay_grad

    ignored, decay_grad = lax.fori_loop(
        0, blocks, backward, (tail, jnp.zeros(decay.shape, f32))
    )
    act_grad_ref[...] = step * weighted[...] + skip_ref[...] * scan_grad[...]
    step_grad = act * weighted[...] + held_sum[...]
    pre_grad = (step_grad * jax.nn.sigmoid(step_pre_ref[...])).astype(bf16)
    small_ref[:rank, :] = jnp.dot(step_low, pre_grad, preferred_element_type=f32)
    small_ref[rank : rank + count, :] = decay_grad * decay
    bias_grad = jnp.sum(pre_grad.astype(f32), axis=0, keepdims=True)
    small_ref[rank + count + 1 : rank + count + 2, :] = bias_grad
    select_grad_ref[:rank, :] += lax.dot_general(
        step_weight_ref[...], pre_grad, contract_last, preferred_element_type=f32
    )

    @pl.when(pl.program_id(0) == pl.num_programs(0) - 1)
    def _():
        for n in range(count):
            at = pl.ds(n, rows, stride=count)
            select_grad_ref[rank + n : rank + n + 1, :] = lane_sums(in_sum[at, :])
            select_grad_ref[rank + count + n : rank + count + n + 1, :] = lane_sums(read_sum[at, :])


def scan_backward(
    selected,
    other,
    step_pre,
    step,
    act,
    projected,
    gated_grad,
    masks,
    decay_log,
    entry,
    passed,
    returning,
    skip_gain,
    step_weight,
):
    rows, width = step.shape
    count = decay_log.shape[0]
    columns = selected.shape[0]
    rank = step_weight.shape[0]
    half_rows = 8 * body_rows * (scan_width // lanes)
    small = rank + count + 2
    return call(
        backward_kernel,
        "scan_backward",
        width,
        [
            whole_spec(columns, rows),
            whole_spec(columns, rows),
            column_spec(rows),
            column_spec(rows),
            column_spec(rows),
            part_spec(1, rows),
            column_spec(rows),
            whole_spec(rows, masks.shape[1]),
            column_spec(count),
            column_spec(count),
            column_spec(2 * count + 8),
            column_spec(count),
            column_spec(1),
            column_spec(rank),
        ],
        [column_spec(rows), whole_spec(columns, rows), column_spec(small)],
        [
            jax.ShapeDtypeStruct((rows, width), f32),
            jax.ShapeDtypeStruct((columns, rows), f32),
            jax.ShapeDtypeStruct((small, width), f32),
        ],
        [pltpu.VMEM((2 * count, rows), f32)]
        + [pltpu.VMEM((rows, scan_width), f32)] * 5
        + [
            pltpu.VMEM(((rows + 1) * count, scan_width), f32),
            pltpu.VMEM((rows * count, scan_width), f32),
            pltpu.VMEM((half_rows, lanes), f32),
            pltpu.VMEM((half_rows, lanes), f32),
            pltpu.VMEM((rows * count, lanes), f32),
            pltpu.VMEM((rows * count, lanes), f32),
        ],
        selected,
        other,
        step_pre,
        step,
        act,
        projected,
        gated_grad,
        masks,
        decay_log,
        entry,
        passed,
        returning,
        skip_gain,
        step_weight,
    )


def conv_grad_kernel(
    select_grad_ref,
    other_ref,
    select_ref,
    act_grad_ref,
    convolved_ref,
    act_ref,
    inner_ref,
    conv_weight_ref,
    mask_ref,
    *rest,
):
    inner_grad_ref, before_ref, last_ref, small_ref, inner, shifted = rest[-6:]
    rows = act_ref.shape[0]
    taps = conv_weight_ref.shape[0]
    columns = select_ref.shape[0]
    select_grad = (select_grad_ref[...] + other_ref[...]).astype(bf16)
    total = act_grad_ref[...] + lax.dot_general(
        select_grad, select_ref[...], contract_first, preferred_element_type=f32
    )
    conv_grad = total * silu_slope(convolved_ref[...])
    small_ref[:columns, :] = jnp.dot(select_grad, act_ref[...], preferred_element_type=f32)
    inner[:halo, :] = inner_ref[rows:, :].astype(f32)
    inner[halo:, :] = inner_ref[:rows, :].astype(f32)
    edges = jnp.zeros((8, conv_grad.shape[1]), f32)
    shifted[:8, :] = edges
    shifted[rows + 8 :, :] = edges
    out = conv_weight_ref[taps - 1 :, :] * conv_grad
    before = edges
    small_ref[columns + taps - 1 : columns + taps, :] = jnp.sum(
        conv_grad * inner[halo:, :], axis=0, keepdims=True
    )
    for lag in range(1, taps):
        masked = conv_grad * mask_ref[:, lag : lag + 1]
        at = taps - 1 - lag
        small_ref[columns + at : columns + at + 1, :] = jnp.sum(
            masked * inner[pl.ds(halo - lag, rows), :], axis=0, keepdims=True
        )
        shifted[8 : rows + 8, :] = masked
        weight = conv_weight_ref[at : at + 1, :]
        out = out + weight * shifted[pl.ds(8 + lag, rows), :]
        before = before + weight * shifted[pl.ds(lag, 8), :]
    small_ref[columns + taps : columns + taps + 1, :] = jnp.sum(conv_grad, axis=0, keepdims=True)
    inner_grad_ref[...] = out.astype(bf16)
    before_ref[...] = before
    last_ref[...] = out[rows - 8 :, :]


def convolve_grad(
    select_grad, other, select_weight, act_grad, convolved, act, projected, conv_weight, masks, waits
):
    rows, width = act.shape
    extended = rows + halo
    columns = select_weight.shape[0]
    taps = conv_weight.shape[0]
    small = columns + taps + 1
    return call(
        conv_grad_kernel,
        "convolve_grad",
        width,
        [
            whole_spec(columns, rows),
            whole_spec(columns, rows),
            column_spec(columns),
            column_spec(rows),
            column_spec(rows),
            column_spec(rows),
            part_spec(0, extended),
            column_spec(taps),
            whole_spec(rows, masks.shape[1]),
        ]
        + [pl.BlockSpec(memory_space=pl.ANY)] * len(waits),
        [column_spec(rows), column_spec(8), column_spec(8), column_spec(small)],
        [
            jax.ShapeDtypeStruct((rows, width), bf16),
            jax.ShapeDtypeStruct((8, width), f32),
            jax.ShapeDtypeStruct((8, width), f32),
            jax.ShapeDtypeStruct((small, width), f32),
        ],
        [pltpu.VMEM((extended, scan_width), f32), pltpu.VMEM((rows + 16, scan_width), f32)],
        select_grad,
        other,
        select_weight,
        act_grad,
        convolved,
        act,
        projected,
        conv_weight,
        masks,
        *waits,
    )


def normalize_kernel(
    own_ref,
    other_ref,
    edge_ref,
    other_edge_ref,
    gain_ref,
    ids_ref,
    whole_ref,
    extended_ref,
    normed_ref,
    inverse_ref,
    mask_ref,
    rows_ref,
):
    rows, half = own_ref.shape
    ids = ids_ref[...].astype(f32)
    place = lax.broadcasted_iota(jnp.int32, ids.shape, 1)
    same = []
    for lag in range(8):
        earlier = jnp.where(place < lag, ids[:, :1], pltpu.roll(ids, lag, 1)) if lag else ids
        same.append(jnp.where(earlier == ids, 1.0, 0.0))
    spare = jnp.zeros((lanes - 8, rows), f32)
    mask_ref[...] = jnp.concatenate(same + [spare]).T
    right = lax.axis_index("narrow") == 1
    for at, own, other in ((0, own_ref, other_ref), (rows, edge_ref, other_edge_ref)):
        end = at + own.shape[0]
        rows_ref[at:end, :half] = jnp.where(right, other[...], own[...])
        rows_ref[at:end, half:] = jnp.where(right, own[...], other[...])
    whole_ref[...] = rows_ref[:rows, :]
    whole = rows_ref[...].astype(f32)
    inverse = lax.rsqrt(jnp.mean(whole * whole, axis=1, keepdims=True) + epsilon)
    normed = (whole * inverse * gain_ref[...]).astype(bf16)
    extended_ref[...] = normed
    normed_ref[...] = normed[:rows]
    inverse_ref[...] = inverse[:rows]


def normalized(own, other, edge, other_edge, gain, ids):
    rows, half = own.shape
    extended = rows + edge.shape[0]
    return pl.pallas_call(
        normalize_kernel,
        out_shape=[
            jax.ShapeDtypeStruct((rows, 2 * half), bf16),
            jax.ShapeDtypeStruct((extended, 2 * half), bf16),
            jax.ShapeDtypeStruct((rows, 2 * half), bf16),
            jax.ShapeDtypeStruct((rows, 1), f32),
            jax.ShapeDtypeStruct((rows, lanes), f32),
        ],
        scratch_shapes=[pltpu.VMEM((extended, 2 * half), bf16)],
        cost_estimate=tiny_cost,
        name="normalized",
    )(own, other, edge, other_edge, gain, ids)


def after(array, *waits):
    anywhere = pl.BlockSpec(memory_space=pl.ANY)
    return pl.pallas_call(
        lambda *refs: None,
        in_specs=[anywhere] * (1 + len(waits)),
        out_specs=anywhere,
        out_shape=jax.ShapeDtypeStruct(array.shape, array.dtype),
        input_output_aliases={0: 0},
        cost_estimate=tiny_cost,
        name="after",
    )(array, *waits)


def patch_kernel(ids_ref, rows_ref, last_ref, next_ref, *rest):
    count = ids_ref.shape[0]
    place = lax.broadcasted_iota(jnp.int32, (8, 1), 0)
    same = jnp.zeros((8, 1), f32)
    for lag in range(8):
        here = jnp.where(ids_ref[count - 1 - lag] == ids_ref[count - 1], 1.0, 0.0)
        same = same + jnp.where(place == 7 - lag, here, 0.0)
    total = last_ref[...] + next_ref[...] * same
    rows = rows_ref[...].astype(f32)
    rest[-1][...] = jnp.concatenate([rows[: halo - 8], total]).astype(bf16)


def patched(ids, grads, last, following, *waits):
    rows, width = grads.shape
    block = pl.BlockSpec((halo, width), lambda j: (rows // halo - 1, 0))
    edge = pl.BlockSpec((8, width), lambda j: (0, 0))
    return pl.pallas_call(
        patch_kernel,
        grid=(1,),
        in_specs=[pl.BlockSpec(memory_space=pltpu.SMEM), block, edge, edge]
        + [pl.BlockSpec(memory_space=pl.ANY)] * len(waits),
        out_specs=block,
        out_shape=jax.ShapeDtypeStruct((rows, width), bf16),
        input_output_aliases={1: 0},
        cost_estimate=tiny_cost,
        name="patched",
    )(ids, grads, last, following, *waits)


def edge_kernel(ids_ref, tokens_ref, out_ref):
    rows = ids_ref.shape[0]
    taps = 4
    out_ref[...] = tokens_ref[...]
    place = lax.broadcasted_iota(jnp.int32, (halo, 1), 0)
    same = jnp.zeros((halo, 1), f32)
    for lag in range(taps):
        here = jnp.where(ids_ref[rows - 1 - lag] == ids_ref[rows - 1], 1.0, 0.0)
        same = same + jnp.where(place == halo - 1 - lag, here, 0.0)
    out_ref[...] = (tokens_ref[...].astype(f32) * same).astype(bf16)


def edge_rows_of(ids, tokens):
    rows, width = tokens.shape
    return pl.pallas_call(
        edge_kernel,
        grid=(1,),
        in_specs=[
            pl.BlockSpec(memory_space=pltpu.SMEM),
            pl.BlockSpec((halo, width), lambda j: (rows // halo - 1, 0)),
        ],
        out_specs=pl.BlockSpec((halo, width), lambda j: (0, 0)),
        out_shape=jax.ShapeDtypeStruct((halo, width), bf16),
        cost_estimate=tiny_cost,
        name="edge_rows",
    )(ids, tokens)


block_rows, used_rows = 16, 12


def small_kernel(core_ref, scan_ref, conv_ref, wait_ref, keep_ref, send_ref, rows, blocks):
    rows[...] = jnp.zeros(rows.shape, f32)
    rows[: scan_ref.shape[0], :] = scan_ref[...]
    rows[scan_ref.shape[0] : scan_ref.shape[0] + conv_ref.shape[0], :] = conv_ref[...]
    blocks[...] = jnp.zeros(blocks.shape, f32)
    for n in range(16):
        blocks[n * block_rows : n * block_rows + used_rows, :] = rows[
            n * used_rows : (n + 1) * used_rows, :
        ]
    half = keep_ref.shape[0]
    mine = pl.ds(pl.multiple_of(core_ref[0] * half, half), half)
    other = pl.ds(pl.multiple_of((1 - core_ref[0]) * half, half), half)
    keep_ref[...] = blocks[mine, :]
    send_ref[...] = blocks[other, :].astype(bf16)


def small_halves(core, scan_small, conv_small, wait):
    width = scan_small.shape[1]
    return pl.pallas_call(
        small_kernel,
        in_specs=[pl.BlockSpec(memory_space=pltpu.SMEM)]
        + [pl.BlockSpec(memory_space=pltpu.VMEM)] * 2
        + [pl.BlockSpec(memory_space=pl.ANY)],
        out_shape=[jax.ShapeDtypeStruct((8 * block_rows, width), kind) for kind in (f32, bf16)],
        scratch_shapes=[
            pltpu.VMEM((16 * used_rows, width), f32),
            pltpu.VMEM((16 * block_rows, width), f32),
        ],
        cost_estimate=tiny_cost,
        name="small_halves",
    )(core, scan_small, conv_small, wait)


def fold_kernel(upper_ref, keep_ref, arrived_ref, out_ref, send_ref):
    size = out_ref.shape[0]
    mine = pl.ds(pl.multiple_of(upper_ref[0] * size, size), size)
    other = pl.ds(pl.multiple_of((1 - upper_ref[0]) * size, size), size)
    out_ref[...] = keep_ref[mine, :] + arrived_ref[mine, :].astype(f32)
    send_ref[...] = (keep_ref[other, :] + arrived_ref[other, :].astype(f32)).astype(bf16)


def folded(upper, keep, arrived):
    rows, width = keep.shape
    return pl.pallas_call(
        fold_kernel,
        in_specs=[pl.BlockSpec(memory_space=pltpu.SMEM)]
        + [pl.BlockSpec(memory_space=pltpu.VMEM)] * 2,
        out_shape=[jax.ShapeDtypeStruct((rows // 2, width), kind) for kind in (f32, bf16)],
        cost_estimate=tiny_cost,
        name="folded",
    )(upper, keep, arrived)


def quarter_kernel(
    place_ref,
    own_ref,
    near_ref,
    far_ref,
    normed_0,
    normed_1,
    normed_2,
    normed_3,
    small_ref,
    arrived_ref,
    *rest,
):
    keep_ref, *sends_refs, piece, small = rest[-6:]
    total = None
    tokens = own_ref.shape[0]
    grads = (own_ref[...], near_ref[...], far_ref[:tokens, :], far_ref[tokens:, :])
    for left, right in zip((normed_0, normed_1, normed_2, normed_3), grads):
        part = lax.dot_general(left[...], right, contract_first, preferred_element_type=f32)
        total = part if total is None else total + part
    piece[...] = total
    small[...] = small_ref[...] + arrived_ref[...].astype(f32)
    rows, spare = piece.shape[0] // 4, small.shape[0] // 4
    for n in range(4):
        block = place_ref[0] ^ n
        inner_rows = piece[pl.ds(pl.multiple_of(block * rows, rows), rows), :]
        small_rows = small[pl.ds(pl.multiple_of(block * spare, spare), spare), :]
        if n == 0:
            keep_ref[:rows, :] = inner_rows
            keep_ref[rows:, :] = small_rows
        else:
            sends_refs[n - 1][:rows, :] = inner_rows.astype(bf16)
            sends_refs[n - 1][rows:, :] = small_rows.astype(bf16)


def inner_quarter(place, own, near, far, normed, smalls, waits):
    width = own.shape[1]
    quarter = normed[0].shape[1]
    spare = smalls[0].shape[0]
    rows = (quarter + spare) // 4
    return pl.pallas_call(
        quarter_kernel,
        in_specs=[pl.BlockSpec(memory_space=pltpu.SMEM)]
        + [pl.BlockSpec(memory_space=pltpu.VMEM)] * 9
        + [pl.BlockSpec(memory_space=pl.ANY)] * len(waits),
        out_shape=[jax.ShapeDtypeStruct((rows, width), f32)]
        + [jax.ShapeDtypeStruct((rows, width), bf16)] * 3,
        scratch_shapes=[pltpu.VMEM((quarter, width), f32), pltpu.VMEM((spare, width), f32)],
        compiler_params=pltpu.CompilerParams(vmem_limit_bytes=vmem_bytes),
        cost_estimate=tiny_cost,
        name="inner_quarter",
    )(place, own, near, far, *normed, *smalls, *waits)


def put_quarter(out_ref, gate_ref, inner_ref):
    rows = out_ref.shape[0] // 4
    out_ref[:, 1, :] = gate_ref[...].astype(f32)
    for n in range(4):
        at = n * (rows + block_rows)
        out_ref[n * rows : (n + 1) * rows, 0, :] = inner_ref[at : at + rows, :].astype(f32)


def first_join_kernel(place_ref, gate_ref, first_ref, second_ref, low_ref, out_ref, wide_ref):
    wide_ref[...] = low_ref[...].astype(f32)

    @pl.when(pl.program_id(0) == 0)
    def _():
        put_quarter(out_ref, gate_ref, first_ref)

    @pl.when(pl.program_id(0) == 1)
    def _():
        put_quarter(out_ref, gate_ref, second_ref)


def last_join_kernel(place_ref, gate_ref, first_ref, second_ref, *rest, small_rows):
    held = rest[:4]
    out_ref, *row_refs, gain_ref, blocks = rest[5:]

    @pl.when(pl.program_id(0) == 0)
    def _():
        put_quarter(out_ref, gate_ref, first_ref)

    @pl.when(pl.program_id(0) == 1)
    def _():
        put_quarter(out_ref, gate_ref, second_ref)
        rows = out_ref.shape[0] // 4
        for flip, ref in enumerate(held):
            number = place_ref[0] ^ flip
            number = (number & 1) * 2 + number // 2
            for n in range(4):
                at = (number * 4 + n) * block_rows
                taken = ref[(n + 1) * rows + n * block_rows : (n + 1) * (rows + block_rows), :]
                blocks[pl.ds(pl.multiple_of(at, block_rows), block_rows), :] = taken.astype(f32)
        for ref, start in zip(row_refs, small_rows):
            for row in range(ref.shape[0]):
                at = (start + row) // used_rows * block_rows + (start + row) % used_rows
                ref[row : row + 1, :] = blocks[at : at + 1, :]
        gain_ref[...] = sum(
            blocks[n * block_rows + used_rows : n * block_rows + used_rows + 1, :] for n in range(16)
        )


def joined(kernel, place, flip, gate, first, second, specs, operands, out_specs, out_shape, scratch, aliases):
    depth, width = gate.shape
    quarter = depth // 4

    def target(j, place):
        return place[0] ^ (flip + j)

    whole = pl.BlockSpec(first.shape, lambda j, place: (0, 0))
    return pl.pallas_call(
        kernel,
        grid_spec=pltpu.PrefetchScalarGridSpec(
            num_scalar_prefetch=1,
            grid=(2,),
            in_specs=[
                pl.BlockSpec((quarter, width), lambda j, place: (target(j, place), 0)),
                whole,
                whole,
            ]
            + specs,
            out_specs=[
                pl.BlockSpec((quarter, 2, width), lambda j, place: (target(j, place), 0, 0))
            ]
            + out_specs,
            scratch_shapes=scratch,
        ),
        out_shape=[jax.ShapeDtypeStruct((depth, 2, width), f32)] + out_shape,
        input_output_aliases=aliases,
        compiler_params=pltpu.CompilerParams(vmem_limit_bytes=vmem_bytes),
        cost_estimate=tiny_cost,
        name="joined",
    )(place, gate, first, second, *operands)


def joined_first(place, gate, first, second, low):
    rows, width = low.shape
    half = pl.BlockSpec((rows // 2, width), lambda j, place: (j, 0))
    kind = jax.ShapeDtypeStruct((rows, width), f32)
    return joined(
        first_join_kernel, place, 0, gate, first, second, [half], [low], [half], [kind], [], {}
    )


def joined_last(place, gate, held, begun, small_rows, small_counts):
    width = gate.shape[1]
    whole = pl.BlockSpec(held[0].shape, lambda j, place: (0, 0))
    return joined(
        functools.partial(last_join_kernel, small_rows=small_rows),
        place,
        2,
        gate,
        held[2],
        held[3],
        [whole] * 4 + [pl.BlockSpec(memory_space=pl.ANY)],
        [*held, begun],
        [pl.BlockSpec((rows, width), lambda j, place: (0, 0)) for rows in small_counts],
        [jax.ShapeDtypeStruct((rows, width), f32) for rows in small_counts],
        [pltpu.VMEM((16 * block_rows, width), f32)],
        {8: 0},
    )


def through(decay, total):
    return jnp.exp(decay * total)


def round_kernel(second_ref, decay_log_ref, own_ref, other_ref, *rest, first):
    count, width = decay_log_ref.shape
    new_passed_ref, *ends_refs = rest if first else rest[1:]
    decay = -jnp.exp(decay_log_ref[...])
    second = second_ref[0] > 0
    own, other = get_ends(own_ref, count), get_ends(other_ref, count)
    early = [jnp.where(second, b, a) for a, b in zip(own, other)]
    late = [jnp.where(second, a, b) for a, b in zip(own, other)]
    state = late[0] + through(decay, late[2]) * early[0]
    adjoint = early[1] + through(decay, early[2]) * late[1]
    if len(ends_refs) == 2:
        ends_refs[0][...] = state.astype(bf16)
        ends_refs[1][...] = adjoint.astype(bf16)
    else:
        put_ends(ends_refs[0], state, adjoint, early[2] + late[2])
    if first:
        before = after = jnp.zeros((count, width), f32)
        before_steps = after_steps = jnp.zeros((1, width), f32)
    else:
        before, after = rest[0][:count], rest[0][count : 2 * count]
        before_steps = rest[0][2 * count : 2 * count + 1]
        after_steps = rest[0][2 * count + 1 : 2 * count + 2]
    new_passed_ref[:count, :] = before + jnp.where(second, through(decay, before_steps) * other[0], 0.0)
    new_passed_ref[count : 2 * count, :] = after + jnp.where(
        second, 0.0, through(decay, after_steps) * other[1]
    )
    new_passed_ref[2 * count : 2 * count + 1, :] = before_steps + jnp.where(second, other[2], 0.0)
    new_passed_ref[2 * count + 1 : 2 * count + 2, :] = after_steps + jnp.where(second, 0.0, other[2])


def carried(ends, decay_log):
    count, width = decay_log.shape
    place = lax.axis_index("wide").astype(jnp.int32)
    state = jax.ShapeDtypeStruct((count, width), bf16)
    passed_kind = jax.ShapeDtypeStruct((2 * count + 8, width), f32)
    packed, passed = ends, []
    vmem = pl.BlockSpec(memory_space=pltpu.VMEM)
    for k, kinds in enumerate(([jax.ShapeDtypeStruct(ends.shape, bf16)], [state, state])):
        new_passed, *out = pl.pallas_call(
            functools.partial(round_kernel, first=k == 0),
            in_specs=[pl.BlockSpec(memory_space=pltpu.SMEM)] + [vmem] * (3 + k),
            out_shape=[passed_kind] + kinds,
            cost_estimate=tiny_cost,
            name="carry_round",
        )((place >> k & 1)[None], decay_log, packed, swapped(packed, "wide", 2**k), *passed)
        packed, passed = out[0], [new_passed]
    from_before = passed_along(out[0], "wide", 4)
    from_after = passed_along(out[1], "wide", -4)
    return passed[0], from_before, from_after


def local(
    tokens,
    norm_gain,
    in_weight,
    conv_weight,
    conv_bias,
    select_weight,
    step_weight,
    step_bias,
    decay_log,
    skip_gain,
    out_weight,
    segment_ids,
    cotangent,
):
    rows, features = tokens.shape
    taps = conv_weight.shape[0]
    columns = select_weight.shape[0]
    rank = step_weight.shape[0]
    count = decay_log.shape[0]
    right_half = lax.axis_index("narrow") == 1

    def both_halves(own, other):
        return jnp.concatenate(
            [jnp.where(right_half, other, own), jnp.where(right_half, own, other)], axis=1
        )

    other_tokens = swapped(tokens, "narrow", 1)
    other_cot = swapped(cotangent, "narrow", 1)
    edge, other_edge = to_next_both(edge_rows_of(segment_ids, tokens))

    whole_low, normed_ext, normed, inverse, masks = normalized(
        tokens, other_tokens, edge, other_edge, norm_gain[None], segment_ids[None]
    )
    projected = jnp.einsum(
        "td,dce->cte", normed_ext, in_weight, preferred_element_type=f32
    ).astype(bf16)
    convolved, act, selected = convolve(
        projected, conv_weight, conv_bias[None], select_weight, masks
    )
    other_selected = swapped(selected, "narrow", 1)
    cot_whole = both_halves(cotangent, other_cot)
    gated_grad = lax.dot_general(
        cot_whole, out_weight, contract_last, preferred_element_type=f32
    )
    step_pre, step, ends = scan_ends(
        selected,
        other_selected,
        step_weight,
        step_bias[None],
        act,
        projected,
        gated_grad,
        masks,
        decay_log,
    )
    passed, entering, returning = carried(ends, decay_log)
    gated, gate_grad, out_product, gate_product, entry = scan_forward(
        selected,
        other_selected,
        step,
        act,
        projected,
        gated_grad,
        masks,
        decay_log,
        passed,
        entering,
        skip_gain[None],
        cot_whole,
        normed,
    )
    products = (after(out_product, returning), gate_product)
    out_sum, gate_sum = lax.psum(products, "wide")
    wide_place = lax.axis_index("wide").astype(jnp.int32)
    four_place = (wide_place & 3)[None]

    def narrow_halves(array):
        low, high = array[:, :features], array[:, features:]
        return jnp.where(right_half, high, low), jnp.where(right_half, low, high)

    def after_forward(products):
        whole = whole_low.astype(f32)
        act_grad, select_grad, scan_small = scan_backward(
            selected,
            other_selected,
            step_pre,
            step,
            act,
            projected,
            gated_grad,
            masks,
            decay_log,
            entry,
            passed,
            returning,
            skip_gain[None],
            step_weight,
        )
        normed_four = quarter_of_four(after(normed, select_grad))
        inner_main, before, last, conv_small = convolve_grad(
            select_grad,
            swapped(select_grad, "narrow", 1),
            select_weight,
            act_grad,
            convolved,
            act,
            projected,
            conv_weight,
            masks,
            [],
        )
        following = passed_along(before, "wide", -1)
        inner_grad = patched(segment_ids, inner_main, last, following, *normed_four)
        near = swapped(inner_grad, "wide", 2)
        keep, send = small_halves(wide_place[None] & 1, scan_small, conv_small, inner_grad)
        keep, send = folded((wide_place >> 1 & 1)[None], keep, swapped(send, "wide", 1))
        smalls = [keep, swapped(send, "wide", 2)]
        normed_part = jnp.einsum(
            "cte,dce->td", jnp.stack([inner_grad, gate_grad]), in_weight, preferred_element_type=f32
        )
        gain_part = jnp.sum(normed_part * whole * inverse, axis=0, keepdims=True)
        row_part = jnp.sum(normed_part * norm_gain * whole, axis=1)[None]
        first_bits, *more_bits = group_bits(2)
        gain_sum = gain_part + swapped(gain_part, "narrow", 1)
        for bit in (bit for bits in more_bits for bit in bits):
            gain_sum = gain_sum + swapped(gain_sum, "wide", bit)
        row_theirs = swapped(row_part, "narrow", 1)
        near = after(near, gain_sum, row_theirs, smalls[1])
        far = swapped(jnp.concatenate([inner_grad, near]), "wide", 1)
        keep, *sends = inner_quarter(
            (wide_place >> 2 & 3)[None],
            inner_grad,
            near,
            far,
            normed_four,
            smalls,
            [],
        )
        normed_mine, normed_other = narrow_halves(normed_part)
        normed_theirs = swapped(after(normed_other, keep), "narrow", 1)
        out_part = jnp.dot(after(gated, keep), out_weight, preferred_element_type=f32)
        out_mine, out_other = narrow_halves(out_part)
        out_theirs = swapped(out_other, "narrow", 1)
        layer_out = (tokens.astype(f32) + (out_mine + out_theirs)).astype(bf16)
        row_sum = (row_part + row_theirs).reshape(rows, 1)
        gain_mine = jnp.where(right_half, norm_gain[features:], norm_gain[:features])
        whole_grad = inverse * (gain_mine * (normed_mine + normed_theirs)) - tokens.astype(f32) * (
            inverse * inverse * inverse
        ) * (row_sum / (2 * features))
        tokens_grad = (whole_grad + cotangent.astype(f32)).astype(bf16)
        held = keep
        for n, flip in enumerate(flips(first_bits)[1:]):
            held = held + swapped(sends[n], "wide", flip).astype(f32)
        for bits in more_bits:
            held = scattered(held, bits)
        held = held.astype(bf16)
        for bits in reversed(more_bits):
            held = gathered(held, bits)
        spare = jnp.broadcast_to(gain_sum, (block_rows - used_rows, gain_sum.shape[1]))
        held = jnp.concatenate([held[: held.shape[0] - spare.shape[0]], spare.astype(bf16)])
        held = gathered(held, first_bits)
        return held, layer_out, tokens_grad

    kinds = jax.eval_shape(after_forward, products)
    held, layer_out, tokens_grad = lax.cond(
        wide_place >= 0,
        after_forward,
        lambda pair: jax.tree.map(lambda kind: jnp.zeros(kind.shape, kind.dtype), kinds),
        products,
    )

    core = swapped(held, "wide", 1)
    begun, out_weight_grad = joined_first(four_place, gate_sum, held, core, out_sum)
    near = swapped(held, "wide", 2)
    far = swapped(near, "wide", 1)
    conv_at = rank + count + 2
    (
        in_weight_grad,
        step_weight_grad,
        decay_log_grad,
        skip_gain_grad,
        step_bias_grad,
        select_weight_grad,
        conv_weight_grad,
        conv_bias_grad,
        norm_gain_grad,
    ) = joined_last(
        four_place,
        gate_sum,
        (held, core, near, far),
        begun,
        (0, rank, rank + count, rank + count + 1, conv_at, conv_at + columns, conv_at + columns + taps),
        (rank, count, 1, 1, columns, taps, 1, 1),
    )
    return (
        layer_out,
        tokens_grad,
        norm_gain_grad[0],
        in_weight_grad,
        conv_weight_grad,
        conv_bias_grad[0],
        select_weight_grad,
        step_weight_grad,
        step_bias_grad[0],
        decay_log_grad,
        skip_gain_grad[0],
        out_weight_grad,
    )


def solution(mesh):
    placed = (
        P("wide", "narrow"),
        P(),
        P(None, None, "narrow"),
        P(None, "narrow"),
        P("narrow"),
        P(None, "narrow"),
        P(None, "narrow"),
        P("narrow"),
        P(None, "narrow"),
        P("narrow"),
        P("narrow", None),
        P("wide"),
        P("wide", "narrow"),
    )
    return jax.shard_map(
        local,
        mesh=mesh,
        in_specs=placed,
        out_specs=(
            P("wide", "narrow"),
            P("wide", "narrow"),
            P(),
            P(None, None, "narrow"),
            P(None, "narrow"),
            P("narrow"),
            P(None, "narrow"),
            P(None, "narrow"),
            P("narrow"),
            P(None, "narrow"),
            P("narrow"),
            P("narrow", None),
        ),
        check_vma=False,
    )
```

```python
import functools

import jax
import jax.numpy as jnp
from jax import lax
from jax.experimental import pallas as pl
from jax.experimental.pallas import tpu as pltpu
from jax.sharding import PartitionSpec as P

epsilon = 1e-05
log2e = 1.4426950408889634
reset_step = 1e30
lanes = 128
halo = 16
body_rows = 32
scan_width = 512
vmem_bytes = 56 * 1024 * 1024
tiny_cost = pl.CostEstimate(flops=1, bytes_accessed=1, transcendentals=0)
f32 = jnp.float32
bf16 = jnp.bfloat16
contract_first = (((0,), (0,)), ((), ()))
contract_last = (((1,), (1,)), ((), ()))


def passed_along(array, axis, by):
    peers = lax.axis_size(axis)
    pairs = [(i, i + by) for i in range(peers) if 0 <= i + by < peers]
    return lax.ppermute(array, axis, pairs)


def swapped(array, axis, bit):
    peers = lax.axis_size(axis)
    return lax.ppermute(array, axis, [(i, i ^ bit) for i in range(peers)])


def wide_bits():
    bit, bits = 1, []
    while bit < lax.axis_size("wide"):
        bits.append(bit)
        bit *= 2
    return bits


def to_next_both(array):
    count, sides = lax.axis_size("wide"), lax.axis_size("narrow")
    pairs = [
        (i * sides + k, (i + 1) * sides + (sides - 1 - k))
        for i in range(count - 1)
        for k in range(sides)
    ]
    return passed_along(array, "wide", 1), lax.ppermute(array, ("wide", "narrow"), pairs)


def is_upper(bit):
    return (lax.axis_index("wide") & bit) != 0


def group_bits(size):
    bits, bit = [], 4
    while bit < lax.axis_size("wide"):
        bits.append(bit)
        bit *= 2
    return [tuple(bits[k : k + size]) for k in range(0, len(bits), size)]


def flips(bits):
    return [sum(b for k, b in enumerate(bits) if n >> k & 1) for n in range(2 ** len(bits))]


def scattered(piece, bits):
    rows = piece.shape[0] // 2 ** len(bits)
    here = sum(is_upper(b).astype(jnp.int32) << k for k, b in enumerate(bits))

    def block(n):
        return lax.dynamic_slice_in_dim(piece, (here ^ n) * rows, rows, 0)

    total = block(0).astype(f32)
    for n, flip in enumerate(flips(bits)):
        if n > 0:
            total = total + swapped(block(n).astype(bf16), "wide", flip).astype(f32)
    return total


def gathered(held, bits):
    blocks = [held] + [swapped(held, "wide", flip) for flip in flips(bits)[1:]]
    for bit in bits:
        upper = is_upper(bit)
        blocks = [
            jnp.concatenate([jnp.where(upper, b, a), jnp.where(upper, a, b)])
            for a, b in zip(blocks[0::2], blocks[1::2])
        ]
    return blocks[0]


def quarter_of_four(array):
    width = array.shape[1] // 4
    here = lax.axis_index("wide") & 3

    def quarter(n):
        return lax.dynamic_slice_in_dim(array, (here ^ n) * width, width, 1)

    return [quarter(0)] + [swapped(quarter(n), "wide", n) for n in (2, 1, 3)]


def silu_slope(values):
    logistic = jax.nn.sigmoid(values)
    return logistic * (1.0 + values * (1.0 - logistic))


def softplus(values):
    return jnp.maximum(values, 0.0) + jnp.log1p(jnp.exp(-jnp.abs(values)))


def column_spec(rows, start=0):
    return pl.BlockSpec((rows, scan_width), lambda j: (0, start + j))


def part_spec(part, rows, start=0):
    return pl.BlockSpec((None, rows, scan_width), lambda j: (part, 0, start + j))


def whole_spec(rows, width):
    return pl.BlockSpec((rows, width), lambda j: (0, 0))


def call(kernel, name, width, in_specs, out_specs, out_shape, scratch, *operands):
    return pl.pallas_call(
        kernel,
        grid=(width // scan_width,),
        in_specs=in_specs,
        out_specs=out_specs,
        out_shape=out_shape,
        scratch_shapes=scratch,
        compiler_params=pltpu.CompilerParams(vmem_limit_bytes=vmem_bytes),
        cost_estimate=tiny_cost,
        name=name,
    )(*operands)


def conv_kernel(
    inner_ref,
    conv_weight_ref,
    conv_bias_ref,
    select_ref,
    mask_ref,
    convolved_ref,
    act_ref,
    selected_ref,
    inner,
):
    rows = act_ref.shape[0]
    taps = conv_weight_ref.shape[0]
    inner[:halo, :] = inner_ref[rows:, :].astype(f32)
    inner[halo:, :] = inner_ref[:rows, :].astype(f32)
    total = conv_bias_ref[...] + conv_weight_ref[taps - 1 :, :] * inner[halo:, :]
    for lag in range(1, taps):
        earlier = inner[pl.ds(halo - lag, rows), :] * mask_ref[:, lag : lag + 1]
        total = total + conv_weight_ref[taps - 1 - lag : taps - lag, :] * earlier
    convolved_ref[...] = total
    act = (total * jax.nn.sigmoid(total)).astype(bf16)
    act_ref[...] = act
    part = lax.dot_general(select_ref[...], act, contract_last, preferred_element_type=f32)

    @pl.when(pl.program_id(0) == 0)
    def _():
        selected_ref[...] = part

    @pl.when(pl.program_id(0) > 0)
    def _():
        selected_ref[...] += part


def convolve(projected, conv_weight, conv_bias, select_weight, masks):
    parts, extended, width = projected.shape
    rows = extended - halo
    taps = conv_weight.shape[0]
    columns = select_weight.shape[0]
    return call(
        conv_kernel,
        "convolve",
        width,
        [
            part_spec(0, extended),
            column_spec(taps),
            column_spec(1),
            column_spec(columns),
            whole_spec(rows, masks.shape[1]),
        ],
        [column_spec(rows), column_spec(rows), whole_spec(columns, rows)],
        [
            jax.ShapeDtypeStruct((rows, width), f32),
            jax.ShapeDtypeStruct((rows, width), bf16),
            jax.ShapeDtypeStruct((columns, rows), f32),
        ],
        [pltpu.VMEM((extended, scan_width), f32)],
        projected,
        conv_weight,
        conv_bias,
        select_weight,
        masks,
    )


def coef_columns(coef, block):
    per_tile = lanes // body_rows
    start = pl.multiple_of((block // per_tile) * lanes, lanes)
    tile = coef[:, pl.ds(start, lanes)]
    back = body_rows * lax.rem(block, per_tile)
    return pltpu.roll(tile, lax.rem(lanes - back, lanes), 1)


def put_ends(ends_ref, state, adjoint, total):
    count, width = state.shape
    ends_ref[:count, :] = state.astype(bf16)
    ends_ref[count : 2 * count, :] = adjoint.astype(bf16)
    high = total.astype(bf16).astype(f32)
    upper = lax.broadcasted_iota(jnp.int32, (16, width), 0) < 8
    ends_ref[2 * count :, :] = jnp.where(upper, high, total - high).astype(bf16)


def get_ends(ends_ref, count):
    total = ends_ref[2 * count :].astype(f32)
    return (
        ends_ref[:count].astype(f32),
        ends_ref[count : 2 * count].astype(f32),
        total[:1] + total[8:9],
    )


def ends_kernel(
    selected_ref,
    other_ref,
    step_weight_ref,
    step_bias_ref,
    act_ref,
    gate_ref,
    gated_grad_ref,
    mask_ref,
    decay_log_ref,
    step_pre_ref,
    step_ref,
    ends_ref,
    coef,
    held_step,
    drive,
    scan_grad,
):
    rows = act_ref.shape[0]
    count = decay_log_ref.shape[0]
    rank = step_weight_ref.shape[0]
    decay2 = -jnp.exp(decay_log_ref[...]) * log2e
    selected = selected_ref[...] + other_ref[...]
    coef[...] = selected[rank:, :]
    step_low = selected[:rank, :].astype(bf16)
    step_pre = step_bias_ref[...] + lax.dot_general(
        step_low, step_weight_ref[...], contract_first, preferred_element_type=f32
    )
    step_pre_ref[...] = step_pre
    step = softplus(step_pre)
    step_ref[...] = step
    held_step[...] = jnp.where(mask_ref[:, 1:2] > 0.0, step, reset_step)
    drive[...] = step * act_ref[...].astype(f32)
    gate = gate_ref[...].astype(f32)
    scan_grad[...] = gated_grad_ref[...] * (gate * jax.nn.sigmoid(gate))
    zero = jnp.zeros(decay2.shape, f32)

    def body(block, carried):
        state, product, adjoint = carried
        columns = coef_columns(coef, block)
        for i in range(body_rows):
            row = pl.ds(block * body_rows + i, 1)
            factor = jnp.exp2(held_step[row, :] * decay2)
            state = factor * state + columns[:count, i : i + 1] * drive[row, :]
            product = factor * product
            adjoint = adjoint + product * (columns[count:, i : i + 1] * scan_grad[row, :])
        return state, product, adjoint

    state, product, adjoint = lax.fori_loop(0, rows // body_rows, body, (zero, zero + 1.0, zero))
    put_ends(ends_ref, state, adjoint, jnp.sum(held_step[...], axis=0, keepdims=True))


def scan_ends(
    selected, other, step_weight, step_bias, act, projected, gated_grad, masks, decay_log
):
    rows, width = act.shape
    count = decay_log.shape[0]
    columns = selected.shape[0]
    rank = step_weight.shape[0]
    return call(
        ends_kernel,
        "scan_ends",
        width,
        [
            whole_spec(columns, rows),
            whole_spec(columns, rows),
            column_spec(rank),
            column_spec(1),
            column_spec(rows),
            part_spec(1, rows),
            column_spec(rows),
            whole_spec(rows, masks.shape[1]),
            column_spec(count),
        ],
        [column_spec(rows), column_spec(rows), column_spec(2 * count + 16)],
        [
            jax.ShapeDtypeStruct((rows, width), f32),
            jax.ShapeDtypeStruct((rows, width), f32),
            jax.ShapeDtypeStruct((2 * count + 16, width), bf16),
        ],
        [pltpu.VMEM((2 * count, rows), f32)] + [pltpu.VMEM((rows, scan_width), f32)] * 3,
        selected,
        other,
        step_weight,
        step_bias,
        act,
        projected,
        gated_grad,
        masks,
        decay_log,
    )


def lane_tiles(values):
    return [values[:, k : k + lanes] for k in range(0, values.shape[1], lanes)]


def tree_sum(parts):
    while len(parts) > 1:
        odd = parts[len(parts) // 2 * 2 :]
        parts = [a + b for a, b in zip(parts[0::2], parts[1::2])] + odd
    return parts[0]


def keep_halves(scratch, i, values):
    for k, tile in enumerate(lane_tiles(values)):
        at = (k * body_rows + i) * 8
        scratch[at : at + 8, :] = tile[:8] + tile[8:]


def put_state_sums(scratch, out_ref, block):
    for group in range(body_rows // 8):
        row = pl.ds(pl.multiple_of(block * body_rows + group * 8, 8), 8)
        for k in range(out_ref.shape[1] // lanes):
            at = (k * body_rows + group * 8) * 8
            total = tree_sum([scratch[pl.ds(at + n, 8, stride=8), :] for n in range(8)])
            out_ref[row, k * lanes : (k + 1) * lanes] = total


def lane_sums(values):
    ones = jnp.ones((8, lanes), bf16)
    high = values.astype(bf16)
    low = (values - high.astype(f32)).astype(bf16)
    total = lax.dot_general(ones, high, contract_last, preferred_element_type=f32)
    total += lax.dot_general(ones, low, contract_last, preferred_element_type=f32)
    return total[:1, :]


def at_token(t, count):
    return pl.ds(pl.multiple_of(t * count, count), count)


def forward_kernel(
    selected_ref,
    other_ref,
    step_ref,
    act_ref,
    gate_ref,
    gated_grad_ref,
    mask_ref,
    decay_log_ref,
    passed_ref,
    entering_ref,
    skip_ref,
    cot_ref,
    normed_ref,
    gated_ref,
    gate_grad_ref,
    out_product_ref,
    gate_product_ref,
    entry_ref,
    coef,
    held_step,
    drive,
    scanned,
    halves,
):
    rows = step_ref.shape[0]
    count = decay_log_ref.shape[0]
    rank = selected_ref.shape[0] - 2 * count
    decay = -jnp.exp(decay_log_ref[...])
    decay2 = decay * log2e
    before_steps = passed_ref[2 * count : 2 * count + 1, :]
    entry = passed_ref[:count, :] + through(decay, before_steps) * entering_ref[...].astype(f32)
    entry_ref[...] = entry
    coef[...] = selected_ref[rank:, :] + other_ref[rank:, :]
    act = act_ref[...].astype(f32)
    held_step[...] = jnp.where(mask_ref[:, 1:2] > 0.0, step_ref[...], reset_step)
    drive[...] = step_ref[...] * act

    def forward(block, state):
        columns = coef_columns(coef, block)
        for i in range(body_rows):
            row = pl.ds(block * body_rows + i, 1)
            factor = jnp.exp2(held_step[row, :] * decay2)
            state = factor * state + columns[:count, i : i + 1] * drive[row, :]
            keep_halves(halves, i, columns[count:, i : i + 1] * state)
        put_state_sums(halves, scanned, block)
        return state

    lax.fori_loop(0, rows // body_rows, forward, entry)
    gate = gate_ref[...].astype(f32)
    logistic = jax.nn.sigmoid(gate)
    total = scanned[...] + skip_ref[...] * act
    gated = (total * (gate * logistic)).astype(bf16)
    gated_ref[...] = gated
    out_product_ref[...] = lax.dot_general(
        gated, cot_ref[...], contract_first, preferred_element_type=f32
    ).astype(bf16)
    slope = logistic * (1.0 + gate * (1.0 - logistic))
    gate_grad = (gated_grad_ref[...] * total * slope).astype(bf16)
    gate_grad_ref[...] = gate_grad
    gate_product_ref[...] = lax.dot_general(
        normed_ref[...], gate_grad, contract_first, preferred_element_type=f32
    ).astype(bf16)


def scan_forward(
    selected,
    other,
    step,
    act,
    projected,
    gated_grad,
    masks,
    decay_log,
    passed,
    entering,
    skip_gain,
    cot,
    normed,
):
    rows, width = step.shape
    count = decay_log.shape[0]
    columns = selected.shape[0]
    return call(
        forward_kernel,
        "scan_forward",
        width,
        [
            whole_spec(columns, rows),
            whole_spec(columns, rows),
            column_spec(rows),
            column_spec(rows),
            part_spec(1, rows),
            column_spec(rows),
            whole_spec(rows, masks.shape[1]),
            column_spec(count),
            column_spec(2 * count + 8),
            column_spec(count),
            column_spec(1),
            whole_spec(*cot.shape),
            whole_spec(*normed.shape),
        ],
        [
            column_spec(rows),
            column_spec(rows),
            pl.BlockSpec((scan_width, cot.shape[1]), lambda j: (j, 0)),
            column_spec(normed.shape[1]),
            column_spec(count),
        ],
        [
            jax.ShapeDtypeStruct((rows, width), bf16),
            jax.ShapeDtypeStruct((rows, width), bf16),
            jax.ShapeDtypeStruct((width, cot.shape[1]), bf16),
            jax.ShapeDtypeStruct((normed.shape[1], width), bf16),
            jax.ShapeDtypeStruct((count, width), f32),
        ],
        [pltpu.VMEM((2 * count, rows), f32)]
        + [pltpu.VMEM((rows, scan_width), f32)] * 3
        + [pltpu.VMEM((8 * body_rows * (scan_width // lanes), lanes), f32)],
        selected,
        other,
        step,
        act,
        projected,
        gated_grad,
        masks,
        decay_log,
        passed,
        entering,
        skip_gain,
        cot,
        normed,
    )


def backward_kernel(
    selected_ref,
    other_ref,
    step_pre_ref,
    step_ref,
    act_ref,
    gate_ref,
    gated_grad_ref,
    mask_ref,
    decay_log_ref,
    entry_ref,
    passed_ref,
    returning_ref,
    skip_ref,
    step_weight_ref,
    act_grad_ref,
    select_grad_ref,
    small_ref,
    coef,
    held_step,
    drive,
    scan_grad,
    weighted,
    held_sum,
    states,
    factors,
    halves,
    more_halves,
    in_sum,
    read_sum,
):
    rows = step_ref.shape[0]
    count = decay_log_ref.shape[0]
    rank = step_weight_ref.shape[0]
    blocks = rows // body_rows
    decay = -jnp.exp(decay_log_ref[...])
    decay2 = decay * log2e
    after_steps = passed_ref[2 * count + 1 : 2 * count + 2, :]
    tail = passed_ref[count : 2 * count, :] + through(decay, after_steps) * returning_ref[...].astype(f32)
    selected = selected_ref[...] + other_ref[...]
    coef[...] = selected[rank:, :]
    step_low = selected[:rank, :].astype(bf16)
    step = step_ref[...]
    act = act_ref[...].astype(f32)
    held_step[...] = jnp.where(mask_ref[:, 1:2] > 0.0, step, reset_step)
    drive[...] = step * act
    gate = gate_ref[...].astype(f32)
    grads = gated_grad_ref[...] * (gate * jax.nn.sigmoid(gate))
    scan_grad[...] = grads
    small_ref[rank + count : rank + count + 1, :] = jnp.sum(grads * act, axis=0, keepdims=True)
    states[:count, :] = entry_ref[...]

    @pl.when(pl.program_id(0) == 0)
    def _():
        in_sum[...] = jnp.zeros(in_sum.shape, f32)
        read_sum[...] = jnp.zeros(read_sum.shape, f32)
        select_grad_ref[...] = jnp.zeros(select_grad_ref.shape, f32)

    def forward(block, state):
        columns = coef_columns(coef, block)
        for i in range(body_rows):
            t = block * body_rows + i
            row = pl.ds(t, 1)
            factor = jnp.exp2(held_step[row, :] * decay2)
            state = factor * state + columns[:count, i : i + 1] * drive[row, :]
            factors[at_token(t, count), :] = factor
            states[at_token(t + 1, count), :] = state
        return state

    lax.fori_loop(0, blocks, forward, entry_ref[...])

    def backward(k, carried):
        adjoint, decay_grad = carried
        block = blocks - 1 - k
        columns = coef_columns(coef, block)
        for i in range(body_rows - 1, -1, -1):
            t = block * body_rows + i
            row = pl.ds(t, 1)
            here = at_token(t, count)
            grad = scan_grad[row, :]
            summed = columns[count:, i : i + 1] * grad + adjoint
            read_sum[here, :] += tree_sum(lane_tiles(grad * states[at_token(t + 1, count), :]))
            in_sum[here, :] += tree_sum(lane_tiles(summed * drive[row, :]))
            keep_halves(halves, i, summed * columns[:count, i : i + 1])
            adjoint = factors[here, :] * summed
            held = adjoint * states[here, :]
            decay_grad = decay_grad + held * step_ref[row, :]
            keep_halves(more_halves, i, held * decay)
        put_state_sums(halves, weighted, block)
        put_state_sums(more_halves, held_sum, block)
        return adjoint, decay_grad

    ignored, decay_grad = lax.fori_loop(
        0, blocks, backward, (tail, jnp.zeros(decay.shape, f32))
    )
    act_grad_ref[...] = step * weighted[...] + skip_ref[...] * scan_grad[...]
    step_grad = act * weighted[...] + held_sum[...]
    pre_grad = (step_grad * jax.nn.sigmoid(step_pre_ref[...])).astype(bf16)
    small_ref[:rank, :] = jnp.dot(step_low, pre_grad, preferred_element_type=f32)
    small_ref[rank : rank + count, :] = decay_grad * decay
    bias_grad = jnp.sum(pre_grad.astype(f32), axis=0, keepdims=True)
    small_ref[rank + count + 1 : rank + count + 2, :] = bias_grad
    select_grad_ref[:rank, :] += lax.dot_general(
        step_weight_ref[...], pre_grad, contract_last, preferred_element_type=f32
    )

    @pl.when(pl.program_id(0) == pl.num_programs(0) - 1)
    def _():
        for n in range(count):
            at = pl.ds(n, rows, stride=count)
            select_grad_ref[rank + n : rank + n + 1, :] = lane_sums(in_sum[at, :])
            select_grad_ref[rank + count + n : rank + count + n + 1, :] = lane_sums(read_sum[at, :])


def scan_backward(
    selected,
    other,
    step_pre,
    step,
    act,
    projected,
    gated_grad,
    masks,
    decay_log,
    entry,
    passed,
    returning,
    skip_gain,
    step_weight,
):
    rows, width = step.shape
    count = decay_log.shape[0]
    columns = selected.shape[0]
    rank = step_weight.shape[0]
    half_rows = 8 * body_rows * (scan_width // lanes)
    small = rank + count + 2
    return call(
        backward_kernel,
        "scan_backward",
        width,
        [
            whole_spec(columns, rows),
            whole_spec(columns, rows),
            column_spec(rows),
            column_spec(rows),
            column_spec(rows),
            part_spec(1, rows),
            column_spec(rows),
            whole_spec(rows, masks.shape[1]),
            column_spec(count),
            column_spec(count),
            column_spec(2 * count + 8),
            column_spec(count),
            column_spec(1),
            column_spec(rank),
        ],
        [column_spec(rows), whole_spec(columns, rows), column_spec(small)],
        [
            jax.ShapeDtypeStruct((rows, width), f32),
            jax.ShapeDtypeStruct((columns, rows), f32),
            jax.ShapeDtypeStruct((small, width), f32),
        ],
        [pltpu.VMEM((2 * count, rows), f32)]
        + [pltpu.VMEM((rows, scan_width), f32)] * 5
        + [
            pltpu.VMEM(((rows + 1) * count, scan_width), f32),
            pltpu.VMEM((rows * count, scan_width), f32),
            pltpu.VMEM((half_rows, lanes), f32),
            pltpu.VMEM((half_rows, lanes), f32),
            pltpu.VMEM((rows * count, lanes), f32),
            pltpu.VMEM((rows * count, lanes), f32),
        ],
        selected,
        other,
        step_pre,
        step,
        act,
        projected,
        gated_grad,
        masks,
        decay_log,
        entry,
        passed,
        returning,
        skip_gain,
        step_weight,
    )


def conv_grad_kernel(
    select_grad_ref,
    other_ref,
    select_ref,
    act_grad_ref,
    convolved_ref,
    act_ref,
    inner_ref,
    conv_weight_ref,
    mask_ref,
    *rest,
):
    inner_grad_ref, before_ref, last_ref, small_ref, inner, shifted = rest[-6:]
    rows = act_ref.shape[0]
    taps = conv_weight_ref.shape[0]
    columns = select_ref.shape[0]
    select_grad = (select_grad_ref[...] + other_ref[...]).astype(bf16)
    total = act_grad_ref[...] + lax.dot_general(
        select_grad, select_ref[...], contract_first, preferred_element_type=f32
    )
    conv_grad = total * silu_slope(convolved_ref[...])
    small_ref[:columns, :] = jnp.dot(select_grad, act_ref[...], preferred_element_type=f32)
    inner[:halo, :] = inner_ref[rows:, :].astype(f32)
    inner[halo:, :] = inner_ref[:rows, :].astype(f32)
    edges = jnp.zeros((8, conv_grad.shape[1]), f32)
    shifted[:8, :] = edges
    shifted[rows + 8 :, :] = edges
    out = conv_weight_ref[taps - 1 :, :] * conv_grad
    before = edges
    small_ref[columns + taps - 1 : columns + taps, :] = jnp.sum(
        conv_grad * inner[halo:, :], axis=0, keepdims=True
    )
    for lag in range(1, taps):
        masked = conv_grad * mask_ref[:, lag : lag + 1]
        at = taps - 1 - lag
        small_ref[columns + at : columns + at + 1, :] = jnp.sum(
            masked * inner[pl.ds(halo - lag, rows), :], axis=0, keepdims=True
        )
        shifted[8 : rows + 8, :] = masked
        weight = conv_weight_ref[at : at + 1, :]
        out = out + weight * shifted[pl.ds(8 + lag, rows), :]
        before = before + weight * shifted[pl.ds(lag, 8), :]
    small_ref[columns + taps : columns + taps + 1, :] = jnp.sum(conv_grad, axis=0, keepdims=True)
    inner_grad_ref[...] = out.astype(bf16)
    before_ref[...] = before
    last_ref[...] = out[rows - 8 :, :]


def convolve_grad(
    select_grad, other, select_weight, act_grad, convolved, act, projected, conv_weight, masks, waits
):
    rows, width = act.shape
    extended = rows + halo
    columns = select_weight.shape[0]
    taps = conv_weight.shape[0]
    small = columns + taps + 1
    return call(
        conv_grad_kernel,
        "convolve_grad",
        width,
        [
            whole_spec(columns, rows),
            whole_spec(columns, rows),
            column_spec(columns),
            column_spec(rows),
            column_spec(rows),
            column_spec(rows),
            part_spec(0, extended),
            column_spec(taps),
            whole_spec(rows, masks.shape[1]),
        ]
        + [pl.BlockSpec(memory_space=pl.ANY)] * len(waits),
        [column_spec(rows), column_spec(8), column_spec(8), column_spec(small)],
        [
            jax.ShapeDtypeStruct((rows, width), bf16),
            jax.ShapeDtypeStruct((8, width), f32),
            jax.ShapeDtypeStruct((8, width), f32),
            jax.ShapeDtypeStruct((small, width), f32),
        ],
        [pltpu.VMEM((extended, scan_width), f32), pltpu.VMEM((rows + 16, scan_width), f32)],
        select_grad,
        other,
        select_weight,
        act_grad,
        convolved,
        act,
        projected,
        conv_weight,
        masks,
        *waits,
    )


def normalize_kernel(
    own_ref,
    other_ref,
    edge_ref,
    other_edge_ref,
    gain_ref,
    ids_ref,
    whole_ref,
    extended_ref,
    normed_ref,
    inverse_ref,
    mask_ref,
    rows_ref,
):
    rows, half = own_ref.shape
    ids = ids_ref[...].astype(f32)
    place = lax.broadcasted_iota(jnp.int32, ids.shape, 1)
    same = []
    for lag in range(8):
        earlier = jnp.where(place < lag, ids[:, :1], pltpu.roll(ids, lag, 1)) if lag else ids
        same.append(jnp.where(earlier == ids, 1.0, 0.0))
    spare = jnp.zeros((lanes - 8, rows), f32)
    mask_ref[...] = jnp.concatenate(same + [spare]).T
    right = lax.axis_index("narrow") == 1
    for at, own, other in ((0, own_ref, other_ref), (rows, edge_ref, other_edge_ref)):
        end = at + own.shape[0]
        rows_ref[at:end, :half] = jnp.where(right, other[...], own[...])
        rows_ref[at:end, half:] = jnp.where(right, own[...], other[...])
    whole_ref[...] = rows_ref[:rows, :]
    whole = rows_ref[...].astype(f32)
    inverse = lax.rsqrt(jnp.mean(whole * whole, axis=1, keepdims=True) + epsilon)
    normed = (whole * inverse * gain_ref[...]).astype(bf16)
    extended_ref[...] = normed
    normed_ref[...] = normed[:rows]
    inverse_ref[...] = inverse[:rows]


def normalized(own, other, edge, other_edge, gain, ids):
    rows, half = own.shape
    extended = rows + edge.shape[0]
    return pl.pallas_call(
        normalize_kernel,
        out_shape=[
            jax.ShapeDtypeStruct((rows, 2 * half), bf16),
            jax.ShapeDtypeStruct((extended, 2 * half), bf16),
            jax.ShapeDtypeStruct((rows, 2 * half), bf16),
            jax.ShapeDtypeStruct((rows, 1), f32),
            jax.ShapeDtypeStruct((rows, lanes), f32),
        ],
        scratch_shapes=[pltpu.VMEM((extended, 2 * half), bf16)],
        cost_estimate=tiny_cost,
        name="normalized",
    )(own, other, edge, other_edge, gain, ids)


def after(array, *waits):
    anywhere = pl.BlockSpec(memory_space=pl.ANY)
    return pl.pallas_call(
        lambda *refs: None,
        in_specs=[anywhere] * (1 + len(waits)),
        out_specs=anywhere,
        out_shape=jax.ShapeDtypeStruct(array.shape, array.dtype),
        input_output_aliases={0: 0},
        cost_estimate=tiny_cost,
        name="after",
    )(array, *waits)


def patch_kernel(ids_ref, rows_ref, last_ref, next_ref, *rest):
    count = ids_ref.shape[0]
    place = lax.broadcasted_iota(jnp.int32, (8, 1), 0)
    same = jnp.zeros((8, 1), f32)
    for lag in range(8):
        here = jnp.where(ids_ref[count - 1 - lag] == ids_ref[count - 1], 1.0, 0.0)
        same = same + jnp.where(place == 7 - lag, here, 0.0)
    total = last_ref[...] + next_ref[...] * same
    rows = rows_ref[...].astype(f32)
    rest[-1][...] = jnp.concatenate([rows[: halo - 8], total]).astype(bf16)


def patched(ids, grads, last, following, *waits):
    rows, width = grads.shape
    block = pl.BlockSpec((halo, width), lambda j: (rows // halo - 1, 0))
    edge = pl.BlockSpec((8, width), lambda j: (0, 0))
    return pl.pallas_call(
        patch_kernel,
        grid=(1,),
        in_specs=[pl.BlockSpec(memory_space=pltpu.SMEM), block, edge, edge]
        + [pl.BlockSpec(memory_space=pl.ANY)] * len(waits),
        out_specs=block,
        out_shape=jax.ShapeDtypeStruct((rows, width), bf16),
        input_output_aliases={1: 0},
        cost_estimate=tiny_cost,
        name="patched",
    )(ids, grads, last, following, *waits)


def edge_kernel(ids_ref, tokens_ref, out_ref):
    rows = ids_ref.shape[0]
    taps = 4
    out_ref[...] = tokens_ref[...]
    place = lax.broadcasted_iota(jnp.int32, (halo, 1), 0)
    same = jnp.zeros((halo, 1), f32)
    for lag in range(taps):
        here = jnp.where(ids_ref[rows - 1 - lag] == ids_ref[rows - 1], 1.0, 0.0)
        same = same + jnp.where(place == halo - 1 - lag, here, 0.0)
    out_ref[...] = (tokens_ref[...].astype(f32) * same).astype(bf16)


def edge_rows_of(ids, tokens):
    rows, width = tokens.shape
    return pl.pallas_call(
        edge_kernel,
        grid=(1,),
        in_specs=[
            pl.BlockSpec(memory_space=pltpu.SMEM),
            pl.BlockSpec((halo, width), lambda j: (rows // halo - 1, 0)),
        ],
        out_specs=pl.BlockSpec((halo, width), lambda j: (0, 0)),
        out_shape=jax.ShapeDtypeStruct((halo, width), bf16),
        cost_estimate=tiny_cost,
        name="edge_rows",
    )(ids, tokens)


block_rows, used_rows = 16, 12


def small_kernel(core_ref, scan_ref, conv_ref, wait_ref, keep_ref, send_ref, rows, blocks):
    rows[...] = jnp.zeros(rows.shape, f32)
    rows[: scan_ref.shape[0], :] = scan_ref[...]
    rows[scan_ref.shape[0] : scan_ref.shape[0] + conv_ref.shape[0], :] = conv_ref[...]
    blocks[...] = jnp.zeros(blocks.shape, f32)
    for n in range(16):
        blocks[n * block_rows : n * block_rows + used_rows, :] = rows[
            n * used_rows : (n + 1) * used_rows, :
        ]
    half = keep_ref.shape[0]
    mine = pl.ds(pl.multiple_of(core_ref[0] * half, half), half)
    other = pl.ds(pl.multiple_of((1 - core_ref[0]) * half, half), half)
    keep_ref[...] = blocks[mine, :]
    send_ref[...] = blocks[other, :].astype(bf16)


def small_halves(core, scan_small, conv_small, wait):
    width = scan_small.shape[1]
    return pl.pallas_call(
        small_kernel,
        in_specs=[pl.BlockSpec(memory_space=pltpu.SMEM)]
        + [pl.BlockSpec(memory_space=pltpu.VMEM)] * 2
        + [pl.BlockSpec(memory_space=pl.ANY)],
        out_shape=[jax.ShapeDtypeStruct((8 * block_rows, width), kind) for kind in (f32, bf16)],
        scratch_shapes=[
            pltpu.VMEM((16 * used_rows, width), f32),
            pltpu.VMEM((16 * block_rows, width), f32),
        ],
        cost_estimate=tiny_cost,
        name="small_halves",
    )(core, scan_small, conv_small, wait)


def fold_kernel(upper_ref, keep_ref, arrived_ref, out_ref, send_ref):
    size = out_ref.shape[0]
    mine = pl.ds(pl.multiple_of(upper_ref[0] * size, size), size)
    other = pl.ds(pl.multiple_of((1 - upper_ref[0]) * size, size), size)
    out_ref[...] = keep_ref[mine, :] + arrived_ref[mine, :].astype(f32)
    send_ref[...] = (keep_ref[other, :] + arrived_ref[other, :].astype(f32)).astype(bf16)


def folded(upper, keep, arrived):
    rows, width = keep.shape
    return pl.pallas_call(
        fold_kernel,
        in_specs=[pl.BlockSpec(memory_space=pltpu.SMEM)]
        + [pl.BlockSpec(memory_space=pltpu.VMEM)] * 2,
        out_shape=[jax.ShapeDtypeStruct((rows // 2, width), kind) for kind in (f32, bf16)],
        cost_estimate=tiny_cost,
        name="folded",
    )(upper, keep, arrived)


def quarter_kernel(
    place_ref,
    own_ref,
    near_ref,
    far_ref,
    normed_0,
    normed_1,
    normed_2,
    normed_3,
    small_ref,
    arrived_ref,
    *rest,
):
    keep_ref, *sends_refs, piece, small = rest[-6:]
    total = None
    tokens = own_ref.shape[0]
    grads = (own_ref[...], near_ref[...], far_ref[:tokens, :], far_ref[tokens:, :])
    for left, right in zip((normed_0, normed_1, normed_2, normed_3), grads):
        part = lax.dot_general(left[...], right, contract_first, preferred_element_type=f32)
        total = part if total is None else total + part
    piece[...] = total
    small[...] = small_ref[...] + arrived_ref[...].astype(f32)
    rows, spare = piece.shape[0] // 4, small.shape[0] // 4
    for n in range(4):
        block = place_ref[0] ^ n
        inner_rows = piece[pl.ds(pl.multiple_of(block * rows, rows), rows), :]
        small_rows = small[pl.ds(pl.multiple_of(block * spare, spare), spare), :]
        if n == 0:
            keep_ref[:rows, :] = inner_rows
            keep_ref[rows:, :] = small_rows
        else:
            sends_refs[n - 1][:rows, :] = inner_rows.astype(bf16)
            sends_refs[n - 1][rows:, :] = small_rows.astype(bf16)


def inner_quarter(place, own, near, far, normed, smalls, waits):
    width = own.shape[1]
    quarter = normed[0].shape[1]
    spare = smalls[0].shape[0]
    rows = (quarter + spare) // 4
    return pl.pallas_call(
        quarter_kernel,
        in_specs=[pl.BlockSpec(memory_space=pltpu.SMEM)]
        + [pl.BlockSpec(memory_space=pltpu.VMEM)] * 9
        + [pl.BlockSpec(memory_space=pl.ANY)] * len(waits),
        out_shape=[jax.ShapeDtypeStruct((rows, width), f32)]
        + [jax.ShapeDtypeStruct((rows, width), bf16)] * 3,
        scratch_shapes=[pltpu.VMEM((quarter, width), f32), pltpu.VMEM((spare, width), f32)],
        compiler_params=pltpu.CompilerParams(vmem_limit_bytes=vmem_bytes),
        cost_estimate=tiny_cost,
        name="inner_quarter",
    )(place, own, near, far, *normed, *smalls, *waits)


def put_quarter(out_ref, gate_ref, inner_ref):
    rows = out_ref.shape[0] // 4
    out_ref[:, 1, :] = gate_ref[...].astype(f32)
    for n in range(4):
        at = n * (rows + block_rows)
        out_ref[n * rows : (n + 1) * rows, 0, :] = inner_ref[at : at + rows, :].astype(f32)


def first_join_kernel(place_ref, gate_ref, first_ref, second_ref, low_ref, out_ref, wide_ref):
    wide_ref[...] = low_ref[...].astype(f32)

    @pl.when(pl.program_id(0) == 0)
    def _():
        put_quarter(out_ref, gate_ref, first_ref)

    @pl.when(pl.program_id(0) == 1)
    def _():
        put_quarter(out_ref, gate_ref, second_ref)


def last_join_kernel(place_ref, gate_ref, first_ref, second_ref, *rest, small_rows):
    held = rest[:4]
    out_ref, *row_refs, gain_ref, blocks = rest[5:]

    @pl.when(pl.program_id(0) == 0)
    def _():
        put_quarter(out_ref, gate_ref, first_ref)

    @pl.when(pl.program_id(0) == 1)
    def _():
        put_quarter(out_ref, gate_ref, second_ref)
        rows = out_ref.shape[0] // 4
        for flip, ref in enumerate(held):
            number = place_ref[0] ^ flip
            number = (number & 1) * 2 + number // 2
            for n in range(4):
                at = (number * 4 + n) * block_rows
                taken = ref[(n + 1) * rows + n * block_rows : (n + 1) * (rows + block_rows), :]
                blocks[pl.ds(pl.multiple_of(at, block_rows), block_rows), :] = taken.astype(f32)
        for ref, start in zip(row_refs, small_rows):
            for row in range(ref.shape[0]):
                at = (start + row) // used_rows * block_rows + (start + row) % used_rows
                ref[row : row + 1, :] = blocks[at : at + 1, :]
        gain_ref[...] = sum(
            blocks[n * block_rows + used_rows : n * block_rows + used_rows + 1, :] for n in range(16)
        )


def joined(kernel, place, flip, gate, first, second, specs, operands, out_specs, out_shape, scratch, aliases):
    depth, width = gate.shape
    quarter = depth // 4

    def target(j, place):
        return place[0] ^ (flip + j)

    whole = pl.BlockSpec(first.shape, lambda j, place: (0, 0))
    return pl.pallas_call(
        kernel,
        grid_spec=pltpu.PrefetchScalarGridSpec(
            num_scalar_prefetch=1,
            grid=(2,),
            in_specs=[
                pl.BlockSpec((quarter, width), lambda j, place: (target(j, place), 0)),
                whole,
                whole,
            ]
            + specs,
            out_specs=[
                pl.BlockSpec((quarter, 2, width), lambda j, place: (target(j, place), 0, 0))
            ]
            + out_specs,
            scratch_shapes=scratch,
        ),
        out_shape=[jax.ShapeDtypeStruct((depth, 2, width), f32)] + out_shape,
        input_output_aliases=aliases,
        compiler_params=pltpu.CompilerParams(vmem_limit_bytes=vmem_bytes),
        cost_estimate=tiny_cost,
        name="joined",
    )(place, gate, first, second, *operands)


def joined_first(place, gate, first, second, low):
    rows, width = low.shape
    half = pl.BlockSpec((rows // 2, width), lambda j, place: (j, 0))
    kind = jax.ShapeDtypeStruct((rows, width), f32)
    return joined(
        first_join_kernel, place, 0, gate, first, second, [half], [low], [half], [kind], [], {}
    )


def joined_last(place, gate, held, begun, small_rows, small_counts):
    width = gate.shape[1]
    whole = pl.BlockSpec(held[0].shape, lambda j, place: (0, 0))
    return joined(
        functools.partial(last_join_kernel, small_rows=small_rows),
        place,
        2,
        gate,
        held[2],
        held[3],
        [whole] * 4 + [pl.BlockSpec(memory_space=pl.ANY)],
        [*held, begun],
        [pl.BlockSpec((rows, width), lambda j, place: (0, 0)) for rows in small_counts],
        [jax.ShapeDtypeStruct((rows, width), f32) for rows in small_counts],
        [pltpu.VMEM((16 * block_rows, width), f32)],
        {8: 0},
    )


def through(decay, total):
    return jnp.exp(decay * total)


def round_kernel(second_ref, decay_log_ref, own_ref, other_ref, *rest, first):
    count, width = decay_log_ref.shape
    new_passed_ref, *ends_refs = rest if first else rest[1:]
    decay = -jnp.exp(decay_log_ref[...])
    second = second_ref[0] > 0
    own, other = get_ends(own_ref, count), get_ends(other_ref, count)
    early = [jnp.where(second, b, a) for a, b in zip(own, other)]
    late = [jnp.where(second, a, b) for a, b in zip(own, other)]
    state = late[0] + through(decay, late[2]) * early[0]
    adjoint = early[1] + through(decay, early[2]) * late[1]
    if len(ends_refs) == 2:
        ends_refs[0][...] = state.astype(bf16)
        ends_refs[1][...] = adjoint.astype(bf16)
    else:
        put_ends(ends_refs[0], state, adjoint, early[2] + late[2])
    if first:
        before = after = jnp.zeros((count, width), f32)
        before_steps = after_steps = jnp.zeros((1, width), f32)
    else:
        before, after = rest[0][:count], rest[0][count : 2 * count]
        before_steps = rest[0][2 * count : 2 * count + 1]
        after_steps = rest[0][2 * count + 1 : 2 * count + 2]
    new_passed_ref[:count, :] = before + jnp.where(second, through(decay, before_steps) * other[0], 0.0)
    new_passed_ref[count : 2 * count, :] = after + jnp.where(
        second, 0.0, through(decay, after_steps) * other[1]
    )
    new_passed_ref[2 * count : 2 * count + 1, :] = before_steps + jnp.where(second, other[2], 0.0)
    new_passed_ref[2 * count + 1 : 2 * count + 2, :] = after_steps + jnp.where(second, 0.0, other[2])


def carried(ends, decay_log):
    count, width = decay_log.shape
    place = lax.axis_index("wide").astype(jnp.int32)
    state = jax.ShapeDtypeStruct((count, width), bf16)
    passed_kind = jax.ShapeDtypeStruct((2 * count + 8, width), f32)
    packed, passed = ends, []
    vmem = pl.BlockSpec(memory_space=pltpu.VMEM)
    for k, kinds in enumerate(([jax.ShapeDtypeStruct(ends.shape, bf16)], [state, state])):
        new_passed, *out = pl.pallas_call(
            functools.partial(round_kernel, first=k == 0),
            in_specs=[pl.BlockSpec(memory_space=pltpu.SMEM)] + [vmem] * (3 + k),
            out_shape=[passed_kind] + kinds,
            cost_estimate=tiny_cost,
            name="carry_round",
        )((place >> k & 1)[None], decay_log, packed, swapped(packed, "wide", 2**k), *passed)
        packed, passed = out[0], [new_passed]
    from_before = passed_along(out[0], "wide", 4)
    from_after = passed_along(out[1], "wide", -4)
    return passed[0], from_before, from_after


def local(
    tokens,
    norm_gain,
    in_weight,
    conv_weight,
    conv_bias,
    select_weight,
    step_weight,
    step_bias,
    decay_log,
    skip_gain,
    out_weight,
    segment_ids,
    cotangent,
):
    rows, features = tokens.shape
    taps = conv_weight.shape[0]
    columns = select_weight.shape[0]
    rank = step_weight.shape[0]
    count = decay_log.shape[0]
    right_half = lax.axis_index("narrow") == 1

    def both_halves(own, other):
        return jnp.concatenate(
            [jnp.where(right_half, other, own), jnp.where(right_half, own, other)], axis=1
        )

    other_tokens = swapped(tokens, "narrow", 1)
    other_cot = swapped(cotangent, "narrow", 1)
    edge, other_edge = to_next_both(edge_rows_of(segment_ids, tokens))

    whole_low, normed_ext, normed, inverse, masks = normalized(
        tokens, other_tokens, edge, other_edge, norm_gain[None], segment_ids[None]
    )
    projected = jnp.einsum(
        "td,dce->cte", normed_ext, in_weight, preferred_element_type=f32
    ).astype(bf16)
    convolved, act, selected = convolve(
        projected, conv_weight, conv_bias[None], select_weight, masks
    )
    other_selected = swapped(selected, "narrow", 1)
    cot_whole = both_halves(cotangent, other_cot)
    gated_grad = lax.dot_general(
        cot_whole, out_weight, contract_last, preferred_element_type=f32
    )
    step_pre, step, ends = scan_ends(
        selected,
        other_selected,
        step_weight,
        step_bias[None],
        act,
        projected,
        gated_grad,
        masks,
        decay_log,
    )
    passed, entering, returning = carried(ends, decay_log)
    gated, gate_grad, out_product, gate_product, entry = scan_forward(
        selected,
        other_selected,
        step,
        act,
        projected,
        gated_grad,
        masks,
        decay_log,
        passed,
        entering,
        skip_gain[None],
        cot_whole,
        normed,
    )
    products = (after(out_product, returning), gate_product)
    out_sum, gate_sum = lax.psum(products, "wide")
    wide_place = lax.axis_index("wide").astype(jnp.int32)
    four_place = (wide_place & 3)[None]

    def narrow_halves(array):
        low, high = array[:, :features], array[:, features:]
        return jnp.where(right_half, high, low), jnp.where(right_half, low, high)

    def after_forward(products):
        whole = whole_low.astype(f32)
        act_grad, select_grad, scan_small = scan_backward(
            selected,
            other_selected,
            step_pre,
            step,
            act,
            projected,
            gated_grad,
            masks,
            decay_log,
            entry,
            passed,
            returning,
            skip_gain[None],
            step_weight,
        )
        normed_four = quarter_of_four(after(normed, select_grad))
        inner_main, before, last, conv_small = convolve_grad(
            select_grad,
            swapped(select_grad, "narrow", 1),
            select_weight,
            act_grad,
            convolved,
            act,
            projected,
            conv_weight,
            masks,
            [],
        )
        following = passed_along(before, "wide", -1)
        inner_grad = patched(segment_ids, inner_main, last, following, *normed_four)
        near = swapped(inner_grad, "wide", 2)
        keep, send = small_halves(wide_place[None] & 1, scan_small, conv_small, inner_grad)
        keep, send = folded((wide_place >> 1 & 1)[None], keep, swapped(send, "wide", 1))
        smalls = [keep, swapped(send, "wide", 2)]
        normed_part = jnp.einsum(
            "cte,dce->td", jnp.stack([inner_grad, gate_grad]), in_weight, preferred_element_type=f32
        )
        gain_part = jnp.sum(normed_part * whole * inverse, axis=0, keepdims=True)
        row_part = jnp.sum(normed_part * norm_gain * whole, axis=1)[None]
        first_bits, *more_bits = group_bits(2)
        gain_sum = gain_part + swapped(gain_part, "narrow", 1)
        for bit in (bit for bits in more_bits for bit in bits):
            gain_sum = gain_sum + swapped(gain_sum, "wide", bit)
        row_theirs = swapped(row_part, "narrow", 1)
        near = after(near, gain_sum, row_theirs, smalls[1])
        far = swapped(jnp.concatenate([inner_grad, near]), "wide", 1)
        keep, *sends = inner_quarter(
            (wide_place >> 2 & 3)[None],
            inner_grad,
            near,
            far,
            normed_four,
            smalls,
            [],
        )
        normed_mine, normed_other = narrow_halves(normed_part)
        normed_theirs = swapped(after(normed_other.astype(bf16), keep), "narrow", 1).astype(f32)
        out_part = jnp.dot(after(gated, keep), out_weight, preferred_element_type=f32)
        out_mine, out_other = narrow_halves(out_part)
        out_theirs = swapped(out_other.astype(bf16), "narrow", 1).astype(f32)
        layer_out = (tokens.astype(f32) + (out_mine + out_theirs)).astype(bf16)
        row_sum = (row_part + row_theirs).reshape(rows, 1)
        gain_mine = jnp.where(right_half, norm_gain[features:], norm_gain[:features])
        whole_grad = inverse * (gain_mine * (normed_mine + normed_theirs)) - tokens.astype(f32) * (
            inverse * inverse * inverse
        ) * (row_sum / (2 * features))
        tokens_grad = (whole_grad + cotangent.astype(f32)).astype(bf16)
        held = keep
        for n, flip in enumerate(flips(first_bits)[1:]):
            held = held + swapped(sends[n], "wide", flip).astype(f32)
        for bits in more_bits:
            held = scattered(held, bits)
        held = held.astype(bf16)
        for bits in reversed(more_bits):
            held = gathered(held, bits)
        spare = jnp.broadcast_to(gain_sum, (block_rows - used_rows, gain_sum.shape[1]))
        held = jnp.concatenate([held[: held.shape[0] - spare.shape[0]], spare.astype(bf16)])
        held = gathered(held, first_bits)
        return held, layer_out, tokens_grad

    kinds = jax.eval_shape(after_forward, products)
    held, layer_out, tokens_grad = lax.cond(
        wide_place >= 0,
        after_forward,
        lambda pair: jax.tree.map(lambda kind: jnp.zeros(kind.shape, kind.dtype), kinds),
        products,
    )

    core = swapped(held, "wide", 1)
    begun, out_weight_grad = joined_first(four_place, gate_sum, held, core, out_sum)
    near = swapped(held, "wide", 2)
    far = swapped(near, "wide", 1)
    conv_at = rank + count + 2
    (
        in_weight_grad,
        step_weight_grad,
        decay_log_grad,
        skip_gain_grad,
        step_bias_grad,
        select_weight_grad,
        conv_weight_grad,
        conv_bias_grad,
        norm_gain_grad,
    ) = joined_last(
        four_place,
        gate_sum,
        (held, core, near, far),
        begun,
        (0, rank, rank + count, rank + count + 1, conv_at, conv_at + columns, conv_at + columns + taps),
        (rank, count, 1, 1, columns, taps, 1, 1),
    )
    return (
        layer_out,
        tokens_grad,
        norm_gain_grad[0],
        in_weight_grad,
        conv_weight_grad,
        conv_bias_grad[0],
        select_weight_grad,
        step_weight_grad,
        step_bias_grad[0],
        decay_log_grad,
        skip_gain_grad[0],
        out_weight_grad,
    )


def solution(mesh):
    placed = (
        P("wide", "narrow"),
        P(),
        P(None, None, "narrow"),
        P(None, "narrow"),
        P("narrow"),
        P(None, "narrow"),
        P(None, "narrow"),
        P("narrow"),
        P(None, "narrow"),
        P("narrow"),
        P("narrow", None),
        P("wide"),
        P("wide", "narrow"),
    )
    return jax.shard_map(
        local,
        mesh=mesh,
        in_specs=placed,
        out_specs=(
            P("wide", "narrow"),
            P("wide", "narrow"),
            P(),
            P(None, None, "narrow"),
            P(None, "narrow"),
            P("narrow"),
            P(None, "narrow"),
            P(None, "narrow"),
            P("narrow"),
            P(None, "narrow"),
            P("narrow"),
            P("narrow", None),
        ),
        check_vma=False,
    )
```
